32 devices in a mesh: seq: 8 (over z, y), batch: 4 (over x, core).
Axes of the slice: x: 2, y: 2, z: 4, core: 2. Of those that a mesh axis runs over, the one named last changes fastest.
Arguments:
- tokens: bfloat16 [4, 3072, 1024], P('batch', 'seq'), may hold values from -6 to 6
- memory: bfloat16 [4, 512, 1024], P('batch', 'seq'), may hold values from -6 to 6
- segment_ids: int32 [4, 3072], P('batch', 'seq'), may hold values from 0 to 2, as said below
- padding_mask: int32 [4, 3072], P('batch', 'seq'), may hold values from 0 to 1, as said below
- cotangent: bfloat16 [4, 3072, 1024], P('batch', 'seq'), may hold values from -6 to 6
- prefix_embed: bfloat16 [30, 1024], replicated, may hold values from -6 to 6
- prefix_first: bfloat16 [1024, 512], replicated, may hold values from -0.1875 to 0.1875
- first_bias: float32 [512], replicated, may hold values from -3 to 3
- prefix_second: bfloat16 [512, 2048], replicated, may hold values from -0.25 to 0.25
- second_bias: float32 [2048], replicated, may hold values from -3 to 3
- adapter_down: bfloat16 [1024, 512], replicated, may hold values from -0.1875 to 0.1875
- down_bias: float32 [512], replicated, may hold values from -3 to 3
- adapter_raise: bfloat16 [512, 1024], replicated, may hold values from -0.0625 to 0.0625
- raise_bias: float32 [1024], replicated, may hold values from -2 to 2
- norm_gain: float32 [3, 1024], replicated, may hold values from 0.25 to 1.75
- norm_shift: float32 [3, 1024], replicated, may hold values from -2 to 2
- self_query: bfloat16 [1024, 1024], replicated, may hold values from -0.1875 to 0.1875
- self_key: bfloat16 [1024, 1024], replicated, may hold values from -0.1875 to 0.1875
- self_value: bfloat16 [1024, 1024], replicated, may hold values from -0.1875 to 0.1875
- self_output: bfloat16 [1024, 1024], replicated, may hold values from -3 to 3
- cross_query: bfloat16 [1024, 1024], replicated, may hold values from -0.1875 to 0.1875
- cross_key: bfloat16 [1024, 1024], replicated, may hold values from -0.1875 to 0.1875
- cross_value: bfloat16 [1024, 1024], replicated, may hold values from -0.1875 to 0.1875
- cross_output: bfloat16 [1024, 1024], replicated, may hold values from -3 to 3
- feed_in: bfloat16 [1024, 4096], replicated, may hold values from -0.1875 to 0.1875
- feed_out: bfloat16 [4096, 1024], replicated, may hold values from -0.09375 to 0.09375
Outputs:
- layer_output: bfloat16 [4, 3072, 1024], P('batch', 'seq')
- token_grad: bfloat16 [4, 3072, 1024], P('batch', 'seq')
- memory_grad: bfloat16 [4, 512, 1024], P('batch', 'seq')
- embed_grad: float32 [30, 1024], replicated
- first_weight_grad: float32 [1024, 512], replicated
- first_bias_grad: float32 [512], replicated
- second_weight_grad: float32 [512, 2048], replicated
- second_bias_grad: float32 [2048], replicated
- down_weight_grad: float32 [1024, 512], replicated
- down_bias_grad: float32 [512], replicated
- raise_weight_grad: float32 [512, 1024], replicated
- raise_bias_grad: float32 [1024], replicated
- gain_grad: float32 [3, 1024], replicated
- shift_grad: float32 [3, 1024], replicated
The draws below stay inside these ranges and needn't reach their ends.
Inputs may be any that keep to these rules, and one draw needn't show every extreme that they name: `segment_ids`: each row is 0 on its first 1 to 192 positions, then 1 up to a position from 2880 to 2976, then 2 to its end. `padding_mask`: each row is 0 on its last 1 to 96 positions and on one run of 1 to 96 positions that starts between 384 and 2304, and 1 elsewhere.
All inputs are finite; a program needn't handle non-finite values.
Results may differ from the reference program's by a relative error of at most 0.033.
Values may be sent and summed in bfloat16 or wider, within the bound.
A program may use at most 320 MiB of HBM per device.

```python
import math
import jax
import jax.numpy as jnp
from jax import lax

D = 1024
H = 16
HD = 64
FF = 4096
AD = 512
PH = 512
NP = 30
SEQ_DEV = 384
SEQLEN = 3072
MEM = 512
ROWS = 4


def draw_segment_ids(key, part):
    key = jax.random.fold_in(key, 11)
    first_key, last_key = jax.random.split(key)
    opening = jax.random.randint(first_key, (ROWS, 1), 1, SEQ_DEV // 2 + 1)
    closing = jax.random.randint(last_key, (ROWS, 1), SEQLEN - SEQ_DEV // 2, SEQLEN - SEQ_DEV // 4 + 1)
    places = jnp.arange(SEQLEN, dtype=jnp.int32)[None, :]
    return (places >= opening).astype(jnp.int32) + (places >= closing).astype(jnp.int32)


def draw_padding_mask(key, part):
    key = jax.random.fold_in(key, 23)
    tail_key, start_key, gap_key = jax.random.split(key, 3)
    tail_len = jax.random.randint(tail_key, (ROWS, 1), 1, SEQ_DEV // 4 + 1)
    gap_start = jax.random.randint(start_key, (ROWS, 1), SEQ_DEV, SEQLEN - 2 * SEQ_DEV + 1)
    gap_len = jax.random.randint(gap_key, (ROWS, 1), 1, SEQ_DEV // 4 + 1)
    places = jnp.arange(SEQLEN, dtype=jnp.int32)[None, :]
    in_gap = (places >= gap_start) & (places < gap_start + gap_len)
    return ((places < SEQLEN - tail_len) & jnp.logical_not(in_gap)).astype(jnp.int32)


def block_levels(rng, extent, pieces, smallest, largest):
    def one(position, blocks):
        heights = jax.random.uniform(jax.random.fold_in(jax.random.fold_in(rng, 6), position), (blocks,), jnp.float32, smallest / len(pieces), largest / len(pieces))
        return jnp.repeat(jnp.exp(heights), extent[position] // blocks).reshape((-1,) + (1,) * (len(extent) - position - 1))

    level = one(*pieces[0])
    for cut in pieces[1:]:
        level = level * one(*cut)
    return level


def noise(key, extent, deviation, limit, cuts=(), held_as=jnp.bfloat16):
    array = deviation * jax.random.normal(key, extent, jnp.float32)
    if cuts:
        array = array * block_levels(key, extent, cuts, -0.22, 0.18)
    return jnp.clip(array, -limit, limit).astype(held_as)


def setup_inputs(seed: int = 0) -> dict:
    arg_keys = jax.random.split(jax.random.key(seed), 27)
    tokens = noise(arg_keys[0], (ROWS, SEQLEN, D), 1.0, 6.0, ((0, 4), (1, 8)))
    memory = noise(arg_keys[1], (ROWS, MEM, D), 1.0, 6.0, ((0, 4), (1, 8)))
    segment_ids = draw_segment_ids(jax.random.fold_in(arg_keys[26], 71), 0)
    padding_mask = draw_padding_mask(jax.random.fold_in(arg_keys[26], 71), 0)
    cotangent = noise(arg_keys[4], (ROWS, SEQLEN, D), 1.0, 6.0, ((0, 4), (1, 8)))
    prefix_embed = noise(arg_keys[5], (NP, D), 1.0, 6.0)
    prefix_first = noise(arg_keys[6], (D, PH), D ** -0.5, 0.1875)
    first_bias = noise(arg_keys[7], (PH,), 0.5, 3.0, (), jnp.float32)
    prefix_second = noise(arg_keys[8], (PH, 2 * D), PH ** -0.5, 0.25)
    second_bias = noise(arg_keys[9], (2 * D,), 0.5, 3.0, (), jnp.float32)
    adapter_down = noise(arg_keys[10], (D, AD), D ** -0.5, 0.1875)
    down_bias = noise(arg_keys[11], (AD,), 0.5, 3.0, (), jnp.float32)
    adapter_raise = noise(arg_keys[12], (AD, D), (16 * AD) ** -0.5, 0.0625)
    raise_bias = noise(arg_keys[13], (D,), 0.25, 2.0, (), jnp.float32)
    norm_gain = jnp.clip(1.0 + 0.15 * jax.random.normal(arg_keys[14], (3, D), jnp.float32), 0.25, 1.75)
    norm_shift = noise(arg_keys[15], (3, D), 0.3, 2.0, (), jnp.float32)
    self_query = noise(arg_keys[16], (D, D), D ** -0.5, 0.1875)
    self_key = noise(arg_keys[17], (D, D), D ** -0.5, 0.1875)
    self_value = noise(arg_keys[18], (D, D), D ** -0.5, 0.1875)
    self_output = noise(arg_keys[19], (D, D), (max(D // 256, 1)) ** -0.5, 3.0)
    cross_query = noise(arg_keys[20], (D, D), D ** -0.5, 0.1875)
    cross_key = noise(arg_keys[21], (D, D), D ** -0.5, 0.1875)
    cross_value = noise(arg_keys[22], (D, D), D ** -0.5, 0.1875)
    cross_output = noise(arg_keys[23], (D, D), (max(D // 256, 1)) ** -0.5, 3.0)
    feed_in = noise(arg_keys[24], (D, FF), D ** -0.5, 0.1875)
    feed_out = noise(arg_keys[25], (FF, D), FF ** -0.5, 0.09375)
    return dict(tokens=tokens, memory=memory, segment_ids=segment_ids, padding_mask=padding_mask, cotangent=cotangent, prefix_embed=prefix_embed, prefix_first=prefix_first, first_bias=first_bias, prefix_second=prefix_second, second_bias=second_bias, adapter_down=adapter_down, down_bias=down_bias, adapter_raise=adapter_raise, raise_bias=raise_bias, norm_gain=norm_gain, norm_shift=norm_shift, self_query=self_query, self_key=self_key, self_value=self_value, self_output=self_output, cross_query=cross_query, cross_key=cross_key, cross_value=cross_value, cross_output=cross_output, feed_in=feed_in, feed_out=feed_out)


@jax.custom_vjp
def low(v):
    return lax.optimization_barrier(v.astype(jnp.bfloat16)).astype(jnp.float32)

@jax.custom_vjp
def low_back(v):
    return v

def low_keep(v):
    return (low(v), None)

def low_pass(kept, grad):
    return (grad,)

def back_keep(v):
    return (v, None)

def back_low(kept, grad):
    return (low(grad),)
low.defvjp(low_keep, low_pass)
low_back.defvjp(back_keep, back_low)
masked_score = -1e+30
norm_eps = 1e-05
block_rows = 512

def matmul(left, right):
    return jnp.dot(left, right, precision=lax.Precision.HIGHEST, preferred_element_type=jnp.float32)

def layer_norm(value, gain, shift):
    center = lax.optimization_barrier(jnp.mean(value, axis=-1, keepdims=True))
    centered = value - center
    spread = lax.optimization_barrier(jnp.mean(centered * centered, axis=-1, keepdims=True))
    return centered * lax.rsqrt(spread + norm_eps) * gain + shift

def exact_gelu(value):
    return jax.nn.gelu(value, approximate=False)

def attend(queries, keys, values, allowed):
    scores = low_back(0.125 * jnp.einsum('ahd,bhd->hab', queries, keys, precision=lax.Precision.HIGHEST))
    scores = jnp.where(allowed[None], scores, masked_score)
    row_max = lax.optimization_barrier(jnp.max(scores, axis=-1, keepdims=True))
    raised = jnp.exp(scores - row_max)
    weights = low(raised / lax.optimization_barrier(jnp.sum(raised, axis=-1, keepdims=True)))
    return jnp.einsum('hab,bhd->ahd', weights, values, precision=lax.Precision.HIGHEST)

def split_heads(value):
    return value.reshape(value.shape[0], H, HD)

def row_layer(row_tokens, row_memory, row_segments, row_padding, prefix_keys, prefix_values, frozen, trained):
    self_query, self_key, self_value, self_output, cross_query, cross_key, cross_value, cross_output, feed_in, feed_out = frozen
    adapter_down, down_bias, adapter_raise, raise_bias, norm_gain, norm_shift = trained
    seq_len = row_tokens.shape[0]
    mem_len = row_memory.shape[0]
    queries = split_heads(low(low_back(matmul(row_tokens, self_query))))
    keys = split_heads(low(low_back(matmul(row_tokens, self_key))))
    values = split_heads(low(low_back(matmul(row_tokens, self_value))))
    all_keys = jnp.concatenate([prefix_keys, keys], 0)
    all_values = jnp.concatenate([prefix_values, values], 0)
    key_tags = jnp.where(row_padding == 1, row_segments, -1)
    key_pos = jnp.arange(seq_len, dtype=jnp.int32)
    query_block = math.gcd(seq_len, block_rows)
    block_ids = jnp.arange(seq_len // query_block, dtype=jnp.int32)

    def self_block(block_index):
        first_row = block_index * query_block
        block_queries = lax.dynamic_slice_in_dim(queries, first_row, query_block, 0)
        block_tags = lax.dynamic_slice_in_dim(row_segments, first_row, query_block, 0)
        query_pos = first_row + jnp.arange(query_block, dtype=jnp.int32)
        own = (block_tags[:, None] == key_tags[None, :]) & (key_pos[None, :] <= query_pos[:, None])
        allowed = jnp.concatenate([jnp.ones((query_block, NP), dtype=jnp.bool_), own], 1)
        return attend(block_queries, all_keys, all_values, allowed)
    attended = low(low_back(lax.map(jax.checkpoint(self_block), block_ids).reshape(seq_len, D)))
    first_sum = row_tokens + low_back(matmul(attended, self_output))
    first_norm = layer_norm(first_sum, norm_gain[0], norm_shift[0])
    cross_queries = split_heads(low(low_back(matmul(low(first_norm), cross_query))))
    mem_keys = split_heads(low(low_back(matmul(row_memory, cross_key))))
    mem_values = split_heads(low(low_back(matmul(row_memory, cross_value))))
    everything = jnp.ones((query_block, mem_len), dtype=jnp.bool_)

    def cross_block(block_index):
        block_queries = lax.dynamic_slice_in_dim(cross_queries, block_index * query_block, query_block, 0)
        return attend(block_queries, mem_keys, mem_values, everything)
    crossed = low(low_back(lax.map(jax.checkpoint(cross_block), block_ids).reshape(seq_len, D)))
    second_sum = first_norm + low_back(matmul(crossed, cross_output))
    second_norm = layer_norm(second_sum, norm_gain[1], norm_shift[1])
    second_low = low(second_norm)
    feed_pre = low_back(matmul(second_low, feed_in))
    feed_act = low(exact_gelu(feed_pre))
    down_pre = low_back(matmul(second_low, adapter_down) + down_bias)
    down_act = low(exact_gelu(down_pre))
    third_sum = second_norm + low_back(matmul(feed_act, feed_out)) + 4.0 * low_back(matmul(down_act, adapter_raise) + raise_bias)
    return layer_norm(third_sum, norm_gain[2], norm_shift[2])

def reference(tokens, memory, segment_ids, padding_mask, cotangent, prefix_embed, prefix_first, first_bias, prefix_second, second_bias, adapter_down, down_bias, adapter_raise, raise_bias, norm_gain, norm_shift, self_query, self_key, self_value, self_output, cross_query, cross_key, cross_value, cross_output, feed_in, feed_out):
    frozen = tuple((weight.astype(jnp.float32) for weight in (self_query, self_key, self_value, self_output, cross_query, cross_key, cross_value, cross_output, feed_in, feed_out)))

    def layer_of(tokens_in, memory_in, embed_in, first_in, fbias_in, second_in, sbias_in, down_in, dbias_in, raise_in, rbias_in, gain_in, shift_in):
        prefix_hidden = jnp.tanh(matmul(embed_in, first_in) + fbias_in)
        prefix_kv = matmul(low(prefix_hidden), second_in) + sbias_in
        prefix_keys = low(prefix_kv[:, :D]).reshape(NP, H, HD)
        prefix_values = low(prefix_kv[:, D:]).reshape(NP, H, HD)
        trained = (down_in, dbias_in, raise_in, rbias_in, gain_in, shift_in)

        def one_row(row_args):
            return row_layer(row_args[0], row_args[1], row_args[2], row_args[3], prefix_keys, prefix_values, frozen, trained)
        return lax.map(one_row, (tokens_in, memory_in, segment_ids, padding_mask))
    floats = (tokens, memory, prefix_embed, prefix_first, first_bias, prefix_second, second_bias, adapter_down, down_bias, adapter_raise, raise_bias, norm_gain, norm_shift)
    floats = tuple((value.astype(jnp.float32) for value in floats))
    result, pullback = jax.vjp(layer_of, *floats)
    grads = pullback(cotangent.astype(jnp.float32))
    return (result.astype(jnp.bfloat16), grads[0].astype(jnp.bfloat16), grads[1].astype(jnp.bfloat16), grads[2], grads[3], grads[4], grads[5], grads[6], grads[7], grads[8], grads[9], grads[10], grads[11], grads[12])
```

```python
import functools

import jax
import jax.numpy as jnp
from jax import lax
from jax.experimental import pallas as pl
from jax.experimental.pallas import tpu as pltpu
from jax.sharding import PartitionSpec as P

H = 16
HD = 64
LANES = 128
PREFIX_ROWS = 32
VMEM_BYTES = 60 * 1024 * 1024
MESH = pl.DeviceIdType.MESH

masked_score = -1e30
norm_eps = 1e-05

def matmul(left, right):
    return jnp.dot(left, right, preferred_element_type=jnp.float32)


def matmul_back(left, right):
    return lax.dot_general(
        left, right, (((left.ndim - 1,), (1,)), ((), ())), preferred_element_type=jnp.float32
    )


def outer_sum(left, right):
    return lax.dot_general(
        left, right, (((0,), (0,)), ((), ())), preferred_element_type=jnp.float32
    )


def precise_back(left, right):
    return lax.dot_general(
        left,
        right,
        (((1,), (1,)), ((), ())),
        precision=lax.Precision.HIGHEST,
        preferred_element_type=jnp.float32,
    )


def precise_outer(left, right):
    return lax.dot_general(
        left,
        right,
        (((0,), (0,)), ((), ())),
        precision=lax.Precision.HIGHEST,
        preferred_element_type=jnp.float32,
    )


def layer_norm(value, gain, shift):
    center = jnp.mean(value, axis=-1, keepdims=True)
    centered = value - center
    spread = jnp.mean(centered * centered, axis=-1, keepdims=True)
    return centered * lax.rsqrt(spread + norm_eps) * gain + shift


def exact_gelu(value):
    return jax.nn.gelu(value, approximate=False)


def to_heads(value):
    return value.reshape(value.shape[0], value.shape[1], H, HD)


def dot_nn(left, right):
    return lax.dot_general(
        left, right, (((1,), (0,)), ((), ())), preferred_element_type=jnp.float32
    )


def dot_nt(left, right):
    return lax.dot_general(
        left, right, (((1,), (1,)), ((), ())), preferred_element_type=jnp.float32
    )


def enter(n, me):
    barrier = pltpu.get_barrier_semaphore()
    for other in range(n):

        @pl.when(other != me)
        def _():
            pl.semaphore_signal(barrier, inc=1, device_id={"seq": other}, device_id_type=MESH)

    pl.semaphore_wait(barrier, n - 1)


def rows_of(index, size):
    return pl.ds(pl.multiple_of(index * size, size), size)


def own_columns(ref, first, me, width):
    if width % LANES == 0:
        return ref[:, pl.ds(pl.multiple_of(first + me * width, LANES), width)].astype(jnp.float32)
    share = LANES // width
    block = ref[:, pl.ds(pl.multiple_of(first + me // share * LANES, LANES), LANES)].astype(
        jnp.float32
    )
    picked = block[:, :width]
    for part in range(1, share):
        picked = jnp.where(me % share == part, block[:, part * width : (part + 1) * width], picked)
    return picked


def head_lanes(shape, head):
    lane = lax.broadcasted_iota(jnp.int32, shape, 1)
    return (lane >= head * HD) & (lane < (head + 1) * HD)


def self_forward_kernel(
    n,
    seg_ref,
    pad_ref,
    tok_ref,
    wq_ref,
    wk_ref,
    wv_ref,
    emb_ref,
    first_ref,
    fbias_ref,
    second_ref,
    sbias_ref,
    att_ref,
    qx_out,
    kx_out,
    v_out,
    pk_out,
    pv_out,
    ot_out,
    lse_out,
    send,
    recv,
    meta_send,
    meta,
    kx,
    qx,
    vt,
    hidden,
    pk,
    pv,
    pvt,
    stat,
    acc,
    o_send,
    o_recv,
    send_sem,
    recv_sem,
    meta_send_sem,
    meta_recv_sem,
    o_send_sem,
    o_recv_sem,
    out_sem,
):
    me = lax.axis_index("seq")
    length, width = tok_ref.shape
    group = width // n
    heads = group // HD
    plane = 2 * length
    planes = n // 2
    block = 2 * LANES
    per_block = block // group
    blocks = width // block

    def meta_copy(peer, slot):
        return pltpu.make_async_remote_copy(
            src_ref=meta_send,
            dst_ref=meta.at[slot],
            send_sem=meta_send_sem.at[peer],
            recv_sem=meta_recv_sem.at[slot],
            device_id={"seq": peer},
            device_id_type=MESH,
        )

    def qkv_copy(peer, slot):
        return pltpu.make_async_remote_copy(
            src_ref=send.at[peer],
            dst_ref=recv.at[:, rows_of(slot, length), :],
            send_sem=send_sem.at[peer],
            recv_sem=recv_sem.at[slot],
            device_id={"seq": peer},
            device_id_type=MESH,
        )

    def out_copy(peer, slot):
        return pltpu.make_async_remote_copy(
            src_ref=o_send.at[peer],
            dst_ref=o_recv.at[slot],
            send_sem=o_send_sem.at[peer],
            recv_sem=o_recv_sem.at[slot],
            device_id={"seq": peer},
            device_id_type=MESH,
        )

    segments = seg_ref[...]
    tags = jnp.where(pad_ref[...] == 1, segments, -1)
    row = lax.broadcasted_iota(jnp.int32, meta_send.shape, 0)
    meta_send[...] = jnp.where(row == 0, segments, tags)
    enter(n, me)
    for other in range(n):

        @pl.when(other != me)
        def _():
            meta_copy(other, me).start()

    meta[me] = meta_send[...]

    def project(step, carry):
        here = lax.rem(me // per_block + 1 + step, blocks)
        columns = pl.ds(pl.multiple_of(here * block, block), block)
        for which, weight in enumerate((wq_ref, wk_ref, wv_ref)):
            piece = dot_nn(tok_ref[...], weight[:, columns]).astype(jnp.bfloat16)
            for part in range(per_block):
                send[here * per_block + part, which] = piece[:, part * group : (part + 1) * group]
        for part in range(per_block):
            peer = here * per_block + part

            @pl.when(peer != me)
            def _():
                qkv_copy(peer, me).start()

            @pl.when(peer == me)
            def _():
                recv[:, rows_of(me, length), :] = send[peer]

        return carry

    lax.fori_loop(0, blocks, project, 0)

    hidden[...] = jnp.zeros_like(hidden)
    hidden[: emb_ref.shape[0], :] = jnp.tanh(dot_nn(emb_ref[...], first_ref[...]) + fbias_ref[...])
    hidden_low = hidden[...].astype(jnp.bfloat16)
    prefix_key = dot_nn(
        hidden_low, own_columns(second_ref, 0, me, group).astype(jnp.bfloat16)
    ) + own_columns(sbias_ref, 0, me, group)
    prefix_value = dot_nn(
        hidden_low, own_columns(second_ref, width, me, group).astype(jnp.bfloat16)
    ) + own_columns(sbias_ref, width, me, group)
    pk[...] = jnp.zeros_like(pk)
    pk[:, :group] = prefix_key.astype(jnp.bfloat16)
    prefix_row = lax.broadcasted_iota(jnp.int32, (pk.shape[0], LANES), 0)
    pk[:, LANES:] = jnp.where(prefix_row < emb_ref.shape[0], 0.0, masked_score).astype(
        jnp.bfloat16
    )
    pv[...] = prefix_value.astype(jnp.bfloat16)
    pvt[...] = prefix_value.T.astype(jnp.bfloat16)

    def arrive(chunk):
        @pl.when(chunk != me)
        def _():
            meta_copy(chunk, chunk).wait_recv()
            qkv_copy(chunk, chunk).wait_recv()

        here = rows_of(chunk, length)
        state = lax.broadcasted_iota(jnp.int32, (LANES, length), 0)
        is_segment = jnp.where(state == meta[chunk, 0:1, :], 1.0, 0.0)
        is_open = jnp.where(state == meta[chunk, 1:2, :], 0.0, masked_score)
        query_state = is_segment.T.astype(jnp.bfloat16)
        kx[here, :group] = recv[1, here, :]
        kx[here, LANES:] = is_open.T.astype(jnp.bfloat16)
        if group < LANES:
            kx[here, group:LANES] = jnp.zeros((length, LANES - group), jnp.bfloat16)
        query = recv[0, here, :].astype(jnp.float32) * 0.125
        for head in range(heads):
            qx[head, here, :group] = jnp.where(
                head_lanes(query.shape, head), query, 0.0
            ).astype(jnp.bfloat16)
            qx[head, here, LANES:] = query_state
            if group < LANES:
                qx[head, here, group:LANES] = jnp.zeros((length, LANES - group), jnp.bfloat16)
        vt[:, here] = recv[2, here, :].astype(jnp.float32).T.astype(jnp.bfloat16)

    def open_plane(which):
        for head in range(heads):
            scores = dot_nt(pk[...], qx[head, rows_of(which, plane), :])
            top = jnp.max(scores, axis=0, keepdims=True)
            raised = jnp.exp(scores - top)
            stat[which, head : head + 1, :] = top
            stat[which, 4 + head : 5 + head, :] = jnp.sum(raised, axis=0, keepdims=True)
            span = slice(head * HD, (head + 1) * HD)
            acc[which, span, :] = dot_nn(pvt[span, :], raised.astype(jnp.bfloat16))

    def pair(upper, lower, diagonal):
        for part in range(2):
            first = length if diagonal and part == 1 else 0
            for head in range(heads):
                queries = qx[head, pl.ds(pl.multiple_of(upper * plane + first, length), plane - first), :]
                keys = pl.ds(pl.multiple_of(lower * plane + part * length, length), length)
                scores = dot_nt(kx[keys, :], queries)
                if diagonal:
                    key_at = lax.broadcasted_iota(jnp.int32, scores.shape, 0)
                    query_at = lax.broadcasted_iota(jnp.int32, scores.shape, 1)
                    scores = jnp.where(key_at <= query_at, scores, masked_score)
                old_top = stat[upper, head : head + 1, first:]
                top = jnp.maximum(old_top, jnp.max(scores, axis=0, keepdims=True))
                scale = jnp.exp(old_top - top)
                raised = jnp.exp(scores - top)
                stat[upper, head : head + 1, first:] = top
                stat[upper, 4 + head : 5 + head, first:] = stat[
                    upper, 4 + head : 5 + head, first:
                ] * scale + jnp.sum(raised, axis=0, keepdims=True)
                span = slice(head * HD, (head + 1) * HD)
                acc[upper, span, first:] = acc[upper, span, first:] * scale + dot_nn(
                    vt[span, keys], raised.astype(jnp.bfloat16)
                )

    def close_plane(which):
        for head in range(heads):
            span = slice(head * HD, (head + 1) * HD)
            total = stat[which, 4 + head : 5 + head, :]
            acc[which, span, :] = acc[which, span, :] / total
            stat[which, head : head + 1, :] = stat[which, head : head + 1, :] + jnp.log(total)
        for part in range(2):
            chunk = 2 * which + part
            o_send[chunk] = acc[which, :, part * length : (part + 1) * length].T.astype(
                jnp.bfloat16
            )

            @pl.when(chunk != me)
            def _():
                out_copy(chunk, me).start()

            @pl.when(chunk == me)
            def _():
                o_recv[me] = o_send[chunk]

    mine = me // 2

    def stage(step, carry):
        here = lax.rem(mine + step, planes)
        arrive(2 * here)
        arrive(2 * here + 1)
        open_plane(here)

        def earlier(back, inner):
            there = lax.rem(mine + back, planes)
            pair(jnp.maximum(here, there), jnp.minimum(here, there), False)
            return inner

        lax.fori_loop(0, step, earlier, 0)
        pair(here, here, True)

        @pl.when((mine + step >= planes) | (mine == 0))
        def _():
            close_plane(here)

        return carry

    lax.fori_loop(0, planes, stage, 0)

    def finish(which, carry):
        close_plane(which)
        return carry

    lax.fori_loop(jnp.where(mine == 0, planes, mine), planes, finish, 0)

    saves = [
        pltpu.make_async_copy(source, target, out_sem.at[index])
        for index, (source, target) in enumerate(
            (
                (qx, qx_out),
                (kx, kx_out),
                (recv.at[2], v_out),
                (pk, pk_out),
                (pv, pv_out),
                (acc, ot_out),
                (stat, lse_out),
            )
        )
    ]
    for save in saves:
        save.start()
    for other in range(n):

        @pl.when(other != me)
        def _():
            out_copy(other, other).wait_recv()

        att_ref[:, other * group : (other + 1) * group] = o_recv[other]
    for other in range(n):

        @pl.when(other != me)
        def _():
            meta_copy(other, me).wait_send()
            qkv_copy(other, me).wait_send()
            out_copy(other, me).wait_send()

    for save in saves:
        save.wait()


def self_forward(n, segments, padding, tokens, weights, prefix):
    length, width = tokens.shape
    group = width // n
    heads = group // HD
    whole = n * length
    planes = n // 2
    low = jnp.bfloat16
    vmem = pl.BlockSpec(memory_space=pltpu.VMEM)
    anywhere = pl.BlockSpec(memory_space=pl.ANY)
    dma = pltpu.SemaphoreType.DMA((n,))
    return pl.pallas_call(
        functools.partial(self_forward_kernel, n),
        out_shape=(
            jax.ShapeDtypeStruct((length, width), low),
            jax.ShapeDtypeStruct((heads, whole, 2 * LANES), low),
            jax.ShapeDtypeStruct((whole, 2 * LANES), low),
            jax.ShapeDtypeStruct((whole, group), low),
            jax.ShapeDtypeStruct((PREFIX_ROWS, 2 * LANES), low),
            jax.ShapeDtypeStruct((PREFIX_ROWS, group), low),
            jax.ShapeDtypeStruct((planes, group, 2 * length), jnp.float32),
            jax.ShapeDtypeStruct((planes, 8, 2 * length), jnp.float32),
        ),
        in_specs=[vmem] * 11,
        out_specs=(vmem,) + (anywhere,) * 7,
        scratch_shapes=[
            pltpu.VMEM((n, 3, length, group), low),
            pltpu.VMEM((3, whole, group), low),
            pltpu.VMEM((8, length), jnp.int32),
            pltpu.VMEM((n, 8, length), jnp.int32),
            pltpu.VMEM((whole, 2 * LANES), low),
            pltpu.VMEM((heads, whole, 2 * LANES), low),
            pltpu.VMEM((group, whole), low),
            pltpu.VMEM((PREFIX_ROWS, weights[0].shape[0] // 2), jnp.float32),
            pltpu.VMEM((PREFIX_ROWS, 2 * LANES), low),
            pltpu.VMEM((PREFIX_ROWS, group), low),
            pltpu.VMEM((group, PREFIX_ROWS), low),
            pltpu.VMEM((planes, 8, 2 * length), jnp.float32),
            pltpu.VMEM((planes, group, 2 * length), jnp.float32),
            pltpu.VMEM((n, length, group), low),
            pltpu.VMEM((n, length, group), low),
            dma,
            dma,
            dma,
            dma,
            dma,
            dma,
            pltpu.SemaphoreType.DMA((7,)),
        ],
        compiler_params=pltpu.CompilerParams(
            collective_id=0, has_side_effects=True, vmem_limit_bytes=VMEM_BYTES
        ),
        name="self_forward",
    )(segments, padding, tokens, *weights, *prefix)


def self_backward_kernel(
    n,
    do_ref,
    base_ref,
    qx_in,
    kx_in,
    v_in,
    pk_in,
    pv_in,
    ot_in,
    lse_in,
    wq_in,
    wk_in,
    wv_in,
    tg_ref,
    pre_ref,
    do_send,
    do_recv,
    qx,
    kx,
    v,
    kt,
    pk,
    pv,
    ot,
    lse,
    weights,
    dom,
    delta,
    dqt,
    dk,
    dv,
    g_send,
    g_recv,
    do_send_sem,
    do_recv_sem,
    g_send_sem,
    g_recv_sem,
    in_sem,
):
    me = lax.axis_index("seq")
    length, width = do_ref.shape
    group = width // n
    heads = group // HD
    plane = 2 * length
    planes = n // 2
    block = 2 * LANES
    per_block = block // group

    def do_copy(peer, slot):
        return pltpu.make_async_remote_copy(
            src_ref=do_send.at[peer],
            dst_ref=do_recv.at[slot],
            send_sem=do_send_sem.at[peer],
            recv_sem=do_recv_sem.at[slot],
            device_id={"seq": peer},
            device_id_type=MESH,
        )

    def g_copy(peer, slot):
        return pltpu.make_async_remote_copy(
            src_ref=g_send.at[peer],
            dst_ref=g_recv.at[slot],
            send_sem=g_send_sem.at[peer],
            recv_sem=g_recv_sem.at[slot],
            device_id={"seq": peer},
            device_id_type=MESH,
        )

    loads = [
        pltpu.make_async_copy(source, target, in_sem.at[index])
        for index, (source, target) in enumerate(
            (
                (kx_in, kx),
                (pk_in, pk),
                (qx_in, qx),
                (pv_in, pv),
                (v_in, v),
                (ot_in, ot),
                (lse_in, lse),
                (wq_in, weights.at[0]),
                (wk_in, weights.at[1]),
                (wv_in, weights.at[2]),
            )
        )
    ]
    for load in loads:
        load.start()
    for other in range(n):
        do_send[other] = do_ref[:, other * group : (other + 1) * group]
    enter(n, me)
    for other in range(n):

        @pl.when(other != me)
        def _():
            do_copy(other, me).start()

    do_recv[me] = do_send[me]
    for load in loads[:7]:
        load.wait()

    def turn(chunk, carry):
        here = rows_of(chunk, length)
        kt[:, here] = kx[here, :group].astype(jnp.float32).T.astype(jnp.bfloat16)
        return carry

    lax.fori_loop(0, n, turn, 0)
    pkt = pk[:, :group].astype(jnp.float32).T.astype(jnp.bfloat16)
    dk[...] = jnp.zeros_like(dk)
    dv[...] = jnp.zeros_like(dv)
    pre_ref[...] = jnp.zeros_like(pre_ref)

    def arrive(step, carry):
        which = lax.rem(me // 2 + step, planes)
        for part in range(2):
            chunk = 2 * which + part

            @pl.when(chunk != me)
            def _():
                do_copy(chunk, chunk).wait_recv()

            grads = do_recv[chunk].astype(jnp.float32)
            for head in range(heads):
                dom[head, rows_of(chunk, length), :] = jnp.where(
                    head_lanes(grads.shape, head), grads, 0.0
                ).astype(jnp.bfloat16)
            here = slice(part * length, (part + 1) * length)
            both = grads.T * ot[which, :, here]
            for head in range(heads):
                delta[which, head : head + 1, here] = jnp.sum(
                    both[head * HD : (head + 1) * HD], axis=0, keepdims=True
                )
        for head in range(heads):
            span = slice(head * HD, (head + 1) * HD)
            queries = qx[head, rows_of(which, plane), :]
            grads = dom[head, rows_of(which, plane), :]
            weight = jnp.exp(dot_nt(pk[...], queries) - lse[which, head : head + 1, :])
            slope = weight * (dot_nt(pv[...], grads) - delta[which, head : head + 1, :])
            slope = slope.astype(jnp.bfloat16)
            pre_ref[0] += dot_nn(slope, queries[:, :group])
            pre_ref[1] += dot_nn(weight.astype(jnp.bfloat16), grads)
            dqt[which, span, :] = dot_nn(pkt[span, :], slope)
        return carry

    lax.fori_loop(0, planes, arrive, 0)

    def pair(upper, lower, diagonal):
        for part in range(2):
            first = length if diagonal and part == 1 else 0
            keys = pl.ds(pl.multiple_of(lower * plane + part * length, length), length)
            key_sum = None
            for head in range(heads):
                span = slice(head * HD, (head + 1) * HD)
                here = pl.ds(pl.multiple_of(upper * plane + first, length), plane - first)
                queries = qx[head, here, :]
                grads = dom[head, here, :]
                scores = dot_nt(kx[keys, :], queries)
                weight = jnp.exp(scores - lse[upper, head : head + 1, first:])
                if diagonal:
                    key_at = lax.broadcasted_iota(jnp.int32, scores.shape, 0)
                    query_at = lax.broadcasted_iota(jnp.int32, scores.shape, 1)
                    weight = jnp.where(key_at <= query_at, weight, 0.0)
                slope = weight * (dot_nt(v[keys, :], grads) - delta[upper, head : head + 1, first:])
                slope = slope.astype(jnp.bfloat16)
                key_part = dot_nn(slope, qx[head, here, :group])
                value_part = dot_nn(weight.astype(jnp.bfloat16), grads)
                if key_sum is None:
                    key_sum, value_sum = key_part, value_part
                else:
                    key_sum, value_sum = key_sum + key_part, value_sum + value_part
                dqt[upper, span, first:] += dot_nn(kt[span, keys], slope)
            dk[keys, :] += key_sum
            dv[keys, :] += value_sum

    def hand_over(which):
        for part in range(2):
            chunk = 2 * which + part
            here = rows_of(chunk, length)
            g_send[chunk, 0] = (
                (dqt[which, :, part * length : (part + 1) * length] * 0.125)
                .T.astype(jnp.bfloat16)
            )
            g_send[chunk, 1] = dk[here, :].astype(jnp.bfloat16)
            g_send[chunk, 2] = dv[here, :].astype(jnp.bfloat16)

            @pl.when(chunk != me)
            def _():
                g_copy(chunk, me).start()

            @pl.when(chunk == me)
            def _():
                g_recv[me] = g_send[chunk]

    rising = lax.rem(me, 2) == 0

    def stage(step, carry):
        here = jnp.where(rising, step, planes - 1 - step)

        def others(index, inner):
            there = jnp.where(rising, here + 1 + index, index)
            pair(jnp.maximum(here, there), jnp.minimum(here, there), False)
            return inner

        lax.fori_loop(0, planes - 1 - step, others, 0)
        pair(here, here, True)
        hand_over(here)
        return carry

    lax.fori_loop(0, planes, stage, 0)
    for load in loads[7:]:
        load.wait()
    total = base_ref[...]
    for here in range(width // block):
        pieces = []
        for part in range(per_block):
            other = here * per_block + part

            @pl.when(other != me)
            def _():
                g_copy(other, other).wait_recv()

        for which in range(3):
            piece = jnp.concatenate(
                [g_recv[here * per_block + part, which] for part in range(per_block)], axis=1
            )
            pieces.append(
                dot_nt(piece, weights[which, :, here * block : (here + 1) * block])
            )
        total = total + (pieces[0] + pieces[1] + pieces[2])
    tg_ref[...] = total.astype(jnp.bfloat16)
    for other in range(n):

        @pl.when(other != me)
        def _():
            do_copy(other, me).wait_send()
            g_copy(other, me).wait_send()


def self_backward(n, out_grad, first_grad, saved, weights):
    length, width = out_grad.shape
    group = width // n
    heads = group // HD
    whole = n * length
    planes = n // 2
    low = jnp.bfloat16
    vmem = pl.BlockSpec(memory_space=pltpu.VMEM)
    anywhere = pl.BlockSpec(memory_space=pl.ANY)
    dma = pltpu.SemaphoreType.DMA((n,))
    return pl.pallas_call(
        functools.partial(self_backward_kernel, n),
        out_shape=(
            jax.ShapeDtypeStruct((length, width), low),
            jax.ShapeDtypeStruct((2, PREFIX_ROWS, group), jnp.float32),
        ),
        in_specs=[vmem, vmem] + [anywhere] * 10,
        out_specs=(vmem, vmem),
        scratch_shapes=[
            pltpu.VMEM((n, length, group), low),
            pltpu.VMEM((n, length, group), low),
            pltpu.VMEM((heads, whole, 2 * LANES), low),
            pltpu.VMEM((whole, 2 * LANES), low),
            pltpu.VMEM((whole, group), low),
            pltpu.VMEM((group, whole), low),
            pltpu.VMEM((PREFIX_ROWS, 2 * LANES), low),
            pltpu.VMEM((PREFIX_ROWS, group), low),
            pltpu.VMEM((planes, group, 2 * length), jnp.float32),
            pltpu.VMEM((planes, 8, 2 * length), jnp.float32),
            pltpu.VMEM((3, width, width), low),
            pltpu.VMEM((heads, whole, group), low),
            pltpu.VMEM((planes, 8, 2 * length), jnp.float32),
            pltpu.VMEM((planes, group, 2 * length), jnp.float32),
            pltpu.VMEM((whole, group), jnp.float32),
            pltpu.VMEM((whole, group), jnp.float32),
            pltpu.VMEM((n, 3, length, group), low),
            pltpu.VMEM((n, 3, length, group), low),
            dma,
            dma,
            dma,
            dma,
            pltpu.SemaphoreType.DMA((10,)),
        ],
        compiler_params=pltpu.CompilerParams(
            collective_id=1, has_side_effects=True, vmem_limit_bytes=VMEM_BYTES
        ),
        name="self_backward",
    )(out_grad, first_grad, *saved, *weights)


def per_device(
    tokens,
    memory,
    segment_ids,
    padding_mask,
    cotangent,
    prefix_embed,
    prefix_first,
    first_bias,
    prefix_second,
    second_bias,
    adapter_down,
    down_bias,
    adapter_raise,
    raise_bias,
    norm_gain,
    norm_shift,
    self_query,
    self_key,
    self_value,
    self_output,
    cross_query,
    cross_key,
    cross_value,
    cross_output,
    feed_in,
    feed_out,
):
    row_count, length, model_width = tokens.shape
    flat_rows = row_count * length
    n = lax.axis_size("seq")
    whole_memory = lax.all_gather(memory, "seq", axis=1, tiled=True)
    attended, *saved = self_forward(
        n,
        segment_ids,
        padding_mask,
        tokens.reshape(flat_rows, model_width),
        (self_query, self_key, self_value),
        (
            prefix_embed,
            prefix_first,
            first_bias.reshape(1, -1),
            prefix_second,
            second_bias.reshape(1, -1),
        ),
    )
    attended_low = attended.reshape(row_count, length, model_width)
    first_sum = (tokens.astype(jnp.float32) + matmul(attended_low, self_output)).reshape(
        flat_rows, model_width
    )
    first_norm, first_back = jax.vjp(layer_norm, first_sum, norm_gain[0], norm_shift[0])
    first_low = first_norm.astype(jnp.bfloat16)
    cross_queries = (
        matmul(first_low, cross_query).astype(jnp.bfloat16).reshape(row_count, length, H, HD)
    )
    mem_keys = matmul(whole_memory, cross_key).astype(jnp.bfloat16)
    mem_values = matmul(whole_memory, cross_value).astype(jnp.bfloat16)
    mem_len = mem_keys.shape[1]
    cross_scores = 0.125 * jnp.einsum(
        "rqhd,rkhd->rhqk", cross_queries, to_heads(mem_keys), preferred_element_type=jnp.float32
    )
    cross_raised = jnp.exp(cross_scores - jnp.max(cross_scores, -1, keepdims=True))
    cross_weights = cross_raised / jnp.sum(cross_raised, -1, keepdims=True)
    cross_low = cross_weights.astype(jnp.bfloat16)
    crossed_low = (
        jnp.einsum(
            "rhqk,rkhd->rqhd", cross_low, to_heads(mem_values), preferred_element_type=jnp.float32
        )
        .reshape(flat_rows, model_width)
        .astype(jnp.bfloat16)
    )
    second_sum = first_norm + matmul(crossed_low, cross_output)
    second_norm, second_back = jax.vjp(layer_norm, second_sum, norm_gain[1], norm_shift[1])
    second_low = second_norm.astype(jnp.bfloat16)
    feed_pre = matmul(second_low, feed_in)
    feed_act, feed_back = jax.vjp(exact_gelu, feed_pre)
    feed_low = feed_act.astype(jnp.bfloat16)
    down_pre = matmul(second_low, adapter_down) + down_bias
    down_act, down_back = jax.vjp(exact_gelu, down_pre)
    down_low = down_act.astype(jnp.bfloat16)
    third_sum = (
        second_norm
        + matmul(feed_low, feed_out)
        + 4.0 * (matmul(down_low, adapter_raise) + raise_bias)
    )
    third_norm, third_back = jax.vjp(layer_norm, third_sum, norm_gain[2], norm_shift[2])
    layer_output = third_norm.astype(jnp.bfloat16).reshape(row_count, length, model_width)
    third_grad, gain_three, shift_three = third_back(
        cotangent.reshape(flat_rows, model_width).astype(jnp.float32)
    )
    third_low = third_grad.astype(jnp.bfloat16)
    feed_grad = feed_back(matmul_back(third_low, feed_out))[0].astype(jnp.bfloat16)
    raise_low = 4.0 * third_low
    raise_weight_grad = outer_sum(down_low, raise_low)
    raise_bias_grad = jnp.sum(raise_low.astype(jnp.float32), 0)
    down_grad = down_back(matmul_back(raise_low, adapter_raise))[0].astype(jnp.bfloat16)
    down_weight_grad = outer_sum(second_low, down_grad)
    down_bias_grad = jnp.sum(down_grad.astype(jnp.float32), 0)
    second_total = (
        third_grad + matmul_back(feed_grad, feed_in) + matmul_back(down_grad, adapter_down)
    )
    second_grad, gain_two, shift_two = second_back(second_total)
    crossed_grad = (
        matmul_back(second_grad.astype(jnp.bfloat16), cross_output)
        .astype(jnp.bfloat16)
        .reshape(row_count, length, H, HD)
    )
    cross_wgrad = jnp.einsum(
        "rqhd,rkhd->rhqk", crossed_grad, to_heads(mem_values), preferred_element_type=jnp.float32
    )
    cross_sgrad = (
        cross_weights * (cross_wgrad - jnp.sum(cross_weights * cross_wgrad, -1, keepdims=True))
    ).astype(jnp.bfloat16)
    cross_qgrad = (
        (
            0.125
            * jnp.einsum(
                "rhqk,rkhd->rqhd",
                cross_sgrad,
                to_heads(mem_keys),
                preferred_element_type=jnp.float32,
            )
        )
        .astype(jnp.bfloat16)
        .reshape(flat_rows, model_width)
    )
    mem_key_grad = 0.125 * jnp.einsum(
        "rhqk,rqhd->rkhd", cross_sgrad, cross_queries, preferred_element_type=jnp.float32
    )
    mem_value_grad = jnp.einsum(
        "rhqk,rqhd->rkhd", cross_low, crossed_grad, preferred_element_type=jnp.float32
    )
    memory_part = matmul_back(
        mem_key_grad.reshape(row_count, mem_len, model_width).astype(jnp.bfloat16), cross_key
    ) + matmul_back(
        mem_value_grad.reshape(row_count, mem_len, model_width).astype(jnp.bfloat16), cross_value
    )
    memory_grad = lax.psum_scatter(
        memory_part.astype(jnp.bfloat16), "seq", scatter_dimension=1, tiled=True
    )
    first_total = second_grad + matmul_back(cross_qgrad, cross_query)
    first_grad, gain_one, shift_one = first_back(first_total)
    out_grad = matmul_back(first_grad.astype(jnp.bfloat16), self_output).astype(jnp.bfloat16)
    token_grad, prefix_part = self_backward(
        n, out_grad, first_grad, saved, (self_query, self_key, self_value)
    )
    token_grad = token_grad.reshape(row_count, length, model_width)
    prefix_rows = prefix_embed.shape[0]
    group = model_width // n
    here = lax.axis_index("seq") * group
    prefix_grad = jnp.zeros((prefix_rows, 2 * model_width), jnp.float32)
    prefix_grad = lax.dynamic_update_slice(prefix_grad, prefix_part[0, :prefix_rows], (0, here))
    prefix_grad = lax.dynamic_update_slice(
        prefix_grad, prefix_part[1, :prefix_rows], (0, model_width + here)
    )
    prefix_grad = lax.psum(prefix_grad, ("seq", "batch"))
    summed = lax.psum(
        (
            down_weight_grad,
            down_bias_grad,
            raise_weight_grad,
            raise_bias_grad,
            jnp.stack([gain_one, gain_two, gain_three]),
            jnp.stack([shift_one, shift_two, shift_three]),
        ),
        ("seq", "batch"),
    )
    prefix_hidden = jnp.tanh(matmul(prefix_embed, prefix_first) + first_bias)
    hidden_low = prefix_hidden.astype(jnp.bfloat16)
    second_weight_grad = precise_outer(hidden_low.astype(jnp.float32), prefix_grad)
    second_bias_grad = jnp.sum(prefix_grad, 0)
    hidden_grad = precise_back(prefix_grad, prefix_second.astype(jnp.float32)) * (
        1.0 - prefix_hidden * prefix_hidden
    )
    first_weight_grad = precise_outer(prefix_embed.astype(jnp.float32), hidden_grad)
    first_bias_grad = jnp.sum(hidden_grad, 0)
    embed_grad = precise_back(hidden_grad, prefix_first.astype(jnp.float32))
    return (
        layer_output,
        token_grad,
        memory_grad,
        embed_grad,
        first_weight_grad,
        first_bias_grad,
        second_weight_grad,
        second_bias_grad,
        summed[0],
        summed[1],
        summed[2],
        summed[3],
        summed[4],
        summed[5],
    )


def solution(mesh):
    placed = (
        P("batch", "seq", None),
        P("batch", "seq", None),
        P("batch", "seq"),
        P("batch", "seq"),
        P("batch", "seq", None),
        P(),
        P(),
        P(),
        P(),
        P(),
        P(),
        P(),
        P(),
        P(),
        P(),
        P(),
        P(),
        P(),
        P(),
        P(),
        P(),
        P(),
        P(),
        P(),
        P(),
        P(),
    )
    return jax.shard_map(
        per_device,
        mesh=mesh,
        in_specs=placed,
        out_specs=(
            P("batch", "seq", None),
            P("batch", "seq", None),
            P("batch", "seq", None),
            P(),
            P(),
            P(),
            P(),
            P(),
            P(),
            P(),
            P(),
            P(),
            P(),
            P(),
        ),
        check_vma=False,
    )
```

```python
import functools

import jax
import jax.numpy as jnp
from jax import lax
from jax.experimental import pallas as pl
from jax.experimental.pallas import tpu as pltpu
from jax.sharding import PartitionSpec as P

H = 16
HD = 64
LANES = 128
PREFIX_ROWS = 32
VMEM_BYTES = 60 * 1024 * 1024
MESH = pl.DeviceIdType.MESH

masked_score = -1e30
norm_eps = 1e-05

def matmul(left, right):
    return jnp.dot(left, right, preferred_element_type=jnp.float32)


def precise_back(left, right):
    return lax.dot_general(
        left,
        right,
        (((1,), (1,)), ((), ())),
        precision=lax.Precision.HIGHEST,
        preferred_element_type=jnp.float32,
    )


def precise_outer(left, right):
    return lax.dot_general(
        left,
        right,
        (((0,), (0,)), ((), ())),
        precision=lax.Precision.HIGHEST,
        preferred_element_type=jnp.float32,
    )


def dot_nn(left, right):
    return lax.dot_general(
        left, right, (((1,), (0,)), ((), ())), preferred_element_type=jnp.float32
    )


def dot_nt(left, right):
    return lax.dot_general(
        left, right, (((1,), (1,)), ((), ())), preferred_element_type=jnp.float32
    )


def dot_tn(left, right):
    return lax.dot_general(
        left, right, (((0,), (0,)), ((), ())), preferred_element_type=jnp.float32
    )


def enter(n, me):
    barrier = pltpu.get_barrier_semaphore()
    for other in range(n):

        @pl.when(other != me)
        def _():
            pl.semaphore_signal(barrier, inc=1, device_id={"seq": other}, device_id_type=MESH)

    pl.semaphore_wait(barrier, n - 1)


def rows_of(index, size):
    return pl.ds(pl.multiple_of(index * size, size), size)


def own_columns(ref, first, me, width):
    if width % LANES == 0:
        return ref[:, pl.ds(pl.multiple_of(first + me * width, LANES), width)].astype(jnp.float32)
    share = LANES // width
    block = ref[:, pl.ds(pl.multiple_of(first + me // share * LANES, LANES), LANES)].astype(
        jnp.float32
    )
    picked = block[:, :width]
    for part in range(1, share):
        picked = jnp.where(me % share == part, block[:, part * width : (part + 1) * width], picked)
    return picked


def head_lanes(shape, head):
    lane = lax.broadcasted_iota(jnp.int32, shape, 1)
    return (lane >= head * HD) & (lane < (head + 1) * HD)


def self_forward_kernel(
    n,
    seg_ref,
    pad_ref,
    tok_ref,
    wq_ref,
    wk_ref,
    wv_ref,
    emb_ref,
    first_ref,
    fbias_ref,
    second_ref,
    sbias_ref,
    att_ref,
    qx_out,
    kx_out,
    v_out,
    pk_out,
    pv_out,
    ot_out,
    lse_out,
    send,
    recv,
    meta_send,
    meta,
    kx,
    qx,
    vt,
    hidden,
    pk,
    pv,
    pvt,
    stat,
    acc,
    o_send,
    o_recv,
    send_sem,
    recv_sem,
    meta_send_sem,
    meta_recv_sem,
    o_send_sem,
    o_recv_sem,
    out_sem,
):
    me = lax.axis_index("seq")
    length, width = tok_ref.shape
    group = width // n
    heads = group // HD
    plane = 2 * length
    planes = n // 2
    block = 2 * LANES
    per_block = block // group
    blocks = width // block

    def meta_copy(peer, slot):
        return pltpu.make_async_remote_copy(
            src_ref=meta_send,
            dst_ref=meta.at[slot],
            send_sem=meta_send_sem.at[peer],
            recv_sem=meta_recv_sem.at[slot],
            device_id={"seq": peer},
            device_id_type=MESH,
        )

    def qkv_copy(peer, slot):
        return pltpu.make_async_remote_copy(
            src_ref=send.at[peer],
            dst_ref=recv.at[:, rows_of(slot, length), :],
            send_sem=send_sem.at[peer],
            recv_sem=recv_sem.at[slot],
            device_id={"seq": peer},
            device_id_type=MESH,
        )

    def out_copy(peer, slot):
        return pltpu.make_async_remote_copy(
            src_ref=o_send.at[peer],
            dst_ref=o_recv.at[slot],
            send_sem=o_send_sem.at[peer],
            recv_sem=o_recv_sem.at[slot],
            device_id={"seq": peer},
            device_id_type=MESH,
        )

    segments = seg_ref[...]
    tags = jnp.where(pad_ref[...] == 1, segments, -1)
    row = lax.broadcasted_iota(jnp.int32, meta_send.shape, 0)
    meta_send[...] = jnp.where(row == 0, segments, tags)
    enter(n, me)
    for other in range(n):

        @pl.when(other != me)
        def _():
            meta_copy(other, me).start()

    meta[me] = meta_send[...]

    def project(step, carry):
        here = lax.rem(me // per_block + 1 + step, blocks)
        columns = pl.ds(pl.multiple_of(here * block, block), block)
        for which, weight in enumerate((wq_ref, wk_ref, wv_ref)):
            piece = dot_nn(tok_ref[...], weight[:, columns]).astype(jnp.bfloat16)
            for part in range(per_block):
                send[here * per_block + part, which] = piece[:, part * group : (part + 1) * group]
        for part in range(per_block):
            peer = here * per_block + part

            @pl.when(peer != me)
            def _():
                qkv_copy(peer, me).start()

            @pl.when(peer == me)
            def _():
                recv[:, rows_of(me, length), :] = send[peer]

        return carry

    lax.fori_loop(0, blocks, project, 0)

    hidden[...] = jnp.zeros_like(hidden)
    hidden[: emb_ref.shape[0], :] = jnp.tanh(dot_nn(emb_ref[...], first_ref[...]) + fbias_ref[...])
    hidden_low = hidden[...].astype(jnp.bfloat16)
    prefix_key = dot_nn(
        hidden_low, own_columns(second_ref, 0, me, group).astype(jnp.bfloat16)
    ) + own_columns(sbias_ref, 0, me, group)
    prefix_value = dot_nn(
        hidden_low, own_columns(second_ref, width, me, group).astype(jnp.bfloat16)
    ) + own_columns(sbias_ref, width, me, group)
    pk[...] = jnp.zeros_like(pk)
    pk[:, :group] = prefix_key.astype(jnp.bfloat16)
    prefix_row = lax.broadcasted_iota(jnp.int32, (pk.shape[0], LANES), 0)
    pk[:, LANES:] = jnp.where(prefix_row < emb_ref.shape[0], 0.0, masked_score).astype(
        jnp.bfloat16
    )
    pv[...] = prefix_value.astype(jnp.bfloat16)
    pvt[...] = prefix_value.T.astype(jnp.bfloat16)

    def arrive(chunk):
        @pl.when(chunk != me)
        def _():
            meta_copy(chunk, chunk).wait_recv()
            qkv_copy(chunk, chunk).wait_recv()

        here = rows_of(chunk, length)
        state = lax.broadcasted_iota(jnp.int32, (LANES, length), 0)
        is_segment = jnp.where(state == meta[chunk, 0:1, :], 1.0, 0.0)
        is_open = jnp.where(state == meta[chunk, 1:2, :], 0.0, masked_score)
        query_state = is_segment.T.astype(jnp.bfloat16)
        kx[here, :group] = recv[1, here, :]
        kx[here, LANES:] = is_open.T.astype(jnp.bfloat16)
        if group < LANES:
            kx[here, group:LANES] = jnp.zeros((length, LANES - group), jnp.bfloat16)
        query = recv[0, here, :].astype(jnp.float32) * 0.125
        for head in range(heads):
            qx[head, here, :group] = jnp.where(
                head_lanes(query.shape, head), query, 0.0
            ).astype(jnp.bfloat16)
            qx[head, here, LANES:] = query_state
            if group < LANES:
                qx[head, here, group:LANES] = jnp.zeros((length, LANES - group), jnp.bfloat16)
        vt[:, here] = recv[2, here, :].astype(jnp.float32).T.astype(jnp.bfloat16)

    def open_plane(which):
        for head in range(heads):
            scores = dot_nt(pk[...], qx[head, rows_of(which, plane), :])
            top = jnp.max(scores, axis=0, keepdims=True)
            raised = jnp.exp(scores - top)
            stat[which, head : head + 1, :] = top
            stat[which, 4 + head : 5 + head, :] = jnp.sum(raised, axis=0, keepdims=True)
            span = slice(head * HD, (head + 1) * HD)
            acc[which, span, :] = dot_nn(pvt[span, :], raised.astype(jnp.bfloat16))

    def pair(upper, lower, diagonal):
        for part in range(2):
            first = length if diagonal and part == 1 else 0
            for head in range(heads):
                queries = qx[head, pl.ds(pl.multiple_of(upper * plane + first, length), plane - first), :]
                keys = pl.ds(pl.multiple_of(lower * plane + part * length, length), length)
                scores = dot_nt(kx[keys, :], queries)
                if diagonal:
                    key_at = lax.broadcasted_iota(jnp.int32, scores.shape, 0)
                    query_at = lax.broadcasted_iota(jnp.int32, scores.shape, 1)
                    scores = jnp.where(key_at <= query_at, scores, masked_score)
                old_top = stat[upper, head : head + 1, first:]
                top = jnp.maximum(old_top, jnp.max(scores, axis=0, keepdims=True))
                scale = jnp.exp(old_top - top)
                raised = jnp.exp(scores - top)
                stat[upper, head : head + 1, first:] = top
                stat[upper, 4 + head : 5 + head, first:] = stat[
                    upper, 4 + head : 5 + head, first:
                ] * scale + jnp.sum(raised, axis=0, keepdims=True)
                span = slice(head * HD, (head + 1) * HD)
                acc[upper, span, first:] = acc[upper, span, first:] * scale + dot_nn(
                    vt[span, keys], raised.astype(jnp.bfloat16)
                )

    def close_plane(which):
        for head in range(heads):
            span = slice(head * HD, (head + 1) * HD)
            total = stat[which, 4 + head : 5 + head, :]
            acc[which, span, :] = acc[which, span, :] / total
            stat[which, head : head + 1, :] = stat[which, head : head + 1, :] + jnp.log(total)
        for part in range(2):
            chunk = 2 * which + part
            o_send[chunk] = acc[which, :, part * length : (part + 1) * length].T.astype(
                jnp.bfloat16
            )

            @pl.when(chunk != me)
            def _():
                out_copy(chunk, me).start()

            @pl.when(chunk == me)
            def _():
                o_recv[me] = o_send[chunk]

    mine = me // 2

    def stage(step, carry):
        here = lax.rem(mine + step, planes)
        arrive(2 * here)
        arrive(2 * here + 1)
        open_plane(here)

        def earlier(back, inner):
            there = lax.rem(mine + back, planes)
            pair(jnp.maximum(here, there), jnp.minimum(here, there), False)
            return inner

        lax.fori_loop(0, step, earlier, 0)
        pair(here, here, True)

        @pl.when((mine + step >= planes) | (mine == 0))
        def _():
            close_plane(here)

        return carry

    lax.fori_loop(0, planes, stage, 0)

    def finish(which, carry):
        close_plane(which)
        return carry

    lax.fori_loop(jnp.where(mine == 0, planes, mine), planes, finish, 0)

    saves = [
        pltpu.make_async_copy(source, target, out_sem.at[index])
        for index, (source, target) in enumerate(
            (
                (qx, qx_out),
                (kx, kx_out),
                (recv.at[2], v_out),
                (pk, pk_out),
                (pv, pv_out),
                (acc, ot_out),
                (stat, lse_out),
            )
        )
    ]
    for save in saves:
        save.start()
    for other in range(n):

        @pl.when(other != me)
        def _():
            out_copy(other, other).wait_recv()

        att_ref[:, other * group : (other + 1) * group] = o_recv[other]
    for other in range(n):

        @pl.when(other != me)
        def _():
            meta_copy(other, me).wait_send()
            qkv_copy(other, me).wait_send()
            out_copy(other, me).wait_send()

    for save in saves:
        save.wait()


def self_forward(n, segments, padding, tokens, weights, prefix):
    length, width = tokens.shape
    group = width // n
    heads = group // HD
    whole = n * length
    planes = n // 2
    low = jnp.bfloat16
    vmem = pl.BlockSpec(memory_space=pltpu.VMEM)
    anywhere = pl.BlockSpec(memory_space=pl.ANY)
    dma = pltpu.SemaphoreType.DMA((n,))
    return pl.pallas_call(
        functools.partial(self_forward_kernel, n),
        out_shape=(
            jax.ShapeDtypeStruct((length, width), low),
            jax.ShapeDtypeStruct((heads, whole, 2 * LANES), low),
            jax.ShapeDtypeStruct((whole, 2 * LANES), low),
            jax.ShapeDtypeStruct((whole, group), low),
            jax.ShapeDtypeStruct((PREFIX_ROWS, 2 * LANES), low),
            jax.ShapeDtypeStruct((PREFIX_ROWS, group), low),
            jax.ShapeDtypeStruct((planes, group, 2 * length), jnp.float32),
            jax.ShapeDtypeStruct((planes, 8, 2 * length), jnp.float32),
        ),
        in_specs=[vmem] * 11,
        out_specs=(vmem,) + (anywhere,) * 7,
        scratch_shapes=[
            pltpu.VMEM((n, 3, length, group), low),
            pltpu.VMEM((3, whole, group), low),
            pltpu.VMEM((8, length), jnp.int32),
            pltpu.VMEM((n, 8, length), jnp.int32),
            pltpu.VMEM((whole, 2 * LANES), low),
            pltpu.VMEM((heads, whole, 2 * LANES), low),
            pltpu.VMEM((group, whole), low),
            pltpu.VMEM((PREFIX_ROWS, weights[0].shape[0] // 2), jnp.float32),
            pltpu.VMEM((PREFIX_ROWS, 2 * LANES), low),
            pltpu.VMEM((PREFIX_ROWS, group), low),
            pltpu.VMEM((group, PREFIX_ROWS), low),
            pltpu.VMEM((planes, 8, 2 * length), jnp.float32),
            pltpu.VMEM((planes, group, 2 * length), jnp.float32),
            pltpu.VMEM((n, length, group), low),
            pltpu.VMEM((n, length, group), low),
            dma,
            dma,
            dma,
            dma,
            dma,
            dma,
            pltpu.SemaphoreType.DMA((7,)),
        ],
        compiler_params=pltpu.CompilerParams(
            collective_id=0, has_side_effects=True, vmem_limit_bytes=VMEM_BYTES
        ),
        name="self_forward",
    )(segments, padding, tokens, *weights, *prefix)


def self_backward_kernel(
    n,
    do_ref,
    base_ref,
    qx_in,
    kx_in,
    v_in,
    pk_in,
    pv_in,
    ot_in,
    lse_in,
    wq_in,
    wk_in,
    wv_in,
    tg_ref,
    pre_ref,
    do_send,
    do_recv,
    qx,
    kx,
    v,
    kt,
    pk,
    pv,
    ot,
    lse,
    weights,
    dom,
    delta,
    dqt,
    dk,
    dv,
    g_send,
    g_recv,
    do_send_sem,
    do_recv_sem,
    g_send_sem,
    g_recv_sem,
    in_sem,
):
    me = lax.axis_index("seq")
    length, width = do_ref.shape
    group = width // n
    heads = group // HD
    plane = 2 * length
    planes = n // 2
    block = 2 * LANES
    per_block = block // group

    def do_copy(peer, slot):
        return pltpu.make_async_remote_copy(
            src_ref=do_send.at[peer],
            dst_ref=do_recv.at[slot],
            send_sem=do_send_sem.at[peer],
            recv_sem=do_recv_sem.at[slot],
            device_id={"seq": peer},
            device_id_type=MESH,
        )

    def g_copy(peer, slot):
        return pltpu.make_async_remote_copy(
            src_ref=g_send.at[peer],
            dst_ref=g_recv.at[slot],
            send_sem=g_send_sem.at[peer],
            recv_sem=g_recv_sem.at[slot],
            device_id={"seq": peer},
            device_id_type=MESH,
        )

    loads = [
        pltpu.make_async_copy(source, target, in_sem.at[index])
        for index, (source, target) in enumerate(
            (
                (kx_in, kx),
                (pk_in, pk),
                (qx_in, qx),
                (pv_in, pv),
                (v_in, v),
                (ot_in, ot),
                (lse_in, lse),
                (wq_in, weights.at[0]),
                (wk_in, weights.at[1]),
                (wv_in, weights.at[2]),
            )
        )
    ]
    for load in loads:
        load.start()
    for other in range(n):
        do_send[other] = do_ref[:, other * group : (other + 1) * group]
    enter(n, me)
    for other in range(n):

        @pl.when(other != me)
        def _():
            do_copy(other, me).start()

    do_recv[me] = do_send[me]
    for load in loads[:7]:
        load.wait()

    def turn(chunk, carry):
        here = rows_of(chunk, length)
        kt[:, here] = kx[here, :group].astype(jnp.float32).T.astype(jnp.bfloat16)
        return carry

    lax.fori_loop(0, n, turn, 0)
    pkt = pk[:, :group].astype(jnp.float32).T.astype(jnp.bfloat16)
    dk[...] = jnp.zeros_like(dk)
    dv[...] = jnp.zeros_like(dv)
    pre_ref[...] = jnp.zeros_like(pre_ref)

    def arrive(step, carry):
        which = lax.rem(me // 2 + step, planes)
        for part in range(2):
            chunk = 2 * which + part

            @pl.when(chunk != me)
            def _():
                do_copy(chunk, chunk).wait_recv()

            grads = do_recv[chunk].astype(jnp.float32)
            for head in range(heads):
                dom[head, rows_of(chunk, length), :] = jnp.where(
                    head_lanes(grads.shape, head), grads, 0.0
                ).astype(jnp.bfloat16)
            here = slice(part * length, (part + 1) * length)
            both = grads.T * ot[which, :, here]
            for head in range(heads):
                delta[which, head : head + 1, here] = jnp.sum(
                    both[head * HD : (head + 1) * HD], axis=0, keepdims=True
                )
        for head in range(heads):
            span = slice(head * HD, (head + 1) * HD)
            queries = qx[head, rows_of(which, plane), :]
            grads = dom[head, rows_of(which, plane), :]
            weight = jnp.exp(dot_nt(pk[...], queries) - lse[which, head : head + 1, :])
            slope = weight * (dot_nt(pv[...], grads) - delta[which, head : head + 1, :])
            slope = slope.astype(jnp.bfloat16)
            pre_ref[0] += dot_nn(slope, queries[:, :group])
            pre_ref[1] += dot_nn(weight.astype(jnp.bfloat16), grads)
            dqt[which, span, :] = dot_nn(pkt[span, :], slope)
        return carry

    lax.fori_loop(0, planes, arrive, 0)

    def pair(upper, lower, diagonal):
        for part in range(2):
            first = length if diagonal and part == 1 else 0
            keys = pl.ds(pl.multiple_of(lower * plane + part * length, length), length)
            key_sum = None
            for head in range(heads):
                span = slice(head * HD, (head + 1) * HD)
                here = pl.ds(pl.multiple_of(upper * plane + first, length), plane - first)
                queries = qx[head, here, :]
                grads = dom[head, here, :]
                scores = dot_nt(kx[keys, :], queries)
                weight = jnp.exp(scores - lse[upper, head : head + 1, first:])
                if diagonal:
                    key_at = lax.broadcasted_iota(jnp.int32, scores.shape, 0)
                    query_at = lax.broadcasted_iota(jnp.int32, scores.shape, 1)
                    weight = jnp.where(key_at <= query_at, weight, 0.0)
                slope = weight * (dot_nt(v[keys, :], grads) - delta[upper, head : head + 1, first:])
                slope = slope.astype(jnp.bfloat16)
                key_part = dot_nn(slope, qx[head, here, :group])
                value_part = dot_nn(weight.astype(jnp.bfloat16), grads)
                if key_sum is None:
                    key_sum, value_sum = key_part, value_part
                else:
                    key_sum, value_sum = key_sum + key_part, value_sum + value_part
                dqt[upper, span, first:] += dot_nn(kt[span, keys], slope)
            dk[keys, :] += key_sum
            dv[keys, :] += value_sum

    def hand_over(which):
        for part in range(2):
            chunk = 2 * which + part
            here = rows_of(chunk, length)
            g_send[chunk, 0] = (
                (dqt[which, :, part * length : (part + 1) * length] * 0.125)
                .T.astype(jnp.bfloat16)
            )
            g_send[chunk, 1] = dk[here, :].astype(jnp.bfloat16)
            g_send[chunk, 2] = dv[here, :].astype(jnp.bfloat16)

            @pl.when(chunk != me)
            def _():
                g_copy(chunk, me).start()

            @pl.when(chunk == me)
            def _():
                g_recv[me] = g_send[chunk]

    rising = lax.rem(me, 2) == 0

    def stage(step, carry):
        here = jnp.where(rising, step, planes - 1 - step)

        def others(index, inner):
            there = jnp.where(rising, here + 1 + index, index)
            pair(jnp.maximum(here, there), jnp.minimum(here, there), False)
            return inner

        lax.fori_loop(0, planes - 1 - step, others, 0)
        pair(here, here, True)
        hand_over(here)
        return carry

    lax.fori_loop(0, planes, stage, 0)
    for load in loads[7:]:
        load.wait()
    total = base_ref[...]
    for here in range(width // block):
        pieces = []
        for part in range(per_block):
            other = here * per_block + part

            @pl.when(other != me)
            def _():
                g_copy(other, other).wait_recv()

        for which in range(3):
            piece = jnp.concatenate(
                [g_recv[here * per_block + part, which] for part in range(per_block)], axis=1
            )
            pieces.append(
                dot_nt(piece, weights[which, :, here * block : (here + 1) * block])
            )
        total = total + (pieces[0] + pieces[1] + pieces[2])
    tg_ref[...] = total.astype(jnp.bfloat16)
    for other in range(n):

        @pl.when(other != me)
        def _():
            do_copy(other, me).wait_send()
            g_copy(other, me).wait_send()


def self_backward(n, out_grad, first_grad, saved, weights):
    length, width = out_grad.shape
    group = width // n
    heads = group // HD
    whole = n * length
    planes = n // 2
    low = jnp.bfloat16
    vmem = pl.BlockSpec(memory_space=pltpu.VMEM)
    anywhere = pl.BlockSpec(memory_space=pl.ANY)
    dma = pltpu.SemaphoreType.DMA((n,))
    return pl.pallas_call(
        functools.partial(self_backward_kernel, n),
        out_shape=(
            jax.ShapeDtypeStruct((length, width), low),
            jax.ShapeDtypeStruct((2, PREFIX_ROWS, group), jnp.float32),
        ),
        in_specs=[vmem, vmem] + [anywhere] * 10,
        out_specs=(vmem, vmem),
        scratch_shapes=[
            pltpu.VMEM((n, length, group), low),
            pltpu.VMEM((n, length, group), low),
            pltpu.VMEM((heads, whole, 2 * LANES), low),
            pltpu.VMEM((whole, 2 * LANES), low),
            pltpu.VMEM((whole, group), low),
            pltpu.VMEM((group, whole), low),
            pltpu.VMEM((PREFIX_ROWS, 2 * LANES), low),
            pltpu.VMEM((PREFIX_ROWS, group), low),
            pltpu.VMEM((planes, group, 2 * length), jnp.float32),
            pltpu.VMEM((planes, 8, 2 * length), jnp.float32),
            pltpu.VMEM((3, width, width), low),
            pltpu.VMEM((heads, whole, group), low),
            pltpu.VMEM((planes, 8, 2 * length), jnp.float32),
            pltpu.VMEM((planes, group, 2 * length), jnp.float32),
            pltpu.VMEM((whole, group), jnp.float32),
            pltpu.VMEM((whole, group), jnp.float32),
            pltpu.VMEM((n, 3, length, group), low),
            pltpu.VMEM((n, 3, length, group), low),
            dma,
            dma,
            dma,
            dma,
            pltpu.SemaphoreType.DMA((10,)),
        ],
        compiler_params=pltpu.CompilerParams(
            collective_id=1, has_side_effects=True, vmem_limit_bytes=VMEM_BYTES
        ),
        name="self_backward",
    )(out_grad, first_grad, *saved, *weights)


def gelu_pair(value):
    scaled = jnp.abs(value) * 0.7071067811865476
    step = 1.0 / (1.0 + 0.3275911 * scaled)
    bell = jnp.exp(-scaled * scaled)
    poly = step * (
        0.254829592
        + step
        * (-0.284496736 + step * (1.421413741 + step * (-1.453152027 + step * 1.061405429)))
    )
    tail = 0.5 * poly * bell
    share = jnp.where(value >= 0.0, 1.0 - tail, tail)
    return value * share, share + value * (bell * 0.3989422804014327)


def normed(value):
    center = jnp.mean(value, axis=-1, keepdims=True)
    centered = value - center
    scale = lax.rsqrt(jnp.mean(centered * centered, axis=-1, keepdims=True) + norm_eps)
    return centered * scale, scale


def norm_back(grad, scale, unit):
    return scale * (
        grad
        - jnp.mean(grad, axis=-1, keepdims=True)
        - unit * jnp.mean(grad * unit, axis=-1, keepdims=True)
    )


def middle_kernel(
    tok_ref,
    att_ref,
    cot_ref,
    mem_ref,
    gain_ref,
    shift_ref,
    dbias_ref,
    rbias_ref,
    wo_in,
    wcq_in,
    wck_in,
    wcv_in,
    wco_in,
    wd_in,
    wr_in,
    win_in,
    wout_in,
    out_ref,
    fgrad_ref,
    ograd_ref,
    mpart_ref,
    sums_ref,
    vecs_ref,
    wo,
    wcq,
    wck,
    wcv,
    wco,
    wd,
    wr,
    win,
    wout,
    unit_one,
    unit_two,
    work,
    total,
    scale_one,
    scale_two,
    low_one,
    low_two,
    low_three,
    query,
    crossed,
    mem_key,
    mem_value,
    weights,
    slopes,
    down_act,
    down_slope,
    down_grad,
    load_sem,
    win_sem,
    wout_sem,
):
    length, width = tok_ref.shape
    mem_len = mem_ref.shape[0]
    tile = win.shape[2]
    tiles = win_in.shape[1] // tile
    rows_step = 128
    low = jnp.bfloat16
    f32 = jnp.float32

    sources = (wo_in, wcq_in, wck_in, wcv_in, wco_in, wd_in, wr_in)
    targets = (wo, wcq, wck, wcv, wco, wd, wr)
    loads = [
        pltpu.make_async_copy(source, target, load_sem.at[index])
        for index, (source, target) in enumerate(zip(sources, targets))
    ]

    def win_load(which):
        slot = lax.rem(which, 2)
        return pltpu.make_async_copy(
            win_in.at[:, rows_of(which, tile)], win.at[slot], win_sem.at[slot]
        )

    def wout_load(which):
        slot = lax.rem(which, 2)
        return pltpu.make_async_copy(
            wout_in.at[rows_of(which, tile), :], wout.at[slot], wout_sem.at[slot]
        )

    for load in loads[:5]:
        load.start()
    for which in range(2):
        win_load(which).start()
        wout_load(which).start()
    for load in loads[5:]:
        load.start()

    def by_columns(extent, step, body):
        def one(index, carry):
            body(pl.ds(pl.multiple_of(index * step, step), step))
            return carry

        lax.fori_loop(0, extent // step, one, 0)

    def by_rows(body, init=0):
        def one(index, carry):
            return body(rows_of(index, rows_step), carry)

        return lax.fori_loop(0, length // rows_step, one, init)

    cols = 512
    half = width // 2

    loads[0].wait()

    def project_out(here):
        work[:, here] = tok_ref[:, here].astype(f32) + dot_nn(att_ref[...], wo[:, here])

    by_columns(width, cols, project_out)

    def first_norm(here, carry):
        unit, scale = normed(work[here, :])
        unit_one[here, :] = unit
        scale_one[here, :] = scale
        value = unit * gain_ref[0:1, :] + shift_ref[0:1, :]
        work[here, :] = value
        low_one[here, :] = value.astype(low)
        return carry

    by_rows(first_norm)

    loads[1].wait()

    def project_query(here):
        query[:, here] = dot_nn(low_one[...], wcq[:, here]).astype(low)

    by_columns(width, cols, project_query)
    loads[2].wait()
    loads[3].wait()

    def project_memory(here):
        mem_key[:, here] = dot_nn(mem_ref[...], wck[:, here]).astype(low)
        mem_value[:, here] = dot_nn(mem_ref[...], wcv[:, here]).astype(low)

    by_columns(width, cols, project_memory)

    per_block = LANES // HD

    def head_queries(here, head):
        both = query[:, here].astype(f32) * 0.125
        return jnp.where(head_lanes(both.shape, head), both, 0.0).astype(low)

    def cross_forward(block, carry):
        here = rows_of(block, LANES)
        keys = mem_key[:, here]
        values = mem_value[:, here].astype(f32).T.astype(low)
        outs = []
        for head in range(per_block):
            scores = dot_nt(keys, head_queries(here, head))
            raised = jnp.exp(scores - jnp.max(scores, axis=0, keepdims=True))
            share = 1.0 / jnp.sum(raised, axis=0, keepdims=True)
            weight = (raised * share).astype(low)
            weights[block * per_block + head] = weight
            outs.append(dot_nn(values[head * HD : (head + 1) * HD, :], weight))
        crossed[:, here] = jnp.concatenate(outs, axis=0).T.astype(low)
        return carry

    lax.fori_loop(0, width // LANES, cross_forward, 0)

    loads[4].wait()

    def project_crossed(here):
        work[:, here] += dot_nn(crossed[...], wco[:, here])

    by_columns(width, cols, project_crossed)

    def second_norm(here, carry):
        unit, scale = normed(work[here, :])
        unit_two[here, :] = unit
        scale_two[here, :] = scale
        value = unit * gain_ref[1:2, :] + shift_ref[1:2, :]
        work[here, :] = value
        low_two[here, :] = value.astype(low)
        return carry

    by_rows(second_norm)

    total[...] = jnp.zeros_like(total)

    def feed_forward(which, carry):
        slot = lax.rem(which, 2)
        win_load(which).wait()
        pre = dot_nn(low_two[...], win[slot])
        act, slope = gelu_pair(pre)
        slopes[:, rows_of(which, tile)] = slope.astype(low)
        wout_load(which).wait()
        total[...] += dot_nn(act.astype(low), wout[slot])

        @pl.when(which + 2 < tiles)
        def _():
            win_load(which + 2).start()
            wout_load(which + 2).start()

        return carry

    lax.fori_loop(0, tiles, feed_forward, 0)
    loads[5].wait()
    loads[6].wait()
    act, slope = gelu_pair(dot_nn(low_two[...], wd[...]) + dbias_ref[...])
    down_act[...] = act.astype(low)
    down_slope[...] = slope.astype(low)

    def project_raise(here):
        work[:, here] += total[:, here] + 4.0 * (
            dot_nn(down_act[...], wr[:, here]) + rbias_ref[:, here]
        )

    by_columns(width, cols, project_raise)
    nothing = jnp.zeros((1, width), f32)

    def third_norm(here, carry):
        gain_sum, shift_sum, bias_sum = carry
        unit, scale = normed(work[here, :])
        gain = gain_ref[2:3, :]
        out_ref[here, :] = (unit * gain + shift_ref[2:3, :]).astype(low)
        grad = cot_ref[here, :].astype(f32)
        back = norm_back(grad * gain, scale, unit)
        total[here, :] = back
        back_low = back.astype(low)
        low_three[here, :] = back_low
        return (
            gain_sum + jnp.sum(grad * unit, axis=0, keepdims=True),
            shift_sum + jnp.sum(grad, axis=0, keepdims=True),
            bias_sum + jnp.sum(back_low.astype(f32), axis=0, keepdims=True),
        )

    gain_three, shift_three, bias_sum = by_rows(third_norm, (nothing, nothing, nothing))
    vecs_ref[0:1, :] = 4.0 * bias_sum

    back = 4.0 * dot_nt(low_three[...], wr[...]) * down_slope[...].astype(f32)
    back_low = back.astype(low)
    down_grad[...] = back_low
    vecs_ref[1:2, :] = jnp.concatenate(
        [
            jnp.sum(back_low.astype(f32), axis=0, keepdims=True),
            jnp.zeros((1, width - wd.shape[1]), f32),
        ],
        axis=1,
    )
    down = wd.shape[1]
    raise_sum = 4.0 * dot_tn(down_act[...], low_three[...])
    for index in range(width // LANES):
        sums_ref[pl.ds(down * width // LANES + index * down, down), :] = raise_sum[
            :, index * LANES : (index + 1) * LANES
        ].astype(low)
    down_sum = dot_tn(low_two[...], down_grad[...])
    for index in range(down // LANES):
        sums_ref[index * width : (index + 1) * width, :] = down_sum[
            :, index * LANES : (index + 1) * LANES
        ].astype(low)

    def feed_backward(step, carry):
        which = tiles - 1 - step
        slot = lax.rem(which, 2)
        here = rows_of(which, tile)

        @pl.when(which < tiles - 2)
        def _():
            wout_load(which).wait()
            win_load(which).wait()

        grad = dot_nt(low_three[...], wout[slot]) * slopes[:, here].astype(f32)
        total[...] += dot_nt(grad.astype(low), win[slot])

        @pl.when(which >= 2)
        def _():
            win_load(which - 2).start()
            wout_load(which - 2).start()

        return carry

    lax.fori_loop(0, tiles, feed_backward, 0)

    def down_back(here):
        total[:, here] += dot_nt(down_grad[...], wd[here, :])

    by_columns(width, cols, down_back)

    def second_back(here, carry):
        gain_sum, shift_sum = carry
        grad = total[here, :]
        unit = unit_two[here, :]
        back = norm_back(grad * gain_ref[1:2, :], scale_two[here, :], unit)
        total[here, :] = back
        low_one[here, :] = back.astype(low)
        return (
            gain_sum + jnp.sum(grad * unit, axis=0, keepdims=True),
            shift_sum + jnp.sum(grad, axis=0, keepdims=True),
        )

    gain_two, shift_two = by_rows(second_back, (nothing, nothing))

    def crossed_back(here):
        crossed[:, here] = dot_nt(low_one[...], wco[here, :]).astype(low)

    by_columns(width, cols, crossed_back)

    def cross_backward(block, carry):
        here = rows_of(block, LANES)
        values = mem_value[:, here]
        keys = mem_key[:, here].astype(f32).T.astype(low)
        grads = crossed[:, here].astype(f32)
        outs = []
        key_sum = None
        for head in range(per_block):
            grad = jnp.where(head_lanes(grads.shape, head), grads, 0.0).astype(low)
            weight_low = weights[block * per_block + head]
            weight = weight_low.astype(f32)
            slope = dot_nt(values, grad)
            slope = weight * (slope - jnp.sum(weight * slope, axis=0, keepdims=True))
            slope = slope.astype(low)
            key_part = dot_nn(slope, head_queries(here, head))
            value_part = dot_nn(weight_low, grad)
            if key_sum is None:
                key_sum, value_sum = key_part, value_part
            else:
                key_sum, value_sum = key_sum + key_part, value_sum + value_part
            outs.append(dot_nn(keys[head * HD : (head + 1) * HD, :], slope))
        mem_key[:, here] = key_sum.astype(low)
        mem_value[:, here] = value_sum.astype(low)
        query[:, here] = (jnp.concatenate(outs, axis=0) * 0.125).T.astype(low)
        return carry

    lax.fori_loop(0, width // LANES, cross_backward, 0)

    def memory_back(here):
        mpart_ref[:, here] = (
            dot_nt(mem_key[...], wck[here, :]) + dot_nt(mem_value[...], wcv[here, :])
        ).astype(low)

    by_columns(width, cols, memory_back)

    def query_back(here):
        total[:, here] += dot_nt(query[...], wcq[here, :])

    by_columns(width, cols, query_back)

    def first_back(here, carry):
        gain_sum, shift_sum = carry
        grad = total[here, :]
        unit = unit_one[here, :]
        back = norm_back(grad * gain_ref[0:1, :], scale_one[here, :], unit)
        fgrad_ref[here, :] = back
        low_one[here, :] = back.astype(low)
        return (
            gain_sum + jnp.sum(grad * unit, axis=0, keepdims=True),
            shift_sum + jnp.sum(grad, axis=0, keepdims=True),
        )

    gain_one, shift_one = by_rows(first_back, (nothing, nothing))

    def out_back(here):
        ograd_ref[:, here] = dot_nt(low_one[...], wo[here, :]).astype(low)

    by_columns(width, cols, out_back)
    for index, vector in enumerate(
        (gain_one, gain_two, gain_three, shift_one, shift_two, shift_three)
    ):
        vecs_ref[2 + index : 3 + index, :] = vector


def middle(tokens, attended, cotangent, memory, gains, shifts, down_bias, raise_bias, weights):
    length, width = tokens.shape
    mem_len = memory.shape[0]
    down = weights[5].shape[1]
    feed = weights[7].shape[1]
    tile = 512
    low = jnp.bfloat16
    f32 = jnp.float32
    vmem = pl.BlockSpec(memory_space=pltpu.VMEM)
    anywhere = pl.BlockSpec(memory_space=pl.ANY)
    square = pltpu.VMEM((width, width), low)
    wide = pltpu.VMEM((length, width), f32)
    narrow = pltpu.VMEM((length, width), low)
    mem_low = pltpu.VMEM((mem_len, width), low)
    return pl.pallas_call(
        middle_kernel,
        out_shape=(
            jax.ShapeDtypeStruct((length, width), low),
            jax.ShapeDtypeStruct((length, width), f32),
            jax.ShapeDtypeStruct((length, width), low),
            jax.ShapeDtypeStruct((mem_len, width), low),
            jax.ShapeDtypeStruct((2 * down * width // LANES, LANES), low),
            jax.ShapeDtypeStruct((8, width), f32),
        ),
        in_specs=[vmem] * 8 + [anywhere] * 9,
        out_specs=(vmem,) * 6,
        scratch_shapes=[
            square,
            square,
            square,
            square,
            square,
            pltpu.VMEM((width, down), low),
            pltpu.VMEM((down, width), low),
            pltpu.VMEM((2, width, tile), low),
            pltpu.VMEM((2, tile, width), low),
            wide,
            wide,
            wide,
            wide,
            pltpu.VMEM((length, 1), f32),
            pltpu.VMEM((length, 1), f32),
            narrow,
            narrow,
            narrow,
            narrow,
            narrow,
            mem_low,
            mem_low,
            pltpu.VMEM((H, mem_len, length), low),
            pltpu.VMEM((length, feed), low),
            pltpu.VMEM((length, down), low),
            pltpu.VMEM((length, down), low),
            pltpu.VMEM((length, down), low),
            pltpu.SemaphoreType.DMA((7,)),
            pltpu.SemaphoreType.DMA((2,)),
            pltpu.SemaphoreType.DMA((2,)),
        ],
        compiler_params=pltpu.CompilerParams(vmem_limit_bytes=VMEM_BYTES + (0 if mem_len <= 512 else 2 * 1024 * 1024)),
        name="middle",
    )(tokens, attended, cotangent, memory, gains, shifts, down_bias, raise_bias, *weights)


def per_device(
    tokens,
    memory,
    segment_ids,
    padding_mask,
    cotangent,
    prefix_embed,
    prefix_first,
    first_bias,
    prefix_second,
    second_bias,
    adapter_down,
    down_bias,
    adapter_raise,
    raise_bias,
    norm_gain,
    norm_shift,
    self_query,
    self_key,
    self_value,
    self_output,
    cross_query,
    cross_key,
    cross_value,
    cross_output,
    feed_in,
    feed_out,
):
    row_count, length, model_width = tokens.shape
    flat_rows = row_count * length
    n = lax.axis_size("seq")
    whole_memory = lax.all_gather(memory, "seq", axis=1, tiled=True)
    attended, *saved = self_forward(
        n,
        segment_ids,
        padding_mask,
        tokens.reshape(flat_rows, model_width),
        (self_query, self_key, self_value),
        (
            prefix_embed,
            prefix_first,
            first_bias.reshape(1, -1),
            prefix_second,
            second_bias.reshape(1, -1),
        ),
    )
    layer_output, first_grad, out_grad, memory_part, weight_sums, vector_sums = middle(
        tokens.reshape(flat_rows, model_width),
        attended,
        cotangent.reshape(flat_rows, model_width),
        whole_memory.reshape(-1, model_width),
        norm_gain,
        norm_shift,
        down_bias.reshape(1, -1),
        raise_bias.reshape(1, -1),
        (
            self_output,
            cross_query,
            cross_key,
            cross_value,
            cross_output,
            adapter_down,
            adapter_raise,
            feed_in,
            feed_out,
        ),
    )
    layer_output = layer_output.reshape(row_count, length, model_width)
    memory_grad = lax.psum_scatter(
        memory_part, "seq", scatter_dimension=0, tiled=True
    ).reshape(memory.shape)
    token_grad, prefix_part = self_backward(
        n, out_grad, first_grad, saved, (self_query, self_key, self_value)
    )
    token_grad = token_grad.reshape(row_count, length, model_width)
    prefix_rows = prefix_embed.shape[0]
    group = model_width // n
    here = lax.axis_index("seq") * group
    prefix_grad = jnp.zeros((prefix_rows, 2 * model_width), jnp.float32)
    prefix_grad = lax.dynamic_update_slice(prefix_grad, prefix_part[0, :prefix_rows], (0, here))
    prefix_grad = lax.dynamic_update_slice(
        prefix_grad, prefix_part[1, :prefix_rows], (0, model_width + here)
    )
    prefix_grad = lax.psum(prefix_grad, ("seq", "batch"))
    weight_sums, vector_sums = lax.psum((weight_sums, vector_sums), ("seq", "batch"))
    down = adapter_down.shape[1]
    split = down * model_width // LANES
    down_weight_grad = (
        weight_sums[:split]
        .reshape(down // LANES, model_width, LANES)
        .swapaxes(0, 1)
        .reshape(model_width, down)
        .astype(jnp.float32)
    )
    raise_weight_grad = (
        weight_sums[split:]
        .reshape(model_width // LANES, down, LANES)
        .swapaxes(0, 1)
        .reshape(down, model_width)
        .astype(jnp.float32)
    )
    summed = (
        down_weight_grad,
        vector_sums[1, :down],
        raise_weight_grad,
        vector_sums[0],
        vector_sums[2:5],
        vector_sums[5:8],
    )
    prefix_hidden = jnp.tanh(matmul(prefix_embed, prefix_first) + first_bias)
    hidden_low = prefix_hidden.astype(jnp.bfloat16)
    second_weight_grad = precise_outer(hidden_low.astype(jnp.float32), prefix_grad)
    second_bias_grad = jnp.sum(prefix_grad, 0)
    hidden_grad = precise_back(prefix_grad, prefix_second.astype(jnp.float32)) * (
        1.0 - prefix_hidden * prefix_hidden
    )
    first_weight_grad = precise_outer(prefix_embed.astype(jnp.float32), hidden_grad)
    first_bias_grad = jnp.sum(hidden_grad, 0)
    embed_grad = precise_back(hidden_grad, prefix_first.astype(jnp.float32))
    return (
        layer_output,
        token_grad,
        memory_grad,
        embed_grad,
        first_weight_grad,
        first_bias_grad,
        second_weight_grad,
        second_bias_grad,
        summed[0],
        summed[1],
        summed[2],
        summed[3],
        summed[4],
        summed[5],
    )


def solution(mesh):
    placed = (
        P("batch", "seq", None),
        P("batch", "seq", None),
        P("batch", "seq"),
        P("batch", "seq"),
        P("batch", "seq", None),
        P(),
        P(),
        P(),
        P(),
        P(),
        P(),
        P(),
        P(),
        P(),
        P(),
        P(),
        P(),
        P(),
        P(),
        P(),
        P(),
        P(),
        P(),
        P(),
        P(),
        P(),
    )
    return jax.shard_map(
        per_device,
        mesh=mesh,
        in_specs=placed,
        out_specs=(
            P("batch", "seq", None),
            P("batch", "seq", None),
            P("batch", "seq", None),
            P(),
            P(),
            P(),
            P(),
            P(),
            P(),
            P(),
            P(),
            P(),
            P(),
            P(),
        ),
        check_vma=False,
    )
```

```python
import functools

import jax
import jax.numpy as jnp
from jax import lax
from jax.experimental import pallas as pl
from jax.experimental.pallas import tpu as pltpu
from jax.sharding import PartitionSpec as P

H = 16
HD = 64
LANES = 128
PREFIX_ROWS = 32
VMEM_BYTES = 60 * 1024 * 1024
MESH = pl.DeviceIdType.MESH

masked_score = -1e30
norm_eps = 1e-05

def dot_nn(left, right):
    return lax.dot_general(
        left, right, (((1,), (0,)), ((), ())), preferred_element_type=jnp.float32
    )


def dot_nt(left, right):
    return lax.dot_general(
        left, right, (((1,), (1,)), ((), ())), preferred_element_type=jnp.float32
    )


def dot_tn(left, right):
    return lax.dot_general(
        left, right, (((0,), (0,)), ((), ())), preferred_element_type=jnp.float32
    )


def remote(source, target, send_sem, recv_sem, axis, peer):
    return pltpu.make_async_remote_copy(
        src_ref=source,
        dst_ref=target,
        send_sem=send_sem,
        recv_sem=recv_sem,
        device_id={axis: peer},
        device_id_type=MESH,
    )


def enter(sizes):
    barrier = pltpu.get_barrier_semaphore()
    for axis, size in sizes.items():
        for other in range(size):

            @pl.when(other != lax.axis_index(axis))
            def _():
                pl.semaphore_signal(barrier, inc=1, device_id={axis: other}, device_id_type=MESH)

    pl.semaphore_wait(barrier, sum(sizes.values()) - len(sizes))


def rows_of(index, size):
    return pl.ds(pl.multiple_of(index * size, size), size)


def own_columns(ref, first, me, width):
    if width % LANES == 0:
        return ref[:, pl.ds(pl.multiple_of(first + me * width, LANES), width)].astype(jnp.float32)
    share = LANES // width
    block = ref[:, pl.ds(pl.multiple_of(first + me // share * LANES, LANES), LANES)].astype(
        jnp.float32
    )
    picked = block[:, :width]
    for part in range(1, share):
        picked = jnp.where(me % share == part, block[:, part * width : (part + 1) * width], picked)
    return picked


def head_lanes(shape, head):
    lane = lax.broadcasted_iota(jnp.int32, shape, 1)
    return (lane >= head * HD) & (lane < (head + 1) * HD)


def self_forward_kernel(
    n,
    seg_ref,
    pad_ref,
    tok_ref,
    wq_ref,
    wk_ref,
    wv_ref,
    emb_ref,
    first_ref,
    fbias_ref,
    second_ref,
    sbias_ref,
    att_ref,
    qx_out,
    kx_out,
    v_out,
    pk_out,
    pv_out,
    ot_out,
    lse_out,
    send,
    recv,
    meta_send,
    meta,
    kx,
    qx,
    vt,
    hidden,
    pk,
    pv,
    pvt,
    stat,
    acc,
    o_send,
    o_recv,
    send_sem,
    recv_sem,
    meta_send_sem,
    meta_recv_sem,
    o_send_sem,
    o_recv_sem,
    out_sem,
):
    me = lax.axis_index("seq")
    length, width = tok_ref.shape
    group = width // n
    heads = group // HD
    plane = 2 * length
    planes = n // 2
    block = 2 * LANES
    per_block = block // group
    blocks = width // block

    def meta_copy(peer, slot):
        return pltpu.make_async_remote_copy(
            src_ref=meta_send,
            dst_ref=meta.at[slot],
            send_sem=meta_send_sem.at[peer],
            recv_sem=meta_recv_sem.at[slot],
            device_id={"seq": peer},
            device_id_type=MESH,
        )

    def qkv_copy(peer, slot):
        return pltpu.make_async_remote_copy(
            src_ref=send.at[peer],
            dst_ref=recv.at[:, rows_of(slot, length), :],
            send_sem=send_sem.at[peer],
            recv_sem=recv_sem.at[slot],
            device_id={"seq": peer},
            device_id_type=MESH,
        )

    def out_copy(peer, slot):
        return pltpu.make_async_remote_copy(
            src_ref=o_send.at[peer],
            dst_ref=o_recv.at[slot],
            send_sem=o_send_sem.at[peer],
            recv_sem=o_recv_sem.at[slot],
            device_id={"seq": peer},
            device_id_type=MESH,
        )

    segments = seg_ref[...]
    tags = jnp.where(pad_ref[...] == 1, segments, -1)
    row = lax.broadcasted_iota(jnp.int32, meta_send.shape, 0)
    meta_send[...] = jnp.where(row == 0, segments, tags)
    enter({"seq": n})
    for other in range(n):

        @pl.when(other != me)
        def _():
            meta_copy(other, me).start()

    meta[me] = meta_send[...]

    def project(step, carry):
        here = lax.rem(me // per_block + 1 + step, blocks)
        columns = pl.ds(pl.multiple_of(here * block, block), block)
        for which, weight in enumerate((wq_ref, wk_ref, wv_ref)):
            piece = dot_nn(tok_ref[...], weight[:, columns]).astype(jnp.bfloat16)
            for part in range(per_block):
                send[here * per_block + part, which] = piece[:, part * group : (part + 1) * group]
        for part in range(per_block):
            peer = here * per_block + part

            @pl.when(peer != me)
            def _():
                qkv_copy(peer, me).start()

            @pl.when(peer == me)
            def _():
                recv[:, rows_of(me, length), :] = send[peer]

        return carry

    lax.fori_loop(0, blocks, project, 0)

    hidden[...] = jnp.zeros_like(hidden)
    hidden[: emb_ref.shape[0], :] = jnp.tanh(dot_nn(emb_ref[...], first_ref[...]) + fbias_ref[...])
    hidden_low = hidden[...].astype(jnp.bfloat16)
    prefix_key = dot_nn(
        hidden_low, own_columns(second_ref, 0, me, group).astype(jnp.bfloat16)
    ) + own_columns(sbias_ref, 0, me, group)
    prefix_value = dot_nn(
        hidden_low, own_columns(second_ref, width, me, group).astype(jnp.bfloat16)
    ) + own_columns(sbias_ref, width, me, group)
    pk[...] = jnp.zeros_like(pk)
    pk[:, :group] = prefix_key.astype(jnp.bfloat16)
    prefix_row = lax.broadcasted_iota(jnp.int32, (pk.shape[0], LANES), 0)
    pk[:, LANES:] = jnp.where(prefix_row < emb_ref.shape[0], 0.0, masked_score).astype(
        jnp.bfloat16
    )
    pv[...] = prefix_value.astype(jnp.bfloat16)
    pvt[...] = prefix_value.T.astype(jnp.bfloat16)

    def arrive(chunk):
        @pl.when(chunk != me)
        def _():
            meta_copy(chunk, chunk).wait_recv()
            qkv_copy(chunk, chunk).wait_recv()

        here = rows_of(chunk, length)
        state = lax.broadcasted_iota(jnp.int32, (LANES, length), 0)
        is_segment = jnp.where(state == meta[chunk, 0:1, :], 1.0, 0.0)
        is_open = jnp.where(state == meta[chunk, 1:2, :], 0.0, masked_score)
        query_state = is_segment.T.astype(jnp.bfloat16)
        kx[here, :group] = recv[1, here, :]
        kx[here, LANES:] = is_open.T.astype(jnp.bfloat16)
        if group < LANES:
            kx[here, group:LANES] = jnp.zeros((length, LANES - group), jnp.bfloat16)
        query = recv[0, here, :].astype(jnp.float32) * 0.125
        for head in range(heads):
            qx[head, here, :group] = jnp.where(
                head_lanes(query.shape, head), query, 0.0
            ).astype(jnp.bfloat16)
            qx[head, here, LANES:] = query_state
            if group < LANES:
                qx[head, here, group:LANES] = jnp.zeros((length, LANES - group), jnp.bfloat16)
        vt[:, here] = recv[2, here, :].astype(jnp.float32).T.astype(jnp.bfloat16)

    def open_plane(which):
        for head in range(heads):
            scores = dot_nt(pk[...], qx[head, rows_of(which, plane), :])
            top = jnp.max(scores, axis=0, keepdims=True)
            raised = jnp.exp(scores - top)
            stat[which, head : head + 1, :] = top
            stat[which, 4 + head : 5 + head, :] = jnp.sum(raised, axis=0, keepdims=True)
            span = slice(head * HD, (head + 1) * HD)
            acc[which, span, :] = dot_nn(pvt[span, :], raised.astype(jnp.bfloat16))

    def pair(upper, lower, diagonal):
        for part in range(2):
            first = length if diagonal and part == 1 else 0
            for head in range(heads):
                queries = qx[head, pl.ds(pl.multiple_of(upper * plane + first, length), plane - first), :]
                keys = pl.ds(pl.multiple_of(lower * plane + part * length, length), length)
                scores = dot_nt(kx[keys, :], queries)
                if diagonal:
                    key_at = lax.broadcasted_iota(jnp.int32, scores.shape, 0)
                    query_at = lax.broadcasted_iota(jnp.int32, scores.shape, 1)
                    scores = jnp.where(key_at <= query_at, scores, masked_score)
                old_top = stat[upper, head : head + 1, first:]
                top = jnp.maximum(old_top, jnp.max(scores, axis=0, keepdims=True))
                scale = jnp.exp(old_top - top)
                raised = jnp.exp(scores - top)
                stat[upper, head : head + 1, first:] = top
                stat[upper, 4 + head : 5 + head, first:] = stat[
                    upper, 4 + head : 5 + head, first:
                ] * scale + jnp.sum(raised, axis=0, keepdims=True)
                span = slice(head * HD, (head + 1) * HD)
                acc[upper, span, first:] = acc[upper, span, first:] * scale + dot_nn(
                    vt[span, keys], raised.astype(jnp.bfloat16)
                )

    def close_plane(which):
        for head in range(heads):
            span = slice(head * HD, (head + 1) * HD)
            total = stat[which, 4 + head : 5 + head, :]
            acc[which, span, :] = acc[which, span, :] / total
            stat[which, head : head + 1, :] = stat[which, head : head + 1, :] + jnp.log(total)
        for part in range(2):
            chunk = 2 * which + part
            o_send[chunk] = acc[which, :, part * length : (part + 1) * length].T.astype(
                jnp.bfloat16
            )

            @pl.when(chunk != me)
            def _():
                out_copy(chunk, me).start()

            @pl.when(chunk == me)
            def _():
                o_recv[me] = o_send[chunk]

    mine = me // 2

    def stage(step, carry):
        here = lax.rem(mine + step, planes)
        arrive(2 * here)
        arrive(2 * here + 1)
        open_plane(here)

        def earlier(back, inner):
            there = lax.rem(mine + back, planes)
            pair(jnp.maximum(here, there), jnp.minimum(here, there), False)
            return inner

        lax.fori_loop(0, step, earlier, 0)
        pair(here, here, True)

        @pl.when((mine + step >= planes) | (mine == 0))
        def _():
            close_plane(here)

        return carry

    lax.fori_loop(0, planes, stage, 0)

    def finish(which, carry):
        close_plane(which)
        return carry

    lax.fori_loop(jnp.where(mine == 0, planes, mine), planes, finish, 0)

    saves = [
        pltpu.make_async_copy(source, target, out_sem.at[index])
        for index, (source, target) in enumerate(
            (
                (qx, qx_out),
                (kx, kx_out),
                (recv.at[2], v_out),
                (pk, pk_out),
                (pv, pv_out),
                (acc, ot_out),
                (stat, lse_out),
            )
        )
    ]
    for save in saves:
        save.start()
    for other in range(n):

        @pl.when(other != me)
        def _():
            out_copy(other, other).wait_recv()

        att_ref[:, other * group : (other + 1) * group] = o_recv[other]
    for other in range(n):

        @pl.when(other != me)
        def _():
            meta_copy(other, me).wait_send()
            qkv_copy(other, me).wait_send()
            out_copy(other, me).wait_send()

    for save in saves:
        save.wait()


def self_forward(n, segments, padding, tokens, weights, prefix):
    length, width = tokens.shape
    group = width // n
    heads = group // HD
    whole = n * length
    planes = n // 2
    low = jnp.bfloat16
    vmem = pl.BlockSpec(memory_space=pltpu.VMEM)
    anywhere = pl.BlockSpec(memory_space=pl.ANY)
    dma = pltpu.SemaphoreType.DMA((n,))
    return pl.pallas_call(
        functools.partial(self_forward_kernel, n),
        out_shape=(
            jax.ShapeDtypeStruct((length, width), low),
            jax.ShapeDtypeStruct((heads, whole, 2 * LANES), low),
            jax.ShapeDtypeStruct((whole, 2 * LANES), low),
            jax.ShapeDtypeStruct((whole, group), low),
            jax.ShapeDtypeStruct((PREFIX_ROWS, 2 * LANES), low),
            jax.ShapeDtypeStruct((PREFIX_ROWS, group), low),
            jax.ShapeDtypeStruct((planes, group, 2 * length), jnp.float32),
            jax.ShapeDtypeStruct((planes, 8, 2 * length), jnp.float32),
        ),
        in_specs=[vmem] * 11,
        out_specs=(vmem,) + (anywhere,) * 7,
        scratch_shapes=[
            pltpu.VMEM((n, 3, length, group), low),
            pltpu.VMEM((3, whole, group), low),
            pltpu.VMEM((8, length), jnp.int32),
            pltpu.VMEM((n, 8, length), jnp.int32),
            pltpu.VMEM((whole, 2 * LANES), low),
            pltpu.VMEM((heads, whole, 2 * LANES), low),
            pltpu.VMEM((group, whole), low),
            pltpu.VMEM((PREFIX_ROWS, weights[0].shape[0] // 2), jnp.float32),
            pltpu.VMEM((PREFIX_ROWS, 2 * LANES), low),
            pltpu.VMEM((PREFIX_ROWS, group), low),
            pltpu.VMEM((group, PREFIX_ROWS), low),
            pltpu.VMEM((planes, 8, 2 * length), jnp.float32),
            pltpu.VMEM((planes, group, 2 * length), jnp.float32),
            pltpu.VMEM((n, length, group), low),
            pltpu.VMEM((n, length, group), low),
            dma,
            dma,
            dma,
            dma,
            dma,
            dma,
            pltpu.SemaphoreType.DMA((7,)),
        ],
        compiler_params=pltpu.CompilerParams(
            collective_id=0, has_side_effects=True, vmem_limit_bytes=VMEM_BYTES
        ),
        name="self_forward",
    )(segments, padding, tokens, *weights, *prefix)


def self_backward_kernel(
    n,
    batches,
    do_ref,
    base_ref,
    sums_in,
    mem_in,
    qx_in,
    kx_in,
    v_in,
    pk_in,
    pv_in,
    ot_in,
    lse_in,
    wq_in,
    wk_in,
    wv_in,
    tg_ref,
    mgrad_ref,
    pkv_ref,
    full_out,
    do_send,
    do_recv,
    qx,
    kx,
    v,
    kt,
    pk,
    pv,
    ot,
    lse,
    weights,
    dom,
    delta,
    dqt,
    dk,
    dv,
    g_send,
    g_recv,
    pre_ref,
    pre_all,
    pre_sum,
    pre_recv,
    sum_own,
    sum_batch,
    sum_mine,
    sum_y,
    sum_z,
    full,
    mem_own,
    mem_y,
    mem_mine,
    mem_z,
    do_send_sem,
    do_recv_sem,
    g_send_sem,
    g_recv_sem,
    in_sem,
    pa_send_sem,
    pa_recv_sem,
    pb_send_sem,
    pb_recv_sem,
    sa_send_sem,
    sa_recv_sem,
    sc_send_sem,
    sc_recv_sem,
    sd_send_sem,
    sd_recv_sem,
    sf_send_sem,
    sf_recv_sem,
    mb_send_sem,
    mb_recv_sem,
    y_send_sem,
    y_recv_sem,
):
    me = lax.axis_index("seq")
    length, width = do_ref.shape
    group = width // n
    heads = group // HD
    plane = 2 * length
    planes = n // 2
    block = 2 * LANES
    per_block = block // group

    def do_copy(peer, slot):
        return pltpu.make_async_remote_copy(
            src_ref=do_send.at[peer],
            dst_ref=do_recv.at[slot],
            send_sem=do_send_sem.at[peer],
            recv_sem=do_recv_sem.at[slot],
            device_id={"seq": peer},
            device_id_type=MESH,
        )

    def g_copy(peer, slot):
        return pltpu.make_async_remote_copy(
            src_ref=g_send.at[peer],
            dst_ref=g_recv.at[slot],
            send_sem=g_send_sem.at[peer],
            recv_sem=g_recv_sem.at[slot],
            device_id={"seq": peer},
            device_id_type=MESH,
        )

    my_batch = lax.axis_index("batch")
    my_plane = me // 2
    my_side = lax.rem(me, 2)
    beside = me + 1 - 2 * my_side

    def others(size, mine, body):
        for other in range(size):

            @pl.when(other != mine)
            def _():
                body(other)

    def sum_a(peer, slot):
        return remote(
            sums_in.at[peer],
            sum_batch.at[slot],
            sa_send_sem.at[peer],
            sa_recv_sem.at[slot],
            "batch",
            peer,
        )

    def sum_b():
        return remote(
            sum_mine.at[1 - my_side], sum_y, y_send_sem.at[0], y_recv_sem.at[0], "seq", beside
        )

    def sum_c(peer, slot):
        return remote(
            sum_mine.at[my_side, peer],
            sum_z.at[slot],
            sc_send_sem.at[peer],
            sc_recv_sem.at[slot],
            "seq",
            2 * peer + my_side,
        )

    def sum_d(peer, slot):
        return remote(
            full.at[my_batch, my_side, slot],
            full.at[my_batch, my_side, slot],
            sd_send_sem.at[peer],
            sd_recv_sem.at[slot],
            "seq",
            2 * peer + my_side,
        )

    def sum_e(side):
        return remote(
            full.at[my_batch, side],
            full.at[my_batch, side],
            y_send_sem.at[1],
            y_recv_sem.at[1],
            "seq",
            beside,
        )

    def sum_f(peer, slot):
        return remote(
            full.at[slot],
            full.at[slot],
            sf_send_sem.at[peer],
            sf_recv_sem.at[slot],
            "batch",
            peer,
        )

    def mem_a():
        return remote(
            mem_in.at[:, 1 - my_side], mem_y, y_send_sem.at[2], y_recv_sem.at[2], "seq", beside
        )

    def mem_b(peer, slot):
        return remote(
            mem_mine.at[peer],
            mem_z.at[slot],
            mb_send_sem.at[peer],
            mb_recv_sem.at[slot],
            "seq",
            2 * peer + my_side,
        )

    def pre_a(peer, slot):
        return remote(
            pre_ref,
            pre_all.at[slot],
            pa_send_sem.at[peer],
            pa_recv_sem.at[slot],
            "batch",
            peer,
        )

    def pre_b(peer, slot):
        return remote(
            pre_sum,
            pre_recv.at[slot],
            pb_send_sem.at[peer],
            pb_recv_sem.at[slot],
            "seq",
            peer,
        )

    loads = [
        pltpu.make_async_copy(source, target, in_sem.at[index])
        for index, (source, target) in enumerate(
            (
                (sums_in.at[my_batch], sum_own),
                (mem_in.at[:, my_side], mem_own),
                (kx_in, kx),
                (pk_in, pk),
                (qx_in, qx),
                (pv_in, pv),
                (v_in, v),
                (ot_in, ot),
                (lse_in, lse),
                (wq_in, weights.at[0]),
                (wk_in, weights.at[1]),
                (wv_in, weights.at[2]),
            )
        )
    ]
    for load in loads:
        load.start()
    for other in range(n):
        do_send[other] = do_ref[:, other * group : (other + 1) * group]
    enter({"seq": n, "batch": batches})
    for other in range(n):

        @pl.when(other != me)
        def _():
            do_copy(other, me).start()

    mem_a().start()
    others(batches, my_batch, lambda peer: sum_a(peer, my_batch).start())
    do_recv[me] = do_send[me]
    for load in loads[:9]:
        load.wait()

    def turn(chunk, carry):
        here = rows_of(chunk, length)
        kt[:, here] = kx[here, :group].astype(jnp.float32).T.astype(jnp.bfloat16)
        return carry

    lax.fori_loop(0, n, turn, 0)
    pkt = pk[:, :group].astype(jnp.float32).T.astype(jnp.bfloat16)
    dk[...] = jnp.zeros_like(dk)
    dv[...] = jnp.zeros_like(dv)
    pre_ref[...] = jnp.zeros_like(pre_ref)

    def arrive(step, carry):
        which = lax.rem(me // 2 + step, planes)
        for part in range(2):
            chunk = 2 * which + part

            @pl.when(chunk != me)
            def _():
                do_copy(chunk, chunk).wait_recv()

            grads = do_recv[chunk].astype(jnp.float32)
            for head in range(heads):
                dom[head, rows_of(chunk, length), :] = jnp.where(
                    head_lanes(grads.shape, head), grads, 0.0
                ).astype(jnp.bfloat16)
            here = slice(part * length, (part + 1) * length)
            both = grads.T * ot[which, :, here]
            for head in range(heads):
                delta[which, head : head + 1, here] = jnp.sum(
                    both[head * HD : (head + 1) * HD], axis=0, keepdims=True
                )
        for head in range(heads):
            span = slice(head * HD, (head + 1) * HD)
            queries = qx[head, rows_of(which, plane), :]
            grads = dom[head, rows_of(which, plane), :]
            weight = jnp.exp(dot_nt(pk[...], queries) - lse[which, head : head + 1, :])
            slope = weight * (dot_nt(pv[...], grads) - delta[which, head : head + 1, :])
            slope = slope.astype(jnp.bfloat16)
            pre_ref[0] += dot_nn(slope, queries[:, :group])
            pre_ref[1] += dot_nn(weight.astype(jnp.bfloat16), grads)
            dqt[which, span, :] = dot_nn(pkt[span, :], slope)
        return carry

    lax.fori_loop(0, planes, arrive, 0)

    def stage_a():
        others(batches, my_batch, lambda peer: pre_a(peer, my_batch).start())
        pre_all[my_batch] = pre_ref[...]
        others(batches, my_batch, lambda peer: sum_a(peer, peer).wait_recv())
        sum_batch[my_batch] = sum_own[...]
        value = sum_batch[0].astype(jnp.float32)
        for other in range(1, batches):
            value = value + sum_batch[other].astype(jnp.float32)
        sum_mine[...] = value.astype(jnp.bfloat16).reshape(sum_mine.shape)
        sum_b().start()
        mem_a().wait_recv()
        mem_mine[...] = (mem_own[...].astype(jnp.float32) + mem_y[...].astype(jnp.float32)).astype(
            jnp.bfloat16
        )
        others(planes, my_plane, lambda peer: mem_b(peer, my_plane).start())

    def stage_b():
        others(batches, my_batch, lambda peer: pre_a(peer, peer).wait_recv())
        value = pre_all[0]
        for other in range(1, batches):
            value = value + pre_all[other]
        pre_sum[...] = value
        others(n, me, lambda peer: pre_b(peer, me).start())
        pre_recv[me] = value
        sum_b().wait()
        sum_mine[my_side] = (
            sum_mine[my_side].astype(jnp.float32) + sum_y[...].astype(jnp.float32)
        ).astype(jnp.bfloat16)
        others(planes, my_plane, lambda peer: sum_c(peer, my_plane).start())

    def stage_c():
        others(planes, my_plane, lambda peer: sum_c(peer, peer).wait_recv())
        sum_z[my_plane] = sum_mine[my_side, my_plane]
        value = sum_z[0].astype(jnp.float32)
        for other in range(1, planes):
            value = value + sum_z[other].astype(jnp.float32)
        full[my_batch, my_side, my_plane] = value.astype(jnp.bfloat16)
        others(planes, my_plane, lambda peer: sum_d(peer, my_plane).start())

    def stage_d():
        others(planes, my_plane, lambda peer: sum_d(peer, peer).wait_recv())
        sum_e(my_side).start()
        others(planes, my_plane, lambda peer: mem_b(peer, peer).wait_recv())
        mem_z[my_plane] = mem_mine[my_plane]
        value = mem_z[0].astype(jnp.float32)
        for other in range(1, planes):
            value = value + mem_z[other].astype(jnp.float32)
        mgrad_ref[...] = value.astype(jnp.bfloat16)

    def stage_e():
        sum_e(1 - my_side).wait_recv()
        others(batches, my_batch, lambda peer: sum_f(peer, my_batch).start())

    def stage_f():
        others(batches, my_batch, lambda peer: sum_f(peer, peer).wait_recv())
        save = pltpu.make_async_copy(full, full_out, in_sem.at[0])
        save.start()
        width_half = width
        for other in range(n):

            @pl.when(other != me)
            def _():
                pre_b(other, other).wait_recv()

            for which in range(2):
                pkv_ref[
                    :, which * width_half + other * group : which * width_half + (other + 1) * group
                ] = pre_recv[other, which]
        return save

    def pair(upper, lower, diagonal):
        for part in range(2):
            first = length if diagonal and part == 1 else 0
            keys = pl.ds(pl.multiple_of(lower * plane + part * length, length), length)
            key_sum = None
            for head in range(heads):
                span = slice(head * HD, (head + 1) * HD)
                here = pl.ds(pl.multiple_of(upper * plane + first, length), plane - first)
                queries = qx[head, here, :]
                grads = dom[head, here, :]
                scores = dot_nt(kx[keys, :], queries)
                weight = jnp.exp(scores - lse[upper, head : head + 1, first:])
                if diagonal:
                    key_at = lax.broadcasted_iota(jnp.int32, scores.shape, 0)
                    query_at = lax.broadcasted_iota(jnp.int32, scores.shape, 1)
                    weight = jnp.where(key_at <= query_at, weight, 0.0)
                slope = weight * (dot_nt(v[keys, :], grads) - delta[upper, head : head + 1, first:])
                slope = slope.astype(jnp.bfloat16)
                key_part = dot_nn(slope, qx[head, here, :group])
                value_part = dot_nn(weight.astype(jnp.bfloat16), grads)
                if key_sum is None:
                    key_sum, value_sum = key_part, value_part
                else:
                    key_sum, value_sum = key_sum + key_part, value_sum + value_part
                dqt[upper, span, first:] += dot_nn(kt[span, keys], slope)
            dk[keys, :] += key_sum
            dv[keys, :] += value_sum

    def hand_over(which):
        for part in range(2):
            chunk = 2 * which + part
            here = rows_of(chunk, length)
            g_send[chunk, 0] = (
                (dqt[which, :, part * length : (part + 1) * length] * 0.125)
                .T.astype(jnp.bfloat16)
            )
            g_send[chunk, 1] = dk[here, :].astype(jnp.bfloat16)
            g_send[chunk, 2] = dv[here, :].astype(jnp.bfloat16)

            @pl.when(chunk != me)
            def _():
                g_copy(chunk, me).start()

            @pl.when(chunk == me)
            def _():
                g_recv[me] = g_send[chunk]

    rising = lax.rem(me, 2) == 0
    stage_a()

    def stage(step, carry):
        here = jnp.where(rising, step, planes - 1 - step)

        def far(index, inner):
            there = jnp.where(rising, here + 1 + index, index)
            pair(jnp.maximum(here, there), jnp.minimum(here, there), False)
            return inner

        lax.fori_loop(0, planes - 1 - step, far, 0)
        pair(here, here, True)
        hand_over(here)
        for at, body in enumerate((stage_b, stage_c, stage_d, stage_e)):
            pl.when(step == at)(body)
        return carry

    lax.fori_loop(0, planes, stage, 0)
    for load in loads[9:]:
        load.wait()
    total = base_ref[...]
    for here in range(width // block):
        pieces = []
        for part in range(per_block):
            other = here * per_block + part

            @pl.when(other != me)
            def _():
                g_copy(other, other).wait_recv()

        for which in range(3):
            piece = jnp.concatenate(
                [g_recv[here * per_block + part, which] for part in range(per_block)], axis=1
            )
            pieces.append(
                dot_nt(piece, weights[which, :, here * block : (here + 1) * block])
            )
        total = total + (pieces[0] + pieces[1] + pieces[2])
    tg_ref[...] = total.astype(jnp.bfloat16)
    save = stage_f()
    others(n, me, lambda peer: do_copy(peer, me).wait_send())
    others(n, me, lambda peer: g_copy(peer, me).wait_send())
    others(n, me, lambda peer: pre_b(peer, me).wait_send())
    others(batches, my_batch, lambda peer: pre_a(peer, my_batch).wait_send())
    others(batches, my_batch, lambda peer: sum_a(peer, my_batch).wait_send())
    others(batches, my_batch, lambda peer: sum_f(peer, my_batch).wait_send())
    others(planes, my_plane, lambda peer: sum_c(peer, my_plane).wait_send())
    others(planes, my_plane, lambda peer: sum_d(peer, my_plane).wait_send())
    others(planes, my_plane, lambda peer: mem_b(peer, my_plane).wait_send())
    sum_e(my_side).wait_send()
    mem_a().wait_send()
    save.wait()


def self_backward(n, batches, out_grad, first_grad, sums, memory_part, saved, weights):
    length, width = out_grad.shape
    group = width // n
    heads = group // HD
    whole = n * length
    planes = n // 2
    low = jnp.bfloat16
    vmem = pl.BlockSpec(memory_space=pltpu.VMEM)
    anywhere = pl.BlockSpec(memory_space=pl.ANY)
    dma = pltpu.SemaphoreType.DMA((n,))
    batch_dma = pltpu.SemaphoreType.DMA((batches,))
    plane_dma = pltpu.SemaphoreType.DMA((planes,))
    sum_rows = sums.shape[0] // (batches * n)
    mem_rows = memory_part.shape[0] // n
    mem_buffer = pltpu.VMEM((planes, mem_rows, width), low)
    return pl.pallas_call(
        functools.partial(self_backward_kernel, n, batches),
        out_shape=(
            jax.ShapeDtypeStruct((length, width), low),
            jax.ShapeDtypeStruct((mem_rows, width), low),
            jax.ShapeDtypeStruct((PREFIX_ROWS, 2 * width), jnp.float32),
            jax.ShapeDtypeStruct((batches, 2, planes, sum_rows, LANES), low),
        ),
        in_specs=[vmem, vmem] + [anywhere] * 12,
        out_specs=(vmem, vmem, vmem, anywhere),
        scratch_shapes=[
            pltpu.VMEM((n, length, group), low),
            pltpu.VMEM((n, length, group), low),
            pltpu.VMEM((heads, whole, 2 * LANES), low),
            pltpu.VMEM((whole, 2 * LANES), low),
            pltpu.VMEM((whole, group), low),
            pltpu.VMEM((group, whole), low),
            pltpu.VMEM((PREFIX_ROWS, 2 * LANES), low),
            pltpu.VMEM((PREFIX_ROWS, group), low),
            pltpu.VMEM((planes, group, 2 * length), jnp.float32),
            pltpu.VMEM((planes, 8, 2 * length), jnp.float32),
            pltpu.VMEM((3, width, width), low),
            pltpu.VMEM((heads, whole, group), low),
            pltpu.VMEM((planes, 8, 2 * length), jnp.float32),
            pltpu.VMEM((planes, group, 2 * length), jnp.float32),
            pltpu.VMEM((whole, group), jnp.float32),
            pltpu.VMEM((whole, group), jnp.float32),
            pltpu.VMEM((n, 3, length, group), low),
            pltpu.VMEM((n, 3, length, group), low),
            pltpu.VMEM((2, PREFIX_ROWS, group), jnp.float32),
            pltpu.VMEM((batches, 2, PREFIX_ROWS, group), jnp.float32),
            pltpu.VMEM((2, PREFIX_ROWS, group), jnp.float32),
            pltpu.VMEM((n, 2, PREFIX_ROWS, group), jnp.float32),
            pltpu.VMEM((2 * planes * sum_rows, LANES), low),
            pltpu.VMEM((batches, 2 * planes * sum_rows, LANES), low),
            pltpu.VMEM((2, planes, sum_rows, LANES), low),
            pltpu.VMEM((planes, sum_rows, LANES), low),
            pltpu.VMEM((planes, sum_rows, LANES), low),
            pltpu.VMEM((batches, 2, planes, sum_rows, LANES), low),
            mem_buffer,
            mem_buffer,
            mem_buffer,
            mem_buffer,
            dma,
            dma,
            dma,
            dma,
            pltpu.SemaphoreType.DMA((12,)),
            batch_dma,
            batch_dma,
            dma,
            dma,
            batch_dma,
            batch_dma,
            plane_dma,
            plane_dma,
            plane_dma,
            plane_dma,
            batch_dma,
            batch_dma,
            plane_dma,
            plane_dma,
            pltpu.SemaphoreType.DMA((3,)),
            pltpu.SemaphoreType.DMA((3,)),
        ],
        compiler_params=pltpu.CompilerParams(
            collective_id=1, has_side_effects=True, vmem_limit_bytes=VMEM_BYTES
        ),
        name="self_backward",
    )(
        out_grad,
        first_grad,
        sums.reshape(batches, -1, LANES),
        memory_part.reshape(planes, 2, mem_rows, width),
        *saved,
        *weights,
    )


def dot_split(dot, left, right):
    high = right.astype(jnp.bfloat16)
    rest = (right - high.astype(jnp.float32)).astype(jnp.bfloat16)
    return dot(left, high) + dot(left, rest)


def split_dot(dot, left, right):
    high = left.astype(jnp.bfloat16)
    rest = (left - high.astype(jnp.float32)).astype(jnp.bfloat16)
    return dot(high, right) + dot(rest, right)


def finish_kernel(
    full_ref,
    pkv_ref,
    emb_ref,
    first_ref,
    fbias_ref,
    second_ref,
    embed_out,
    first_out,
    fbias_out,
    second_out,
    sbias_out,
    down_out,
    dbias_out,
    raise_out,
    rbias_out,
    gain_out,
    shift_out,
    first_grad,
    second_grad,
    down_grad,
    raise_grad,
    emb,
    hidden,
    vecs,
    out_sem,
):
    f32 = jnp.float32
    low = jnp.bfloat16
    width = emb_ref.shape[1]
    down = dbias_out.shape[1]
    count = emb_ref.shape[0]
    saves = [
        pltpu.make_async_copy(source, target, out_sem.at[index])
        for index, (source, target) in enumerate(
            (
                (second_grad, second_out),
                (first_grad, first_out),
                (down_grad, down_out),
                (raise_grad, raise_out),
            )
        )
    ]
    emb[...] = jnp.zeros_like(emb)
    emb[:count, :] = emb_ref[...].astype(f32)
    emb_low = emb[...].astype(low)
    row = lax.broadcasted_iota(jnp.int32, hidden.shape, 0)
    hidden[...] = jnp.where(
        row < count, jnp.tanh(dot_nn(emb_low, first_ref[...]) + fbias_ref[...]), 0.0
    )
    hidden_low = hidden[...].astype(low)
    prefix = pkv_ref[...]
    tile = 512
    for index in range(prefix.shape[1] // tile):
        here = slice(index * tile, (index + 1) * tile)
        second_grad[:, here] = dot_split(dot_tn, hidden_low, prefix[:, here])
    saves[0].start()
    sbias_out[...] = jnp.sum(prefix, axis=0, keepdims=True)
    value = hidden[...]
    hidden_grad = split_dot(dot_nt, prefix, second_ref[...]) * (1.0 - value * value)
    fbias_out[...] = jnp.sum(hidden_grad, axis=0, keepdims=True)
    first_grad[...] = dot_split(dot_tn, emb_low, hidden_grad)
    saves[1].start()
    embed_out[...] = split_dot(dot_nt, hidden_grad, first_ref[...])[:count, :]
    for index in range(down // LANES):
        down_grad[:, index * LANES : (index + 1) * LANES] = full_ref[
            index * width : (index + 1) * width, :
        ].astype(f32)
    saves[2].start()
    first = down * width // LANES
    for index in range(width // LANES):
        raise_grad[:, index * LANES : (index + 1) * LANES] = full_ref[
            first + index * down : first + (index + 1) * down, :
        ].astype(f32)
    saves[3].start()
    first = 2 * first
    for index in range(width // LANES // 2):
        both = full_ref[first + 16 * index : first + 16 * (index + 1), :].astype(f32)
        vecs[:, 2 * index * LANES : (2 * index + 1) * LANES] = both[:8]
        vecs[:, (2 * index + 1) * LANES : (2 * index + 2) * LANES] = both[8:]
    rbias_out[...] = vecs[0:1, :]
    dbias_out[...] = vecs[1:2, :down]
    gain_out[...] = vecs[2:5, :]
    shift_out[...] = vecs[5:8, :]
    for save in saves:
        save.wait()


def finish(full, prefix_grad, embed, first, first_bias, second, down):
    f32 = jnp.float32
    count, width = embed.shape
    hidden = first.shape[1]
    vmem = pl.BlockSpec(memory_space=pltpu.VMEM)
    anywhere = pl.BlockSpec(memory_space=pl.ANY)
    shapes = (
        (count, width),
        (width, hidden),
        (1, hidden),
        (hidden, 2 * width),
        (1, 2 * width),
        (width, down),
        (1, down),
        (down, width),
        (1, width),
        (3, width),
        (3, width),
    )
    return pl.pallas_call(
        finish_kernel,
        out_shape=tuple(jax.ShapeDtypeStruct(shape, f32) for shape in shapes),
        in_specs=[vmem] * 6,
        out_specs=(
            vmem,
            anywhere,
            vmem,
            anywhere,
            vmem,
            anywhere,
            vmem,
            anywhere,
            vmem,
            vmem,
            vmem,
        ),
        scratch_shapes=[
            pltpu.VMEM((width, hidden), f32),
            pltpu.VMEM((hidden, 2 * width), f32),
            pltpu.VMEM((width, down), f32),
            pltpu.VMEM((down, width), f32),
            pltpu.VMEM((PREFIX_ROWS, width), f32),
            pltpu.VMEM((PREFIX_ROWS, hidden), f32),
            pltpu.VMEM((8, width), f32),
            pltpu.SemaphoreType.DMA((4,)),
        ],
        compiler_params=pltpu.CompilerParams(vmem_limit_bytes=VMEM_BYTES),
        name="finish",
    )(full, prefix_grad, embed, first, first_bias, second)


def gelu_pair(value):
    scaled = jnp.abs(value) * 0.7071067811865476
    step = 1.0 / (1.0 + 0.3275911 * scaled)
    bell = jnp.exp(-scaled * scaled)
    poly = step * (
        0.254829592
        + step
        * (-0.284496736 + step * (1.421413741 + step * (-1.453152027 + step * 1.061405429)))
    )
    tail = 0.5 * poly * bell
    share = jnp.where(value >= 0.0, 1.0 - tail, tail)
    return value * share, share + value * (bell * 0.3989422804014327)


def normed(value):
    center = jnp.mean(value, axis=-1, keepdims=True)
    centered = value - center
    scale = lax.rsqrt(jnp.mean(centered * centered, axis=-1, keepdims=True) + norm_eps)
    return centered * scale, scale


def norm_back(grad, scale, unit):
    return scale * (
        grad
        - jnp.mean(grad, axis=-1, keepdims=True)
        - unit * jnp.mean(grad * unit, axis=-1, keepdims=True)
    )


def middle_kernel(
    tok_ref,
    att_ref,
    cot_ref,
    mem_ref,
    gain_ref,
    shift_ref,
    dbias_ref,
    rbias_ref,
    wo_in,
    wcq_in,
    wck_in,
    wcv_in,
    wco_in,
    wd_in,
    wr_in,
    win_in,
    wout_in,
    out_ref,
    fgrad_ref,
    ograd_ref,
    mpart_ref,
    sums_ref,
    wo,
    wcq,
    wck,
    wcv,
    wco,
    wd,
    wr,
    win,
    wout,
    unit_one,
    unit_two,
    work,
    total,
    scale_one,
    scale_two,
    low_one,
    low_two,
    low_three,
    query,
    crossed,
    mem_key,
    mem_value,
    weights,
    slopes,
    down_act,
    down_slope,
    down_grad,
    vecs_ref,
    load_sem,
    win_sem,
    wout_sem,
):
    length, width = tok_ref.shape
    mem_len = mem_ref.shape[0]
    tile = win.shape[2]
    tiles = win_in.shape[1] // tile
    rows_step = 128
    low = jnp.bfloat16
    f32 = jnp.float32

    sources = (wo_in, wcq_in, wck_in, wcv_in, wco_in, wd_in, wr_in)
    targets = (wo, wcq, wck, wcv, wco, wd, wr)
    loads = [
        pltpu.make_async_copy(source, target, load_sem.at[index])
        for index, (source, target) in enumerate(zip(sources, targets))
    ]

    def win_load(which):
        slot = lax.rem(which, 2)
        return pltpu.make_async_copy(
            win_in.at[:, rows_of(which, tile)], win.at[slot], win_sem.at[slot]
        )

    def wout_load(which):
        slot = lax.rem(which, 2)
        return pltpu.make_async_copy(
            wout_in.at[rows_of(which, tile), :], wout.at[slot], wout_sem.at[slot]
        )

    for load in loads[:5]:
        load.start()
    for which in range(2):
        win_load(which).start()
        wout_load(which).start()
    for load in loads[5:]:
        load.start()

    def by_columns(extent, step, body):
        def one(index, carry):
            body(pl.ds(pl.multiple_of(index * step, step), step))
            return carry

        lax.fori_loop(0, extent // step, one, 0)

    def by_rows(body, init=0):
        def one(index, carry):
            return body(rows_of(index, rows_step), carry)

        return lax.fori_loop(0, length // rows_step, one, init)

    cols = 512
    half = width // 2

    loads[0].wait()

    def project_out(here):
        work[:, here] = tok_ref[:, here].astype(f32) + dot_nn(att_ref[...], wo[:, here])

    by_columns(width, cols, project_out)

    def first_norm(here, carry):
        unit, scale = normed(work[here, :])
        unit_one[here, :] = unit
        scale_one[here, :] = scale
        value = unit * gain_ref[0:1, :] + shift_ref[0:1, :]
        work[here, :] = value
        low_one[here, :] = value.astype(low)
        return carry

    by_rows(first_norm)

    loads[1].wait()

    def project_query(here):
        query[:, here] = dot_nn(low_one[...], wcq[:, here]).astype(low)

    by_columns(width, cols, project_query)
    loads[2].wait()
    loads[3].wait()

    def project_memory(here):
        mem_key[:, here] = dot_nn(mem_ref[...], wck[:, here]).astype(low)
        mem_value[:, here] = dot_nn(mem_ref[...], wcv[:, here]).astype(low)

    by_columns(width, cols, project_memory)

    per_block = LANES // HD

    def head_queries(here, head):
        both = query[:, here].astype(f32) * 0.125
        return jnp.where(head_lanes(both.shape, head), both, 0.0).astype(low)

    def cross_forward(block, carry):
        here = rows_of(block, LANES)
        keys = mem_key[:, here]
        values = mem_value[:, here].astype(f32).T.astype(low)
        outs = []
        for head in range(per_block):
            scores = dot_nt(keys, head_queries(here, head))
            raised = jnp.exp(scores - jnp.max(scores, axis=0, keepdims=True))
            share = 1.0 / jnp.sum(raised, axis=0, keepdims=True)
            weight = (raised * share).astype(low)
            weights[block * per_block + head] = weight
            outs.append(dot_nn(values[head * HD : (head + 1) * HD, :], weight))
        crossed[:, here] = jnp.concatenate(outs, axis=0).T.astype(low)
        return carry

    lax.fori_loop(0, width // LANES, cross_forward, 0)

    loads[4].wait()

    def project_crossed(here):
        work[:, here] += dot_nn(crossed[...], wco[:, here])

    by_columns(width, cols, project_crossed)

    def second_norm(here, carry):
        unit, scale = normed(work[here, :])
        unit_two[here, :] = unit
        scale_two[here, :] = scale
        value = unit * gain_ref[1:2, :] + shift_ref[1:2, :]
        work[here, :] = value
        low_two[here, :] = value.astype(low)
        return carry

    by_rows(second_norm)

    total[...] = jnp.zeros_like(total)

    def feed_forward(which, carry):
        slot = lax.rem(which, 2)
        win_load(which).wait()
        pre = dot_nn(low_two[...], win[slot])
        act, slope = gelu_pair(pre)
        slopes[:, rows_of(which, tile)] = slope.astype(low)
        wout_load(which).wait()
        total[...] += dot_nn(act.astype(low), wout[slot])

        @pl.when(which + 2 < tiles)
        def _():
            win_load(which + 2).start()
            wout_load(which + 2).start()

        return carry

    lax.fori_loop(0, tiles, feed_forward, 0)
    loads[5].wait()
    loads[6].wait()
    act, slope = gelu_pair(dot_nn(low_two[...], wd[...]) + dbias_ref[...])
    down_act[...] = act.astype(low)
    down_slope[...] = slope.astype(low)

    def project_raise(here):
        work[:, here] += total[:, here] + 4.0 * (
            dot_nn(down_act[...], wr[:, here]) + rbias_ref[:, here]
        )

    by_columns(width, cols, project_raise)
    nothing = jnp.zeros((1, width), f32)

    def third_norm(here, carry):
        gain_sum, shift_sum, bias_sum = carry
        unit, scale = normed(work[here, :])
        gain = gain_ref[2:3, :]
        out_ref[here, :] = (unit * gain + shift_ref[2:3, :]).astype(low)
        grad = cot_ref[here, :].astype(f32)
        back = norm_back(grad * gain, scale, unit)
        total[here, :] = back
        back_low = back.astype(low)
        low_three[here, :] = back_low
        return (
            gain_sum + jnp.sum(grad * unit, axis=0, keepdims=True),
            shift_sum + jnp.sum(grad, axis=0, keepdims=True),
            bias_sum + jnp.sum(back_low.astype(f32), axis=0, keepdims=True),
        )

    gain_three, shift_three, bias_sum = by_rows(third_norm, (nothing, nothing, nothing))
    vecs_ref[0:1, :] = 4.0 * bias_sum

    back = 4.0 * dot_nt(low_three[...], wr[...]) * down_slope[...].astype(f32)
    back_low = back.astype(low)
    down_grad[...] = back_low
    vecs_ref[1:2, :] = jnp.concatenate(
        [
            jnp.sum(back_low.astype(f32), axis=0, keepdims=True),
            jnp.zeros((1, width - wd.shape[1]), f32),
        ],
        axis=1,
    )
    down = wd.shape[1]
    raise_sum = 4.0 * dot_tn(down_act[...], low_three[...])
    for index in range(width // LANES):
        sums_ref[pl.ds(down * width // LANES + index * down, down), :] = raise_sum[
            :, index * LANES : (index + 1) * LANES
        ].astype(low)
    down_sum = dot_tn(low_two[...], down_grad[...])
    for index in range(down // LANES):
        sums_ref[index * width : (index + 1) * width, :] = down_sum[
            :, index * LANES : (index + 1) * LANES
        ].astype(low)

    def feed_backward(step, carry):
        which = tiles - 1 - step
        slot = lax.rem(which, 2)
        here = rows_of(which, tile)

        @pl.when(which < tiles - 2)
        def _():
            wout_load(which).wait()
            win_load(which).wait()

        grad = dot_nt(low_three[...], wout[slot]) * slopes[:, here].astype(f32)
        total[...] += dot_nt(grad.astype(low), win[slot])

        @pl.when(which >= 2)
        def _():
            win_load(which - 2).start()
            wout_load(which - 2).start()

        return carry

    lax.fori_loop(0, tiles, feed_backward, 0)

    def down_back(here):
        total[:, here] += dot_nt(down_grad[...], wd[here, :])

    by_columns(width, cols, down_back)

    def second_back(here, carry):
        gain_sum, shift_sum = carry
        grad = total[here, :]
        unit = unit_two[here, :]
        back = norm_back(grad * gain_ref[1:2, :], scale_two[here, :], unit)
        total[here, :] = back
        low_one[here, :] = back.astype(low)
        return (
            gain_sum + jnp.sum(grad * unit, axis=0, keepdims=True),
            shift_sum + jnp.sum(grad, axis=0, keepdims=True),
        )

    gain_two, shift_two = by_rows(second_back, (nothing, nothing))

    def crossed_back(here):
        crossed[:, here] = dot_nt(low_one[...], wco[here, :]).astype(low)

    by_columns(width, cols, crossed_back)

    def cross_backward(block, carry):
        here = rows_of(block, LANES)
        values = mem_value[:, here]
        keys = mem_key[:, here].astype(f32).T.astype(low)
        grads = crossed[:, here].astype(f32)
        outs = []
        key_sum = None
        for head in range(per_block):
            grad = jnp.where(head_lanes(grads.shape, head), grads, 0.0).astype(low)
            weight_low = weights[block * per_block + head]
            weight = weight_low.astype(f32)
            slope = dot_nt(values, grad)
            slope = weight * (slope - jnp.sum(weight * slope, axis=0, keepdims=True))
            slope = slope.astype(low)
            key_part = dot_nn(slope, head_queries(here, head))
            value_part = dot_nn(weight_low, grad)
            if key_sum is None:
                key_sum, value_sum = key_part, value_part
            else:
                key_sum, value_sum = key_sum + key_part, value_sum + value_part
            outs.append(dot_nn(keys[head * HD : (head + 1) * HD, :], slope))
        mem_key[:, here] = key_sum.astype(low)
        mem_value[:, here] = value_sum.astype(low)
        query[:, here] = (jnp.concatenate(outs, axis=0) * 0.125).T.astype(low)
        return carry

    lax.fori_loop(0, width // LANES, cross_backward, 0)

    def memory_back(here):
        mpart_ref[:, here] = (
            dot_nt(mem_key[...], wck[here, :]) + dot_nt(mem_value[...], wcv[here, :])
        ).astype(low)

    by_columns(width, cols, memory_back)

    def query_back(here):
        total[:, here] += dot_nt(query[...], wcq[here, :])

    by_columns(width, cols, query_back)

    def first_back(here, carry):
        gain_sum, shift_sum = carry
        grad = total[here, :]
        unit = unit_one[here, :]
        back = norm_back(grad * gain_ref[0:1, :], scale_one[here, :], unit)
        fgrad_ref[here, :] = back
        low_one[here, :] = back.astype(low)
        return (
            gain_sum + jnp.sum(grad * unit, axis=0, keepdims=True),
            shift_sum + jnp.sum(grad, axis=0, keepdims=True),
        )

    gain_one, shift_one = by_rows(first_back, (nothing, nothing))

    def out_back(here):
        ograd_ref[:, here] = dot_nt(low_one[...], wo[here, :]).astype(low)

    by_columns(width, cols, out_back)
    for index, vector in enumerate(
        (gain_one, gain_two, gain_three, shift_one, shift_two, shift_three)
    ):
        vecs_ref[2 + index : 3 + index, :] = vector
    first = 2 * down * width // LANES
    for index in range(width // LANES // 2):
        here = 2 * index * LANES
        sums_ref[first + 16 * index : first + 16 * (index + 1), :] = jnp.concatenate(
            [vecs_ref[:, here : here + LANES], vecs_ref[:, here + LANES : here + 2 * LANES]], axis=0
        ).astype(low)
    first += 8 * width // LANES
    rest = sums_ref.shape[0] - first
    if rest:
        sums_ref[first:, :] = jnp.zeros((rest, LANES), low)


def middle(tokens, attended, cotangent, memory, gains, shifts, down_bias, raise_bias, weights, sum_rows):
    length, width = tokens.shape
    mem_len = memory.shape[0]
    down = weights[5].shape[1]
    feed = weights[7].shape[1]
    tile = 512 if mem_len <= 512 else 256
    low = jnp.bfloat16
    f32 = jnp.float32
    vmem = pl.BlockSpec(memory_space=pltpu.VMEM)
    anywhere = pl.BlockSpec(memory_space=pl.ANY)
    square = pltpu.VMEM((width, width), low)
    wide = pltpu.VMEM((length, width), f32)
    narrow = pltpu.VMEM((length, width), low)
    mem_low = pltpu.VMEM((mem_len, width), low)
    return pl.pallas_call(
        middle_kernel,
        out_shape=(
            jax.ShapeDtypeStruct((length, width), low),
            jax.ShapeDtypeStruct((length, width), f32),
            jax.ShapeDtypeStruct((length, width), low),
            jax.ShapeDtypeStruct((mem_len, width), low),
            jax.ShapeDtypeStruct((sum_rows, LANES), low),
        ),
        in_specs=[vmem] * 8 + [anywhere] * 9,
        out_specs=(vmem,) * 5,
        scratch_shapes=[
            square,
            square,
            square,
            square,
            square,
            pltpu.VMEM((width, down), low),
            pltpu.VMEM((down, width), low),
            pltpu.VMEM((2, width, tile), low),
            pltpu.VMEM((2, tile, width), low),
            wide,
            wide,
            wide,
            wide,
            pltpu.VMEM((length, 1), f32),
            pltpu.VMEM((length, 1), f32),
            narrow,
            narrow,
            narrow,
            narrow,
            narrow,
            mem_low,
            mem_low,
            pltpu.VMEM((H, mem_len, length), low),
            pltpu.VMEM((length, feed), low),
            pltpu.VMEM((length, down), low),
            pltpu.VMEM((length, down), low),
            pltpu.VMEM((length, down), low),
            pltpu.VMEM((8, width), f32),
            pltpu.SemaphoreType.DMA((7,)),
            pltpu.SemaphoreType.DMA((2,)),
            pltpu.SemaphoreType.DMA((2,)),
        ],
        compiler_params=pltpu.CompilerParams(vmem_limit_bytes=VMEM_BYTES + (0 if mem_len <= 512 else 2 * 1024 * 1024)),
        name="middle",
    )(tokens, attended, cotangent, memory, gains, shifts, down_bias, raise_bias, *weights)


def per_device(
    tokens,
    memory,
    segment_ids,
    padding_mask,
    cotangent,
    prefix_embed,
    prefix_first,
    first_bias,
    prefix_second,
    second_bias,
    adapter_down,
    down_bias,
    adapter_raise,
    raise_bias,
    norm_gain,
    norm_shift,
    self_query,
    self_key,
    self_value,
    self_output,
    cross_query,
    cross_key,
    cross_value,
    cross_output,
    feed_in,
    feed_out,
):
    row_count, length, model_width = tokens.shape
    flat_rows = row_count * length
    n = lax.axis_size("seq")
    whole_memory = lax.all_gather(memory, "seq", axis=1, tiled=True)
    batches = lax.axis_size("batch")
    down = adapter_down.shape[1]
    share = 16 * n * batches
    sum_rows = -(-(2 * down * model_width + 8 * model_width) // (LANES * share)) * share
    attended, *saved = self_forward(
        n,
        segment_ids,
        padding_mask,
        tokens.reshape(flat_rows, model_width),
        (self_query, self_key, self_value),
        (
            prefix_embed,
            prefix_first,
            first_bias.reshape(1, -1),
            prefix_second,
            second_bias.reshape(1, -1),
        ),
    )
    layer_output, first_grad, out_grad, memory_part, weight_sums = middle(
        tokens.reshape(flat_rows, model_width),
        attended,
        cotangent.reshape(flat_rows, model_width),
        whole_memory.reshape(-1, model_width),
        norm_gain,
        norm_shift,
        down_bias.reshape(1, -1),
        raise_bias.reshape(1, -1),
        (
            self_output,
            cross_query,
            cross_key,
            cross_value,
            cross_output,
            adapter_down,
            adapter_raise,
            feed_in,
            feed_out,
        ),
        sum_rows,
    )
    layer_output = layer_output.reshape(row_count, length, model_width)
    token_grad, memory_grad, prefix_grad, full_sums = self_backward(
        n,
        batches,
        out_grad,
        first_grad,
        weight_sums,
        memory_part,
        saved,
        (self_query, self_key, self_value),
    )
    token_grad = token_grad.reshape(row_count, length, model_width)
    memory_grad = memory_grad.reshape(memory.shape)
    replicated = finish(
        full_sums.reshape(sum_rows, LANES),
        prefix_grad,
        prefix_embed,
        prefix_first,
        first_bias.reshape(1, -1),
        prefix_second,
        down,
    )
    replicated = [
        value.reshape(-1) if value.shape[0] == 1 else value for value in replicated
    ]
    return (layer_output, token_grad, memory_grad, *replicated)


def solution(mesh):
    placed = (
        P("batch", "seq", None),
        P("batch", "seq", None),
        P("batch", "seq"),
        P("batch", "seq"),
        P("batch", "seq", None),
        P(),
        P(),
        P(),
        P(),
        P(),
        P(),
        P(),
        P(),
        P(),
        P(),
        P(),
        P(),
        P(),
        P(),
        P(),
        P(),
        P(),
        P(),
        P(),
        P(),
        P(),
    )
    return jax.shard_map(
        per_device,
        mesh=mesh,
        in_specs=placed,
        out_specs=(
            P("batch", "seq", None),
            P("batch", "seq", None),
            P("batch", "seq", None),
            P(),
            P(),
            P(),
            P(),
            P(),
            P(),
            P(),
            P(),
            P(),
            P(),
            P(),
        ),
        check_vma=False,
    )
```

```python
import functools

import jax
import jax.numpy as jnp
from jax import lax
from jax.experimental import pallas as pl
from jax.experimental.pallas import tpu as pltpu
from jax.sharding import PartitionSpec as P

H = 16
HD = 64
LANES = 128
PREFIX_ROWS = 32
VMEM_BYTES = 60 * 1024 * 1024
SUM_ROWS = 16
MESH = pl.DeviceIdType.MESH

masked_score = -1e30
norm_eps = 1e-05

def dot_nn(left, right):
    return lax.dot_general(
        left, right, (((1,), (0,)), ((), ())), preferred_element_type=jnp.float32
    )


def dot_nt(left, right):
    return lax.dot_general(
        left, right, (((1,), (1,)), ((), ())), preferred_element_type=jnp.float32
    )


def dot_tn(left, right):
    return lax.dot_general(
        left, right, (((0,), (0,)), ((), ())), preferred_element_type=jnp.float32
    )


def remote(source, target, send_sem, recv_sem, axis, peer):
    return pltpu.make_async_remote_copy(
        src_ref=source,
        dst_ref=target,
        send_sem=send_sem,
        recv_sem=recv_sem,
        device_id={axis: peer},
        device_id_type=MESH,
    )


def enter(sizes):
    barrier = pltpu.get_barrier_semaphore()
    for axis, size in sizes.items():
        for other in range(size):

            @pl.when(other != lax.axis_index(axis))
            def _():
                pl.semaphore_signal(barrier, inc=1, device_id={axis: other}, device_id_type=MESH)

    pl.semaphore_wait(barrier, sum(sizes.values()) - len(sizes))


def rows_of(index, size):
    return pl.ds(pl.multiple_of(index * size, size), size)


def own_columns(ref, first, me, width):
    if width % LANES == 0:
        return ref[:, pl.ds(pl.multiple_of(first + me * width, LANES), width)].astype(jnp.float32)
    share = LANES // width
    block = ref[:, pl.ds(pl.multiple_of(first + me // share * LANES, LANES), LANES)].astype(
        jnp.float32
    )
    picked = block[:, :width]
    for part in range(1, share):
        picked = jnp.where(me % share == part, block[:, part * width : (part + 1) * width], picked)
    return picked


def head_lanes(shape, head):
    lane = lax.broadcasted_iota(jnp.int32, shape, 1)
    return (lane >= head * HD) & (lane < (head + 1) * HD)


def self_forward_kernel(
    n,
    seg_ref,
    pad_ref,
    tok_ref,
    wq_ref,
    wk_ref,
    wv_ref,
    emb_ref,
    first_ref,
    fbias_ref,
    second_ref,
    sbias_ref,
    mem_ref,
    att_ref,
    qx_out,
    kx_out,
    v_out,
    pk_out,
    pv_out,
    ot_out,
    lse_out,
    mem_out,
    send,
    recv,
    meta_send,
    meta,
    kx,
    qx,
    vt,
    hidden,
    pk,
    pv,
    pvt,
    stat,
    acc,
    o_send,
    o_recv,
    mem_all,
    send_sem,
    recv_sem,
    meta_send_sem,
    meta_recv_sem,
    o_send_sem,
    o_recv_sem,
    mem_send_sem,
    mem_recv_sem,
    out_sem,
):
    me = lax.axis_index("seq")
    length, width = tok_ref.shape
    group = width // n
    heads = group // HD
    plane = 2 * length
    planes = n // 2
    block = 2 * LANES
    per_block = block // group
    blocks = width // block

    def meta_copy(peer, slot):
        return pltpu.make_async_remote_copy(
            src_ref=meta_send,
            dst_ref=meta.at[slot],
            send_sem=meta_send_sem.at[peer],
            recv_sem=meta_recv_sem.at[slot],
            device_id={"seq": peer},
            device_id_type=MESH,
        )

    def qkv_copy(peer, slot):
        return pltpu.make_async_remote_copy(
            src_ref=send.at[peer],
            dst_ref=recv.at[:, rows_of(slot, length), :],
            send_sem=send_sem.at[peer],
            recv_sem=recv_sem.at[slot],
            device_id={"seq": peer},
            device_id_type=MESH,
        )

    def out_copy(peer, slot):
        return pltpu.make_async_remote_copy(
            src_ref=o_send.at[peer],
            dst_ref=o_recv.at[slot],
            send_sem=o_send_sem.at[peer],
            recv_sem=o_recv_sem.at[slot],
            device_id={"seq": peer},
            device_id_type=MESH,
        )

    my_plane = me // 2
    my_side = lax.rem(me, 2)

    def mem_along(peer, slot):
        return remote(
            mem_all.at[slot, my_side],
            mem_all.at[slot, my_side],
            mem_send_sem.at[peer],
            mem_recv_sem.at[slot],
            "seq",
            2 * peer + my_side,
        )

    def mem_across(side):
        return remote(
            mem_all.at[:, side],
            mem_all.at[:, side],
            mem_send_sem.at[planes],
            mem_recv_sem.at[planes],
            "seq",
            me + 1 - 2 * my_side,
        )

    segments = seg_ref[...]
    tags = jnp.where(pad_ref[...] == 1, segments, -1)
    row = lax.broadcasted_iota(jnp.int32, meta_send.shape, 0)
    meta_send[...] = jnp.where(row == 0, segments, tags)
    enter({"seq": n})
    for other in range(n):

        @pl.when(other != me)
        def _():
            meta_copy(other, me).start()

    meta[me] = meta_send[...]

    def project(step, carry):
        here = lax.rem(me // per_block + 1 + step, blocks)
        columns = pl.ds(pl.multiple_of(here * block, block), block)
        for which, weight in enumerate((wq_ref, wk_ref, wv_ref)):
            piece = dot_nn(tok_ref[...], weight[:, columns]).astype(jnp.bfloat16)
            for part in range(per_block):
                send[here * per_block + part, which] = piece[:, part * group : (part + 1) * group]
        for part in range(per_block):
            peer = here * per_block + part

            @pl.when(peer != me)
            def _():
                qkv_copy(peer, me).start()

            @pl.when(peer == me)
            def _():
                recv[:, rows_of(me, length), :] = send[peer]

        return carry

    lax.fori_loop(0, blocks, project, 0)
    mem_all[my_plane, my_side] = mem_ref[...]
    for other in range(planes):

        @pl.when(other != my_plane)
        def _():
            mem_along(other, my_plane).start()

    hidden[...] = jnp.zeros_like(hidden)
    hidden[: emb_ref.shape[0], :] = jnp.tanh(dot_nn(emb_ref[...], first_ref[...]) + fbias_ref[...])
    hidden_low = hidden[...].astype(jnp.bfloat16)
    prefix_key = dot_nn(
        hidden_low, own_columns(second_ref, 0, me, group).astype(jnp.bfloat16)
    ) + own_columns(sbias_ref, 0, me, group)
    prefix_value = dot_nn(
        hidden_low, own_columns(second_ref, width, me, group).astype(jnp.bfloat16)
    ) + own_columns(sbias_ref, width, me, group)
    pk[...] = jnp.zeros_like(pk)
    pk[:, :group] = prefix_key.astype(jnp.bfloat16)
    prefix_row = lax.broadcasted_iota(jnp.int32, (pk.shape[0], LANES), 0)
    pk[:, LANES:] = jnp.where(prefix_row < emb_ref.shape[0], 0.0, masked_score).astype(
        jnp.bfloat16
    )
    pv[...] = prefix_value.astype(jnp.bfloat16)

    def arrive(chunk):
        @pl.when(chunk != me)
        def _():
            meta_copy(chunk, chunk).wait_recv()
            qkv_copy(chunk, chunk).wait_recv()

        here = rows_of(chunk, length)
        state = lax.broadcasted_iota(jnp.int32, (LANES, length), 0)
        is_segment = jnp.where(state == meta[chunk, 0:1, :], 1.0, 0.0)
        is_open = jnp.where(state == meta[chunk, 1:2, :], 0.0, masked_score)
        query_state = is_segment.T.astype(jnp.bfloat16)
        kx[here, :group] = recv[1, here, :]
        kx[here, LANES:] = is_open.T.astype(jnp.bfloat16)
        if group < LANES:
            kx[here, group:LANES] = jnp.zeros((length, LANES - group), jnp.bfloat16)
        query = recv[0, here, :].astype(jnp.float32) * 0.125
        for head in range(heads):
            qx[head, here, :group] = jnp.where(
                head_lanes(query.shape, head), query, 0.0
            ).astype(jnp.bfloat16)
            qx[head, here, LANES:] = query_state
            if group < LANES:
                qx[head, here, group:LANES] = jnp.zeros((length, LANES - group), jnp.bfloat16)
        values = recv[2, here, :].astype(jnp.float32).T.astype(jnp.bfloat16)
        for head in range(heads):
            vt[head, :HD, here] = values[head * HD : (head + 1) * HD, :]

    ones = jnp.ones((SUM_ROWS, length), jnp.bfloat16)
    for chunk in range(n):
        for head in range(heads):
            vt[head, HD:, chunk * length : (chunk + 1) * length] = ones
    pvt[:, :HD, :] = prefix_value.T.astype(jnp.bfloat16).reshape(heads, HD, PREFIX_ROWS)
    pvt[:, HD:, :] = jnp.ones((heads, SUM_ROWS, PREFIX_ROWS), jnp.bfloat16)

    def open_plane(which):
        for head in range(heads):
            scores = dot_nt(pk[...], qx[head, rows_of(which, plane), :])
            top = jnp.max(scores, axis=0, keepdims=True)
            raised = jnp.exp(scores - top)
            stat[which, head : head + 1, :] = top
            acc[which, head] = dot_nn(pvt[head], raised.astype(jnp.bfloat16))

    def pair_part(upper, lower, head, first, count, keys, diagonal):
        here = slice(first, first + count)
        queries = qx[head, pl.ds(pl.multiple_of(upper * plane + first, LANES), count), :]
        key_rows = pl.ds(pl.multiple_of(lower * plane, LANES), keys)
        scores = dot_nt(kx[key_rows, :], queries)
        if diagonal:
            key_at = lax.broadcasted_iota(jnp.int32, scores.shape, 0)
            query_at = lax.broadcasted_iota(jnp.int32, scores.shape, 1) + first
            scores = jnp.where(key_at <= query_at, scores, masked_score)
        old_top = stat[upper, head : head + 1, here]
        top = jnp.maximum(old_top, jnp.max(scores, axis=0, keepdims=True))
        raised = jnp.exp(scores - top).astype(jnp.bfloat16)
        stat[upper, head : head + 1, here] = top
        acc[upper, head, :, here] = acc[upper, head, :, here] * jnp.exp(old_top - top) + dot_nn(
            vt[head, :, key_rows], raised
        )

    def pair(upper, lower):
        for head in range(heads):
            pair_part(upper, lower, head, 0, plane, plane, False)

    def pair_diagonal(which):
        for part in range(2):
            for head in range(heads):
                pair_part(
                    which, which, head, part * length, length, (part + 1) * length, True
                )

    def close_plane(which):
        for head in range(heads):
            total = acc[which, head, HD : HD + 1, :]
            acc[which, head, :HD, :] = acc[which, head, :HD, :] / total
            stat[which, head : head + 1, :] = stat[which, head : head + 1, :] + jnp.log(total)
        for part in range(2):
            chunk = 2 * which + part
            here = slice(part * length, (part + 1) * length)
            o_send[chunk] = jnp.concatenate(
                [acc[which, head, :HD, here] for head in range(heads)], axis=0
            ).T.astype(jnp.bfloat16)

            @pl.when(chunk != me)
            def _():
                out_copy(chunk, me).start()

            @pl.when(chunk == me)
            def _():
                o_recv[me] = o_send[chunk]

    mine = my_plane

    def stage(step, carry):
        here = lax.rem(mine + step, planes)
        arrive(2 * here)
        arrive(2 * here + 1)
        open_plane(here)

        def earlier(back, inner):
            there = lax.rem(mine + back, planes)
            pair(jnp.maximum(here, there), jnp.minimum(here, there))
            return inner

        lax.fori_loop(0, step, earlier, 0)
        pair_diagonal(here)

        @pl.when(step == planes // 2)
        def _():
            for other in range(planes):

                @pl.when(other != my_plane)
                def _():
                    mem_along(other, other).wait_recv()

            mem_across(my_side).start()

        @pl.when((mine + step >= planes) | (mine == 0))
        def _():
            close_plane(here)

        return carry

    lax.fori_loop(0, planes, stage, 0)

    def finish(which, carry):
        close_plane(which)
        return carry

    lax.fori_loop(jnp.where(mine == 0, planes, mine), planes, finish, 0)

    saves = [
        pltpu.make_async_copy(source, target, out_sem.at[index])
        for index, (source, target) in enumerate(
            (
                (qx, qx_out),
                (kx, kx_out),
                (recv.at[2], v_out),
                (pk, pk_out),
                (pv, pv_out),
                (acc, ot_out),
                (stat, lse_out),
            )
        )
    ]
    for save in saves:
        save.start()
    mem_across(1 - my_side).wait_recv()
    save = pltpu.make_async_copy(mem_all, mem_out, out_sem.at[7])
    save.start()
    saves.append(save)
    for other in range(n):

        @pl.when(other != me)
        def _():
            out_copy(other, other).wait_recv()

        att_ref[:, other * group : (other + 1) * group] = o_recv[other]
    for other in range(n):

        @pl.when(other != me)
        def _():
            meta_copy(other, me).wait_send()
            qkv_copy(other, me).wait_send()
            out_copy(other, me).wait_send()

    for other in range(planes):

        @pl.when(other != my_plane)
        def _():
            mem_along(other, my_plane).wait_send()

    mem_across(my_side).wait_send()
    for save in saves:
        save.wait()


def self_forward(n, segments, padding, tokens, weights, prefix, memory):
    length, width = tokens.shape
    group = width // n
    heads = group // HD
    whole = n * length
    planes = n // 2
    low = jnp.bfloat16
    vmem = pl.BlockSpec(memory_space=pltpu.VMEM)
    anywhere = pl.BlockSpec(memory_space=pl.ANY)
    dma = pltpu.SemaphoreType.DMA((n,))
    return pl.pallas_call(
        functools.partial(self_forward_kernel, n),
        out_shape=(
            jax.ShapeDtypeStruct((length, width), low),
            jax.ShapeDtypeStruct((heads, whole, 2 * LANES), low),
            jax.ShapeDtypeStruct((whole, 2 * LANES), low),
            jax.ShapeDtypeStruct((whole, group), low),
            jax.ShapeDtypeStruct((PREFIX_ROWS, 2 * LANES), low),
            jax.ShapeDtypeStruct((PREFIX_ROWS, group), low),
            jax.ShapeDtypeStruct((planes, heads, HD + SUM_ROWS, 2 * length), jnp.float32),
            jax.ShapeDtypeStruct((planes, 8, 2 * length), jnp.float32),
            jax.ShapeDtypeStruct((planes, 2) + memory.shape, low),
        ),
        in_specs=[vmem] * 12,
        out_specs=(vmem,) + (anywhere,) * 8,
        scratch_shapes=[
            pltpu.VMEM((n, 3, length, group), low),
            pltpu.VMEM((3, whole, group), low),
            pltpu.VMEM((8, length), jnp.int32),
            pltpu.VMEM((n, 8, length), jnp.int32),
            pltpu.VMEM((whole, 2 * LANES), low),
            pltpu.VMEM((heads, whole, 2 * LANES), low),
            pltpu.VMEM((heads, HD + SUM_ROWS, whole), low),
            pltpu.VMEM((PREFIX_ROWS, weights[0].shape[0] // 2), jnp.float32),
            pltpu.VMEM((PREFIX_ROWS, 2 * LANES), low),
            pltpu.VMEM((PREFIX_ROWS, group), low),
            pltpu.VMEM((heads, HD + SUM_ROWS, PREFIX_ROWS), low),
            pltpu.VMEM((planes, 8, 2 * length), jnp.float32),
            pltpu.VMEM((planes, heads, HD + SUM_ROWS, 2 * length), jnp.float32),
            pltpu.VMEM((n, length, group), low),
            pltpu.VMEM((n, length, group), low),
            pltpu.VMEM((planes, 2) + memory.shape, low),
            dma,
            dma,
            dma,
            dma,
            dma,
            dma,
            dma,
            dma,
            pltpu.SemaphoreType.DMA((8,)),
        ],
        compiler_params=pltpu.CompilerParams(
            collective_id=0, has_side_effects=True, vmem_limit_bytes=VMEM_BYTES
        ),
        name="self_forward",
    )(segments, padding, tokens, *weights, *prefix, memory)


def self_backward_kernel(
    n,
    batches,
    do_ref,
    base_ref,
    sums_in,
    mem_in,
    vecs_in,
    qx_in,
    kx_in,
    v_in,
    pk_in,
    pv_in,
    ot_in,
    lse_in,
    wq_in,
    wk_in,
    wv_in,
    tg_ref,
    mgrad_ref,
    pkv_ref,
    vecs_ref,
    full_out,
    do_send,
    do_recv,
    qx,
    kx,
    v,
    kt,
    pk,
    pv,
    ot,
    lse,
    weights,
    dom,
    delta,
    dqt,
    dk,
    dv,
    g_send,
    g_recv,
    pre_ref,
    pre_all,
    pre_sum,
    pre_recv,
    full,
    mem_z,
    vec_all,
    vec_sum,
    vec_y,
    vec_both,
    vec_z,
    do_send_sem,
    do_recv_sem,
    g_send_sem,
    g_recv_sem,
    in_sem,
    send_sem,
    recv_sem,
):
    me = lax.axis_index("seq")
    length, width = do_ref.shape
    group = width // n
    heads = group // HD
    plane = 2 * length
    planes = n // 2
    block = 2 * LANES
    per_block = block // group

    def do_copy(peer, slot):
        return pltpu.make_async_remote_copy(
            src_ref=do_send.at[peer],
            dst_ref=do_recv.at[slot],
            send_sem=do_send_sem.at[peer],
            recv_sem=do_recv_sem.at[slot],
            device_id={"seq": peer},
            device_id_type=MESH,
        )

    def g_copy(peer, slot):
        return pltpu.make_async_remote_copy(
            src_ref=g_send.at[peer],
            dst_ref=g_recv.at[slot],
            send_sem=g_send_sem.at[peer],
            recv_sem=g_recv_sem.at[slot],
            device_id={"seq": peer},
            device_id_type=MESH,
        )

    my_batch = lax.axis_index("batch")
    my_core = lax.rem(my_batch, 2)
    my_high = my_batch // 2
    highs = batches // 2
    my_plane = me // 2
    my_side = lax.rem(me, 2)
    beside = me + 1 - 2 * my_side
    slots = iter(range(1000))

    def numbers(count):
        return [next(slots) for _ in range(count)][0]

    e_slot = numbers(1)
    x_slot = numbers(highs)
    core_slot = numbers(1)
    mem_slot = numbers(planes)
    va_slot = numbers(batches)
    vb_slot = numbers(1)
    vc_slot = numbers(planes)
    pa_slot = numbers(batches)
    pb_slot = numbers(n)

    def send(source, target, first, peer_index, slot_index, axis, peer):
        return remote(
            source,
            target,
            send_sem.at[first + peer_index],
            recv_sem.at[first + slot_index],
            axis,
            peer,
        )

    def sum_y(side):
        return send(sums_in, full.at[my_core, my_high, side], e_slot, 0, 0, "seq", beside)

    def sum_x(peer, slot):
        part = full.at[my_core, slot]
        return send(part, part, x_slot, peer, slot, "batch", 2 * peer + my_core)

    def sum_core(core):
        part = full.at[core]
        return send(part, part, core_slot, 0, 0, "batch", my_batch + 1 - 2 * my_core)

    def mem_b(peer, slot):
        return send(
            mem_in.at[peer], mem_z.at[slot], mem_slot, peer, slot, "seq", 2 * peer + my_side
        )

    def vec_a(peer, slot):
        return send(vecs_in, vec_all.at[slot], va_slot, peer, slot, "batch", peer)

    def vec_b(side):
        return send(vec_sum, vec_y.at[side], vb_slot, 0, 0, "seq", beside)

    def vec_c(peer, slot):
        return send(
            vec_both, vec_z.at[slot], vc_slot, peer, slot, "seq", 2 * peer + my_side
        )

    def pre_a(peer, slot):
        return send(pre_ref, pre_all.at[slot], pa_slot, peer, slot, "batch", peer)

    def pre_b(peer, slot):
        return send(pre_sum, pre_recv.at[slot], pb_slot, peer, slot, "seq", peer)

    def others(size, mine, body):
        for other in range(size):

            @pl.when(other != mine)
            def _():
                body(other)

    def added(ref, size, start=0):
        value = ref[start].astype(jnp.float32)
        for other in range(start + 1, size):
            value = value + ref[other].astype(jnp.float32)
        return value

    loads = [
        pltpu.make_async_copy(source, target, in_sem.at[index])
        for index, (source, target) in enumerate(
            (
                (sums_in, full.at[my_core, my_high, my_side]),
                (mem_in.at[my_plane], mem_z.at[my_plane]),
                (vecs_in, vec_all.at[my_batch]),
                (kx_in, kx),
                (pk_in, pk),
                (qx_in, qx),
                (pv_in, pv),
                (v_in, v),
                (ot_in, ot),
                (lse_in, lse),
                (wq_in, weights.at[0]),
                (wk_in, weights.at[1]),
                (wv_in, weights.at[2]),
            )
        )
    ]
    for load in loads:
        load.start()
    for other in range(n):
        do_send[other] = do_ref[:, other * group : (other + 1) * group]
    enter({"seq": n, "batch": batches})
    for other in range(n):

        @pl.when(other != me)
        def _():
            do_copy(other, me).start()

    sum_y(my_side).start()
    others(batches, my_batch, lambda peer: vec_a(peer, my_batch).start())
    others(planes, my_plane, lambda peer: mem_b(peer, my_plane).start())
    do_recv[me] = do_send[me]
    for load in loads[:10]:
        load.wait()

    def turn(chunk, carry):
        here = rows_of(chunk, length)
        kt[:, here] = kx[here, :group].astype(jnp.float32).T.astype(jnp.bfloat16)
        return carry

    lax.fori_loop(0, n, turn, 0)
    pkt = pk[:, :group].astype(jnp.float32).T.astype(jnp.bfloat16)
    dk[...] = jnp.zeros_like(dk)
    dv[...] = jnp.zeros_like(dv)
    pre_ref[...] = jnp.zeros_like(pre_ref)

    def arrive(step, carry):
        which = lax.rem(me // 2 + step, planes)
        for part in range(2):
            chunk = 2 * which + part

            @pl.when(chunk != me)
            def _():
                do_copy(chunk, chunk).wait_recv()

            grads = do_recv[chunk].astype(jnp.float32)
            for head in range(heads):
                dom[head, rows_of(chunk, length), :] = jnp.where(
                    head_lanes(grads.shape, head), grads, 0.0
                ).astype(jnp.bfloat16)
            here = slice(part * length, (part + 1) * length)
            turned = grads.T
            for head in range(heads):
                delta[which, head : head + 1, here] = jnp.sum(
                    turned[head * HD : (head + 1) * HD] * ot[which, head, :HD, here],
                    axis=0,
                    keepdims=True,
                )
        for head in range(heads):
            span = slice(head * HD, (head + 1) * HD)
            queries = qx[head, rows_of(which, plane), :]
            grads = dom[head, rows_of(which, plane), :]
            weight = jnp.exp(dot_nt(pk[...], queries) - lse[which, head : head + 1, :])
            slope = weight * (dot_nt(pv[...], grads) - delta[which, head : head + 1, :])
            slope = slope.astype(jnp.bfloat16)
            pre_ref[0] += dot_nn(slope, queries[:, :group])
            pre_ref[1] += dot_nn(weight.astype(jnp.bfloat16), grads)
            dqt[which, span, :] = dot_nn(pkt[span, :], slope)
        return carry

    lax.fori_loop(0, planes, arrive, 0)

    def stage_a():
        others(batches, my_batch, lambda peer: pre_a(peer, my_batch).start())
        pre_all[my_batch] = pre_ref[...]
        sum_y(1 - my_side).wait_recv()
        others(highs, my_high, lambda peer: sum_x(peer, my_high).start())
        others(batches, my_batch, lambda peer: vec_a(peer, peer).wait_recv())
        vec_sum[...] = added(vec_all, batches)
        vec_b(my_side).start()
        vec_y[my_side] = vec_sum[...]

    def stage_b():
        others(batches, my_batch, lambda peer: pre_a(peer, peer).wait_recv())
        pre_sum[...] = added(pre_all, batches)
        others(n, me, lambda peer: pre_b(peer, me).start())
        pre_recv[me] = pre_sum[...]
        vec_b(1 - my_side).wait_recv()
        vec_both[...] = vec_y[0] + vec_y[1]
        others(planes, my_plane, lambda peer: vec_c(peer, my_plane).start())
        vec_z[my_plane] = vec_both[...]
        others(highs, my_high, lambda peer: sum_x(peer, peer).wait_recv())
        sum_core(my_core).start()

    def stage_c():
        others(planes, my_plane, lambda peer: mem_b(peer, peer).wait_recv())
        mgrad_ref[...] = added(mem_z, planes).astype(jnp.bfloat16)
        others(planes, my_plane, lambda peer: vec_c(peer, peer).wait_recv())
        vecs_ref[...] = added(vec_z, planes)

    def stage_d():
        sum_core(1 - my_core).wait_recv()
        save_full.start()
        for other in range(n):

            @pl.when(other != me)
            def _():
                pre_b(other, other).wait_recv()

            for which in range(2):
                pkv_ref[
                    :, which * width + other * group : which * width + (other + 1) * group
                ] = pre_recv[other, which]

    save_full = pltpu.make_async_copy(full, full_out, in_sem.at[0])

    def pair(upper, lower, diagonal):
        for part in range(2):
            first = length if diagonal and part == 1 else 0
            keys = pl.ds(pl.multiple_of(lower * plane + part * length, length), length)
            key_sum = None
            for head in range(heads):
                span = slice(head * HD, (head + 1) * HD)
                here = pl.ds(pl.multiple_of(upper * plane + first, length), plane - first)
                queries = qx[head, here, :]
                grads = dom[head, here, :]
                scores = dot_nt(kx[keys, :], queries)
                weight = jnp.exp(scores - lse[upper, head : head + 1, first:])
                if diagonal:
                    key_at = lax.broadcasted_iota(jnp.int32, scores.shape, 0)
                    query_at = lax.broadcasted_iota(jnp.int32, scores.shape, 1)
                    weight = jnp.where(key_at <= query_at, weight, 0.0)
                slope = weight * (dot_nt(v[keys, :], grads) - delta[upper, head : head + 1, first:])
                slope = slope.astype(jnp.bfloat16)
                key_part = dot_nn(slope, qx[head, here, :group])
                value_part = dot_nn(weight.astype(jnp.bfloat16), grads)
                if key_sum is None:
                    key_sum, value_sum = key_part, value_part
                else:
                    key_sum, value_sum = key_sum + key_part, value_sum + value_part
                dqt[upper, span, first:] += dot_nn(kt[span, keys], slope)
            dk[keys, :] += key_sum
            dv[keys, :] += value_sum

    def hand_over(which):
        for part in range(2):
            chunk = 2 * which + part
            here = rows_of(chunk, length)
            g_send[chunk, 0] = (
                (dqt[which, :, part * length : (part + 1) * length] * 0.125)
                .T.astype(jnp.bfloat16)
            )
            g_send[chunk, 1] = dk[here, :].astype(jnp.bfloat16)
            g_send[chunk, 2] = dv[here, :].astype(jnp.bfloat16)

            @pl.when(chunk != me)
            def _():
                g_copy(chunk, me).start()

            @pl.when(chunk == me)
            def _():
                g_recv[me] = g_send[chunk]

    rising = lax.rem(me, 2) == 0
    stage_a()

    def stage(step, carry):
        here = jnp.where(rising, step, planes - 1 - step)

        def far(index, inner):
            there = jnp.where(rising, here + 1 + index, index)
            pair(jnp.maximum(here, there), jnp.minimum(here, there), False)
            return inner

        lax.fori_loop(0, planes - 1 - step, far, 0)
        pair(here, here, True)
        hand_over(here)
        for at, body in enumerate((stage_b, stage_c, stage_d)):
            pl.when(step == at)(body)
        return carry

    lax.fori_loop(0, planes, stage, 0)
    for load in loads[10:]:
        load.wait()
    total = base_ref[...]
    for here in range(width // block):
        pieces = []
        for part in range(per_block):
            other = here * per_block + part

            @pl.when(other != me)
            def _():
                g_copy(other, other).wait_recv()

        for which in range(3):
            piece = jnp.concatenate(
                [g_recv[here * per_block + part, which] for part in range(per_block)], axis=1
            )
            pieces.append(
                dot_nt(piece, weights[which, :, here * block : (here + 1) * block])
            )
        total = total + (pieces[0] + pieces[1] + pieces[2])
    tg_ref[...] = total.astype(jnp.bfloat16)
    others(n, me, lambda peer: do_copy(peer, me).wait_send())
    others(n, me, lambda peer: g_copy(peer, me).wait_send())
    others(n, me, lambda peer: pre_b(peer, me).wait_send())
    others(batches, my_batch, lambda peer: pre_a(peer, my_batch).wait_send())
    others(batches, my_batch, lambda peer: vec_a(peer, my_batch).wait_send())
    others(highs, my_high, lambda peer: sum_x(peer, my_high).wait_send())
    others(planes, my_plane, lambda peer: vec_c(peer, my_plane).wait_send())
    others(planes, my_plane, lambda peer: mem_b(peer, my_plane).wait_send())
    sum_y(my_side).wait_send()
    sum_core(my_core).wait_send()
    vec_b(my_side).wait_send()
    save_full.wait()


def self_backward(n, batches, out_grad, first_grad, sums, memory_part, vecs, saved, weights):
    length, width = out_grad.shape
    group = width // n
    heads = group // HD
    whole = n * length
    planes = n // 2
    low = jnp.bfloat16
    vmem = pl.BlockSpec(memory_space=pltpu.VMEM)
    anywhere = pl.BlockSpec(memory_space=pl.ANY)
    dma = pltpu.SemaphoreType.DMA((n,))
    sum_rows = sums.shape[1]
    mem_rows = memory_part.shape[1]
    vec = pltpu.VMEM((8, width), jnp.float32)
    copies = 2 + batches // 2 + 1 + 2 * planes + 2 * batches + n
    return pl.pallas_call(
        functools.partial(self_backward_kernel, n, batches),
        out_shape=(
            jax.ShapeDtypeStruct((length, width), low),
            jax.ShapeDtypeStruct((mem_rows, width), low),
            jax.ShapeDtypeStruct((PREFIX_ROWS, 2 * width), jnp.float32),
            jax.ShapeDtypeStruct((8, width), jnp.float32),
            jax.ShapeDtypeStruct((2, batches // 2, 2, planes, sum_rows, LANES), low),
        ),
        in_specs=[vmem, vmem] + [anywhere] * 13,
        out_specs=(vmem, vmem, vmem, vmem, anywhere),
        scratch_shapes=[
            pltpu.VMEM((n, length, group), low),
            pltpu.VMEM((n, length, group), low),
            pltpu.VMEM((heads, whole, 2 * LANES), low),
            pltpu.VMEM((whole, 2 * LANES), low),
            pltpu.VMEM((whole, group), low),
            pltpu.VMEM((group, whole), low),
            pltpu.VMEM((PREFIX_ROWS, 2 * LANES), low),
            pltpu.VMEM((PREFIX_ROWS, group), low),
            pltpu.VMEM((planes, heads, HD + SUM_ROWS, 2 * length), jnp.float32),
            pltpu.VMEM((planes, 8, 2 * length), jnp.float32),
            pltpu.VMEM((3, width, width), low),
            pltpu.VMEM((heads, whole, group), low),
            pltpu.VMEM((planes, 8, 2 * length), jnp.float32),
            pltpu.VMEM((planes, group, 2 * length), jnp.float32),
            pltpu.VMEM((whole, group), jnp.float32),
            pltpu.VMEM((whole, group), jnp.float32),
            pltpu.VMEM((n, 3, length, group), low),
            pltpu.VMEM((n, 3, length, group), low),
            pltpu.VMEM((2, PREFIX_ROWS, group), jnp.float32),
            pltpu.VMEM((batches, 2, PREFIX_ROWS, group), jnp.float32),
            pltpu.VMEM((2, PREFIX_ROWS, group), jnp.float32),
            pltpu.VMEM((n, 2, PREFIX_ROWS, group), jnp.float32),
            pltpu.VMEM((2, batches // 2, 2, planes, sum_rows, LANES), low),
            pltpu.VMEM((planes, mem_rows, width), low),
            pltpu.VMEM((batches, 8, width), jnp.float32),
            vec,
            pltpu.VMEM((2, 8, width), jnp.float32),
            vec,
            pltpu.VMEM((planes, 8, width), jnp.float32),
            dma,
            dma,
            dma,
            dma,
            pltpu.SemaphoreType.DMA((13,)),
            pltpu.SemaphoreType.DMA((copies,)),
            pltpu.SemaphoreType.DMA((copies,)),
        ],
        compiler_params=pltpu.CompilerParams(
            collective_id=1, has_side_effects=True, vmem_limit_bytes=VMEM_BYTES
        ),
        name="self_backward",
    )(
        out_grad,
        first_grad,
        sums,
        memory_part,
        vecs,
        *saved,
        *weights,
    )


def both_parts(value):
    high = value.astype(jnp.bfloat16).astype(jnp.float32)
    return jnp.concatenate([high, value - high], axis=0).astype(jnp.bfloat16)


def finish_kernel(
    full_ref,
    vecs_ref,
    pkv_ref,
    emb_ref,
    first_ref,
    fbias_ref,
    second_ref,
    embed_out,
    first_out,
    fbias_out,
    second_out,
    sbias_out,
    down_out,
    dbias_out,
    raise_out,
    rbias_out,
    gain_out,
    shift_out,
    first_grad,
    second_grad,
    down_grad,
    raise_grad,
    emb,
    hidden,
    out_sem,
):
    f32 = jnp.float32
    low = jnp.bfloat16
    width = emb_ref.shape[1]
    down = dbias_out.shape[1]
    count = emb_ref.shape[0]
    saves = []

    def save(source, target, rows=None):
        if rows is not None:
            source, target = source.at[rows], target.at[rows]
        copy = pltpu.make_async_copy(source, target, out_sem.at[len(saves)])
        copy.start()
        saves.append(copy)

    first = down * width // LANES
    for index in range(width // LANES):
        raise_grad[:, index * LANES : (index + 1) * LANES] = full_ref[
            first + index * down : first + (index + 1) * down, :
        ].astype(f32)
    save(raise_grad, raise_out)
    for index in range(down // LANES):
        down_grad[:, index * LANES : (index + 1) * LANES] = full_ref[
            index * width : (index + 1) * width, :
        ].astype(f32)
    save(down_grad, down_out)
    emb[...] = jnp.zeros_like(emb)
    emb[:count, :] = emb_ref[...].astype(f32)
    emb_low = emb[...].astype(low)
    row = lax.broadcasted_iota(jnp.int32, hidden.shape, 0)
    hidden[...] = jnp.where(
        row < count, jnp.tanh(dot_nn(emb_low, first_ref[...]) + fbias_ref[...]), 0.0
    )
    value = hidden[...]
    prefix = pkv_ref[...]
    parts = both_parts(prefix)
    hidden_twice = jnp.concatenate([value, value], axis=0).T.astype(low)
    tile = 128
    for index in range(second_grad.shape[0] // tile):
        here = slice(index * tile, (index + 1) * tile)
        second_grad[here, :] = dot_nn(hidden_twice[here, :], parts)
        save(second_grad, second_out, here)
    sbias_out[...] = jnp.sum(prefix, axis=0, keepdims=True)
    grad = dot_nt(parts, second_ref[...])
    grad = (grad[:PREFIX_ROWS] + grad[PREFIX_ROWS:]) * (1.0 - value * value)
    fbias_out[...] = jnp.sum(grad, axis=0, keepdims=True)
    parts = both_parts(grad)
    emb_twice = jnp.concatenate([emb[...], emb[...]], axis=0).T.astype(low)
    first_grad[...] = dot_nn(emb_twice, parts)
    save(first_grad, first_out)
    back = dot_nt(parts, first_ref[...])
    embed_out[...] = (back[:PREFIX_ROWS] + back[PREFIX_ROWS:])[:count, :]
    rbias_out[...] = vecs_ref[0:1, :]
    dbias_out[...] = vecs_ref[1:2, :down]
    gain_out[...] = vecs_ref[2:5, :]
    shift_out[...] = vecs_ref[5:8, :]
    for copy in saves:
        copy.wait()


def finish(full, vecs, prefix_grad, embed, first, first_bias, second, down):
    f32 = jnp.float32
    count, width = embed.shape
    hidden = first.shape[1]
    vmem = pl.BlockSpec(memory_space=pltpu.VMEM)
    anywhere = pl.BlockSpec(memory_space=pl.ANY)
    shapes = (
        (count, width),
        (width, hidden),
        (1, hidden),
        (hidden, 2 * width),
        (1, 2 * width),
        (width, down),
        (1, down),
        (down, width),
        (1, width),
        (3, width),
        (3, width),
    )
    return pl.pallas_call(
        finish_kernel,
        out_shape=tuple(jax.ShapeDtypeStruct(shape, f32) for shape in shapes),
        in_specs=[vmem] * 7,
        out_specs=(
            vmem,
            anywhere,
            vmem,
            anywhere,
            vmem,
            anywhere,
            vmem,
            anywhere,
            vmem,
            vmem,
            vmem,
        ),
        scratch_shapes=[
            pltpu.VMEM((width, hidden), f32),
            pltpu.VMEM((hidden, 2 * width), f32),
            pltpu.VMEM((width, down), f32),
            pltpu.VMEM((down, width), f32),
            pltpu.VMEM((PREFIX_ROWS, width), f32),
            pltpu.VMEM((PREFIX_ROWS, hidden), f32),
            pltpu.SemaphoreType.DMA((3 + hidden // 128,)),
        ],
        compiler_params=pltpu.CompilerParams(vmem_limit_bytes=VMEM_BYTES),
        name="finish",
    )(full, vecs, prefix_grad, embed, first, first_bias, second)


def gelu_pair(value):
    scaled = jnp.abs(value) * 0.7071067811865476
    step = 1.0 / (1.0 + 0.3275911 * scaled)
    bell = jnp.exp(-scaled * scaled)
    poly = step * (
        0.254829592
        + step
        * (-0.284496736 + step * (1.421413741 + step * (-1.453152027 + step * 1.061405429)))
    )
    tail = 0.5 * poly * bell
    share = jnp.where(value >= 0.0, 1.0 - tail, tail)
    return value * share, share + value * (bell * 0.3989422804014327)


def normed(value):
    center = jnp.mean(value, axis=-1, keepdims=True)
    centered = value - center
    scale = lax.rsqrt(jnp.mean(centered * centered, axis=-1, keepdims=True) + norm_eps)
    return centered * scale, scale


def norm_back(grad, scale, unit):
    return scale * (
        grad
        - jnp.mean(grad, axis=-1, keepdims=True)
        - unit * jnp.mean(grad * unit, axis=-1, keepdims=True)
    )


def middle_kernel(
    n,
    batches,
    tok_ref,
    att_ref,
    cot_ref,
    mem_ref,
    gain_ref,
    shift_ref,
    dbias_ref,
    rbias_ref,
    wo_in,
    wcq_in,
    wck_in,
    wcv_in,
    wco_in,
    wd_in,
    wr_in,
    win_in,
    wout_in,
    out_ref,
    fgrad_ref,
    ograd_ref,
    mem_out,
    sums_out,
    vecs_ref,
    wo,
    wcq,
    wck,
    wcv,
    wco,
    wd,
    wr,
    win,
    wout,
    unit_one,
    unit_two,
    work,
    total,
    scale_one,
    scale_two,
    low_one,
    low_two,
    low_three,
    query,
    crossed,
    mem_key,
    mem_value,
    weights,
    slopes,
    pre_now,
    down_act,
    down_slope,
    down_grad,
    sums_ref,
    sums_core,
    sums_x,
    sums_y,
    sums_z,
    sums_full,
    mpart,
    mem_y,
    load_sem,
    win_sem,
    wout_sem,
    send_sem,
    recv_sem,
):
    length, width = tok_ref.shape
    mem_len = mem_ref.shape[0]
    tile = win.shape[2]
    tiles = win_in.shape[1] // tile
    rows_step = 128
    low = jnp.bfloat16
    f32 = jnp.float32

    me = lax.axis_index("seq")
    planes = n // 2
    my_plane = me // 2
    my_side = lax.rem(me, 2)
    beside = me + 1 - 2 * my_side
    my_batch = lax.axis_index("batch")
    my_core = lax.rem(my_batch, 2)
    my_high = my_batch // 2
    highs = batches // 2
    mem_rows = mem_len // n
    half_rows = sums_ref.shape[0] // 2
    x_rows = half_rows // highs
    y_rows = x_rows // 2
    z_rows = y_rows // planes
    core_row = pl.multiple_of(my_core * half_rows, half_rows)
    x_row = pl.multiple_of(core_row + my_high * x_rows, x_rows)
    y_row = pl.multiple_of(x_row + my_side * y_rows, y_rows)
    z_row = pl.multiple_of(y_row + my_plane * z_rows, z_rows)

    def others(size, mine, body):
        for other in range(size):

            @pl.when(other != mine)
            def _():
                body(other)

    def send(source, target, first, peer_index, slot_index, axis, peer):
        return remote(
            source,
            target,
            send_sem.at[first + peer_index],
            recv_sem.at[first + slot_index],
            axis,
            peer,
        )

    def part(row, count):
        return sums_ref.at[pl.ds(pl.multiple_of(row, count), count)]

    def sum_core():
        return send(
            part((1 - my_core) * half_rows, half_rows),
            sums_core,
            0,
            0,
            0,
            "batch",
            my_batch + 1 - 2 * my_core,
        )

    def sum_x(peer, slot):
        return send(
            part(core_row + peer * x_rows, x_rows),
            sums_x.at[slot],
            3,
            peer,
            slot,
            "batch",
            2 * peer + my_core,
        )

    def sum_y():
        return send(
            part(x_row + (1 - my_side) * y_rows, y_rows), sums_y, 1, 0, 0, "seq", beside
        )

    def sum_z(peer, slot):
        return send(
            part(y_row + peer * z_rows, z_rows),
            sums_z.at[slot],
            3 + highs,
            peer,
            slot,
            "seq",
            2 * peer + my_side,
        )

    def sum_back(peer, slot):
        return send(
            sums_full.at[slot],
            sums_full.at[slot],
            3 + highs + planes,
            peer,
            slot,
            "seq",
            2 * peer + my_side,
        )

    def mem_across():
        return send(mpart.at[:, 1 - my_side], mem_y, 2, 0, 0, "seq", beside)

    def added(first, ref):
        return (first.astype(f32) + ref.astype(f32)).astype(low)

    def stage_core():
        sum_core().wait_recv()
        here = pl.ds(core_row, half_rows)
        sums_ref[here] = added(sums_ref[here], sums_core[...])
        others(highs, my_high, lambda peer: sum_x(peer, my_high).start())

    def stage_x():
        here = pl.ds(x_row, x_rows)
        value = sums_ref[here].astype(f32)
        others(highs, my_high, lambda peer: sum_x(peer, peer).wait_recv())
        sums_x[my_high] = jnp.zeros((x_rows, LANES), low)
        for other in range(highs):
            value = value + sums_x[other].astype(f32)
        sums_ref[here] = value.astype(low)
        sum_y().start()

    def stage_y():
        sum_y().wait_recv()
        here = pl.ds(y_row, y_rows)
        sums_ref[here] = added(sums_ref[here], sums_y[...])
        others(planes, my_plane, lambda peer: sum_z(peer, my_plane).start())

    def stage_z():
        value = sums_ref[pl.ds(z_row, z_rows)].astype(f32)
        others(planes, my_plane, lambda peer: sum_z(peer, peer).wait_recv())
        sums_z[my_plane] = jnp.zeros((z_rows, LANES), low)
        for other in range(planes):
            value = value + sums_z[other].astype(f32)
        sums_full[my_plane] = value.astype(low)
        others(planes, my_plane, lambda peer: sum_back(peer, my_plane).start())

    sources = (wo_in, wcq_in, wck_in, wcv_in, wco_in, wd_in, wr_in)
    targets = (wo, wcq, wck, wcv, wco, wd, wr)
    loads = [
        pltpu.make_async_copy(source, target, load_sem.at[index])
        for index, (source, target) in enumerate(zip(sources, targets))
    ]

    def win_load(which):
        slot = lax.rem(which, 2)
        return pltpu.make_async_copy(
            win_in.at[:, rows_of(which, tile)], win.at[slot], win_sem.at[slot]
        )

    def wout_load(which):
        slot = lax.rem(which, 2)
        return pltpu.make_async_copy(
            wout_in.at[rows_of(which, tile), :], wout.at[slot], wout_sem.at[slot]
        )

    for load in loads[:5]:
        load.start()
    for which in range(2):
        win_load(which).start()
        wout_load(which).start()
    for load in loads[5:]:
        load.start()
    enter({"seq": n, "batch": batches})

    def by_columns(extent, step, body):
        def one(index, carry):
            body(pl.ds(pl.multiple_of(index * step, step), step))
            return carry

        lax.fori_loop(0, extent // step, one, 0)

    def by_rows(body, init=0):
        def one(index, carry):
            return body(rows_of(index, rows_step), carry)

        return lax.fori_loop(0, length // rows_step, one, init)

    cols = 512
    half = width // 2

    loads[0].wait()

    def project_out(here):
        work[:, here] = tok_ref[:, here].astype(f32) + dot_nn(att_ref[...], wo[:, here])

    by_columns(width, cols, project_out)

    def first_norm(here, carry):
        unit, scale = normed(work[here, :])
        unit_one[here, :] = unit
        scale_one[here, :] = scale
        value = unit * gain_ref[0:1, :] + shift_ref[0:1, :]
        work[here, :] = value
        low_one[here, :] = value.astype(low)
        return carry

    by_rows(first_norm)

    loads[1].wait()

    def project_query(here):
        query[:, here] = dot_nn(low_one[...], wcq[:, here]).astype(low)

    by_columns(width, cols, project_query)
    loads[2].wait()
    loads[3].wait()

    def project_memory(here):
        mem_key[:, here] = dot_nn(mem_ref[...], wck[:, here]).astype(low)
        mem_value[:, here] = dot_nn(mem_ref[...], wcv[:, here]).astype(low)

    by_columns(width, cols, project_memory)

    per_block = LANES // HD

    def head_queries(here, head):
        both = query[:, here].astype(f32) * 0.125
        return jnp.where(head_lanes(both.shape, head), both, 0.0).astype(low)

    def cross_forward(block):
        here = rows_of(block, LANES)
        keys = mem_key[:, here]
        values = mem_value[:, here].astype(f32).T.astype(low)
        outs = []
        for head in range(per_block):
            scores = dot_nt(keys, head_queries(here, head))
            raised = jnp.exp(scores - jnp.max(scores, axis=0, keepdims=True))
            share = 1.0 / jnp.sum(raised, axis=0, keepdims=True)
            weight = (raised * share).astype(low)
            weights[block * per_block + head] = weight
            outs.append(dot_nn(values[head * HD : (head + 1) * HD, :], weight))
        crossed[:, here] = jnp.concatenate(outs, axis=0).T.astype(low)

    def cross_forward_both(step, carry):
        cross_forward(2 * step)
        cross_forward(2 * step + 1)
        return carry

    lax.fori_loop(0, width // LANES // 2, cross_forward_both, 0)

    loads[4].wait()

    def project_crossed(here):
        work[:, here] += dot_nn(crossed[...], wco[:, here])

    by_columns(width, cols, project_crossed)

    def second_norm(here, carry):
        unit, scale = normed(work[here, :])
        unit_two[here, :] = unit
        scale_two[here, :] = scale
        value = unit * gain_ref[1:2, :] + shift_ref[1:2, :]
        work[here, :] = value
        low_two[here, :] = value.astype(low)
        return carry

    by_rows(second_norm)

    total[...] = jnp.zeros_like(total)

    win_load(0).wait()
    pre_now[...] = dot_nn(low_two[...], win[0])

    def feed_forward(which, carry):
        slot = lax.rem(which, 2)
        ahead = lax.rem(which + 1, tiles)

        @pl.when(which + 1 < tiles)
        def _():
            win_load(which + 1).wait()

        wout_load(which).wait()
        pre = pre_now[...]
        pre_now[...] = dot_nn(low_two[...], win[lax.rem(ahead, 2)])
        act, slope = gelu_pair(pre)
        slopes[:, rows_of(which, tile)] = slope.astype(low)
        total[...] += dot_nn(act.astype(low), wout[slot])

        @pl.when(which + 2 < tiles)
        def _():
            win_load(which + 2).start()
            wout_load(which + 2).start()

        return carry

    lax.fori_loop(0, tiles, feed_forward, 0)
    loads[5].wait()
    loads[6].wait()
    act, slope = gelu_pair(dot_nn(low_two[...], wd[...]) + dbias_ref[...])
    down_act[...] = act.astype(low)
    down_slope[...] = slope.astype(low)

    def project_raise(here):
        work[:, here] += total[:, here] + 4.0 * (
            dot_nn(down_act[...], wr[:, here]) + rbias_ref[:, here]
        )

    by_columns(width, cols, project_raise)
    nothing = jnp.zeros((1, width), f32)

    def third_norm(here, carry):
        gain_sum, shift_sum, bias_sum = carry
        unit, scale = normed(work[here, :])
        gain = gain_ref[2:3, :]
        out_ref[here, :] = (unit * gain + shift_ref[2:3, :]).astype(low)
        grad = cot_ref[here, :].astype(f32)
        back = norm_back(grad * gain, scale, unit)
        total[here, :] = back
        back_low = back.astype(low)
        low_three[here, :] = back_low
        return (
            gain_sum + jnp.sum(grad * unit, axis=0, keepdims=True),
            shift_sum + jnp.sum(grad, axis=0, keepdims=True),
            bias_sum + jnp.sum(back_low.astype(f32), axis=0, keepdims=True),
        )

    gain_three, shift_three, bias_sum = by_rows(third_norm, (nothing, nothing, nothing))
    vecs_ref[0:1, :] = 4.0 * bias_sum

    back = 4.0 * dot_nt(low_three[...], wr[...]) * down_slope[...].astype(f32)
    back_low = back.astype(low)
    down_grad[...] = back_low
    vecs_ref[1:2, :] = jnp.concatenate(
        [
            jnp.sum(back_low.astype(f32), axis=0, keepdims=True),
            jnp.zeros((1, width - wd.shape[1]), f32),
        ],
        axis=1,
    )
    down = wd.shape[1]
    raise_sum = 4.0 * dot_tn(down_act[...], low_three[...])
    for index in range(width // LANES):
        sums_ref[pl.ds(down * width // LANES + index * down, down), :] = raise_sum[
            :, index * LANES : (index + 1) * LANES
        ].astype(low)
    down_sum = dot_tn(low_two[...], down_grad[...])
    for index in range(down // LANES):
        sums_ref[index * width : (index + 1) * width, :] = down_sum[
            :, index * LANES : (index + 1) * LANES
        ].astype(low)

    sum_core().start()

    def feed_backward(step, carry):
        which = tiles - 1 - step
        slot = lax.rem(which, 2)
        here = rows_of(which, tile)

        @pl.when(which < tiles - 2)
        def _():
            wout_load(which).wait()
            win_load(which).wait()

        grad = dot_nt(low_three[...], wout[slot]) * slopes[:, here].astype(f32)
        total[...] += dot_nt(grad.astype(low), win[slot])

        @pl.when(which >= 2)
        def _():
            win_load(which - 2).start()
            wout_load(which - 2).start()

        pl.when(step == tiles // 4)(stage_core)
        return carry

    lax.fori_loop(0, tiles, feed_backward, 0)

    def down_back(here):
        total[:, here] += dot_nt(down_grad[...], wd[here, :])

    by_columns(width, cols, down_back)

    def second_back(here, carry):
        gain_sum, shift_sum = carry
        grad = total[here, :]
        unit = unit_two[here, :]
        back = norm_back(grad * gain_ref[1:2, :], scale_two[here, :], unit)
        total[here, :] = back
        low_one[here, :] = back.astype(low)
        return (
            gain_sum + jnp.sum(grad * unit, axis=0, keepdims=True),
            shift_sum + jnp.sum(grad, axis=0, keepdims=True),
        )

    gain_two, shift_two = by_rows(second_back, (nothing, nothing))

    def crossed_back(here):
        crossed[:, here] = dot_nt(low_one[...], wco[here, :]).astype(low)

    by_columns(width, cols, crossed_back)

    def cross_backward(block):
        here = rows_of(block, LANES)
        values = mem_value[:, here]
        keys = mem_key[:, here].astype(f32).T.astype(low)
        grads = crossed[:, here].astype(f32)
        outs = []
        key_sum = None
        for head in range(per_block):
            grad = jnp.where(head_lanes(grads.shape, head), grads, 0.0).astype(low)
            weight_low = weights[block * per_block + head]
            weight = weight_low.astype(f32)
            slope = dot_nt(values, grad)
            slope = weight * (slope - jnp.sum(weight * slope, axis=0, keepdims=True))
            slope = slope.astype(low)
            key_part = dot_nn(slope, head_queries(here, head))
            value_part = dot_nn(weight_low, grad)
            if key_sum is None:
                key_sum, value_sum = key_part, value_part
            else:
                key_sum, value_sum = key_sum + key_part, value_sum + value_part
            outs.append(dot_nn(keys[head * HD : (head + 1) * HD, :], slope))
        mem_key[:, here] = key_sum.astype(low)
        mem_value[:, here] = value_sum.astype(low)
        query[:, here] = (jnp.concatenate(outs, axis=0) * 0.125).T.astype(low)

    def cross_backward_both(step, carry):
        cross_backward(2 * step)
        cross_backward(2 * step + 1)
        pl.when(step == 2)(stage_y)
        return carry

    stage_x()
    lax.fori_loop(0, width // LANES // 2, cross_backward_both, 0)
    stage_z()

    def memory_back(here):
        mpart[:, :, :, here] = (
            (dot_nt(mem_key[...], wck[here, :]) + dot_nt(mem_value[...], wcv[here, :]))
            .astype(low)
            .reshape(planes, 2, mem_rows, cols)
        )

    by_columns(width, cols, memory_back)
    mem_across().start()

    def query_back(here):
        total[:, here] += dot_nt(query[...], wcq[here, :])

    by_columns(width, cols, query_back)

    def first_back(here, carry):
        gain_sum, shift_sum = carry
        grad = total[here, :]
        unit = unit_one[here, :]
        back = norm_back(grad * gain_ref[0:1, :], scale_one[here, :], unit)
        fgrad_ref[here, :] = back
        low_one[here, :] = back.astype(low)
        return (
            gain_sum + jnp.sum(grad * unit, axis=0, keepdims=True),
            shift_sum + jnp.sum(grad, axis=0, keepdims=True),
        )

    gain_one, shift_one = by_rows(first_back, (nothing, nothing))

    def out_back(here):
        ograd_ref[:, here] = dot_nt(low_one[...], wo[here, :]).astype(low)

    by_columns(width, cols, out_back)
    for index, vector in enumerate(
        (gain_one, gain_two, gain_three, shift_one, shift_two, shift_three)
    ):
        vecs_ref[2 + index : 3 + index, :] = vector
    mem_across().wait_recv()
    mem_out[...] = added(mpart[:, my_side], mem_y[...])
    others(planes, my_plane, lambda peer: sum_back(peer, peer).wait_recv())
    sums_out[...] = sums_full[...]
    sum_core().wait_send()
    sum_y().wait_send()
    mem_across().wait_send()
    others(highs, my_high, lambda peer: sum_x(peer, my_high).wait_send())
    others(planes, my_plane, lambda peer: sum_z(peer, my_plane).wait_send())
    others(planes, my_plane, lambda peer: sum_back(peer, my_plane).wait_send())


def middle(tokens, attended, cotangent, memory, gains, shifts, down_bias, raise_bias, weights, n, batches):
    length, width = tokens.shape
    mem_len = memory.shape[0]
    down = weights[5].shape[1]
    feed = weights[7].shape[1]
    tile = 512 if mem_len <= 512 else 128
    low = jnp.bfloat16
    f32 = jnp.float32
    vmem = pl.BlockSpec(memory_space=pltpu.VMEM)
    anywhere = pl.BlockSpec(memory_space=pl.ANY)
    planes = n // 2
    sum_rows = 2 * down * width // LANES
    z_rows = sum_rows // (n * batches)
    copies = 3 + batches // 2 + 2 * planes
    square = pltpu.VMEM((width, width), low)
    wide = pltpu.VMEM((length, width), f32)
    narrow = pltpu.VMEM((length, width), low)
    mem_low = pltpu.VMEM((mem_len, width), low)
    return pl.pallas_call(
        functools.partial(middle_kernel, n, batches),
        out_shape=(
            jax.ShapeDtypeStruct((length, width), low),
            jax.ShapeDtypeStruct((length, width), f32),
            jax.ShapeDtypeStruct((length, width), low),
            jax.ShapeDtypeStruct((planes, mem_len // n, width), low),
            jax.ShapeDtypeStruct((planes, z_rows, LANES), low),
            jax.ShapeDtypeStruct((8, width), f32),
        ),
        in_specs=[vmem] * 8 + [anywhere] * 9,
        out_specs=(vmem,) * 6,
        scratch_shapes=[
            square,
            square,
            square,
            square,
            square,
            pltpu.VMEM((width, down), low),
            pltpu.VMEM((down, width), low),
            pltpu.VMEM((2, width, tile), low),
            pltpu.VMEM((2, tile, width), low),
            wide,
            wide,
            wide,
            wide,
            pltpu.VMEM((length, 1), f32),
            pltpu.VMEM((length, 1), f32),
            narrow,
            narrow,
            narrow,
            narrow,
            narrow,
            mem_low,
            mem_low,
            pltpu.VMEM((H, mem_len, length), low),
            pltpu.VMEM((length, feed), low),
            pltpu.VMEM((length, tile), f32),
            pltpu.VMEM((length, down), low),
            pltpu.VMEM((length, down), low),
            pltpu.VMEM((length, down), low),
            pltpu.VMEM((sum_rows, LANES), low),
            pltpu.VMEM((sum_rows // 2, LANES), low),
            pltpu.VMEM((batches // 2, sum_rows // batches, LANES), low),
            pltpu.VMEM((planes * z_rows, LANES), low),
            pltpu.VMEM((planes, z_rows, LANES), low),
            pltpu.VMEM((planes, z_rows, LANES), low),
            pltpu.VMEM((planes, 2, mem_len // n, width), low),
            pltpu.VMEM((planes, mem_len // n, width), low),
            pltpu.SemaphoreType.DMA((7,)),
            pltpu.SemaphoreType.DMA((2,)),
            pltpu.SemaphoreType.DMA((2,)),
            pltpu.SemaphoreType.DMA((copies,)),
            pltpu.SemaphoreType.DMA((copies,)),
        ],
        compiler_params=pltpu.CompilerParams(collective_id=2, has_side_effects=True, vmem_limit_bytes=VMEM_BYTES + (0 if mem_len <= 512 else 3 * 1024 * 1024)),
        name="middle",
    )(tokens, attended, cotangent, memory, gains, shifts, down_bias, raise_bias, *weights)


def per_device(
    tokens,
    memory,
    segment_ids,
    padding_mask,
    cotangent,
    prefix_embed,
    prefix_first,
    first_bias,
    prefix_second,
    second_bias,
    adapter_down,
    down_bias,
    adapter_raise,
    raise_bias,
    norm_gain,
    norm_shift,
    self_query,
    self_key,
    self_value,
    self_output,
    cross_query,
    cross_key,
    cross_value,
    cross_output,
    feed_in,
    feed_out,
):
    row_count, length, model_width = tokens.shape
    flat_rows = row_count * length
    n = lax.axis_size("seq")
    batches = lax.axis_size("batch")
    down = adapter_down.shape[1]
    attended, *saved, whole_memory = self_forward(
        n,
        segment_ids,
        padding_mask,
        tokens.reshape(flat_rows, model_width),
        (self_query, self_key, self_value),
        (
            prefix_embed,
            prefix_first,
            first_bias.reshape(1, -1),
            prefix_second,
            second_bias.reshape(1, -1),
        ),
        memory.reshape(-1, model_width),
    )
    layer_output, first_grad, out_grad, memory_part, weight_sums, vector_sums = middle(
        tokens.reshape(flat_rows, model_width),
        attended,
        cotangent.reshape(flat_rows, model_width),
        whole_memory.reshape(-1, model_width),
        norm_gain,
        norm_shift,
        down_bias.reshape(1, -1),
        raise_bias.reshape(1, -1),
        (
            self_output,
            cross_query,
            cross_key,
            cross_value,
            cross_output,
            adapter_down,
            adapter_raise,
            feed_in,
            feed_out,
        ),
        n,
        batches,
    )
    layer_output = layer_output.reshape(row_count, length, model_width)
    token_grad, memory_grad, prefix_grad, vector_sums, full_sums = self_backward(
        n,
        batches,
        out_grad,
        first_grad,
        weight_sums,
        memory_part,
        vector_sums,
        saved,
        (self_query, self_key, self_value),
    )
    token_grad = token_grad.reshape(row_count, length, model_width)
    memory_grad = memory_grad.reshape(memory.shape)
    replicated = finish(
        full_sums.reshape(-1, LANES),
        vector_sums,
        prefix_grad,
        prefix_embed,
        prefix_first,
        first_bias.reshape(1, -1),
        prefix_second,
        down,
    )
    replicated = [
        value.reshape(-1) if value.shape[0] == 1 else value for value in replicated
    ]
    return (layer_output, token_grad, memory_grad, *replicated)


def solution(mesh):
    placed = (
        P("batch", "seq", None),
        P("batch", "seq", None),
        P("batch", "seq"),
        P("batch", "seq"),
        P("batch", "seq", None),
        P(),
        P(),
        P(),
        P(),
        P(),
        P(),
        P(),
        P(),
        P(),
        P(),
        P(),
        P(),
        P(),
        P(),
        P(),
        P(),
        P(),
        P(),
        P(),
        P(),
        P(),
    )
    return jax.shard_map(
        per_device,
        mesh=mesh,
        in_specs=placed,
        out_specs=(
            P("batch", "seq", None),
            P("batch", "seq", None),
            P("batch", "seq", None),
            P(),
            P(),
            P(),
            P(),
            P(),
            P(),
            P(),
            P(),
            P(),
            P(),
            P(),
        ),
        check_vma=False,
    )
```

```python
import functools

import jax
import jax.numpy as jnp
from jax import lax
from jax.experimental import pallas as pl
from jax.experimental.pallas import tpu as pltpu
from jax.sharding import PartitionSpec as P

H = 16
HD = 64
LANES = 128
PREFIX_ROWS = 32
VMEM_BYTES = 60 * 1024 * 1024
SUM_ROWS = 16
MESH = pl.DeviceIdType.MESH

masked_score = -1e30
norm_eps = 1e-05

def dot_nn(left, right):
    return lax.dot_general(
        left, right, (((1,), (0,)), ((), ())), preferred_element_type=jnp.float32
    )


def dot_nt(left, right):
    return lax.dot_general(
        left, right, (((1,), (1,)), ((), ())), preferred_element_type=jnp.float32
    )


def dot_tn(left, right):
    return lax.dot_general(
        left, right, (((0,), (0,)), ((), ())), preferred_element_type=jnp.float32
    )


def remote(source, target, send_sem, recv_sem, axis, peer):
    return pltpu.make_async_remote_copy(
        src_ref=source,
        dst_ref=target,
        send_sem=send_sem,
        recv_sem=recv_sem,
        device_id={axis: peer},
        device_id_type=MESH,
    )


def enter(sizes):
    barrier = pltpu.get_barrier_semaphore()
    for axis, size in sizes.items():
        for other in range(size):

            @pl.when(other != lax.axis_index(axis))
            def _():
                pl.semaphore_signal(barrier, inc=1, device_id={axis: other}, device_id_type=MESH)

    pl.semaphore_wait(barrier, sum(sizes.values()) - len(sizes))


def others(size, mine, body):
    for other in range(size):

        @pl.when(other != mine)
        def _():
            body(other)


def rows_of(index, size):
    return pl.ds(pl.multiple_of(index * size, size), size)


def span_of(start, size):
    return pl.ds(pl.multiple_of(start, LANES), size)


def own_columns(ref, first, me, width):
    if width % LANES == 0:
        return ref[:, pl.ds(pl.multiple_of(first + me * width, LANES), width)].astype(jnp.float32)
    share = LANES // width
    block = ref[:, pl.ds(pl.multiple_of(first + me // share * LANES, LANES), LANES)].astype(
        jnp.float32
    )
    picked = block[:, :width]
    for part in range(1, share):
        picked = jnp.where(me % share == part, block[:, part * width : (part + 1) * width], picked)
    return picked


def head_lanes(shape, head):
    lane = lax.broadcasted_iota(jnp.int32, shape, 1)
    return (lane >= head * HD) & (lane < (head + 1) * HD)


def self_forward_kernel(
    n,
    seg_ref,
    pad_ref,
    tok_ref,
    wq_ref,
    wk_ref,
    wv_ref,
    emb_ref,
    first_ref,
    fbias_ref,
    second_ref,
    sbias_ref,
    mem_ref,
    att_ref,
    qx_out,
    kx_out,
    raw_out,
    pk_out,
    pv_out,
    pkt_out,
    ot_out,
    lse_out,
    mem_out,
    send,
    recv,
    meta_send,
    meta,
    kx,
    qx,
    vt,
    hidden,
    pk,
    pv,
    pkt,
    pvt,
    stat,
    acc,
    o_send,
    o_recv,
    mem_all,
    send_sem,
    recv_sem,
    meta_send_sem,
    meta_recv_sem,
    o_send_sem,
    o_recv_sem,
    mem_send_sem,
    mem_recv_sem,
    out_sem,
):
    low = jnp.bfloat16
    f32 = jnp.float32
    me = lax.axis_index("seq")
    length, width = tok_ref.shape
    group = width // n
    heads = group // HD
    plane = 2 * length
    planes = n // 2
    block = 2 * LANES
    per_block = block // group
    blocks = width // block
    step_rows = 256
    steps = plane // step_rows
    my_plane = me // 2
    my_side = lax.rem(me, 2)

    def meta_copy(peer, slot):
        return remote(
            meta_send, meta.at[slot], meta_send_sem.at[peer], meta_recv_sem.at[slot], "seq", peer
        )

    def qkv_copy(head, peer, slot):
        return remote(
            send.at[peer, head],
            recv.at[head, slot],
            send_sem.at[head, peer],
            recv_sem.at[head, slot],
            "seq",
            peer,
        )

    def out_copy(head, peer, slot):
        return remote(
            o_send.at[head, peer],
            o_recv.at[slot, head],
            o_send_sem.at[head, peer],
            o_recv_sem.at[head, slot],
            "seq",
            peer,
        )

    def mem_along(which, toward):
        part = mem_all.at[which, my_side]
        return remote(
            part,
            part,
            mem_send_sem.at[(toward + 1) // 2, which],
            mem_recv_sem.at[which],
            "seq",
            me + 2 * toward,
        )

    def mem_across(side):
        part = mem_all.at[:, side]
        return remote(
            part,
            part,
            mem_send_sem.at[0, planes],
            mem_recv_sem.at[planes],
            "seq",
            me + 1 - 2 * my_side,
        )

    def mem_hops(hop, body):
        for toward in (1, -1):
            which = my_plane - toward * hop
            ahead = my_plane + toward

            @pl.when((which >= 0) & (which < planes) & (ahead >= 0) & (ahead < planes))
            def _():
                body(mem_along(which, toward))

    def mem_arrivals(hop):
        for toward in (1, -1):
            which = my_plane - toward * hop

            @pl.when((which >= 0) & (which < planes))
            def _():
                mem_along(which, -toward).wait_recv()

    segments = seg_ref[...]
    tags = jnp.where(pad_ref[...] == 1, segments, -1)
    row = lax.broadcasted_iota(jnp.int32, meta_send.shape, 0)
    meta_send[...] = jnp.where(row == 0, segments, tags)
    mem_all[my_plane, my_side] = mem_ref[...]
    enter({"seq": n})
    others(n, me, lambda peer: meta_copy(peer, me).start())
    meta[me] = meta_send[...]

    def project(step, carry):
        here = lax.rem(my_plane + 1 + step, planes) * (blocks // planes)
        for sub in range(blocks // planes):
            at = here + sub
            columns = rows_of(at, block)
            for which, weight in enumerate((wq_ref, wk_ref, wv_ref)):
                piece = dot_nn(tok_ref[...], weight[:, columns]).T.astype(low)
                for part in range(per_block):
                    for head in range(heads):
                        first = part * group + head * HD
                        send[at * per_block + part, head, which] = piece[first : first + HD]
            for part in range(per_block):
                peer = at * per_block + part

                @pl.when(peer != me)
                def _():
                    qkv_copy(0, peer, me).start()

                @pl.when(peer == me)
                def _():
                    for head in range(heads):
                        recv[head, me] = send[peer, head]

        return carry

    if blocks >= planes:
        lax.fori_loop(0, planes, project, 0)
    else:

        def project_wide(step, carry):
            at = lax.rem(me // per_block + 1 + step, blocks)
            columns = rows_of(at, block)
            for which, weight in enumerate((wq_ref, wk_ref, wv_ref)):
                piece = dot_nn(tok_ref[...], weight[:, columns]).T.astype(low)
                for part in range(per_block):
                    for head in range(heads):
                        first = part * group + head * HD
                        send[at * per_block + part, head, which] = piece[first : first + HD]
            for part in range(per_block):
                peer = at * per_block + part

                @pl.when(peer != me)
                def _():
                    qkv_copy(0, peer, me).start()

                @pl.when(peer == me)
                def _():
                    for head in range(heads):
                        recv[head, me] = send[peer, head]

            return carry

        lax.fori_loop(0, blocks, project_wide, 0)

    mem_hops(0, lambda copy: copy.start())

    hidden[...] = jnp.zeros_like(hidden)
    hidden[: emb_ref.shape[0], :] = jnp.tanh(dot_nn(emb_ref[...], first_ref[...]) + fbias_ref[...])
    hidden_low = hidden[...].astype(low)
    prefix_key = dot_nn(hidden_low, own_columns(second_ref, 0, me, group).astype(low)) + own_columns(
        sbias_ref, 0, me, group
    )
    prefix_value = dot_nn(
        hidden_low, own_columns(second_ref, width, me, group).astype(low)
    ) + own_columns(sbias_ref, width, me, group)
    prefix_row = lax.broadcasted_iota(jnp.int32, (PREFIX_ROWS, HD), 0)
    prefix_open = jnp.where(prefix_row < emb_ref.shape[0], 0.0, masked_score)
    nothing = jnp.zeros((PREFIX_ROWS, HD), f32)
    for head in range(heads):
        here = slice(head * HD, (head + 1) * HD)
        pk[head] = jnp.concatenate([prefix_key[:, here], prefix_open], axis=1).astype(low)
        pv[head] = jnp.concatenate([nothing, prefix_value[:, here]], axis=1).astype(low)
    pkt[...] = prefix_key.T.astype(low).reshape(heads, HD, PREFIX_ROWS)
    pvt[:, :HD, :] = prefix_value.T.astype(low).reshape(heads, HD, PREFIX_ROWS)
    pvt[:, HD:, :] = jnp.ones((heads, SUM_ROWS, PREFIX_ROWS), low)
    vt[:, HD:, :] = jnp.ones((heads, SUM_ROWS, n * length), low)

    def arrive(head, chunk):
        @pl.when(chunk != me)
        def _():
            @pl.when(head == 0)
            def _():
                meta_copy(chunk, chunk).wait_recv()

            qkv_copy(head, chunk, chunk).wait_recv()

        here = rows_of(chunk, length)
        state = lax.broadcasted_iota(jnp.int32, (HD, length), 0)
        qx[head, :HD, here] = (recv[head, chunk, 0].astype(f32) * 0.125).astype(low)
        qx[head, HD:, here] = jnp.where(state == meta[chunk, 0:1, :], 1.0, 0.0).astype(low)
        is_open = jnp.where(state == meta[chunk, 1:2, :], 0.0, masked_score)
        kx[head, here, :] = jnp.concatenate(
            [recv[head, chunk, 1].astype(f32), is_open], axis=0
        ).T.astype(low)
        vt[head, :HD, here] = recv[head, chunk, 2]

    def open_plane(head, which):
        scores = dot_nn(pk[head], qx[head, :, rows_of(which, plane)])
        top = jnp.max(scores, axis=0, keepdims=True)
        raised = jnp.exp(scores - top)
        stat[which, head, 0:1, :] = top
        acc[which, head] = dot_nn(pvt[head], raised.astype(low))

    def pair_part(head, upper, lower, first, keys, diagonal):
        here = slice(first, first + step_rows)
        queries = qx[head, :, span_of(upper * plane + first, step_rows)]
        key_rows = span_of(lower * plane, keys)
        scores = dot_nn(kx[head, key_rows, :], queries)
        if diagonal:
            key_at = lax.broadcasted_iota(jnp.int32, scores.shape, 0)
            query_at = lax.broadcasted_iota(jnp.int32, scores.shape, 1) + first
            scores = jnp.where(key_at <= query_at, scores, masked_score)
        old_top = stat[upper, head, 0:1, here]
        top = jnp.maximum(old_top, jnp.max(scores, axis=0, keepdims=True))
        raised = jnp.exp(scores - top).astype(low)
        stat[upper, head, 0:1, here] = top
        acc[upper, head, :, here] = acc[upper, head, :, here] * jnp.exp(old_top - top) + dot_nn(
            vt[head, :, key_rows], raised
        )

    def pair(head, upper, lower):
        for part in range(steps):
            pair_part(head, upper, lower, part * step_rows, plane, False)

    def pair_diagonal(head, which):
        for part in range(steps):
            pair_part(head, which, which, part * step_rows, (part + 1) * step_rows, True)

    def close_plane(head, which):
        total = acc[which, head, HD : HD + 1, :]
        value = acc[which, head, :HD, :] / total
        acc[which, head, :HD, :] = value
        stat[which, head, 0:1, :] = stat[which, head, 0:1, :] + jnp.log(total)
        for part in range(2):
            chunk = 2 * which + part
            o_send[head, chunk] = value[:, part * length : (part + 1) * length].astype(low)

            @pl.when(chunk != me)
            def _():
                out_copy(head, chunk, me).start()

            @pl.when(chunk == me)
            def _():
                o_recv[me, head] = o_send[head, chunk]

    def stage(index, carry):
        head = index // planes
        step = lax.rem(index, planes)

        @pl.when(head + 1 < heads)
        def _():
            there = lax.rem(my_plane + 1 + step, planes)
            for part in range(2):
                peer = 2 * there + part

                @pl.when(peer != me)
                def _():
                    qkv_copy(head, peer, me).wait_send()
                    qkv_copy(head + 1, peer, me).start()

        here = lax.rem(my_plane + step, planes)
        arrive(head, 2 * here)
        arrive(head, 2 * here + 1)
        open_plane(head, here)
        pair_diagonal(head, here)

        def earlier(back, inner):
            there = lax.rem(my_plane + back, planes)
            pair(head, jnp.maximum(here, there), jnp.minimum(here, there))
            return inner

        lax.fori_loop(0, step, earlier, 0)
        for hop in range(1, planes - 1):

            @pl.when(index == hop)
            def _():
                mem_arrivals(hop)
                mem_hops(hop, lambda copy: copy.start())

        @pl.when(index == planes - 1)
        def _():
            mem_arrivals(planes - 1)
            mem_across(my_side).start()

        @pl.when((my_plane + step >= planes) | (my_plane == 0))
        def _():
            close_plane(head, here)

        @pl.when(step == planes - 1)
        def _():
            def finish(which, inner):
                close_plane(head, which)
                return inner

            lax.fori_loop(jnp.where(my_plane == 0, planes, my_plane), planes, finish, 0)

        return carry

    lax.fori_loop(0, heads * planes, stage, 0)

    saves = []

    def save(source, target):
        copy = pltpu.make_async_copy(source, target, out_sem.at[len(saves)])
        copy.start()
        saves.append(copy)

    save(qx, qx_out)
    save(kx, kx_out)
    save(recv, raw_out)
    save(pk, pk_out)
    save(pv, pv_out)
    save(pkt, pkt_out)
    save(acc, ot_out)
    save(stat, lse_out)
    mem_across(1 - my_side).wait_recv()
    save(mem_all, mem_out)
    for other in range(n):

        @pl.when(other != me)
        def _():
            for head in range(heads):
                out_copy(head, other, other).wait_recv()

        att_ref[:, other * group : (other + 1) * group] = (
            o_recv[other].reshape(group, length).astype(f32).T.astype(low)
        )

    def drain(peer):
        meta_copy(peer, me).wait_send()
        qkv_copy(heads - 1, peer, me).wait_send()
        for head in range(heads):
            out_copy(head, peer, me).wait_send()

    others(n, me, drain)
    for hop in range(planes - 1):
        mem_hops(hop, lambda copy: copy.wait_send())
    mem_across(my_side).wait_send()
    for copy in saves:
        copy.wait()


def self_forward(n, segments, padding, tokens, weights, prefix, memory):
    length, width = tokens.shape
    group = width // n
    heads = group // HD
    whole = n * length
    planes = n // 2
    low = jnp.bfloat16
    f32 = jnp.float32
    vmem = pl.BlockSpec(memory_space=pltpu.VMEM)
    anywhere = pl.BlockSpec(memory_space=pl.ANY)
    dma = pltpu.SemaphoreType.DMA
    shapes = (
        ((heads, 2 * HD, whole), low),
        ((heads, whole, 2 * HD), low),
        ((heads, n, 3, HD, length), low),
        ((heads, PREFIX_ROWS, 2 * HD), low),
        ((heads, PREFIX_ROWS, 2 * HD), low),
        ((heads, HD, PREFIX_ROWS), low),
        ((planes, heads, HD + SUM_ROWS, 2 * length), f32),
        ((planes, heads, 8, 2 * length), f32),
        ((planes, 2) + memory.shape, low),
    )
    qx, kx, raw, pk, pv, pkt, acc, stat, mem_all = (pltpu.VMEM(*shape) for shape in shapes)
    return pl.pallas_call(
        functools.partial(self_forward_kernel, n),
        out_shape=(jax.ShapeDtypeStruct((length, width), low),)
        + tuple(jax.ShapeDtypeStruct(*shape) for shape in shapes),
        in_specs=[vmem] * 12,
        out_specs=(vmem,) + (anywhere,) * 9,
        scratch_shapes=[
            pltpu.VMEM((n, heads, 3, HD, length), low),
            raw,
            pltpu.VMEM((8, length), jnp.int32),
            pltpu.VMEM((n, 8, length), jnp.int32),
            kx,
            qx,
            pltpu.VMEM((heads, HD + SUM_ROWS, whole), low),
            pltpu.VMEM((PREFIX_ROWS, weights[0].shape[0] // 2), f32),
            pk,
            pv,
            pkt,
            pltpu.VMEM((heads, HD + SUM_ROWS, PREFIX_ROWS), low),
            stat,
            acc,
            pltpu.VMEM((heads, n, HD, length), low),
            pltpu.VMEM((n, heads, HD, length), low),
            mem_all,
            dma((heads, n)),
            dma((heads, n)),
            dma((n,)),
            dma((n,)),
            dma((heads, n)),
            dma((heads, n)),
            dma((2, planes + 1)),
            dma((planes + 1,)),
            dma((9,)),
        ],
        compiler_params=pltpu.CompilerParams(
            collective_id=0, has_side_effects=True, vmem_limit_bytes=VMEM_BYTES
        ),
        name="self_forward",
    )(segments, padding, tokens, *weights, *prefix, memory)


def self_backward_kernel(
    n,
    batches,
    base_ref,
    do_in,
    sums_in,
    mem_in,
    vecs_in,
    qx_in,
    kx_in,
    raw_in,
    pk_in,
    pv_in,
    pkt_in,
    ot_in,
    lse_in,
    wq_in,
    wk_in,
    wv_in,
    tg_ref,
    mgrad_ref,
    pkv_ref,
    vecs_ref,
    full_out,
    do_recv,
    qx,
    kx,
    raw,
    kt,
    qv,
    q0,
    dox,
    do0,
    pk,
    pv,
    pkt,
    ot,
    stat,
    weights,
    dqt,
    dkv,
    g_send,
    g_recv,
    pre_ref,
    pre_all,
    pre_sum,
    pre_recv,
    full,
    mem_z,
    vec_all,
    vec_sum,
    vec_y,
    vec_both,
    vec_z,
    do_send_sem,
    do_recv_sem,
    g_send_sem,
    g_recv_sem,
    in_sem,
    send_sem,
    recv_sem,
):
    low = jnp.bfloat16
    f32 = jnp.float32
    me = lax.axis_index("seq")
    length, width = base_ref.shape
    group = width // n
    heads = group // HD
    plane = 2 * length
    planes = n // 2
    step_rows = 256
    steps = plane // step_rows
    my_batch = lax.axis_index("batch")
    my_core = lax.rem(my_batch, 2)
    my_high = my_batch // 2
    highs = batches // 2
    my_plane = me // 2
    my_side = lax.rem(me, 2)
    beside = me + 1 - 2 * my_side
    used = [0]

    def numbers(count):
        used[0] += count
        return used[0] - count

    z_slot = numbers(planes)
    e_slot = numbers(1)
    x_slot = numbers(highs)
    core_slot = numbers(1)
    mem_slot = numbers(planes)
    va_slot = numbers(batches)
    vb_slot = numbers(1)
    vc_slot = numbers(planes)
    pa_slot = numbers(batches)
    pb_slot = numbers(n)

    def send(source, target, first, peer_index, slot_index, axis, peer):
        return remote(
            source,
            target,
            send_sem.at[first + peer_index],
            recv_sem.at[first + slot_index],
            axis,
            peer,
        )

    def sum_z(peer, slot):
        return send(
            sums_in,
            full.at[my_core, my_high, my_side, slot],
            z_slot,
            peer,
            slot,
            "seq",
            2 * peer + my_side,
        )

    def sum_y(side):
        part = full.at[my_core, my_high, side]
        return send(part, part, e_slot, 0, 0, "seq", beside)

    def sum_x(peer, slot):
        part = full.at[my_core, slot]
        return send(part, part, x_slot, peer, slot, "batch", 2 * peer + my_core)

    def sum_core(core):
        part = full.at[core]
        return send(part, part, core_slot, 0, 0, "batch", my_batch + 1 - 2 * my_core)

    def mem_b(peer, slot):
        return send(
            mem_in.at[peer], mem_z.at[slot], mem_slot, peer, slot, "seq", 2 * peer + my_side
        )

    def vec_a(peer, slot):
        return send(vecs_in, vec_all.at[slot], va_slot, peer, slot, "batch", peer)

    def vec_b(side):
        return send(vec_sum, vec_y.at[side], vb_slot, 0, 0, "seq", beside)

    def vec_c(peer, slot):
        return send(vec_both, vec_z.at[slot], vc_slot, peer, slot, "seq", 2 * peer + my_side)

    def pre_a(peer, slot):
        return send(pre_ref, pre_all.at[slot], pa_slot, peer, slot, "batch", peer)

    def pre_b(peer, slot):
        return send(pre_sum, pre_recv.at[slot], pb_slot, peer, slot, "seq", peer)

    def do_copy(head, peer, slot):
        return remote(
            do_in.at[peer, head],
            do_recv.at[head, slot],
            do_send_sem.at[head, peer],
            do_recv_sem.at[head, slot],
            "seq",
            peer,
        )

    def q_copy(head, peer, slot):
        return remote(
            g_send.at[peer, head, 0],
            g_recv.at[0, slot, head],
            g_send_sem.at[0, head, peer],
            g_recv_sem.at[0, head, slot],
            "seq",
            peer,
        )

    def kv_copy(head, peer, slot):
        return remote(
            g_send.at[peer, head, pl.ds(1, 2)],
            g_recv.at[pl.ds(1, 2), slot, head],
            g_send_sem.at[1, head, peer],
            g_recv_sem.at[1, head, slot],
            "seq",
            peer,
        )

    def added(ref, size):
        value = ref[0].astype(f32)
        for other in range(1, size):
            value = value + ref[other].astype(f32)
        return value

    loads = [
        pltpu.make_async_copy(source, target, in_sem.at[index])
        for index, (source, target) in enumerate(
            (
                (raw_in, raw),
                (kx_in, kx),
                (pk_in, pk),
                (pv_in, pv),
                (pkt_in, pkt),
                (qx_in, qx),
                (ot_in, ot),
                (lse_in, stat),
                (sums_in, full.at[my_core, my_high, my_side, my_plane]),
                (mem_in.at[my_plane], mem_z.at[my_plane]),
                (vecs_in, vec_all.at[my_batch]),
                (wq_in, weights.at[0]),
                (wk_in, weights.at[1]),
                (wv_in, weights.at[2]),
            )
        )
    ]
    own_do = pltpu.make_async_copy(do_in.at[me], do_recv.at[:, me], in_sem.at[len(loads)])
    own_do.start()
    for load in loads:
        load.start()
    enter({"seq": n, "batch": batches})
    others(n, me, lambda peer: do_copy(0, peer, me).start())
    others(planes, my_plane, lambda peer: sum_z(peer, my_plane).start())
    others(batches, my_batch, lambda peer: vec_a(peer, my_batch).start())
    dox[:, :HD, :] = jnp.zeros((heads, HD, n * length), low)
    dkv[...] = jnp.zeros_like(dkv)
    pre_ref[...] = jnp.zeros_like(pre_ref)
    for load in loads[:11]:
        load.wait()
    own_do.wait()
    zero = jnp.zeros((HD, length), f32)

    def turn(index, carry):
        head = index // n
        chunk = lax.rem(index, n)
        here = rows_of(chunk, length)
        kt[head, :, here] = raw[head, chunk, 1]
        query = raw[head, chunk, 0].astype(f32) * 0.125
        both = jnp.concatenate([query, raw[head, chunk, 2].astype(f32)], axis=0).T
        qv[head, here, :] = both.astype(low)
        q0[head, here, :] = jnp.where(head_lanes(both.shape, 0), both, 0.0).astype(low)
        return carry

    lax.fori_loop(0, heads * n, turn, 0)

    def next_head(head):
        @pl.when(head + 1 < heads)
        def _():
            def move(peer):
                do_copy(head, peer, me).wait_send()
                do_copy(head + 1, peer, me).start()

            others(n, me, move)

    def arrive(head, which):
        for part in range(2):
            chunk = 2 * which + part

            @pl.when(chunk != me)
            def _():
                do_copy(head, chunk, chunk).wait_recv()

            grads = do_recv[head, chunk]
            dox[head, HD:, rows_of(chunk, length)] = grads
            grads = grads.astype(f32)
            do0[head, rows_of(chunk, length), :] = (
                jnp.concatenate([zero, grads], axis=0).T.astype(low)
            )
            here = slice(part * length, (part + 1) * length)
            stat[which, head, 1:2, here] = jnp.sum(
                grads * ot[which, head, :HD, here], axis=0, keepdims=True
            )
        here = rows_of(which, plane)
        weight = jnp.exp(dot_nn(pk[head], qx[head, :, here]) - stat[which, head, 0:1, :])
        slope = weight * (dot_nn(pv[head], dox[head, :, here]) - stat[which, head, 1:2, :])
        slope = slope.astype(low)
        pre_ref[head] += dot_nn(slope, q0[head, here, :]) + dot_nn(
            weight.astype(low), do0[head, here, :]
        )
        dqt[which, head] = dot_nn(pkt[head], slope)

    def stage_a():
        others(planes, my_plane, lambda peer: sum_z(peer, peer).wait_recv())
        sum_y(my_side).start()
        others(batches, my_batch, lambda peer: vec_a(peer, peer).wait_recv())
        vec_sum[...] = added(vec_all, batches)
        vec_b(my_side).start()
        vec_y[my_side] = vec_sum[...]
        others(planes, my_plane, lambda peer: mem_b(peer, my_plane).start())

    def stage_b():
        sum_y(1 - my_side).wait_recv()
        others(highs, my_high, lambda peer: sum_x(peer, my_high).start())
        vec_b(1 - my_side).wait_recv()
        vec_both[...] = vec_y[0] + vec_y[1]
        others(planes, my_plane, lambda peer: vec_c(peer, my_plane).start())
        vec_z[my_plane] = vec_both[...]

    def stage_c():
        others(highs, my_high, lambda peer: sum_x(peer, peer).wait_recv())
        sum_core(my_core).start()
        others(planes, my_plane, lambda peer: mem_b(peer, peer).wait_recv())
        mgrad_ref[...] = added(mem_z, planes).astype(low)
        others(planes, my_plane, lambda peer: vec_c(peer, peer).wait_recv())
        vecs_ref[...] = added(vec_z, planes)

    def stage_d():
        sum_core(1 - my_core).wait_recv()
        save_full.start()

    def stage_pa():
        others(batches, my_batch, lambda peer: pre_a(peer, my_batch).start())
        pre_all[my_batch] = pre_ref[...]

    def stage_pb():
        others(batches, my_batch, lambda peer: pre_a(peer, peer).wait_recv())
        pre_sum[...] = added(pre_all, batches).astype(low)
        others(n, me, lambda peer: pre_b(peer, me).start())
        pre_recv[me] = pre_sum[...]

    save_full = pltpu.make_async_copy(full, full_out, in_sem.at[0])

    def pair(head, upper, lower, diagonal):
        for part in range(steps):
            first = part * step_rows if diagonal else 0
            count = plane - first
            keys = span_of(lower * plane + part * step_rows, step_rows)
            here = span_of(upper * plane + first, count)
            at = slice(first, plane)
            scores = dot_nn(kx[head, keys, :], qx[head, :, here])
            weight = jnp.exp(scores - stat[upper, head, 0:1, at])
            if diagonal:
                key_at = lax.broadcasted_iota(jnp.int32, scores.shape, 0)
                query_at = lax.broadcasted_iota(jnp.int32, scores.shape, 1)
                weight = jnp.where(key_at <= query_at, weight, 0.0)
            slope = dot_nn(qv[head, keys, :], dox[head, :, here]) - stat[upper, head, 1:2, at]
            slope = (weight * slope).astype(low)
            dkv[head, keys, :] += dot_nn(slope, q0[head, here, :]) + dot_nn(
                weight.astype(low), do0[head, here, :]
            )
            dqt[upper, head, :, at] += dot_nn(kt[head, :, keys], slope)

    def hand_queries(head, which):
        for part in range(2):
            chunk = 2 * which + part
            g_send[chunk, head, 0] = (
                dqt[which, head, :, part * length : (part + 1) * length] * 0.125
            ).astype(low)

            @pl.when(chunk != me)
            def _():
                q_copy(head, chunk, me).start()

            @pl.when(chunk == me)
            def _():
                g_recv[0, me, head] = g_send[chunk, head, 0]

    def hand_keys(head, which):
        for part in range(2):
            chunk = 2 * which + part
            turned = dkv[head, rows_of(chunk, length), :].T.astype(low)
            g_send[chunk, head, 1] = turned[:HD]
            g_send[chunk, head, 2] = turned[HD:]

            @pl.when(chunk != me)
            def _():
                kv_copy(head, chunk, me).start()

            @pl.when(chunk == me)
            def _():
                g_recv[pl.ds(1, 2), me, head] = g_send[chunk, head, pl.ds(1, 2)]

    rising = my_side == 0

    def stage(index, carry):
        head = index // planes
        step = lax.rem(index, planes)
        here = jnp.where(rising, step, planes - 1 - step)

        @pl.when((step == 0) | ((step == 1) & jnp.logical_not(rising)))
        def _():
            @pl.when(rising | (step == 0))
            def _():
                arrive(head, here)

            @pl.when(jnp.logical_not(rising) & (step == 1))
            def _():
                next_head(head)

                def rest(which, inner):
                    arrive(head, planes - 2 - which)
                    return inner

                lax.fori_loop(0, planes - 1, rest, 0)

        pair(head, here, here, True)

        @pl.when(rising)
        def _():
            hand_queries(head, here)

        @pl.when(jnp.logical_not(rising))
        def _():
            hand_keys(head, here)

        def far(at, inner):
            there = jnp.where(rising, here + 1 + at, here - 1 - at)

            @pl.when(rising & (step == 0))
            def _():
                arrive(head, there)

            pair(head, jnp.maximum(here, there), jnp.minimum(here, there), False)
            return inner

        lax.fori_loop(0, planes - 1 - step, far, 0)

        @pl.when(rising & (step == 0))
        def _():
            next_head(head)

        @pl.when(rising)
        def _():
            hand_keys(head, here)

        @pl.when(jnp.logical_not(rising))
        def _():
            hand_queries(head, here)

        final = (heads - 1) * planes
        for at, body in (
            (0, stage_a),
            (1, stage_b),
            (2, stage_c),
            (3, stage_d),
            (final + 1, stage_pa),
            (final + 2, stage_pb),
        ):
            pl.when(index == at)(body)
        return carry

    lax.fori_loop(0, heads * planes, stage, 0)
    for load in loads[11:]:
        load.wait()

    def gathered(peer):
        for head in range(heads):
            q_copy(head, peer, peer).wait_recv()
            kv_copy(head, peer, peer).wait_recv()

    others(n, me, gathered)
    tile = 256
    grads = [g_recv[which].reshape(width, length) for which in range(3)]

    def last_product(index, carry):
        here = rows_of(index, tile)
        value = dot_nn(weights[0, here, :], grads[0])
        value = value + dot_nn(weights[1, here, :], grads[1])
        value = value + dot_nn(weights[2, here, :], grads[2])
        tg_ref[:, here] = (base_ref[:, here] + value.T).astype(low)
        return carry

    lax.fori_loop(0, width // tile, last_product, 0)
    for other in range(n):

        @pl.when(other != me)
        def _():
            pre_b(other, other).wait_recv()

        value = pre_recv[other].astype(f32)
        for which in range(2):
            pkv_ref[:, which * width + other * group : which * width + (other + 1) * group] = (
                jnp.concatenate(
                    [value[head, :, which * HD : (which + 1) * HD] for head in range(heads)], axis=1
                )
            )

    def drain(peer):
        do_copy(heads - 1, peer, me).wait_send()
        pre_b(peer, me).wait_send()
        for head in range(heads):
            q_copy(head, peer, me).wait_send()
            kv_copy(head, peer, me).wait_send()

    others(n, me, drain)
    others(batches, my_batch, lambda peer: pre_a(peer, my_batch).wait_send())
    others(batches, my_batch, lambda peer: vec_a(peer, my_batch).wait_send())
    others(highs, my_high, lambda peer: sum_x(peer, my_high).wait_send())
    others(planes, my_plane, lambda peer: sum_z(peer, my_plane).wait_send())
    others(planes, my_plane, lambda peer: vec_c(peer, my_plane).wait_send())
    others(planes, my_plane, lambda peer: mem_b(peer, my_plane).wait_send())
    sum_y(my_side).wait_send()
    sum_core(my_core).wait_send()
    vec_b(my_side).wait_send()
    save_full.wait()


def self_backward(n, batches, first_grad, out_grad, sums, memory_part, vecs, saved, weights):
    length, width = first_grad.shape
    group = width // n
    heads = group // HD
    whole = n * length
    planes = n // 2
    low = jnp.bfloat16
    f32 = jnp.float32
    vmem = pl.BlockSpec(memory_space=pltpu.VMEM)
    anywhere = pl.BlockSpec(memory_space=pl.ANY)
    dma = pltpu.SemaphoreType.DMA
    sum_rows = sums.shape[0]
    mem_rows = memory_part.shape[1]
    vec = pltpu.VMEM((8, width), f32)
    copies = 3 + batches // 2 + 4 * planes + 2 * batches + n
    qx, kx, raw, pk, pv, pkt, ot, stat = (pltpu.VMEM(value.shape, value.dtype) for value in saved)
    return pl.pallas_call(
        functools.partial(self_backward_kernel, n, batches),
        out_shape=(
            jax.ShapeDtypeStruct((length, width), low),
            jax.ShapeDtypeStruct((mem_rows, width), low),
            jax.ShapeDtypeStruct((PREFIX_ROWS, 2 * width), f32),
            jax.ShapeDtypeStruct((8, width), f32),
            jax.ShapeDtypeStruct((2, batches // 2, 2, planes, sum_rows, LANES), low),
        ),
        in_specs=[vmem] + [anywhere] * 15,
        out_specs=(vmem, vmem, vmem, vmem, anywhere),
        scratch_shapes=[
            pltpu.VMEM((heads, n, HD, length), low),
            qx,
            kx,
            raw,
            pltpu.VMEM((heads, HD, whole), low),
            pltpu.VMEM((heads, whole, 2 * HD), low),
            pltpu.VMEM((heads, whole, 2 * HD), low),
            pltpu.VMEM((heads, 2 * HD, whole), low),
            pltpu.VMEM((heads, whole, 2 * HD), low),
            pk,
            pv,
            pkt,
            ot,
            stat,
            pltpu.VMEM((3, width, width), low),
            pltpu.VMEM((planes, heads, HD, 2 * length), f32),
            pltpu.VMEM((heads, whole, 2 * HD), f32),
            pltpu.VMEM((n, heads, 3, HD, length), low),
            pltpu.VMEM((3, n, heads, HD, length), low),
            pltpu.VMEM((heads, PREFIX_ROWS, 2 * HD), f32),
            pltpu.VMEM((batches, heads, PREFIX_ROWS, 2 * HD), f32),
            pltpu.VMEM((heads, PREFIX_ROWS, 2 * HD), low),
            pltpu.VMEM((n, heads, PREFIX_ROWS, 2 * HD), low),
            pltpu.VMEM((2, batches // 2, 2, planes, sum_rows, LANES), low),
            pltpu.VMEM((planes, mem_rows, width), low),
            pltpu.VMEM((batches, 8, width), f32),
            vec,
            pltpu.VMEM((2, 8, width), f32),
            vec,
            pltpu.VMEM((planes, 8, width), f32),
            dma((heads, n)),
            dma((heads, n)),
            dma((2, heads, n)),
            dma((2, heads, n)),
            dma((15,)),
            dma((copies,)),
            dma((copies,)),
        ],
        compiler_params=pltpu.CompilerParams(
            collective_id=1, has_side_effects=True, vmem_limit_bytes=VMEM_BYTES
        ),
        name="self_backward",
    )(first_grad, out_grad, sums, memory_part, vecs, *saved, *weights)


def both_parts(value):
    high = value.astype(jnp.bfloat16).astype(jnp.float32)
    return jnp.concatenate([high, value - high], axis=0).astype(jnp.bfloat16)


def finish_kernel(
    full_ref,
    vecs_ref,
    pkv_ref,
    emb_ref,
    first_ref,
    fbias_ref,
    second_ref,
    embed_out,
    first_out,
    fbias_out,
    second_out,
    sbias_out,
    down_out,
    dbias_out,
    raise_out,
    rbias_out,
    gain_out,
    shift_out,
    first_grad,
    second_grad,
    down_grad,
    raise_grad,
    emb,
    hidden,
    out_sem,
):
    f32 = jnp.float32
    low = jnp.bfloat16
    width = emb_ref.shape[1]
    down = dbias_out.shape[1]
    count = emb_ref.shape[0]
    saves = []

    def save(source, target, rows=None):
        if rows is not None:
            source, target = source.at[rows], target.at[rows]
        copy = pltpu.make_async_copy(source, target, out_sem.at[len(saves)])
        copy.start()
        saves.append(copy)

    first = down * width // LANES
    for index in range(width // LANES):
        raise_grad[:, index * LANES : (index + 1) * LANES] = full_ref[
            first + index * down : first + (index + 1) * down, :
        ].astype(f32)
    save(raise_grad, raise_out)
    for index in range(down // LANES):
        down_grad[:, index * LANES : (index + 1) * LANES] = full_ref[
            index * width : (index + 1) * width, :
        ].astype(f32)
    save(down_grad, down_out)
    emb[...] = jnp.zeros_like(emb)
    emb[:count, :] = emb_ref[...].astype(f32)
    emb_low = emb[...].astype(low)
    row = lax.broadcasted_iota(jnp.int32, hidden.shape, 0)
    hidden[...] = jnp.where(
        row < count, jnp.tanh(dot_nn(emb_low, first_ref[...]) + fbias_ref[...]), 0.0
    )
    value = hidden[...]
    prefix = pkv_ref[...]
    parts = both_parts(prefix)
    hidden_twice = jnp.concatenate([value, value], axis=0).T.astype(low)
    tile = 128
    for index in range(second_grad.shape[0] // tile):
        here = slice(index * tile, (index + 1) * tile)
        second_grad[here, :] = dot_nn(hidden_twice[here, :], parts)
        save(second_grad, second_out, here)
    sbias_out[...] = jnp.sum(prefix, axis=0, keepdims=True)
    grad = dot_nt(parts, second_ref[...])
    grad = (grad[:PREFIX_ROWS] + grad[PREFIX_ROWS:]) * (1.0 - value * value)
    fbias_out[...] = jnp.sum(grad, axis=0, keepdims=True)
    parts = both_parts(grad)
    emb_twice = jnp.concatenate([emb[...], emb[...]], axis=0).T.astype(low)
    first_grad[...] = dot_nn(emb_twice, parts)
    save(first_grad, first_out)
    back = dot_nt(parts, first_ref[...])
    embed_out[...] = (back[:PREFIX_ROWS] + back[PREFIX_ROWS:])[:count, :]
    rbias_out[...] = vecs_ref[0:1, :]
    dbias_out[...] = vecs_ref[1:2, :down]
    gain_out[...] = vecs_ref[2:5, :]
    shift_out[...] = vecs_ref[5:8, :]
    for copy in saves:
        copy.wait()


def finish(full, vecs, prefix_grad, embed, first, first_bias, second, down):
    f32 = jnp.float32
    count, width = embed.shape
    hidden = first.shape[1]
    vmem = pl.BlockSpec(memory_space=pltpu.VMEM)
    anywhere = pl.BlockSpec(memory_space=pl.ANY)
    shapes = (
        (count, width),
        (width, hidden),
        (1, hidden),
        (hidden, 2 * width),
        (1, 2 * width),
        (width, down),
        (1, down),
        (down, width),
        (1, width),
        (3, width),
        (3, width),
    )
    return pl.pallas_call(
        finish_kernel,
        out_shape=tuple(jax.ShapeDtypeStruct(shape, f32) for shape in shapes),
        in_specs=[vmem] * 7,
        out_specs=(
            vmem,
            anywhere,
            vmem,
            anywhere,
            vmem,
            anywhere,
            vmem,
            anywhere,
            vmem,
            vmem,
            vmem,
        ),
        scratch_shapes=[
            pltpu.VMEM((width, hidden), f32),
            pltpu.VMEM((hidden, 2 * width), f32),
            pltpu.VMEM((width, down), f32),
            pltpu.VMEM((down, width), f32),
            pltpu.VMEM((PREFIX_ROWS, width), f32),
            pltpu.VMEM((PREFIX_ROWS, hidden), f32),
            pltpu.SemaphoreType.DMA((3 + hidden // 128,)),
        ],
        compiler_params=pltpu.CompilerParams(vmem_limit_bytes=VMEM_BYTES),
        name="finish",
    )(full, vecs, prefix_grad, embed, first, first_bias, second)


def gelu_pair(value):
    scaled = jnp.abs(value) * 0.7071067811865476
    step = 1.0 / (1.0 + 0.3275911 * scaled)
    bell = jnp.exp(-scaled * scaled)
    poly = step * (
        0.254829592
        + step
        * (-0.284496736 + step * (1.421413741 + step * (-1.453152027 + step * 1.061405429)))
    )
    tail = 0.5 * poly * bell
    share = jnp.where(value >= 0.0, 1.0 - tail, tail)
    return value * share, share + value * (bell * 0.3989422804014327)


def normed(value):
    center = jnp.mean(value, axis=-1, keepdims=True)
    centered = value - center
    scale = lax.rsqrt(jnp.mean(centered * centered, axis=-1, keepdims=True) + norm_eps)
    return centered * scale, scale


def norm_back(grad, scale, unit):
    return scale * (
        grad
        - jnp.mean(grad, axis=-1, keepdims=True)
        - unit * jnp.mean(grad * unit, axis=-1, keepdims=True)
    )


def middle_kernel(
    n,
    batches,
    tok_ref,
    att_ref,
    cot_ref,
    mem_ref,
    gain_ref,
    shift_ref,
    dbias_ref,
    rbias_ref,
    wo_in,
    wcq_in,
    wck_in,
    wcv_in,
    wco_in,
    wd_in,
    wr_in,
    win_in,
    wout_in,
    out_ref,
    fgrad_ref,
    ograd_ref,
    mem_out,
    sums_out,
    vecs_ref,
    wo,
    wcq,
    wck,
    wcv,
    wco,
    wd,
    wr,
    win,
    wout,
    unit_one,
    unit_two,
    work,
    total,
    scale_one,
    scale_two,
    low_one,
    low_two,
    low_three,
    query,
    crossed,
    mem_key,
    mem_value,
    weights,
    slopes,
    pre_now,
    down_act,
    down_slope,
    down_grad,
    sums_ref,
    sums_core,
    sums_x,
    sums_y,
    sums_z,
    mpart,
    mem_y,
    load_sem,
    win_sem,
    wout_sem,
    send_sem,
    recv_sem,
):
    length, width = tok_ref.shape
    mem_len = mem_ref.shape[0]
    tile = win.shape[2]
    tiles = win_in.shape[1] // tile
    rows_step = 128
    low = jnp.bfloat16
    f32 = jnp.float32

    me = lax.axis_index("seq")
    planes = n // 2
    my_plane = me // 2
    my_side = lax.rem(me, 2)
    beside = me + 1 - 2 * my_side
    my_batch = lax.axis_index("batch")
    my_core = lax.rem(my_batch, 2)
    my_high = my_batch // 2
    highs = batches // 2
    mem_rows = mem_len // n
    half_rows = sums_ref.shape[0] // 2
    x_rows = half_rows // highs
    y_rows = x_rows // 2
    z_rows = y_rows // planes
    core_row = pl.multiple_of(my_core * half_rows, half_rows)
    x_row = pl.multiple_of(core_row + my_high * x_rows, x_rows)
    y_row = pl.multiple_of(x_row + my_side * y_rows, y_rows)
    z_row = pl.multiple_of(y_row + my_plane * z_rows, z_rows)

    def send(source, target, first, peer_index, slot_index, axis, peer):
        return remote(
            source,
            target,
            send_sem.at[first + peer_index],
            recv_sem.at[first + slot_index],
            axis,
            peer,
        )

    def part(row, count):
        return sums_ref.at[pl.ds(pl.multiple_of(row, count), count)]

    def sum_core():
        return send(
            part((1 - my_core) * half_rows, half_rows),
            sums_core,
            0,
            0,
            0,
            "batch",
            my_batch + 1 - 2 * my_core,
        )

    def sum_x(peer, slot):
        return send(
            part(core_row + peer * x_rows, x_rows),
            sums_x.at[slot],
            3,
            peer,
            slot,
            "batch",
            2 * peer + my_core,
        )

    def sum_y():
        return send(
            part(x_row + (1 - my_side) * y_rows, y_rows), sums_y, 1, 0, 0, "seq", beside
        )

    def sum_z(peer, slot):
        return send(
            part(y_row + peer * z_rows, z_rows),
            sums_z.at[slot],
            3 + highs,
            peer,
            slot,
            "seq",
            2 * peer + my_side,
        )

    def mem_across():
        return send(mpart.at[:, 1 - my_side], mem_y, 2, 0, 0, "seq", beside)

    def added(first, ref):
        return (first.astype(f32) + ref.astype(f32)).astype(low)

    def stage_core():
        sum_core().wait_recv()
        here = pl.ds(core_row, half_rows)
        sums_ref[here] = added(sums_ref[here], sums_core[...])
        others(highs, my_high, lambda peer: sum_x(peer, my_high).start())

    def stage_x():
        here = pl.ds(x_row, x_rows)
        value = sums_ref[here].astype(f32)
        others(highs, my_high, lambda peer: sum_x(peer, peer).wait_recv())
        sums_x[my_high] = jnp.zeros((x_rows, LANES), low)
        for other in range(highs):
            value = value + sums_x[other].astype(f32)
        sums_ref[here] = value.astype(low)
        sum_y().start()

    def stage_y():
        sum_y().wait_recv()
        here = pl.ds(y_row, y_rows)
        sums_ref[here] = added(sums_ref[here], sums_y[...])
        others(planes, my_plane, lambda peer: sum_z(peer, my_plane).start())

    def stage_z():
        value = sums_ref[pl.ds(z_row, z_rows)].astype(f32)
        others(planes, my_plane, lambda peer: sum_z(peer, peer).wait_recv())
        sums_z[my_plane] = jnp.zeros((z_rows, LANES), low)
        for other in range(planes):
            value = value + sums_z[other].astype(f32)
        sums_out[...] = value.astype(low)

    sources = (wo_in, wcq_in, wck_in, wcv_in, wco_in, wd_in, wr_in)
    targets = (wo, wcq, wck, wcv, wco, wd, wr)
    loads = [
        pltpu.make_async_copy(source, target, load_sem.at[index])
        for index, (source, target) in enumerate(zip(sources, targets))
    ]

    def win_load(which):
        slot = lax.rem(which, 2)
        return pltpu.make_async_copy(
            win_in.at[:, rows_of(which, tile)], win.at[slot], win_sem.at[slot]
        )

    def wout_load(which):
        slot = lax.rem(which, 2)
        return pltpu.make_async_copy(
            wout_in.at[rows_of(which, tile), :], wout.at[slot], wout_sem.at[slot]
        )

    for load in loads[:5]:
        load.start()
    for which in range(2):
        win_load(which).start()
        wout_load(which).start()
    for load in loads[5:]:
        load.start()
    enter({"seq": n, "batch": batches})

    def by_columns(extent, step, body):
        def one(index, carry):
            body(pl.ds(pl.multiple_of(index * step, step), step))
            return carry

        lax.fori_loop(0, extent // step, one, 0)

    def by_rows(body, init=0):
        def one(index, carry):
            return body(rows_of(index, rows_step), carry)

        return lax.fori_loop(0, length // rows_step, one, init)

    cols = 512
    half = width // 2

    loads[0].wait()

    def project_out(here):
        work[:, here] = tok_ref[:, here].astype(f32) + dot_nn(att_ref[...], wo[:, here])

    by_columns(width, cols, project_out)

    def first_norm(here, carry):
        unit, scale = normed(work[here, :])
        unit_one[here, :] = unit
        scale_one[here, :] = scale
        value = unit * gain_ref[0:1, :] + shift_ref[0:1, :]
        work[here, :] = value
        low_one[here, :] = value.astype(low)
        return carry

    by_rows(first_norm)

    loads[1].wait()

    def project_query(here):
        query[:, here] = dot_nn(low_one[...], wcq[:, here]).astype(low)

    by_columns(width, cols, project_query)
    loads[2].wait()
    loads[3].wait()

    def project_memory(here):
        mem_key[:, here] = dot_nn(mem_ref[...], wck[:, here]).astype(low)
        mem_value[:, here] = dot_nn(mem_ref[...], wcv[:, here]).astype(low)

    by_columns(width, cols, project_memory)

    per_block = LANES // HD

    def head_queries(here, head):
        both = query[:, here].astype(f32) * 0.125
        return jnp.where(head_lanes(both.shape, head), both, 0.0).astype(low)

    def cross_forward(block):
        here = rows_of(block, LANES)
        keys = mem_key[:, here]
        values = mem_value[:, here].astype(f32).T.astype(low)
        outs = []
        for head in range(per_block):
            scores = dot_nt(keys, head_queries(here, head))
            raised = jnp.exp(scores - jnp.max(scores, axis=0, keepdims=True))
            share = 1.0 / jnp.sum(raised, axis=0, keepdims=True)
            weight = (raised * share).astype(low)
            weights[block * per_block + head] = weight
            outs.append(dot_nn(values[head * HD : (head + 1) * HD, :], weight))
        crossed[:, here] = jnp.concatenate(outs, axis=0).T.astype(low)

    def cross_forward_both(step, carry):
        cross_forward(2 * step)
        cross_forward(2 * step + 1)
        return carry

    lax.fori_loop(0, width // LANES // 2, cross_forward_both, 0)

    loads[4].wait()

    def project_crossed(here):
        work[:, here] += dot_nn(crossed[...], wco[:, here])

    by_columns(width, cols, project_crossed)

    def second_norm(here, carry):
        unit, scale = normed(work[here, :])
        unit_two[here, :] = unit
        scale_two[here, :] = scale
        value = unit * gain_ref[1:2, :] + shift_ref[1:2, :]
        work[here, :] = value
        low_two[here, :] = value.astype(low)
        return carry

    by_rows(second_norm)

    total[...] = jnp.zeros_like(total)

    win_load(0).wait()
    pre_now[...] = dot_nn(low_two[...], win[0])

    def feed_forward(which, carry):
        slot = lax.rem(which, 2)
        ahead = lax.rem(which + 1, tiles)

        @pl.when(which + 1 < tiles)
        def _():
            win_load(which + 1).wait()

        wout_load(which).wait()
        pre = pre_now[...]
        pre_now[...] = dot_nn(low_two[...], win[lax.rem(ahead, 2)])
        act, slope = gelu_pair(pre)
        slopes[:, rows_of(which, tile)] = slope.astype(low)
        total[...] += dot_nn(act.astype(low), wout[slot])

        @pl.when(which + 2 < tiles)
        def _():
            win_load(which + 2).start()
            wout_load(which + 2).start()

        return carry

    lax.fori_loop(0, tiles, feed_forward, 0)
    loads[5].wait()
    loads[6].wait()
    act, slope = gelu_pair(dot_nn(low_two[...], wd[...]) + dbias_ref[...])
    down_act[...] = act.astype(low)
    down_slope[...] = slope.astype(low)

    def project_raise(here):
        work[:, here] += total[:, here] + 4.0 * (
            dot_nn(down_act[...], wr[:, here]) + rbias_ref[:, here]
        )

    by_columns(width, cols, project_raise)
    nothing = jnp.zeros((1, width), f32)

    def third_norm(here, carry):
        gain_sum, shift_sum, bias_sum = carry
        unit, scale = normed(work[here, :])
        gain = gain_ref[2:3, :]
        out_ref[here, :] = (unit * gain + shift_ref[2:3, :]).astype(low)
        grad = cot_ref[here, :].astype(f32)
        back = norm_back(grad * gain, scale, unit)
        total[here, :] = back
        back_low = back.astype(low)
        low_three[here, :] = back_low
        return (
            gain_sum + jnp.sum(grad * unit, axis=0, keepdims=True),
            shift_sum + jnp.sum(grad, axis=0, keepdims=True),
            bias_sum + jnp.sum(back_low.astype(f32), axis=0, keepdims=True),
        )

    gain_three, shift_three, bias_sum = by_rows(third_norm, (nothing, nothing, nothing))
    vecs_ref[0:1, :] = 4.0 * bias_sum

    back = 4.0 * dot_nt(low_three[...], wr[...]) * down_slope[...].astype(f32)
    back_low = back.astype(low)
    down_grad[...] = back_low
    vecs_ref[1:2, :] = jnp.concatenate(
        [
            jnp.sum(back_low.astype(f32), axis=0, keepdims=True),
            jnp.zeros((1, width - wd.shape[1]), f32),
        ],
        axis=1,
    )
    down = wd.shape[1]
    raise_sum = 4.0 * dot_tn(down_act[...], low_three[...])
    for index in range(width // LANES):
        sums_ref[pl.ds(down * width // LANES + index * down, down), :] = raise_sum[
            :, index * LANES : (index + 1) * LANES
        ].astype(low)
    down_sum = dot_tn(low_two[...], down_grad[...])
    for index in range(down // LANES):
        sums_ref[index * width : (index + 1) * width, :] = down_sum[
            :, index * LANES : (index + 1) * LANES
        ].astype(low)

    sum_core().start()

    def feed_backward(step, carry):
        which = tiles - 1 - step
        slot = lax.rem(which, 2)
        here = rows_of(which, tile)

        @pl.when(which < tiles - 2)
        def _():
            wout_load(which).wait()
            win_load(which).wait()

        grad = dot_nt(low_three[...], wout[slot]) * slopes[:, here].astype(f32)
        total[...] += dot_nt(grad.astype(low), win[slot])

        @pl.when(which >= 2)
        def _():
            win_load(which - 2).start()
            wout_load(which - 2).start()

        return carry

    lax.fori_loop(0, tiles, feed_backward, 0)
    stage_core()

    def down_back(here):
        total[:, here] += dot_nt(down_grad[...], wd[here, :])

    by_columns(width, cols, down_back)

    def second_back(here, carry):
        gain_sum, shift_sum = carry
        grad = total[here, :]
        unit = unit_two[here, :]
        back = norm_back(grad * gain_ref[1:2, :], scale_two[here, :], unit)
        total[here, :] = back
        low_one[here, :] = back.astype(low)
        return (
            gain_sum + jnp.sum(grad * unit, axis=0, keepdims=True),
            shift_sum + jnp.sum(grad, axis=0, keepdims=True),
        )

    gain_two, shift_two = by_rows(second_back, (nothing, nothing))

    def crossed_back(here):
        crossed[:, here] = dot_nt(low_one[...], wco[here, :]).astype(low)

    by_columns(width, cols, crossed_back)

    def cross_backward(block):
        here = rows_of(block, LANES)
        values = mem_value[:, here]
        keys = mem_key[:, here].astype(f32).T.astype(low)
        grads = crossed[:, here].astype(f32)
        outs = []
        key_sum = None
        for head in range(per_block):
            grad = jnp.where(head_lanes(grads.shape, head), grads, 0.0).astype(low)
            weight_low = weights[block * per_block + head]
            weight = weight_low.astype(f32)
            slope = dot_nt(values, grad)
            slope = weight * (slope - jnp.sum(weight * slope, axis=0, keepdims=True))
            slope = slope.astype(low)
            key_part = dot_nn(slope, head_queries(here, head))
            value_part = dot_nn(weight_low, grad)
            if key_sum is None:
                key_sum, value_sum = key_part, value_part
            else:
                key_sum, value_sum = key_sum + key_part, value_sum + value_part
            outs.append(dot_nn(keys[head * HD : (head + 1) * HD, :], slope))
        mem_key[:, here] = key_sum.astype(low)
        mem_value[:, here] = value_sum.astype(low)
        query[:, here] = (jnp.concatenate(outs, axis=0) * 0.125).T.astype(low)

    def cross_backward_both(step, carry):
        cross_backward(2 * step)
        cross_backward(2 * step + 1)
        pl.when(step == 2)(stage_x)
        return carry

    lax.fori_loop(0, width // LANES // 2, cross_backward_both, 0)

    def memory_back(here):
        mpart[:, :, :, here] = (
            (dot_nt(mem_key[...], wck[here, :]) + dot_nt(mem_value[...], wcv[here, :]))
            .astype(low)
            .reshape(planes, 2, mem_rows, cols)
        )

    by_columns(width, cols, memory_back)
    mem_across().start()
    stage_y()

    def query_back(here):
        total[:, here] += dot_nt(query[...], wcq[here, :])

    by_columns(width, cols, query_back)

    def first_back(here, carry):
        gain_sum, shift_sum = carry
        grad = total[here, :]
        unit = unit_one[here, :]
        back = norm_back(grad * gain_ref[0:1, :], scale_one[here, :], unit)
        fgrad_ref[here, :] = back
        low_one[here, :] = back.astype(low)
        return (
            gain_sum + jnp.sum(grad * unit, axis=0, keepdims=True),
            shift_sum + jnp.sum(grad, axis=0, keepdims=True),
        )

    gain_one, shift_one = by_rows(first_back, (nothing, nothing))

    def out_back(here):
        ograd_ref[here, :] = dot_nt(low_one[...], wo[here, :]).T.astype(low)

    by_columns(width, cols, out_back)
    for index, vector in enumerate(
        (gain_one, gain_two, gain_three, shift_one, shift_two, shift_three)
    ):
        vecs_ref[2 + index : 3 + index, :] = vector
    mem_across().wait_recv()
    mem_out[...] = added(mpart[:, my_side], mem_y[...])
    stage_z()
    sum_core().wait_send()
    sum_y().wait_send()
    mem_across().wait_send()
    others(highs, my_high, lambda peer: sum_x(peer, my_high).wait_send())
    others(planes, my_plane, lambda peer: sum_z(peer, my_plane).wait_send())


def middle(tokens, attended, cotangent, memory, gains, shifts, down_bias, raise_bias, weights, n, batches):
    length, width = tokens.shape
    mem_len = memory.shape[0]
    down = weights[5].shape[1]
    feed = weights[7].shape[1]
    tile = 512 if mem_len <= 512 else 128
    low = jnp.bfloat16
    f32 = jnp.float32
    vmem = pl.BlockSpec(memory_space=pltpu.VMEM)
    anywhere = pl.BlockSpec(memory_space=pl.ANY)
    planes = n // 2
    sum_rows = 2 * down * width // LANES
    z_rows = sum_rows // (n * batches)
    copies = 3 + batches // 2 + planes
    square = pltpu.VMEM((width, width), low)
    wide = pltpu.VMEM((length, width), f32)
    narrow = pltpu.VMEM((length, width), low)
    mem_low = pltpu.VMEM((mem_len, width), low)
    return pl.pallas_call(
        functools.partial(middle_kernel, n, batches),
        out_shape=(
            jax.ShapeDtypeStruct((length, width), low),
            jax.ShapeDtypeStruct((length, width), f32),
            jax.ShapeDtypeStruct((width, length), low),
            jax.ShapeDtypeStruct((planes, mem_len // n, width), low),
            jax.ShapeDtypeStruct((z_rows, LANES), low),
            jax.ShapeDtypeStruct((8, width), f32),
        ),
        in_specs=[vmem] * 8 + [anywhere] * 9,
        out_specs=(vmem,) * 6,
        scratch_shapes=[
            square,
            square,
            square,
            square,
            square,
            pltpu.VMEM((width, down), low),
            pltpu.VMEM((down, width), low),
            pltpu.VMEM((2, width, tile), low),
            pltpu.VMEM((2, tile, width), low),
            wide,
            wide,
            wide,
            wide,
            pltpu.VMEM((length, 1), f32),
            pltpu.VMEM((length, 1), f32),
            narrow,
            narrow,
            narrow,
            narrow,
            narrow,
            mem_low,
            mem_low,
            pltpu.VMEM((H, mem_len, length), low),
            pltpu.VMEM((length, feed), low),
            pltpu.VMEM((length, tile), f32),
            pltpu.VMEM((length, down), low),
            pltpu.VMEM((length, down), low),
            pltpu.VMEM((length, down), low),
            pltpu.VMEM((sum_rows, LANES), low),
            pltpu.VMEM((sum_rows // 2, LANES), low),
            pltpu.VMEM((batches // 2, sum_rows // batches, LANES), low),
            pltpu.VMEM((planes * z_rows, LANES), low),
            pltpu.VMEM((planes, z_rows, LANES), low),
            pltpu.VMEM((planes, 2, mem_len // n, width), low),
            pltpu.VMEM((planes, mem_len // n, width), low),
            pltpu.SemaphoreType.DMA((7,)),
            pltpu.SemaphoreType.DMA((2,)),
            pltpu.SemaphoreType.DMA((2,)),
            pltpu.SemaphoreType.DMA((copies,)),
            pltpu.SemaphoreType.DMA((copies,)),
        ],
        compiler_params=pltpu.CompilerParams(collective_id=2, has_side_effects=True, vmem_limit_bytes=VMEM_BYTES + (0 if mem_len <= 512 else 3 * 1024 * 1024)),
        name="middle",
    )(tokens, attended, cotangent, memory, gains, shifts, down_bias, raise_bias, *weights)


def per_device(
    tokens,
    memory,
    segment_ids,
    padding_mask,
    cotangent,
    prefix_embed,
    prefix_first,
    first_bias,
    prefix_second,
    second_bias,
    adapter_down,
    down_bias,
    adapter_raise,
    raise_bias,
    norm_gain,
    norm_shift,
    self_query,
    self_key,
    self_value,
    self_output,
    cross_query,
    cross_key,
    cross_value,
    cross_output,
    feed_in,
    feed_out,
):
    row_count, length, model_width = tokens.shape
    flat_rows = row_count * length
    n = lax.axis_size("seq")
    batches = lax.axis_size("batch")
    down = adapter_down.shape[1]
    attended, *saved, whole_memory = self_forward(
        n,
        segment_ids,
        padding_mask,
        tokens.reshape(flat_rows, model_width),
        (self_query, self_key, self_value),
        (
            prefix_embed,
            prefix_first,
            first_bias.reshape(1, -1),
            prefix_second,
            second_bias.reshape(1, -1),
        ),
        memory.reshape(-1, model_width),
    )
    layer_output, first_grad, out_grad, memory_part, weight_sums, vector_sums = middle(
        tokens.reshape(flat_rows, model_width),
        attended,
        cotangent.reshape(flat_rows, model_width),
        whole_memory.reshape(-1, model_width),
        norm_gain,
        norm_shift,
        down_bias.reshape(1, -1),
        raise_bias.reshape(1, -1),
        (
            self_output,
            cross_query,
            cross_key,
            cross_value,
            cross_output,
            adapter_down,
            adapter_raise,
            feed_in,
            feed_out,
        ),
        n,
        batches,
    )
    layer_output = layer_output.reshape(row_count, length, model_width)
    token_grad, memory_grad, prefix_grad, vector_sums, full_sums = self_backward(
        n,
        batches,
        first_grad,
        out_grad.reshape(n, -1, HD, length),
        weight_sums,
        memory_part,
        vector_sums,
        saved,
        (self_query, self_key, self_value),
    )
    token_grad = token_grad.reshape(row_count, length, model_width)
    memory_grad = memory_grad.reshape(memory.shape)
    replicated = finish(
        full_sums.reshape(-1, LANES),
        vector_sums,
        prefix_grad,
        prefix_embed,
        prefix_first,
        first_bias.reshape(1, -1),
        prefix_second,
        down,
    )
    replicated = [
        value.reshape(-1) if value.shape[0] == 1 else value for value in replicated
    ]
    return (layer_output, token_grad, memory_grad, *replicated)


def solution(mesh):
    placed = (
        P("batch", "seq", None),
        P("batch", "seq", None),
        P("batch", "seq"),
        P("batch", "seq"),
        P("batch", "seq", None),
        P(),
        P(),
        P(),
        P(),
        P(),
        P(),
        P(),
        P(),
        P(),
        P(),
        P(),
        P(),
        P(),
        P(),
        P(),
        P(),
        P(),
        P(),
        P(),
        P(),
        P(),
    )
    return jax.shard_map(
        per_device,
        mesh=mesh,
        in_specs=placed,
        out_specs=(
            P("batch", "seq", None),
            P("batch", "seq", None),
            P("batch", "seq", None),
            P(),
            P(),
            P(),
            P(),
            P(),
            P(),
            P(),
            P(),
            P(),
            P(),
            P(),
        ),
        check_vma=False,
    )
```

```python
import functools

import jax
import jax.numpy as jnp
from jax import lax
from jax.experimental import pallas as pl
from jax.experimental.pallas import tpu as pltpu
from jax.sharding import PartitionSpec as P

H = 16
HD = 64
LANES = 128
PREFIX_ROWS = 32
VMEM_BYTES = 60 * 1024 * 1024
SUM_ROWS = 16
MESH = pl.DeviceIdType.MESH

masked_score = -1e30
norm_eps = 1e-05

def dot_nn(left, right):
    return lax.dot_general(
        left, right, (((1,), (0,)), ((), ())), preferred_element_type=jnp.float32
    )


def dot_nt(left, right):
    return lax.dot_general(
        left, right, (((1,), (1,)), ((), ())), preferred_element_type=jnp.float32
    )


def dot_tn(left, right):
    return lax.dot_general(
        left, right, (((0,), (0,)), ((), ())), preferred_element_type=jnp.float32
    )


def remote(source, target, send_sem, recv_sem, axis, peer):
    return pltpu.make_async_remote_copy(
        src_ref=source,
        dst_ref=target,
        send_sem=send_sem,
        recv_sem=recv_sem,
        device_id={axis: peer},
        device_id_type=MESH,
    )


def enter(sizes):
    barrier = pltpu.get_barrier_semaphore()
    for axis, size in sizes.items():
        for other in range(size):

            @pl.when(other != lax.axis_index(axis))
            def _():
                pl.semaphore_signal(barrier, inc=1, device_id={axis: other}, device_id_type=MESH)

    pl.semaphore_wait(barrier, sum(sizes.values()) - len(sizes))


def others(size, mine, body):
    for other in range(size):

        @pl.when(other != mine)
        def _():
            body(other)


def rows_of(index, size):
    return pl.ds(pl.multiple_of(index * size, size), size)


def span_of(start, size):
    return pl.ds(pl.multiple_of(start, LANES), size)


def own_columns(ref, first, me, width):
    if width % LANES == 0:
        return ref[:, pl.ds(pl.multiple_of(first + me * width, LANES), width)].astype(jnp.float32)
    share = LANES // width
    block = ref[:, pl.ds(pl.multiple_of(first + me // share * LANES, LANES), LANES)].astype(
        jnp.float32
    )
    picked = block[:, :width]
    for part in range(1, share):
        picked = jnp.where(me % share == part, block[:, part * width : (part + 1) * width], picked)
    return picked


def head_lanes(shape, head):
    lane = lax.broadcasted_iota(jnp.int32, shape, 1)
    return (lane >= head * HD) & (lane < (head + 1) * HD)


def self_forward_kernel(
    n,
    seg_ref,
    pad_ref,
    tok_ref,
    wq_ref,
    wk_ref,
    wv_ref,
    emb_ref,
    first_ref,
    fbias_ref,
    second_ref,
    sbias_ref,
    mem_ref,
    wck_in,
    wcv_in,
    att_ref,
    mkey_ref,
    mvalue_ref,
    qx_out,
    kx_out,
    raw_out,
    pk_out,
    pv_out,
    pkt_out,
    ot_out,
    lse_out,
    send,
    recv,
    meta_send,
    meta,
    kx,
    qx,
    vt,
    hidden,
    pk,
    pv,
    pkt,
    pvt,
    stat,
    acc,
    o_send,
    o_recv,
    mem_all,
    wck,
    wcv,
    send_sem,
    recv_sem,
    meta_send_sem,
    meta_recv_sem,
    o_send_sem,
    o_recv_sem,
    mem_send_sem,
    mem_recv_sem,
    out_sem,
):
    low = jnp.bfloat16
    f32 = jnp.float32
    me = lax.axis_index("seq")
    length, width = tok_ref.shape
    group = width // n
    heads = group // HD
    plane = 2 * length
    planes = n // 2
    block = 2 * LANES
    per_block = block // group
    blocks = width // block
    step_rows = 256
    steps = plane // step_rows
    my_plane = me // 2
    my_side = lax.rem(me, 2)

    def meta_copy(peer, slot):
        return remote(
            meta_send, meta.at[slot], meta_send_sem.at[peer], meta_recv_sem.at[slot], "seq", peer
        )

    def qkv_copy(head, peer, slot):
        return remote(
            send.at[peer, head],
            recv.at[head, slot],
            send_sem.at[head, peer],
            recv_sem.at[head, slot],
            "seq",
            peer,
        )

    def out_copy(head, peer, slot):
        return remote(
            o_send.at[head, peer],
            o_recv.at[slot, head],
            o_send_sem.at[head, peer],
            o_recv_sem.at[head, slot],
            "seq",
            peer,
        )

    def mem_along(which, toward):
        part = mem_all.at[which, my_side]
        return remote(
            part,
            part,
            mem_send_sem.at[(toward + 1) // 2, which],
            mem_recv_sem.at[which],
            "seq",
            me + 2 * toward,
        )

    def mem_across(side):
        part = mem_all.at[:, side]
        return remote(
            part,
            part,
            mem_send_sem.at[0, planes],
            mem_recv_sem.at[planes],
            "seq",
            me + 1 - 2 * my_side,
        )

    def mem_hops(hop, body):
        for toward in (1, -1):
            which = my_plane - toward * hop
            ahead = my_plane + toward

            @pl.when((which >= 0) & (which < planes) & (ahead >= 0) & (ahead < planes))
            def _():
                body(mem_along(which, toward))

    def mem_arrivals(hop):
        for toward in (1, -1):
            which = my_plane - toward * hop

            @pl.when((which >= 0) & (which < planes))
            def _():
                mem_along(which, -toward).wait_recv()

    loads = [
        pltpu.make_async_copy(wck_in, wck, out_sem.at[8]),
        pltpu.make_async_copy(wcv_in, wcv, out_sem.at[9]),
    ]
    for load in loads:
        load.start()
    segments = seg_ref[...]
    tags = jnp.where(pad_ref[...] == 1, segments, -1)
    row = lax.broadcasted_iota(jnp.int32, meta_send.shape, 0)
    meta_send[...] = jnp.where(row == 0, segments, tags)
    mem_all[my_plane, my_side] = mem_ref[...]
    enter({"seq": n})
    others(n, me, lambda peer: meta_copy(peer, me).start())
    meta[me] = meta_send[...]

    def project(step, carry):
        here = lax.rem(my_plane + 1 + step, planes) * (blocks // planes)
        for sub in range(blocks // planes):
            at = here + sub
            columns = rows_of(at, block)
            for which, weight in enumerate((wq_ref, wk_ref, wv_ref)):
                piece = dot_nn(tok_ref[...], weight[:, columns]).T.astype(low)
                for part in range(per_block):
                    for head in range(heads):
                        first = part * group + head * HD
                        send[at * per_block + part, head, which] = piece[first : first + HD]
            for part in range(per_block):
                peer = at * per_block + part

                @pl.when(peer != me)
                def _():
                    qkv_copy(0, peer, me).start()

                @pl.when(peer == me)
                def _():
                    for head in range(heads):
                        recv[head, me] = send[peer, head]

        return carry

    if blocks >= planes:
        lax.fori_loop(0, planes, project, 0)
    else:

        def project_wide(step, carry):
            at = lax.rem(me // per_block + 1 + step, blocks)
            columns = rows_of(at, block)
            for which, weight in enumerate((wq_ref, wk_ref, wv_ref)):
                piece = dot_nn(tok_ref[...], weight[:, columns]).T.astype(low)
                for part in range(per_block):
                    for head in range(heads):
                        first = part * group + head * HD
                        send[at * per_block + part, head, which] = piece[first : first + HD]
            for part in range(per_block):
                peer = at * per_block + part

                @pl.when(peer != me)
                def _():
                    qkv_copy(0, peer, me).start()

                @pl.when(peer == me)
                def _():
                    for head in range(heads):
                        recv[head, me] = send[peer, head]

            return carry

        lax.fori_loop(0, blocks, project_wide, 0)

    mem_hops(0, lambda copy: copy.start())

    hidden[...] = jnp.zeros_like(hidden)
    hidden[: emb_ref.shape[0], :] = jnp.tanh(dot_nn(emb_ref[...], first_ref[...]) + fbias_ref[...])
    hidden_low = hidden[...].astype(low)
    prefix_key = dot_nn(hidden_low, own_columns(second_ref, 0, me, group).astype(low)) + own_columns(
        sbias_ref, 0, me, group
    )
    prefix_value = dot_nn(
        hidden_low, own_columns(second_ref, width, me, group).astype(low)
    ) + own_columns(sbias_ref, width, me, group)
    prefix_row = lax.broadcasted_iota(jnp.int32, (PREFIX_ROWS, HD), 0)
    prefix_open = jnp.where(prefix_row < emb_ref.shape[0], 0.0, masked_score)
    nothing = jnp.zeros((PREFIX_ROWS, HD), f32)
    for head in range(heads):
        here = slice(head * HD, (head + 1) * HD)
        pk[head] = jnp.concatenate([prefix_key[:, here], prefix_open], axis=1).astype(low)
        pv[head] = jnp.concatenate([nothing, prefix_value[:, here]], axis=1).astype(low)
    pkt[...] = prefix_key.T.astype(low).reshape(heads, HD, PREFIX_ROWS)
    pvt[:, :HD, :] = prefix_value.T.astype(low).reshape(heads, HD, PREFIX_ROWS)
    pvt[:, HD:, :] = jnp.ones((heads, SUM_ROWS, PREFIX_ROWS), low)
    vt[:, HD:, :] = jnp.ones((heads, SUM_ROWS, n * length), low)

    def arrive(head, chunk):
        @pl.when(chunk != me)
        def _():
            @pl.when(head == 0)
            def _():
                meta_copy(chunk, chunk).wait_recv()

            qkv_copy(head, chunk, chunk).wait_recv()

        here = rows_of(chunk, length)
        state = lax.broadcasted_iota(jnp.int32, (HD, length), 0)
        qx[head, :HD, here] = (recv[head, chunk, 0].astype(f32) * 0.125).astype(low)
        qx[head, HD:, here] = jnp.where(state == meta[chunk, 0:1, :], 1.0, 0.0).astype(low)
        is_open = jnp.where(state == meta[chunk, 1:2, :], 0.0, masked_score)
        kx[head, here, :] = jnp.concatenate(
            [recv[head, chunk, 1].astype(f32), is_open], axis=0
        ).T.astype(low)
        vt[head, :HD, here] = recv[head, chunk, 2]

    def open_plane(head, which):
        scores = dot_nn(pk[head], qx[head, :, rows_of(which, plane)])
        top = jnp.max(scores, axis=0, keepdims=True)
        raised = jnp.exp(scores - top)
        stat[which, head, 0:1, :] = top
        acc[which, head] = dot_nn(pvt[head], raised.astype(low))

    def pair_part(head, upper, lower, first, keys, diagonal):
        here = slice(first, first + step_rows)
        queries = qx[head, :, span_of(upper * plane + first, step_rows)]
        key_rows = span_of(lower * plane, keys)
        scores = dot_nn(kx[head, key_rows, :], queries)
        if diagonal:
            key_at = lax.broadcasted_iota(jnp.int32, scores.shape, 0)
            query_at = lax.broadcasted_iota(jnp.int32, scores.shape, 1) + first
            scores = jnp.where(key_at <= query_at, scores, masked_score)
        old_top = stat[upper, head, 0:1, here]
        top = jnp.maximum(old_top, jnp.max(scores, axis=0, keepdims=True))
        raised = jnp.exp(scores - top).astype(low)
        stat[upper, head, 0:1, here] = top
        acc[upper, head, :, here] = acc[upper, head, :, here] * jnp.exp(old_top - top) + dot_nn(
            vt[head, :, key_rows], raised
        )

    def pair(head, upper, lower):
        for part in range(steps):
            pair_part(head, upper, lower, part * step_rows, plane, False)

    def pair_diagonal(head, which):
        for part in range(steps):
            pair_part(head, which, which, part * step_rows, (part + 1) * step_rows, True)

    def close_plane(head, which):
        total = acc[which, head, HD : HD + 1, :]
        value = acc[which, head, :HD, :] / total
        acc[which, head, :HD, :] = value
        stat[which, head, 0:1, :] = stat[which, head, 0:1, :] + jnp.log(total)
        for part in range(2):
            chunk = 2 * which + part
            o_send[head, chunk] = value[:, part * length : (part + 1) * length].astype(low)

            @pl.when(chunk != me)
            def _():
                out_copy(head, chunk, me).start()

            @pl.when(chunk == me)
            def _():
                o_recv[me, head] = o_send[head, chunk]

    def project_memory():
        mem_across(1 - my_side).wait_recv()
        for load in loads:
            load.wait()
        whole = mem_all[...].reshape(mkey_ref.shape)

        def one(index, carry):
            here = rows_of(index, block)
            mkey_ref[:, here] = dot_nn(whole, wck[:, here]).astype(low)
            mvalue_ref[:, here] = dot_nn(whole, wcv[:, here]).astype(low)
            return carry

        lax.fori_loop(0, blocks, one, 0)

    def stage(index, carry):
        head = index // planes
        step = lax.rem(index, planes)

        @pl.when(head + 1 < heads)
        def _():
            there = lax.rem(my_plane + 1 + step, planes)
            for part in range(2):
                peer = 2 * there + part

                @pl.when(peer != me)
                def _():
                    qkv_copy(head, peer, me).wait_send()
                    qkv_copy(head + 1, peer, me).start()

        here = lax.rem(my_plane + step, planes)
        arrive(head, 2 * here)
        arrive(head, 2 * here + 1)
        open_plane(head, here)
        pair_diagonal(head, here)

        def earlier(back, inner):
            there = lax.rem(my_plane + back, planes)
            pair(head, jnp.maximum(here, there), jnp.minimum(here, there))
            return inner

        lax.fori_loop(0, step, earlier, 0)
        for hop in range(1, planes - 1):

            @pl.when(index == hop)
            def _():
                mem_arrivals(hop)
                mem_hops(hop, lambda copy: copy.start())

        @pl.when(index == planes - 1)
        def _():
            mem_arrivals(planes - 1)
            mem_across(my_side).start()

        if heads > 1:
            pl.when(index == planes + 1)(project_memory)

        @pl.when((my_plane + step >= planes) | (my_plane == 0))
        def _():
            close_plane(head, here)

        @pl.when(step == planes - 1)
        def _():
            def finish(which, inner):
                close_plane(head, which)
                return inner

            lax.fori_loop(jnp.where(my_plane == 0, planes, my_plane), planes, finish, 0)

        return carry

    lax.fori_loop(0, heads * planes, stage, 0)

    saves = []

    def save(source, target):
        copy = pltpu.make_async_copy(source, target, out_sem.at[len(saves)])
        copy.start()
        saves.append(copy)

    save(qx, qx_out)
    save(kx, kx_out)
    save(recv, raw_out)
    save(pk, pk_out)
    save(pv, pv_out)
    save(pkt, pkt_out)
    save(acc, ot_out)
    save(stat, lse_out)
    if heads == 1:
        project_memory()
    for other in range(n):

        @pl.when(other != me)
        def _():
            for head in range(heads):
                out_copy(head, other, other).wait_recv()

        att_ref[:, other * group : (other + 1) * group] = (
            o_recv[other].reshape(group, length).astype(f32).T.astype(low)
        )

    def drain(peer):
        meta_copy(peer, me).wait_send()
        qkv_copy(heads - 1, peer, me).wait_send()
        for head in range(heads):
            out_copy(head, peer, me).wait_send()

    others(n, me, drain)
    for hop in range(planes - 1):
        mem_hops(hop, lambda copy: copy.wait_send())
    mem_across(my_side).wait_send()
    for copy in saves:
        copy.wait()


def self_forward(n, segments, padding, tokens, weights, prefix, memory, mem_weights):
    length, width = tokens.shape
    group = width // n
    heads = group // HD
    whole = n * length
    planes = n // 2
    low = jnp.bfloat16
    f32 = jnp.float32
    vmem = pl.BlockSpec(memory_space=pltpu.VMEM)
    anywhere = pl.BlockSpec(memory_space=pl.ANY)
    dma = pltpu.SemaphoreType.DMA
    shapes = (
        ((heads, 2 * HD, whole), low),
        ((heads, whole, 2 * HD), low),
        ((heads, n, 3, HD, length), low),
        ((heads, PREFIX_ROWS, 2 * HD), low),
        ((heads, PREFIX_ROWS, 2 * HD), low),
        ((heads, HD, PREFIX_ROWS), low),
        ((planes, heads, HD + SUM_ROWS, 2 * length), f32),
        ((planes, heads, 8, 2 * length), f32),
    )
    qx, kx, raw, pk, pv, pkt, acc, stat = (pltpu.VMEM(*shape) for shape in shapes)
    return pl.pallas_call(
        functools.partial(self_forward_kernel, n),
        out_shape=(
            jax.ShapeDtypeStruct((length, width), low),
            jax.ShapeDtypeStruct((n * memory.shape[0], width), low),
            jax.ShapeDtypeStruct((n * memory.shape[0], width), low),
        )
        + tuple(jax.ShapeDtypeStruct(*shape) for shape in shapes),
        in_specs=[vmem] * 12 + [anywhere] * 2,
        out_specs=(vmem,) * 3 + (anywhere,) * 8,
        scratch_shapes=[
            pltpu.VMEM((n, heads, 3, HD, length), low),
            raw,
            pltpu.VMEM((8, length), jnp.int32),
            pltpu.VMEM((n, 8, length), jnp.int32),
            kx,
            qx,
            pltpu.VMEM((heads, HD + SUM_ROWS, whole), low),
            pltpu.VMEM((PREFIX_ROWS, weights[0].shape[0] // 2), f32),
            pk,
            pv,
            pkt,
            pltpu.VMEM((heads, HD + SUM_ROWS, PREFIX_ROWS), low),
            stat,
            acc,
            pltpu.VMEM((heads, n, HD, length), low),
            pltpu.VMEM((n, heads, HD, length), low),
            pltpu.VMEM((planes, 2) + memory.shape, low),
            pltpu.VMEM((width, width), low),
            pltpu.VMEM((width, width), low),
            dma((heads, n)),
            dma((heads, n)),
            dma((n,)),
            dma((n,)),
            dma((heads, n)),
            dma((heads, n)),
            dma((2, planes + 1)),
            dma((planes + 1,)),
            dma((10,)),
        ],
        compiler_params=pltpu.CompilerParams(
            collective_id=0, has_side_effects=True, vmem_limit_bytes=VMEM_BYTES
        ),
        name="self_forward",
    )(segments, padding, tokens, *weights, *prefix, memory, *mem_weights)


def self_backward_kernel(
    n,
    batches,
    base_ref,
    do_in,
    sums_in,
    mkey_in,
    mvalue_in,
    wck_in,
    wcv_in,
    vecs_in,
    qx_in,
    kx_in,
    raw_in,
    pk_in,
    pv_in,
    pkt_in,
    ot_in,
    lse_in,
    wq_in,
    wk_in,
    wv_in,
    tg_ref,
    mgrad_ref,
    pkv_ref,
    vecs_ref,
    full_out,
    do_recv,
    qx,
    kx,
    raw,
    kt,
    qv,
    q0,
    dox,
    do0,
    pk,
    pv,
    pkt,
    ot,
    stat,
    weights,
    dqt,
    dkv,
    g_send,
    g_recv,
    pre_ref,
    pre_all,
    pre_sum,
    pre_recv,
    sums_mine,
    sums_core,
    sums_x,
    sums_side,
    sums_z,
    full,
    mkey,
    mvalue,
    wck,
    wcv,
    mem_part,
    mem_side,
    mem_up,
    mem_down,
    vec_all,
    vec_sum,
    vec_y,
    vec_both,
    vec_z,
    do_send_sem,
    do_recv_sem,
    g_send_sem,
    g_recv_sem,
    in_sem,
    send_sem,
    recv_sem,
):
    low = jnp.bfloat16
    f32 = jnp.float32
    me = lax.axis_index("seq")
    length, width = base_ref.shape
    group = width // n
    heads = group // HD
    plane = 2 * length
    planes = n // 2
    step_rows = 256
    steps = plane // step_rows
    my_batch = lax.axis_index("batch")
    my_core = lax.rem(my_batch, 2)
    my_high = my_batch // 2
    highs = batches // 2
    my_plane = me // 2
    my_side = lax.rem(me, 2)
    beside = me + 1 - 2 * my_side
    used = [0]

    def numbers(count):
        used[0] += count
        return used[0] - count

    core_slot = numbers(2)
    x_slot = numbers(2 * highs)
    y_slot = numbers(3)
    z_slot = numbers(2 * planes)
    up_slot = numbers(planes)
    down_slot = numbers(planes)
    va_slot = numbers(batches)
    vb_slot = numbers(1)
    vc_slot = numbers(planes)
    pa_slot = numbers(batches)
    pb_slot = numbers(n)

    def send(source, target, first, peer_index, slot_index, axis, peer):
        return remote(
            source,
            target,
            send_sem.at[first + peer_index],
            recv_sem.at[first + slot_index],
            axis,
            peer,
        )

    half_rows = 2 * planes * highs * sums_z.shape[1]
    x_rows = half_rows // highs
    y_rows = x_rows // 2
    z_rows = y_rows // planes
    x_row = pl.multiple_of(my_high * x_rows, x_rows)
    y_row = pl.multiple_of(x_row + my_side * y_rows, y_rows)

    def part(row, count):
        return sums_mine.at[pl.ds(pl.multiple_of(row, count), count)]

    def reduce_core():
        return send(
            sums_in.at[1 - my_core], sums_core, core_slot, 0, 0, "batch", my_batch + 1 - 2 * my_core
        )

    def reduce_x(peer, slot):
        return send(
            part(peer * x_rows, x_rows),
            sums_x.at[slot],
            x_slot,
            peer,
            slot,
            "batch",
            2 * peer + my_core,
        )

    def reduce_y():
        return send(
            part(x_row + (1 - my_side) * y_rows, y_rows), sums_side, y_slot, 0, 0, "seq", beside
        )

    def reduce_z(peer, slot):
        return send(
            part(y_row + peer * z_rows, z_rows),
            sums_z.at[slot],
            z_slot,
            peer,
            slot,
            "seq",
            2 * peer + my_side,
        )

    def gather_z(peer, slot):
        piece = full.at[my_core, my_high, my_side, slot]
        return send(piece, piece, z_slot + planes, peer, slot, "seq", 2 * peer + my_side)

    def gather_y(side):
        piece = full.at[my_core, my_high, side]
        return send(piece, piece, y_slot + 1, 0, 0, "seq", beside)

    def gather_x(peer, slot):
        piece = full.at[my_core, slot]
        return send(piece, piece, x_slot + highs, peer, slot, "batch", 2 * peer + my_core)

    def gather_core(core):
        piece = full.at[core]
        return send(piece, piece, core_slot + 1, 0, 0, "batch", my_batch + 1 - 2 * my_core)

    def mem_across():
        return send(
            mem_part.at[:, 1 - my_side], mem_side, y_slot + 2, 0, 0, "seq", beside
        )

    def mem_hop(target, toward, peer=None):
        buffer, slot = (mem_up, up_slot) if toward > 0 else (mem_down, down_slot)
        return send(
            mem_part.at[target, my_side],
            buffer.at[target],
            slot,
            target,
            target,
            "seq",
            me + 2 * toward if peer is None else peer,
        )

    def mem_from(target, toward):
        return mem_hop(target, toward, me - 2 * toward)

    def mem_pass(toward):
        buffer = mem_up if toward > 0 else mem_down
        first = 0 if toward > 0 else planes - 1
        for target in range(planes):

            @pl.when((target - my_plane) * toward > 0)
            def _():
                @pl.when(my_plane != first)
                def _():
                    mem_from(target, toward).wait_recv()
                    mem_part[target, my_side] = (
                        mem_part[target, my_side].astype(f32) + buffer[target].astype(f32)
                    ).astype(low)

                mem_hop(target, toward).start()

    def mem_stage(at):
        pl.when(my_plane == at)(lambda: mem_pass(1))
        pl.when(my_plane == planes - 1 - at)(lambda: mem_pass(-1))

    def mem_end():
        value = mem_part[my_plane, my_side].astype(f32)
        mgrad_ref[...] = value.astype(low)

        @pl.when(my_plane > 0)
        def _():
            mem_from(my_plane, 1).wait_recv()
            mgrad_ref[...] = (mgrad_ref[...].astype(f32) + mem_up[my_plane].astype(f32)).astype(low)

        @pl.when(my_plane < planes - 1)
        def _():
            mem_from(my_plane, -1).wait_recv()
            mgrad_ref[...] = (
                mgrad_ref[...].astype(f32) + mem_down[my_plane].astype(f32)
            ).astype(low)

    def mem_drain():
        for target in range(planes):

            @pl.when(target > my_plane)
            def _():
                mem_hop(target, 1).wait_send()

            @pl.when(target < my_plane)
            def _():
                mem_hop(target, -1).wait_send()

    def vec_a(peer, slot):
        return send(vecs_in, vec_all.at[slot], va_slot, peer, slot, "batch", peer)

    def vec_b(side):
        return send(vec_sum, vec_y.at[side], vb_slot, 0, 0, "seq", beside)

    def vec_c(peer, slot):
        return send(vec_both, vec_z.at[slot], vc_slot, peer, slot, "seq", 2 * peer + my_side)

    def pre_a(peer, slot):
        return send(pre_ref, pre_all.at[slot], pa_slot, peer, slot, "batch", peer)

    def pre_b(peer, slot):
        return send(pre_sum, pre_recv.at[slot], pb_slot, peer, slot, "seq", peer)

    def do_copy(head, peer, slot):
        return remote(
            do_in.at[peer, head],
            do_recv.at[head, slot],
            do_send_sem.at[head, peer],
            do_recv_sem.at[head, slot],
            "seq",
            peer,
        )

    def q_copy(head, peer, slot):
        return remote(
            g_send.at[peer, head, 0],
            g_recv.at[0, slot, head],
            g_send_sem.at[0, head, peer],
            g_recv_sem.at[0, head, slot],
            "seq",
            peer,
        )

    def kv_copy(head, peer, slot):
        return remote(
            g_send.at[peer, head, pl.ds(1, 2)],
            g_recv.at[pl.ds(1, 2), slot, head],
            g_send_sem.at[1, head, peer],
            g_recv_sem.at[1, head, slot],
            "seq",
            peer,
        )

    def added(ref, size):
        value = ref[0].astype(f32)
        for other in range(1, size):
            value = value + ref[other].astype(f32)
        return value

    loads = [
        pltpu.make_async_copy(source, target, in_sem.at[index])
        for index, (source, target) in enumerate(
            (
                (raw_in, raw),
                (kx_in, kx),
                (pk_in, pk),
                (pv_in, pv),
                (pkt_in, pkt),
                (qx_in, qx),
                (ot_in, ot),
                (lse_in, stat),
                (sums_in.at[my_core], sums_mine),
                (vecs_in, vec_all.at[my_batch]),
                (mkey_in, mkey),
                (mvalue_in, mvalue),
                (wck_in, wck),
                (wcv_in, wcv),
                (wq_in, weights.at[0]),
                (wk_in, weights.at[1]),
                (wv_in, weights.at[2]),
            )
        )
    ]
    own_do = pltpu.make_async_copy(do_in.at[me], do_recv.at[:, me], in_sem.at[len(loads)])
    own_do.start()
    for load in loads:
        load.start()
    enter({"seq": n, "batch": batches})
    others(n, me, lambda peer: do_copy(0, peer, me).start())
    reduce_core().start()
    others(batches, my_batch, lambda peer: vec_a(peer, my_batch).start())
    dox[:, :HD, :] = jnp.zeros((heads, HD, n * length), low)
    dkv[...] = jnp.zeros_like(dkv)
    pre_ref[...] = jnp.zeros_like(pre_ref)
    for load in loads[:14]:
        load.wait()
    own_do.wait()
    zero = jnp.zeros((HD, length), f32)

    def turn(index, carry):
        head = index // n
        chunk = lax.rem(index, n)
        here = rows_of(chunk, length)
        kt[head, :, here] = raw[head, chunk, 1]
        query = raw[head, chunk, 0].astype(f32) * 0.125
        both = jnp.concatenate([query, raw[head, chunk, 2].astype(f32)], axis=0).T
        qv[head, here, :] = both.astype(low)
        q0[head, here, :] = jnp.where(head_lanes(both.shape, 0), both, 0.0).astype(low)
        return carry

    lax.fori_loop(0, heads * n, turn, 0)

    def memory_back(index, carry):
        here = rows_of(index, step_rows)
        value = dot_nt(mkey[...], wck[here, :]) + dot_nt(mvalue[...], wcv[here, :])
        mem_part[:, :, :, here] = value.astype(low).reshape(mem_part.shape[:3] + (step_rows,))
        return carry

    lax.fori_loop(0, width // step_rows, memory_back, 0)
    mem_across().start()

    def next_head(head):
        @pl.when(head + 1 < heads)
        def _():
            def move(peer):
                do_copy(head, peer, me).wait_send()
                do_copy(head + 1, peer, me).start()

            others(n, me, move)

    def arrive(head, which):
        for part in range(2):
            chunk = 2 * which + part

            @pl.when(chunk != me)
            def _():
                do_copy(head, chunk, chunk).wait_recv()

            grads = do_recv[head, chunk]
            dox[head, HD:, rows_of(chunk, length)] = grads
            grads = grads.astype(f32)
            do0[head, rows_of(chunk, length), :] = (
                jnp.concatenate([zero, grads], axis=0).T.astype(low)
            )
            here = slice(part * length, (part + 1) * length)
            stat[which, head, 1:2, here] = jnp.sum(
                grads * ot[which, head, :HD, here], axis=0, keepdims=True
            )
        here = rows_of(which, plane)
        weight = jnp.exp(dot_nn(pk[head], qx[head, :, here]) - stat[which, head, 0:1, :])
        slope = weight * (dot_nn(pv[head], dox[head, :, here]) - stat[which, head, 1:2, :])
        slope = slope.astype(low)
        pre_ref[head] += dot_nn(slope, q0[head, here, :]) + dot_nn(
            weight.astype(low), do0[head, here, :]
        )
        dqt[which, head] = dot_nn(pkt[head], slope)

    def plus(first, second):
        return (first.astype(f32) + second.astype(f32)).astype(low)

    def sum_one():
        reduce_core().wait_recv()
        sums_mine[...] = plus(sums_mine[...], sums_core[...])
        others(highs, my_high, lambda peer: reduce_x(peer, my_high).start())

    def sum_two():
        here = pl.ds(x_row, x_rows)
        others(highs, my_high, lambda peer: reduce_x(peer, peer).wait_recv())
        sums_x[my_high] = sums_mine[here]
        sums_mine[here] = added(sums_x, highs).astype(low)
        reduce_y().start()

    def sum_three():
        here = pl.ds(y_row, y_rows)
        reduce_y().wait_recv()
        sums_mine[here] = plus(sums_mine[here], sums_side[...])
        others(planes, my_plane, lambda peer: reduce_z(peer, my_plane).start())

    def sum_four():
        here = pl.ds(pl.multiple_of(y_row + my_plane * z_rows, z_rows), z_rows)
        others(planes, my_plane, lambda peer: reduce_z(peer, peer).wait_recv())
        sums_z[my_plane] = sums_mine[here]
        full[my_core, my_high, my_side, my_plane] = added(sums_z, planes).astype(low)
        others(planes, my_plane, lambda peer: gather_z(peer, my_plane).start())

    def sum_five():
        others(planes, my_plane, lambda peer: gather_z(peer, peer).wait_recv())
        gather_y(my_side).start()

    def sum_six():
        gather_y(1 - my_side).wait_recv()
        others(highs, my_high, lambda peer: gather_x(peer, my_high).start())

    def sum_seven():
        others(highs, my_high, lambda peer: gather_x(peer, peer).wait_recv())
        gather_core(my_core).start()

    def sum_end():
        gather_core(1 - my_core).wait_recv()
        save_full.start()

    def vec_one():
        others(batches, my_batch, lambda peer: vec_a(peer, peer).wait_recv())
        vec_sum[...] = added(vec_all, batches)
        vec_b(my_side).start()
        vec_y[my_side] = vec_sum[...]

    def vec_two():
        vec_b(1 - my_side).wait_recv()
        vec_both[...] = vec_y[0] + vec_y[1]
        others(planes, my_plane, lambda peer: vec_c(peer, my_plane).start())
        vec_z[my_plane] = vec_both[...]

    def vec_end():
        others(planes, my_plane, lambda peer: vec_c(peer, peer).wait_recv())
        vecs_ref[...] = added(vec_z, planes)

    def mem_one():
        mem_across().wait_recv()
        mem_part[:, my_side] = plus(mem_part[:, my_side], mem_side[...])

    def stage_pa():
        others(batches, my_batch, lambda peer: pre_a(peer, my_batch).start())
        pre_all[my_batch] = pre_ref[...]

    def stage_pb():
        others(batches, my_batch, lambda peer: pre_a(peer, peer).wait_recv())
        pre_sum[...] = added(pre_all, batches).astype(low)
        others(n, me, lambda peer: pre_b(peer, me).start())
        pre_recv[me] = pre_sum[...]

    save_full = pltpu.make_async_copy(full, full_out, in_sem.at[0])

    def pair(head, upper, lower, diagonal):
        for part in range(steps):
            first = part * step_rows if diagonal else 0
            count = plane - first
            keys = span_of(lower * plane + part * step_rows, step_rows)
            here = span_of(upper * plane + first, count)
            at = slice(first, plane)
            scores = dot_nn(kx[head, keys, :], qx[head, :, here])
            weight = jnp.exp(scores - stat[upper, head, 0:1, at])
            if diagonal:
                key_at = lax.broadcasted_iota(jnp.int32, scores.shape, 0)
                query_at = lax.broadcasted_iota(jnp.int32, scores.shape, 1)
                weight = jnp.where(key_at <= query_at, weight, 0.0)
            slope = dot_nn(qv[head, keys, :], dox[head, :, here]) - stat[upper, head, 1:2, at]
            slope = (weight * slope).astype(low)
            dkv[head, keys, :] += dot_nn(slope, q0[head, here, :]) + dot_nn(
                weight.astype(low), do0[head, here, :]
            )
            dqt[upper, head, :, at] += dot_nn(kt[head, :, keys], slope)

    def hand_queries(head, which):
        for part in range(2):
            chunk = 2 * which + part
            g_send[chunk, head, 0] = (
                dqt[which, head, :, part * length : (part + 1) * length] * 0.125
            ).astype(low)

            @pl.when(chunk != me)
            def _():
                q_copy(head, chunk, me).start()

            @pl.when(chunk == me)
            def _():
                g_recv[0, me, head] = g_send[chunk, head, 0]

    def hand_keys(head, which):
        for part in range(2):
            chunk = 2 * which + part
            turned = dkv[head, rows_of(chunk, length), :].T.astype(low)
            g_send[chunk, head, 1] = turned[:HD]
            g_send[chunk, head, 2] = turned[HD:]

            @pl.when(chunk != me)
            def _():
                kv_copy(head, chunk, me).start()

            @pl.when(chunk == me)
            def _():
                g_recv[pl.ds(1, 2), me, head] = g_send[chunk, head, pl.ds(1, 2)]

    rising = my_plane >= planes // 2
    total = heads * planes * (planes + 1) // 2
    hooks = [
        (2, sum_one),
        (3, mem_one),
        (4, lambda: mem_stage(0)),
        (5, sum_two),
        (5, vec_one),
        (7, sum_three),
        (8, vec_two),
        (9, sum_four),
        (10, sum_five),
        (12, sum_six),
        (15, sum_seven),
        (16, vec_end),
    ] + [(4 + 3 * at, functools.partial(mem_stage, at)) for at in range(1, planes - 1)]
    final = total - planes * (planes + 1) // 2
    hooks += [(final + planes + 1, stage_pa), (final + 2 * planes - 1, stage_pb)]

    def hook(pairs):
        for number, body in sorted(hooks, key=lambda item: item[0]):
            pl.when(pairs == number)(body)


    def stage(index, carry):
        head = index // planes
        step = lax.rem(index, planes)
        here = jnp.where(rising, step, planes - 1 - step)

        @pl.when((step == 0) | ((step == 1) & jnp.logical_not(rising)))
        def _():
            @pl.when(rising | (step == 0))
            def _():
                arrive(head, here)

            @pl.when(jnp.logical_not(rising) & (step == 1))
            def _():
                next_head(head)

                def rest(which, inner):
                    arrive(head, planes - 2 - which)
                    return inner

                lax.fori_loop(0, planes - 1, rest, 0)

        begun = head * (planes * (planes + 1) // 2) + step * planes - step * (step - 1) // 2
        hook(begun)
        pair(head, here, here, True)

        @pl.when(rising)
        def _():
            hand_queries(head, here)

        @pl.when(jnp.logical_not(rising))
        def _():
            hand_keys(head, here)

        def far(at, inner):
            there = jnp.where(rising, here + 1 + at, here - 1 - at)

            @pl.when(rising & (step == 0))
            def _():
                arrive(head, there)

            hook(begun + 1 + at)
            pair(head, jnp.maximum(here, there), jnp.minimum(here, there), False)
            return inner

        lax.fori_loop(0, planes - 1 - step, far, 0)

        @pl.when(rising & (step == 0))
        def _():
            next_head(head)

        @pl.when(rising)
        def _():
            hand_keys(head, here)

        @pl.when(jnp.logical_not(rising))
        def _():
            hand_queries(head, here)

        return carry

    lax.fori_loop(0, heads * planes, stage, 0)
    sum_end()
    mem_end()
    for load in loads[14:]:
        load.wait()

    def gathered(peer):
        for head in range(heads):
            q_copy(head, peer, peer).wait_recv()
            kv_copy(head, peer, peer).wait_recv()

    others(n, me, gathered)
    tile = 256
    grads = [g_recv[which].reshape(width, length) for which in range(3)]

    def last_product(index, carry):
        here = rows_of(index, tile)
        value = dot_nn(weights[0, here, :], grads[0])
        value = value + dot_nn(weights[1, here, :], grads[1])
        value = value + dot_nn(weights[2, here, :], grads[2])
        tg_ref[:, here] = (base_ref[:, here] + value.T).astype(low)
        return carry

    lax.fori_loop(0, width // tile, last_product, 0)
    for other in range(n):

        @pl.when(other != me)
        def _():
            pre_b(other, other).wait_recv()

        value = pre_recv[other].astype(f32)
        for which in range(2):
            pkv_ref[:, which * width + other * group : which * width + (other + 1) * group] = (
                jnp.concatenate(
                    [value[head, :, which * HD : (which + 1) * HD] for head in range(heads)], axis=1
                )
            )

    def drain(peer):
        do_copy(heads - 1, peer, me).wait_send()
        pre_b(peer, me).wait_send()
        for head in range(heads):
            q_copy(head, peer, me).wait_send()
            kv_copy(head, peer, me).wait_send()

    others(n, me, drain)
    others(batches, my_batch, lambda peer: pre_a(peer, my_batch).wait_send())
    others(batches, my_batch, lambda peer: vec_a(peer, my_batch).wait_send())
    reduce_core().wait_send()
    others(highs, my_high, lambda peer: reduce_x(peer, my_high).wait_send())
    reduce_y().wait_send()
    others(planes, my_plane, lambda peer: reduce_z(peer, my_plane).wait_send())
    others(planes, my_plane, lambda peer: gather_z(peer, my_plane).wait_send())
    gather_y(my_side).wait_send()
    others(highs, my_high, lambda peer: gather_x(peer, my_high).wait_send())
    gather_core(my_core).wait_send()
    mem_across().wait_send()
    mem_drain()
    others(planes, my_plane, lambda peer: vec_c(peer, my_plane).wait_send())
    vec_b(my_side).wait_send()
    save_full.wait()


def self_backward(
    n, batches, first_grad, out_grad, sums, mem_grads, mem_weights, vecs, saved, weights
):
    length, width = first_grad.shape
    group = width // n
    heads = group // HD
    whole = n * length
    planes = n // 2
    low = jnp.bfloat16
    f32 = jnp.float32
    vmem = pl.BlockSpec(memory_space=pltpu.VMEM)
    anywhere = pl.BlockSpec(memory_space=pl.ANY)
    dma = pltpu.SemaphoreType.DMA
    sum_rows = sums.shape[0] // (n * batches)
    mem_len = mem_grads[0].shape[0]
    mem_rows = mem_len // n
    mem_part = pltpu.VMEM((planes, mem_rows, width), low)
    mem_low = pltpu.VMEM((mem_len, width), low)
    square = pltpu.VMEM((width, width), low)
    vec = pltpu.VMEM((8, width), f32)
    copies = 6 + 2 * (batches // 2) + 5 * planes + 2 * batches + n
    qx, kx, raw, pk, pv, pkt, ot, stat = (pltpu.VMEM(value.shape, value.dtype) for value in saved)
    return pl.pallas_call(
        functools.partial(self_backward_kernel, n, batches),
        out_shape=(
            jax.ShapeDtypeStruct((length, width), low),
            jax.ShapeDtypeStruct((mem_rows, width), low),
            jax.ShapeDtypeStruct((PREFIX_ROWS, 2 * width), f32),
            jax.ShapeDtypeStruct((8, width), f32),
            jax.ShapeDtypeStruct((2, batches // 2, 2, planes, sum_rows, LANES), low),
        ),
        in_specs=[vmem] + [anywhere] * 18,
        out_specs=(vmem, vmem, vmem, vmem, anywhere),
        scratch_shapes=[
            pltpu.VMEM((heads, n, HD, length), low),
            qx,
            kx,
            raw,
            pltpu.VMEM((heads, HD, whole), low),
            pltpu.VMEM((heads, whole, 2 * HD), low),
            pltpu.VMEM((heads, whole, 2 * HD), low),
            pltpu.VMEM((heads, 2 * HD, whole), low),
            pltpu.VMEM((heads, whole, 2 * HD), low),
            pk,
            pv,
            pkt,
            ot,
            stat,
            pltpu.VMEM((3, width, width), low),
            pltpu.VMEM((planes, heads, HD, 2 * length), f32),
            pltpu.VMEM((heads, whole, 2 * HD), f32),
            pltpu.VMEM((n, heads, 3, HD, length), low),
            pltpu.VMEM((3, n, heads, HD, length), low),
            pltpu.VMEM((heads, PREFIX_ROWS, 2 * HD), f32),
            pltpu.VMEM((batches, heads, PREFIX_ROWS, 2 * HD), f32),
            pltpu.VMEM((heads, PREFIX_ROWS, 2 * HD), low),
            pltpu.VMEM((n, heads, PREFIX_ROWS, 2 * HD), low),
            pltpu.VMEM((sums.shape[0] // 2, LANES), low),
            pltpu.VMEM((sums.shape[0] // 2, LANES), low),
            pltpu.VMEM((batches // 2, sums.shape[0] // batches, LANES), low),
            pltpu.VMEM((planes * sum_rows, LANES), low),
            pltpu.VMEM((planes, sum_rows, LANES), low),
            pltpu.VMEM((2, batches // 2, 2, planes, sum_rows, LANES), low),
            mem_low,
            mem_low,
            square,
            square,
            pltpu.VMEM((planes, 2, mem_rows, width), low),
            mem_part,
            mem_part,
            mem_part,
            pltpu.VMEM((batches, 8, width), f32),
            vec,
            pltpu.VMEM((2, 8, width), f32),
            vec,
            pltpu.VMEM((planes, 8, width), f32),
            dma((heads, n)),
            dma((heads, n)),
            dma((2, heads, n)),
            dma((2, heads, n)),
            dma((18,)),
            dma((copies,)),
            dma((copies,)),
        ],
        compiler_params=pltpu.CompilerParams(
            collective_id=1, has_side_effects=True, vmem_limit_bytes=VMEM_BYTES
        ),
        name="self_backward",
    )(
        first_grad,
        out_grad,
        sums.reshape(2, -1, LANES),
        *mem_grads,
        *mem_weights,
        vecs,
        *saved,
        *weights,
    )


def both_parts(value):
    high = value.astype(jnp.bfloat16).astype(jnp.float32)
    return jnp.concatenate([high, value - high], axis=0).astype(jnp.bfloat16)


def finish_kernel(
    full_ref,
    vecs_ref,
    pkv_ref,
    emb_ref,
    first_ref,
    fbias_ref,
    second_ref,
    embed_out,
    first_out,
    fbias_out,
    second_out,
    sbias_out,
    down_out,
    dbias_out,
    raise_out,
    rbias_out,
    gain_out,
    shift_out,
    first_grad,
    second_grad,
    down_grad,
    raise_grad,
    emb,
    hidden,
    out_sem,
):
    f32 = jnp.float32
    low = jnp.bfloat16
    width = emb_ref.shape[1]
    down = dbias_out.shape[1]
    count = emb_ref.shape[0]
    saves = []

    def save(source, target, rows=None):
        if rows is not None:
            source, target = source.at[rows], target.at[rows]
        copy = pltpu.make_async_copy(source, target, out_sem.at[len(saves)])
        copy.start()
        saves.append(copy)

    first = down * width // LANES
    for index in range(width // LANES):
        raise_grad[:, index * LANES : (index + 1) * LANES] = full_ref[
            first + index * down : first + (index + 1) * down, :
        ].astype(f32)
    save(raise_grad, raise_out)
    for index in range(down // LANES):
        down_grad[:, index * LANES : (index + 1) * LANES] = full_ref[
            index * width : (index + 1) * width, :
        ].astype(f32)
    save(down_grad, down_out)
    emb[...] = jnp.zeros_like(emb)
    emb[:count, :] = emb_ref[...].astype(f32)
    emb_low = emb[...].astype(low)
    row = lax.broadcasted_iota(jnp.int32, hidden.shape, 0)
    hidden[...] = jnp.where(
        row < count, jnp.tanh(dot_nn(emb_low, first_ref[...]) + fbias_ref[...]), 0.0
    )
    value = hidden[...]
    prefix = pkv_ref[...]
    parts = both_parts(prefix)
    hidden_twice = jnp.concatenate([value, value], axis=0).T.astype(low)
    tile = 128
    for index in range(second_grad.shape[0] // tile):
        here = slice(index * tile, (index + 1) * tile)
        second_grad[here, :] = dot_nn(hidden_twice[here, :], parts)
        save(second_grad, second_out, here)
    sbias_out[...] = jnp.sum(prefix, axis=0, keepdims=True)
    grad = dot_nt(parts, second_ref[...])
    grad = (grad[:PREFIX_ROWS] + grad[PREFIX_ROWS:]) * (1.0 - value * value)
    fbias_out[...] = jnp.sum(grad, axis=0, keepdims=True)
    parts = both_parts(grad)
    emb_twice = jnp.concatenate([emb[...], emb[...]], axis=0).T.astype(low)
    first_grad[...] = dot_nn(emb_twice, parts)
    save(first_grad, first_out)
    back = dot_nt(parts, first_ref[...])
    embed_out[...] = (back[:PREFIX_ROWS] + back[PREFIX_ROWS:])[:count, :]
    rbias_out[...] = vecs_ref[0:1, :]
    dbias_out[...] = vecs_ref[1:2, :down]
    gain_out[...] = vecs_ref[2:5, :]
    shift_out[...] = vecs_ref[5:8, :]
    for copy in saves:
        copy.wait()


def finish(full, vecs, prefix_grad, embed, first, first_bias, second, down):
    f32 = jnp.float32
    count, width = embed.shape
    hidden = first.shape[1]
    vmem = pl.BlockSpec(memory_space=pltpu.VMEM)
    anywhere = pl.BlockSpec(memory_space=pl.ANY)
    shapes = (
        (count, width),
        (width, hidden),
        (1, hidden),
        (hidden, 2 * width),
        (1, 2 * width),
        (width, down),
        (1, down),
        (down, width),
        (1, width),
        (3, width),
        (3, width),
    )
    return pl.pallas_call(
        finish_kernel,
        out_shape=tuple(jax.ShapeDtypeStruct(shape, f32) for shape in shapes),
        in_specs=[vmem] * 7,
        out_specs=(
            vmem,
            anywhere,
            vmem,
            anywhere,
            vmem,
            anywhere,
            vmem,
            anywhere,
            vmem,
            vmem,
            vmem,
        ),
        scratch_shapes=[
            pltpu.VMEM((width, hidden), f32),
            pltpu.VMEM((hidden, 2 * width), f32),
            pltpu.VMEM((width, down), f32),
            pltpu.VMEM((down, width), f32),
            pltpu.VMEM((PREFIX_ROWS, width), f32),
            pltpu.VMEM((PREFIX_ROWS, hidden), f32),
            pltpu.SemaphoreType.DMA((3 + hidden // 128,)),
        ],
        compiler_params=pltpu.CompilerParams(vmem_limit_bytes=VMEM_BYTES),
        name="finish",
    )(full, vecs, prefix_grad, embed, first, first_bias, second)


def gelu_pair(value):
    scaled = jnp.abs(value) * 0.7071067811865476
    step = 1.0 / (1.0 + 0.3275911 * scaled)
    bell = jnp.exp(-scaled * scaled)
    poly = step * (
        0.254829592
        + step
        * (-0.284496736 + step * (1.421413741 + step * (-1.453152027 + step * 1.061405429)))
    )
    tail = 0.5 * poly * bell
    share = jnp.where(value >= 0.0, 1.0 - tail, tail)
    return value * share, share + value * (bell * 0.3989422804014327)


def normed(value):
    center = jnp.mean(value, axis=-1, keepdims=True)
    centered = value - center
    scale = lax.rsqrt(jnp.mean(centered * centered, axis=-1, keepdims=True) + norm_eps)
    return centered * scale, scale


def norm_back(grad, scale, unit):
    return scale * (
        grad
        - jnp.mean(grad, axis=-1, keepdims=True)
        - unit * jnp.mean(grad * unit, axis=-1, keepdims=True)
    )


def middle_kernel(
    tok_ref,
    att_ref,
    cot_ref,
    mkey_ref,
    mvalue_ref,
    gain_ref,
    shift_ref,
    dbias_ref,
    rbias_ref,
    wo_in,
    wcq_in,
    wco_in,
    wd_in,
    wr_in,
    win_in,
    wout_in,
    out_ref,
    fgrad_ref,
    ograd_ref,
    mkey_out,
    mvalue_out,
    sums_ref,
    vecs_ref,
    wo,
    wcq,
    wco,
    wd,
    wr,
    win,
    wout,
    unit_one,
    unit_two,
    work,
    total,
    scale_one,
    scale_two,
    low_one,
    low_two,
    low_three,
    query,
    crossed,
    weights,
    slopes,
    pre_now,
    down_act,
    down_slope,
    down_grad,
    load_sem,
    win_sem,
    wout_sem,
):
    length, width = tok_ref.shape
    tile = win.shape[2]
    tiles = win_in.shape[1] // tile
    rows_step = 128
    low = jnp.bfloat16
    f32 = jnp.float32

    sources = (wo_in, wcq_in, wco_in, wd_in, wr_in)
    targets = (wo, wcq, wco, wd, wr)
    loads = [
        pltpu.make_async_copy(source, target, load_sem.at[index])
        for index, (source, target) in enumerate(zip(sources, targets))
    ]

    def win_load(which):
        slot = lax.rem(which, 2)
        return pltpu.make_async_copy(
            win_in.at[:, rows_of(which, tile)], win.at[slot], win_sem.at[slot]
        )

    def wout_load(which):
        slot = lax.rem(which, 2)
        return pltpu.make_async_copy(
            wout_in.at[rows_of(which, tile), :], wout.at[slot], wout_sem.at[slot]
        )

    for load in loads[:3]:
        load.start()
    for which in range(2):
        win_load(which).start()
        wout_load(which).start()
    for load in loads[3:]:
        load.start()

    def by_columns(extent, step, body):
        def one(index, carry):
            body(pl.ds(pl.multiple_of(index * step, step), step))
            return carry

        lax.fori_loop(0, extent // step, one, 0)

    def by_rows(body, init=0):
        def one(index, carry):
            return body(rows_of(index, rows_step), carry)

        return lax.fori_loop(0, length // rows_step, one, init)

    cols = 512
    half = width // 2

    loads[0].wait()

    def project_out(here):
        work[:, here] = tok_ref[:, here].astype(f32) + dot_nn(att_ref[...], wo[:, here])

    by_columns(width, cols, project_out)

    def first_norm(here, carry):
        unit, scale = normed(work[here, :])
        unit_one[here, :] = unit
        scale_one[here, :] = scale
        value = unit * gain_ref[0:1, :] + shift_ref[0:1, :]
        work[here, :] = value
        low_one[here, :] = value.astype(low)
        return carry

    by_rows(first_norm)

    loads[1].wait()

    def project_query(here):
        query[:, here] = dot_nn(low_one[...], wcq[:, here]).astype(low)

    by_columns(width, cols, project_query)
    per_block = LANES // HD

    def head_queries(here, head):
        both = query[:, here].astype(f32) * 0.125
        return jnp.where(head_lanes(both.shape, head), both, 0.0).astype(low)

    def cross_forward(block):
        here = rows_of(block, LANES)
        keys = mkey_ref[:, here]
        values = mvalue_ref[:, here].astype(f32).T.astype(low)
        outs = []
        for head in range(per_block):
            scores = dot_nt(keys, head_queries(here, head))
            raised = jnp.exp(scores - jnp.max(scores, axis=0, keepdims=True))
            share = 1.0 / jnp.sum(raised, axis=0, keepdims=True)
            weight = (raised * share).astype(low)
            weights[block * per_block + head] = weight
            outs.append(dot_nn(values[head * HD : (head + 1) * HD, :], weight))
        crossed[:, here] = jnp.concatenate(outs, axis=0).T.astype(low)

    def cross_forward_both(step, carry):
        cross_forward(2 * step)
        cross_forward(2 * step + 1)
        return carry

    lax.fori_loop(0, width // LANES // 2, cross_forward_both, 0)

    loads[2].wait()

    def project_crossed(here):
        work[:, here] += dot_nn(crossed[...], wco[:, here])

    by_columns(width, cols, project_crossed)

    def second_norm(here, carry):
        unit, scale = normed(work[here, :])
        unit_two[here, :] = unit
        scale_two[here, :] = scale
        value = unit * gain_ref[1:2, :] + shift_ref[1:2, :]
        work[here, :] = value
        low_two[here, :] = value.astype(low)
        return carry

    by_rows(second_norm)

    total[...] = jnp.zeros_like(total)

    win_load(0).wait()
    pre_now[...] = dot_nn(low_two[...], win[0])

    def feed_forward(which, carry):
        slot = lax.rem(which, 2)
        ahead = lax.rem(which + 1, tiles)

        @pl.when(which + 1 < tiles)
        def _():
            win_load(which + 1).wait()

        wout_load(which).wait()
        pre = pre_now[...]
        pre_now[...] = dot_nn(low_two[...], win[lax.rem(ahead, 2)])
        act, slope = gelu_pair(pre)
        slopes[:, rows_of(which, tile)] = slope.astype(low)
        total[...] += dot_nn(act.astype(low), wout[slot])

        @pl.when(which + 2 < tiles)
        def _():
            win_load(which + 2).start()
            wout_load(which + 2).start()

        return carry

    lax.fori_loop(0, tiles, feed_forward, 0)
    loads[3].wait()
    loads[4].wait()
    act, slope = gelu_pair(dot_nn(low_two[...], wd[...]) + dbias_ref[...])
    down_act[...] = act.astype(low)
    down_slope[...] = slope.astype(low)

    def project_raise(here):
        work[:, here] += total[:, here] + 4.0 * (
            dot_nn(down_act[...], wr[:, here]) + rbias_ref[:, here]
        )

    by_columns(width, cols, project_raise)
    nothing = jnp.zeros((1, width), f32)

    def third_norm(here, carry):
        gain_sum, shift_sum, bias_sum = carry
        unit, scale = normed(work[here, :])
        gain = gain_ref[2:3, :]
        out_ref[here, :] = (unit * gain + shift_ref[2:3, :]).astype(low)
        grad = cot_ref[here, :].astype(f32)
        back = norm_back(grad * gain, scale, unit)
        total[here, :] = back
        back_low = back.astype(low)
        low_three[here, :] = back_low
        return (
            gain_sum + jnp.sum(grad * unit, axis=0, keepdims=True),
            shift_sum + jnp.sum(grad, axis=0, keepdims=True),
            bias_sum + jnp.sum(back_low.astype(f32), axis=0, keepdims=True),
        )

    gain_three, shift_three, bias_sum = by_rows(third_norm, (nothing, nothing, nothing))
    vecs_ref[0:1, :] = 4.0 * bias_sum

    back = 4.0 * dot_nt(low_three[...], wr[...]) * down_slope[...].astype(f32)
    back_low = back.astype(low)
    down_grad[...] = back_low
    vecs_ref[1:2, :] = jnp.concatenate(
        [
            jnp.sum(back_low.astype(f32), axis=0, keepdims=True),
            jnp.zeros((1, width - wd.shape[1]), f32),
        ],
        axis=1,
    )
    down = wd.shape[1]
    raise_sum = 4.0 * dot_tn(down_act[...], low_three[...])
    for index in range(width // LANES):
        sums_ref[pl.ds(down * width // LANES + index * down, down), :] = raise_sum[
            :, index * LANES : (index + 1) * LANES
        ].astype(low)
    down_sum = dot_tn(low_two[...], down_grad[...])
    for index in range(down // LANES):
        sums_ref[index * width : (index + 1) * width, :] = down_sum[
            :, index * LANES : (index + 1) * LANES
        ].astype(low)

    def feed_backward(step, carry):
        which = tiles - 1 - step
        slot = lax.rem(which, 2)
        here = rows_of(which, tile)

        @pl.when(which < tiles - 2)
        def _():
            wout_load(which).wait()
            win_load(which).wait()

        grad = dot_nt(low_three[...], wout[slot]) * slopes[:, here].astype(f32)
        total[...] += dot_nt(grad.astype(low), win[slot])

        @pl.when(which >= 2)
        def _():
            win_load(which - 2).start()
            wout_load(which - 2).start()

        return carry

    lax.fori_loop(0, tiles, feed_backward, 0)

    def down_back(here):
        total[:, here] += dot_nt(down_grad[...], wd[here, :])

    by_columns(width, cols, down_back)

    def second_back(here, carry):
        gain_sum, shift_sum = carry
        grad = total[here, :]
        unit = unit_two[here, :]
        back = norm_back(grad * gain_ref[1:2, :], scale_two[here, :], unit)
        total[here, :] = back
        low_one[here, :] = back.astype(low)
        return (
            gain_sum + jnp.sum(grad * unit, axis=0, keepdims=True),
            shift_sum + jnp.sum(grad, axis=0, keepdims=True),
        )

    gain_two, shift_two = by_rows(second_back, (nothing, nothing))

    def crossed_back(here):
        crossed[:, here] = dot_nt(low_one[...], wco[here, :]).astype(low)

    by_columns(width, cols, crossed_back)

    def cross_backward(block):
        here = rows_of(block, LANES)
        values = mvalue_ref[:, here]
        keys = mkey_ref[:, here].astype(f32).T.astype(low)
        grads = crossed[:, here].astype(f32)
        outs = []
        key_sum = None
        for head in range(per_block):
            grad = jnp.where(head_lanes(grads.shape, head), grads, 0.0).astype(low)
            weight_low = weights[block * per_block + head]
            weight = weight_low.astype(f32)
            slope = dot_nt(values, grad)
            slope = weight * (slope - jnp.sum(weight * slope, axis=0, keepdims=True))
            slope = slope.astype(low)
            key_part = dot_nn(slope, head_queries(here, head))
            value_part = dot_nn(weight_low, grad)
            if key_sum is None:
                key_sum, value_sum = key_part, value_part
            else:
                key_sum, value_sum = key_sum + key_part, value_sum + value_part
            outs.append(dot_nn(keys[head * HD : (head + 1) * HD, :], slope))
        mkey_out[:, here] = key_sum.astype(low)
        mvalue_out[:, here] = value_sum.astype(low)
        query[:, here] = (jnp.concatenate(outs, axis=0) * 0.125).T.astype(low)

    def cross_backward_both(step, carry):
        cross_backward(2 * step)
        cross_backward(2 * step + 1)
        return carry

    lax.fori_loop(0, width // LANES // 2, cross_backward_both, 0)

    def query_back(here):
        total[:, here] += dot_nt(query[...], wcq[here, :])

    by_columns(width, cols, query_back)

    def first_back(here, carry):
        gain_sum, shift_sum = carry
        grad = total[here, :]
        unit = unit_one[here, :]
        back = norm_back(grad * gain_ref[0:1, :], scale_one[here, :], unit)
        fgrad_ref[here, :] = back
        low_one[here, :] = back.astype(low)
        return (
            gain_sum + jnp.sum(grad * unit, axis=0, keepdims=True),
            shift_sum + jnp.sum(grad, axis=0, keepdims=True),
        )

    gain_one, shift_one = by_rows(first_back, (nothing, nothing))

    def out_back(here):
        ograd_ref[here, :] = dot_nt(low_one[...], wo[here, :]).T.astype(low)

    by_columns(width, cols, out_back)
    for index, vector in enumerate(
        (gain_one, gain_two, gain_three, shift_one, shift_two, shift_three)
    ):
        vecs_ref[2 + index : 3 + index, :] = vector


def middle(
    tokens, attended, cotangent, mem_key, mem_value, gains, shifts, down_bias, raise_bias, weights
):
    length, width = tokens.shape
    mem_len = mem_key.shape[0]
    down = weights[3].shape[1]
    feed = weights[5].shape[1]
    tile = 512 if mem_len <= 512 else 128
    low = jnp.bfloat16
    f32 = jnp.float32
    vmem = pl.BlockSpec(memory_space=pltpu.VMEM)
    anywhere = pl.BlockSpec(memory_space=pl.ANY)
    square = pltpu.VMEM((width, width), low)
    wide = pltpu.VMEM((length, width), f32)
    narrow = pltpu.VMEM((length, width), low)
    return pl.pallas_call(
        middle_kernel,
        out_shape=(
            jax.ShapeDtypeStruct((length, width), low),
            jax.ShapeDtypeStruct((length, width), f32),
            jax.ShapeDtypeStruct((width, length), low),
            jax.ShapeDtypeStruct((mem_len, width), low),
            jax.ShapeDtypeStruct((mem_len, width), low),
            jax.ShapeDtypeStruct((2 * down * width // LANES, LANES), low),
            jax.ShapeDtypeStruct((8, width), f32),
        ),
        in_specs=[vmem] * 9 + [anywhere] * 7,
        out_specs=(vmem,) * 7,
        scratch_shapes=[
            square,
            square,
            square,
            pltpu.VMEM((width, down), low),
            pltpu.VMEM((down, width), low),
            pltpu.VMEM((2, width, tile), low),
            pltpu.VMEM((2, tile, width), low),
            wide,
            wide,
            wide,
            wide,
            pltpu.VMEM((length, 1), f32),
            pltpu.VMEM((length, 1), f32),
            narrow,
            narrow,
            narrow,
            narrow,
            narrow,
            pltpu.VMEM((H, mem_len, length), low),
            pltpu.VMEM((length, feed), low),
            pltpu.VMEM((length, tile), f32),
            pltpu.VMEM((length, down), low),
            pltpu.VMEM((length, down), low),
            pltpu.VMEM((length, down), low),
            pltpu.SemaphoreType.DMA((5,)),
            pltpu.SemaphoreType.DMA((2,)),
            pltpu.SemaphoreType.DMA((2,)),
        ],
        compiler_params=pltpu.CompilerParams(vmem_limit_bytes=VMEM_BYTES + (0 if mem_len <= 512 else 3 * 1024 * 1024)),
        name="middle",
    )(tokens, attended, cotangent, mem_key, mem_value, gains, shifts, down_bias, raise_bias, *weights)


def per_device(
    tokens,
    memory,
    segment_ids,
    padding_mask,
    cotangent,
    prefix_embed,
    prefix_first,
    first_bias,
    prefix_second,
    second_bias,
    adapter_down,
    down_bias,
    adapter_raise,
    raise_bias,
    norm_gain,
    norm_shift,
    self_query,
    self_key,
    self_value,
    self_output,
    cross_query,
    cross_key,
    cross_value,
    cross_output,
    feed_in,
    feed_out,
):
    row_count, length, model_width = tokens.shape
    flat_rows = row_count * length
    n = lax.axis_size("seq")
    batches = lax.axis_size("batch")
    down = adapter_down.shape[1]
    attended, mem_key, mem_value, *saved = self_forward(
        n,
        segment_ids,
        padding_mask,
        tokens.reshape(flat_rows, model_width),
        (self_query, self_key, self_value),
        (
            prefix_embed,
            prefix_first,
            first_bias.reshape(1, -1),
            prefix_second,
            second_bias.reshape(1, -1),
        ),
        memory.reshape(-1, model_width),
        (cross_key, cross_value),
    )
    layer_output, first_grad, out_grad, *mem_grads, weight_sums, vector_sums = middle(
        tokens.reshape(flat_rows, model_width),
        attended,
        cotangent.reshape(flat_rows, model_width),
        mem_key,
        mem_value,
        norm_gain,
        norm_shift,
        down_bias.reshape(1, -1),
        raise_bias.reshape(1, -1),
        (
            self_output,
            cross_query,
            cross_output,
            adapter_down,
            adapter_raise,
            feed_in,
            feed_out,
        ),
    )
    layer_output = layer_output.reshape(row_count, length, model_width)
    token_grad, memory_grad, prefix_grad, vector_sums, full_sums = self_backward(
        n,
        batches,
        first_grad,
        out_grad.reshape(n, -1, HD, length),
        weight_sums,
        mem_grads,
        (cross_key, cross_value),
        vector_sums,
        saved,
        (self_query, self_key, self_value),
    )
    token_grad = token_grad.reshape(row_count, length, model_width)
    memory_grad = memory_grad.reshape(memory.shape)
    replicated = finish(
        full_sums.reshape(-1, LANES),
        vector_sums,
        prefix_grad,
        prefix_embed,
        prefix_first,
        first_bias.reshape(1, -1),
        prefix_second,
        down,
    )
    replicated = [
        value.reshape(-1) if value.shape[0] == 1 else value for value in replicated
    ]
    return (layer_output, token_grad, memory_grad, *replicated)


def solution(mesh):
    placed = (
        P("batch", "seq", None),
        P("batch", "seq", None),
        P("batch", "seq"),
        P("batch", "seq"),
        P("batch", "seq", None),
        P(),
        P(),
        P(),
        P(),
        P(),
        P(),
        P(),
        P(),
        P(),
        P(),
        P(),
        P(),
        P(),
        P(),
        P(),
        P(),
        P(),
        P(),
        P(),
        P(),
        P(),
    )
    return jax.shard_map(
        per_device,
        mesh=mesh,
        in_specs=placed,
        out_specs=(
            P("batch", "seq", None),
            P("batch", "seq", None),
            P("batch", "seq", None),
            P(),
            P(),
            P(),
            P(),
            P(),
            P(),
            P(),
            P(),
            P(),
            P(),
            P(),
        ),
        check_vma=False,
    )
```

```python
import functools

import jax
import jax.numpy as jnp
from jax import lax
from jax.experimental import pallas as pl
from jax.experimental.pallas import tpu as pltpu
from jax.sharding import PartitionSpec as P

H = 16
HD = 64
LANES = 128
PREFIX_ROWS = 32
VMEM_BYTES = 60 * 1024 * 1024
SUM_ROWS = 16
MESH = pl.DeviceIdType.MESH

masked_score = -1e30
norm_eps = 1e-05

def dot_nn(left, right):
    return lax.dot_general(
        left, right, (((1,), (0,)), ((), ())), preferred_element_type=jnp.float32
    )


def dot_nt(left, right):
    return lax.dot_general(
        left, right, (((1,), (1,)), ((), ())), preferred_element_type=jnp.float32
    )


def dot_tn(left, right):
    return lax.dot_general(
        left, right, (((0,), (0,)), ((), ())), preferred_element_type=jnp.float32
    )


def remote(source, target, send_sem, recv_sem, axis, peer):
    return pltpu.make_async_remote_copy(
        src_ref=source,
        dst_ref=target,
        send_sem=send_sem,
        recv_sem=recv_sem,
        device_id={axis: peer},
        device_id_type=MESH,
    )


def enter(sizes):
    barrier = pltpu.get_barrier_semaphore()
    for axis, size in sizes.items():
        for other in range(size):

            @pl.when(other != lax.axis_index(axis))
            def _():
                pl.semaphore_signal(barrier, inc=1, device_id={axis: other}, device_id_type=MESH)

    pl.semaphore_wait(barrier, sum(sizes.values()) - len(sizes))


def others(size, mine, body):
    for other in range(size):

        @pl.when(other != mine)
        def _():
            body(other)


def rows_of(index, size):
    return pl.ds(pl.multiple_of(index * size, size), size)


def span_of(start, size):
    return pl.ds(pl.multiple_of(start, LANES), size)


def own_columns(ref, first, me, width):
    if width % LANES == 0:
        return ref[:, pl.ds(pl.multiple_of(first + me * width, LANES), width)].astype(jnp.float32)
    share = LANES // width
    block = ref[:, pl.ds(pl.multiple_of(first + me // share * LANES, LANES), LANES)].astype(
        jnp.float32
    )
    picked = block[:, :width]
    for part in range(1, share):
        picked = jnp.where(me % share == part, block[:, part * width : (part + 1) * width], picked)
    return picked


def head_lanes(shape, head):
    lane = lax.broadcasted_iota(jnp.int32, shape, 1)
    return (lane >= head * HD) & (lane < (head + 1) * HD)


def self_forward_kernel(
    n,
    seg_ref,
    pad_ref,
    tok_ref,
    wq_in,
    wk_in,
    wv_in,
    emb_ref,
    first_in,
    fbias_ref,
    second_in,
    sbias_ref,
    mem_ref,
    wck_in,
    wcv_in,
    att_ref,
    mkey_ref,
    mvalue_ref,
    qx_out,
    kx_out,
    raw_out,
    pk_out,
    pv_out,
    pkt_out,
    ot_out,
    lse_out,
    send,
    recv,
    meta_send,
    meta,
    kx,
    qx,
    vt,
    hidden,
    pk,
    pv,
    pkt,
    pvt,
    stat,
    acc,
    o_send,
    o_recv,
    mem_all,
    wck,
    wcv,
    wq_ref,
    wk_ref,
    wv_ref,
    first_ref,
    second_ref,
    send_sem,
    recv_sem,
    meta_send_sem,
    meta_recv_sem,
    o_send_sem,
    o_recv_sem,
    mem_send_sem,
    mem_recv_sem,
    out_sem,
    weight_sem,
    in_sem,
):
    low = jnp.bfloat16
    f32 = jnp.float32
    me = lax.axis_index("seq")
    length, width = tok_ref.shape
    group = width // n
    heads = group // HD
    plane = 2 * length
    planes = n // 2
    block = 2 * LANES
    per_block = block // group
    blocks = width // block
    step_rows = 256
    steps = plane // step_rows
    my_plane = me // 2
    my_side = lax.rem(me, 2)

    def meta_copy(peer, slot):
        return remote(
            meta_send, meta.at[slot], meta_send_sem.at[peer], meta_recv_sem.at[slot], "seq", peer
        )

    def qkv_copy(head, peer, slot):
        return remote(
            send.at[peer, head],
            recv.at[head, slot],
            send_sem.at[head, peer],
            recv_sem.at[head, slot],
            "seq",
            peer,
        )

    def out_copy(head, peer, slot):
        return remote(
            o_send.at[head, peer],
            o_recv.at[slot, head],
            o_send_sem.at[head, peer],
            o_recv_sem.at[head, slot],
            "seq",
            peer,
        )

    def mem_along(which, toward):
        part = mem_all.at[which, my_side]
        return remote(
            part,
            part,
            mem_send_sem.at[(toward + 1) // 2, which],
            mem_recv_sem.at[which],
            "seq",
            me + 2 * toward,
        )

    def mem_across(side):
        part = mem_all.at[:, side]
        return remote(
            part,
            part,
            mem_send_sem.at[0, planes],
            mem_recv_sem.at[planes],
            "seq",
            me + 1 - 2 * my_side,
        )

    def mem_hops(hop, body):
        for toward in (1, -1):
            which = my_plane - toward * hop
            ahead = my_plane + toward

            @pl.when((which >= 0) & (which < planes) & (ahead >= 0) & (ahead < planes))
            def _():
                body(mem_along(which, toward))

    def mem_arrivals(hop):
        for toward in (1, -1):
            which = my_plane - toward * hop

            @pl.when((which >= 0) & (which < planes))
            def _():
                mem_along(which, -toward).wait_recv()

    def block_at(step):
        if blocks >= planes:
            share = blocks // planes
            return lax.rem(my_plane + 1 + step // share, planes) * share + step % share
        return lax.rem(me // per_block + 1 + step, blocks)

    def weight_load(step, which):
        columns = rows_of(block_at(step), block)
        source = (wq_in, wk_in, wv_in)[which]
        target = (wq_ref, wk_ref, wv_ref)[which]
        return pltpu.make_async_copy(
            source.at[:, columns], target.at[:, columns], weight_sem.at[step, which]
        )

    for step in range(blocks):
        for which in range(3):
            weight_load(step, which).start()
    loads = [
        pltpu.make_async_copy(source, target, in_sem.at[index])
        for index, (source, target) in enumerate(
            ((first_in, first_ref), (second_in, second_ref), (wck_in, wck), (wcv_in, wcv))
        )
    ]
    for load in loads:
        load.start()
    segments = seg_ref[...]
    tags = jnp.where(pad_ref[...] == 1, segments, -1)
    row = lax.broadcasted_iota(jnp.int32, meta_send.shape, 0)
    meta_send[...] = jnp.where(row == 0, segments, tags)
    mem_all[my_plane, my_side] = mem_ref[...]
    enter({"seq": n})
    others(n, me, lambda peer: meta_copy(peer, me).start())
    meta[me] = meta_send[...]

    for step in range(blocks):
        at = block_at(step)
        columns = rows_of(at, block)
        for which, weight in enumerate((wq_ref, wk_ref, wv_ref)):
            weight_load(step, which).wait()
            piece = dot_nn(tok_ref[...], weight[:, columns]).T.astype(low)
            for part in range(per_block):
                for head in range(heads):
                    first = part * group + head * HD
                    send[at * per_block + part, head, which] = piece[first : first + HD]
        for part in range(per_block):
            peer = at * per_block + part

            @pl.when(peer != me)
            def _():
                qkv_copy(0, peer, me).start()

            @pl.when(peer == me)
            def _():
                for head in range(heads):
                    recv[head, me] = send[peer, head]

    mem_hops(0, lambda copy: copy.start())

    loads[0].wait()
    loads[1].wait()
    hidden[...] = jnp.zeros_like(hidden)
    hidden[: emb_ref.shape[0], :] = jnp.tanh(dot_nn(emb_ref[...], first_ref[...]) + fbias_ref[...])
    hidden_low = hidden[...].astype(low)
    prefix_key = dot_nn(hidden_low, own_columns(second_ref, 0, me, group).astype(low)) + own_columns(
        sbias_ref, 0, me, group
    )
    prefix_value = dot_nn(
        hidden_low, own_columns(second_ref, width, me, group).astype(low)
    ) + own_columns(sbias_ref, width, me, group)
    prefix_row = lax.broadcasted_iota(jnp.int32, (PREFIX_ROWS, HD), 0)
    prefix_open = jnp.where(prefix_row < emb_ref.shape[0], 0.0, masked_score)
    for head in range(heads):
        here = slice(head * HD, (head + 1) * HD)
        pk[head] = jnp.concatenate([prefix_key[:, here], prefix_open], axis=1).astype(low)
        pv[head] = prefix_value[:, here].astype(low)
    pkt[...] = prefix_key.T.astype(low).reshape(heads, HD, PREFIX_ROWS)
    pvt[:, :HD, :] = prefix_value.T.astype(low).reshape(heads, HD, PREFIX_ROWS)
    pvt[:, HD:, :] = jnp.ones((heads, SUM_ROWS, PREFIX_ROWS), low)
    vt[:, HD:, :] = jnp.ones((heads, SUM_ROWS, n * length), low)

    def arrive(head, chunk):
        @pl.when(chunk != me)
        def _():
            @pl.when(head == 0)
            def _():
                meta_copy(chunk, chunk).wait_recv()

            qkv_copy(head, chunk, chunk).wait_recv()

        here = rows_of(chunk, length)
        state = lax.broadcasted_iota(jnp.int32, (HD, length), 0)
        qx[head, :HD, here] = (recv[head, chunk, 0].astype(f32) * 0.125).astype(low)
        qx[head, HD:, here] = jnp.where(state == meta[chunk, 0:1, :], 1.0, 0.0).astype(low)
        is_open = jnp.where(state == meta[chunk, 1:2, :], 0.0, masked_score)
        kx[head, here, :] = jnp.concatenate(
            [recv[head, chunk, 1].astype(f32), is_open], axis=0
        ).T.astype(low)
        vt[head, :HD, here] = recv[head, chunk, 2]

    def open_plane(head, which):
        scores = dot_nn(pk[head], qx[head, :, rows_of(which, plane)])
        top = jnp.max(scores, axis=0, keepdims=True)
        raised = jnp.exp(scores - top)
        stat[which, head, 0:1, :] = top
        acc[which, head] = dot_nn(pvt[head], raised.astype(low))

    def pair_part(head, upper, lower, first, keys, diagonal):
        here = slice(first, first + step_rows)
        queries = qx[head, :, span_of(upper * plane + first, step_rows)]
        key_rows = span_of(lower * plane, keys)
        scores = dot_nn(kx[head, key_rows, :], queries)
        if diagonal:
            key_at = lax.broadcasted_iota(jnp.int32, scores.shape, 0)
            query_at = lax.broadcasted_iota(jnp.int32, scores.shape, 1) + first
            scores = jnp.where(key_at <= query_at, scores, masked_score)
        old_top = stat[upper, head, 0:1, here]
        top = jnp.maximum(old_top, jnp.max(scores, axis=0, keepdims=True))
        raised = jnp.exp(scores - top).astype(low)
        stat[upper, head, 0:1, here] = top
        acc[upper, head, :, here] = acc[upper, head, :, here] * jnp.exp(old_top - top) + dot_nn(
            vt[head, :, key_rows], raised
        )

    def pair(head, upper, lower):
        for part in range(steps):
            pair_part(head, upper, lower, part * step_rows, plane, False)

    def pair_diagonal(head, which):
        for part in range(steps):
            pair_part(head, which, which, part * step_rows, (part + 1) * step_rows, True)

    def close_plane(head, which):
        total = acc[which, head, HD : HD + 1, :]
        value = acc[which, head, :HD, :] / total
        acc[which, head, :HD, :] = value
        stat[which, head, 0:1, :] = stat[which, head, 0:1, :] + jnp.log(total)
        for part in range(2):
            chunk = 2 * which + part
            o_send[head, chunk] = value[:, part * length : (part + 1) * length].astype(low)

            @pl.when(chunk != me)
            def _():
                out_copy(head, chunk, me).start()

            @pl.when(chunk == me)
            def _():
                o_recv[me, head] = o_send[head, chunk]

    def project_memory():
        mem_across(1 - my_side).wait_recv()
        for load in loads[2:]:
            load.wait()
        whole = mem_all[...].reshape(mkey_ref.shape)

        def one(index, carry):
            here = rows_of(index, block)
            mkey_ref[:, here] = dot_nn(whole, wck[:, here]).astype(low)
            mvalue_ref[:, here] = dot_nn(whole, wcv[:, here]).astype(low)
            return carry

        lax.fori_loop(0, blocks, one, 0)

    def stage(index, carry):
        head = index // planes
        step = lax.rem(index, planes)

        @pl.when(head + 1 < heads)
        def _():
            there = lax.rem(my_plane + 1 + step, planes)
            for part in range(2):
                peer = 2 * there + part

                @pl.when(peer != me)
                def _():
                    qkv_copy(head, peer, me).wait_send()
                    qkv_copy(head + 1, peer, me).start()

        here = lax.rem(my_plane + step, planes)
        arrive(head, 2 * here)
        arrive(head, 2 * here + 1)
        open_plane(head, here)
        pair_diagonal(head, here)

        def earlier(back, inner):
            there = lax.rem(my_plane + back, planes)
            pair(head, jnp.maximum(here, there), jnp.minimum(here, there))

            @pl.when((step == planes - 1) & (there > here))
            def _():
                close_plane(head, there)

            return inner

        lax.fori_loop(0, step, earlier, 0)
        for hop in range(1, planes - 1):

            @pl.when(index == hop)
            def _():
                mem_arrivals(hop)
                mem_hops(hop, lambda copy: copy.start())

        @pl.when(index == planes - 1)
        def _():
            mem_arrivals(planes - 1)
            mem_across(my_side).start()

        @pl.when((my_plane + step >= planes) | (my_plane == 0))
        def _():
            close_plane(head, here)

        return carry

    lax.fori_loop(0, heads * planes, stage, 0)

    saves = []

    def save(source, target):
        copy = pltpu.make_async_copy(source, target, out_sem.at[len(saves)])
        copy.start()
        saves.append(copy)

    save(qx, qx_out)
    save(kx, kx_out)
    save(recv, raw_out)
    save(pk, pk_out)
    save(pv, pv_out)
    save(pkt, pkt_out)
    save(acc, ot_out)
    save(stat, lse_out)
    project_memory()
    for other in range(n):

        @pl.when(other != me)
        def _():
            for head in range(heads):
                out_copy(head, other, other).wait_recv()

        att_ref[:, other * group : (other + 1) * group] = (
            o_recv[other].reshape(group, length).astype(f32).T.astype(low)
        )

    def drain(peer):
        meta_copy(peer, me).wait_send()
        qkv_copy(heads - 1, peer, me).wait_send()
        for head in range(heads):
            out_copy(head, peer, me).wait_send()

    others(n, me, drain)
    for hop in range(planes - 1):
        mem_hops(hop, lambda copy: copy.wait_send())
    mem_across(my_side).wait_send()
    for copy in saves:
        copy.wait()


def self_forward(n, segments, padding, tokens, weights, prefix, memory, mem_weights):
    length, width = tokens.shape
    group = width // n
    heads = group // HD
    whole = n * length
    planes = n // 2
    low = jnp.bfloat16
    f32 = jnp.float32
    vmem = pl.BlockSpec(memory_space=pltpu.VMEM)
    anywhere = pl.BlockSpec(memory_space=pl.ANY)
    dma = pltpu.SemaphoreType.DMA
    shapes = (
        ((heads, 2 * HD, whole), low),
        ((heads, whole, 2 * HD), low),
        ((heads, n, 3, HD, length), low),
        ((heads, PREFIX_ROWS, 2 * HD), low),
        ((heads, PREFIX_ROWS, HD), low),
        ((heads, HD, PREFIX_ROWS), low),
        ((planes, heads, HD + SUM_ROWS, 2 * length), f32),
        ((planes, heads, 8, 2 * length), f32),
    )
    square = pltpu.VMEM((width, width), low)
    qx, kx, raw, pk, pv, pkt, acc, stat = (pltpu.VMEM(*shape) for shape in shapes)
    return pl.pallas_call(
        functools.partial(self_forward_kernel, n),
        out_shape=(
            jax.ShapeDtypeStruct((length, width), low),
            jax.ShapeDtypeStruct((n * memory.shape[0], width), low),
            jax.ShapeDtypeStruct((n * memory.shape[0], width), low),
        )
        + tuple(jax.ShapeDtypeStruct(*shape) for shape in shapes),
        in_specs=[vmem] * 3
        + [anywhere] * 3
        + [vmem, anywhere, vmem, anywhere, vmem, vmem]
        + [anywhere] * 2,
        out_specs=(vmem,) * 3 + (anywhere,) * 8,
        scratch_shapes=[
            pltpu.VMEM((n, heads, 3, HD, length), low),
            raw,
            pltpu.VMEM((8, length), jnp.int32),
            pltpu.VMEM((n, 8, length), jnp.int32),
            kx,
            qx,
            pltpu.VMEM((heads, HD + SUM_ROWS, whole), low),
            pltpu.VMEM((PREFIX_ROWS, weights[0].shape[0] // 2), f32),
            pk,
            pv,
            pkt,
            pltpu.VMEM((heads, HD + SUM_ROWS, PREFIX_ROWS), low),
            stat,
            acc,
            pltpu.VMEM((heads, n, HD, length), low),
            pltpu.VMEM((n, heads, HD, length), low),
            pltpu.VMEM((planes, 2) + memory.shape, low),
            square,
            square,
            square,
            square,
            square,
            pltpu.VMEM(prefix[1].shape, low),
            pltpu.VMEM(prefix[3].shape, low),
            dma((heads, n)),
            dma((heads, n)),
            dma((n,)),
            dma((n,)),
            dma((heads, n)),
            dma((heads, n)),
            dma((2, planes + 1)),
            dma((planes + 1,)),
            dma((8,)),
            dma((width // (2 * LANES), 3)),
            dma((4,)),
        ],
        compiler_params=pltpu.CompilerParams(
            collective_id=0, has_side_effects=True, vmem_limit_bytes=VMEM_BYTES
        ),
        name="self_forward",
    )(segments, padding, tokens, *weights, *prefix, memory, *mem_weights)


def self_backward_kernel(
    n,
    batches,
    base_in,
    do_in,
    sums_in,
    mkey_in,
    mvalue_in,
    wck_in,
    wcv_in,
    vecs_in,
    qx_in,
    kx_in,
    raw_in,
    pk_in,
    pv_in,
    pkt_in,
    ot_in,
    lse_in,
    wq_in,
    wk_in,
    wv_in,
    tg_ref,
    mgrad_ref,
    pkv_ref,
    vecs_ref,
    full_out,
    do_recv,
    qx,
    kx,
    raw,
    kt,
    values,
    dot,
    qdo,
    pk,
    pv,
    pkt,
    ot,
    stat,
    weights,
    dqt,
    dkv,
    g_send,
    g_recv,
    pre_ref,
    pre_all,
    pre_sum,
    pre_recv,
    sums_mine,
    sums_core,
    sums_x,
    sums_side,
    sums_z,
    full,
    mkey,
    mvalue,
    wck,
    wcv,
    mem_part,
    mem_side,
    mem_up,
    mem_down,
    vec_all,
    vec_sum,
    vec_y,
    vec_both,
    vec_z,
    base_ref,
    do_send_sem,
    do_recv_sem,
    g_send_sem,
    g_recv_sem,
    in_sem,
    send_sem,
    recv_sem,
):
    low = jnp.bfloat16
    f32 = jnp.float32
    me = lax.axis_index("seq")
    length, width = tg_ref.shape
    group = width // n
    heads = group // HD
    plane = 2 * length
    planes = n // 2
    step_rows = 256
    my_batch = lax.axis_index("batch")
    my_core = lax.rem(my_batch, 2)
    my_high = my_batch // 2
    highs = batches // 2
    my_plane = me // 2
    my_side = lax.rem(me, 2)
    beside = me + 1 - 2 * my_side
    used = [0]

    def numbers(count):
        used[0] += count
        return used[0] - count

    core_slot = numbers(2)
    x_slot = numbers(2 * highs)
    y_slot = numbers(3)
    z_slot = numbers(2 * planes)
    up_slot = numbers(planes)
    down_slot = numbers(planes)
    va_slot = numbers(batches)
    vb_slot = numbers(1)
    vc_slot = numbers(planes)
    pa_slot = numbers(batches)
    pb_slot = numbers(n)

    def send(source, target, first, peer_index, slot_index, axis, peer):
        return remote(
            source,
            target,
            send_sem.at[first + peer_index],
            recv_sem.at[first + slot_index],
            axis,
            peer,
        )

    half_rows = 2 * planes * highs * sums_z.shape[1]
    x_rows = half_rows // highs
    y_rows = x_rows // 2
    z_rows = y_rows // planes
    x_row = pl.multiple_of(my_high * x_rows, x_rows)
    y_row = pl.multiple_of(x_row + my_side * y_rows, y_rows)

    def part(row, count):
        return sums_mine.at[pl.ds(pl.multiple_of(row, count), count)]

    def reduce_core():
        return send(
            sums_in.at[1 - my_core], sums_core, core_slot, 0, 0, "batch", my_batch + 1 - 2 * my_core
        )

    def reduce_x(peer, slot):
        return send(
            part(peer * x_rows, x_rows),
            sums_x.at[slot],
            x_slot,
            peer,
            slot,
            "batch",
            2 * peer + my_core,
        )

    def reduce_y():
        return send(
            part(x_row + (1 - my_side) * y_rows, y_rows), sums_side, y_slot, 0, 0, "seq", beside
        )

    def reduce_z(peer, slot):
        return send(
            part(y_row + peer * z_rows, z_rows),
            sums_z.at[slot],
            z_slot,
            peer,
            slot,
            "seq",
            2 * peer + my_side,
        )

    def gather_z(peer, slot):
        piece = full.at[my_core, my_high, my_side, slot]
        return send(piece, piece, z_slot + planes, peer, slot, "seq", 2 * peer + my_side)

    def gather_y(side):
        piece = full.at[my_core, my_high, side]
        return send(piece, piece, y_slot + 1, 0, 0, "seq", beside)

    def gather_x(peer, slot):
        piece = full.at[my_core, slot]
        return send(piece, piece, x_slot + highs, peer, slot, "batch", 2 * peer + my_core)

    def gather_core(core):
        piece = full.at[core]
        return send(piece, piece, core_slot + 1, 0, 0, "batch", my_batch + 1 - 2 * my_core)

    def mem_across():
        return send(
            mem_part.at[:, 1 - my_side], mem_side, y_slot + 2, 0, 0, "seq", beside
        )

    def mem_hop(target, toward, peer=None):
        buffer, slot = (mem_up, up_slot) if toward > 0 else (mem_down, down_slot)
        return send(
            mem_part.at[target, my_side],
            buffer.at[target],
            slot,
            target,
            target,
            "seq",
            me + 2 * toward if peer is None else peer,
        )

    def mem_from(target, toward):
        return mem_hop(target, toward, me - 2 * toward)

    def mem_pass(toward):
        buffer = mem_up if toward > 0 else mem_down
        first = 0 if toward > 0 else planes - 1
        for target in range(planes):

            @pl.when((target - my_plane) * toward > 0)
            def _():
                @pl.when(my_plane != first)
                def _():
                    mem_from(target, toward).wait_recv()
                    mem_part[target, my_side] = (
                        mem_part[target, my_side].astype(f32) + buffer[target].astype(f32)
                    ).astype(low)

                mem_hop(target, toward).start()

    def mem_stage(at):
        pl.when(my_plane == at)(lambda: mem_pass(1))
        pl.when(my_plane == planes - 1 - at)(lambda: mem_pass(-1))

    def mem_end():
        value = mem_part[my_plane, my_side].astype(f32)
        mgrad_ref[...] = value.astype(low)

        @pl.when(my_plane > 0)
        def _():
            mem_from(my_plane, 1).wait_recv()
            mgrad_ref[...] = (mgrad_ref[...].astype(f32) + mem_up[my_plane].astype(f32)).astype(low)

        @pl.when(my_plane < planes - 1)
        def _():
            mem_from(my_plane, -1).wait_recv()
            mgrad_ref[...] = (
                mgrad_ref[...].astype(f32) + mem_down[my_plane].astype(f32)
            ).astype(low)

    def mem_drain():
        for target in range(planes):

            @pl.when(target > my_plane)
            def _():
                mem_hop(target, 1).wait_send()

            @pl.when(target < my_plane)
            def _():
                mem_hop(target, -1).wait_send()

    def vec_a(peer, slot):
        return send(vecs_in, vec_all.at[slot], va_slot, peer, slot, "batch", peer)

    def vec_b(side):
        return send(vec_sum, vec_y.at[side], vb_slot, 0, 0, "seq", beside)

    def vec_c(peer, slot):
        return send(vec_both, vec_z.at[slot], vc_slot, peer, slot, "seq", 2 * peer + my_side)

    def pre_a(peer, slot):
        return send(pre_ref, pre_all.at[slot], pa_slot, peer, slot, "batch", peer)

    def pre_b(peer, slot):
        return send(pre_sum, pre_recv.at[slot], pb_slot, peer, slot, "seq", peer)

    def do_copy(head, peer, slot):
        return remote(
            do_in.at[peer, head],
            do_recv.at[head, slot],
            do_send_sem.at[head, peer],
            do_recv_sem.at[head, slot],
            "seq",
            peer,
        )

    def q_copy(head, peer, slot):
        return remote(
            g_send.at[peer, head, 0],
            g_recv.at[0, slot, head],
            g_send_sem.at[0, head, peer],
            g_recv_sem.at[0, head, slot],
            "seq",
            peer,
        )

    def kv_copy(head, peer, slot):
        return remote(
            g_send.at[peer, head, pl.ds(1, 2)],
            g_recv.at[pl.ds(1, 2), slot, head],
            g_send_sem.at[1, head, peer],
            g_recv_sem.at[1, head, slot],
            "seq",
            peer,
        )

    def added(ref, size):
        value = ref[0].astype(f32)
        for other in range(1, size):
            value = value + ref[other].astype(f32)
        return value

    loads = [
        pltpu.make_async_copy(source, target, in_sem.at[index])
        for index, (source, target) in enumerate(
            (
                (raw_in, raw),
                (kx_in, kx),
                (pk_in, pk),
                (pv_in, pv),
                (pkt_in, pkt),
                (qx_in, qx),
                (ot_in, ot),
                (lse_in, stat),
                (sums_in.at[my_core], sums_mine),
                (vecs_in, vec_all.at[my_batch]),
                (mkey_in, mkey),
                (mvalue_in, mvalue),
                (wck_in, wck),
                (wcv_in, wcv),
                (base_in, base_ref),
                (wq_in, weights.at[0]),
                (wk_in, weights.at[1]),
                (wv_in, weights.at[2]),
            )
        )
    ]
    own_do = pltpu.make_async_copy(do_in.at[me], do_recv.at[:, me], in_sem.at[len(loads)])
    own_do.start()
    for load in loads:
        load.start()
    enter({"seq": n, "batch": batches})
    others(n, me, lambda peer: do_copy(0, peer, me).start())
    reduce_core().start()
    others(batches, my_batch, lambda peer: vec_a(peer, my_batch).start())
    dkv[...] = jnp.zeros_like(dkv)
    pre_ref[...] = jnp.zeros_like(pre_ref)
    for load in loads[:14]:
        load.wait()
    own_do.wait()

    def turn(index, carry):
        head = index // n
        chunk = lax.rem(index, n)
        here = rows_of(chunk, length)
        kt[head, :, here] = raw[head, chunk, 1]
        values[head, here, :] = raw[head, chunk, 2].astype(f32).T.astype(low)
        return carry

    lax.fori_loop(0, heads * n, turn, 0)

    def memory_back(index, carry):
        here = rows_of(index, step_rows)
        value = dot_nt(mkey[...], wck[here, :]) + dot_nt(mvalue[...], wcv[here, :])
        mem_part[:, :, :, here] = value.astype(low).reshape(mem_part.shape[:3] + (step_rows,))
        return carry

    lax.fori_loop(0, width // step_rows, memory_back, 0)
    mem_across().start()

    def next_head(head):
        @pl.when(head + 1 < heads)
        def _():
            def move(peer):
                do_copy(head, peer, me).wait_send()
                do_copy(head + 1, peer, me).start()

            others(n, me, move)

    def arrive(head, which):
        for part in range(2):
            chunk = 2 * which + part

            @pl.when(chunk != me)
            def _():
                do_copy(head, chunk, chunk).wait_recv()

            grads = do_recv[head, chunk]
            dot[head, :, rows_of(chunk, length)] = grads
            grads = grads.astype(f32)
            query = raw[head, chunk, 0].astype(f32) * 0.125
            qdo[head, rows_of(chunk, length), :] = (
                jnp.concatenate([query, grads], axis=0).T.astype(low)
            )
            here = slice(part * length, (part + 1) * length)
            stat[which, head, 1:2, here] = jnp.sum(
                grads * ot[which, head, :HD, here], axis=0, keepdims=True
            )
        here = rows_of(which, plane)
        weight = jnp.exp(dot_nn(pk[head], qx[head, :, here]) - stat[which, head, 0:1, :])
        slope = weight * (dot_nn(pv[head], dot[head, :, here]) - stat[which, head, 1:2, :])
        both = jnp.concatenate([slope, weight], axis=0).astype(low)
        sums = dot_nn(both, qdo[head, here, :])
        pre_ref[head] += jnp.where(
            head_lanes((PREFIX_ROWS, 2 * HD), 0), sums[:PREFIX_ROWS], sums[PREFIX_ROWS:]
        )
        slope = slope.astype(low)
        dqt[which, head] = dot_nn(pkt[head], slope)

    def plus(first, second):
        return (first.astype(f32) + second.astype(f32)).astype(low)

    def sum_one():
        reduce_core().wait_recv()
        sums_mine[...] = plus(sums_mine[...], sums_core[...])
        others(highs, my_high, lambda peer: reduce_x(peer, my_high).start())

    def sum_two():
        here = pl.ds(x_row, x_rows)
        others(highs, my_high, lambda peer: reduce_x(peer, peer).wait_recv())
        sums_x[my_high] = sums_mine[here]
        sums_mine[here] = added(sums_x, highs).astype(low)
        reduce_y().start()

    def sum_three():
        here = pl.ds(y_row, y_rows)
        reduce_y().wait_recv()
        sums_mine[here] = plus(sums_mine[here], sums_side[...])
        others(planes, my_plane, lambda peer: reduce_z(peer, my_plane).start())

    def sum_four():
        here = pl.ds(pl.multiple_of(y_row + my_plane * z_rows, z_rows), z_rows)
        others(planes, my_plane, lambda peer: reduce_z(peer, peer).wait_recv())
        sums_z[my_plane] = sums_mine[here]
        full[my_core, my_high, my_side, my_plane] = added(sums_z, planes).astype(low)
        others(planes, my_plane, lambda peer: gather_z(peer, my_plane).start())

    def sum_five():
        others(planes, my_plane, lambda peer: gather_z(peer, peer).wait_recv())
        gather_y(my_side).start()

    def sum_six():
        gather_y(1 - my_side).wait_recv()
        others(highs, my_high, lambda peer: gather_x(peer, my_high).start())

    def sum_seven():
        others(highs, my_high, lambda peer: gather_x(peer, peer).wait_recv())
        gather_core(my_core).start()

    def sum_end():
        gather_core(1 - my_core).wait_recv()
        save_full.start()

    def vec_one():
        others(batches, my_batch, lambda peer: vec_a(peer, peer).wait_recv())
        vec_sum[...] = added(vec_all, batches)
        vec_b(my_side).start()
        vec_y[my_side] = vec_sum[...]

    def vec_two():
        vec_b(1 - my_side).wait_recv()
        vec_both[...] = vec_y[0] + vec_y[1]
        others(planes, my_plane, lambda peer: vec_c(peer, my_plane).start())
        vec_z[my_plane] = vec_both[...]

    def vec_end():
        others(planes, my_plane, lambda peer: vec_c(peer, peer).wait_recv())
        vecs_ref[...] = added(vec_z, planes)

    def mem_one():
        mem_across().wait_recv()
        mem_part[:, my_side] = plus(mem_part[:, my_side], mem_side[...])

    def stage_pa():
        others(batches, my_batch, lambda peer: pre_a(peer, my_batch).start())
        pre_all[my_batch] = pre_ref[...]

    def stage_pb():
        others(batches, my_batch, lambda peer: pre_a(peer, peer).wait_recv())
        pre_sum[...] = added(pre_all, batches).astype(low)
        others(n, me, lambda peer: pre_b(peer, me).start())
        pre_recv[me] = pre_sum[...]

    save_full = pltpu.make_async_copy(full, full_out, in_sem.at[0])

    def pair_part(head, upper, lower, first, count, diagonal):
        keys = span_of(lower * plane + first, count)
        here = span_of(upper * plane + first, plane - first)
        at = slice(first, plane)
        scores = dot_nn(kx[head, keys, :], qx[head, :, here])
        slope = dot_nn(values[head, keys, :], dot[head, :, here]) - stat[upper, head, 1:2, at]
        weight = jnp.exp(scores - stat[upper, head, 0:1, at])
        if diagonal:
            key_at = lax.broadcasted_iota(jnp.int32, scores.shape, 0)
            query_at = lax.broadcasted_iota(jnp.int32, scores.shape, 1)
            weight = jnp.where(key_at <= query_at, weight, 0.0)
        both = jnp.concatenate([(weight * slope).astype(low), weight.astype(low)], axis=0)
        sums = dot_nn(both, qdo[head, here, :])
        dkv[head, keys, :] += jnp.where(
            head_lanes((count, 2 * HD), 0), sums[:count], sums[count:]
        )
        dqt[upper, head, :, at] += dot_nn(kt[head, :, keys], both[:count])

    def pair(head, upper, lower, diagonal):
        if diagonal:
            pair_part(head, upper, lower, 0, length, True)
            pair_part(head, upper, lower, length, length, True)
        else:
            pair_part(head, upper, lower, 0, plane, False)

    def hand_queries(head, which):
        for part in range(2):
            chunk = 2 * which + part
            g_send[chunk, head, 0] = (
                dqt[which, head, :, part * length : (part + 1) * length] * 0.125
            ).astype(low)

            @pl.when(chunk != me)
            def _():
                q_copy(head, chunk, me).start()

            @pl.when(chunk == me)
            def _():
                g_recv[0, me, head] = g_send[chunk, head, 0]

    def hand_keys(head, which):
        for part in range(2):
            chunk = 2 * which + part
            turned = dkv[head, rows_of(chunk, length), :].T.astype(low)
            g_send[chunk, head, 1] = turned[:HD]
            g_send[chunk, head, 2] = turned[HD:]

            @pl.when(chunk != me)
            def _():
                kv_copy(head, chunk, me).start()

            @pl.when(chunk == me)
            def _():
                g_recv[pl.ds(1, 2), me, head] = g_send[chunk, head, pl.ds(1, 2)]

    rising = my_plane >= planes // 2
    total = heads * planes * (planes + 1) // 2
    hooks = [
        (2, sum_one),
        (3, mem_one),
        (4, lambda: mem_stage(0)),
        (5, sum_two),
        (5, vec_one),
        (7, sum_three),
        (8, vec_two),
        (9, sum_four),
        (10, sum_five),
        (12, sum_six),
        (15, sum_seven),
        (16, vec_end),
    ] + [(4 + 3 * at, functools.partial(mem_stage, at)) for at in range(1, planes - 1)]
    final = total - planes * (planes + 1) // 2
    hooks += [(final + planes + 1, stage_pa), (final + 2 * planes - 1, stage_pb)]

    def hook(pairs):
        for number, body in sorted(hooks, key=lambda item: item[0]):
            pl.when(pairs == number)(body)


    def stage(index, carry):
        head = index // planes
        step = lax.rem(index, planes)
        here = jnp.where(rising, step, planes - 1 - step)

        @pl.when((step == 0) | ((step == 1) & jnp.logical_not(rising)))
        def _():
            @pl.when(rising | (step == 0))
            def _():
                arrive(head, here)

            @pl.when(jnp.logical_not(rising) & (step == 1))
            def _():
                next_head(head)

                def rest(which, inner):
                    arrive(head, planes - 2 - which)
                    return inner

                lax.fori_loop(0, planes - 1, rest, 0)

        begun = head * (planes * (planes + 1) // 2) + step * planes - step * (step - 1) // 2
        hook(begun)
        pair(head, here, here, True)

        @pl.when(rising)
        def _():
            hand_queries(head, here)

        @pl.when(jnp.logical_not(rising))
        def _():
            hand_keys(head, here)

        def far(at, inner):
            there = jnp.where(rising, here + 1 + at, here - 1 - at)

            @pl.when(rising & (step == 0))
            def _():
                arrive(head, there)

            hook(begun + 1 + at)
            pair(head, jnp.maximum(here, there), jnp.minimum(here, there), False)
            return inner

        lax.fori_loop(0, planes - 1 - step, far, 0)

        @pl.when(rising & (step == 0))
        def _():
            next_head(head)

        @pl.when(rising)
        def _():
            hand_keys(head, here)

        @pl.when(jnp.logical_not(rising))
        def _():
            hand_queries(head, here)

        return carry

    lax.fori_loop(0, heads * planes, stage, 0)
    sum_end()
    mem_end()
    for load in loads[14:]:
        load.wait()

    def gathered(peer):
        for head in range(heads):
            q_copy(head, peer, peer).wait_recv()
            kv_copy(head, peer, peer).wait_recv()

    others(n, me, gathered)
    tile = 256
    grads = [g_recv[which].reshape(width, length) for which in range(3)]

    def last_product(index, carry):
        here = rows_of(index, tile)
        value = dot_nn(weights[0, here, :], grads[0])
        value = value + dot_nn(weights[1, here, :], grads[1])
        value = value + dot_nn(weights[2, here, :], grads[2])
        tg_ref[:, here] = (base_ref[:, here] + value.T).astype(low)
        return carry

    lax.fori_loop(0, width // tile, last_product, 0)
    for other in range(n):

        @pl.when(other != me)
        def _():
            pre_b(other, other).wait_recv()

        value = pre_recv[other].astype(f32)
        for which in range(2):
            pkv_ref[:, which * width + other * group : which * width + (other + 1) * group] = (
                jnp.concatenate(
                    [value[head, :, which * HD : (which + 1) * HD] for head in range(heads)], axis=1
                )
            )

    def drain(peer):
        do_copy(heads - 1, peer, me).wait_send()
        pre_b(peer, me).wait_send()
        for head in range(heads):
            q_copy(head, peer, me).wait_send()
            kv_copy(head, peer, me).wait_send()

    others(n, me, drain)
    others(batches, my_batch, lambda peer: pre_a(peer, my_batch).wait_send())
    others(batches, my_batch, lambda peer: vec_a(peer, my_batch).wait_send())
    reduce_core().wait_send()
    others(highs, my_high, lambda peer: reduce_x(peer, my_high).wait_send())
    reduce_y().wait_send()
    others(planes, my_plane, lambda peer: reduce_z(peer, my_plane).wait_send())
    others(planes, my_plane, lambda peer: gather_z(peer, my_plane).wait_send())
    gather_y(my_side).wait_send()
    others(highs, my_high, lambda peer: gather_x(peer, my_high).wait_send())
    gather_core(my_core).wait_send()
    mem_across().wait_send()
    mem_drain()
    others(planes, my_plane, lambda peer: vec_c(peer, my_plane).wait_send())
    vec_b(my_side).wait_send()
    save_full.wait()


def self_backward(
    n, batches, first_grad, out_grad, sums, mem_grads, mem_weights, vecs, saved, weights
):
    length, width = first_grad.shape
    group = width // n
    heads = group // HD
    whole = n * length
    planes = n // 2
    low = jnp.bfloat16
    f32 = jnp.float32
    vmem = pl.BlockSpec(memory_space=pltpu.VMEM)
    anywhere = pl.BlockSpec(memory_space=pl.ANY)
    dma = pltpu.SemaphoreType.DMA
    sum_rows = sums.shape[0] // (n * batches)
    mem_len = mem_grads[0].shape[0]
    mem_rows = mem_len // n
    mem_part = pltpu.VMEM((planes, mem_rows, width), low)
    mem_low = pltpu.VMEM((mem_len, width), low)
    square = pltpu.VMEM((width, width), low)
    vec = pltpu.VMEM((8, width), f32)
    copies = 6 + 2 * (batches // 2) + 5 * planes + 2 * batches + n
    qx, kx, raw, pk, pv, pkt, ot, stat = (pltpu.VMEM(value.shape, value.dtype) for value in saved)
    return pl.pallas_call(
        functools.partial(self_backward_kernel, n, batches),
        out_shape=(
            jax.ShapeDtypeStruct((length, width), low),
            jax.ShapeDtypeStruct((mem_rows, width), low),
            jax.ShapeDtypeStruct((PREFIX_ROWS, 2 * width), f32),
            jax.ShapeDtypeStruct((8, width), f32),
            jax.ShapeDtypeStruct((2, batches // 2, 2, planes, sum_rows, LANES), low),
        ),
        in_specs=[anywhere] * 19,
        out_specs=(vmem, vmem, vmem, vmem, anywhere),
        scratch_shapes=[
            pltpu.VMEM((heads, n, HD, length), low),
            qx,
            kx,
            raw,
            pltpu.VMEM((heads, HD, whole), low),
            pltpu.VMEM((heads, whole, HD), low),
            pltpu.VMEM((heads, HD, whole), low),
            pltpu.VMEM((heads, whole, 2 * HD), low),
            pk,
            pv,
            pkt,
            ot,
            stat,
            pltpu.VMEM((3, width, width), low),
            pltpu.VMEM((planes, heads, HD, 2 * length), f32),
            pltpu.VMEM((heads, whole, 2 * HD), f32),
            pltpu.VMEM((n, heads, 3, HD, length), low),
            pltpu.VMEM((3, n, heads, HD, length), low),
            pltpu.VMEM((heads, PREFIX_ROWS, 2 * HD), f32),
            pltpu.VMEM((batches, heads, PREFIX_ROWS, 2 * HD), f32),
            pltpu.VMEM((heads, PREFIX_ROWS, 2 * HD), low),
            pltpu.VMEM((n, heads, PREFIX_ROWS, 2 * HD), low),
            pltpu.VMEM((sums.shape[0] // 2, LANES), low),
            pltpu.VMEM((sums.shape[0] // 2, LANES), low),
            pltpu.VMEM((batches // 2, sums.shape[0] // batches, LANES), low),
            pltpu.VMEM((planes * sum_rows, LANES), low),
            pltpu.VMEM((planes, sum_rows, LANES), low),
            pltpu.VMEM((2, batches // 2, 2, planes, sum_rows, LANES), low),
            mem_low,
            mem_low,
            square,
            square,
            pltpu.VMEM((planes, 2, mem_rows, width), low),
            mem_part,
            mem_part,
            mem_part,
            pltpu.VMEM((batches, 8, width), f32),
            vec,
            pltpu.VMEM((2, 8, width), f32),
            vec,
            pltpu.VMEM((planes, 8, width), f32),
            pltpu.VMEM((length, width), f32),
            dma((heads, n)),
            dma((heads, n)),
            dma((2, heads, n)),
            dma((2, heads, n)),
            dma((19,)),
            dma((copies,)),
            dma((copies,)),
        ],
        compiler_params=pltpu.CompilerParams(
            collective_id=1, has_side_effects=True, vmem_limit_bytes=VMEM_BYTES
        ),
        name="self_backward",
    )(
        first_grad,
        out_grad,
        sums.reshape(2, -1, LANES),
        *mem_grads,
        *mem_weights,
        vecs,
        *saved,
        *weights,
    )


def both_parts(value):
    high = value.astype(jnp.bfloat16).astype(jnp.float32)
    return jnp.concatenate([high, value - high], axis=0).astype(jnp.bfloat16)


def finish_kernel(
    full_ref,
    vecs_ref,
    pkv_ref,
    emb_ref,
    first_ref,
    fbias_ref,
    second_ref,
    embed_out,
    first_out,
    fbias_out,
    second_out,
    sbias_out,
    down_out,
    dbias_out,
    raise_out,
    rbias_out,
    gain_out,
    shift_out,
    first_grad,
    second_grad,
    down_grad,
    raise_grad,
    emb,
    hidden,
    out_sem,
):
    f32 = jnp.float32
    low = jnp.bfloat16
    width = emb_ref.shape[1]
    down = dbias_out.shape[1]
    count = emb_ref.shape[0]
    saves = []

    def save(source, target, rows=None):
        if rows is not None:
            source, target = source.at[rows], target.at[rows]
        copy = pltpu.make_async_copy(source, target, out_sem.at[len(saves)])
        copy.start()
        saves.append(copy)

    first = down * width // LANES
    for index in range(width // LANES):
        raise_grad[:, index * LANES : (index + 1) * LANES] = full_ref[
            first + index * down : first + (index + 1) * down, :
        ].astype(f32)
    save(raise_grad, raise_out)
    for index in range(down // LANES):
        down_grad[:, index * LANES : (index + 1) * LANES] = full_ref[
            index * width : (index + 1) * width, :
        ].astype(f32)
    save(down_grad, down_out)
    emb[...] = jnp.zeros_like(emb)
    emb[:count, :] = emb_ref[...].astype(f32)
    emb_low = emb[...].astype(low)
    row = lax.broadcasted_iota(jnp.int32, hidden.shape, 0)
    hidden[...] = jnp.where(
        row < count, jnp.tanh(dot_nn(emb_low, first_ref[...]) + fbias_ref[...]), 0.0
    )
    value = hidden[...]
    prefix = pkv_ref[...]
    parts = both_parts(prefix)
    hidden_twice = jnp.concatenate([value, value], axis=0).T.astype(low)
    tile = 128
    for index in range(second_grad.shape[0] // tile):
        here = slice(index * tile, (index + 1) * tile)
        second_grad[here, :] = dot_nn(hidden_twice[here, :], parts)
        save(second_grad, second_out, here)
    sbias_out[...] = jnp.sum(prefix, axis=0, keepdims=True)
    grad = dot_nt(parts, second_ref[...])
    grad = (grad[:PREFIX_ROWS] + grad[PREFIX_ROWS:]) * (1.0 - value * value)
    fbias_out[...] = jnp.sum(grad, axis=0, keepdims=True)
    parts = both_parts(grad)
    emb_twice = jnp.concatenate([emb[...], emb[...]], axis=0).T.astype(low)
    first_grad[...] = dot_nn(emb_twice, parts)
    save(first_grad, first_out)
    back = dot_nt(parts, first_ref[...])
    embed_out[...] = (back[:PREFIX_ROWS] + back[PREFIX_ROWS:])[:count, :]
    rbias_out[...] = vecs_ref[0:1, :]
    dbias_out[...] = vecs_ref[1:2, :down]
    gain_out[...] = vecs_ref[2:5, :]
    shift_out[...] = vecs_ref[5:8, :]
    for copy in saves:
        copy.wait()


def finish(full, vecs, prefix_grad, embed, first, first_bias, second, down):
    f32 = jnp.float32
    count, width = embed.shape
    hidden = first.shape[1]
    vmem = pl.BlockSpec(memory_space=pltpu.VMEM)
    anywhere = pl.BlockSpec(memory_space=pl.ANY)
    shapes = (
        (count, width),
        (width, hidden),
        (1, hidden),
        (hidden, 2 * width),
        (1, 2 * width),
        (width, down),
        (1, down),
        (down, width),
        (1, width),
        (3, width),
        (3, width),
    )
    return pl.pallas_call(
        finish_kernel,
        out_shape=tuple(jax.ShapeDtypeStruct(shape, f32) for shape in shapes),
        in_specs=[vmem] * 7,
        out_specs=(
            vmem,
            anywhere,
            vmem,
            anywhere,
            vmem,
            anywhere,
            vmem,
            anywhere,
            vmem,
            vmem,
            vmem,
        ),
        scratch_shapes=[
            pltpu.VMEM((width, hidden), f32),
            pltpu.VMEM((hidden, 2 * width), f32),
            pltpu.VMEM((width, down), f32),
            pltpu.VMEM((down, width), f32),
            pltpu.VMEM((PREFIX_ROWS, width), f32),
            pltpu.VMEM((PREFIX_ROWS, hidden), f32),
            pltpu.SemaphoreType.DMA((3 + hidden // 128,)),
        ],
        compiler_params=pltpu.CompilerParams(vmem_limit_bytes=VMEM_BYTES),
        name="finish",
    )(full, vecs, prefix_grad, embed, first, first_bias, second)


def gelu_pair(value):
    scaled = jnp.abs(value) * 0.7071067811865476
    step = 1.0 / (1.0 + 0.3275911 * scaled)
    bell = jnp.exp(-scaled * scaled)
    poly = step * (
        0.254829592
        + step
        * (-0.284496736 + step * (1.421413741 + step * (-1.453152027 + step * 1.061405429)))
    )
    tail = 0.5 * poly * bell
    share = jnp.where(value >= 0.0, 1.0 - tail, tail)
    return value * share, share + value * (bell * 0.3989422804014327)


def normed(value):
    center = jnp.mean(value, axis=-1, keepdims=True)
    centered = value - center
    scale = lax.rsqrt(jnp.mean(centered * centered, axis=-1, keepdims=True) + norm_eps)
    return centered * scale, scale


def norm_back(grad, scale, unit):
    return scale * (
        grad
        - jnp.mean(grad, axis=-1, keepdims=True)
        - unit * jnp.mean(grad * unit, axis=-1, keepdims=True)
    )


def middle_kernel(
    tok_in,
    att_in,
    cot_in,
    mkey_in,
    mvalue_in,
    gain_ref,
    shift_ref,
    dbias_ref,
    rbias_ref,
    wo_in,
    wcq_in,
    wco_in,
    wd_in,
    wr_in,
    win_in,
    wout_in,
    layer_out,
    fgrad_ref,
    ograd_ref,
    mkey_out,
    mvalue_out,
    sums_out,
    vecs_ref,
    tok_ref,
    att_ref,
    cot_ref,
    mkey_ref,
    mvalue_ref,
    out_ref,
    sums_ref,
    wo,
    wcq,
    wco,
    wd,
    wr,
    win,
    wout,
    unit_one,
    unit_two,
    work,
    total,
    scale_one,
    scale_two,
    low_one,
    low_two,
    low_three,
    query,
    crossed,
    weights,
    slopes,
    down_act,
    down_slope,
    down_grad,
    load_sem,
    win_sem,
    wout_sem,
    out_sem,
):
    length, width = tok_ref.shape
    tile = win.shape[2]
    tiles = win_in.shape[1] // tile
    rows_step = 128
    low = jnp.bfloat16
    f32 = jnp.float32

    sources = (
        att_in,
        wo_in,
        tok_in,
        wcq_in,
        mkey_in,
        mvalue_in,
        wco_in,
        wd_in,
        wr_in,
        cot_in,
    )
    targets = (att_ref, wo, tok_ref, wcq, mkey_ref, mvalue_ref, wco, wd, wr, cot_ref)
    loads = [
        pltpu.make_async_copy(source, target, load_sem.at[index])
        for index, (source, target) in enumerate(zip(sources, targets))
    ]

    def win_load(which):
        slot = lax.rem(which, 2)
        return pltpu.make_async_copy(
            win_in.at[:, rows_of(which, tile)], win.at[slot], win_sem.at[slot]
        )

    def wout_load(which):
        slot = lax.rem(which, 2)
        return pltpu.make_async_copy(
            wout_in.at[rows_of(which, tile), :], wout.at[slot], wout_sem.at[slot]
        )

    for load in loads[:7]:
        load.start()
    for which in range(2):
        win_load(which).start()
        wout_load(which).start()
    for load in loads[7:]:
        load.start()

    def by_columns(extent, step, body):
        def one(index, carry):
            body(pl.ds(pl.multiple_of(index * step, step), step))
            return carry

        lax.fori_loop(0, extent // step, one, 0)

    def by_rows(body, init=0):
        def one(index, carry):
            return body(rows_of(index, rows_step), carry)

        return lax.fori_loop(0, length // rows_step, one, init)

    cols = 512
    half = width // 2

    for load in loads[:3]:
        load.wait()

    def project_out(here):
        work[:, here] = tok_ref[:, here].astype(f32) + dot_nn(att_ref[...], wo[:, here])

    by_columns(width, cols, project_out)

    def first_norm(here, carry):
        unit, scale = normed(work[here, :])
        unit_one[here, :] = unit
        scale_one[here, :] = scale
        value = unit * gain_ref[0:1, :] + shift_ref[0:1, :]
        work[here, :] = value
        low_one[here, :] = value.astype(low)
        return carry

    by_rows(first_norm)

    loads[3].wait()

    def project_query(here):
        query[:, here] = dot_nn(low_one[...], wcq[:, here]).astype(low)

    by_columns(width, cols, project_query)
    per_block = LANES // HD

    def head_queries(here, head):
        both = query[:, here].astype(f32) * 0.125
        return jnp.where(head_lanes(both.shape, head), both, 0.0).astype(low)

    def cross_forward(block):
        here = rows_of(block, LANES)
        keys = mkey_ref[:, here]
        values = mvalue_ref[:, here].astype(f32).T.astype(low)
        outs = []
        for head in range(per_block):
            scores = dot_nt(keys, head_queries(here, head))
            raised = jnp.exp(scores - jnp.max(scores, axis=0, keepdims=True))
            share = 1.0 / jnp.sum(raised, axis=0, keepdims=True)
            weight = (raised * share).astype(low)
            weights[block * per_block + head] = weight
            outs.append(dot_nn(values[head * HD : (head + 1) * HD, :], weight))
        crossed[:, here] = jnp.concatenate(outs, axis=0).T.astype(low)

    loads[4].wait()
    loads[5].wait()

    def cross_forward_both(step, carry):
        cross_forward(2 * step)
        cross_forward(2 * step + 1)
        return carry

    lax.fori_loop(0, width // LANES // 2, cross_forward_both, 0)

    loads[6].wait()

    def project_crossed(here):
        work[:, here] += dot_nn(crossed[...], wco[:, here])

    by_columns(width, cols, project_crossed)

    def second_norm(here, carry):
        unit, scale = normed(work[here, :])
        unit_two[here, :] = unit
        scale_two[here, :] = scale
        value = unit * gain_ref[1:2, :] + shift_ref[1:2, :]
        work[here, :] = value
        low_two[here, :] = value.astype(low)
        return carry

    by_rows(second_norm)

    total[...] = jnp.zeros_like(total)

    def feed_forward(which, carry):
        slot = lax.rem(which, 2)
        win_load(which).wait()
        wout_load(which).wait()
        act, slope = gelu_pair(dot_nn(low_two[...], win[slot]))
        slopes[:, rows_of(which, tile)] = slope.astype(low)
        total[...] += dot_nn(act.astype(low), wout[slot])

        @pl.when(which + 2 < tiles)
        def _():
            win_load(which + 2).start()
            wout_load(which + 2).start()

        return carry

    lax.fori_loop(0, tiles, feed_forward, 0)
    loads[7].wait()
    loads[8].wait()
    loads[9].wait()
    act, slope = gelu_pair(dot_nn(low_two[...], wd[...]) + dbias_ref[...])
    down_act[...] = act.astype(low)
    down_slope[...] = slope.astype(low)

    def project_raise(here):
        work[:, here] += total[:, here] + 4.0 * (
            dot_nn(down_act[...], wr[:, here]) + rbias_ref[:, here]
        )

    by_columns(width, cols, project_raise)
    nothing = jnp.zeros((1, width), f32)

    def third_norm(here, carry):
        gain_sum, shift_sum, bias_sum = carry
        unit, scale = normed(work[here, :])
        gain = gain_ref[2:3, :]
        out_ref[here, :] = (unit * gain + shift_ref[2:3, :]).astype(low)
        grad = cot_ref[here, :].astype(f32)
        back = norm_back(grad * gain, scale, unit)
        total[here, :] = back
        back_low = back.astype(low)
        low_three[here, :] = back_low
        return (
            gain_sum + jnp.sum(grad * unit, axis=0, keepdims=True),
            shift_sum + jnp.sum(grad, axis=0, keepdims=True),
            bias_sum + jnp.sum(back_low.astype(f32), axis=0, keepdims=True),
        )

    gain_three, shift_three, bias_sum = by_rows(third_norm, (nothing, nothing, nothing))
    saves = []

    def save(source, target):
        copy = pltpu.make_async_copy(source, target, out_sem.at[len(saves)])
        copy.start()
        saves.append(copy)

    save(out_ref, layer_out)
    vecs_ref[0:1, :] = 4.0 * bias_sum

    back = 4.0 * dot_nt(low_three[...], wr[...]) * down_slope[...].astype(f32)
    back_low = back.astype(low)
    down_grad[...] = back_low
    vecs_ref[1:2, :] = jnp.concatenate(
        [
            jnp.sum(back_low.astype(f32), axis=0, keepdims=True),
            jnp.zeros((1, width - wd.shape[1]), f32),
        ],
        axis=1,
    )
    down = wd.shape[1]
    raise_sum = 4.0 * dot_tn(down_act[...], low_three[...])
    for index in range(width // LANES):
        sums_ref[pl.ds(down * width // LANES + index * down, down), :] = raise_sum[
            :, index * LANES : (index + 1) * LANES
        ].astype(low)
    down_sum = dot_tn(low_two[...], down_grad[...])
    for index in range(down // LANES):
        sums_ref[index * width : (index + 1) * width, :] = down_sum[
            :, index * LANES : (index + 1) * LANES
        ].astype(low)

    save(sums_ref, sums_out)

    def feed_backward(step, carry):
        which = tiles - 1 - step
        slot = lax.rem(which, 2)
        here = rows_of(which, tile)

        @pl.when(which < tiles - 2)
        def _():
            wout_load(which).wait()
            win_load(which).wait()

        grad = dot_nt(low_three[...], wout[slot]) * slopes[:, here].astype(f32)
        total[...] += dot_nt(grad.astype(low), win[slot])

        @pl.when(which >= 2)
        def _():
            win_load(which - 2).start()
            wout_load(which - 2).start()

        return carry

    lax.fori_loop(0, tiles, feed_backward, 0)

    def down_back(here):
        total[:, here] += dot_nt(down_grad[...], wd[here, :])

    by_columns(width, cols, down_back)

    def second_back(here, carry):
        gain_sum, shift_sum = carry
        grad = total[here, :]
        unit = unit_two[here, :]
        back = norm_back(grad * gain_ref[1:2, :], scale_two[here, :], unit)
        total[here, :] = back
        low_one[here, :] = back.astype(low)
        return (
            gain_sum + jnp.sum(grad * unit, axis=0, keepdims=True),
            shift_sum + jnp.sum(grad, axis=0, keepdims=True),
        )

    gain_two, shift_two = by_rows(second_back, (nothing, nothing))

    def crossed_back(here):
        crossed[:, here] = dot_nt(low_one[...], wco[here, :]).astype(low)

    by_columns(width, cols, crossed_back)

    def cross_backward(block):
        here = rows_of(block, LANES)
        values = mvalue_ref[:, here]
        keys = mkey_ref[:, here].astype(f32).T.astype(low)
        grads = crossed[:, here].astype(f32)
        outs = []
        key_sum = None
        for head in range(per_block):
            grad = jnp.where(head_lanes(grads.shape, head), grads, 0.0).astype(low)
            weight_low = weights[block * per_block + head]
            weight = weight_low.astype(f32)
            slope = dot_nt(values, grad)
            slope = weight * (slope - jnp.sum(weight * slope, axis=0, keepdims=True))
            slope = slope.astype(low)
            key_part = dot_nn(slope, head_queries(here, head))
            value_part = dot_nn(weight_low, grad)
            if key_sum is None:
                key_sum, value_sum = key_part, value_part
            else:
                key_sum, value_sum = key_sum + key_part, value_sum + value_part
            outs.append(dot_nn(keys[head * HD : (head + 1) * HD, :], slope))
        mkey_ref[:, here] = key_sum.astype(low)
        mvalue_ref[:, here] = value_sum.astype(low)
        query[:, here] = (jnp.concatenate(outs, axis=0) * 0.125).T.astype(low)

    def cross_backward_both(step, carry):
        cross_backward(2 * step)
        cross_backward(2 * step + 1)
        return carry

    lax.fori_loop(0, width // LANES // 2, cross_backward_both, 0)
    save(mkey_ref, mkey_out)
    save(mvalue_ref, mvalue_out)

    def query_back(here):
        total[:, here] += dot_nt(query[...], wcq[here, :])

    by_columns(width, cols, query_back)

    def first_back(here, carry):
        gain_sum, shift_sum = carry
        grad = total[here, :]
        unit = unit_one[here, :]
        back = norm_back(grad * gain_ref[0:1, :], scale_one[here, :], unit)
        fgrad_ref[here, :] = back
        low_one[here, :] = back.astype(low)
        return (
            gain_sum + jnp.sum(grad * unit, axis=0, keepdims=True),
            shift_sum + jnp.sum(grad, axis=0, keepdims=True),
        )

    gain_one, shift_one = by_rows(first_back, (nothing, nothing))

    def out_back(here):
        ograd_ref[here, :] = dot_nt(low_one[...], wo[here, :]).T.astype(low)

    by_columns(width, cols, out_back)
    for index, vector in enumerate(
        (gain_one, gain_two, gain_three, shift_one, shift_two, shift_three)
    ):
        vecs_ref[2 + index : 3 + index, :] = vector
    for copy in saves:
        copy.wait()


def middle(
    tokens, attended, cotangent, mem_key, mem_value, gains, shifts, down_bias, raise_bias, weights
):
    length, width = tokens.shape
    mem_len = mem_key.shape[0]
    down = weights[3].shape[1]
    feed = weights[5].shape[1]
    tile = 512 if mem_len <= 512 else 128
    low = jnp.bfloat16
    f32 = jnp.float32
    vmem = pl.BlockSpec(memory_space=pltpu.VMEM)
    anywhere = pl.BlockSpec(memory_space=pl.ANY)
    square = pltpu.VMEM((width, width), low)
    wide = pltpu.VMEM((length, width), f32)
    narrow = pltpu.VMEM((length, width), low)
    return pl.pallas_call(
        middle_kernel,
        out_shape=(
            jax.ShapeDtypeStruct((length, width), low),
            jax.ShapeDtypeStruct((length, width), f32),
            jax.ShapeDtypeStruct((width, length), low),
            jax.ShapeDtypeStruct((mem_len, width), low),
            jax.ShapeDtypeStruct((mem_len, width), low),
            jax.ShapeDtypeStruct((2 * down * width // LANES, LANES), low),
            jax.ShapeDtypeStruct((8, width), f32),
        ),
        in_specs=[anywhere] * 5 + [vmem] * 4 + [anywhere] * 7,
        out_specs=(anywhere, vmem, vmem, anywhere, anywhere, anywhere, vmem),
        scratch_shapes=[
            narrow,
            narrow,
            narrow,
            pltpu.VMEM((mem_len, width), low),
            pltpu.VMEM((mem_len, width), low),
            narrow,
            pltpu.VMEM((2 * down * width // LANES, LANES), low),
            square,
            square,
            square,
            pltpu.VMEM((width, down), low),
            pltpu.VMEM((down, width), low),
            pltpu.VMEM((2, width, tile), low),
            pltpu.VMEM((2, tile, width), low),
            wide,
            wide,
            wide,
            wide,
            pltpu.VMEM((length, 1), f32),
            pltpu.VMEM((length, 1), f32),
            narrow,
            narrow,
            narrow,
            narrow,
            narrow,
            pltpu.VMEM((H, mem_len, length), low),
            pltpu.VMEM((length, feed), low),
            pltpu.VMEM((length, down), low),
            pltpu.VMEM((length, down), low),
            pltpu.VMEM((length, down), low),
            pltpu.SemaphoreType.DMA((10,)),
            pltpu.SemaphoreType.DMA((2,)),
            pltpu.SemaphoreType.DMA((2,)),
            pltpu.SemaphoreType.DMA((4,)),
        ],
        compiler_params=pltpu.CompilerParams(vmem_limit_bytes=VMEM_BYTES + (0 if mem_len <= 512 else 3 * 1024 * 1024)),
        name="middle",
    )(tokens, attended, cotangent, mem_key, mem_value, gains, shifts, down_bias, raise_bias, *weights)


def per_device(
    tokens,
    memory,
    segment_ids,
    padding_mask,
    cotangent,
    prefix_embed,
    prefix_first,
    first_bias,
    prefix_second,
    second_bias,
    adapter_down,
    down_bias,
    adapter_raise,
    raise_bias,
    norm_gain,
    norm_shift,
    self_query,
    self_key,
    self_value,
    self_output,
    cross_query,
    cross_key,
    cross_value,
    cross_output,
    feed_in,
    feed_out,
):
    row_count, length, model_width = tokens.shape
    flat_rows = row_count * length
    n = lax.axis_size("seq")
    batches = lax.axis_size("batch")
    down = adapter_down.shape[1]
    attended, mem_key, mem_value, *saved = self_forward(
        n,
        segment_ids,
        padding_mask,
        tokens.reshape(flat_rows, model_width),
        (self_query, self_key, self_value),
        (
            prefix_embed,
            prefix_first,
            first_bias.reshape(1, -1),
            prefix_second,
            second_bias.reshape(1, -1),
        ),
        memory.reshape(-1, model_width),
        (cross_key, cross_value),
    )
    layer_output, first_grad, out_grad, *mem_grads, weight_sums, vector_sums = middle(
        tokens.reshape(flat_rows, model_width),
        attended,
        cotangent.reshape(flat_rows, model_width),
        mem_key,
        mem_value,
        norm_gain,
        norm_shift,
        down_bias.reshape(1, -1),
        raise_bias.reshape(1, -1),
        (
            self_output,
            cross_query,
            cross_output,
            adapter_down,
            adapter_raise,
            feed_in,
            feed_out,
        ),
    )
    layer_output = layer_output.reshape(row_count, length, model_width)
    token_grad, memory_grad, prefix_grad, vector_sums, full_sums = self_backward(
        n,
        batches,
        first_grad,
        out_grad.reshape(n, -1, HD, length),
        weight_sums,
        mem_grads,
        (cross_key, cross_value),
        vector_sums,
        saved,
        (self_query, self_key, self_value),
    )
    token_grad = token_grad.reshape(row_count, length, model_width)
    memory_grad = memory_grad.reshape(memory.shape)
    replicated = finish(
        full_sums.reshape(-1, LANES),
        vector_sums,
        prefix_grad,
        prefix_embed,
        prefix_first,
        first_bias.reshape(1, -1),
        prefix_second,
        down,
    )
    replicated = [
        value.reshape(-1) if value.shape[0] == 1 else value for value in replicated
    ]
    return (layer_output, token_grad, memory_grad, *replicated)


def solution(mesh):
    placed = (
        P("batch", "seq", None),
        P("batch", "seq", None),
        P("batch", "seq"),
        P("batch", "seq"),
        P("batch", "seq", None),
        P(),
        P(),
        P(),
        P(),
        P(),
        P(),
        P(),
        P(),
        P(),
        P(),
        P(),
        P(),
        P(),
        P(),
        P(),
        P(),
        P(),
        P(),
        P(),
        P(),
        P(),
    )
    return jax.shard_map(
        per_device,
        mesh=mesh,
        in_specs=placed,
        out_specs=(
            P("batch", "seq", None),
            P("batch", "seq", None),
            P("batch", "seq", None),
            P(),
            P(),
            P(),
            P(),
            P(),
            P(),
            P(),
            P(),
            P(),
            P(),
            P(),
        ),
        check_vma=False,
    )
```

```python
import functools

import jax
import jax.numpy as jnp
from jax import lax
from jax.experimental import pallas as pl
from jax.experimental.pallas import tpu as pltpu
from jax.sharding import PartitionSpec as P

H = 16
HD = 64
LANES = 128
PREFIX_ROWS = 32
VMEM_BYTES = 60 * 1024 * 1024
SUM_ROWS = 16
MESH = pl.DeviceIdType.MESH

masked_score = -1e30
norm_eps = 1e-05

def dot_nn(left, right):
    return lax.dot_general(
        left, right, (((1,), (0,)), ((), ())), preferred_element_type=jnp.float32
    )


def dot_nt(left, right):
    return lax.dot_general(
        left, right, (((1,), (1,)), ((), ())), preferred_element_type=jnp.float32
    )


def dot_tn(left, right):
    return lax.dot_general(
        left, right, (((0,), (0,)), ((), ())), preferred_element_type=jnp.float32
    )


def remote(source, target, send_sem, recv_sem, axis, peer):
    return pltpu.make_async_remote_copy(
        src_ref=source,
        dst_ref=target,
        send_sem=send_sem,
        recv_sem=recv_sem,
        device_id={axis: peer},
        device_id_type=MESH,
    )


def enter(sizes):
    barrier = pltpu.get_barrier_semaphore()
    for axis, size in sizes.items():
        for other in range(size):

            @pl.when(other != lax.axis_index(axis))
            def _():
                pl.semaphore_signal(barrier, inc=1, device_id={axis: other}, device_id_type=MESH)

    pl.semaphore_wait(barrier, sum(sizes.values()) - len(sizes))


def others(size, mine, body):
    for other in range(size):

        @pl.when(other != mine)
        def _():
            body(other)


def rows_of(index, size):
    return pl.ds(pl.multiple_of(index * size, size), size)


def span_of(start, size):
    return pl.ds(pl.multiple_of(start, LANES), size)


def own_columns(ref, first, me, width):
    if width % LANES == 0:
        return ref[:, pl.ds(pl.multiple_of(first + me * width, LANES), width)].astype(jnp.float32)
    share = LANES // width
    block = ref[:, pl.ds(pl.multiple_of(first + me // share * LANES, LANES), LANES)].astype(
        jnp.float32
    )
    picked = block[:, :width]
    for part in range(1, share):
        picked = jnp.where(me % share == part, block[:, part * width : (part + 1) * width], picked)
    return picked


def head_lanes(shape, head):
    lane = lax.broadcasted_iota(jnp.int32, shape, 1)
    return (lane >= head * HD) & (lane < (head + 1) * HD)


def self_forward_kernel(
    n,
    seg_ref,
    pad_ref,
    tok_ref,
    wq_in,
    wk_in,
    wv_in,
    emb_ref,
    first_in,
    fbias_ref,
    second_in,
    sbias_ref,
    mem_ref,
    wck_in,
    wcv_in,
    att_ref,
    mkey_ref,
    mvalue_ref,
    qx_out,
    kx_out,
    raw_out,
    pk_out,
    pv_out,
    pkt_out,
    ot_out,
    lse_out,
    send,
    recv,
    meta_send,
    meta,
    kx,
    qx,
    vt,
    hidden,
    pk,
    pv,
    pkt,
    pvt,
    stat,
    acc,
    o_send,
    o_recv,
    mem_all,
    wck,
    wcv,
    wq_ref,
    wk_ref,
    wv_ref,
    first_ref,
    second_ref,
    send_sem,
    recv_sem,
    meta_send_sem,
    meta_recv_sem,
    o_send_sem,
    o_recv_sem,
    mem_send_sem,
    mem_recv_sem,
    out_sem,
    weight_sem,
    in_sem,
):
    low = jnp.bfloat16
    f32 = jnp.float32
    me = lax.axis_index("seq")
    length, width = tok_ref.shape
    group = width // n
    heads = group // HD
    plane = 2 * length
    planes = n // 2
    block = 2 * LANES
    per_block = block // group
    blocks = width // block
    step_rows = 256
    steps = plane // step_rows
    my_plane = me // 2
    my_side = lax.rem(me, 2)

    def meta_copy(peer, slot):
        return remote(
            meta_send, meta.at[slot], meta_send_sem.at[peer], meta_recv_sem.at[slot], "seq", peer
        )

    def qkv_copy(head, peer, slot):
        return remote(
            send.at[peer, head],
            recv.at[head, slot],
            send_sem.at[head, peer],
            recv_sem.at[head, slot],
            "seq",
            peer,
        )

    def out_copy(head, peer, slot):
        return remote(
            o_send.at[head, peer],
            o_recv.at[slot, head],
            o_send_sem.at[head, peer],
            o_recv_sem.at[head, slot],
            "seq",
            peer,
        )

    def mem_along(which, toward):
        part = mem_all.at[which, my_side]
        return remote(
            part,
            part,
            mem_send_sem.at[(toward + 1) // 2, which],
            mem_recv_sem.at[which],
            "seq",
            me + 2 * toward,
        )

    def mem_across(side):
        part = mem_all.at[:, side]
        return remote(
            part,
            part,
            mem_send_sem.at[0, planes],
            mem_recv_sem.at[planes],
            "seq",
            me + 1 - 2 * my_side,
        )

    def mem_hops(hop, body):
        for toward in (1, -1):
            which = my_plane - toward * hop
            ahead = my_plane + toward

            @pl.when((which >= 0) & (which < planes) & (ahead >= 0) & (ahead < planes))
            def _():
                body(mem_along(which, toward))

    def mem_arrivals(hop):
        for toward in (1, -1):
            which = my_plane - toward * hop

            @pl.when((which >= 0) & (which < planes))
            def _():
                mem_along(which, -toward).wait_recv()

    def block_at(step):
        if blocks >= planes:
            share = blocks // planes
            return lax.rem(my_plane + 1 + step // share, planes) * share + step % share
        return lax.rem(me // per_block + 1 + step, blocks)

    def weight_load(step, which):
        columns = rows_of(block_at(step), block)
        source = (wq_in, wk_in, wv_in)[which]
        target = (wq_ref, wk_ref, wv_ref)[which]
        return pltpu.make_async_copy(
            source.at[:, columns], target.at[:, columns], weight_sem.at[step, which]
        )

    for step in range(blocks):
        for which in range(3):
            weight_load(step, which).start()
    loads = [
        pltpu.make_async_copy(source, target, in_sem.at[index])
        for index, (source, target) in enumerate(
            ((first_in, first_ref), (second_in, second_ref), (wck_in, wck), (wcv_in, wcv))
        )
    ]
    for load in loads:
        load.start()
    segments = seg_ref[...]
    tags = jnp.where(pad_ref[...] == 1, segments, -1)
    row = lax.broadcasted_iota(jnp.int32, meta_send.shape, 0)
    meta_send[...] = jnp.where(row == 0, segments, tags)
    mem_all[my_plane, my_side] = mem_ref[...]
    enter({"seq": n})
    others(n, me, lambda peer: meta_copy(peer, me).start())
    meta[me] = meta_send[...]

    for step in range(blocks):
        at = block_at(step)
        columns = rows_of(at, block)
        for which, weight in enumerate((wq_ref, wk_ref, wv_ref)):
            weight_load(step, which).wait()
            piece = dot_nn(tok_ref[...], weight[:, columns]).T.astype(low)
            for part in range(per_block):
                for head in range(heads):
                    first = part * group + head * HD
                    send[at * per_block + part, head, which] = piece[first : first + HD]
        for part in range(per_block):
            peer = at * per_block + part

            @pl.when(peer != me)
            def _():
                qkv_copy(0, peer, me).start()

            @pl.when(peer == me)
            def _():
                for head in range(heads):
                    recv[head, me] = send[peer, head]

    mem_hops(0, lambda copy: copy.start())

    loads[0].wait()
    loads[1].wait()
    hidden[...] = jnp.zeros_like(hidden)
    hidden[: emb_ref.shape[0], :] = jnp.tanh(dot_nn(emb_ref[...], first_ref[...]) + fbias_ref[...])
    hidden_low = hidden[...].astype(low)
    prefix_key = dot_nn(hidden_low, own_columns(second_ref, 0, me, group).astype(low)) + own_columns(
        sbias_ref, 0, me, group
    )
    prefix_value = dot_nn(
        hidden_low, own_columns(second_ref, width, me, group).astype(low)
    ) + own_columns(sbias_ref, width, me, group)
    prefix_row = lax.broadcasted_iota(jnp.int32, (PREFIX_ROWS, HD), 0)
    prefix_open = jnp.where(prefix_row < emb_ref.shape[0], 0.0, masked_score)
    for head in range(heads):
        here = slice(head * HD, (head + 1) * HD)
        pk[head] = jnp.concatenate([prefix_key[:, here], prefix_open], axis=1).astype(low)
        pv[head] = prefix_value[:, here].astype(low)
    pkt[...] = prefix_key.T.astype(low).reshape(heads, HD, PREFIX_ROWS)
    pvt[:, :HD, :] = prefix_value.T.astype(low).reshape(heads, HD, PREFIX_ROWS)
    pvt[:, HD:, :] = jnp.ones((heads, SUM_ROWS, PREFIX_ROWS), low)
    vt[:, HD:, :] = jnp.ones((heads, SUM_ROWS, n * length), low)

    def arrive(head, chunk):
        @pl.when(chunk != me)
        def _():
            @pl.when(head == 0)
            def _():
                meta_copy(chunk, chunk).wait_recv()

            qkv_copy(head, chunk, chunk).wait_recv()

        here = rows_of(chunk, length)
        state = lax.broadcasted_iota(jnp.int32, (HD, length), 0)
        qx[head, :HD, here] = (recv[head, chunk, 0].astype(f32) * 0.125).astype(low)
        qx[head, HD:, here] = jnp.where(state == meta[chunk, 0:1, :], 1.0, 0.0).astype(low)
        is_open = jnp.where(state == meta[chunk, 1:2, :], 0.0, masked_score)
        kx[head, here, :] = jnp.concatenate(
            [recv[head, chunk, 1].astype(f32), is_open], axis=0
        ).T.astype(low)
        vt[head, :HD, here] = recv[head, chunk, 2]

    def open_plane(head, which):
        scores = dot_nn(pk[head], qx[head, :, rows_of(which, plane)])
        top = jnp.max(scores, axis=0, keepdims=True)
        raised = jnp.exp(scores - top)
        stat[which, head, 0:1, :] = top
        acc[which, head] = dot_nn(pvt[head], raised.astype(low))

    def pair_part(head, upper, lower, first, keys, diagonal):
        here = slice(first, first + step_rows)
        queries = qx[head, :, span_of(upper * plane + first, step_rows)]
        key_rows = span_of(lower * plane, keys)
        scores = dot_nn(kx[head, key_rows, :], queries)
        if diagonal:
            key_at = lax.broadcasted_iota(jnp.int32, scores.shape, 0)
            query_at = lax.broadcasted_iota(jnp.int32, scores.shape, 1) + first
            scores = jnp.where(key_at <= query_at, scores, masked_score)
        old_top = stat[upper, head, 0:1, here]
        top = jnp.maximum(old_top, jnp.max(scores, axis=0, keepdims=True))
        raised = jnp.exp(scores - top).astype(low)
        stat[upper, head, 0:1, here] = top
        acc[upper, head, :, here] = acc[upper, head, :, here] * jnp.exp(old_top - top) + dot_nn(
            vt[head, :, key_rows], raised
        )

    def pair(head, upper, lower):
        for part in range(steps):
            pair_part(head, upper, lower, part * step_rows, plane, False)

    def pair_diagonal(head, which):
        for part in range(steps):
            pair_part(head, which, which, part * step_rows, (part + 1) * step_rows, True)

    def close_plane(head, which):
        total = acc[which, head, HD : HD + 1, :]
        value = acc[which, head, :HD, :] / total
        acc[which, head, :HD, :] = value
        stat[which, head, 0:1, :] = stat[which, head, 0:1, :] + jnp.log(total)
        for part in range(2):
            chunk = 2 * which + part
            o_send[head, chunk] = value[:, part * length : (part + 1) * length].astype(low)

            @pl.when(chunk != me)
            def _():
                out_copy(head, chunk, me).start()

            @pl.when(chunk == me)
            def _():
                o_recv[me, head] = o_send[head, chunk]

    def project_memory():
        mem_across(1 - my_side).wait_recv()
        for load in loads[2:]:
            load.wait()
        whole = mem_all[...].reshape(mkey_ref.shape)

        def one(index, carry):
            here = rows_of(index, block)
            mkey_ref[:, here] = dot_nn(whole, wck[:, here]).astype(low)
            mvalue_ref[:, here] = dot_nn(whole, wcv[:, here]).astype(low)
            return carry

        lax.fori_loop(0, blocks, one, 0)

    def stage(index, carry):
        head = index // planes
        step = lax.rem(index, planes)

        @pl.when(head + 1 < heads)
        def _():
            there = lax.rem(my_plane + 1 + step, planes)
            for part in range(2):
                peer = 2 * there + part

                @pl.when(peer != me)
                def _():
                    qkv_copy(head, peer, me).wait_send()
                    qkv_copy(head + 1, peer, me).start()

        here = lax.rem(my_plane + step, planes)
        arrive(head, 2 * here)
        arrive(head, 2 * here + 1)
        open_plane(head, here)
        pair_diagonal(head, here)

        def earlier(back, inner):
            there = lax.rem(my_plane + back, planes)
            pair(head, jnp.maximum(here, there), jnp.minimum(here, there))

            @pl.when((step == planes - 1) & (there > here))
            def _():
                close_plane(head, there)

            return inner

        lax.fori_loop(0, step, earlier, 0)
        for hop in range(1, planes - 1):

            @pl.when(index == hop)
            def _():
                mem_arrivals(hop)
                mem_hops(hop, lambda copy: copy.start())

        @pl.when(index == planes - 1)
        def _():
            mem_arrivals(planes - 1)
            mem_across(my_side).start()

        @pl.when((my_plane + step >= planes) | (my_plane == 0))
        def _():
            close_plane(head, here)

        return carry

    lax.fori_loop(0, heads * planes, stage, 0)

    saves = []

    def save(source, target):
        copy = pltpu.make_async_copy(source, target, out_sem.at[len(saves)])
        copy.start()
        saves.append(copy)

    save(qx, qx_out)
    save(kx, kx_out)
    save(recv, raw_out)
    save(pk, pk_out)
    save(pv, pv_out)
    save(pkt, pkt_out)
    save(acc, ot_out)
    save(stat, lse_out)
    project_memory()
    for other in range(n):

        @pl.when(other != me)
        def _():
            for head in range(heads):
                out_copy(head, other, other).wait_recv()

        att_ref[:, other * group : (other + 1) * group] = (
            o_recv[other].reshape(group, length).astype(f32).T.astype(low)
        )

    def drain(peer):
        meta_copy(peer, me).wait_send()
        qkv_copy(heads - 1, peer, me).wait_send()
        for head in range(heads):
            out_copy(head, peer, me).wait_send()

    others(n, me, drain)
    for hop in range(planes - 1):
        mem_hops(hop, lambda copy: copy.wait_send())
    mem_across(my_side).wait_send()
    for copy in saves:
        copy.wait()


def self_forward(n, segments, padding, tokens, weights, prefix, memory, mem_weights):
    length, width = tokens.shape
    group = width // n
    heads = group // HD
    whole = n * length
    planes = n // 2
    low = jnp.bfloat16
    f32 = jnp.float32
    vmem = pl.BlockSpec(memory_space=pltpu.VMEM)
    anywhere = pl.BlockSpec(memory_space=pl.ANY)
    dma = pltpu.SemaphoreType.DMA
    shapes = (
        ((heads, 2 * HD, whole), low),
        ((heads, whole, 2 * HD), low),
        ((heads, n, 3, HD, length), low),
        ((heads, PREFIX_ROWS, 2 * HD), low),
        ((heads, PREFIX_ROWS, HD), low),
        ((heads, HD, PREFIX_ROWS), low),
        ((planes, heads, HD + SUM_ROWS, 2 * length), f32),
        ((planes, heads, 8, 2 * length), f32),
    )
    square = pltpu.VMEM((width, width), low)
    qx, kx, raw, pk, pv, pkt, acc, stat = (pltpu.VMEM(*shape) for shape in shapes)
    return pl.pallas_call(
        functools.partial(self_forward_kernel, n),
        out_shape=(
            jax.ShapeDtypeStruct((length, width), low),
            jax.ShapeDtypeStruct((n * memory.shape[0], width), low),
            jax.ShapeDtypeStruct((n * memory.shape[0], width), low),
        )
        + tuple(jax.ShapeDtypeStruct(*shape) for shape in shapes),
        in_specs=[vmem] * 3
        + [anywhere] * 3
        + [vmem, anywhere, vmem, anywhere, vmem, vmem]
        + [anywhere] * 2,
        out_specs=(vmem,) * 3 + (anywhere,) * 8,
        scratch_shapes=[
            pltpu.VMEM((n, heads, 3, HD, length), low),
            raw,
            pltpu.VMEM((8, length), jnp.int32),
            pltpu.VMEM((n, 8, length), jnp.int32),
            kx,
            qx,
            pltpu.VMEM((heads, HD + SUM_ROWS, whole), low),
            pltpu.VMEM((PREFIX_ROWS, weights[0].shape[0] // 2), f32),
            pk,
            pv,
            pkt,
            pltpu.VMEM((heads, HD + SUM_ROWS, PREFIX_ROWS), low),
            stat,
            acc,
            pltpu.VMEM((heads, n, HD, length), low),
            pltpu.VMEM((n, heads, HD, length), low),
            pltpu.VMEM((planes, 2) + memory.shape, low),
            square,
            square,
            square,
            square,
            square,
            pltpu.VMEM(prefix[1].shape, low),
            pltpu.VMEM(prefix[3].shape, low),
            dma((heads, n)),
            dma((heads, n)),
            dma((n,)),
            dma((n,)),
            dma((heads, n)),
            dma((heads, n)),
            dma((2, planes + 1)),
            dma((planes + 1,)),
            dma((8,)),
            dma((width // (2 * LANES), 3)),
            dma((4,)),
        ],
        compiler_params=pltpu.CompilerParams(
            collective_id=0, has_side_effects=True, vmem_limit_bytes=VMEM_BYTES
        ),
        name="self_forward",
    )(segments, padding, tokens, *weights, *prefix, memory, *mem_weights)


def self_backward_kernel(
    n,
    batches,
    base_in,
    do_in,
    sums_in,
    mkey_in,
    mvalue_in,
    wck_in,
    wcv_in,
    vecs_in,
    qx_in,
    kx_in,
    raw_in,
    pk_in,
    pv_in,
    pkt_in,
    ot_in,
    lse_in,
    wq_in,
    wk_in,
    wv_in,
    tg_ref,
    mgrad_ref,
    pkv_ref,
    vecs_ref,
    full_out,
    do_recv,
    qx,
    kx,
    raw,
    kt,
    values,
    dot,
    qdo,
    pk,
    pv,
    pkt,
    ot,
    stat,
    weights,
    dqt,
    dkv,
    g_send,
    g_recv,
    pre_ref,
    pre_all,
    pre_sum,
    pre_recv,
    sums_mine,
    sums_core,
    sums_x,
    sums_side,
    sums_z,
    full,
    mkey,
    mvalue,
    wck,
    wcv,
    mem_part,
    mem_side,
    mem_up,
    mem_down,
    vec_all,
    vec_sum,
    vec_y,
    vec_both,
    vec_z,
    product,
    base_ref,
    do_send_sem,
    do_recv_sem,
    g_send_sem,
    g_recv_sem,
    in_sem,
    send_sem,
    recv_sem,
):
    low = jnp.bfloat16
    f32 = jnp.float32
    me = lax.axis_index("seq")
    length, width = tg_ref.shape
    group = width // n
    heads = group // HD
    plane = 2 * length
    planes = n // 2
    step_rows = 256
    my_batch = lax.axis_index("batch")
    my_core = lax.rem(my_batch, 2)
    my_high = my_batch // 2
    highs = batches // 2
    my_plane = me // 2
    my_side = lax.rem(me, 2)
    beside = me + 1 - 2 * my_side
    used = [0]

    def numbers(count):
        used[0] += count
        return used[0] - count

    core_slot = numbers(2)
    x_slot = numbers(2 * highs)
    y_slot = numbers(3)
    z_slot = numbers(2 * planes)
    up_slot = numbers(planes)
    down_slot = numbers(planes)
    va_slot = numbers(batches)
    vb_slot = numbers(1)
    vc_slot = numbers(planes)
    pa_slot = numbers(batches)
    pb_slot = numbers(n)

    def send(source, target, first, peer_index, slot_index, axis, peer):
        return remote(
            source,
            target,
            send_sem.at[first + peer_index],
            recv_sem.at[first + slot_index],
            axis,
            peer,
        )

    half_rows = 2 * planes * highs * sums_z.shape[1]
    x_rows = half_rows // highs
    y_rows = x_rows // 2
    z_rows = y_rows // planes
    x_row = pl.multiple_of(my_high * x_rows, x_rows)
    y_row = pl.multiple_of(x_row + my_side * y_rows, y_rows)

    def part(row, count):
        return sums_mine.at[pl.ds(pl.multiple_of(row, count), count)]

    def reduce_core():
        return send(
            sums_in.at[1 - my_core], sums_core, core_slot, 0, 0, "batch", my_batch + 1 - 2 * my_core
        )

    def reduce_x(peer, slot):
        return send(
            part(peer * x_rows, x_rows),
            sums_x.at[slot],
            x_slot,
            peer,
            slot,
            "batch",
            2 * peer + my_core,
        )

    def reduce_y():
        return send(
            part(x_row + (1 - my_side) * y_rows, y_rows), sums_side, y_slot, 0, 0, "seq", beside
        )

    def reduce_z(peer, slot):
        return send(
            part(y_row + peer * z_rows, z_rows),
            sums_z.at[slot],
            z_slot,
            peer,
            slot,
            "seq",
            2 * peer + my_side,
        )

    def gather_z(peer, slot):
        piece = full.at[my_core, my_high, my_side, slot]
        return send(piece, piece, z_slot + planes, peer, slot, "seq", 2 * peer + my_side)

    def gather_y(side):
        piece = full.at[my_core, my_high, side]
        return send(piece, piece, y_slot + 1, 0, 0, "seq", beside)

    def gather_x(peer, slot):
        piece = full.at[my_core, slot]
        return send(piece, piece, x_slot + highs, peer, slot, "batch", 2 * peer + my_core)

    def gather_core(core):
        piece = full.at[core]
        return send(piece, piece, core_slot + 1, 0, 0, "batch", my_batch + 1 - 2 * my_core)

    def mem_across():
        return send(
            mem_part.at[:, 1 - my_side], mem_side, y_slot + 2, 0, 0, "seq", beside
        )

    def mem_hop(target, toward, peer=None):
        buffer, slot = (mem_up, up_slot) if toward > 0 else (mem_down, down_slot)
        return send(
            mem_part.at[target, my_side],
            buffer.at[target],
            slot,
            target,
            target,
            "seq",
            me + 2 * toward if peer is None else peer,
        )

    def mem_from(target, toward):
        return mem_hop(target, toward, me - 2 * toward)

    def mem_pass(toward):
        buffer = mem_up if toward > 0 else mem_down
        first = 0 if toward > 0 else planes - 1
        for target in range(planes):

            @pl.when((target - my_plane) * toward > 0)
            def _():
                @pl.when(my_plane != first)
                def _():
                    mem_from(target, toward).wait_recv()
                    mem_part[target, my_side] = (
                        mem_part[target, my_side].astype(f32) + buffer[target].astype(f32)
                    ).astype(low)

                mem_hop(target, toward).start()

    def mem_stage(at):
        pl.when(my_plane == at)(lambda: mem_pass(1))
        pl.when(my_plane == planes - 1 - at)(lambda: mem_pass(-1))

    def mem_end():
        value = mem_part[my_plane, my_side].astype(f32)
        mgrad_ref[...] = value.astype(low)

        @pl.when(my_plane > 0)
        def _():
            mem_from(my_plane, 1).wait_recv()
            mgrad_ref[...] = (mgrad_ref[...].astype(f32) + mem_up[my_plane].astype(f32)).astype(low)

        @pl.when(my_plane < planes - 1)
        def _():
            mem_from(my_plane, -1).wait_recv()
            mgrad_ref[...] = (
                mgrad_ref[...].astype(f32) + mem_down[my_plane].astype(f32)
            ).astype(low)

    def mem_drain():
        for target in range(planes):

            @pl.when(target > my_plane)
            def _():
                mem_hop(target, 1).wait_send()

            @pl.when(target < my_plane)
            def _():
                mem_hop(target, -1).wait_send()

    def vec_a(peer, slot):
        return send(vecs_in, vec_all.at[slot], va_slot, peer, slot, "batch", peer)

    def vec_b(side):
        return send(vec_sum, vec_y.at[side], vb_slot, 0, 0, "seq", beside)

    def vec_c(peer, slot):
        return send(vec_both, vec_z.at[slot], vc_slot, peer, slot, "seq", 2 * peer + my_side)

    def pre_a(peer, slot):
        return send(pre_ref, pre_all.at[slot], pa_slot, peer, slot, "batch", peer)

    def pre_b(peer, slot):
        return send(pre_sum, pre_recv.at[slot], pb_slot, peer, slot, "seq", peer)

    def do_copy(head, peer, slot):
        return remote(
            do_in.at[peer, head],
            do_recv.at[head, slot],
            do_send_sem.at[head, peer],
            do_recv_sem.at[head, slot],
            "seq",
            peer,
        )

    def q_copy(head, peer, slot):
        return remote(
            g_send.at[peer, head, 0],
            g_recv.at[0, slot, head],
            g_send_sem.at[0, head, peer],
            g_recv_sem.at[0, head, slot],
            "seq",
            peer,
        )

    def kv_copy(head, peer, slot):
        return remote(
            g_send.at[peer, head, pl.ds(1, 2)],
            g_recv.at[pl.ds(1, 2), slot, head],
            g_send_sem.at[1, head, peer],
            g_recv_sem.at[1, head, slot],
            "seq",
            peer,
        )

    def added(ref, size):
        value = ref[0].astype(f32)
        for other in range(1, size):
            value = value + ref[other].astype(f32)
        return value

    loads = [
        pltpu.make_async_copy(source, target, in_sem.at[index])
        for index, (source, target) in enumerate(
            (
                (raw_in, raw),
                (kx_in, kx),
                (pk_in, pk),
                (pv_in, pv),
                (pkt_in, pkt),
                (qx_in, qx),
                (ot_in, ot),
                (lse_in, stat),
                (sums_in.at[my_core], sums_mine),
                (vecs_in, vec_all.at[my_batch]),
                (mkey_in, mkey),
                (mvalue_in, mvalue),
                (wck_in, wck),
                (wcv_in, wcv),
                (base_in, base_ref),
                (wq_in, weights.at[0]),
                (wk_in, weights.at[1]),
                (wv_in, weights.at[2]),
            )
        )
    ]
    own_do = pltpu.make_async_copy(do_in.at[me], do_recv.at[:, me], in_sem.at[len(loads)])
    own_do.start()
    for load in loads:
        load.start()
    enter({"seq": n, "batch": batches})
    others(n, me, lambda peer: do_copy(0, peer, me).start())
    reduce_core().start()
    others(batches, my_batch, lambda peer: vec_a(peer, my_batch).start())
    dkv[...] = jnp.zeros_like(dkv)
    product[...] = jnp.zeros_like(product)
    pre_ref[...] = jnp.zeros_like(pre_ref)
    for load in loads[:14]:
        load.wait()
    own_do.wait()

    def turn(index, carry):
        head = index // n
        chunk = lax.rem(index, n)
        here = rows_of(chunk, length)
        kt[head, :, here] = raw[head, chunk, 1]
        values[head, here, :] = raw[head, chunk, 2].astype(f32).T.astype(low)
        return carry

    lax.fori_loop(0, heads * n, turn, 0)

    def memory_back(index, carry):
        here = rows_of(index, step_rows)
        value = dot_nt(mkey[...], wck[here, :]) + dot_nt(mvalue[...], wcv[here, :])
        mem_part[:, :, :, here] = value.astype(low).reshape(mem_part.shape[:3] + (step_rows,))
        return carry

    lax.fori_loop(0, width // step_rows, memory_back, 0)
    mem_across().start()

    def next_head(head):
        @pl.when(head + 1 < heads)
        def _():
            def move(peer):
                do_copy(head, peer, me).wait_send()
                do_copy(head + 1, peer, me).start()

            others(n, me, move)

    def arrive(head, which):
        for part in range(2):
            chunk = 2 * which + part

            @pl.when(chunk != me)
            def _():
                do_copy(head, chunk, chunk).wait_recv()

            grads = do_recv[head, chunk]
            dot[head, :, rows_of(chunk, length)] = grads
            grads = grads.astype(f32)
            query = raw[head, chunk, 0].astype(f32) * 0.125
            qdo[head, rows_of(chunk, length), :] = (
                jnp.concatenate([query, grads], axis=0).T.astype(low)
            )
            here = slice(part * length, (part + 1) * length)
            stat[which, head, 1:2, here] = jnp.sum(
                grads * ot[which, head, :HD, here], axis=0, keepdims=True
            )
        here = rows_of(which, plane)
        weight = jnp.exp(dot_nn(pk[head], qx[head, :, here]) - stat[which, head, 0:1, :])
        slope = weight * (dot_nn(pv[head], dot[head, :, here]) - stat[which, head, 1:2, :])
        both = jnp.concatenate([slope, weight], axis=0).astype(low)
        sums = dot_nn(both, qdo[head, here, :])
        pre_ref[head] += jnp.where(
            head_lanes((PREFIX_ROWS, 2 * HD), 0), sums[:PREFIX_ROWS], sums[PREFIX_ROWS:]
        )
        slope = slope.astype(low)
        dqt[which, head] = dot_nn(pkt[head], slope)

    def plus(first, second):
        return (first.astype(f32) + second.astype(f32)).astype(low)

    def sum_one():
        reduce_core().wait_recv()
        sums_mine[...] = plus(sums_mine[...], sums_core[...])
        others(highs, my_high, lambda peer: reduce_x(peer, my_high).start())

    def sum_two():
        here = pl.ds(x_row, x_rows)
        others(highs, my_high, lambda peer: reduce_x(peer, peer).wait_recv())
        sums_x[my_high] = sums_mine[here]
        sums_mine[here] = added(sums_x, highs).astype(low)
        reduce_y().start()

    def sum_three():
        here = pl.ds(y_row, y_rows)
        reduce_y().wait_recv()
        sums_mine[here] = plus(sums_mine[here], sums_side[...])
        others(planes, my_plane, lambda peer: reduce_z(peer, my_plane).start())

    def sum_four():
        here = pl.ds(pl.multiple_of(y_row + my_plane * z_rows, z_rows), z_rows)
        others(planes, my_plane, lambda peer: reduce_z(peer, peer).wait_recv())
        sums_z[my_plane] = sums_mine[here]
        full[my_core, my_high, my_side, my_plane] = added(sums_z, planes).astype(low)
        others(planes, my_plane, lambda peer: gather_z(peer, my_plane).start())

    def sum_five():
        others(planes, my_plane, lambda peer: gather_z(peer, peer).wait_recv())
        gather_y(my_side).start()

    def sum_six():
        gather_y(1 - my_side).wait_recv()
        others(highs, my_high, lambda peer: gather_x(peer, my_high).start())

    def sum_seven():
        others(highs, my_high, lambda peer: gather_x(peer, peer).wait_recv())
        gather_core(my_core).start()

    def sum_end():
        gather_core(1 - my_core).wait_recv()
        save_full.start()

    def vec_one():
        others(batches, my_batch, lambda peer: vec_a(peer, peer).wait_recv())
        vec_sum[...] = added(vec_all, batches)
        vec_b(my_side).start()
        vec_y[my_side] = vec_sum[...]

    def vec_two():
        vec_b(1 - my_side).wait_recv()
        value = (vec_y[0] + vec_y[1]).astype(f32)
        vec_both[...] = jnp.concatenate(
            [value[:, : width // 2], value[:, width // 2 :]], axis=0
        ).astype(low)
        others(planes, my_plane, lambda peer: vec_c(peer, my_plane).start())
        vec_z[my_plane] = vec_both[...]

    def vec_end():
        others(planes, my_plane, lambda peer: vec_c(peer, peer).wait_recv())
        value = added(vec_z, planes)
        vecs_ref[:, : width // 2] = value[:8]
        vecs_ref[:, width // 2 :] = value[8:]

    def mem_one():
        mem_across().wait_recv()
        mem_part[:, my_side] = plus(mem_part[:, my_side], mem_side[...])

    def stage_pa():
        others(batches, my_batch, lambda peer: pre_a(peer, my_batch).start())
        pre_all[my_batch] = pre_ref[...]

    def stage_pb():
        others(batches, my_batch, lambda peer: pre_a(peer, peer).wait_recv())
        pre_sum[...] = added(pre_all, batches).astype(low)
        others(n, me, lambda peer: pre_b(peer, me).start())
        pre_recv[me] = pre_sum[...]

    save_full = pltpu.make_async_copy(full, full_out, in_sem.at[0])

    def pair_part(head, upper, lower, first, count, diagonal):
        keys = span_of(lower * plane + first, count)
        here = span_of(upper * plane + first, plane - first)
        at = slice(first, plane)
        scores = dot_nn(kx[head, keys, :], qx[head, :, here])
        slope = dot_nn(values[head, keys, :], dot[head, :, here]) - stat[upper, head, 1:2, at]
        weight = jnp.exp(scores - stat[upper, head, 0:1, at])
        if diagonal:
            key_at = lax.broadcasted_iota(jnp.int32, scores.shape, 0)
            query_at = lax.broadcasted_iota(jnp.int32, scores.shape, 1)
            weight = jnp.where(key_at <= query_at, weight, 0.0)
        both = jnp.concatenate([(weight * slope).astype(low), weight.astype(low)], axis=0)
        sums = dot_nn(both, qdo[head, here, :])
        dkv[head, keys, :] += jnp.where(
            head_lanes((count, 2 * HD), 0), sums[:count], sums[count:]
        )
        dqt[upper, head, :, at] += dot_nn(kt[head, :, keys], both[:count])

    def pair(head, upper, lower, diagonal):
        if diagonal:
            pair_part(head, upper, lower, 0, length, True)
            pair_part(head, upper, lower, length, length, True)
        else:
            pair_part(head, upper, lower, 0, plane, False)

    def hand_queries(head, which):
        for part in range(2):
            chunk = 2 * which + part
            g_send[chunk, head, 0] = (
                dqt[which, head, :, part * length : (part + 1) * length] * 0.125
            ).astype(low)

            @pl.when(chunk != me)
            def _():
                q_copy(head, chunk, me).start()

            @pl.when(chunk == me)
            def _():
                g_recv[0, me, head] = g_send[chunk, head, 0]

    def hand_keys(head, which):
        for part in range(2):
            chunk = 2 * which + part
            turned = dkv[head, rows_of(chunk, length), :].T.astype(low)
            g_send[chunk, head, 1] = turned[:HD]
            g_send[chunk, head, 2] = turned[HD:]

            @pl.when(chunk != me)
            def _():
                kv_copy(head, chunk, me).start()

            @pl.when(chunk == me)
            def _():
                g_recv[pl.ds(1, 2), me, head] = g_send[chunk, head, pl.ds(1, 2)]

    rising = my_plane >= planes // 2
    total = heads * planes * (planes + 1) // 2
    hooks = [
        (2, sum_one),
        (3, mem_one),
        (4, lambda: mem_stage(0)),
        (5, sum_two),
        (5, vec_one),
        (7, sum_three),
        (8, vec_two),
        (9, sum_four),
        (10, sum_five),
        (12, sum_six),
        (15, sum_seven),
        (16, vec_end),
    ] + [(4 + 3 * at, functools.partial(mem_stage, at)) for at in range(1, planes - 1)]
    final = total - planes * (planes + 1) // 2
    hooks += [(final + planes + 1, stage_pa), (final + 2 * planes - 1, stage_pb)]

    def hook(pairs):
        for number, body in sorted(hooks, key=lambda item: item[0]):
            pl.when(pairs == number)(body)


    def stage(index, carry):
        head = index // planes
        step = lax.rem(index, planes)
        here = jnp.where(rising, step, planes - 1 - step)

        @pl.when((step == 0) | ((step == 1) & jnp.logical_not(rising)))
        def _():
            @pl.when(rising | (step == 0))
            def _():
                arrive(head, here)

            @pl.when(jnp.logical_not(rising) & (step == 1))
            def _():
                next_head(head)

                def rest(which, inner):
                    arrive(head, planes - 2 - which)
                    return inner

                lax.fori_loop(0, planes - 1, rest, 0)

        begun = head * (planes * (planes + 1) // 2) + step * planes - step * (step - 1) // 2
        hook(begun)
        pair(head, here, here, True)

        @pl.when(rising)
        def _():
            hand_queries(head, here)

        @pl.when(jnp.logical_not(rising))
        def _():
            hand_keys(head, here)

        def far(at, inner):
            there = jnp.where(rising, here + 1 + at, here - 1 - at)

            @pl.when(rising & (step == 0))
            def _():
                arrive(head, there)

            hook(begun + 1 + at)
            pair(head, jnp.maximum(here, there), jnp.minimum(here, there), False)
            return inner

        lax.fori_loop(0, planes - 1 - step, far, 0)

        @pl.when(rising & (step == 0))
        def _():
            next_head(head)

        @pl.when(rising)
        def _():
            hand_keys(head, here)

        @pl.when(jnp.logical_not(rising))
        def _():
            hand_queries(head, here)

        return carry

    lax.fori_loop(0, heads * planes, stage, 0)
    sum_end()
    mem_end()
    for load in loads[14:]:
        load.wait()

    def gathered(peer):
        for head in range(heads):
            q_copy(head, peer, peer).wait_recv()
            kv_copy(head, peer, peer).wait_recv()

    half = width // 2

    def gather_plane(step, carry):
        which = lax.rem(my_plane + step, planes)
        for part in range(2):
            peer = 2 * which + part

            @pl.when(peer != me)
            def _():
                gathered(peer)

        columns = rows_of(which, 2 * group)
        for part in range(2):
            here = slice(part * half, (part + 1) * half)
            value = product[here, :]
            for kind in range(3):
                grads = g_recv[kind, pl.ds(2 * which, 2)].reshape(2 * group, length)
                value = value + dot_nn(weights[kind, here, columns], grads)
            product[here, :] = value
        return carry

    lax.fori_loop(0, planes, gather_plane, 0)
    tile = 256
    for index in range(width // tile):
        here = slice(index * tile, (index + 1) * tile)
        tg_ref[:, here] = (base_ref[:, here] + product[here, :].T).astype(low)
    for other in range(n):

        @pl.when(other != me)
        def _():
            pre_b(other, other).wait_recv()

        value = pre_recv[other].astype(f32)
        for which in range(2):
            pkv_ref[:, which * width + other * group : which * width + (other + 1) * group] = (
                jnp.concatenate(
                    [value[head, :, which * HD : (which + 1) * HD] for head in range(heads)], axis=1
                )
            )

    def drain(peer):
        do_copy(heads - 1, peer, me).wait_send()
        pre_b(peer, me).wait_send()
        for head in range(heads):
            q_copy(head, peer, me).wait_send()
            kv_copy(head, peer, me).wait_send()

    others(n, me, drain)
    others(batches, my_batch, lambda peer: pre_a(peer, my_batch).wait_send())
    others(batches, my_batch, lambda peer: vec_a(peer, my_batch).wait_send())
    reduce_core().wait_send()
    others(highs, my_high, lambda peer: reduce_x(peer, my_high).wait_send())
    reduce_y().wait_send()
    others(planes, my_plane, lambda peer: reduce_z(peer, my_plane).wait_send())
    others(planes, my_plane, lambda peer: gather_z(peer, my_plane).wait_send())
    gather_y(my_side).wait_send()
    others(highs, my_high, lambda peer: gather_x(peer, my_high).wait_send())
    gather_core(my_core).wait_send()
    mem_across().wait_send()
    mem_drain()
    others(planes, my_plane, lambda peer: vec_c(peer, my_plane).wait_send())
    vec_b(my_side).wait_send()
    save_full.wait()


def self_backward(
    n, batches, first_grad, out_grad, sums, mem_grads, mem_weights, vecs, saved, weights
):
    length, width = first_grad.shape
    group = width // n
    heads = group // HD
    whole = n * length
    planes = n // 2
    low = jnp.bfloat16
    f32 = jnp.float32
    vmem = pl.BlockSpec(memory_space=pltpu.VMEM)
    anywhere = pl.BlockSpec(memory_space=pl.ANY)
    dma = pltpu.SemaphoreType.DMA
    sum_rows = sums.shape[0] // (n * batches)
    mem_len = mem_grads[0].shape[0]
    mem_rows = mem_len // n
    mem_part = pltpu.VMEM((planes, mem_rows, width), low)
    mem_low = pltpu.VMEM((mem_len, width), low)
    square = pltpu.VMEM((width, width), low)
    vec = pltpu.VMEM((8, width), f32)
    copies = 6 + 2 * (batches // 2) + 5 * planes + 2 * batches + n
    qx, kx, raw, pk, pv, pkt, ot, stat = (pltpu.VMEM(value.shape, value.dtype) for value in saved)
    return pl.pallas_call(
        functools.partial(self_backward_kernel, n, batches),
        out_shape=(
            jax.ShapeDtypeStruct((length, width), low),
            jax.ShapeDtypeStruct((mem_rows, width), low),
            jax.ShapeDtypeStruct((PREFIX_ROWS, 2 * width), f32),
            jax.ShapeDtypeStruct((8, width), f32),
            jax.ShapeDtypeStruct((2, batches // 2, 2, planes, sum_rows, LANES), low),
        ),
        in_specs=[anywhere] * 19,
        out_specs=(vmem, vmem, vmem, vmem, anywhere),
        scratch_shapes=[
            pltpu.VMEM((heads, n, HD, length), low),
            qx,
            kx,
            raw,
            pltpu.VMEM((heads, HD, whole), low),
            pltpu.VMEM((heads, whole, HD), low),
            pltpu.VMEM((heads, HD, whole), low),
            pltpu.VMEM((heads, whole, 2 * HD), low),
            pk,
            pv,
            pkt,
            ot,
            stat,
            pltpu.VMEM((3, width, width), low),
            pltpu.VMEM((planes, heads, HD, 2 * length), f32),
            pltpu.VMEM((heads, whole, 2 * HD), f32),
            pltpu.VMEM((n, heads, 3, HD, length), low),
            pltpu.VMEM((3, n, heads, HD, length), low),
            pltpu.VMEM((heads, PREFIX_ROWS, 2 * HD), f32),
            pltpu.VMEM((batches, heads, PREFIX_ROWS, 2 * HD), f32),
            pltpu.VMEM((heads, PREFIX_ROWS, 2 * HD), low),
            pltpu.VMEM((n, heads, PREFIX_ROWS, 2 * HD), low),
            pltpu.VMEM((sums.shape[0] // 2, LANES), low),
            pltpu.VMEM((sums.shape[0] // 2, LANES), low),
            pltpu.VMEM((batches // 2, sums.shape[0] // batches, LANES), low),
            pltpu.VMEM((planes * sum_rows, LANES), low),
            pltpu.VMEM((planes, sum_rows, LANES), low),
            pltpu.VMEM((2, batches // 2, 2, planes, sum_rows, LANES), low),
            mem_low,
            mem_low,
            square,
            square,
            pltpu.VMEM((planes, 2, mem_rows, width), low),
            mem_part,
            mem_part,
            mem_part,
            pltpu.VMEM((batches, 8, width), f32),
            vec,
            pltpu.VMEM((2, 8, width), f32),
            pltpu.VMEM((16, width // 2), low),
            pltpu.VMEM((planes, 16, width // 2), low),
            pltpu.VMEM((width, length), f32),
            pltpu.VMEM((length, width), f32),
            dma((heads, n)),
            dma((heads, n)),
            dma((2, heads, n)),
            dma((2, heads, n)),
            dma((19,)),
            dma((copies,)),
            dma((copies,)),
        ],
        compiler_params=pltpu.CompilerParams(
            collective_id=1, has_side_effects=True, vmem_limit_bytes=VMEM_BYTES
        ),
        name="self_backward",
    )(
        first_grad,
        out_grad,
        sums.reshape(2, -1, LANES),
        *mem_grads,
        *mem_weights,
        vecs,
        *saved,
        *weights,
    )


def both_parts(value):
    high = value.astype(jnp.bfloat16).astype(jnp.float32)
    return jnp.concatenate([high, value - high], axis=0).astype(jnp.bfloat16)


def finish_kernel(
    full_in,
    vecs_ref,
    pkv_ref,
    emb_ref,
    first_in,
    fbias_ref,
    second_in,
    token_in,
    mem_in,
    embed_out,
    first_out,
    fbias_out,
    second_out,
    sbias_out,
    down_out,
    dbias_out,
    raise_out,
    rbias_out,
    gain_out,
    shift_out,
    token_out,
    mem_out,
    full_ref,
    first_ref,
    second_ref,
    first_grad,
    second_grad,
    down_grad,
    raise_grad,
    emb,
    hidden,
    out_sem,
    in_sem,
):
    f32 = jnp.float32
    low = jnp.bfloat16
    width = emb_ref.shape[1]
    down = dbias_out.shape[1]
    count = emb_ref.shape[0]
    first = down * width // LANES
    loads = [
        pltpu.make_async_copy(source, target, in_sem.at[index])
        for index, (source, target) in enumerate(
            (
                (full_in.at[first:], full_ref.at[first:]),
                (full_in.at[:first], full_ref.at[:first]),
                (first_in, first_ref),
                (second_in, second_ref),
            )
        )
    ]
    for load in loads:
        load.start()
    saves = []

    def save(source, target, rows=None):
        if rows is not None:
            source, target = source.at[rows], target.at[rows]
        copy = pltpu.make_async_copy(source, target, out_sem.at[len(saves)])
        copy.start()
        saves.append(copy)

    save(token_in, token_out)
    save(mem_in, mem_out)
    loads[0].wait()
    for index in range(width // LANES):
        raise_grad[:, index * LANES : (index + 1) * LANES] = full_ref[
            first + index * down : first + (index + 1) * down, :
        ].astype(f32)
    save(raise_grad, raise_out)
    loads[1].wait()
    for index in range(down // LANES):
        down_grad[:, index * LANES : (index + 1) * LANES] = full_ref[
            index * width : (index + 1) * width, :
        ].astype(f32)
    save(down_grad, down_out)
    loads[2].wait()
    emb[...] = jnp.zeros_like(emb)
    emb[:count, :] = emb_ref[...].astype(f32)
    emb_low = emb[...].astype(low)
    row = lax.broadcasted_iota(jnp.int32, hidden.shape, 0)
    hidden[...] = jnp.where(
        row < count, jnp.tanh(dot_nn(emb_low, first_ref[...]) + fbias_ref[...]), 0.0
    )
    value = hidden[...]
    prefix = pkv_ref[...]
    parts = both_parts(prefix)
    hidden_twice = jnp.concatenate([value, value], axis=0).T.astype(low)
    tile = 128
    for index in range(second_grad.shape[0] // tile):
        here = slice(index * tile, (index + 1) * tile)
        second_grad[here, :] = dot_nn(hidden_twice[here, :], parts)
        save(second_grad, second_out, here)
    sbias_out[...] = jnp.sum(prefix, axis=0, keepdims=True)
    loads[3].wait()
    grad = dot_nt(parts, second_ref[...])
    grad = (grad[:PREFIX_ROWS] + grad[PREFIX_ROWS:]) * (1.0 - value * value)
    fbias_out[...] = jnp.sum(grad, axis=0, keepdims=True)
    parts = both_parts(grad)
    emb_twice = jnp.concatenate([emb[...], emb[...]], axis=0).T.astype(low)
    first_grad[...] = dot_nn(emb_twice, parts)
    save(first_grad, first_out)
    back = dot_nt(parts, first_ref[...])
    embed_out[...] = (back[:PREFIX_ROWS] + back[PREFIX_ROWS:])[:count, :]
    rbias_out[...] = vecs_ref[0:1, :]
    dbias_out[...] = vecs_ref[1:2, :down]
    gain_out[...] = vecs_ref[2:5, :]
    shift_out[...] = vecs_ref[5:8, :]
    for copy in saves:
        copy.wait()


def finish(full, vecs, prefix_grad, embed, first, first_bias, second, down, token_grad, memory_grad):
    f32 = jnp.float32
    count, width = embed.shape
    hidden = first.shape[1]
    vmem = pl.BlockSpec(memory_space=pltpu.VMEM)
    anywhere = pl.BlockSpec(memory_space=pl.ANY)
    shapes = (
        (count, width),
        (width, hidden),
        (1, hidden),
        (hidden, 2 * width),
        (1, 2 * width),
        (width, down),
        (1, down),
        (down, width),
        (1, width),
        (3, width),
        (3, width),
    )
    return pl.pallas_call(
        finish_kernel,
        out_shape=tuple(jax.ShapeDtypeStruct(shape, f32) for shape in shapes)
        + tuple(
            jax.ShapeDtypeStruct(value.shape, value.dtype) for value in (token_grad, memory_grad)
        ),
        in_specs=[anywhere, vmem, vmem, vmem, anywhere, vmem, anywhere, anywhere, anywhere],
        out_specs=(
            vmem,
            anywhere,
            vmem,
            anywhere,
            vmem,
            anywhere,
            vmem,
            anywhere,
            vmem,
            vmem,
            vmem,
            anywhere,
            anywhere,
        ),
        scratch_shapes=[
            pltpu.VMEM(full.shape, jnp.bfloat16),
            pltpu.VMEM(first.shape, jnp.bfloat16),
            pltpu.VMEM(second.shape, jnp.bfloat16),
            pltpu.VMEM((width, hidden), f32),
            pltpu.VMEM((hidden, 2 * width), f32),
            pltpu.VMEM((width, down), f32),
            pltpu.VMEM((down, width), f32),
            pltpu.VMEM((PREFIX_ROWS, width), f32),
            pltpu.VMEM((PREFIX_ROWS, hidden), f32),
            pltpu.SemaphoreType.DMA((5 + hidden // 128,)),
            pltpu.SemaphoreType.DMA((4,)),
        ],
        compiler_params=pltpu.CompilerParams(vmem_limit_bytes=VMEM_BYTES),
        name="finish",
    )(full, vecs, prefix_grad, embed, first, first_bias, second, token_grad, memory_grad)


def gelu_pair(value):
    size = jnp.abs(value)
    step = 1.0 / (1.0 + (0.3275911 * 0.7071067811865476) * size)
    bell = jnp.exp(-0.5 * value * value)
    poly = step * (
        0.127414796
        + step
        * (-0.142248368 + step * (0.7107068705 + step * (-0.7265760135 + step * 0.5307027145)))
    )
    act = jnp.maximum(value, 0.0) - size * (poly * bell)
    turn = bell * (0.3989422804014327 * size - poly)
    return act, jnp.where(value >= 0.0, 1.0 + turn, -turn)


def normed(value):
    center = jnp.mean(value, axis=-1, keepdims=True)
    centered = value - center
    scale = lax.rsqrt(jnp.mean(centered * centered, axis=-1, keepdims=True) + norm_eps)
    return centered * scale, scale


def norm_back(grad, scale, unit):
    return scale * (
        grad
        - jnp.mean(grad, axis=-1, keepdims=True)
        - unit * jnp.mean(grad * unit, axis=-1, keepdims=True)
    )


def middle_kernel(
    tok_in,
    att_in,
    cot_in,
    mkey_in,
    mvalue_in,
    gain_ref,
    shift_ref,
    dbias_ref,
    rbias_ref,
    wo_in,
    wcq_in,
    wco_in,
    wd_in,
    wr_in,
    win_in,
    wout_in,
    layer_out,
    fgrad_ref,
    ograd_ref,
    mkey_out,
    mvalue_out,
    sums_out,
    vecs_ref,
    tok_ref,
    att_ref,
    cot_ref,
    mkey_ref,
    mvalue_ref,
    out_ref,
    sums_ref,
    wo,
    wcq,
    wco,
    wd,
    wr,
    win,
    wout,
    unit_one,
    unit_two,
    work,
    total,
    scale_one,
    scale_two,
    low_one,
    low_two,
    low_three,
    query,
    crossed,
    weights,
    slopes,
    down_act,
    down_slope,
    down_grad,
    load_sem,
    win_sem,
    wout_sem,
    out_sem,
):
    length, width = tok_ref.shape
    tile = win.shape[2]
    tiles = win_in.shape[1] // tile
    rows_step = 128
    low = jnp.bfloat16
    f32 = jnp.float32

    sources = (
        att_in,
        wo_in,
        tok_in,
        wcq_in,
        mkey_in,
        mvalue_in,
        wco_in,
        wd_in,
        wr_in,
        cot_in,
    )
    targets = (att_ref, wo, tok_ref, wcq, mkey_ref, mvalue_ref, wco, wd, wr, cot_ref)
    loads = [
        pltpu.make_async_copy(source, target, load_sem.at[index])
        for index, (source, target) in enumerate(zip(sources, targets))
    ]

    def win_load(which):
        slot = lax.rem(which, 2)
        return pltpu.make_async_copy(
            win_in.at[:, rows_of(which, tile)], win.at[slot], win_sem.at[slot]
        )

    def wout_load(which):
        slot = lax.rem(which, 2)
        return pltpu.make_async_copy(
            wout_in.at[rows_of(which, tile), :], wout.at[slot], wout_sem.at[slot]
        )

    for load in loads[:7]:
        load.start()
    for which in range(2):
        win_load(which).start()
        wout_load(which).start()
    for load in loads[7:]:
        load.start()

    def by_columns(extent, step, body):
        def one(index, carry):
            body(pl.ds(pl.multiple_of(index * step, step), step))
            return carry

        lax.fori_loop(0, extent // step, one, 0)

    def by_rows(body, init=0):
        def one(index, carry):
            return body(rows_of(index, rows_step), carry)

        return lax.fori_loop(0, length // rows_step, one, init)

    cols = 512
    half = width // 2

    for load in loads[:3]:
        load.wait()

    def project_out(here):
        work[:, here] = tok_ref[:, here].astype(f32) + dot_nn(att_ref[...], wo[:, here])

    by_columns(width, cols, project_out)

    def first_norm(here, carry):
        unit, scale = normed(work[here, :])
        unit_one[here, :] = unit
        scale_one[here, :] = scale
        value = unit * gain_ref[0:1, :] + shift_ref[0:1, :]
        work[here, :] = value
        low_one[here, :] = value.astype(low)
        return carry

    by_rows(first_norm)

    loads[3].wait()

    def project_query(here):
        query[:, here] = dot_nn(low_one[...], wcq[:, here]).astype(low)

    by_columns(width, cols, project_query)
    per_block = LANES // HD

    def head_queries(here, head):
        both = query[:, here].astype(f32) * 0.125
        return jnp.where(head_lanes(both.shape, head), both, 0.0).astype(low)

    def cross_forward(block):
        here = rows_of(block, LANES)
        keys = mkey_ref[:, here]
        values = mvalue_ref[:, here].astype(f32).T.astype(low)
        outs = []
        for head in range(per_block):
            scores = dot_nt(keys, head_queries(here, head))
            raised = jnp.exp(scores - jnp.max(scores, axis=0, keepdims=True))
            share = 1.0 / jnp.sum(raised, axis=0, keepdims=True)
            weight = (raised * share).astype(low)
            weights[block * per_block + head] = weight
            outs.append(dot_nn(values[head * HD : (head + 1) * HD, :], weight))
        crossed[:, here] = jnp.concatenate(outs, axis=0).T.astype(low)

    loads[4].wait()
    loads[5].wait()

    def cross_forward_both(step, carry):
        cross_forward(2 * step)
        cross_forward(2 * step + 1)
        return carry

    lax.fori_loop(0, width // LANES // 2, cross_forward_both, 0)

    loads[6].wait()

    def project_crossed(here):
        work[:, here] += dot_nn(crossed[...], wco[:, here])

    by_columns(width, cols, project_crossed)

    def second_norm(here, carry):
        unit, scale = normed(work[here, :])
        unit_two[here, :] = unit
        scale_two[here, :] = scale
        value = unit * gain_ref[1:2, :] + shift_ref[1:2, :]
        work[here, :] = value
        low_two[here, :] = value.astype(low)
        return carry

    by_rows(second_norm)

    total[...] = jnp.zeros_like(total)

    def feed_forward(step, carry):
        for slot in range(2):
            win_load(2 * step + slot).wait()
            wout_load(2 * step + slot).wait()
        pres = [dot_nn(low_two[...], win[slot]) for slot in range(2)]
        parts = []
        for slot in range(2):
            act, slope = gelu_pair(pres[slot])
            slopes[:, rows_of(2 * step + slot, tile)] = slope.astype(low)
            parts.append(dot_nn(act.astype(low), wout[slot]))
        total[...] += parts[0] + parts[1]

        @pl.when(step + 1 < tiles // 2)
        def _():
            for slot in range(2):
                win_load(2 * step + 2 + slot).start()
                wout_load(2 * step + 2 + slot).start()

        return carry

    lax.fori_loop(0, tiles // 2, feed_forward, 0)
    loads[7].wait()
    loads[8].wait()
    loads[9].wait()
    act, slope = gelu_pair(dot_nn(low_two[...], wd[...]) + dbias_ref[...])
    down_act[...] = act.astype(low)
    down_slope[...] = slope.astype(low)

    def project_raise(here):
        work[:, here] += total[:, here] + 4.0 * (
            dot_nn(down_act[...], wr[:, here]) + rbias_ref[:, here]
        )

    by_columns(width, cols, project_raise)
    nothing = jnp.zeros((1, width), f32)

    def third_norm(here, carry):
        gain_sum, shift_sum, bias_sum = carry
        unit, scale = normed(work[here, :])
        gain = gain_ref[2:3, :]
        out_ref[here, :] = (unit * gain + shift_ref[2:3, :]).astype(low)
        grad = cot_ref[here, :].astype(f32)
        back = norm_back(grad * gain, scale, unit)
        total[here, :] = back
        back_low = back.astype(low)
        low_three[here, :] = back_low
        return (
            gain_sum + jnp.sum(grad * unit, axis=0, keepdims=True),
            shift_sum + jnp.sum(grad, axis=0, keepdims=True),
            bias_sum + jnp.sum(back_low.astype(f32), axis=0, keepdims=True),
        )

    gain_three, shift_three, bias_sum = by_rows(third_norm, (nothing, nothing, nothing))
    saves = []

    def save(source, target):
        copy = pltpu.make_async_copy(source, target, out_sem.at[len(saves)])
        copy.start()
        saves.append(copy)

    save(out_ref, layer_out)
    vecs_ref[0:1, :] = 4.0 * bias_sum

    back = 4.0 * dot_nt(low_three[...], wr[...]) * down_slope[...].astype(f32)
    back_low = back.astype(low)
    down_grad[...] = back_low
    vecs_ref[1:2, :] = jnp.concatenate(
        [
            jnp.sum(back_low.astype(f32), axis=0, keepdims=True),
            jnp.zeros((1, width - wd.shape[1]), f32),
        ],
        axis=1,
    )
    down = wd.shape[1]
    raise_sum = 4.0 * dot_tn(down_act[...], low_three[...])
    for index in range(width // LANES):
        sums_ref[pl.ds(down * width // LANES + index * down, down), :] = raise_sum[
            :, index * LANES : (index + 1) * LANES
        ].astype(low)
    down_sum = dot_tn(low_two[...], down_grad[...])
    for index in range(down // LANES):
        sums_ref[index * width : (index + 1) * width, :] = down_sum[
            :, index * LANES : (index + 1) * LANES
        ].astype(low)

    save(sums_ref, sums_out)

    def feed_backward(step, carry):
        which = tiles - 1 - step
        slot = lax.rem(which, 2)
        here = rows_of(which, tile)

        @pl.when(which < tiles - 2)
        def _():
            wout_load(which).wait()
            win_load(which).wait()

        grad = dot_nt(low_three[...], wout[slot]) * slopes[:, here].astype(f32)
        total[...] += dot_nt(grad.astype(low), win[slot])

        @pl.when(which >= 2)
        def _():
            win_load(which - 2).start()
            wout_load(which - 2).start()

        return carry

    lax.fori_loop(0, tiles, feed_backward, 0)

    def down_back(here):
        total[:, here] += dot_nt(down_grad[...], wd[here, :])

    by_columns(width, cols, down_back)

    def second_back(here, carry):
        gain_sum, shift_sum = carry
        grad = total[here, :]
        unit = unit_two[here, :]
        back = norm_back(grad * gain_ref[1:2, :], scale_two[here, :], unit)
        total[here, :] = back
        low_one[here, :] = back.astype(low)
        return (
            gain_sum + jnp.sum(grad * unit, axis=0, keepdims=True),
            shift_sum + jnp.sum(grad, axis=0, keepdims=True),
        )

    gain_two, shift_two = by_rows(second_back, (nothing, nothing))

    def crossed_back(here):
        crossed[:, here] = dot_nt(low_one[...], wco[here, :]).astype(low)

    by_columns(width, cols, crossed_back)

    def cross_backward(block):
        here = rows_of(block, LANES)
        values = mvalue_ref[:, here]
        keys = mkey_ref[:, here].astype(f32).T.astype(low)
        grads = crossed[:, here].astype(f32)
        outs = []
        key_sum = None
        for head in range(per_block):
            grad = jnp.where(head_lanes(grads.shape, head), grads, 0.0).astype(low)
            weight_low = weights[block * per_block + head]
            weight = weight_low.astype(f32)
            slope = dot_nt(values, grad)
            slope = weight * (slope - jnp.sum(weight * slope, axis=0, keepdims=True))
            slope = slope.astype(low)
            key_part = dot_nn(slope, head_queries(here, head))
            value_part = dot_nn(weight_low, grad)
            if key_sum is None:
                key_sum, value_sum = key_part, value_part
            else:
                key_sum, value_sum = key_sum + key_part, value_sum + value_part
            outs.append(dot_nn(keys[head * HD : (head + 1) * HD, :], slope))
        mkey_ref[:, here] = key_sum.astype(low)
        mvalue_ref[:, here] = value_sum.astype(low)
        query[:, here] = (jnp.concatenate(outs, axis=0) * 0.125).T.astype(low)

    def cross_backward_both(step, carry):
        cross_backward(2 * step)
        cross_backward(2 * step + 1)
        return carry

    lax.fori_loop(0, width // LANES // 2, cross_backward_both, 0)
    save(mkey_ref, mkey_out)
    save(mvalue_ref, mvalue_out)

    def query_back(here):
        total[:, here] += dot_nt(query[...], wcq[here, :])

    by_columns(width, cols, query_back)

    def first_back(here, carry):
        gain_sum, shift_sum = carry
        grad = total[here, :]
        unit = unit_one[here, :]
        back = norm_back(grad * gain_ref[0:1, :], scale_one[here, :], unit)
        fgrad_ref[here, :] = back
        low_one[here, :] = back.astype(low)
        return (
            gain_sum + jnp.sum(grad * unit, axis=0, keepdims=True),
            shift_sum + jnp.sum(grad, axis=0, keepdims=True),
        )

    gain_one, shift_one = by_rows(first_back, (nothing, nothing))

    def out_back(here):
        ograd_ref[here, :] = dot_nt(low_one[...], wo[here, :]).T.astype(low)

    by_columns(width, cols, out_back)
    for index, vector in enumerate(
        (gain_one, gain_two, gain_three, shift_one, shift_two, shift_three)
    ):
        vecs_ref[2 + index : 3 + index, :] = vector
    for copy in saves:
        copy.wait()


def middle(
    tokens, attended, cotangent, mem_key, mem_value, gains, shifts, down_bias, raise_bias, weights
):
    length, width = tokens.shape
    mem_len = mem_key.shape[0]
    down = weights[3].shape[1]
    feed = weights[5].shape[1]
    tile = 512 if mem_len <= 512 else 128
    low = jnp.bfloat16
    f32 = jnp.float32
    vmem = pl.BlockSpec(memory_space=pltpu.VMEM)
    anywhere = pl.BlockSpec(memory_space=pl.ANY)
    square = pltpu.VMEM((width, width), low)
    wide = pltpu.VMEM((length, width), f32)
    narrow = pltpu.VMEM((length, width), low)
    return pl.pallas_call(
        middle_kernel,
        out_shape=(
            jax.ShapeDtypeStruct((length, width), low),
            jax.ShapeDtypeStruct((length, width), f32),
            jax.ShapeDtypeStruct((width, length), low),
            jax.ShapeDtypeStruct((mem_len, width), low),
            jax.ShapeDtypeStruct((mem_len, width), low),
            jax.ShapeDtypeStruct((2 * down * width // LANES, LANES), low),
            jax.ShapeDtypeStruct((8, width), f32),
        ),
        in_specs=[anywhere] * 5 + [vmem] * 4 + [anywhere] * 7,
        out_specs=(anywhere, vmem, vmem, anywhere, anywhere, anywhere, vmem),
        scratch_shapes=[
            narrow,
            narrow,
            narrow,
            pltpu.VMEM((mem_len, width), low),
            pltpu.VMEM((mem_len, width), low),
            narrow,
            pltpu.VMEM((2 * down * width // LANES, LANES), low),
            square,
            square,
            square,
            pltpu.VMEM((width, down), low),
            pltpu.VMEM((down, width), low),
            pltpu.VMEM((2, width, tile), low),
            pltpu.VMEM((2, tile, width), low),
            wide,
            wide,
            wide,
            wide,
            pltpu.VMEM((length, 1), f32),
            pltpu.VMEM((length, 1), f32),
            narrow,
            narrow,
            narrow,
            narrow,
            narrow,
            pltpu.VMEM((H, mem_len, length), low),
            pltpu.VMEM((length, feed), low),
            pltpu.VMEM((length, down), low),
            pltpu.VMEM((length, down), low),
            pltpu.VMEM((length, down), low),
            pltpu.SemaphoreType.DMA((10,)),
            pltpu.SemaphoreType.DMA((2,)),
            pltpu.SemaphoreType.DMA((2,)),
            pltpu.SemaphoreType.DMA((4,)),
        ],
        compiler_params=pltpu.CompilerParams(vmem_limit_bytes=VMEM_BYTES + (0 if mem_len <= 512 else 3 * 1024 * 1024)),
        name="middle",
    )(tokens, attended, cotangent, mem_key, mem_value, gains, shifts, down_bias, raise_bias, *weights)


def per_device(
    tokens,
    memory,
    segment_ids,
    padding_mask,
    cotangent,
    prefix_embed,
    prefix_first,
    first_bias,
    prefix_second,
    second_bias,
    adapter_down,
    down_bias,
    adapter_raise,
    raise_bias,
    norm_gain,
    norm_shift,
    self_query,
    self_key,
    self_value,
    self_output,
    cross_query,
    cross_key,
    cross_value,
    cross_output,
    feed_in,
    feed_out,
):
    row_count, length, model_width = tokens.shape
    flat_rows = row_count * length
    n = lax.axis_size("seq")
    batches = lax.axis_size("batch")
    down = adapter_down.shape[1]
    attended, mem_key, mem_value, *saved = self_forward(
        n,
        segment_ids,
        padding_mask,
        tokens.reshape(flat_rows, model_width),
        (self_query, self_key, self_value),
        (
            prefix_embed,
            prefix_first,
            first_bias.reshape(1, -1),
            prefix_second,
            second_bias.reshape(1, -1),
        ),
        memory.reshape(-1, model_width),
        (cross_key, cross_value),
    )
    layer_output, first_grad, out_grad, *mem_grads, weight_sums, vector_sums = middle(
        tokens.reshape(flat_rows, model_width),
        attended,
        cotangent.reshape(flat_rows, model_width),
        mem_key,
        mem_value,
        norm_gain,
        norm_shift,
        down_bias.reshape(1, -1),
        raise_bias.reshape(1, -1),
        (
            self_output,
            cross_query,
            cross_output,
            adapter_down,
            adapter_raise,
            feed_in,
            feed_out,
        ),
    )
    layer_output = layer_output.reshape(row_count, length, model_width)
    token_grad, memory_grad, prefix_grad, vector_sums, full_sums = self_backward(
        n,
        batches,
        first_grad,
        out_grad.reshape(n, -1, HD, length),
        weight_sums,
        mem_grads,
        (cross_key, cross_value),
        vector_sums,
        saved,
        (self_query, self_key, self_value),
    )
    *replicated, token_grad, memory_grad = finish(
        full_sums.reshape(-1, LANES),
        vector_sums,
        prefix_grad,
        prefix_embed,
        prefix_first,
        first_bias.reshape(1, -1),
        prefix_second,
        down,
        token_grad,
        memory_grad,
    )
    token_grad = token_grad.reshape(row_count, length, model_width)
    memory_grad = memory_grad.reshape(memory.shape)
    replicated = [
        value.reshape(-1) if value.shape[0] == 1 else value for value in replicated
    ]
    return (layer_output, token_grad, memory_grad, *replicated)


def solution(mesh):
    placed = (
        P("batch", "seq", None),
        P("batch", "seq", None),
        P("batch", "seq"),
        P("batch", "seq"),
        P("batch", "seq", None),
        P(),
        P(),
        P(),
        P(),
        P(),
        P(),
        P(),
        P(),
        P(),
        P(),
        P(),
        P(),
        P(),
        P(),
        P(),
        P(),
        P(),
        P(),
        P(),
        P(),
        P(),
    )
    return jax.shard_map(
        per_device,
        mesh=mesh,
        in_specs=placed,
        out_specs=(
            P("batch", "seq", None),
            P("batch", "seq", None),
            P("batch", "seq", None),
            P(),
            P(),
            P(),
            P(),
            P(),
            P(),
            P(),
            P(),
            P(),
            P(),
            P(),
        ),
        check_vma=False,
    )
```

```python
import functools

import jax
import jax.numpy as jnp
from jax import lax
from jax.experimental import pallas as pl
from jax.experimental.pallas import tpu as pltpu
from jax.sharding import PartitionSpec as P

H = 16
HD = 64
LANES = 128
PREFIX_ROWS = 32
VMEM_BYTES = 60 * 1024 * 1024
SUM_ROWS = 16
MESH = pl.DeviceIdType.MESH

masked_score = -1e30
norm_eps = 1e-05

def dot_nn(left, right):
    return lax.dot_general(
        left, right, (((1,), (0,)), ((), ())), preferred_element_type=jnp.float32
    )


def dot_nt(left, right):
    return lax.dot_general(
        left, right, (((1,), (1,)), ((), ())), preferred_element_type=jnp.float32
    )


def dot_tn(left, right):
    return lax.dot_general(
        left, right, (((0,), (0,)), ((), ())), preferred_element_type=jnp.float32
    )


def remote(source, target, send_sem, recv_sem, axis, peer):
    return pltpu.make_async_remote_copy(
        src_ref=source,
        dst_ref=target,
        send_sem=send_sem,
        recv_sem=recv_sem,
        device_id={axis: peer},
        device_id_type=MESH,
    )


def enter(sizes):
    barrier = pltpu.get_barrier_semaphore()
    for axis, size in sizes.items():
        for other in range(size):

            @pl.when(other != lax.axis_index(axis))
            def _():
                pl.semaphore_signal(barrier, inc=1, device_id={axis: other}, device_id_type=MESH)

    pl.semaphore_wait(barrier, sum(sizes.values()) - len(sizes))


def others(size, mine, body):
    for other in range(size):

        @pl.when(other != mine)
        def _():
            body(other)


def rows_of(index, size):
    return pl.ds(pl.multiple_of(index * size, size), size)


def span_of(start, size):
    return pl.ds(pl.multiple_of(start, LANES), size)


def own_columns(ref, first, me, width):
    if width % LANES == 0:
        return ref[:, pl.ds(pl.multiple_of(first + me * width, LANES), width)].astype(jnp.float32)
    share = LANES // width
    block = ref[:, pl.ds(pl.multiple_of(first + me // share * LANES, LANES), LANES)].astype(
        jnp.float32
    )
    picked = block[:, :width]
    for part in range(1, share):
        picked = jnp.where(me % share == part, block[:, part * width : (part + 1) * width], picked)
    return picked


def head_lanes(shape, head):
    lane = lax.broadcasted_iota(jnp.int32, shape, 1)
    return (lane >= head * HD) & (lane < (head + 1) * HD)


def self_forward_kernel(
    n,
    seg_ref,
    pad_ref,
    tok_ref,
    wq_in,
    wk_in,
    wv_in,
    emb_ref,
    first_in,
    fbias_ref,
    second_in,
    sbias_ref,
    mem_ref,
    wck_in,
    wcv_in,
    att_ref,
    mkey_ref,
    mvalue_ref,
    qx_out,
    kx_out,
    raw_out,
    pk_out,
    pv_out,
    pkt_out,
    ot_out,
    lse_out,
    send,
    recv,
    meta_send,
    meta,
    kx,
    qx,
    vt,
    hidden,
    pk,
    pv,
    pkt,
    pvt,
    stat,
    acc,
    o_send,
    o_recv,
    mem_all,
    wck,
    wcv,
    wq_ref,
    wk_ref,
    wv_ref,
    first_ref,
    second_ref,
    send_sem,
    recv_sem,
    meta_send_sem,
    meta_recv_sem,
    o_send_sem,
    o_recv_sem,
    mem_send_sem,
    mem_recv_sem,
    out_sem,
    weight_sem,
    in_sem,
):
    low = jnp.bfloat16
    f32 = jnp.float32
    me = lax.axis_index("seq")
    length, width = tok_ref.shape
    group = width // n
    heads = group // HD
    plane = 2 * length
    planes = n // 2
    block = 2 * LANES
    per_block = block // group
    blocks = width // block
    step_rows = 256
    steps = plane // step_rows
    my_plane = me // 2
    my_side = lax.rem(me, 2)

    def meta_copy(peer, slot):
        return remote(
            meta_send, meta.at[slot], meta_send_sem.at[peer], meta_recv_sem.at[slot], "seq", peer
        )

    def qkv_copy(head, peer, slot):
        return remote(
            send.at[peer, head],
            recv.at[head, slot],
            send_sem.at[head, peer],
            recv_sem.at[head, slot],
            "seq",
            peer,
        )

    def out_copy(head, peer, slot):
        return remote(
            o_send.at[head, peer],
            o_recv.at[slot, head],
            o_send_sem.at[head, peer],
            o_recv_sem.at[head, slot],
            "seq",
            peer,
        )

    def mem_along(which, toward):
        part = mem_all.at[which, my_side]
        return remote(
            part,
            part,
            mem_send_sem.at[(toward + 1) // 2, which],
            mem_recv_sem.at[which],
            "seq",
            me + 2 * toward,
        )

    def mem_across(side):
        part = mem_all.at[:, side]
        return remote(
            part,
            part,
            mem_send_sem.at[0, planes],
            mem_recv_sem.at[planes],
            "seq",
            me + 1 - 2 * my_side,
        )

    def mem_hops(hop, body):
        for toward in (1, -1):
            which = my_plane - toward * hop
            ahead = my_plane + toward

            @pl.when((which >= 0) & (which < planes) & (ahead >= 0) & (ahead < planes))
            def _():
                body(mem_along(which, toward))

    def mem_arrivals(hop):
        for toward in (1, -1):
            which = my_plane - toward * hop

            @pl.when((which >= 0) & (which < planes))
            def _():
                mem_along(which, -toward).wait_recv()

    def block_at(step):
        if blocks >= planes:
            share = blocks // planes
            return lax.rem(my_plane + 1 + step // share, planes) * share + step % share
        return lax.rem(me // per_block + 1 + step, blocks)

    def weight_load(step, which):
        columns = rows_of(block_at(step), block)
        source = (wq_in, wk_in, wv_in)[which]
        target = (wq_ref, wk_ref, wv_ref)[which]
        return pltpu.make_async_copy(
            source.at[:, columns], target.at[:, columns], weight_sem.at[step, which]
        )

    for step in range(blocks):
        for which in range(3):
            weight_load(step, which).start()
    loads = [
        pltpu.make_async_copy(source, target, in_sem.at[index])
        for index, (source, target) in enumerate(
            ((first_in, first_ref), (second_in, second_ref), (wck_in, wck), (wcv_in, wcv))
        )
    ]
    for load in loads:
        load.start()
    segments = seg_ref[...]
    tags = jnp.where(pad_ref[...] == 1, segments, -1)
    row = lax.broadcasted_iota(jnp.int32, meta_send.shape, 0)
    meta_send[...] = jnp.where(row == 0, segments, tags)
    mem_all[my_plane, my_side] = mem_ref[...]
    enter({"seq": n})
    others(n, me, lambda peer: meta_copy(peer, me).start())
    meta[me] = meta_send[...]

    for step in range(blocks):
        at = block_at(step)
        columns = rows_of(at, block)
        for which, weight in enumerate((wq_ref, wk_ref, wv_ref)):
            weight_load(step, which).wait()
            piece = dot_nn(tok_ref[...], weight[:, columns]).T.astype(low)
            for part in range(per_block):
                for head in range(heads):
                    first = part * group + head * HD
                    send[at * per_block + part, head, which] = piece[first : first + HD]
        for part in range(per_block):
            peer = at * per_block + part

            @pl.when(peer != me)
            def _():
                qkv_copy(0, peer, me).start()

            @pl.when(peer == me)
            def _():
                for head in range(heads):
                    recv[head, me] = send[peer, head]

    mem_hops(0, lambda copy: copy.start())

    loads[0].wait()
    loads[1].wait()
    hidden[...] = jnp.zeros_like(hidden)
    hidden[: emb_ref.shape[0], :] = jnp.tanh(dot_nn(emb_ref[...], first_ref[...]) + fbias_ref[...])
    hidden_low = hidden[...].astype(low)
    prefix_key = dot_nn(hidden_low, own_columns(second_ref, 0, me, group).astype(low)) + own_columns(
        sbias_ref, 0, me, group
    )
    prefix_value = dot_nn(
        hidden_low, own_columns(second_ref, width, me, group).astype(low)
    ) + own_columns(sbias_ref, width, me, group)
    prefix_row = lax.broadcasted_iota(jnp.int32, (PREFIX_ROWS, HD), 0)
    prefix_open = jnp.where(prefix_row < emb_ref.shape[0], 0.0, masked_score)
    for head in range(heads):
        here = slice(head * HD, (head + 1) * HD)
        pk[head] = jnp.concatenate([prefix_key[:, here], prefix_open], axis=1).astype(low)
        pv[head] = prefix_value[:, here].astype(low)
    pkt[...] = prefix_key.T.astype(low).reshape(heads, HD, PREFIX_ROWS)
    pvt[:, :HD, :] = prefix_value.T.astype(low).reshape(heads, HD, PREFIX_ROWS)
    pvt[:, HD:, :] = jnp.ones((heads, SUM_ROWS, PREFIX_ROWS), low)
    vt[:, HD:, :] = jnp.ones((heads, SUM_ROWS, n * length), low)

    def arrive(head, chunk):
        @pl.when(chunk != me)
        def _():
            @pl.when(head == 0)
            def _():
                meta_copy(chunk, chunk).wait_recv()

            qkv_copy(head, chunk, chunk).wait_recv()

        here = rows_of(chunk, length)
        state = lax.broadcasted_iota(jnp.int32, (HD, length), 0)
        qx[head, :HD, here] = (recv[head, chunk, 0].astype(f32) * 0.125).astype(low)
        qx[head, HD:, here] = jnp.where(state == meta[chunk, 0:1, :], 1.0, 0.0).astype(low)
        is_open = jnp.where(state == meta[chunk, 1:2, :], 0.0, masked_score)
        kx[head, here, :] = jnp.concatenate(
            [recv[head, chunk, 1].astype(f32), is_open], axis=0
        ).T.astype(low)
        vt[head, :HD, here] = recv[head, chunk, 2]

    def open_plane(head, which):
        scores = dot_nn(pk[head], qx[head, :, rows_of(which, plane)])
        top = jnp.max(scores, axis=0, keepdims=True)
        raised = jnp.exp(scores - top)
        stat[which, head, 0:1, :] = top
        acc[which, head] = dot_nn(pvt[head], raised.astype(low))

    def pair_part(head, upper, lower, first, keys, diagonal):
        here = slice(first, first + step_rows)
        queries = qx[head, :, span_of(upper * plane + first, step_rows)]
        key_rows = span_of(lower * plane, keys)
        scores = dot_nn(kx[head, key_rows, :], queries)
        if diagonal:
            key_at = lax.broadcasted_iota(jnp.int32, scores.shape, 0)
            query_at = lax.broadcasted_iota(jnp.int32, scores.shape, 1) + first
            scores = jnp.where(key_at <= query_at, scores, masked_score)
        old_top = stat[upper, head, 0:1, here]
        top = jnp.maximum(old_top, jnp.max(scores, axis=0, keepdims=True))
        raised = jnp.exp(scores - top).astype(low)
        stat[upper, head, 0:1, here] = top
        acc[upper, head, :, here] = acc[upper, head, :, here] * jnp.exp(old_top - top) + dot_nn(
            vt[head, :, key_rows], raised
        )

    def pair(head, upper, lower):
        for part in range(steps):
            pair_part(head, upper, lower, part * step_rows, plane, False)

    def pair_diagonal(head, which):
        for part in range(steps):
            pair_part(head, which, which, part * step_rows, (part + 1) * step_rows, True)

    def close_plane(head, which):
        total = acc[which, head, HD : HD + 1, :]
        value = acc[which, head, :HD, :] / total
        acc[which, head, :HD, :] = value
        stat[which, head, 0:1, :] = stat[which, head, 0:1, :] + jnp.log(total)
        for part in range(2):
            chunk = 2 * which + part
            o_send[head, chunk] = value[:, part * length : (part + 1) * length].astype(low)

            @pl.when(chunk != me)
            def _():
                out_copy(head, chunk, me).start()

            @pl.when(chunk == me)
            def _():
                o_recv[me, head] = o_send[head, chunk]

    def project_memory():
        mem_across(1 - my_side).wait_recv()
        for load in loads[2:]:
            load.wait()
        whole = mem_all[...].reshape(mkey_ref.shape)

        def one(index, carry):
            here = rows_of(index, block)
            mkey_ref[:, here] = dot_nn(whole, wck[:, here]).astype(low)
            mvalue_ref[:, here] = dot_nn(whole, wcv[:, here]).astype(low)
            return carry

        lax.fori_loop(0, blocks, one, 0)

    def stage(index, carry):
        head = index // planes
        step = lax.rem(index, planes)

        @pl.when(head + 1 < heads)
        def _():
            there = lax.rem(my_plane + 1 + step, planes)
            for part in range(2):
                peer = 2 * there + part

                @pl.when(peer != me)
                def _():
                    qkv_copy(head, peer, me).wait_send()
                    qkv_copy(head + 1, peer, me).start()

        here = lax.rem(my_plane + step, planes)
        arrive(head, 2 * here)
        arrive(head, 2 * here + 1)
        open_plane(head, here)
        pair_diagonal(head, here)

        def earlier(back, inner):
            there = lax.rem(my_plane + back, planes)
            pair(head, jnp.maximum(here, there), jnp.minimum(here, there))

            @pl.when((step == planes - 1) & (there > here))
            def _():
                close_plane(head, there)

            return inner

        lax.fori_loop(0, step, earlier, 0)
        for hop in range(1, planes - 1):

            @pl.when(index == hop)
            def _():
                mem_arrivals(hop)
                mem_hops(hop, lambda copy: copy.start())

        @pl.when(index == planes - 1)
        def _():
            mem_arrivals(planes - 1)
            mem_across(my_side).start()

        @pl.when((my_plane + step >= planes) | (my_plane == 0))
        def _():
            close_plane(head, here)

        return carry

    lax.fori_loop(0, heads * planes, stage, 0)

    saves = []

    def save(source, target):
        copy = pltpu.make_async_copy(source, target, out_sem.at[len(saves)])
        copy.start()
        saves.append(copy)

    save(qx, qx_out)
    save(kx, kx_out)
    save(recv, raw_out)
    save(pk, pk_out)
    save(pv, pv_out)
    save(pkt, pkt_out)
    save(acc, ot_out)
    save(stat, lse_out)
    project_memory()
    for other in range(n):

        @pl.when(other != me)
        def _():
            for head in range(heads):
                out_copy(head, other, other).wait_recv()

        att_ref[:, other * group : (other + 1) * group] = (
            o_recv[other].reshape(group, length).astype(f32).T.astype(low)
        )

    def drain(peer):
        meta_copy(peer, me).wait_send()
        qkv_copy(heads - 1, peer, me).wait_send()
        for head in range(heads):
            out_copy(head, peer, me).wait_send()

    others(n, me, drain)
    for hop in range(planes - 1):
        mem_hops(hop, lambda copy: copy.wait_send())
    mem_across(my_side).wait_send()
    for copy in saves:
        copy.wait()


def self_forward(n, segments, padding, tokens, weights, prefix, memory, mem_weights):
    length, width = tokens.shape
    group = width // n
    heads = group // HD
    whole = n * length
    planes = n // 2
    low = jnp.bfloat16
    f32 = jnp.float32
    vmem = pl.BlockSpec(memory_space=pltpu.VMEM)
    anywhere = pl.BlockSpec(memory_space=pl.ANY)
    dma = pltpu.SemaphoreType.DMA
    shapes = (
        ((heads, 2 * HD, whole), low),
        ((heads, whole, 2 * HD), low),
        ((heads, n, 3, HD, length), low),
        ((heads, PREFIX_ROWS, 2 * HD), low),
        ((heads, PREFIX_ROWS, HD), low),
        ((heads, HD, PREFIX_ROWS), low),
        ((planes, heads, HD + SUM_ROWS, 2 * length), f32),
        ((planes, heads, 8, 2 * length), f32),
    )
    square = pltpu.VMEM((width, width), low)
    qx, kx, raw, pk, pv, pkt, acc, stat = (pltpu.VMEM(*shape) for shape in shapes)
    return pl.pallas_call(
        functools.partial(self_forward_kernel, n),
        out_shape=(
            jax.ShapeDtypeStruct((length, width), low),
            jax.ShapeDtypeStruct((n * memory.shape[0], width), low),
            jax.ShapeDtypeStruct((n * memory.shape[0], width), low),
        )
        + tuple(jax.ShapeDtypeStruct(*shape) for shape in shapes),
        in_specs=[vmem] * 3
        + [anywhere] * 3
        + [vmem, anywhere, vmem, anywhere, vmem, vmem]
        + [anywhere] * 2,
        out_specs=(vmem,) * 3 + (anywhere,) * 8,
        scratch_shapes=[
            pltpu.VMEM((n, heads, 3, HD, length), low),
            raw,
            pltpu.VMEM((8, length), jnp.int32),
            pltpu.VMEM((n, 8, length), jnp.int32),
            kx,
            qx,
            pltpu.VMEM((heads, HD + SUM_ROWS, whole), low),
            pltpu.VMEM((PREFIX_ROWS, weights[0].shape[0] // 2), f32),
            pk,
            pv,
            pkt,
            pltpu.VMEM((heads, HD + SUM_ROWS, PREFIX_ROWS), low),
            stat,
            acc,
            pltpu.VMEM((heads, n, HD, length), low),
            pltpu.VMEM((n, heads, HD, length), low),
            pltpu.VMEM((planes, 2) + memory.shape, low),
            square,
            square,
            square,
            square,
            square,
            pltpu.VMEM(prefix[1].shape, low),
            pltpu.VMEM(prefix[3].shape, low),
            dma((heads, n)),
            dma((heads, n)),
            dma((n,)),
            dma((n,)),
            dma((heads, n)),
            dma((heads, n)),
            dma((2, planes + 1)),
            dma((planes + 1,)),
            dma((8,)),
            dma((width // (2 * LANES), 3)),
            dma((4,)),
        ],
        compiler_params=pltpu.CompilerParams(
            collective_id=0, has_side_effects=True, vmem_limit_bytes=VMEM_BYTES
        ),
        name="self_forward",
    )(segments, padding, tokens, *weights, *prefix, memory, *mem_weights)


def self_backward_kernel(
    n,
    batches,
    base_in,
    do_in,
    sums_in,
    mkey_in,
    mvalue_in,
    wck_in,
    wcv_in,
    vecs_in,
    qx_in,
    kx_in,
    raw_in,
    pk_in,
    pv_in,
    pkt_in,
    ot_in,
    lse_in,
    wq_in,
    wk_in,
    wv_in,
    tg_ref,
    mgrad_ref,
    pkv_ref,
    vecs_ref,
    full_out,
    do_recv,
    qx,
    kx,
    raw,
    kt,
    values,
    dot,
    qdo,
    pk,
    pv,
    pkt,
    ot,
    stat,
    weights,
    dqt,
    dkv,
    g_send,
    g_recv,
    pre_ref,
    pre_all,
    pre_sum,
    pre_recv,
    sums_mine,
    sums_core,
    sums_x,
    sums_side,
    sums_z,
    full,
    mkey,
    mvalue,
    wck,
    wcv,
    mem_part,
    mem_side,
    mem_up,
    mem_down,
    vec_all,
    vec_sum,
    vec_y,
    vec_both,
    vec_z,
    product,
    base_ref,
    do_send_sem,
    do_recv_sem,
    g_send_sem,
    g_recv_sem,
    in_sem,
    send_sem,
    recv_sem,
):
    low = jnp.bfloat16
    f32 = jnp.float32
    me = lax.axis_index("seq")
    length, width = tg_ref.shape
    group = width // n
    heads = group // HD
    plane = 2 * length
    planes = n // 2
    step_rows = 256
    my_batch = lax.axis_index("batch")
    my_core = lax.rem(my_batch, 2)
    my_high = my_batch // 2
    highs = batches // 2
    my_plane = me // 2
    my_side = lax.rem(me, 2)
    beside = me + 1 - 2 * my_side
    used = [0]

    def numbers(count):
        used[0] += count
        return used[0] - count

    core_slot = numbers(2)
    x_slot = numbers(2 * highs)
    y_slot = numbers(3)
    z_slot = numbers(2 * planes)
    up_slot = numbers(planes)
    down_slot = numbers(planes)
    va_slot = numbers(batches)
    vb_slot = numbers(1)
    vc_slot = numbers(planes)
    pa_slot = numbers(batches)
    pb_slot = numbers(n)

    def send(source, target, first, peer_index, slot_index, axis, peer):
        return remote(
            source,
            target,
            send_sem.at[first + peer_index],
            recv_sem.at[first + slot_index],
            axis,
            peer,
        )

    half_rows = 2 * planes * highs * sums_z.shape[1]
    x_rows = half_rows // highs
    y_rows = x_rows // 2
    z_rows = y_rows // planes
    x_row = pl.multiple_of(my_high * x_rows, x_rows)
    y_row = pl.multiple_of(x_row + my_side * y_rows, y_rows)

    def part(row, count):
        return sums_mine.at[pl.ds(pl.multiple_of(row, count), count)]

    def reduce_core():
        return send(
            sums_in.at[1 - my_core], sums_core, core_slot, 0, 0, "batch", my_batch + 1 - 2 * my_core
        )

    def reduce_x(peer, slot):
        return send(
            part(peer * x_rows, x_rows),
            sums_x.at[slot],
            x_slot,
            peer,
            slot,
            "batch",
            2 * peer + my_core,
        )

    def reduce_y():
        return send(
            part(x_row + (1 - my_side) * y_rows, y_rows), sums_side, y_slot, 0, 0, "seq", beside
        )

    def reduce_z(peer, slot):
        return send(
            part(y_row + peer * z_rows, z_rows),
            sums_z.at[slot],
            z_slot,
            peer,
            slot,
            "seq",
            2 * peer + my_side,
        )

    def gather_z(peer, slot):
        piece = full.at[my_core, my_high, my_side, slot]
        return send(piece, piece, z_slot + planes, peer, slot, "seq", 2 * peer + my_side)

    def gather_y(side):
        piece = full.at[my_core, my_high, side]
        return send(piece, piece, y_slot + 1, 0, 0, "seq", beside)

    def gather_x(peer, slot):
        piece = full.at[my_core, slot]
        return send(piece, piece, x_slot + highs, peer, slot, "batch", 2 * peer + my_core)

    def gather_core(core):
        piece = full.at[core]
        return send(piece, piece, core_slot + 1, 0, 0, "batch", my_batch + 1 - 2 * my_core)

    def mem_across():
        return send(
            mem_part.at[:, 1 - my_side], mem_side, y_slot + 2, 0, 0, "seq", beside
        )

    def mem_hop(target, toward, peer=None):
        buffer, slot = (mem_up, up_slot) if toward > 0 else (mem_down, down_slot)
        return send(
            mem_part.at[target, my_side],
            buffer.at[target],
            slot,
            target,
            target,
            "seq",
            me + 2 * toward if peer is None else peer,
        )

    def mem_from(target, toward):
        return mem_hop(target, toward, me - 2 * toward)

    def mem_pass(toward):
        buffer = mem_up if toward > 0 else mem_down
        first = 0 if toward > 0 else planes - 1
        for target in range(planes):

            @pl.when((target - my_plane) * toward > 0)
            def _():
                @pl.when(my_plane != first)
                def _():
                    mem_from(target, toward).wait_recv()
                    mem_part[target, my_side] = (
                        mem_part[target, my_side].astype(f32) + buffer[target].astype(f32)
                    ).astype(low)

                mem_hop(target, toward).start()

    def mem_stage(at):
        pl.when(my_plane == at)(lambda: mem_pass(1))
        pl.when(my_plane == planes - 1 - at)(lambda: mem_pass(-1))

    def mem_end():
        value = mem_part[my_plane, my_side].astype(f32)
        mgrad_ref[...] = value.astype(low)

        @pl.when(my_plane > 0)
        def _():
            mem_from(my_plane, 1).wait_recv()
            mgrad_ref[...] = (mgrad_ref[...].astype(f32) + mem_up[my_plane].astype(f32)).astype(low)

        @pl.when(my_plane < planes - 1)
        def _():
            mem_from(my_plane, -1).wait_recv()
            mgrad_ref[...] = (
                mgrad_ref[...].astype(f32) + mem_down[my_plane].astype(f32)
            ).astype(low)

    def mem_drain():
        for target in range(planes):

            @pl.when(target > my_plane)
            def _():
                mem_hop(target, 1).wait_send()

            @pl.when(target < my_plane)
            def _():
                mem_hop(target, -1).wait_send()

    def vec_a(peer, slot):
        return send(vecs_in, vec_all.at[slot], va_slot, peer, slot, "batch", peer)

    def vec_b(side):
        return send(vec_sum, vec_y.at[side], vb_slot, 0, 0, "seq", beside)

    def vec_c(peer, slot):
        return send(vec_both, vec_z.at[slot], vc_slot, peer, slot, "seq", 2 * peer + my_side)

    def pre_a(peer, slot):
        return send(pre_ref, pre_all.at[slot], pa_slot, peer, slot, "batch", peer)

    def pre_b(peer, slot):
        return send(pre_sum, pre_recv.at[slot], pb_slot, peer, slot, "seq", peer)

    def do_copy(head, peer, slot):
        return remote(
            do_in.at[peer, head],
            do_recv.at[head, slot],
            do_send_sem.at[head, peer],
            do_recv_sem.at[head, slot],
            "seq",
            peer,
        )

    def q_copy(head, peer, slot):
        return remote(
            g_send.at[peer, head, 0],
            g_recv.at[0, slot, head],
            g_send_sem.at[0, head, peer],
            g_recv_sem.at[0, head, slot],
            "seq",
            peer,
        )

    def kv_copy(head, peer, slot):
        return remote(
            g_send.at[peer, head, pl.ds(1, 2)],
            g_recv.at[pl.ds(1, 2), slot, head],
            g_send_sem.at[1, head, peer],
            g_recv_sem.at[1, head, slot],
            "seq",
            peer,
        )

    def added(ref, size):
        value = ref[0].astype(f32)
        for other in range(1, size):
            value = value + ref[other].astype(f32)
        return value

    loads = [
        pltpu.make_async_copy(source, target, in_sem.at[index])
        for index, (source, target) in enumerate(
            (
                (raw_in, raw),
                (kx_in, kx),
                (pk_in, pk),
                (pv_in, pv),
                (pkt_in, pkt),
                (qx_in, qx),
                (ot_in, ot),
                (lse_in, stat),
                (sums_in.at[my_core], sums_mine),
                (vecs_in, vec_all.at[my_batch]),
                (mkey_in, mkey),
                (mvalue_in, mvalue),
                (wck_in, wck),
                (wcv_in, wcv),
                (base_in, base_ref),
                (wq_in, weights.at[0]),
                (wk_in, weights.at[1]),
                (wv_in, weights.at[2]),
            )
        )
    ]
    own_do = pltpu.make_async_copy(do_in.at[me], do_recv.at[:, me], in_sem.at[len(loads)])
    own_do.start()
    for load in loads:
        load.start()
    enter({"seq": n, "batch": batches})
    others(n, me, lambda peer: do_copy(0, peer, me).start())
    reduce_core().start()
    others(batches, my_batch, lambda peer: vec_a(peer, my_batch).start())
    dkv[...] = jnp.zeros_like(dkv)
    product[...] = jnp.zeros_like(product)
    pre_ref[...] = jnp.zeros_like(pre_ref)
    for load in loads[:14]:
        load.wait()
    own_do.wait()

    def turn(index, carry):
        head = index // n
        chunk = lax.rem(index, n)
        here = rows_of(chunk, length)
        kt[head, :, here] = raw[head, chunk, 1]
        values[head, here, :] = raw[head, chunk, 2].astype(f32).T.astype(low)
        return carry

    lax.fori_loop(0, heads * n, turn, 0)

    def memory_back(index, carry):
        here = rows_of(index, step_rows)
        value = dot_nt(mkey[...], wck[here, :]) + dot_nt(mvalue[...], wcv[here, :])
        mem_part[:, :, :, here] = value.astype(low).reshape(mem_part.shape[:3] + (step_rows,))
        return carry

    lax.fori_loop(0, width // step_rows, memory_back, 0)
    mem_across().start()

    def next_head(head):
        @pl.when(head + 1 < heads)
        def _():
            def move(peer):
                do_copy(head, peer, me).wait_send()
                do_copy(head + 1, peer, me).start()

            others(n, me, move)

    def arrive(head, which):
        for part in range(2):
            chunk = 2 * which + part

            @pl.when(chunk != me)
            def _():
                do_copy(head, chunk, chunk).wait_recv()

            grads = do_recv[head, chunk]
            dot[head, :, rows_of(chunk, length)] = grads
            grads = grads.astype(f32)
            query = raw[head, chunk, 0].astype(f32) * 0.125
            qdo[head, rows_of(chunk, length), :] = (
                jnp.concatenate([query, grads], axis=0).T.astype(low)
            )
            here = slice(part * length, (part + 1) * length)
            stat[which, head, 1:2, here] = jnp.sum(
                grads * ot[which, head, :HD, here], axis=0, keepdims=True
            )
        here = rows_of(which, plane)
        weight = jnp.exp(dot_nn(pk[head], qx[head, :, here]) - stat[which, head, 0:1, :])
        slope = weight * (dot_nn(pv[head], dot[head, :, here]) - stat[which, head, 1:2, :])
        both = jnp.concatenate([slope, weight], axis=0).astype(low)
        sums = dot_nn(both, qdo[head, here, :])
        pre_ref[head] += jnp.where(
            head_lanes((PREFIX_ROWS, 2 * HD), 0), sums[:PREFIX_ROWS], sums[PREFIX_ROWS:]
        )
        slope = slope.astype(low)
        dqt[which, head] = dot_nn(pkt[head], slope)

    def plus(first, second):
        return (first.astype(f32) + second.astype(f32)).astype(low)

    def sum_one():
        reduce_core().wait_recv()
        sums_mine[...] = plus(sums_mine[...], sums_core[...])
        others(highs, my_high, lambda peer: reduce_x(peer, my_high).start())

    def sum_two():
        here = pl.ds(x_row, x_rows)
        others(highs, my_high, lambda peer: reduce_x(peer, peer).wait_recv())
        sums_x[my_high] = sums_mine[here]
        sums_mine[here] = added(sums_x, highs).astype(low)
        reduce_y().start()

    def sum_three():
        here = pl.ds(y_row, y_rows)
        reduce_y().wait_recv()
        sums_mine[here] = plus(sums_mine[here], sums_side[...])
        others(planes, my_plane, lambda peer: reduce_z(peer, my_plane).start())

    def sum_four():
        here = pl.ds(pl.multiple_of(y_row + my_plane * z_rows, z_rows), z_rows)
        others(planes, my_plane, lambda peer: reduce_z(peer, peer).wait_recv())
        sums_z[my_plane] = sums_mine[here]
        full[my_core, my_high, my_side, my_plane] = added(sums_z, planes).astype(low)
        others(planes, my_plane, lambda peer: gather_z(peer, my_plane).start())

    def sum_five():
        others(planes, my_plane, lambda peer: gather_z(peer, peer).wait_recv())
        gather_y(my_side).start()

    def sum_six():
        gather_y(1 - my_side).wait_recv()
        others(highs, my_high, lambda peer: gather_x(peer, my_high).start())

    def sum_seven():
        others(highs, my_high, lambda peer: gather_x(peer, peer).wait_recv())
        gather_core(my_core).start()

    def sum_end():
        gather_core(1 - my_core).wait_recv()
        save_full.start()

    def vec_one():
        others(batches, my_batch, lambda peer: vec_a(peer, peer).wait_recv())
        vec_sum[...] = added(vec_all, batches)
        vec_b(my_side).start()
        vec_y[my_side] = vec_sum[...]

    def vec_two():
        vec_b(1 - my_side).wait_recv()
        value = (vec_y[0] + vec_y[1]).astype(f32)
        vec_both[...] = jnp.concatenate(
            [value[:, : width // 2], value[:, width // 2 :]], axis=0
        ).astype(low)
        others(planes, my_plane, lambda peer: vec_c(peer, my_plane).start())
        vec_z[my_plane] = vec_both[...]

    def vec_end():
        others(planes, my_plane, lambda peer: vec_c(peer, peer).wait_recv())
        value = added(vec_z, planes)
        vecs_ref[:, : width // 2] = value[:8]
        vecs_ref[:, width // 2 :] = value[8:]

    def mem_one():
        mem_across().wait_recv()
        mem_part[:, my_side] = plus(mem_part[:, my_side], mem_side[...])

    def stage_pa():
        others(batches, my_batch, lambda peer: pre_a(peer, my_batch).start())
        pre_all[my_batch] = pre_ref[...]

    def stage_pb():
        others(batches, my_batch, lambda peer: pre_a(peer, peer).wait_recv())
        pre_sum[...] = added(pre_all, batches).astype(low)
        others(n, me, lambda peer: pre_b(peer, me).start())
        pre_recv[me] = pre_sum[...]

    save_full = pltpu.make_async_copy(full, full_out, in_sem.at[0])

    def pair_part(head, upper, lower, first, count, diagonal):
        keys = span_of(lower * plane + first, count)
        here = span_of(upper * plane + first, plane - first)
        at = slice(first, plane)
        scores = dot_nn(kx[head, keys, :], qx[head, :, here])
        slope = dot_nn(values[head, keys, :], dot[head, :, here]) - stat[upper, head, 1:2, at]
        weight = jnp.exp(scores - stat[upper, head, 0:1, at])
        if diagonal:
            key_at = lax.broadcasted_iota(jnp.int32, scores.shape, 0)
            query_at = lax.broadcasted_iota(jnp.int32, scores.shape, 1)
            weight = jnp.where(key_at <= query_at, weight, 0.0)
        both = jnp.concatenate([(weight * slope).astype(low), weight.astype(low)], axis=0)
        sums = dot_nn(both, qdo[head, here, :])
        dkv[head, keys, :] += jnp.where(
            head_lanes((count, 2 * HD), 0), sums[:count], sums[count:]
        )
        dqt[upper, head, :, at] += dot_nn(kt[head, :, keys], both[:count])

    def pair(head, upper, lower, diagonal):
        if diagonal:
            pair_part(head, upper, lower, 0, length, True)
            pair_part(head, upper, lower, length, length, True)
        else:
            pair_part(head, upper, lower, 0, plane, False)

    def hand_queries(head, which):
        for part in range(2):
            chunk = 2 * which + part
            g_send[chunk, head, 0] = (
                dqt[which, head, :, part * length : (part + 1) * length] * 0.125
            ).astype(low)

            @pl.when(chunk != me)
            def _():
                q_copy(head, chunk, me).start()

            @pl.when(chunk == me)
            def _():
                g_recv[0, me, head] = g_send[chunk, head, 0]

    def hand_keys(head, which):
        for part in range(2):
            chunk = 2 * which + part
            turned = dkv[head, rows_of(chunk, length), :].T.astype(low)
            g_send[chunk, head, 1] = turned[:HD]
            g_send[chunk, head, 2] = turned[HD:]

            @pl.when(chunk != me)
            def _():
                kv_copy(head, chunk, me).start()

            @pl.when(chunk == me)
            def _():
                g_recv[pl.ds(1, 2), me, head] = g_send[chunk, head, pl.ds(1, 2)]

    rising = my_plane >= planes // 2
    total = heads * planes * (planes + 1) // 2
    hooks = [
        (2, sum_one),
        (3, mem_one),
        (4, lambda: mem_stage(0)),
        (5, vec_one),
        (6, sum_two),
        (8, sum_three),
        (9, vec_two),
        (11, sum_four),
        (14, sum_five),
        (16, sum_six),
        (16, vec_end),
        (19, sum_seven),
    ] + [(4 + 3 * at, functools.partial(mem_stage, at)) for at in range(1, planes - 1)]
    final = total - planes * (planes + 1) // 2
    hooks += [(final + planes + 1, stage_pa), (final + 2 * planes - 1, stage_pb)]

    def hook(pairs):
        for number, body in sorted(hooks, key=lambda item: item[0]):
            pl.when(pairs == number)(body)


    def stage(index, carry):
        head = index // planes
        step = lax.rem(index, planes)
        here = jnp.where(rising, step, planes - 1 - step)

        @pl.when((step == 0) | ((step == 1) & jnp.logical_not(rising)))
        def _():
            @pl.when(rising | (step == 0))
            def _():
                arrive(head, here)

            @pl.when(jnp.logical_not(rising) & (step == 1))
            def _():
                next_head(head)

                def rest(which, inner):
                    arrive(head, planes - 2 - which)
                    return inner

                lax.fori_loop(0, planes - 1, rest, 0)

        begun = head * (planes * (planes + 1) // 2) + step * planes - step * (step - 1) // 2
        hook(begun)
        pair(head, here, here, True)

        @pl.when(rising)
        def _():
            hand_queries(head, here)

        @pl.when(jnp.logical_not(rising))
        def _():
            hand_keys(head, here)

        def far(at, inner):
            there = jnp.where(rising, here + 1 + at, here - 1 - at)

            @pl.when(rising & (step == 0))
            def _():
                arrive(head, there)

            hook(begun + 1 + at)
            pair(head, jnp.maximum(here, there), jnp.minimum(here, there), False)
            return inner

        lax.fori_loop(0, planes - 1 - step, far, 0)

        @pl.when(rising & (step == 0))
        def _():
            next_head(head)

        @pl.when(rising)
        def _():
            hand_keys(head, here)

        @pl.when(jnp.logical_not(rising))
        def _():
            hand_queries(head, here)

        return carry

    lax.fori_loop(0, heads * planes, stage, 0)
    mem_end()
    for load in loads[14:]:
        load.wait()

    def gathered(peer):
        for head in range(heads):
            q_copy(head, peer, peer).wait_recv()
            kv_copy(head, peer, peer).wait_recv()

    half = width // 2

    def gather_plane(step, carry):
        which = lax.rem(my_plane + step, planes)
        for part in range(2):
            peer = 2 * which + part

            @pl.when(peer != me)
            def _():
                gathered(peer)

        columns = rows_of(which, 2 * group)
        for part in range(2):
            here = slice(part * half, (part + 1) * half)
            value = product[here, :]
            for kind in range(3):
                grads = g_recv[kind, pl.ds(2 * which, 2)].reshape(2 * group, length)
                value = value + dot_nn(weights[kind, here, columns], grads)
            product[here, :] = value
        return carry

    lax.fori_loop(0, planes, gather_plane, 0)
    sum_end()
    tile = 256
    for index in range(width // tile):
        here = slice(index * tile, (index + 1) * tile)
        tg_ref[:, here] = (base_ref[:, here] + product[here, :].T).astype(low)
    for other in range(n):

        @pl.when(other != me)
        def _():
            pre_b(other, other).wait_recv()

        value = pre_recv[other].astype(f32)
        for which in range(2):
            pkv_ref[:, which * width + other * group : which * width + (other + 1) * group] = (
                jnp.concatenate(
                    [value[head, :, which * HD : (which + 1) * HD] for head in range(heads)], axis=1
                )
            )

    def drain(peer):
        do_copy(heads - 1, peer, me).wait_send()
        pre_b(peer, me).wait_send()
        for head in range(heads):
            q_copy(head, peer, me).wait_send()
            kv_copy(head, peer, me).wait_send()

    others(n, me, drain)
    others(batches, my_batch, lambda peer: pre_a(peer, my_batch).wait_send())
    others(batches, my_batch, lambda peer: vec_a(peer, my_batch).wait_send())
    reduce_core().wait_send()
    others(highs, my_high, lambda peer: reduce_x(peer, my_high).wait_send())
    reduce_y().wait_send()
    others(planes, my_plane, lambda peer: reduce_z(peer, my_plane).wait_send())
    others(planes, my_plane, lambda peer: gather_z(peer, my_plane).wait_send())
    gather_y(my_side).wait_send()
    others(highs, my_high, lambda peer: gather_x(peer, my_high).wait_send())
    gather_core(my_core).wait_send()
    mem_across().wait_send()
    mem_drain()
    others(planes, my_plane, lambda peer: vec_c(peer, my_plane).wait_send())
    vec_b(my_side).wait_send()
    save_full.wait()


def self_backward(
    n, batches, first_grad, out_grad, sums, mem_grads, mem_weights, vecs, saved, weights
):
    length, width = first_grad.shape
    group = width // n
    heads = group // HD
    whole = n * length
    planes = n // 2
    low = jnp.bfloat16
    f32 = jnp.float32
    vmem = pl.BlockSpec(memory_space=pltpu.VMEM)
    anywhere = pl.BlockSpec(memory_space=pl.ANY)
    dma = pltpu.SemaphoreType.DMA
    sum_rows = sums.shape[0] // (n * batches)
    mem_len = mem_grads[0].shape[0]
    mem_rows = mem_len // n
    mem_part = pltpu.VMEM((planes, mem_rows, width), low)
    mem_low = pltpu.VMEM((mem_len, width), low)
    square = pltpu.VMEM((width, width), low)
    vec = pltpu.VMEM((8, width), f32)
    copies = 6 + 2 * (batches // 2) + 5 * planes + 2 * batches + n
    qx, kx, raw, pk, pv, pkt, ot, stat = (pltpu.VMEM(value.shape, value.dtype) for value in saved)
    return pl.pallas_call(
        functools.partial(self_backward_kernel, n, batches),
        out_shape=(
            jax.ShapeDtypeStruct((length, width), low),
            jax.ShapeDtypeStruct((mem_rows, width), low),
            jax.ShapeDtypeStruct((PREFIX_ROWS, 2 * width), f32),
            jax.ShapeDtypeStruct((8, width), f32),
            jax.ShapeDtypeStruct((2, batches // 2, 2, planes, sum_rows, LANES), low),
        ),
        in_specs=[anywhere] * 19,
        out_specs=(vmem, vmem, vmem, vmem, anywhere),
        scratch_shapes=[
            pltpu.VMEM((heads, n, HD, length), low),
            qx,
            kx,
            raw,
            pltpu.VMEM((heads, HD, whole), low),
            pltpu.VMEM((heads, whole, HD), low),
            pltpu.VMEM((heads, HD, whole), low),
            pltpu.VMEM((heads, whole, 2 * HD), low),
            pk,
            pv,
            pkt,
            ot,
            stat,
            pltpu.VMEM((3, width, width), low),
            pltpu.VMEM((planes, heads, HD, 2 * length), f32),
            pltpu.VMEM((heads, whole, 2 * HD), f32),
            pltpu.VMEM((n, heads, 3, HD, length), low),
            pltpu.VMEM((3, n, heads, HD, length), low),
            pltpu.VMEM((heads, PREFIX_ROWS, 2 * HD), f32),
            pltpu.VMEM((batches, heads, PREFIX_ROWS, 2 * HD), f32),
            pltpu.VMEM((heads, PREFIX_ROWS, 2 * HD), low),
            pltpu.VMEM((n, heads, PREFIX_ROWS, 2 * HD), low),
            pltpu.VMEM((sums.shape[0] // 2, LANES), low),
            pltpu.VMEM((sums.shape[0] // 2, LANES), low),
            pltpu.VMEM((batches // 2, sums.shape[0] // batches, LANES), low),
            pltpu.VMEM((planes * sum_rows, LANES), low),
            pltpu.VMEM((planes, sum_rows, LANES), low),
            pltpu.VMEM((2, batches // 2, 2, planes, sum_rows, LANES), low),
            mem_low,
            mem_low,
            square,
            square,
            pltpu.VMEM((planes, 2, mem_rows, width), low),
            mem_part,
            mem_part,
            mem_part,
            pltpu.VMEM((batches, 8, width), f32),
            vec,
            pltpu.VMEM((2, 8, width), f32),
            pltpu.VMEM((16, width // 2), low),
            pltpu.VMEM((planes, 16, width // 2), low),
            pltpu.VMEM((width, length), f32),
            pltpu.VMEM((length, width), f32),
            dma((heads, n)),
            dma((heads, n)),
            dma((2, heads, n)),
            dma((2, heads, n)),
            dma((19,)),
            dma((copies,)),
            dma((copies,)),
        ],
        compiler_params=pltpu.CompilerParams(
            collective_id=1, has_side_effects=True, vmem_limit_bytes=VMEM_BYTES
        ),
        name="self_backward",
    )(
        first_grad,
        out_grad,
        sums.reshape(2, -1, LANES),
        *mem_grads,
        *mem_weights,
        vecs,
        *saved,
        *weights,
    )


def both_parts(value):
    high = value.astype(jnp.bfloat16).astype(jnp.float32)
    return jnp.concatenate([high, value - high], axis=0).astype(jnp.bfloat16)


def finish_kernel(
    full_in,
    vecs_ref,
    pkv_ref,
    emb_ref,
    first_in,
    fbias_ref,
    second_in,
    token_in,
    mem_in,
    embed_out,
    first_out,
    fbias_out,
    second_out,
    sbias_out,
    down_out,
    dbias_out,
    raise_out,
    rbias_out,
    gain_out,
    shift_out,
    token_out,
    mem_out,
    full_ref,
    first_ref,
    second_ref,
    token_ref,
    mem_ref,
    first_grad,
    second_grad,
    down_grad,
    raise_grad,
    emb,
    hidden,
    out_sem,
    in_sem,
):
    f32 = jnp.float32
    low = jnp.bfloat16
    width = emb_ref.shape[1]
    down = dbias_out.shape[1]
    count = emb_ref.shape[0]
    first = down * width // LANES
    loads = [
        pltpu.make_async_copy(source, target, in_sem.at[index])
        for index, (source, target) in enumerate(
            (
                (full_in.at[first:], full_ref.at[first:]),
                (full_in.at[:first], full_ref.at[:first]),
                (first_in, first_ref),
                (second_in, second_ref),
                (token_in, token_ref),
                (mem_in, mem_ref),
            )
        )
    ]
    for load in loads:
        load.start()
    saves = []

    def save(source, target, rows=None):
        if rows is not None:
            source, target = source.at[rows], target.at[rows]
        copy = pltpu.make_async_copy(source, target, out_sem.at[len(saves)])
        copy.start()
        saves.append(copy)

    loads[0].wait()
    for index in range(width // LANES):
        raise_grad[:, index * LANES : (index + 1) * LANES] = full_ref[
            first + index * down : first + (index + 1) * down, :
        ].astype(f32)
    save(raise_grad, raise_out)
    loads[1].wait()
    for index in range(down // LANES):
        down_grad[:, index * LANES : (index + 1) * LANES] = full_ref[
            index * width : (index + 1) * width, :
        ].astype(f32)
    save(down_grad, down_out)
    for load in loads[4:]:
        load.wait()
    save(token_ref, token_out)
    save(mem_ref, mem_out)
    loads[2].wait()
    emb[...] = jnp.zeros_like(emb)
    emb[:count, :] = emb_ref[...].astype(f32)
    emb_low = emb[...].astype(low)
    row = lax.broadcasted_iota(jnp.int32, hidden.shape, 0)
    hidden[...] = jnp.where(
        row < count, jnp.tanh(dot_nn(emb_low, first_ref[...]) + fbias_ref[...]), 0.0
    )
    value = hidden[...]
    prefix = pkv_ref[...]
    parts = both_parts(prefix)
    hidden_twice = jnp.concatenate([value, value], axis=0).T.astype(low)
    tile = 128
    for index in range(second_grad.shape[0] // tile):
        here = slice(index * tile, (index + 1) * tile)
        second_grad[here, :] = dot_nn(hidden_twice[here, :], parts)
        save(second_grad, second_out, here)
    sbias_out[...] = jnp.sum(prefix, axis=0, keepdims=True)
    loads[3].wait()
    grad = dot_nt(parts, second_ref[...])
    grad = (grad[:PREFIX_ROWS] + grad[PREFIX_ROWS:]) * (1.0 - value * value)
    fbias_out[...] = jnp.sum(grad, axis=0, keepdims=True)
    parts = both_parts(grad)
    emb_twice = jnp.concatenate([emb[...], emb[...]], axis=0).T.astype(low)
    first_grad[...] = dot_nn(emb_twice, parts)
    save(first_grad, first_out)
    back = dot_nt(parts, first_ref[...])
    embed_out[...] = (back[:PREFIX_ROWS] + back[PREFIX_ROWS:])[:count, :]
    rbias_out[...] = vecs_ref[0:1, :]
    dbias_out[...] = vecs_ref[1:2, :down]
    gain_out[...] = vecs_ref[2:5, :]
    shift_out[...] = vecs_ref[5:8, :]
    for copy in saves:
        copy.wait()


def finish(full, vecs, prefix_grad, embed, first, first_bias, second, down, token_grad, memory_grad):
    f32 = jnp.float32
    count, width = embed.shape
    hidden = first.shape[1]
    vmem = pl.BlockSpec(memory_space=pltpu.VMEM)
    anywhere = pl.BlockSpec(memory_space=pl.ANY)
    shapes = (
        (count, width),
        (width, hidden),
        (1, hidden),
        (hidden, 2 * width),
        (1, 2 * width),
        (width, down),
        (1, down),
        (down, width),
        (1, width),
        (3, width),
        (3, width),
    )
    return pl.pallas_call(
        finish_kernel,
        out_shape=tuple(jax.ShapeDtypeStruct(shape, f32) for shape in shapes)
        + tuple(
            jax.ShapeDtypeStruct(value.shape, value.dtype) for value in (token_grad, memory_grad)
        ),
        in_specs=[anywhere, vmem, vmem, vmem, anywhere, vmem, anywhere, anywhere, anywhere],
        out_specs=(
            vmem,
            anywhere,
            vmem,
            anywhere,
            vmem,
            anywhere,
            vmem,
            anywhere,
            vmem,
            vmem,
            vmem,
            anywhere,
            anywhere,
        ),
        scratch_shapes=[
            pltpu.VMEM(full.shape, jnp.bfloat16),
            pltpu.VMEM(first.shape, jnp.bfloat16),
            pltpu.VMEM(second.shape, jnp.bfloat16),
            pltpu.VMEM(token_grad.shape, token_grad.dtype),
            pltpu.VMEM(memory_grad.shape, memory_grad.dtype),
            pltpu.VMEM((width, hidden), f32),
            pltpu.VMEM((hidden, 2 * width), f32),
            pltpu.VMEM((width, down), f32),
            pltpu.VMEM((down, width), f32),
            pltpu.VMEM((PREFIX_ROWS, width), f32),
            pltpu.VMEM((PREFIX_ROWS, hidden), f32),
            pltpu.SemaphoreType.DMA((5 + hidden // 128,)),
            pltpu.SemaphoreType.DMA((6,)),
        ],
        compiler_params=pltpu.CompilerParams(vmem_limit_bytes=VMEM_BYTES),
        name="finish",
    )(full, vecs, prefix_grad, embed, first, first_bias, second, token_grad, memory_grad)


def gelu_pair(value):
    size = jnp.abs(value)
    step = 1.0 / (1.0 + (0.3275911 * 0.7071067811865476) * size)
    bell = jnp.exp(-0.5 * value * value)
    poly = step * (
        0.127414796
        + step
        * (-0.142248368 + step * (0.7107068705 + step * (-0.7265760135 + step * 0.5307027145)))
    )
    act = jnp.maximum(value, 0.0) - size * (poly * bell)
    turn = bell * (0.3989422804014327 * size - poly)
    return act, jnp.where(value >= 0.0, 1.0 + turn, -turn)


def normed(value):
    center = jnp.mean(value, axis=-1, keepdims=True)
    centered = value - center
    scale = lax.rsqrt(jnp.mean(centered * centered, axis=-1, keepdims=True) + norm_eps)
    return centered * scale, scale


def norm_back(grad, scale, unit):
    return scale * (
        grad
        - jnp.mean(grad, axis=-1, keepdims=True)
        - unit * jnp.mean(grad * unit, axis=-1, keepdims=True)
    )


def middle_kernel(
    tok_in,
    att_in,
    cot_in,
    mkey_in,
    mvalue_in,
    gain_ref,
    shift_ref,
    dbias_ref,
    rbias_ref,
    wo_in,
    wcq_in,
    wco_in,
    wd_in,
    wr_in,
    win_in,
    wout_in,
    layer_out,
    fgrad_ref,
    ograd_ref,
    mkey_out,
    mvalue_out,
    sums_out,
    vecs_ref,
    tok_ref,
    att_ref,
    cot_ref,
    mkey_ref,
    mvalue_ref,
    out_ref,
    sums_ref,
    wo,
    wcq,
    wco,
    wd,
    wr,
    win,
    wout,
    unit_one,
    unit_two,
    work,
    total,
    scale_one,
    scale_two,
    low_one,
    low_two,
    low_three,
    query,
    crossed,
    weights,
    slopes,
    down_act,
    down_slope,
    down_grad,
    load_sem,
    win_sem,
    wout_sem,
    out_sem,
):
    length, width = tok_ref.shape
    tile = win.shape[2]
    tiles = win_in.shape[1] // tile
    rows_step = 128
    low = jnp.bfloat16
    f32 = jnp.float32

    sources = (
        att_in,
        wo_in,
        tok_in,
        wcq_in,
        mkey_in,
        mvalue_in,
        wco_in,
        wd_in,
        wr_in,
        cot_in,
    )
    targets = (att_ref, wo, tok_ref, wcq, mkey_ref, mvalue_ref, wco, wd, wr, cot_ref)
    loads = [
        pltpu.make_async_copy(source, target, load_sem.at[index])
        for index, (source, target) in enumerate(zip(sources, targets))
    ]

    def win_load(which):
        slot = lax.rem(which, 2)
        return pltpu.make_async_copy(
            win_in.at[:, rows_of(which, tile)], win.at[slot], win_sem.at[slot]
        )

    def wout_load(which):
        slot = lax.rem(which, 2)
        return pltpu.make_async_copy(
            wout_in.at[rows_of(which, tile), :], wout.at[slot], wout_sem.at[slot]
        )

    for load in loads[:7]:
        load.start()
    for which in range(2):
        win_load(which).start()
        wout_load(which).start()
    for load in loads[7:]:
        load.start()

    def by_columns(extent, step, body):
        def one(index, carry):
            body(pl.ds(pl.multiple_of(index * step, step), step))
            return carry

        lax.fori_loop(0, extent // step, one, 0)

    def by_rows(body, init=0):
        def one(index, carry):
            return body(rows_of(index, rows_step), carry)

        return lax.fori_loop(0, length // rows_step, one, init)

    cols = 512
    half = width // 2

    for load in loads[:3]:
        load.wait()

    def project_out(here):
        work[:, here] = tok_ref[:, here].astype(f32) + dot_nn(att_ref[...], wo[:, here])

    by_columns(width, cols, project_out)

    def first_norm(here, carry):
        unit, scale = normed(work[here, :])
        unit_one[here, :] = unit
        scale_one[here, :] = scale
        value = unit * gain_ref[0:1, :] + shift_ref[0:1, :]
        work[here, :] = value
        low_one[here, :] = value.astype(low)
        return carry

    by_rows(first_norm)

    loads[3].wait()

    def project_query(here):
        query[:, here] = dot_nn(low_one[...], wcq[:, here]).astype(low)

    by_columns(width, cols, project_query)
    per_block = LANES // HD

    def head_queries(here, head):
        both = query[:, here].astype(f32) * 0.125
        return jnp.where(head_lanes(both.shape, head), both, 0.0).astype(low)

    def cross_forward(block):
        here = rows_of(block, LANES)
        keys = mkey_ref[:, here]
        values = mvalue_ref[:, here].astype(f32).T.astype(low)
        outs = []
        for head in range(per_block):
            scores = dot_nt(keys, head_queries(here, head))
            raised = jnp.exp(scores - jnp.max(scores, axis=0, keepdims=True))
            share = 1.0 / jnp.sum(raised, axis=0, keepdims=True)
            weight = (raised * share).astype(low)
            weights[block * per_block + head] = weight
            outs.append(dot_nn(values[head * HD : (head + 1) * HD, :], weight))
        crossed[:, here] = jnp.concatenate(outs, axis=0).T.astype(low)

    loads[4].wait()
    loads[5].wait()

    def cross_forward_step(block, carry):
        cross_forward(block)
        return carry

    lax.fori_loop(0, width // LANES, cross_forward_step, 0)

    loads[6].wait()

    def project_crossed(here):
        work[:, here] += dot_nn(crossed[...], wco[:, here])

    by_columns(width, cols, project_crossed)

    def second_norm(here, carry):
        unit, scale = normed(work[here, :])
        unit_two[here, :] = unit
        scale_two[here, :] = scale
        value = unit * gain_ref[1:2, :] + shift_ref[1:2, :]
        work[here, :] = value
        low_two[here, :] = value.astype(low)
        return carry

    by_rows(second_norm)

    total[...] = jnp.zeros_like(total)

    def feed_forward(which, carry):
        slot = lax.rem(which, 2)
        win_load(which).wait()
        wout_load(which).wait()
        act, slope = gelu_pair(dot_nn(low_two[...], win[slot]))
        slopes[:, rows_of(which, tile)] = slope.astype(low)
        total[...] += dot_nn(act.astype(low), wout[slot])

        @pl.when(which + 2 < tiles)
        def _():
            win_load(which + 2).start()
            wout_load(which + 2).start()

        return carry

    lax.fori_loop(0, tiles, feed_forward, 0)
    loads[7].wait()
    loads[8].wait()
    loads[9].wait()
    act, slope = gelu_pair(dot_nn(low_two[...], wd[...]) + dbias_ref[...])
    down_act[...] = act.astype(low)
    down_slope[...] = slope.astype(low)

    def project_raise(here):
        work[:, here] += total[:, here] + 4.0 * (
            dot_nn(down_act[...], wr[:, here]) + rbias_ref[:, here]
        )

    by_columns(width, cols, project_raise)
    nothing = jnp.zeros((1, width), f32)

    def third_norm(here, carry):
        gain_sum, shift_sum, bias_sum = carry
        unit, scale = normed(work[here, :])
        gain = gain_ref[2:3, :]
        out_ref[here, :] = (unit * gain + shift_ref[2:3, :]).astype(low)
        grad = cot_ref[here, :].astype(f32)
        back = norm_back(grad * gain, scale, unit)
        total[here, :] = back
        back_low = back.astype(low)
        low_three[here, :] = back_low
        return (
            gain_sum + jnp.sum(grad * unit, axis=0, keepdims=True),
            shift_sum + jnp.sum(grad, axis=0, keepdims=True),
            bias_sum + jnp.sum(back_low.astype(f32), axis=0, keepdims=True),
        )

    gain_three, shift_three, bias_sum = by_rows(third_norm, (nothing, nothing, nothing))
    saves = []

    def save(source, target):
        copy = pltpu.make_async_copy(source, target, out_sem.at[len(saves)])
        copy.start()
        saves.append(copy)

    save(out_ref, layer_out)
    vecs_ref[0:1, :] = 4.0 * bias_sum

    back = 4.0 * dot_nt(low_three[...], wr[...]) * down_slope[...].astype(f32)
    back_low = back.astype(low)
    down_grad[...] = back_low
    vecs_ref[1:2, :] = jnp.concatenate(
        [
            jnp.sum(back_low.astype(f32), axis=0, keepdims=True),
            jnp.zeros((1, width - wd.shape[1]), f32),
        ],
        axis=1,
    )
    down = wd.shape[1]
    raise_sum = 4.0 * dot_tn(down_act[...], low_three[...])
    for index in range(width // LANES):
        sums_ref[pl.ds(down * width // LANES + index * down, down), :] = raise_sum[
            :, index * LANES : (index + 1) * LANES
        ].astype(low)
    down_sum = dot_tn(low_two[...], down_grad[...])
    for index in range(down // LANES):
        sums_ref[index * width : (index + 1) * width, :] = down_sum[
            :, index * LANES : (index + 1) * LANES
        ].astype(low)

    save(sums_ref, sums_out)

    def feed_backward(step, carry):
        which = tiles - 1 - step
        slot = lax.rem(which, 2)
        here = rows_of(which, tile)

        @pl.when(which < tiles - 2)
        def _():
            wout_load(which).wait()
            win_load(which).wait()

        grad = dot_nt(low_three[...], wout[slot]) * slopes[:, here].astype(f32)
        total[...] += dot_nt(grad.astype(low), win[slot])

        @pl.when(which >= 2)
        def _():
            win_load(which - 2).start()
            wout_load(which - 2).start()

        return carry

    lax.fori_loop(0, tiles, feed_backward, 0)

    def down_back(here):
        total[:, here] += dot_nt(down_grad[...], wd[here, :])

    by_columns(width, cols, down_back)

    def second_back(here, carry):
        gain_sum, shift_sum = carry
        grad = total[here, :]
        unit = unit_two[here, :]
        back = norm_back(grad * gain_ref[1:2, :], scale_two[here, :], unit)
        total[here, :] = back
        low_one[here, :] = back.astype(low)
        return (
            gain_sum + jnp.sum(grad * unit, axis=0, keepdims=True),
            shift_sum + jnp.sum(grad, axis=0, keepdims=True),
        )

    gain_two, shift_two = by_rows(second_back, (nothing, nothing))

    def crossed_back(here):
        crossed[:, here] = dot_nt(low_one[...], wco[here, :]).astype(low)

    by_columns(width, cols, crossed_back)

    def cross_backward(block):
        here = rows_of(block, LANES)
        values = mvalue_ref[:, here]
        keys = mkey_ref[:, here].astype(f32).T.astype(low)
        grads = crossed[:, here].astype(f32)
        outs = []
        key_sum = None
        for head in range(per_block):
            grad = jnp.where(head_lanes(grads.shape, head), grads, 0.0).astype(low)
            weight_low = weights[block * per_block + head]
            weight = weight_low.astype(f32)
            slope = dot_nt(values, grad)
            slope = weight * (slope - jnp.sum(weight * slope, axis=0, keepdims=True))
            slope = slope.astype(low)
            key_part = dot_nn(slope, head_queries(here, head))
            value_part = dot_nn(weight_low, grad)
            if key_sum is None:
                key_sum, value_sum = key_part, value_part
            else:
                key_sum, value_sum = key_sum + key_part, value_sum + value_part
            outs.append(dot_nn(keys[head * HD : (head + 1) * HD, :], slope))
        mkey_ref[:, here] = key_sum.astype(low)
        mvalue_ref[:, here] = value_sum.astype(low)
        query[:, here] = (jnp.concatenate(outs, axis=0) * 0.125).T.astype(low)

    def cross_backward_step(block, carry):
        cross_backward(block)
        return carry

    lax.fori_loop(0, width // LANES, cross_backward_step, 0)
    save(mkey_ref, mkey_out)
    save(mvalue_ref, mvalue_out)

    def query_back(here):
        total[:, here] += dot_nt(query[...], wcq[here, :])

    by_columns(width, cols, query_back)

    def first_back(here, carry):
        gain_sum, shift_sum = carry
        grad = total[here, :]
        unit = unit_one[here, :]
        back = norm_back(grad * gain_ref[0:1, :], scale_one[here, :], unit)
        fgrad_ref[here, :] = back
        low_one[here, :] = back.astype(low)
        return (
            gain_sum + jnp.sum(grad * unit, axis=0, keepdims=True),
            shift_sum + jnp.sum(grad, axis=0, keepdims=True),
        )

    gain_one, shift_one = by_rows(first_back, (nothing, nothing))

    def out_back(here):
        ograd_ref[here, :] = dot_nt(low_one[...], wo[here, :]).T.astype(low)

    by_columns(width, cols, out_back)
    for index, vector in enumerate(
        (gain_one, gain_two, gain_three, shift_one, shift_two, shift_three)
    ):
        vecs_ref[2 + index : 3 + index, :] = vector
    for copy in saves:
        copy.wait()


def middle(
    tokens, attended, cotangent, mem_key, mem_value, gains, shifts, down_bias, raise_bias, weights
):
    length, width = tokens.shape
    mem_len = mem_key.shape[0]
    down = weights[3].shape[1]
    feed = weights[5].shape[1]
    tile = 512 if mem_len <= 512 else 128
    low = jnp.bfloat16
    f32 = jnp.float32
    vmem = pl.BlockSpec(memory_space=pltpu.VMEM)
    anywhere = pl.BlockSpec(memory_space=pl.ANY)
    square = pltpu.VMEM((width, width), low)
    wide = pltpu.VMEM((length, width), f32)
    narrow = pltpu.VMEM((length, width), low)
    return pl.pallas_call(
        middle_kernel,
        out_shape=(
            jax.ShapeDtypeStruct((length, width), low),
            jax.ShapeDtypeStruct((length, width), f32),
            jax.ShapeDtypeStruct((width, length), low),
            jax.ShapeDtypeStruct((mem_len, width), low),
            jax.ShapeDtypeStruct((mem_len, width), low),
            jax.ShapeDtypeStruct((2 * down * width // LANES, LANES), low),
            jax.ShapeDtypeStruct((8, width), f32),
        ),
        in_specs=[anywhere] * 5 + [vmem] * 4 + [anywhere] * 7,
        out_specs=(anywhere, vmem, vmem, anywhere, anywhere, anywhere, vmem),
        scratch_shapes=[
            narrow,
            narrow,
            narrow,
            pltpu.VMEM((mem_len, width), low),
            pltpu.VMEM((mem_len, width), low),
            narrow,
            pltpu.VMEM((2 * down * width // LANES, LANES), low),
            square,
            square,
            square,
            pltpu.VMEM((width, down), low),
            pltpu.VMEM((down, width), low),
            pltpu.VMEM((2, width, tile), low),
            pltpu.VMEM((2, tile, width), low),
            wide,
            wide,
            wide,
            wide,
            pltpu.VMEM((length, 1), f32),
            pltpu.VMEM((length, 1), f32),
            narrow,
            narrow,
            narrow,
            narrow,
            narrow,
            pltpu.VMEM((H, mem_len, length), low),
            pltpu.VMEM((length, feed), low),
            pltpu.VMEM((length, down), low),
            pltpu.VMEM((length, down), low),
            pltpu.VMEM((length, down), low),
            pltpu.SemaphoreType.DMA((10,)),
            pltpu.SemaphoreType.DMA((2,)),
            pltpu.SemaphoreType.DMA((2,)),
            pltpu.SemaphoreType.DMA((4,)),
        ],
        compiler_params=pltpu.CompilerParams(vmem_limit_bytes=VMEM_BYTES + (0 if mem_len <= 512 else 3 * 1024 * 1024)),
        name="middle",
    )(tokens, attended, cotangent, mem_key, mem_value, gains, shifts, down_bias, raise_bias, *weights)


def per_device(
    tokens,
    memory,
    segment_ids,
    padding_mask,
    cotangent,
    prefix_embed,
    prefix_first,
    first_bias,
    prefix_second,
    second_bias,
    adapter_down,
    down_bias,
    adapter_raise,
    raise_bias,
    norm_gain,
    norm_shift,
    self_query,
    self_key,
    self_value,
    self_output,
    cross_query,
    cross_key,
    cross_value,
    cross_output,
    feed_in,
    feed_out,
):
    row_count, length, model_width = tokens.shape
    flat_rows = row_count * length
    n = lax.axis_size("seq")
    batches = lax.axis_size("batch")
    down = adapter_down.shape[1]
    attended, mem_key, mem_value, *saved = self_forward(
        n,
        segment_ids,
        padding_mask,
        tokens.reshape(flat_rows, model_width),
        (self_query, self_key, self_value),
        (
            prefix_embed,
            prefix_first,
            first_bias.reshape(1, -1),
            prefix_second,
            second_bias.reshape(1, -1),
        ),
        memory.reshape(-1, model_width),
        (cross_key, cross_value),
    )
    layer_output, first_grad, out_grad, *mem_grads, weight_sums, vector_sums = middle(
        tokens.reshape(flat_rows, model_width),
        attended,
        cotangent.reshape(flat_rows, model_width),
        mem_key,
        mem_value,
        norm_gain,
        norm_shift,
        down_bias.reshape(1, -1),
        raise_bias.reshape(1, -1),
        (
            self_output,
            cross_query,
            cross_output,
            adapter_down,
            adapter_raise,
            feed_in,
            feed_out,
        ),
    )
    layer_output = layer_output.reshape(row_count, length, model_width)
    token_grad, memory_grad, prefix_grad, vector_sums, full_sums = self_backward(
        n,
        batches,
        first_grad,
        out_grad.reshape(n, -1, HD, length),
        weight_sums,
        mem_grads,
        (cross_key, cross_value),
        vector_sums,
        saved,
        (self_query, self_key, self_value),
    )
    *replicated, token_grad, memory_grad = finish(
        full_sums.reshape(-1, LANES),
        vector_sums,
        prefix_grad,
        prefix_embed,
        prefix_first,
        first_bias.reshape(1, -1),
        prefix_second,
        down,
        token_grad,
        memory_grad,
    )
    token_grad = token_grad.reshape(row_count, length, model_width)
    memory_grad = memory_grad.reshape(memory.shape)
    replicated = [
        value.reshape(-1) if value.shape[0] == 1 else value for value in replicated
    ]
    return (layer_output, token_grad, memory_grad, *replicated)


def solution(mesh):
    placed = (
        P("batch", "seq", None),
        P("batch", "seq", None),
        P("batch", "seq"),
        P("batch", "seq"),
        P("batch", "seq", None),
        P(),
        P(),
        P(),
        P(),
        P(),
        P(),
        P(),
        P(),
        P(),
        P(),
        P(),
        P(),
        P(),
        P(),
        P(),
        P(),
        P(),
        P(),
        P(),
        P(),
        P(),
    )
    return jax.shard_map(
        per_device,
        mesh=mesh,
        in_specs=placed,
        out_specs=(
            P("batch", "seq", None),
            P("batch", "seq", None),
            P("batch", "seq", None),
            P(),
            P(),
            P(),
            P(),
            P(),
            P(),
            P(),
            P(),
            P(),
            P(),
            P(),
        ),
        check_vma=False,
    )
```

```python
import functools

import jax
import jax.numpy as jnp
from jax import lax
from jax.experimental import pallas as pl
from jax.experimental.pallas import tpu as pltpu
from jax.sharding import PartitionSpec as P

H = 16
HD = 64
LANES = 128
PREFIX_ROWS = 32
VMEM_BYTES = 60 * 1024 * 1024
SUM_ROWS = 16
MESH = pl.DeviceIdType.MESH

masked_score = -1e30
norm_eps = 1e-05

def dot_nn(left, right):
    return lax.dot_general(
        left, right, (((1,), (0,)), ((), ())), preferred_element_type=jnp.float32
    )


def dot_nt(left, right):
    return lax.dot_general(
        left, right, (((1,), (1,)), ((), ())), preferred_element_type=jnp.float32
    )


def dot_tn(left, right):
    return lax.dot_general(
        left, right, (((0,), (0,)), ((), ())), preferred_element_type=jnp.float32
    )


def remote(source, target, send_sem, recv_sem, axis, peer):
    return pltpu.make_async_remote_copy(
        src_ref=source,
        dst_ref=target,
        send_sem=send_sem,
        recv_sem=recv_sem,
        device_id={axis: peer},
        device_id_type=MESH,
    )


def enter(sizes):
    barrier = pltpu.get_barrier_semaphore()
    for axis, size in sizes.items():
        for other in range(size):

            @pl.when(other != lax.axis_index(axis))
            def _():
                pl.semaphore_signal(barrier, inc=1, device_id={axis: other}, device_id_type=MESH)

    pl.semaphore_wait(barrier, sum(sizes.values()) - len(sizes))


def others(size, mine, body):
    for other in range(size):

        @pl.when(other != mine)
        def _():
            body(other)


def rows_of(index, size):
    return pl.ds(pl.multiple_of(index * size, size), size)


def span_of(start, size):
    return pl.ds(pl.multiple_of(start, LANES), size)


def own_columns(ref, first, me, width):
    if width % LANES == 0:
        return ref[:, pl.ds(pl.multiple_of(first + me * width, LANES), width)].astype(jnp.float32)
    share = LANES // width
    block = ref[:, pl.ds(pl.multiple_of(first + me // share * LANES, LANES), LANES)].astype(
        jnp.float32
    )
    picked = block[:, :width]
    for part in range(1, share):
        picked = jnp.where(me % share == part, block[:, part * width : (part + 1) * width], picked)
    return picked


def head_lanes(shape, head):
    lane = lax.broadcasted_iota(jnp.int32, shape, 1)
    return (lane >= head * HD) & (lane < (head + 1) * HD)


def self_forward_kernel(
    n,
    seg_ref,
    pad_ref,
    tok_ref,
    wq_in,
    wk_in,
    wv_in,
    emb_ref,
    first_in,
    fbias_ref,
    second_in,
    sbias_ref,
    mem_ref,
    wck_in,
    wcv_in,
    att_ref,
    mkey_ref,
    mvalue_ref,
    qx_out,
    kx_out,
    raw_out,
    pk_out,
    pv_out,
    pkt_out,
    ot_out,
    lse_out,
    send,
    recv,
    meta_send,
    meta,
    kx,
    qx,
    vt,
    hidden,
    pk,
    pv,
    pkt,
    pvt,
    stat,
    acc,
    o_send,
    o_recv,
    mem_all,
    wck,
    wcv,
    wq_ref,
    wk_ref,
    wv_ref,
    first_ref,
    second_ref,
    send_sem,
    recv_sem,
    meta_send_sem,
    meta_recv_sem,
    o_send_sem,
    o_recv_sem,
    mem_send_sem,
    mem_recv_sem,
    out_sem,
    weight_sem,
    in_sem,
):
    low = jnp.bfloat16
    f32 = jnp.float32
    me = lax.axis_index("seq")
    length, width = tok_ref.shape
    group = width // n
    heads = group // HD
    plane = 2 * length
    planes = n // 2
    block = 2 * LANES
    per_block = block // group
    blocks = width // block
    step_rows = 256
    steps = plane // step_rows
    my_plane = me // 2
    my_side = lax.rem(me, 2)

    def meta_copy(peer, slot):
        return remote(
            meta_send, meta.at[slot], meta_send_sem.at[peer], meta_recv_sem.at[slot], "seq", peer
        )

    def qkv_copy(head, peer, slot):
        return remote(
            send.at[peer, head],
            recv.at[head, slot],
            send_sem.at[head, peer],
            recv_sem.at[head, slot],
            "seq",
            peer,
        )

    def out_copy(head, peer, slot):
        return remote(
            o_send.at[head, peer],
            o_recv.at[slot, head],
            o_send_sem.at[head, peer],
            o_recv_sem.at[head, slot],
            "seq",
            peer,
        )

    def mem_along(which, toward):
        part = mem_all.at[which, my_side]
        return remote(
            part,
            part,
            mem_send_sem.at[(toward + 1) // 2, which],
            mem_recv_sem.at[which],
            "seq",
            me + 2 * toward,
        )

    def mem_across(side):
        part = mem_all.at[:, side]
        return remote(
            part,
            part,
            mem_send_sem.at[0, planes],
            mem_recv_sem.at[planes],
            "seq",
            me + 1 - 2 * my_side,
        )

    def mem_hops(hop, body):
        for toward in (1, -1):
            which = my_plane - toward * hop
            ahead = my_plane + toward

            @pl.when((which >= 0) & (which < planes) & (ahead >= 0) & (ahead < planes))
            def _():
                body(mem_along(which, toward))

    def mem_arrivals(hop):
        for toward in (1, -1):
            which = my_plane - toward * hop

            @pl.when((which >= 0) & (which < planes))
            def _():
                mem_along(which, -toward).wait_recv()

    def block_at(step):
        if blocks >= planes:
            share = blocks // planes
            return lax.rem(my_plane + 1 + step // share, planes) * share + step % share
        return lax.rem(me // per_block + 1 + step, blocks)

    def weight_load(step, which):
        columns = rows_of(block_at(step), block)
        source = (wq_in, wk_in, wv_in)[which]
        target = (wq_ref, wk_ref, wv_ref)[which]
        return pltpu.make_async_copy(
            source.at[:, columns], target.at[:, columns], weight_sem.at[step, which]
        )

    for step in range(blocks):
        for which in range(3):
            weight_load(step, which).start()
    loads = [
        pltpu.make_async_copy(source, target, in_sem.at[index])
        for index, (source, target) in enumerate(
            ((first_in, first_ref), (second_in, second_ref), (wck_in, wck), (wcv_in, wcv))
        )
    ]
    for load in loads:
        load.start()
    segments = seg_ref[...]
    tags = jnp.where(pad_ref[...] == 1, segments, -1)
    row = lax.broadcasted_iota(jnp.int32, meta_send.shape, 0)
    meta_send[...] = jnp.where(row == 0, segments, tags)
    mem_all[my_plane, my_side] = mem_ref[...]
    enter({"seq": n})
    others(n, me, lambda peer: meta_copy(peer, me).start())
    meta[me] = meta_send[...]

    for step in range(blocks):
        at = block_at(step)
        columns = rows_of(at, block)
        for which, weight in enumerate((wq_ref, wk_ref, wv_ref)):
            weight_load(step, which).wait()
            piece = dot_nn(tok_ref[...], weight[:, columns]).T.astype(low)
            for part in range(per_block):
                for head in range(heads):
                    first = part * group + head * HD
                    send[at * per_block + part, head, which] = piece[first : first + HD]
        for part in range(per_block):
            peer = at * per_block + part

            @pl.when(peer != me)
            def _():
                qkv_copy(0, peer, me).start()

            @pl.when(peer == me)
            def _():
                for head in range(heads):
                    recv[head, me] = send[peer, head]

    mem_hops(0, lambda copy: copy.start())

    loads[0].wait()
    loads[1].wait()
    hidden[...] = jnp.zeros_like(hidden)
    hidden[: emb_ref.shape[0], :] = jnp.tanh(dot_nn(emb_ref[...], first_ref[...]) + fbias_ref[...])
    hidden_low = hidden[...].astype(low)
    prefix_key = dot_nn(hidden_low, own_columns(second_ref, 0, me, group).astype(low)) + own_columns(
        sbias_ref, 0, me, group
    )
    prefix_value = dot_nn(
        hidden_low, own_columns(second_ref, width, me, group).astype(low)
    ) + own_columns(sbias_ref, width, me, group)
    prefix_row = lax.broadcasted_iota(jnp.int32, (PREFIX_ROWS, HD), 0)
    prefix_open = jnp.where(prefix_row < emb_ref.shape[0], 0.0, masked_score)
    for head in range(heads):
        here = slice(head * HD, (head + 1) * HD)
        pk[head] = jnp.concatenate([prefix_key[:, here], prefix_open], axis=1).astype(low)
        pv[head] = prefix_value[:, here].astype(low)
    pkt[...] = prefix_key.T.astype(low).reshape(heads, HD, PREFIX_ROWS)
    pvt[:, :HD, :] = prefix_value.T.astype(low).reshape(heads, HD, PREFIX_ROWS)
    pvt[:, HD:, :] = jnp.ones((heads, SUM_ROWS, PREFIX_ROWS), low)
    vt[:, HD:, :] = jnp.ones((heads, SUM_ROWS, n * length), low)

    def arrive(head, chunk):
        @pl.when(chunk != me)
        def _():
            @pl.when(head == 0)
            def _():
                meta_copy(chunk, chunk).wait_recv()

            qkv_copy(head, chunk, chunk).wait_recv()

        here = rows_of(chunk, length)
        state = lax.broadcasted_iota(jnp.int32, (HD, length), 0)
        qx[head, :HD, here] = (recv[head, chunk, 0].astype(f32) * 0.125).astype(low)
        qx[head, HD:, here] = jnp.where(state == meta[chunk, 0:1, :], 1.0, 0.0).astype(low)
        is_open = jnp.where(state == meta[chunk, 1:2, :], 0.0, masked_score)
        kx[head, here, :] = jnp.concatenate(
            [recv[head, chunk, 1].astype(f32), is_open], axis=0
        ).T.astype(low)
        vt[head, :HD, here] = recv[head, chunk, 2]

    def open_plane(head, which):
        scores = dot_nn(pk[head], qx[head, :, rows_of(which, plane)])
        top = jnp.max(scores, axis=0, keepdims=True)
        raised = jnp.exp(scores - top)
        stat[which, head, 0:1, :] = top
        acc[which, head] = dot_nn(pvt[head], raised.astype(low))

    def pair_part(head, upper, lower, first, keys, diagonal):
        here = slice(first, first + step_rows)
        queries = qx[head, :, span_of(upper * plane + first, step_rows)]
        key_rows = span_of(lower * plane, keys)
        scores = dot_nn(kx[head, key_rows, :], queries)
        if diagonal:
            key_at = lax.broadcasted_iota(jnp.int32, scores.shape, 0)
            query_at = lax.broadcasted_iota(jnp.int32, scores.shape, 1) + first
            scores = jnp.where(key_at <= query_at, scores, masked_score)
        old_top = stat[upper, head, 0:1, here]
        top = jnp.maximum(old_top, jnp.max(scores, axis=0, keepdims=True))
        raised = jnp.exp(scores - top).astype(low)
        stat[upper, head, 0:1, here] = top
        acc[upper, head, :, here] = acc[upper, head, :, here] * jnp.exp(old_top - top) + dot_nn(
            vt[head, :, key_rows], raised
        )

    def pair(head, upper, lower):
        for part in range(steps):
            pair_part(head, upper, lower, part * step_rows, plane, False)

    def pair_diagonal(head, which):
        for part in range(steps):
            pair_part(head, which, which, part * step_rows, (part + 1) * step_rows, True)

    def close_plane(head, which):
        total = acc[which, head, HD : HD + 1, :]
        value = acc[which, head, :HD, :] / total
        acc[which, head, :HD, :] = value
        stat[which, head, 0:1, :] = stat[which, head, 0:1, :] + jnp.log(total)
        for part in range(2):
            chunk = 2 * which + part
            o_send[head, chunk] = value[:, part * length : (part + 1) * length].astype(low)

            @pl.when(chunk != me)
            def _():
                out_copy(head, chunk, me).start()

            @pl.when(chunk == me)
            def _():
                o_recv[me, head] = o_send[head, chunk]

    def project_memory():
        mem_across(1 - my_side).wait_recv()
        for load in loads[2:]:
            load.wait()
        whole = mem_all[...].reshape(mkey_ref.shape)

        def one(index, carry):
            here = rows_of(index, block)
            mkey_ref[:, here] = dot_nn(whole, wck[:, here]).astype(low)
            mvalue_ref[:, here] = dot_nn(whole, wcv[:, here]).astype(low)
            return carry

        lax.fori_loop(0, blocks, one, 0)

    def stage(index, carry):
        head = index // planes
        step = lax.rem(index, planes)

        @pl.when(head + 1 < heads)
        def _():
            there = lax.rem(my_plane + 1 + step, planes)
            for part in range(2):
                peer = 2 * there + part

                @pl.when(peer != me)
                def _():
                    qkv_copy(head, peer, me).wait_send()
                    qkv_copy(head + 1, peer, me).start()

        here = lax.rem(my_plane + step, planes)
        arrive(head, 2 * here)
        arrive(head, 2 * here + 1)
        open_plane(head, here)
        pair_diagonal(head, here)

        def earlier(back, inner):
            there = lax.rem(my_plane + back, planes)
            pair(head, jnp.maximum(here, there), jnp.minimum(here, there))

            @pl.when((step == planes - 1) & (there > here))
            def _():
                close_plane(head, there)

            return inner

        lax.fori_loop(0, step, earlier, 0)
        for hop in range(1, planes - 1):

            @pl.when(index == hop)
            def _():
                mem_arrivals(hop)
                mem_hops(hop, lambda copy: copy.start())

        @pl.when(index == planes - 1)
        def _():
            mem_arrivals(planes - 1)
            mem_across(my_side).start()

        @pl.when((my_plane + step >= planes) | (my_plane == 0))
        def _():
            close_plane(head, here)

        return carry

    lax.fori_loop(0, heads * planes, stage, 0)

    saves = []

    def save(source, target):
        copy = pltpu.make_async_copy(source, target, out_sem.at[len(saves)])
        copy.start()
        saves.append(copy)

    save(qx, qx_out)
    save(kx, kx_out)
    save(recv, raw_out)
    save(pk, pk_out)
    save(pv, pv_out)
    save(pkt, pkt_out)
    save(acc, ot_out)
    save(stat, lse_out)
    project_memory()
    for other in range(n):

        @pl.when(other != me)
        def _():
            for head in range(heads):
                out_copy(head, other, other).wait_recv()

        att_ref[:, other * group : (other + 1) * group] = (
            o_recv[other].reshape(group, length).astype(f32).T.astype(low)
        )

    def drain(peer):
        meta_copy(peer, me).wait_send()
        qkv_copy(heads - 1, peer, me).wait_send()
        for head in range(heads):
            out_copy(head, peer, me).wait_send()

    others(n, me, drain)
    for hop in range(planes - 1):
        mem_hops(hop, lambda copy: copy.wait_send())
    mem_across(my_side).wait_send()
    for copy in saves:
        copy.wait()


def self_forward(n, segments, padding, tokens, weights, prefix, memory, mem_weights):
    length, width = tokens.shape
    group = width // n
    heads = group // HD
    whole = n * length
    planes = n // 2
    low = jnp.bfloat16
    f32 = jnp.float32
    vmem = pl.BlockSpec(memory_space=pltpu.VMEM)
    anywhere = pl.BlockSpec(memory_space=pl.ANY)
    dma = pltpu.SemaphoreType.DMA
    shapes = (
        ((heads, 2 * HD, whole), low),
        ((heads, whole, 2 * HD), low),
        ((heads, n, 3, HD, length), low),
        ((heads, PREFIX_ROWS, 2 * HD), low),
        ((heads, PREFIX_ROWS, HD), low),
        ((heads, HD, PREFIX_ROWS), low),
        ((planes, heads, HD + SUM_ROWS, 2 * length), f32),
        ((planes, heads, 8, 2 * length), f32),
    )
    square = pltpu.VMEM((width, width), low)
    qx, kx, raw, pk, pv, pkt, acc, stat = (pltpu.VMEM(*shape) for shape in shapes)
    return pl.pallas_call(
        functools.partial(self_forward_kernel, n),
        out_shape=(
            jax.ShapeDtypeStruct((length, width), low),
            jax.ShapeDtypeStruct((n * memory.shape[0], width), low),
            jax.ShapeDtypeStruct((n * memory.shape[0], width), low),
        )
        + tuple(jax.ShapeDtypeStruct(*shape) for shape in shapes),
        in_specs=[vmem] * 3
        + [anywhere] * 3
        + [vmem, anywhere, vmem, anywhere, vmem, vmem]
        + [anywhere] * 2,
        out_specs=(vmem,) * 3 + (anywhere,) * 8,
        scratch_shapes=[
            pltpu.VMEM((n, heads, 3, HD, length), low),
            raw,
            pltpu.VMEM((8, length), jnp.int32),
            pltpu.VMEM((n, 8, length), jnp.int32),
            kx,
            qx,
            pltpu.VMEM((heads, HD + SUM_ROWS, whole), low),
            pltpu.VMEM((PREFIX_ROWS, weights[0].shape[0] // 2), f32),
            pk,
            pv,
            pkt,
            pltpu.VMEM((heads, HD + SUM_ROWS, PREFIX_ROWS), low),
            stat,
            acc,
            pltpu.VMEM((heads, n, HD, length), low),
            pltpu.VMEM((n, heads, HD, length), low),
            pltpu.VMEM((planes, 2) + memory.shape, low),
            square,
            square,
            square,
            square,
            square,
            pltpu.VMEM(prefix[1].shape, low),
            pltpu.VMEM(prefix[3].shape, low),
            dma((heads, n)),
            dma((heads, n)),
            dma((n,)),
            dma((n,)),
            dma((heads, n)),
            dma((heads, n)),
            dma((2, planes + 1)),
            dma((planes + 1,)),
            dma((8,)),
            dma((width // (2 * LANES), 3)),
            dma((4,)),
        ],
        compiler_params=pltpu.CompilerParams(
            collective_id=0, has_side_effects=True, vmem_limit_bytes=VMEM_BYTES
        ),
        name="self_forward",
    )(segments, padding, tokens, *weights, *prefix, memory, *mem_weights)


def self_backward_kernel(
    n,
    batches,
    base_in,
    do_in,
    sums_in,
    mkey_in,
    mvalue_in,
    wck_in,
    wcv_in,
    vecs_in,
    qx_in,
    kx_in,
    raw_in,
    pk_in,
    pv_in,
    pkt_in,
    ot_in,
    lse_in,
    wq_in,
    wk_in,
    wv_in,
    tg_ref,
    mgrad_ref,
    pkv_ref,
    vecs_ref,
    full_out,
    do_recv,
    qx,
    kx,
    raw,
    kt,
    values,
    dot,
    qdo,
    pk,
    pv,
    pkt,
    ot,
    stat,
    weights,
    dqt,
    dkv,
    g_send,
    g_recv,
    pre_ref,
    pre_all,
    pre_sum,
    pre_recv,
    sums_mine,
    sums_core,
    sums_x,
    sums_side,
    sums_z,
    full,
    mkey,
    mvalue,
    wck,
    wcv,
    mem_part,
    mem_side,
    mem_up,
    mem_down,
    vec_all,
    vec_sum,
    vec_y,
    vec_both,
    vec_z,
    product,
    base_ref,
    do_send_sem,
    do_recv_sem,
    g_send_sem,
    g_recv_sem,
    in_sem,
    send_sem,
    recv_sem,
):
    low = jnp.bfloat16
    f32 = jnp.float32
    me = lax.axis_index("seq")
    length, width = tg_ref.shape
    group = width // n
    heads = group // HD
    plane = 2 * length
    planes = n // 2
    step_rows = 256
    my_batch = lax.axis_index("batch")
    my_core = lax.rem(my_batch, 2)
    my_high = my_batch // 2
    highs = batches // 2
    my_plane = me // 2
    my_side = lax.rem(me, 2)
    beside = me + 1 - 2 * my_side
    used = [0]

    def numbers(count):
        used[0] += count
        return used[0] - count

    core_slot = numbers(2)
    x_slot = numbers(2 * highs)
    y_slot = numbers(3)
    z_slot = numbers(2 * planes)
    up_slot = numbers(planes)
    down_slot = numbers(planes)
    va_slot = numbers(batches)
    vb_slot = numbers(1)
    vc_slot = numbers(planes)
    pa_slot = numbers(batches)
    pb_slot = numbers(n)

    def send(source, target, first, peer_index, slot_index, axis, peer):
        return remote(
            source,
            target,
            send_sem.at[first + peer_index],
            recv_sem.at[first + slot_index],
            axis,
            peer,
        )

    half_rows = 2 * planes * highs * sums_z.shape[1]
    x_rows = half_rows // highs
    y_rows = x_rows // 2
    z_rows = y_rows // planes
    x_row = pl.multiple_of(my_high * x_rows, x_rows)
    y_row = pl.multiple_of(x_row + my_side * y_rows, y_rows)

    def part(row, count):
        return sums_mine.at[pl.ds(pl.multiple_of(row, count), count)]

    def reduce_core():
        return send(
            sums_in.at[1 - my_core], sums_core, core_slot, 0, 0, "batch", my_batch + 1 - 2 * my_core
        )

    def reduce_x(peer, slot):
        return send(
            part(peer * x_rows, x_rows),
            sums_x.at[slot],
            x_slot,
            peer,
            slot,
            "batch",
            2 * peer + my_core,
        )

    def reduce_y():
        return send(
            part(x_row + (1 - my_side) * y_rows, y_rows), sums_side, y_slot, 0, 0, "seq", beside
        )

    def reduce_z(peer, slot):
        return send(
            part(y_row + peer * z_rows, z_rows),
            sums_z.at[slot],
            z_slot,
            peer,
            slot,
            "seq",
            2 * peer + my_side,
        )

    def gather_z(peer, slot):
        piece = full.at[my_core, my_high, my_side, slot]
        return send(piece, piece, z_slot + planes, peer, slot, "seq", 2 * peer + my_side)

    def gather_y(side):
        piece = full.at[my_core, my_high, side]
        return send(piece, piece, y_slot + 1, 0, 0, "seq", beside)

    def gather_x(peer, slot):
        piece = full.at[my_core, slot]
        return send(piece, piece, x_slot + highs, peer, slot, "batch", 2 * peer + my_core)

    def gather_core(core):
        piece = full.at[core]
        return send(piece, piece, core_slot + 1, 0, 0, "batch", my_batch + 1 - 2 * my_core)

    def mem_across():
        return send(
            mem_part.at[:, 1 - my_side], mem_side, y_slot + 2, 0, 0, "seq", beside
        )

    def mem_hop(target, toward, peer=None):
        buffer, slot = (mem_up, up_slot) if toward > 0 else (mem_down, down_slot)
        return send(
            mem_part.at[target, my_side],
            buffer.at[target],
            slot,
            target,
            target,
            "seq",
            me + 2 * toward if peer is None else peer,
        )

    def mem_from(target, toward):
        return mem_hop(target, toward, me - 2 * toward)

    def mem_pass(toward):
        buffer = mem_up if toward > 0 else mem_down
        first = 0 if toward > 0 else planes - 1
        for target in range(planes):

            @pl.when((target - my_plane) * toward > 0)
            def _():
                @pl.when(my_plane != first)
                def _():
                    mem_from(target, toward).wait_recv()
                    mem_part[target, my_side] = (
                        mem_part[target, my_side].astype(f32) + buffer[target].astype(f32)
                    ).astype(low)

                mem_hop(target, toward).start()

    def mem_stage(at):
        pl.when(my_plane == at)(lambda: mem_pass(1))
        pl.when(my_plane == planes - 1 - at)(lambda: mem_pass(-1))

    def mem_end():
        value = mem_part[my_plane, my_side].astype(f32)
        mgrad_ref[...] = value.astype(low)

        @pl.when(my_plane > 0)
        def _():
            mem_from(my_plane, 1).wait_recv()
            mgrad_ref[...] = (mgrad_ref[...].astype(f32) + mem_up[my_plane].astype(f32)).astype(low)

        @pl.when(my_plane < planes - 1)
        def _():
            mem_from(my_plane, -1).wait_recv()
            mgrad_ref[...] = (
                mgrad_ref[...].astype(f32) + mem_down[my_plane].astype(f32)
            ).astype(low)

    def mem_drain():
        for target in range(planes):

            @pl.when(target > my_plane)
            def _():
                mem_hop(target, 1).wait_send()

            @pl.when(target < my_plane)
            def _():
                mem_hop(target, -1).wait_send()

    def vec_a(peer, slot):
        return send(vecs_in, vec_all.at[slot], va_slot, peer, slot, "batch", peer)

    def vec_b(side):
        return send(vec_sum, vec_y.at[side], vb_slot, 0, 0, "seq", beside)

    def vec_c(peer, slot):
        return send(vec_both, vec_z.at[slot], vc_slot, peer, slot, "seq", 2 * peer + my_side)

    def pre_a(peer, slot):
        return send(pre_ref, pre_all.at[slot], pa_slot, peer, slot, "batch", peer)

    def pre_b(peer, slot):
        return send(pre_sum, pre_recv.at[slot], pb_slot, peer, slot, "seq", peer)

    def do_copy(head, peer, slot):
        return remote(
            do_in.at[peer, head],
            do_recv.at[head, slot],
            do_send_sem.at[head, peer],
            do_recv_sem.at[head, slot],
            "seq",
            peer,
        )

    def q_copy(head, peer, slot):
        return remote(
            g_send.at[peer, head, 0],
            g_recv.at[0, slot, head],
            g_send_sem.at[0, head, peer],
            g_recv_sem.at[0, head, slot],
            "seq",
            peer,
        )

    def kv_copy(head, peer, slot):
        return remote(
            g_send.at[peer, head, pl.ds(1, 2)],
            g_recv.at[pl.ds(1, 2), slot, head],
            g_send_sem.at[1, head, peer],
            g_recv_sem.at[1, head, slot],
            "seq",
            peer,
        )

    def added(ref, size):
        value = ref[0].astype(f32)
        for other in range(1, size):
            value = value + ref[other].astype(f32)
        return value

    loads = [
        pltpu.make_async_copy(source, target, in_sem.at[index])
        for index, (source, target) in enumerate(
            (
                (raw_in, raw),
                (kx_in, kx),
                (pk_in, pk),
                (pv_in, pv),
                (pkt_in, pkt),
                (qx_in, qx),
                (ot_in, ot),
                (lse_in, stat),
                (sums_in.at[my_core], sums_mine),
                (vecs_in, vec_all.at[my_batch]),
                (mkey_in, mkey),
                (mvalue_in, mvalue),
                (wck_in, wck),
                (wcv_in, wcv),
                (base_in, base_ref),
                (wq_in, weights.at[0]),
                (wk_in, weights.at[1]),
                (wv_in, weights.at[2]),
            )
        )
    ]
    own_do = pltpu.make_async_copy(do_in.at[me], do_recv.at[:, me], in_sem.at[len(loads)])
    own_do.start()
    for load in loads:
        load.start()
    enter({"seq": n, "batch": batches})
    others(n, me, lambda peer: do_copy(0, peer, me).start())
    reduce_core().start()
    others(batches, my_batch, lambda peer: vec_a(peer, my_batch).start())
    dkv[...] = jnp.zeros_like(dkv)
    product[...] = jnp.zeros_like(product)
    pre_ref[...] = jnp.zeros_like(pre_ref)
    for load in loads[:14]:
        load.wait()
    own_do.wait()

    def turn(index, carry):
        head = index // n
        chunk = lax.rem(index, n)
        here = rows_of(chunk, length)
        kt[head, :, here] = raw[head, chunk, 1]
        values[head, here, :] = raw[head, chunk, 2].astype(f32).T.astype(low)
        return carry

    lax.fori_loop(0, heads * n, turn, 0)

    def memory_back(index, carry):
        here = rows_of(index, step_rows)
        value = dot_nt(mkey[...], wck[here, :]) + dot_nt(mvalue[...], wcv[here, :])
        mem_part[:, :, :, here] = value.astype(low).reshape(mem_part.shape[:3] + (step_rows,))
        return carry

    lax.fori_loop(0, width // step_rows, memory_back, 0)
    mem_across().start()

    def next_head(head):
        def move(peer):
            do_copy(head, peer, me).wait_send()
            do_copy(head + 1, peer, me).start()

        others(n, me, move)

    def arrive(head, which):
        for part in range(2):
            chunk = 2 * which + part

            @pl.when(chunk != me)
            def _():
                do_copy(head, chunk, chunk).wait_recv()

            grads = do_recv[head, chunk]
            dot[head, :, rows_of(chunk, length)] = grads
            grads = grads.astype(f32)
            query = raw[head, chunk, 0].astype(f32) * 0.125
            qdo[head, rows_of(chunk, length), :] = (
                jnp.concatenate([query, grads], axis=0).T.astype(low)
            )
            here = slice(part * length, (part + 1) * length)
            stat[which, head, 1:2, here] = jnp.sum(
                grads * ot[which, head, :HD, here], axis=0, keepdims=True
            )
        here = rows_of(which, plane)
        weight = jnp.exp(dot_nn(pk[head], qx[head, :, here]) - stat[which, head, 0:1, :])
        slope = weight * (dot_nn(pv[head], dot[head, :, here]) - stat[which, head, 1:2, :])
        both = jnp.concatenate([slope, weight], axis=0).astype(low)
        sums = dot_nn(both, qdo[head, here, :])
        pre_ref[head] += jnp.where(
            head_lanes((PREFIX_ROWS, 2 * HD), 0), sums[:PREFIX_ROWS], sums[PREFIX_ROWS:]
        )
        slope = slope.astype(low)
        dqt[which, head] = dot_nn(pkt[head], slope)

    def plus(first, second):
        return (first.astype(f32) + second.astype(f32)).astype(low)

    def sum_one():
        reduce_core().wait_recv()
        sums_mine[...] = plus(sums_mine[...], sums_core[...])
        others(highs, my_high, lambda peer: reduce_x(peer, my_high).start())

    def sum_two():
        here = pl.ds(x_row, x_rows)
        others(highs, my_high, lambda peer: reduce_x(peer, peer).wait_recv())
        sums_x[my_high] = sums_mine[here]
        sums_mine[here] = added(sums_x, highs).astype(low)
        reduce_y().start()

    def sum_three():
        here = pl.ds(y_row, y_rows)
        reduce_y().wait_recv()
        sums_mine[here] = plus(sums_mine[here], sums_side[...])
        others(planes, my_plane, lambda peer: reduce_z(peer, my_plane).start())

    def sum_four():
        here = pl.ds(pl.multiple_of(y_row + my_plane * z_rows, z_rows), z_rows)
        others(planes, my_plane, lambda peer: reduce_z(peer, peer).wait_recv())
        sums_z[my_plane] = sums_mine[here]
        full[my_core, my_high, my_side, my_plane] = added(sums_z, planes).astype(low)
        others(planes, my_plane, lambda peer: gather_z(peer, my_plane).start())

    def sum_five():
        others(planes, my_plane, lambda peer: gather_z(peer, peer).wait_recv())
        gather_y(my_side).start()

    def sum_six():
        gather_y(1 - my_side).wait_recv()
        others(highs, my_high, lambda peer: gather_x(peer, my_high).start())

    def sum_seven():
        others(highs, my_high, lambda peer: gather_x(peer, peer).wait_recv())
        gather_core(my_core).start()

    def sum_end():
        gather_core(1 - my_core).wait_recv()
        save_full.start()

    def vec_one():
        others(batches, my_batch, lambda peer: vec_a(peer, peer).wait_recv())
        vec_sum[...] = added(vec_all, batches)
        vec_b(my_side).start()
        vec_y[my_side] = vec_sum[...]

    def vec_two():
        vec_b(1 - my_side).wait_recv()
        value = (vec_y[0] + vec_y[1]).astype(f32)
        vec_both[...] = jnp.concatenate(
            [value[:, : width // 2], value[:, width // 2 :]], axis=0
        ).astype(low)
        others(planes, my_plane, lambda peer: vec_c(peer, my_plane).start())
        vec_z[my_plane] = vec_both[...]

    def vec_end():
        others(planes, my_plane, lambda peer: vec_c(peer, peer).wait_recv())
        value = added(vec_z, planes)
        vecs_ref[:, : width // 2] = value[:8]
        vecs_ref[:, width // 2 :] = value[8:]

    def mem_one():
        mem_across().wait_recv()
        mem_part[:, my_side] = plus(mem_part[:, my_side], mem_side[...])

    def stage_pa():
        others(batches, my_batch, lambda peer: pre_a(peer, my_batch).start())
        pre_all[my_batch] = pre_ref[...]

    def stage_pb():
        others(batches, my_batch, lambda peer: pre_a(peer, peer).wait_recv())
        pre_sum[...] = added(pre_all, batches).astype(low)
        others(n, me, lambda peer: pre_b(peer, me).start())
        pre_recv[me] = pre_sum[...]

    save_full = pltpu.make_async_copy(full, full_out, in_sem.at[0])

    def pair_part(head, upper, lower, first, count, diagonal):
        keys = span_of(lower * plane + first, count)
        here = span_of(upper * plane + first, plane - first)
        at = slice(first, plane)
        scores = dot_nn(kx[head, keys, :], qx[head, :, here])
        slope = dot_nn(values[head, keys, :], dot[head, :, here]) - stat[upper, head, 1:2, at]
        weight = jnp.exp(scores - stat[upper, head, 0:1, at])
        if diagonal:
            key_at = lax.broadcasted_iota(jnp.int32, scores.shape, 0)
            query_at = lax.broadcasted_iota(jnp.int32, scores.shape, 1)
            weight = jnp.where(key_at <= query_at, weight, 0.0)
        both = jnp.concatenate([(weight * slope).astype(low), weight.astype(low)], axis=0)
        sums = dot_nn(both, qdo[head, here, :])
        dkv[head, keys, :] += jnp.where(
            head_lanes((count, 2 * HD), 0), sums[:count], sums[count:]
        )
        dqt[upper, head, :, at] += dot_nn(kt[head, :, keys], both[:count])

    def pair(head, upper, lower, diagonal):
        if diagonal:
            pair_part(head, upper, lower, 0, length, True)
            pair_part(head, upper, lower, length, length, True)
        else:
            pair_part(head, upper, lower, 0, plane, False)

    def hand_queries(head, which):
        for part in range(2):
            chunk = 2 * which + part
            g_send[chunk, head, 0] = (
                dqt[which, head, :, part * length : (part + 1) * length] * 0.125
            ).astype(low)

            @pl.when(chunk != me)
            def _():
                q_copy(head, chunk, me).start()

            @pl.when(chunk == me)
            def _():
                g_recv[0, me, head] = g_send[chunk, head, 0]

    def hand_keys(head, which):
        for part in range(2):
            chunk = 2 * which + part
            turned = dkv[head, rows_of(chunk, length), :].T.astype(low)
            g_send[chunk, head, 1] = turned[:HD]
            g_send[chunk, head, 2] = turned[HD:]

            @pl.when(chunk != me)
            def _():
                kv_copy(head, chunk, me).start()

            @pl.when(chunk == me)
            def _():
                g_recv[pl.ds(1, 2), me, head] = g_send[chunk, head, pl.ds(1, 2)]

    rising = my_plane >= planes // 2
    total = heads * planes * (planes + 1) // 2
    hooks = [
        (2, sum_one),
        (3, mem_one),
        (4, lambda: mem_stage(0)),
        (5, vec_one),
        (5, sum_two),
        (7, sum_three),
        (8, vec_two),
        (10, sum_four),
        (12, sum_five),
        (14, sum_six),
        (16, vec_end),
        (17, sum_seven),
    ] + [(4 + 3 * at, functools.partial(mem_stage, at)) for at in range(1, planes - 1)]
    hooks += [
        (1 + head * total // heads, functools.partial(next_head, head)) for head in range(heads - 1)
    ]
    final = total - planes * (planes + 1) // 2
    hooks += [(final + planes + 1, stage_pa), (final + 2 * planes - 1, stage_pb)]

    def hook(pairs):
        for number, body in sorted(hooks, key=lambda item: item[0]):
            pl.when(pairs == number)(body)


    def stage(index, carry):
        head = index // planes
        step = lax.rem(index, planes)
        here = jnp.where(rising, step, planes - 1 - step)

        @pl.when((step == 0) | ((step == 1) & jnp.logical_not(rising)))
        def _():
            @pl.when(rising | (step == 0))
            def _():
                arrive(head, here)

            @pl.when(jnp.logical_not(rising) & (step == 1))
            def _():
                def rest(which, inner):
                    arrive(head, planes - 2 - which)
                    return inner

                lax.fori_loop(0, planes - 1, rest, 0)

        begun = head * (planes * (planes + 1) // 2) + step * planes - step * (step - 1) // 2
        hook(begun)
        pair(head, here, here, True)

        @pl.when(rising)
        def _():
            hand_queries(head, here)

        @pl.when(jnp.logical_not(rising))
        def _():
            hand_keys(head, here)

        def far(at, inner):
            there = jnp.where(rising, here + 1 + at, here - 1 - at)

            @pl.when(rising & (step == 0))
            def _():
                arrive(head, there)

            hook(begun + 1 + at)
            pair(head, jnp.maximum(here, there), jnp.minimum(here, there), False)
            return inner

        lax.fori_loop(0, planes - 1 - step, far, 0)

        @pl.when(rising)
        def _():
            hand_keys(head, here)

        @pl.when(jnp.logical_not(rising))
        def _():
            hand_queries(head, here)

        return carry

    lax.fori_loop(0, heads * planes, stage, 0)
    mem_end()
    for load in loads[14:]:
        load.wait()

    def gathered(peer):
        for head in range(heads):
            q_copy(head, peer, peer).wait_recv()
            kv_copy(head, peer, peer).wait_recv()

    half = width // 2

    def gather_plane(step, carry):
        which = lax.rem(my_plane + step, planes)
        for part in range(2):
            peer = 2 * which + part

            @pl.when(peer != me)
            def _():
                gathered(peer)

        columns = rows_of(which, 2 * group)
        for part in range(2):
            here = slice(part * half, (part + 1) * half)
            value = product[here, :]
            for kind in range(3):
                grads = g_recv[kind, pl.ds(2 * which, 2)].reshape(2 * group, length)
                value = value + dot_nn(weights[kind, here, columns], grads)
            product[here, :] = value
        return carry

    lax.fori_loop(0, planes, gather_plane, 0)
    sum_end()
    tile = 256
    for index in range(width // tile):
        here = slice(index * tile, (index + 1) * tile)
        tg_ref[:, here] = (base_ref[:, here] + product[here, :].T).astype(low)
    for other in range(n):

        @pl.when(other != me)
        def _():
            pre_b(other, other).wait_recv()

        value = pre_recv[other].astype(f32)
        for which in range(2):
            pkv_ref[:, which * width + other * group : which * width + (other + 1) * group] = (
                jnp.concatenate(
                    [value[head, :, which * HD : (which + 1) * HD] for head in range(heads)], axis=1
                )
            )

    def drain(peer):
        do_copy(heads - 1, peer, me).wait_send()
        pre_b(peer, me).wait_send()
        for head in range(heads):
            q_copy(head, peer, me).wait_send()
            kv_copy(head, peer, me).wait_send()

    others(n, me, drain)
    others(batches, my_batch, lambda peer: pre_a(peer, my_batch).wait_send())
    others(batches, my_batch, lambda peer: vec_a(peer, my_batch).wait_send())
    reduce_core().wait_send()
    others(highs, my_high, lambda peer: reduce_x(peer, my_high).wait_send())
    reduce_y().wait_send()
    others(planes, my_plane, lambda peer: reduce_z(peer, my_plane).wait_send())
    others(planes, my_plane, lambda peer: gather_z(peer, my_plane).wait_send())
    gather_y(my_side).wait_send()
    others(highs, my_high, lambda peer: gather_x(peer, my_high).wait_send())
    gather_core(my_core).wait_send()
    mem_across().wait_send()
    mem_drain()
    others(planes, my_plane, lambda peer: vec_c(peer, my_plane).wait_send())
    vec_b(my_side).wait_send()
    save_full.wait()


def self_backward(
    n, batches, first_grad, out_grad, sums, mem_grads, mem_weights, vecs, saved, weights
):
    length, width = first_grad.shape
    group = width // n
    heads = group // HD
    whole = n * length
    planes = n // 2
    low = jnp.bfloat16
    f32 = jnp.float32
    vmem = pl.BlockSpec(memory_space=pltpu.VMEM)
    anywhere = pl.BlockSpec(memory_space=pl.ANY)
    dma = pltpu.SemaphoreType.DMA
    sum_rows = sums.shape[0] // (n * batches)
    mem_len = mem_grads[0].shape[0]
    mem_rows = mem_len // n
    mem_part = pltpu.VMEM((planes, mem_rows, width), low)
    mem_low = pltpu.VMEM((mem_len, width), low)
    square = pltpu.VMEM((width, width), low)
    vec = pltpu.VMEM((8, width), f32)
    copies = 6 + 2 * (batches // 2) + 5 * planes + 2 * batches + n
    qx, kx, raw, pk, pv, pkt, ot, stat = (pltpu.VMEM(value.shape, value.dtype) for value in saved)
    return pl.pallas_call(
        functools.partial(self_backward_kernel, n, batches),
        out_shape=(
            jax.ShapeDtypeStruct((length, width), low),
            jax.ShapeDtypeStruct((mem_rows, width), low),
            jax.ShapeDtypeStruct((PREFIX_ROWS, 2 * width), f32),
            jax.ShapeDtypeStruct((8, width), f32),
            jax.ShapeDtypeStruct((2, batches // 2, 2, planes, sum_rows, LANES), low),
        ),
        in_specs=[anywhere] * 19,
        out_specs=(vmem, vmem, vmem, vmem, anywhere),
        scratch_shapes=[
            pltpu.VMEM((heads, n, HD, length), low),
            qx,
            kx,
            raw,
            pltpu.VMEM((heads, HD, whole), low),
            pltpu.VMEM((heads, whole, HD), low),
            pltpu.VMEM((heads, HD, whole), low),
            pltpu.VMEM((heads, whole, 2 * HD), low),
            pk,
            pv,
            pkt,
            ot,
            stat,
            pltpu.VMEM((3, width, width), low),
            pltpu.VMEM((planes, heads, HD, 2 * length), f32),
            pltpu.VMEM((heads, whole, 2 * HD), f32),
            pltpu.VMEM((n, heads, 3, HD, length), low),
            pltpu.VMEM((3, n, heads, HD, length), low),
            pltpu.VMEM((heads, PREFIX_ROWS, 2 * HD), f32),
            pltpu.VMEM((batches, heads, PREFIX_ROWS, 2 * HD), f32),
            pltpu.VMEM((heads, PREFIX_ROWS, 2 * HD), low),
            pltpu.VMEM((n, heads, PREFIX_ROWS, 2 * HD), low),
            pltpu.VMEM((sums.shape[0] // 2, LANES), low),
            pltpu.VMEM((sums.shape[0] // 2, LANES), low),
            pltpu.VMEM((batches // 2, sums.shape[0] // batches, LANES), low),
            pltpu.VMEM((planes * sum_rows, LANES), low),
            pltpu.VMEM((planes, sum_rows, LANES), low),
            pltpu.VMEM((2, batches // 2, 2, planes, sum_rows, LANES), low),
            mem_low,
            mem_low,
            square,
            square,
            pltpu.VMEM((planes, 2, mem_rows, width), low),
            mem_part,
            mem_part,
            mem_part,
            pltpu.VMEM((batches, 8, width), f32),
            vec,
            pltpu.VMEM((2, 8, width), f32),
            pltpu.VMEM((16, width // 2), low),
            pltpu.VMEM((planes, 16, width // 2), low),
            pltpu.VMEM((width, length), f32),
            pltpu.VMEM((length, width), f32),
            dma((heads, n)),
            dma((heads, n)),
            dma((2, heads, n)),
            dma((2, heads, n)),
            dma((19,)),
            dma((copies,)),
            dma((copies,)),
        ],
        compiler_params=pltpu.CompilerParams(
            collective_id=1, has_side_effects=True, vmem_limit_bytes=VMEM_BYTES
        ),
        name="self_backward",
    )(
        first_grad,
        out_grad,
        sums.reshape(2, -1, LANES),
        *mem_grads,
        *mem_weights,
        vecs,
        *saved,
        *weights,
    )


def both_parts(value):
    high = value.astype(jnp.bfloat16).astype(jnp.float32)
    return jnp.concatenate([high, value - high], axis=0).astype(jnp.bfloat16)


def finish_kernel(
    full_in,
    vecs_ref,
    pkv_ref,
    emb_ref,
    first_in,
    fbias_ref,
    second_in,
    token_in,
    mem_in,
    embed_out,
    first_out,
    fbias_out,
    second_out,
    sbias_out,
    down_out,
    dbias_out,
    raise_out,
    rbias_out,
    gain_out,
    shift_out,
    token_out,
    mem_out,
    full_ref,
    first_ref,
    second_ref,
    token_ref,
    mem_ref,
    first_grad,
    second_grad,
    down_grad,
    raise_grad,
    emb,
    hidden,
    out_sem,
    in_sem,
):
    f32 = jnp.float32
    low = jnp.bfloat16
    width = emb_ref.shape[1]
    down = dbias_out.shape[1]
    count = emb_ref.shape[0]
    first = down * width // LANES
    loads = [
        pltpu.make_async_copy(source, target, in_sem.at[index])
        for index, (source, target) in enumerate(
            (
                (full_in.at[first:], full_ref.at[first:]),
                (full_in.at[:first], full_ref.at[:first]),
                (first_in, first_ref),
                (second_in, second_ref),
                (token_in, token_ref),
                (mem_in, mem_ref),
            )
        )
    ]
    for load in loads:
        load.start()
    saves = []

    def save(source, target, rows=None):
        if rows is not None:
            source, target = source.at[rows], target.at[rows]
        copy = pltpu.make_async_copy(source, target, out_sem.at[len(saves)])
        copy.start()
        saves.append(copy)

    loads[0].wait()
    for index in range(width // LANES):
        raise_grad[:, index * LANES : (index + 1) * LANES] = full_ref[
            first + index * down : first + (index + 1) * down, :
        ].astype(f32)
    save(raise_grad, raise_out)
    loads[1].wait()
    for index in range(down // LANES):
        down_grad[:, index * LANES : (index + 1) * LANES] = full_ref[
            index * width : (index + 1) * width, :
        ].astype(f32)
    save(down_grad, down_out)
    for load in loads[4:]:
        load.wait()
    save(token_ref, token_out)
    save(mem_ref, mem_out)
    loads[2].wait()
    emb[...] = jnp.zeros_like(emb)
    emb[:count, :] = emb_ref[...].astype(f32)
    emb_low = emb[...].astype(low)
    row = lax.broadcasted_iota(jnp.int32, hidden.shape, 0)
    hidden[...] = jnp.where(
        row < count, jnp.tanh(dot_nn(emb_low, first_ref[...]) + fbias_ref[...]), 0.0
    )
    value = hidden[...]
    prefix = pkv_ref[...]
    parts = both_parts(prefix)
    hidden_twice = jnp.concatenate([value, value], axis=0).T.astype(low)
    tile = 128
    for index in range(second_grad.shape[0] // tile):
        here = slice(index * tile, (index + 1) * tile)
        second_grad[here, :] = dot_nn(hidden_twice[here, :], parts)
        save(second_grad, second_out, here)
    sbias_out[...] = jnp.sum(prefix, axis=0, keepdims=True)
    loads[3].wait()
    grad = dot_nt(parts, second_ref[...])
    grad = (grad[:PREFIX_ROWS] + grad[PREFIX_ROWS:]) * (1.0 - value * value)
    fbias_out[...] = jnp.sum(grad, axis=0, keepdims=True)
    parts = both_parts(grad)
    emb_twice = jnp.concatenate([emb[...], emb[...]], axis=0).T.astype(low)
    first_grad[...] = dot_nn(emb_twice, parts)
    save(first_grad, first_out)
    back = dot_nt(parts, first_ref[...])
    embed_out[...] = (back[:PREFIX_ROWS] + back[PREFIX_ROWS:])[:count, :]
    rbias_out[...] = vecs_ref[0:1, :]
    dbias_out[...] = vecs_ref[1:2, :down]
    gain_out[...] = vecs_ref[2:5, :]
    shift_out[...] = vecs_ref[5:8, :]
    for copy in saves:
        copy.wait()


def finish(full, vecs, prefix_grad, embed, first, first_bias, second, down, token_grad, memory_grad):
    f32 = jnp.float32
    count, width = embed.shape
    hidden = first.shape[1]
    vmem = pl.BlockSpec(memory_space=pltpu.VMEM)
    anywhere = pl.BlockSpec(memory_space=pl.ANY)
    shapes = (
        (count, width),
        (width, hidden),
        (1, hidden),
        (hidden, 2 * width),
        (1, 2 * width),
        (width, down),
        (1, down),
        (down, width),
        (1, width),
        (3, width),
        (3, width),
    )
    return pl.pallas_call(
        finish_kernel,
        out_shape=tuple(jax.ShapeDtypeStruct(shape, f32) for shape in shapes)
        + tuple(
            jax.ShapeDtypeStruct(value.shape, value.dtype) for value in (token_grad, memory_grad)
        ),
        in_specs=[anywhere, vmem, vmem, vmem, anywhere, vmem, anywhere, anywhere, anywhere],
        out_specs=(
            vmem,
            anywhere,
            vmem,
            anywhere,
            vmem,
            anywhere,
            vmem,
            anywhere,
            vmem,
            vmem,
            vmem,
            anywhere,
            anywhere,
        ),
        scratch_shapes=[
            pltpu.VMEM(full.shape, jnp.bfloat16),
            pltpu.VMEM(first.shape, jnp.bfloat16),
            pltpu.VMEM(second.shape, jnp.bfloat16),
            pltpu.VMEM(token_grad.shape, token_grad.dtype),
            pltpu.VMEM(memory_grad.shape, memory_grad.dtype),
            pltpu.VMEM((width, hidden), f32),
            pltpu.VMEM((hidden, 2 * width), f32),
            pltpu.VMEM((width, down), f32),
            pltpu.VMEM((down, width), f32),
            pltpu.VMEM((PREFIX_ROWS, width), f32),
            pltpu.VMEM((PREFIX_ROWS, hidden), f32),
            pltpu.SemaphoreType.DMA((5 + hidden // 128,)),
            pltpu.SemaphoreType.DMA((6,)),
        ],
        compiler_params=pltpu.CompilerParams(vmem_limit_bytes=VMEM_BYTES),
        name="finish",
    )(full, vecs, prefix_grad, embed, first, first_bias, second, token_grad, memory_grad)


def gelu_pair(value):
    size = jnp.abs(value)
    step = 1.0 / (1.0 + (0.3275911 * 0.7071067811865476) * size)
    bell = jnp.exp(-0.5 * value * value)
    poly = step * (
        0.127414796
        + step
        * (-0.142248368 + step * (0.7107068705 + step * (-0.7265760135 + step * 0.5307027145)))
    )
    act = jnp.maximum(value, 0.0) - size * (poly * bell)
    turn = bell * (0.3989422804014327 * size - poly)
    return act, jnp.where(value >= 0.0, 1.0 + turn, -turn)


def normed(value):
    center = jnp.mean(value, axis=-1, keepdims=True)
    centered = value - center
    scale = lax.rsqrt(jnp.mean(centered * centered, axis=-1, keepdims=True) + norm_eps)
    return centered * scale, scale


def norm_back(grad, scale, unit):
    return scale * (
        grad
        - jnp.mean(grad, axis=-1, keepdims=True)
        - unit * jnp.mean(grad * unit, axis=-1, keepdims=True)
    )


def middle_kernel(
    tok_in,
    att_in,
    cot_in,
    mkey_in,
    mvalue_in,
    gain_ref,
    shift_ref,
    dbias_ref,
    rbias_ref,
    wo_in,
    wcq_in,
    wco_in,
    wd_in,
    wr_in,
    win_in,
    wout_in,
    layer_out,
    fgrad_ref,
    ograd_ref,
    mkey_out,
    mvalue_out,
    sums_out,
    vecs_ref,
    tok_ref,
    att_ref,
    cot_ref,
    mkey_ref,
    mvalue_ref,
    out_ref,
    sums_ref,
    wo,
    wcq,
    wco,
    wd,
    wr,
    win,
    wout,
    unit_one,
    unit_two,
    work,
    total,
    scale_one,
    scale_two,
    low_one,
    low_two,
    low_three,
    query,
    crossed,
    weights,
    slopes,
    down_act,
    down_slope,
    down_grad,
    load_sem,
    win_sem,
    wout_sem,
    out_sem,
):
    length, width = tok_ref.shape
    tile = win.shape[2]
    tiles = win_in.shape[1] // tile
    rows_step = 128
    low = jnp.bfloat16
    f32 = jnp.float32

    sources = (
        att_in,
        wo_in,
        tok_in,
        wcq_in,
        mkey_in,
        mvalue_in,
        wco_in,
        wd_in,
        wr_in,
        cot_in,
    )
    targets = (att_ref, wo, tok_ref, wcq, mkey_ref, mvalue_ref, wco, wd, wr, cot_ref)
    loads = [
        pltpu.make_async_copy(source, target, load_sem.at[index])
        for index, (source, target) in enumerate(zip(sources, targets))
    ]

    def win_load(which):
        slot = lax.rem(which, 2)
        return pltpu.make_async_copy(
            win_in.at[:, rows_of(which, tile)], win.at[slot], win_sem.at[slot]
        )

    def wout_load(which):
        slot = lax.rem(which, 2)
        return pltpu.make_async_copy(
            wout_in.at[rows_of(which, tile), :], wout.at[slot], wout_sem.at[slot]
        )

    for load in loads[:7]:
        load.start()
    for which in range(2):
        win_load(which).start()
        wout_load(which).start()
    for load in loads[7:]:
        load.start()

    def by_columns(extent, step, body):
        def one(index, carry):
            body(pl.ds(pl.multiple_of(index * step, step), step))
            return carry

        lax.fori_loop(0, extent // step, one, 0)

    def by_rows(body, init=0):
        def one(index, carry):
            return body(rows_of(index, rows_step), carry)

        return lax.fori_loop(0, length // rows_step, one, init)

    cols = 512
    half = width // 2

    for load in loads[:3]:
        load.wait()

    def project_out(here):
        work[:, here] = tok_ref[:, here].astype(f32) + dot_nn(att_ref[...], wo[:, here])

    by_columns(width, cols, project_out)

    def first_norm(here, carry):
        unit, scale = normed(work[here, :])
        unit_one[here, :] = unit
        scale_one[here, :] = scale
        value = unit * gain_ref[0:1, :] + shift_ref[0:1, :]
        work[here, :] = value
        low_one[here, :] = value.astype(low)
        return carry

    by_rows(first_norm)

    loads[3].wait()

    def project_query(here):
        query[:, here] = dot_nn(low_one[...], wcq[:, here]).astype(low)

    by_columns(width, cols, project_query)
    per_block = LANES // HD

    def head_queries(here, head):
        both = query[:, here].astype(f32) * 0.125
        return jnp.where(head_lanes(both.shape, head), both, 0.0).astype(low)

    def cross_forward(block):
        here = rows_of(block, LANES)
        keys = mkey_ref[:, here]
        values = mvalue_ref[:, here].astype(f32).T.astype(low)
        outs = []
        for head in range(per_block):
            scores = dot_nt(keys, head_queries(here, head))
            raised = jnp.exp(scores - jnp.max(scores, axis=0, keepdims=True))
            share = 1.0 / jnp.sum(raised, axis=0, keepdims=True)
            weight = (raised * share).astype(low)
            weights[block * per_block + head] = weight
            outs.append(dot_nn(values[head * HD : (head + 1) * HD, :], weight))
        crossed[:, here] = jnp.concatenate(outs, axis=0).T.astype(low)

    loads[4].wait()
    loads[5].wait()

    def cross_forward_both(step, carry):
        cross_forward(2 * step)
        cross_forward(2 * step + 1)
        return carry

    lax.fori_loop(0, width // LANES // 2, cross_forward_both, 0)

    loads[6].wait()

    def project_crossed(here):
        work[:, here] += dot_nn(crossed[...], wco[:, here])

    by_columns(width, cols, project_crossed)

    def second_norm(here, carry):
        unit, scale = normed(work[here, :])
        unit_two[here, :] = unit
        scale_two[here, :] = scale
        value = unit * gain_ref[1:2, :] + shift_ref[1:2, :]
        work[here, :] = value
        low_two[here, :] = value.astype(low)
        return carry

    by_rows(second_norm)

    total[...] = jnp.zeros_like(total)

    def feed_forward(which, carry):
        slot = lax.rem(which, 2)
        win_load(which).wait()
        wout_load(which).wait()
        act, slope = gelu_pair(dot_nn(low_two[...], win[slot]))
        slopes[:, rows_of(which, tile)] = slope.astype(low)
        total[...] += dot_nn(act.astype(low), wout[slot])

        @pl.when(which + 2 < tiles)
        def _():
            win_load(which + 2).start()
            wout_load(which + 2).start()

        return carry

    lax.fori_loop(0, tiles, feed_forward, 0)
    loads[7].wait()
    loads[8].wait()
    loads[9].wait()
    act, slope = gelu_pair(dot_nn(low_two[...], wd[...]) + dbias_ref[...])
    down_act[...] = act.astype(low)
    down_slope[...] = slope.astype(low)

    def project_raise(here):
        work[:, here] += total[:, here] + 4.0 * (
            dot_nn(down_act[...], wr[:, here]) + rbias_ref[:, here]
        )

    by_columns(width, cols, project_raise)
    nothing = jnp.zeros((1, width), f32)

    def third_norm(here, carry):
        gain_sum, shift_sum, bias_sum = carry
        unit, scale = normed(work[here, :])
        gain = gain_ref[2:3, :]
        out_ref[here, :] = (unit * gain + shift_ref[2:3, :]).astype(low)
        grad = cot_ref[here, :].astype(f32)
        back = norm_back(grad * gain, scale, unit)
        total[here, :] = back
        back_low = back.astype(low)
        low_three[here, :] = back_low
        return (
            gain_sum + jnp.sum(grad * unit, axis=0, keepdims=True),
            shift_sum + jnp.sum(grad, axis=0, keepdims=True),
            bias_sum + jnp.sum(back_low.astype(f32), axis=0, keepdims=True),
        )

    gain_three, shift_three, bias_sum = by_rows(third_norm, (nothing, nothing, nothing))
    saves = []

    def save(source, target):
        copy = pltpu.make_async_copy(source, target, out_sem.at[len(saves)])
        copy.start()
        saves.append(copy)

    save(out_ref, layer_out)
    vecs_ref[0:1, :] = 4.0 * bias_sum

    back = 4.0 * dot_nt(low_three[...], wr[...]) * down_slope[...].astype(f32)
    back_low = back.astype(low)
    down_grad[...] = back_low
    vecs_ref[1:2, :] = jnp.concatenate(
        [
            jnp.sum(back_low.astype(f32), axis=0, keepdims=True),
            jnp.zeros((1, width - wd.shape[1]), f32),
        ],
        axis=1,
    )
    down = wd.shape[1]
    raise_sum = 4.0 * dot_tn(down_act[...], low_three[...])
    for index in range(width // LANES):
        sums_ref[pl.ds(down * width // LANES + index * down, down), :] = raise_sum[
            :, index * LANES : (index + 1) * LANES
        ].astype(low)
    down_sum = dot_tn(low_two[...], down_grad[...])
    for index in range(down // LANES):
        sums_ref[index * width : (index + 1) * width, :] = down_sum[
            :, index * LANES : (index + 1) * LANES
        ].astype(low)

    save(sums_ref, sums_out)

    def feed_backward(step, carry):
        which = tiles - 1 - step
        slot = lax.rem(which, 2)
        here = rows_of(which, tile)

        @pl.when(which < tiles - 2)
        def _():
            wout_load(which).wait()
            win_load(which).wait()

        grad = dot_nt(low_three[...], wout[slot]) * slopes[:, here].astype(f32)
        total[...] += dot_nt(grad.astype(low), win[slot])

        @pl.when(which >= 2)
        def _():
            win_load(which - 2).start()
            wout_load(which - 2).start()

        return carry

    lax.fori_loop(0, tiles, feed_backward, 0)

    def down_back(here):
        total[:, here] += dot_nt(down_grad[...], wd[here, :])

    by_columns(width, cols, down_back)

    def second_back(here, carry):
        gain_sum, shift_sum = carry
        grad = total[here, :]
        unit = unit_two[here, :]
        back = norm_back(grad * gain_ref[1:2, :], scale_two[here, :], unit)
        total[here, :] = back
        low_one[here, :] = back.astype(low)
        return (
            gain_sum + jnp.sum(grad * unit, axis=0, keepdims=True),
            shift_sum + jnp.sum(grad, axis=0, keepdims=True),
        )

    gain_two, shift_two = by_rows(second_back, (nothing, nothing))

    def crossed_back(here):
        crossed[:, here] = dot_nt(low_one[...], wco[here, :]).astype(low)

    by_columns(width, cols, crossed_back)

    def cross_backward(block):
        here = rows_of(block, LANES)
        values = mvalue_ref[:, here]
        keys = mkey_ref[:, here].astype(f32).T.astype(low)
        grads = crossed[:, here].astype(f32)
        outs = []
        key_sum = None
        for head in range(per_block):
            grad = jnp.where(head_lanes(grads.shape, head), grads, 0.0).astype(low)
            weight_low = weights[block * per_block + head]
            weight = weight_low.astype(f32)
            slope = dot_nt(values, grad)
            slope = weight * (slope - jnp.sum(weight * slope, axis=0, keepdims=True))
            slope = slope.astype(low)
            key_part = dot_nn(slope, head_queries(here, head))
            value_part = dot_nn(weight_low, grad)
            if key_sum is None:
                key_sum, value_sum = key_part, value_part
            else:
                key_sum, value_sum = key_sum + key_part, value_sum + value_part
            outs.append(dot_nn(keys[head * HD : (head + 1) * HD, :], slope))
        mkey_ref[:, here] = key_sum.astype(low)
        mvalue_ref[:, here] = value_sum.astype(low)
        query[:, here] = (jnp.concatenate(outs, axis=0) * 0.125).T.astype(low)

    def cross_backward_both(step, carry):
        cross_backward(2 * step)
        cross_backward(2 * step + 1)
        return carry

    lax.fori_loop(0, width // LANES // 2, cross_backward_both, 0)
    save(mkey_ref, mkey_out)
    save(mvalue_ref, mvalue_out)

    def query_back(here):
        total[:, here] += dot_nt(query[...], wcq[here, :])

    by_columns(width, cols, query_back)

    def first_back(here, carry):
        gain_sum, shift_sum = carry
        grad = total[here, :]
        unit = unit_one[here, :]
        back = norm_back(grad * gain_ref[0:1, :], scale_one[here, :], unit)
        fgrad_ref[here, :] = back
        low_one[here, :] = back.astype(low)
        return (
            gain_sum + jnp.sum(grad * unit, axis=0, keepdims=True),
            shift_sum + jnp.sum(grad, axis=0, keepdims=True),
        )

    gain_one, shift_one = by_rows(first_back, (nothing, nothing))

    def out_back(here):
        ograd_ref[here, :] = dot_nt(low_one[...], wo[here, :]).T.astype(low)

    by_columns(width, cols, out_back)
    for index, vector in enumerate(
        (gain_one, gain_two, gain_three, shift_one, shift_two, shift_three)
    ):
        vecs_ref[2 + index : 3 + index, :] = vector
    for copy in saves:
        copy.wait()


def middle(
    tokens, attended, cotangent, mem_key, mem_value, gains, shifts, down_bias, raise_bias, weights
):
    length, width = tokens.shape
    mem_len = mem_key.shape[0]
    down = weights[3].shape[1]
    feed = weights[5].shape[1]
    tile = 512 if mem_len <= 512 else 128
    low = jnp.bfloat16
    f32 = jnp.float32
    vmem = pl.BlockSpec(memory_space=pltpu.VMEM)
    anywhere = pl.BlockSpec(memory_space=pl.ANY)
    square = pltpu.VMEM((width, width), low)
    wide = pltpu.VMEM((length, width), f32)
    narrow = pltpu.VMEM((length, width), low)
    return pl.pallas_call(
        middle_kernel,
        out_shape=(
            jax.ShapeDtypeStruct((length, width), low),
            jax.ShapeDtypeStruct((length, width), f32),
            jax.ShapeDtypeStruct((width, length), low),
            jax.ShapeDtypeStruct((mem_len, width), low),
            jax.ShapeDtypeStruct((mem_len, width), low),
            jax.ShapeDtypeStruct((2 * down * width // LANES, LANES), low),
            jax.ShapeDtypeStruct((8, width), f32),
        ),
        in_specs=[anywhere] * 5 + [vmem] * 4 + [anywhere] * 7,
        out_specs=(anywhere, vmem, vmem, anywhere, anywhere, anywhere, vmem),
        scratch_shapes=[
            narrow,
            narrow,
            narrow,
            pltpu.VMEM((mem_len, width), low),
            pltpu.VMEM((mem_len, width), low),
            narrow,
            pltpu.VMEM((2 * down * width // LANES, LANES), low),
            square,
            square,
            square,
            pltpu.VMEM((width, down), low),
            pltpu.VMEM((down, width), low),
            pltpu.VMEM((2, width, tile), low),
            pltpu.VMEM((2, tile, width), low),
            wide,
            wide,
            wide,
            wide,
            pltpu.VMEM((length, 1), f32),
            pltpu.VMEM((length, 1), f32),
            narrow,
            narrow,
            narrow,
            narrow,
            narrow,
            pltpu.VMEM((H, mem_len, length), low),
            pltpu.VMEM((length, feed), low),
            pltpu.VMEM((length, down), low),
            pltpu.VMEM((length, down), low),
            pltpu.VMEM((length, down), low),
            pltpu.SemaphoreType.DMA((10,)),
            pltpu.SemaphoreType.DMA((2,)),
            pltpu.SemaphoreType.DMA((2,)),
            pltpu.SemaphoreType.DMA((4,)),
        ],
        compiler_params=pltpu.CompilerParams(vmem_limit_bytes=VMEM_BYTES + (0 if mem_len <= 512 else 3 * 1024 * 1024)),
        name="middle",
    )(tokens, attended, cotangent, mem_key, mem_value, gains, shifts, down_bias, raise_bias, *weights)


def per_device(
    tokens,
    memory,
    segment_ids,
    padding_mask,
    cotangent,
    prefix_embed,
    prefix_first,
    first_bias,
    prefix_second,
    second_bias,
    adapter_down,
    down_bias,
    adapter_raise,
    raise_bias,
    norm_gain,
    norm_shift,
    self_query,
    self_key,
    self_value,
    self_output,
    cross_query,
    cross_key,
    cross_value,
    cross_output,
    feed_in,
    feed_out,
):
    row_count, length, model_width = tokens.shape
    flat_rows = row_count * length
    n = lax.axis_size("seq")
    batches = lax.axis_size("batch")
    down = adapter_down.shape[1]
    attended, mem_key, mem_value, *saved = self_forward(
        n,
        segment_ids,
        padding_mask,
        tokens.reshape(flat_rows, model_width),
        (self_query, self_key, self_value),
        (
            prefix_embed,
            prefix_first,
            first_bias.reshape(1, -1),
            prefix_second,
            second_bias.reshape(1, -1),
        ),
        memory.reshape(-1, model_width),
        (cross_key, cross_value),
    )
    layer_output, first_grad, out_grad, *mem_grads, weight_sums, vector_sums = middle(
        tokens.reshape(flat_rows, model_width),
        attended,
        cotangent.reshape(flat_rows, model_width),
        mem_key,
        mem_value,
        norm_gain,
        norm_shift,
        down_bias.reshape(1, -1),
        raise_bias.reshape(1, -1),
        (
            self_output,
            cross_query,
            cross_output,
            adapter_down,
            adapter_raise,
            feed_in,
            feed_out,
        ),
    )
    layer_output = layer_output.reshape(row_count, length, model_width)
    token_grad, memory_grad, prefix_grad, vector_sums, full_sums = self_backward(
        n,
        batches,
        first_grad,
        out_grad.reshape(n, -1, HD, length),
        weight_sums,
        mem_grads,
        (cross_key, cross_value),
        vector_sums,
        saved,
        (self_query, self_key, self_value),
    )
    *replicated, token_grad, memory_grad = finish(
        full_sums.reshape(-1, LANES),
        vector_sums,
        prefix_grad,
        prefix_embed,
        prefix_first,
        first_bias.reshape(1, -1),
        prefix_second,
        down,
        token_grad,
        memory_grad,
    )
    token_grad = token_grad.reshape(row_count, length, model_width)
    memory_grad = memory_grad.reshape(memory.shape)
    replicated = [
        value.reshape(-1) if value.shape[0] == 1 else value for value in replicated
    ]
    return (layer_output, token_grad, memory_grad, *replicated)


def solution(mesh):
    placed = (
        P("batch", "seq", None),
        P("batch", "seq", None),
        P("batch", "seq"),
        P("batch", "seq"),
        P("batch", "seq", None),
        P(),
        P(),
        P(),
        P(),
        P(),
        P(),
        P(),
        P(),
        P(),
        P(),
        P(),
        P(),
        P(),
        P(),
        P(),
        P(),
        P(),
        P(),
        P(),
        P(),
        P(),
    )
    return jax.shard_map(
        per_device,
        mesh=mesh,
        in_specs=placed,
        out_specs=(
            P("batch", "seq", None),
            P("batch", "seq", None),
            P("batch", "seq", None),
            P(),
            P(),
            P(),
            P(),
            P(),
            P(),
            P(),
            P(),
            P(),
            P(),
            P(),
        ),
        check_vma=False,
    )
```

```python
import functools

import jax
import jax.numpy as jnp
from jax import lax
from jax.experimental import pallas as pl
from jax.experimental.pallas import tpu as pltpu
from jax.sharding import PartitionSpec as P

H = 16
HD = 64
LANES = 128
PREFIX_ROWS = 32
VMEM_BYTES = 60 * 1024 * 1024
SUM_ROWS = 16
MESH = pl.DeviceIdType.MESH

masked_score = -1e30
norm_eps = 1e-05

def dot_nn(left, right):
    return lax.dot_general(
        left, right, (((1,), (0,)), ((), ())), preferred_element_type=jnp.float32
    )


def dot_nt(left, right):
    return lax.dot_general(
        left, right, (((1,), (1,)), ((), ())), preferred_element_type=jnp.float32
    )


def dot_tn(left, right):
    return lax.dot_general(
        left, right, (((0,), (0,)), ((), ())), preferred_element_type=jnp.float32
    )


def remote(source, target, send_sem, recv_sem, axis, peer):
    return pltpu.make_async_remote_copy(
        src_ref=source,
        dst_ref=target,
        send_sem=send_sem,
        recv_sem=recv_sem,
        device_id={axis: peer},
        device_id_type=MESH,
    )


def enter(sizes):
    barrier = pltpu.get_barrier_semaphore()
    for axis, size in sizes.items():
        for other in range(size):

            @pl.when(other != lax.axis_index(axis))
            def _():
                pl.semaphore_signal(barrier, inc=1, device_id={axis: other}, device_id_type=MESH)

    pl.semaphore_wait(barrier, sum(sizes.values()) - len(sizes))


def others(size, mine, body):
    for other in range(size):

        @pl.when(other != mine)
        def _():
            body(other)


def rows_of(index, size):
    return pl.ds(pl.multiple_of(index * size, size), size)


def span_of(start, size):
    return pl.ds(pl.multiple_of(start, LANES), size)


def own_columns(ref, first, me, width):
    if width % LANES == 0:
        return ref[:, pl.ds(pl.multiple_of(first + me * width, LANES), width)].astype(jnp.float32)
    share = LANES // width
    block = ref[:, pl.ds(pl.multiple_of(first + me // share * LANES, LANES), LANES)].astype(
        jnp.float32
    )
    picked = block[:, :width]
    for part in range(1, share):
        picked = jnp.where(me % share == part, block[:, part * width : (part + 1) * width], picked)
    return picked


def head_lanes(shape, head):
    lane = lax.broadcasted_iota(jnp.int32, shape, 1)
    return (lane >= head * HD) & (lane < (head + 1) * HD)


def self_forward_kernel(
    n,
    seg_ref,
    pad_ref,
    tok_ref,
    wq_in,
    wk_in,
    wv_in,
    emb_ref,
    first_in,
    fbias_ref,
    second_in,
    sbias_ref,
    mem_ref,
    wck_in,
    wcv_in,
    att_ref,
    mkey_out,
    mvalue_out,
    qx_out,
    kx_out,
    raw_out,
    pk_out,
    pv_out,
    pkt_out,
    ot_out,
    lse_out,
    send,
    recv,
    meta_send,
    meta,
    kx,
    qx,
    vt,
    hidden,
    pk,
    pv,
    pkt,
    pvt,
    stat,
    acc,
    o_send,
    o_recv,
    mem_all,
    wck,
    wcv,
    mkey_ref,
    mvalue_ref,
    wq_ref,
    wk_ref,
    wv_ref,
    first_ref,
    second_ref,
    send_sem,
    recv_sem,
    meta_send_sem,
    meta_recv_sem,
    o_send_sem,
    o_recv_sem,
    mem_send_sem,
    mem_recv_sem,
    out_sem,
    weight_sem,
    in_sem,
):
    low = jnp.bfloat16
    f32 = jnp.float32
    me = lax.axis_index("seq")
    length, width = tok_ref.shape
    group = width // n
    heads = group // HD
    plane = 2 * length
    planes = n // 2
    block = 2 * LANES
    per_block = block // group
    blocks = width // block
    step_rows = 256
    steps = plane // step_rows
    my_plane = me // 2
    my_side = lax.rem(me, 2)

    def meta_copy(peer, slot):
        return remote(
            meta_send, meta.at[slot], meta_send_sem.at[peer], meta_recv_sem.at[slot], "seq", peer
        )

    def qkv_copy(head, peer, slot):
        return remote(
            send.at[peer, head],
            recv.at[head, slot],
            send_sem.at[head, peer],
            recv_sem.at[head, slot],
            "seq",
            peer,
        )

    def out_copy(head, peer, slot):
        return remote(
            o_send.at[head, peer],
            o_recv.at[slot, head],
            o_send_sem.at[head, peer],
            o_recv_sem.at[head, slot],
            "seq",
            peer,
        )

    def mem_along(which, toward):
        part = mem_all.at[which, my_side]
        return remote(
            part,
            part,
            mem_send_sem.at[(toward + 1) // 2, which],
            mem_recv_sem.at[which],
            "seq",
            me + 2 * toward,
        )

    def mem_across(side):
        part = mem_all.at[:, side]
        return remote(
            part,
            part,
            mem_send_sem.at[0, planes],
            mem_recv_sem.at[planes],
            "seq",
            me + 1 - 2 * my_side,
        )

    def mem_hops(hop, body):
        for toward in (1, -1):
            which = my_plane - toward * hop
            ahead = my_plane + toward

            @pl.when((which >= 0) & (which < planes) & (ahead >= 0) & (ahead < planes))
            def _():
                body(mem_along(which, toward))

    def mem_arrivals(hop):
        for toward in (1, -1):
            which = my_plane - toward * hop

            @pl.when((which >= 0) & (which < planes))
            def _():
                mem_along(which, -toward).wait_recv()

    def block_at(step):
        if blocks >= planes:
            share = blocks // planes
            return lax.rem(my_plane + 1 + step // share, planes) * share + step % share
        return lax.rem(me // per_block + 1 + step, blocks)

    def weight_load(step, which):
        columns = rows_of(block_at(step), block)
        source = (wq_in, wk_in, wv_in)[which]
        target = (wq_ref, wk_ref, wv_ref)[which]
        return pltpu.make_async_copy(
            source.at[:, columns], target.at[:, columns], weight_sem.at[step, which]
        )

    for step in range(blocks):
        for which in range(3):
            weight_load(step, which).start()
    loads = [
        pltpu.make_async_copy(source, target, in_sem.at[index])
        for index, (source, target) in enumerate(
            ((first_in, first_ref), (second_in, second_ref), (wck_in, wck), (wcv_in, wcv))
        )
    ]
    for load in loads:
        load.start()
    segments = seg_ref[...]
    tags = jnp.where(pad_ref[...] == 1, segments, -1)
    row = lax.broadcasted_iota(jnp.int32, meta_send.shape, 0)
    meta_send[...] = jnp.where(row == 0, segments, tags)
    mem_all[my_plane, my_side] = mem_ref[...]
    enter({"seq": n})
    others(n, me, lambda peer: meta_copy(peer, me).start())
    mem_hops(0, lambda copy: copy.start())
    meta[me] = meta_send[...]

    for step in range(blocks):
        at = block_at(step)
        columns = rows_of(at, block)
        for which, weight in enumerate((wq_ref, wk_ref, wv_ref)):
            weight_load(step, which).wait()
            piece = dot_nn(tok_ref[...], weight[:, columns]).T.astype(low)
            for part in range(per_block):
                for head in range(heads):
                    first = part * group + head * HD
                    send[at * per_block + part, head, which] = piece[first : first + HD]
        for part in range(per_block):
            peer = at * per_block + part

            @pl.when(peer != me)
            def _():
                qkv_copy(0, peer, me).start()

            @pl.when(peer == me)
            def _():
                for head in range(heads):
                    recv[head, me] = send[peer, head]

    loads[0].wait()
    loads[1].wait()
    hidden[...] = jnp.zeros_like(hidden)
    hidden[: emb_ref.shape[0], :] = jnp.tanh(dot_nn(emb_ref[...], first_ref[...]) + fbias_ref[...])
    hidden_low = hidden[...].astype(low)
    prefix_key = dot_nn(hidden_low, own_columns(second_ref, 0, me, group).astype(low)) + own_columns(
        sbias_ref, 0, me, group
    )
    prefix_value = dot_nn(
        hidden_low, own_columns(second_ref, width, me, group).astype(low)
    ) + own_columns(sbias_ref, width, me, group)
    prefix_row = lax.broadcasted_iota(jnp.int32, (PREFIX_ROWS, HD), 0)
    prefix_open = jnp.where(prefix_row < emb_ref.shape[0], 0.0, masked_score)
    for head in range(heads):
        here = slice(head * HD, (head + 1) * HD)
        pk[head] = jnp.concatenate([prefix_key[:, here], prefix_open], axis=1).astype(low)
        pv[head] = prefix_value[:, here].astype(low)
    pkt[...] = prefix_key.T.astype(low).reshape(heads, HD, PREFIX_ROWS)
    pvt[:, :HD, :] = prefix_value.T.astype(low).reshape(heads, HD, PREFIX_ROWS)
    pvt[:, HD:, :] = jnp.ones((heads, SUM_ROWS, PREFIX_ROWS), low)
    vt[:, HD:, :] = jnp.ones((heads, SUM_ROWS, n * length), low)

    def arrive(head, chunk):
        @pl.when(chunk != me)
        def _():
            @pl.when(head == 0)
            def _():
                meta_copy(chunk, chunk).wait_recv()

            qkv_copy(head, chunk, chunk).wait_recv()

        here = rows_of(chunk, length)
        state = lax.broadcasted_iota(jnp.int32, (HD, length), 0)
        qx[head, :HD, here] = (recv[head, chunk, 0].astype(f32) * 0.125).astype(low)
        qx[head, HD:, here] = jnp.where(state == meta[chunk, 0:1, :], 1.0, 0.0).astype(low)
        is_open = jnp.where(state == meta[chunk, 1:2, :], 0.0, masked_score)
        kx[head, here, :] = jnp.concatenate(
            [recv[head, chunk, 1].astype(f32), is_open], axis=0
        ).T.astype(low)
        vt[head, :HD, here] = recv[head, chunk, 2]

    def open_plane(head, which):
        scores = dot_nn(pk[head], qx[head, :, rows_of(which, plane)])
        top = jnp.max(scores, axis=0, keepdims=True)
        raised = jnp.exp(scores - top)
        stat[which, head, 0:1, :] = top
        acc[which, head] = dot_nn(pvt[head], raised.astype(low))

    def pair_part(head, upper, lower, first, keys, diagonal):
        here = slice(first, first + step_rows)
        queries = qx[head, :, span_of(upper * plane + first, step_rows)]
        key_rows = span_of(lower * plane, keys)
        scores = dot_nn(kx[head, key_rows, :], queries)
        if diagonal:
            key_at = lax.broadcasted_iota(jnp.int32, scores.shape, 0)
            query_at = lax.broadcasted_iota(jnp.int32, scores.shape, 1) + first
            scores = jnp.where(key_at <= query_at, scores, masked_score)
        old_top = stat[upper, head, 0:1, here]
        top = jnp.maximum(old_top, jnp.max(scores, axis=0, keepdims=True))
        raised = jnp.exp(scores - top).astype(low)
        stat[upper, head, 0:1, here] = top
        acc[upper, head, :, here] = acc[upper, head, :, here] * jnp.exp(old_top - top) + dot_nn(
            vt[head, :, key_rows], raised
        )

    def pair(head, upper, lower):
        for part in range(steps):
            pair_part(head, upper, lower, part * step_rows, plane, False)

    def pair_diagonal(head, which):
        for part in range(steps):
            pair_part(head, which, which, part * step_rows, (part + 1) * step_rows, True)

    def close_plane(head, which):
        total = acc[which, head, HD : HD + 1, :]
        value = acc[which, head, :HD, :] / total
        acc[which, head, :HD, :] = value
        stat[which, head, 0:1, :] = stat[which, head, 0:1, :] + jnp.log(total)
        for part in range(2):
            chunk = 2 * which + part
            o_send[head, chunk] = value[:, part * length : (part + 1) * length].astype(low)

            @pl.when(chunk != me)
            def _():
                out_copy(head, chunk, me).start()

            @pl.when(chunk == me)
            def _():
                o_recv[me, head] = o_send[head, chunk]

    def project_memory():
        mem_across(1 - my_side).wait_recv()
        for load in loads[2:]:
            load.wait()
        whole = mem_all[...].reshape(mkey_ref.shape)

        def one(index, carry):
            here = rows_of(index, block)
            mkey_ref[:, here] = dot_nn(whole, wck[:, here]).astype(low)
            mvalue_ref[:, here] = dot_nn(whole, wcv[:, here]).astype(low)
            return carry

        lax.fori_loop(0, blocks, one, 0)

    def stage(index, carry):
        head = index // planes
        step = lax.rem(index, planes)

        @pl.when(head + 1 < heads)
        def _():
            there = lax.rem(my_plane + 1 + step, planes)
            for part in range(2):
                peer = 2 * there + part

                @pl.when(peer != me)
                def _():
                    qkv_copy(head, peer, me).wait_send()
                    qkv_copy(head + 1, peer, me).start()

        here = lax.rem(my_plane + step, planes)
        arrive(head, 2 * here)
        arrive(head, 2 * here + 1)
        open_plane(head, here)
        pair_diagonal(head, here)

        def earlier(back, inner):
            there = lax.rem(my_plane + back, planes)
            pair(head, jnp.maximum(here, there), jnp.minimum(here, there))

            @pl.when((step == planes - 1) & (there > here))
            def _():
                close_plane(head, there)

            return inner

        lax.fori_loop(0, step, earlier, 0)
        for hop in range(1, planes - 1):

            @pl.when(index == hop - 1)
            def _():
                mem_arrivals(hop)
                mem_hops(hop, lambda copy: copy.start())

        @pl.when(index == planes - 2)
        def _():
            mem_arrivals(planes - 1)
            mem_across(my_side).start()

        @pl.when((my_plane + step >= planes) | (my_plane == 0))
        def _():
            close_plane(head, here)

        return carry

    lax.fori_loop(0, heads * planes, stage, 0)

    saves = []

    def save(source, target):
        copy = pltpu.make_async_copy(source, target, out_sem.at[len(saves)])
        copy.start()
        saves.append(copy)

    save(qx, qx_out)
    save(kx, kx_out)
    save(recv, raw_out)
    save(pk, pk_out)
    save(pv, pv_out)
    save(pkt, pkt_out)
    save(acc, ot_out)
    save(stat, lse_out)
    project_memory()
    save(mkey_ref, mkey_out)
    save(mvalue_ref, mvalue_out)
    for other in range(n):

        @pl.when(other != me)
        def _():
            for head in range(heads):
                out_copy(head, other, other).wait_recv()

        att_ref[:, other * group : (other + 1) * group] = (
            o_recv[other].reshape(group, length).astype(f32).T.astype(low)
        )

    def drain(peer):
        meta_copy(peer, me).wait_send()
        qkv_copy(heads - 1, peer, me).wait_send()
        for head in range(heads):
            out_copy(head, peer, me).wait_send()

    others(n, me, drain)
    for hop in range(planes - 1):
        mem_hops(hop, lambda copy: copy.wait_send())
    mem_across(my_side).wait_send()
    for copy in saves:
        copy.wait()


def self_forward(n, segments, padding, tokens, weights, prefix, memory, mem_weights):
    length, width = tokens.shape
    group = width // n
    heads = group // HD
    whole = n * length
    planes = n // 2
    low = jnp.bfloat16
    f32 = jnp.float32
    vmem = pl.BlockSpec(memory_space=pltpu.VMEM)
    anywhere = pl.BlockSpec(memory_space=pl.ANY)
    dma = pltpu.SemaphoreType.DMA
    shapes = (
        ((heads, 2 * HD, whole), low),
        ((heads, whole, 2 * HD), low),
        ((heads, n, 3, HD, length), low),
        ((heads, PREFIX_ROWS, 2 * HD), low),
        ((heads, PREFIX_ROWS, HD), low),
        ((heads, HD, PREFIX_ROWS), low),
        ((planes, heads, HD + SUM_ROWS, 2 * length), f32),
        ((planes, heads, 8, 2 * length), f32),
    )
    square = pltpu.VMEM((width, width), low)
    qx, kx, raw, pk, pv, pkt, acc, stat = (pltpu.VMEM(*shape) for shape in shapes)
    return pl.pallas_call(
        functools.partial(self_forward_kernel, n),
        out_shape=(
            jax.ShapeDtypeStruct((length, width), low),
            jax.ShapeDtypeStruct((n * memory.shape[0], width), low),
            jax.ShapeDtypeStruct((n * memory.shape[0], width), low),
        )
        + tuple(jax.ShapeDtypeStruct(*shape) for shape in shapes),
        in_specs=[vmem] * 3
        + [anywhere] * 3
        + [vmem, anywhere, vmem, anywhere, vmem, vmem]
        + [anywhere] * 2,
        out_specs=(vmem,) + (anywhere,) * 10,
        scratch_shapes=[
            pltpu.VMEM((n, heads, 3, HD, length), low),
            raw,
            pltpu.VMEM((8, length), jnp.int32),
            pltpu.VMEM((n, 8, length), jnp.int32),
            kx,
            qx,
            pltpu.VMEM((heads, HD + SUM_ROWS, whole), low),
            pltpu.VMEM((PREFIX_ROWS, weights[0].shape[0] // 2), f32),
            pk,
            pv,
            pkt,
            pltpu.VMEM((heads, HD + SUM_ROWS, PREFIX_ROWS), low),
            stat,
            acc,
            pltpu.VMEM((heads, n, HD, length), low),
            pltpu.VMEM((n, heads, HD, length), low),
            pltpu.VMEM((planes, 2) + memory.shape, low),
            square,
            square,
            pltpu.VMEM((n * memory.shape[0], width), low),
            pltpu.VMEM((n * memory.shape[0], width), low),
            square,
            square,
            square,
            pltpu.VMEM(prefix[1].shape, low),
            pltpu.VMEM(prefix[3].shape, low),
            dma((heads, n)),
            dma((heads, n)),
            dma((n,)),
            dma((n,)),
            dma((heads, n)),
            dma((heads, n)),
            dma((2, planes + 1)),
            dma((planes + 1,)),
            dma((10,)),
            dma((width // (2 * LANES), 3)),
            dma((4,)),
        ],
        compiler_params=pltpu.CompilerParams(
            collective_id=0, has_side_effects=True, vmem_limit_bytes=VMEM_BYTES
        ),
        name="self_forward",
    )(segments, padding, tokens, *weights, *prefix, memory, *mem_weights)


def self_backward_kernel(
    n,
    batches,
    base_in,
    do_in,
    sums_in,
    mkey_in,
    mvalue_in,
    wck_in,
    wcv_in,
    vecs_in,
    qx_in,
    kx_in,
    raw_in,
    pk_in,
    pv_in,
    pkt_in,
    ot_in,
    lse_in,
    wq_in,
    wk_in,
    wv_in,
    tg_ref,
    mgrad_ref,
    pkv_ref,
    vecs_ref,
    full_out,
    do_recv,
    qx,
    kx,
    raw,
    kt,
    values,
    dot,
    qdo,
    pk,
    pv,
    pkt,
    ot,
    stat,
    weights,
    dqt,
    dkv,
    g_send,
    g_recv,
    pre_ref,
    pre_all,
    pre_sum,
    pre_recv,
    sums_mine,
    sums_core,
    sums_x,
    sums_side,
    sums_z,
    full,
    mkey,
    mvalue,
    wck,
    wcv,
    mem_part,
    mem_side,
    mem_up,
    mem_down,
    vec_all,
    vec_sum,
    vec_y,
    vec_both,
    vec_z,
    product,
    base_ref,
    do_send_sem,
    do_recv_sem,
    g_send_sem,
    g_recv_sem,
    in_sem,
    send_sem,
    recv_sem,
):
    low = jnp.bfloat16
    f32 = jnp.float32
    me = lax.axis_index("seq")
    length, width = tg_ref.shape
    group = width // n
    heads = group // HD
    plane = 2 * length
    planes = n // 2
    step_rows = 256
    my_batch = lax.axis_index("batch")
    my_core = lax.rem(my_batch, 2)
    my_high = my_batch // 2
    highs = batches // 2
    my_plane = me // 2
    my_side = lax.rem(me, 2)
    beside = me + 1 - 2 * my_side
    used = [0]

    def numbers(count):
        used[0] += count
        return used[0] - count

    core_slot = numbers(2)
    x_slot = numbers(2 * highs)
    y_slot = numbers(3)
    z_slot = numbers(2 * planes)
    up_slot = numbers(planes)
    down_slot = numbers(planes)
    va_slot = numbers(batches)
    vb_slot = numbers(1)
    vc_slot = numbers(planes)
    pa_slot = numbers(batches)
    pb_slot = numbers(n)

    def send(source, target, first, peer_index, slot_index, axis, peer):
        return remote(
            source,
            target,
            send_sem.at[first + peer_index],
            recv_sem.at[first + slot_index],
            axis,
            peer,
        )

    half_rows = 2 * planes * highs * sums_z.shape[1]
    x_rows = half_rows // highs
    y_rows = x_rows // 2
    z_rows = y_rows // planes
    x_row = pl.multiple_of(my_high * x_rows, x_rows)
    y_row = pl.multiple_of(x_row + my_side * y_rows, y_rows)

    def part(row, count):
        return sums_mine.at[pl.ds(pl.multiple_of(row, count), count)]

    def reduce_core():
        return send(
            sums_in.at[1 - my_core], sums_core, core_slot, 0, 0, "batch", my_batch + 1 - 2 * my_core
        )

    def reduce_x(peer, slot):
        return send(
            part(peer * x_rows, x_rows),
            sums_x.at[slot],
            x_slot,
            peer,
            slot,
            "batch",
            2 * peer + my_core,
        )

    def reduce_y():
        return send(
            part(x_row + (1 - my_side) * y_rows, y_rows), sums_side, y_slot, 0, 0, "seq", beside
        )

    def reduce_z(peer, slot):
        return send(
            part(y_row + peer * z_rows, z_rows),
            sums_z.at[slot],
            z_slot,
            peer,
            slot,
            "seq",
            2 * peer + my_side,
        )

    def gather_z(peer, slot):
        piece = full.at[my_core, my_high, my_side, slot]
        return send(piece, piece, z_slot + planes, peer, slot, "seq", 2 * peer + my_side)

    def gather_y(side):
        piece = full.at[my_core, my_high, side]
        return send(piece, piece, y_slot + 1, 0, 0, "seq", beside)

    def gather_x(peer, slot):
        piece = full.at[my_core, slot]
        return send(piece, piece, x_slot + highs, peer, slot, "batch", 2 * peer + my_core)

    def gather_core(core):
        piece = full.at[core]
        return send(piece, piece, core_slot + 1, 0, 0, "batch", my_batch + 1 - 2 * my_core)

    def mem_across():
        return send(
            mem_part.at[:, 1 - my_side], mem_side, y_slot + 2, 0, 0, "seq", beside
        )

    def mem_hop(target, toward, peer=None):
        buffer, slot = (mem_up, up_slot) if toward > 0 else (mem_down, down_slot)
        return send(
            mem_part.at[target, my_side],
            buffer.at[target],
            slot,
            target,
            target,
            "seq",
            me + 2 * toward if peer is None else peer,
        )

    def mem_from(target, toward):
        return mem_hop(target, toward, me - 2 * toward)

    def mem_pass(toward):
        buffer = mem_up if toward > 0 else mem_down
        first = 0 if toward > 0 else planes - 1
        for target in range(planes):

            @pl.when((target - my_plane) * toward > 0)
            def _():
                @pl.when(my_plane != first)
                def _():
                    mem_from(target, toward).wait_recv()
                    mem_part[target, my_side] = (
                        mem_part[target, my_side].astype(f32) + buffer[target].astype(f32)
                    ).astype(low)

                mem_hop(target, toward).start()

    def mem_stage(at):
        pl.when(my_plane == at)(lambda: mem_pass(1))
        pl.when(my_plane == planes - 1 - at)(lambda: mem_pass(-1))

    def mem_end():
        value = mem_part[my_plane, my_side].astype(f32)
        mgrad_ref[...] = value.astype(low)

        @pl.when(my_plane > 0)
        def _():
            mem_from(my_plane, 1).wait_recv()
            mgrad_ref[...] = (mgrad_ref[...].astype(f32) + mem_up[my_plane].astype(f32)).astype(low)

        @pl.when(my_plane < planes - 1)
        def _():
            mem_from(my_plane, -1).wait_recv()
            mgrad_ref[...] = (
                mgrad_ref[...].astype(f32) + mem_down[my_plane].astype(f32)
            ).astype(low)

    def mem_drain():
        for target in range(planes):

            @pl.when(target > my_plane)
            def _():
                mem_hop(target, 1).wait_send()

            @pl.when(target < my_plane)
            def _():
                mem_hop(target, -1).wait_send()

    def vec_a(peer, slot):
        return send(vecs_in, vec_all.at[slot], va_slot, peer, slot, "batch", peer)

    def vec_b(side):
        return send(vec_sum, vec_y.at[side], vb_slot, 0, 0, "seq", beside)

    def vec_c(peer, slot):
        return send(vec_both, vec_z.at[slot], vc_slot, peer, slot, "seq", 2 * peer + my_side)

    def pre_a(peer, slot):
        return send(pre_ref, pre_all.at[slot], pa_slot, peer, slot, "batch", peer)

    def pre_b(peer, slot):
        return send(pre_sum, pre_recv.at[slot], pb_slot, peer, slot, "seq", peer)

    def do_copy(head, peer, slot):
        return remote(
            do_in.at[peer, head],
            do_recv.at[head, slot],
            do_send_sem.at[head, peer],
            do_recv_sem.at[head, slot],
            "seq",
            peer,
        )

    def q_copy(head, peer, slot):
        return remote(
            g_send.at[peer, head, 0],
            g_recv.at[0, slot, head],
            g_send_sem.at[0, head, peer],
            g_recv_sem.at[0, head, slot],
            "seq",
            peer,
        )

    def kv_copy(head, peer, slot):
        return remote(
            g_send.at[peer, head, pl.ds(1, 2)],
            g_recv.at[pl.ds(1, 2), slot, head],
            g_send_sem.at[1, head, peer],
            g_recv_sem.at[1, head, slot],
            "seq",
            peer,
        )

    def added(ref, size):
        value = ref[0].astype(f32)
        for other in range(1, size):
            value = value + ref[other].astype(f32)
        return value

    loads = [
        pltpu.make_async_copy(source, target, in_sem.at[index])
        for index, (source, target) in enumerate(
            (
                (raw_in, raw),
                (kx_in, kx),
                (pk_in, pk),
                (pv_in, pv),
                (pkt_in, pkt),
                (qx_in, qx),
                (ot_in, ot),
                (lse_in, stat),
                (sums_in.at[my_core], sums_mine),
                (vecs_in, vec_all.at[my_batch]),
                (mkey_in, mkey),
                (mvalue_in, mvalue),
                (wck_in, wck),
                (wcv_in, wcv),
                (base_in, base_ref),
                (wq_in, weights.at[0]),
                (wk_in, weights.at[1]),
                (wv_in, weights.at[2]),
            )
        )
    ]
    own_do = pltpu.make_async_copy(do_in.at[me], do_recv.at[:, me], in_sem.at[len(loads)])
    own_do.start()
    for load in loads:
        load.start()
    enter({"seq": n, "batch": batches})
    others(n, me, lambda peer: do_copy(0, peer, me).start())
    reduce_core().start()
    others(batches, my_batch, lambda peer: vec_a(peer, my_batch).start())
    dkv[...] = jnp.zeros_like(dkv)
    product[...] = jnp.zeros_like(product)
    pre_ref[...] = jnp.zeros_like(pre_ref)
    for load in loads[:14]:
        load.wait()
    own_do.wait()

    def turn(index, carry):
        head = index // n
        chunk = lax.rem(index, n)
        here = rows_of(chunk, length)
        kt[head, :, here] = raw[head, chunk, 1]
        values[head, here, :] = raw[head, chunk, 2].astype(f32).T.astype(low)
        return carry

    lax.fori_loop(0, heads * n, turn, 0)

    def memory_back(index, carry):
        here = rows_of(index, step_rows)
        value = dot_nt(mkey[...], wck[here, :]) + dot_nt(mvalue[...], wcv[here, :])
        mem_part[:, :, :, here] = value.astype(low).reshape(mem_part.shape[:3] + (step_rows,))
        return carry

    lax.fori_loop(0, width // step_rows, memory_back, 0)
    mem_across().start()

    def next_head(head):
        def move(peer):
            do_copy(head, peer, me).wait_send()
            do_copy(head + 1, peer, me).start()

        others(n, me, move)

    def arrive(head, which):
        for part in range(2):
            chunk = 2 * which + part

            @pl.when(chunk != me)
            def _():
                do_copy(head, chunk, chunk).wait_recv()

            grads = do_recv[head, chunk]
            dot[head, :, rows_of(chunk, length)] = grads
            grads = grads.astype(f32)
            query = raw[head, chunk, 0].astype(f32) * 0.125
            qdo[head, rows_of(chunk, length), :] = (
                jnp.concatenate([query, grads], axis=0).T.astype(low)
            )
            here = slice(part * length, (part + 1) * length)
            stat[which, head, 1:2, here] = jnp.sum(
                grads * ot[which, head, :HD, here], axis=0, keepdims=True
            )
        here = rows_of(which, plane)
        weight = jnp.exp(dot_nn(pk[head], qx[head, :, here]) - stat[which, head, 0:1, :])
        slope = weight * (dot_nn(pv[head], dot[head, :, here]) - stat[which, head, 1:2, :])
        both = jnp.concatenate([slope, weight], axis=0).astype(low)
        sums = dot_nn(both, qdo[head, here, :])
        pre_ref[head] += jnp.where(
            head_lanes((PREFIX_ROWS, 2 * HD), 0), sums[:PREFIX_ROWS], sums[PREFIX_ROWS:]
        )
        slope = slope.astype(low)
        dqt[which, head] = dot_nn(pkt[head], slope)

    def plus(first, second):
        return (first.astype(f32) + second.astype(f32)).astype(low)

    def sum_one():
        reduce_core().wait_recv()
        sums_mine[...] = plus(sums_mine[...], sums_core[...])
        others(highs, my_high, lambda peer: reduce_x(peer, my_high).start())

    def sum_two():
        here = pl.ds(x_row, x_rows)
        others(highs, my_high, lambda peer: reduce_x(peer, peer).wait_recv())
        sums_x[my_high] = sums_mine[here]
        sums_mine[here] = added(sums_x, highs).astype(low)
        reduce_y().start()

    def sum_three():
        here = pl.ds(y_row, y_rows)
        reduce_y().wait_recv()
        sums_mine[here] = plus(sums_mine[here], sums_side[...])
        others(planes, my_plane, lambda peer: reduce_z(peer, my_plane).start())

    def sum_four():
        here = pl.ds(pl.multiple_of(y_row + my_plane * z_rows, z_rows), z_rows)
        others(planes, my_plane, lambda peer: reduce_z(peer, peer).wait_recv())
        sums_z[my_plane] = sums_mine[here]
        full[my_core, my_high, my_side, my_plane] = added(sums_z, planes).astype(low)
        others(planes, my_plane, lambda peer: gather_z(peer, my_plane).start())

    def sum_five():
        others(planes, my_plane, lambda peer: gather_z(peer, peer).wait_recv())
        gather_y(my_side).start()

    def sum_six():
        gather_y(1 - my_side).wait_recv()
        others(highs, my_high, lambda peer: gather_x(peer, my_high).start())

    def sum_seven():
        others(highs, my_high, lambda peer: gather_x(peer, peer).wait_recv())
        gather_core(my_core).start()

    def sum_end():
        gather_core(1 - my_core).wait_recv()
        save_full.start()

    def vec_one():
        others(batches, my_batch, lambda peer: vec_a(peer, peer).wait_recv())
        vec_sum[...] = added(vec_all, batches)
        vec_b(my_side).start()
        vec_y[my_side] = vec_sum[...]

    def vec_two():
        vec_b(1 - my_side).wait_recv()
        value = (vec_y[0] + vec_y[1]).astype(f32)
        vec_both[...] = jnp.concatenate(
            [value[:, : width // 2], value[:, width // 2 :]], axis=0
        ).astype(low)
        others(planes, my_plane, lambda peer: vec_c(peer, my_plane).start())
        vec_z[my_plane] = vec_both[...]

    def vec_end():
        others(planes, my_plane, lambda peer: vec_c(peer, peer).wait_recv())
        value = added(vec_z, planes)
        vecs_ref[:, : width // 2] = value[:8]
        vecs_ref[:, width // 2 :] = value[8:]

    def mem_one():
        mem_across().wait_recv()
        mem_part[:, my_side] = plus(mem_part[:, my_side], mem_side[...])

    def stage_pa():
        others(batches, my_batch, lambda peer: pre_a(peer, my_batch).start())
        pre_all[my_batch] = pre_ref[...]

    def stage_pb():
        others(batches, my_batch, lambda peer: pre_a(peer, peer).wait_recv())
        pre_sum[...] = added(pre_all, batches).astype(low)
        others(n, me, lambda peer: pre_b(peer, me).start())
        pre_recv[me] = pre_sum[...]

    save_full = pltpu.make_async_copy(full, full_out, in_sem.at[0])

    def pair_part(head, upper, lower, first, count, diagonal):
        keys = span_of(lower * plane + first, count)
        here = span_of(upper * plane + first, plane - first)
        at = slice(first, plane)
        scores = dot_nn(kx[head, keys, :], qx[head, :, here])
        slope = dot_nn(values[head, keys, :], dot[head, :, here]) - stat[upper, head, 1:2, at]
        weight = jnp.exp(scores - stat[upper, head, 0:1, at])
        if diagonal:
            key_at = lax.broadcasted_iota(jnp.int32, scores.shape, 0)
            query_at = lax.broadcasted_iota(jnp.int32, scores.shape, 1)
            weight = jnp.where(key_at <= query_at, weight, 0.0)
        both = jnp.concatenate([(weight * slope).astype(low), weight.astype(low)], axis=0)
        sums = dot_nn(both, qdo[head, here, :])
        dkv[head, keys, :] += jnp.where(
            head_lanes((count, 2 * HD), 0), sums[:count], sums[count:]
        )
        dqt[upper, head, :, at] += dot_nn(kt[head, :, keys], both[:count])

    def pair(head, upper, lower, diagonal):
        if diagonal:
            pair_part(head, upper, lower, 0, length, True)
            pair_part(head, upper, lower, length, length, True)
        else:
            pair_part(head, upper, lower, 0, plane, False)

    def hand_queries(head, which):
        for part in range(2):
            chunk = 2 * which + part
            g_send[chunk, head, 0] = (
                dqt[which, head, :, part * length : (part + 1) * length] * 0.125
            ).astype(low)

            @pl.when(chunk != me)
            def _():
                q_copy(head, chunk, me).start()

            @pl.when(chunk == me)
            def _():
                g_recv[0, me, head] = g_send[chunk, head, 0]

    def hand_keys(head, which):
        for part in range(2):
            chunk = 2 * which + part
            turned = dkv[head, rows_of(chunk, length), :].T.astype(low)
            g_send[chunk, head, 1] = turned[:HD]
            g_send[chunk, head, 2] = turned[HD:]

            @pl.when(chunk != me)
            def _():
                kv_copy(head, chunk, me).start()

            @pl.when(chunk == me)
            def _():
                g_recv[pl.ds(1, 2), me, head] = g_send[chunk, head, pl.ds(1, 2)]

    rising = my_plane >= planes // 2
    total = heads * planes * (planes + 1) // 2
    hooks = [
        (2, sum_one),
        (3, mem_one),
        (4, lambda: mem_stage(0)),
        (5, vec_one),
        (5, sum_two),
        (7, sum_three),
        (8, vec_two),
        (10, sum_four),
        (12, sum_five),
        (14, sum_six),
        (16, vec_end),
        (17, sum_seven),
    ] + [(4 + 3 * at, functools.partial(mem_stage, at)) for at in range(1, planes - 1)]
    hooks += [
        (1 + head * total // heads, functools.partial(next_head, head)) for head in range(heads - 1)
    ]
    final = total - planes * (planes + 1) // 2
    hooks += [(final + planes + 1, stage_pa), (final + 2 * planes - 1, stage_pb)]

    def hook(pairs):
        for number, body in sorted(hooks, key=lambda item: item[0]):
            pl.when(pairs == number)(body)


    def stage(index, carry):
        head = index // planes
        step = lax.rem(index, planes)
        here = jnp.where(rising, step, planes - 1 - step)

        @pl.when((step == 0) | ((step == 1) & jnp.logical_not(rising)))
        def _():
            @pl.when(rising | (step == 0))
            def _():
                arrive(head, here)

            @pl.when(jnp.logical_not(rising) & (step == 1))
            def _():
                def rest(which, inner):
                    arrive(head, planes - 2 - which)
                    return inner

                lax.fori_loop(0, planes - 1, rest, 0)

        begun = head * (planes * (planes + 1) // 2) + step * planes - step * (step - 1) // 2
        hook(begun)
        pair(head, here, here, True)

        @pl.when(rising)
        def _():
            hand_queries(head, here)

        @pl.when(jnp.logical_not(rising))
        def _():
            hand_keys(head, here)

        def far(at, inner):
            there = jnp.where(rising, here + 1 + at, here - 1 - at)

            @pl.when(rising & (step == 0))
            def _():
                arrive(head, there)

            hook(begun + 1 + at)
            pair(head, jnp.maximum(here, there), jnp.minimum(here, there), False)
            return inner

        lax.fori_loop(0, planes - 1 - step, far, 0)

        @pl.when(rising)
        def _():
            hand_keys(head, here)

        @pl.when(jnp.logical_not(rising))
        def _():
            hand_queries(head, here)

        return carry

    lax.fori_loop(0, heads * planes, stage, 0)
    mem_end()
    for load in loads[14:]:
        load.wait()

    def gathered(peer):
        for head in range(heads):
            q_copy(head, peer, peer).wait_recv()
            kv_copy(head, peer, peer).wait_recv()

    half = width // 2

    def gather_plane(step, carry):
        which = lax.rem(my_plane + step, planes)
        for part in range(2):
            peer = 2 * which + part

            @pl.when(peer != me)
            def _():
                gathered(peer)

        columns = rows_of(which, 2 * group)
        for part in range(2):
            here = slice(part * half, (part + 1) * half)
            value = product[here, :]
            for kind in range(3):
                grads = g_recv[kind, pl.ds(2 * which, 2)].reshape(2 * group, length)
                value = value + dot_nn(weights[kind, here, columns], grads)
            product[here, :] = value
        return carry

    lax.fori_loop(0, planes, gather_plane, 0)
    sum_end()
    tile = 256
    for index in range(width // tile):
        here = slice(index * tile, (index + 1) * tile)
        tg_ref[:, here] = (base_ref[:, here] + product[here, :].T).astype(low)
    for other in range(n):

        @pl.when(other != me)
        def _():
            pre_b(other, other).wait_recv()

        value = pre_recv[other].astype(f32)
        for which in range(2):
            pkv_ref[:, which * width + other * group : which * width + (other + 1) * group] = (
                jnp.concatenate(
                    [value[head, :, which * HD : (which + 1) * HD] for head in range(heads)], axis=1
                )
            )

    def drain(peer):
        do_copy(heads - 1, peer, me).wait_send()
        pre_b(peer, me).wait_send()
        for head in range(heads):
            q_copy(head, peer, me).wait_send()
            kv_copy(head, peer, me).wait_send()

    others(n, me, drain)
    others(batches, my_batch, lambda peer: pre_a(peer, my_batch).wait_send())
    others(batches, my_batch, lambda peer: vec_a(peer, my_batch).wait_send())
    reduce_core().wait_send()
    others(highs, my_high, lambda peer: reduce_x(peer, my_high).wait_send())
    reduce_y().wait_send()
    others(planes, my_plane, lambda peer: reduce_z(peer, my_plane).wait_send())
    others(planes, my_plane, lambda peer: gather_z(peer, my_plane).wait_send())
    gather_y(my_side).wait_send()
    others(highs, my_high, lambda peer: gather_x(peer, my_high).wait_send())
    gather_core(my_core).wait_send()
    mem_across().wait_send()
    mem_drain()
    others(planes, my_plane, lambda peer: vec_c(peer, my_plane).wait_send())
    vec_b(my_side).wait_send()
    save_full.wait()


def self_backward(
    n, batches, first_grad, out_grad, sums, mem_grads, mem_weights, vecs, saved, weights
):
    length, width = first_grad.shape
    group = width // n
    heads = group // HD
    whole = n * length
    planes = n // 2
    low = jnp.bfloat16
    f32 = jnp.float32
    vmem = pl.BlockSpec(memory_space=pltpu.VMEM)
    anywhere = pl.BlockSpec(memory_space=pl.ANY)
    dma = pltpu.SemaphoreType.DMA
    sum_rows = sums.shape[0] // (n * batches)
    mem_len = mem_grads[0].shape[0]
    mem_rows = mem_len // n
    mem_part = pltpu.VMEM((planes, mem_rows, width), low)
    mem_low = pltpu.VMEM((mem_len, width), low)
    square = pltpu.VMEM((width, width), low)
    vec = pltpu.VMEM((8, width), f32)
    copies = 6 + 2 * (batches // 2) + 5 * planes + 2 * batches + n
    qx, kx, raw, pk, pv, pkt, ot, stat = (pltpu.VMEM(value.shape, value.dtype) for value in saved)
    return pl.pallas_call(
        functools.partial(self_backward_kernel, n, batches),
        out_shape=(
            jax.ShapeDtypeStruct((length, width), low),
            jax.ShapeDtypeStruct((mem_rows, width), low),
            jax.ShapeDtypeStruct((PREFIX_ROWS, 2 * width), f32),
            jax.ShapeDtypeStruct((8, width), f32),
            jax.ShapeDtypeStruct((2, batches // 2, 2, planes, sum_rows, LANES), low),
        ),
        in_specs=[anywhere] * 19,
        out_specs=(vmem, vmem, vmem, vmem, anywhere),
        scratch_shapes=[
            pltpu.VMEM((heads, n, HD, length), low),
            qx,
            kx,
            raw,
            pltpu.VMEM((heads, HD, whole), low),
            pltpu.VMEM((heads, whole, HD), low),
            pltpu.VMEM((heads, HD, whole), low),
            pltpu.VMEM((heads, whole, 2 * HD), low),
            pk,
            pv,
            pkt,
            ot,
            stat,
            pltpu.VMEM((3, width, width), low),
            pltpu.VMEM((planes, heads, HD, 2 * length), f32),
            pltpu.VMEM((heads, whole, 2 * HD), f32),
            pltpu.VMEM((n, heads, 3, HD, length), low),
            pltpu.VMEM((3, n, heads, HD, length), low),
            pltpu.VMEM((heads, PREFIX_ROWS, 2 * HD), f32),
            pltpu.VMEM((batches, heads, PREFIX_ROWS, 2 * HD), f32),
            pltpu.VMEM((heads, PREFIX_ROWS, 2 * HD), low),
            pltpu.VMEM((n, heads, PREFIX_ROWS, 2 * HD), low),
            pltpu.VMEM((sums.shape[0] // 2, LANES), low),
            pltpu.VMEM((sums.shape[0] // 2, LANES), low),
            pltpu.VMEM((batches // 2, sums.shape[0] // batches, LANES), low),
            pltpu.VMEM((planes * sum_rows, LANES), low),
            pltpu.VMEM((planes, sum_rows, LANES), low),
            pltpu.VMEM((2, batches // 2, 2, planes, sum_rows, LANES), low),
            mem_low,
            mem_low,
            square,
            square,
            pltpu.VMEM((planes, 2, mem_rows, width), low),
            mem_part,
            mem_part,
            mem_part,
            pltpu.VMEM((batches, 8, width), f32),
            vec,
            pltpu.VMEM((2, 8, width), f32),
            pltpu.VMEM((16, width // 2), low),
            pltpu.VMEM((planes, 16, width // 2), low),
            pltpu.VMEM((width, length), f32),
            pltpu.VMEM((length, width), f32),
            dma((heads, n)),
            dma((heads, n)),
            dma((2, heads, n)),
            dma((2, heads, n)),
            dma((19,)),
            dma((copies,)),
            dma((copies,)),
        ],
        compiler_params=pltpu.CompilerParams(
            collective_id=1, has_side_effects=True, vmem_limit_bytes=VMEM_BYTES
        ),
        name="self_backward",
    )(
        first_grad,
        out_grad,
        sums.reshape(2, -1, LANES),
        *mem_grads,
        *mem_weights,
        vecs,
        *saved,
        *weights,
    )


def both_parts(value):
    high = value.astype(jnp.bfloat16).astype(jnp.float32)
    return jnp.concatenate([high, value - high], axis=0).astype(jnp.bfloat16)


def finish_kernel(
    full_in,
    vecs_ref,
    pkv_ref,
    emb_ref,
    first_in,
    fbias_ref,
    second_in,
    token_in,
    mem_in,
    embed_out,
    first_out,
    fbias_out,
    second_out,
    sbias_out,
    down_out,
    dbias_out,
    raise_out,
    rbias_out,
    gain_out,
    shift_out,
    token_out,
    mem_out,
    full_ref,
    first_ref,
    second_ref,
    token_ref,
    mem_ref,
    first_grad,
    second_grad,
    down_grad,
    raise_grad,
    emb,
    hidden,
    out_sem,
    in_sem,
):
    f32 = jnp.float32
    low = jnp.bfloat16
    width = emb_ref.shape[1]
    down = dbias_out.shape[1]
    count = emb_ref.shape[0]
    first = down * width // LANES
    loads = [
        pltpu.make_async_copy(source, target, in_sem.at[index])
        for index, (source, target) in enumerate(
            (
                (full_in.at[first:], full_ref.at[first:]),
                (full_in.at[:first], full_ref.at[:first]),
                (first_in, first_ref),
                (second_in, second_ref),
                (token_in, token_ref),
                (mem_in, mem_ref),
            )
        )
    ]
    for load in loads:
        load.start()
    saves = []

    def save(source, target, rows=None):
        if rows is not None:
            source, target = source.at[rows], target.at[rows]
        copy = pltpu.make_async_copy(source, target, out_sem.at[len(saves)])
        copy.start()
        saves.append(copy)

    loads[0].wait()
    for index in range(width // LANES):
        raise_grad[:, index * LANES : (index + 1) * LANES] = full_ref[
            first + index * down : first + (index + 1) * down, :
        ].astype(f32)
    save(raise_grad, raise_out)
    loads[1].wait()
    for index in range(down // LANES):
        down_grad[:, index * LANES : (index + 1) * LANES] = full_ref[
            index * width : (index + 1) * width, :
        ].astype(f32)
    save(down_grad, down_out)
    for load in loads[4:]:
        load.wait()
    save(token_ref, token_out)
    save(mem_ref, mem_out)
    loads[2].wait()
    emb[...] = jnp.zeros_like(emb)
    emb[:count, :] = emb_ref[...].astype(f32)
    emb_low = emb[...].astype(low)
    row = lax.broadcasted_iota(jnp.int32, hidden.shape, 0)
    hidden[...] = jnp.where(
        row < count, jnp.tanh(dot_nn(emb_low, first_ref[...]) + fbias_ref[...]), 0.0
    )
    value = hidden[...]
    prefix = pkv_ref[...]
    parts = both_parts(prefix)
    hidden_twice = jnp.concatenate([value, value], axis=0).T.astype(low)
    tile = 128
    for index in range(second_grad.shape[0] // tile):
        here = slice(index * tile, (index + 1) * tile)
        second_grad[here, :] = dot_nn(hidden_twice[here, :], parts)
        save(second_grad, second_out, here)
    sbias_out[...] = jnp.sum(prefix, axis=0, keepdims=True)
    loads[3].wait()
    grad = dot_nt(parts, second_ref[...])
    grad = (grad[:PREFIX_ROWS] + grad[PREFIX_ROWS:]) * (1.0 - value * value)
    fbias_out[...] = jnp.sum(grad, axis=0, keepdims=True)
    parts = both_parts(grad)
    emb_twice = jnp.concatenate([emb[...], emb[...]], axis=0).T.astype(low)
    first_grad[...] = dot_nn(emb_twice, parts)
    save(first_grad, first_out)
    back = dot_nt(parts, first_ref[...])
    embed_out[...] = (back[:PREFIX_ROWS] + back[PREFIX_ROWS:])[:count, :]
    rbias_out[...] = vecs_ref[0:1, :]
    dbias_out[...] = vecs_ref[1:2, :down]
    gain_out[...] = vecs_ref[2:5, :]
    shift_out[...] = vecs_ref[5:8, :]
    for copy in saves:
        copy.wait()


def finish(full, vecs, prefix_grad, embed, first, first_bias, second, down, token_grad, memory_grad):
    f32 = jnp.float32
    count, width = embed.shape
    hidden = first.shape[1]
    vmem = pl.BlockSpec(memory_space=pltpu.VMEM)
    anywhere = pl.BlockSpec(memory_space=pl.ANY)
    shapes = (
        (count, width),
        (width, hidden),
        (1, hidden),
        (hidden, 2 * width),
        (1, 2 * width),
        (width, down),
        (1, down),
        (down, width),
        (1, width),
        (3, width),
        (3, width),
    )
    return pl.pallas_call(
        finish_kernel,
        out_shape=tuple(jax.ShapeDtypeStruct(shape, f32) for shape in shapes)
        + tuple(
            jax.ShapeDtypeStruct(value.shape, value.dtype) for value in (token_grad, memory_grad)
        ),
        in_specs=[anywhere, vmem, vmem, vmem, anywhere, vmem, anywhere, anywhere, anywhere],
        out_specs=(
            vmem,
            anywhere,
            vmem,
            anywhere,
            vmem,
            anywhere,
            vmem,
            anywhere,
            vmem,
            vmem,
            vmem,
            anywhere,
            anywhere,
        ),
        scratch_shapes=[
            pltpu.VMEM(full.shape, jnp.bfloat16),
            pltpu.VMEM(first.shape, jnp.bfloat16),
            pltpu.VMEM(second.shape, jnp.bfloat16),
            pltpu.VMEM(token_grad.shape, token_grad.dtype),
            pltpu.VMEM(memory_grad.shape, memory_grad.dtype),
            pltpu.VMEM((width, hidden), f32),
            pltpu.VMEM((hidden, 2 * width), f32),
            pltpu.VMEM((width, down), f32),
            pltpu.VMEM((down, width), f32),
            pltpu.VMEM((PREFIX_ROWS, width), f32),
            pltpu.VMEM((PREFIX_ROWS, hidden), f32),
            pltpu.SemaphoreType.DMA((5 + hidden // 128,)),
            pltpu.SemaphoreType.DMA((6,)),
        ],
        compiler_params=pltpu.CompilerParams(vmem_limit_bytes=VMEM_BYTES),
        name="finish",
    )(full, vecs, prefix_grad, embed, first, first_bias, second, token_grad, memory_grad)


def gelu_pair(value):
    size = jnp.abs(value)
    step = 1.0 / (1.0 + (0.3275911 * 0.7071067811865476) * size)
    bell = jnp.exp(-0.5 * value * value)
    poly = step * (
        0.127414796
        + step
        * (-0.142248368 + step * (0.7107068705 + step * (-0.7265760135 + step * 0.5307027145)))
    )
    act = jnp.maximum(value, 0.0) - size * (poly * bell)
    turn = bell * (0.3989422804014327 * size - poly)
    return act, jnp.where(value >= 0.0, 1.0 + turn, -turn)


def normed(value):
    center = jnp.mean(value, axis=-1, keepdims=True)
    centered = value - center
    scale = lax.rsqrt(jnp.mean(centered * centered, axis=-1, keepdims=True) + norm_eps)
    return centered * scale, scale


def norm_back(grad, scale, unit):
    return scale * (
        grad
        - jnp.mean(grad, axis=-1, keepdims=True)
        - unit * jnp.mean(grad * unit, axis=-1, keepdims=True)
    )


def middle_kernel(
    tok_in,
    att_in,
    cot_in,
    mkey_in,
    mvalue_in,
    gain_ref,
    shift_ref,
    dbias_ref,
    rbias_ref,
    wo_in,
    wcq_in,
    wco_in,
    wd_in,
    wr_in,
    win_in,
    wout_in,
    layer_out,
    fgrad_out,
    ograd_out,
    mkey_out,
    mvalue_out,
    sums_out,
    vecs_ref,
    tok_ref,
    att_ref,
    cot_ref,
    mkey_ref,
    mvalue_ref,
    out_ref,
    fgrad_ref,
    ograd_ref,
    sums_ref,
    wo,
    wcq,
    wco,
    wd,
    wr,
    win,
    wout,
    unit_one,
    unit_two,
    work,
    total,
    scale_one,
    scale_two,
    low_one,
    low_two,
    low_three,
    query,
    crossed,
    weights,
    slopes,
    down_act,
    down_slope,
    down_grad,
    load_sem,
    win_sem,
    wout_sem,
    out_sem,
):
    length, width = tok_ref.shape
    slots, tile = win.shape[0], win.shape[2]
    tiles = win_in.shape[1] // tile
    rows_step = 128
    low = jnp.bfloat16
    f32 = jnp.float32

    sources = (
        att_in,
        wo_in,
        tok_in,
        wcq_in,
        mkey_in,
        mvalue_in,
        wco_in,
        wd_in,
        wr_in,
        cot_in,
    )
    targets = (att_ref, wo, tok_ref, wcq, mkey_ref, mvalue_ref, wco, wd, wr, cot_ref)
    loads = [
        pltpu.make_async_copy(source, target, load_sem.at[index])
        for index, (source, target) in enumerate(zip(sources, targets))
    ]

    def win_load(which):
        slot = which % slots
        return pltpu.make_async_copy(
            win_in.at[:, rows_of(which, tile)], win.at[slot], win_sem.at[slot]
        )

    def wout_load(which):
        slot = which % slots
        return pltpu.make_async_copy(
            wout_in.at[rows_of(which, tile), :], wout.at[slot], wout_sem.at[slot]
        )

    for load in loads[:7]:
        load.start()

    def by_columns(extent, step, body):
        def one(index, carry):
            body(pl.ds(pl.multiple_of(index * step, step), step))
            return carry

        lax.fori_loop(0, extent // step, one, 0)

    def by_rows(body, init=0):
        def one(index, carry):
            return body(rows_of(index, rows_step), carry)

        return lax.fori_loop(0, length // rows_step, one, init)

    cols = 512
    half = width // 2

    for load in loads[:3]:
        load.wait()
    for load in loads[7:]:
        load.start()
    for which in range(slots):
        win_load(which).start()
        wout_load(which).start()

    def project_out(here):
        work[:, here] = tok_ref[:, here].astype(f32) + dot_nn(att_ref[...], wo[:, here])

    by_columns(width, cols, project_out)

    def first_norm(here, carry):
        unit, scale = normed(work[here, :])
        unit_one[here, :] = unit
        scale_one[here, :] = scale
        value = unit * gain_ref[0:1, :] + shift_ref[0:1, :]
        work[here, :] = value
        low_one[here, :] = value.astype(low)
        return carry

    by_rows(first_norm)

    loads[3].wait()

    def project_query(here):
        query[:, here] = dot_nn(low_one[...], wcq[:, here]).astype(low)

    by_columns(width, cols, project_query)
    per_block = LANES // HD

    def head_queries(here, head):
        both = query[:, here].astype(f32) * 0.125
        return jnp.where(head_lanes(both.shape, head), both, 0.0).astype(low)

    def cross_forward(block):
        here = rows_of(block, LANES)
        keys = mkey_ref[:, here]
        values = mvalue_ref[:, here].astype(f32).T.astype(low)
        outs = []
        for head in range(per_block):
            scores = dot_nt(keys, head_queries(here, head))
            raised = jnp.exp(scores - jnp.max(scores, axis=0, keepdims=True))
            share = 1.0 / jnp.sum(raised, axis=0, keepdims=True)
            weight = (raised * share).astype(low)
            weights[block * per_block + head] = weight
            outs.append(dot_nn(values[head * HD : (head + 1) * HD, :], weight))
        crossed[:, here] = jnp.concatenate(outs, axis=0).T.astype(low)

    loads[4].wait()
    loads[5].wait()

    def cross_forward_four(step, carry):
        for part in range(4):
            cross_forward(4 * step + part)
        return carry

    lax.fori_loop(0, width // LANES // 4, cross_forward_four, 0)

    loads[6].wait()

    def project_crossed(here):
        work[:, here] += dot_nn(crossed[...], wco[:, here])

    by_columns(width, cols, project_crossed)

    def second_norm(here, carry):
        unit, scale = normed(work[here, :])
        unit_two[here, :] = unit
        scale_two[here, :] = scale
        value = unit * gain_ref[1:2, :] + shift_ref[1:2, :]
        work[here, :] = value
        low_two[here, :] = value.astype(low)
        return carry

    by_rows(second_norm)

    total[...] = jnp.zeros_like(total)

    def feed_forward(which, carry):
        slot = lax.rem(which, slots)
        win_load(which).wait()
        wout_load(which).wait()
        act, slope = gelu_pair(dot_nn(low_two[...], win[slot]))
        slopes[:, rows_of(which, tile)] = slope.astype(low)
        total[...] += dot_nn(act.astype(low), wout[slot])

        if slots < tiles:

            @pl.when(which + slots < tiles)
            def _():
                win_load(which + slots).start()
                wout_load(which + slots).start()

        return carry

    lax.fori_loop(0, tiles, feed_forward, 0)
    loads[7].wait()
    loads[8].wait()
    loads[9].wait()
    act, slope = gelu_pair(dot_nn(low_two[...], wd[...]) + dbias_ref[...])
    down_act[...] = act.astype(low)
    down_slope[...] = slope.astype(low)

    def project_raise(here):
        work[:, here] += total[:, here] + 4.0 * (
            dot_nn(down_act[...], wr[:, here]) + rbias_ref[:, here]
        )

    by_columns(width, cols, project_raise)
    nothing = jnp.zeros((1, width), f32)

    def third_norm(here, carry):
        gain_sum, shift_sum, bias_sum = carry
        unit, scale = normed(work[here, :])
        gain = gain_ref[2:3, :]
        out_ref[here, :] = (unit * gain + shift_ref[2:3, :]).astype(low)
        grad = cot_ref[here, :].astype(f32)
        back = norm_back(grad * gain, scale, unit)
        total[here, :] = back
        back_low = back.astype(low)
        low_three[here, :] = back_low
        return (
            gain_sum + jnp.sum(grad * unit, axis=0, keepdims=True),
            shift_sum + jnp.sum(grad, axis=0, keepdims=True),
            bias_sum + jnp.sum(back_low.astype(f32), axis=0, keepdims=True),
        )

    gain_three, shift_three, bias_sum = by_rows(third_norm, (nothing, nothing, nothing))
    saves = []

    def save(source, target):
        copy = pltpu.make_async_copy(source, target, out_sem.at[len(saves)])
        copy.start()
        saves.append(copy)

    save(out_ref, layer_out)
    vecs_ref[0:1, :] = 4.0 * bias_sum

    back = 4.0 * dot_nt(low_three[...], wr[...]) * down_slope[...].astype(f32)
    back_low = back.astype(low)
    down_grad[...] = back_low
    vecs_ref[1:2, :] = jnp.concatenate(
        [
            jnp.sum(back_low.astype(f32), axis=0, keepdims=True),
            jnp.zeros((1, width - wd.shape[1]), f32),
        ],
        axis=1,
    )
    down = wd.shape[1]
    raise_sum = 4.0 * dot_tn(down_act[...], low_three[...])
    for index in range(width // LANES):
        sums_ref[pl.ds(down * width // LANES + index * down, down), :] = raise_sum[
            :, index * LANES : (index + 1) * LANES
        ].astype(low)
    down_sum = dot_tn(low_two[...], down_grad[...])
    for index in range(down // LANES):
        sums_ref[index * width : (index + 1) * width, :] = down_sum[
            :, index * LANES : (index + 1) * LANES
        ].astype(low)

    save(sums_ref, sums_out)

    def feed_backward(step, carry):
        which = tiles - 1 - step
        slot = lax.rem(which, slots)
        here = rows_of(which, tile)

        if slots < tiles:

            @pl.when(which < tiles - slots)
            def _():
                wout_load(which).wait()
                win_load(which).wait()

        grad = dot_nt(low_three[...], wout[slot]) * slopes[:, here].astype(f32)
        total[...] += dot_nt(grad.astype(low), win[slot])

        if slots < tiles:

            @pl.when(which >= slots)
            def _():
                win_load(which - slots).start()
                wout_load(which - slots).start()

        return carry

    lax.fori_loop(0, tiles, feed_backward, 0)

    def down_back(here):
        total[:, here] += dot_nt(down_grad[...], wd[here, :])

    by_columns(width, cols, down_back)

    def second_back(here, carry):
        gain_sum, shift_sum = carry
        grad = total[here, :]
        unit = unit_two[here, :]
        back = norm_back(grad * gain_ref[1:2, :], scale_two[here, :], unit)
        total[here, :] = back
        low_one[here, :] = back.astype(low)
        return (
            gain_sum + jnp.sum(grad * unit, axis=0, keepdims=True),
            shift_sum + jnp.sum(grad, axis=0, keepdims=True),
        )

    gain_two, shift_two = by_rows(second_back, (nothing, nothing))

    def crossed_back(here):
        crossed[:, here] = dot_nt(low_one[...], wco[here, :]).astype(low)

    by_columns(width, cols, crossed_back)

    def cross_backward(block):
        here = rows_of(block, LANES)
        values = mvalue_ref[:, here]
        keys = mkey_ref[:, here].astype(f32).T.astype(low)
        grads = crossed[:, here].astype(f32)
        outs = []
        key_sum = None
        for head in range(per_block):
            grad = jnp.where(head_lanes(grads.shape, head), grads, 0.0).astype(low)
            weight_low = weights[block * per_block + head]
            weight = weight_low.astype(f32)
            slope = dot_nt(values, grad)
            slope = weight * (slope - jnp.sum(weight * slope, axis=0, keepdims=True))
            slope = slope.astype(low)
            key_part = dot_nn(slope, head_queries(here, head))
            value_part = dot_nn(weight_low, grad)
            if key_sum is None:
                key_sum, value_sum = key_part, value_part
            else:
                key_sum, value_sum = key_sum + key_part, value_sum + value_part
            outs.append(dot_nn(keys[head * HD : (head + 1) * HD, :], slope))
        mkey_ref[:, here] = key_sum.astype(low)
        mvalue_ref[:, here] = value_sum.astype(low)
        query[:, here] = (jnp.concatenate(outs, axis=0) * 0.125).T.astype(low)

    def cross_backward_four(step, carry):
        for part in range(4):
            cross_backward(4 * step + part)
        return carry

    lax.fori_loop(0, width // LANES // 4, cross_backward_four, 0)
    save(mkey_ref, mkey_out)
    save(mvalue_ref, mvalue_out)

    def query_back(here):
        total[:, here] += dot_nt(query[...], wcq[here, :])

    by_columns(width, cols, query_back)

    def first_back(here, carry):
        gain_sum, shift_sum = carry
        grad = total[here, :]
        unit = unit_one[here, :]
        back = norm_back(grad * gain_ref[0:1, :], scale_one[here, :], unit)
        fgrad_ref[here, :] = back
        low_one[here, :] = back.astype(low)
        return (
            gain_sum + jnp.sum(grad * unit, axis=0, keepdims=True),
            shift_sum + jnp.sum(grad, axis=0, keepdims=True),
        )

    gain_one, shift_one = by_rows(first_back, (nothing, nothing))
    save(fgrad_ref, fgrad_out)

    for index in range(width // cols):
        here = slice(index * cols, (index + 1) * cols)
        ograd_ref[here, :] = dot_nt(low_one[...], wo[here, :]).T.astype(low)
        save(ograd_ref.at[here], ograd_out.at[here])
    for index, vector in enumerate(
        (gain_one, gain_two, gain_three, shift_one, shift_two, shift_three)
    ):
        vecs_ref[2 + index : 3 + index, :] = vector
    for copy in saves:
        copy.wait()


def middle(
    tokens, attended, cotangent, mem_key, mem_value, gains, shifts, down_bias, raise_bias, weights
):
    length, width = tokens.shape
    mem_len = mem_key.shape[0]
    down = weights[3].shape[1]
    feed = weights[5].shape[1]
    tile = 512 if mem_len <= 512 else 128
    slots = feed // tile if mem_len <= 512 else 2
    low = jnp.bfloat16
    f32 = jnp.float32
    vmem = pl.BlockSpec(memory_space=pltpu.VMEM)
    anywhere = pl.BlockSpec(memory_space=pl.ANY)
    square = pltpu.VMEM((width, width), low)
    wide = pltpu.VMEM((length, width), f32)
    narrow = pltpu.VMEM((length, width), low)
    return pl.pallas_call(
        middle_kernel,
        out_shape=(
            jax.ShapeDtypeStruct((length, width), low),
            jax.ShapeDtypeStruct((length, width), f32),
            jax.ShapeDtypeStruct((width, length), low),
            jax.ShapeDtypeStruct((mem_len, width), low),
            jax.ShapeDtypeStruct((mem_len, width), low),
            jax.ShapeDtypeStruct((2 * down * width // LANES, LANES), low),
            jax.ShapeDtypeStruct((8, width), f32),
        ),
        in_specs=[anywhere] * 5 + [vmem] * 4 + [anywhere] * 7,
        out_specs=(anywhere,) * 6 + (vmem,),
        scratch_shapes=[
            narrow,
            narrow,
            narrow,
            pltpu.VMEM((mem_len, width), low),
            pltpu.VMEM((mem_len, width), low),
            narrow,
            wide,
            pltpu.VMEM((width, length), low),
            pltpu.VMEM((2 * down * width // LANES, LANES), low),
            square,
            square,
            square,
            pltpu.VMEM((width, down), low),
            pltpu.VMEM((down, width), low),
            pltpu.VMEM((slots, width, tile), low),
            pltpu.VMEM((slots, tile, width), low),
            wide,
            wide,
            wide,
            wide,
            pltpu.VMEM((length, 1), f32),
            pltpu.VMEM((length, 1), f32),
            narrow,
            narrow,
            narrow,
            narrow,
            narrow,
            pltpu.VMEM((H, mem_len, length), low),
            pltpu.VMEM((length, feed), low),
            pltpu.VMEM((length, down), low),
            pltpu.VMEM((length, down), low),
            pltpu.VMEM((length, down), low),
            pltpu.SemaphoreType.DMA((10,)),
            pltpu.SemaphoreType.DMA((slots,)),
            pltpu.SemaphoreType.DMA((slots,)),
            pltpu.SemaphoreType.DMA((5 + width // 512,)),
        ],
        compiler_params=pltpu.CompilerParams(vmem_limit_bytes=VMEM_BYTES + (0 if mem_len <= 512 else 3 * 1024 * 1024)),
        name="middle",
    )(tokens, attended, cotangent, mem_key, mem_value, gains, shifts, down_bias, raise_bias, *weights)


def per_device(
    tokens,
    memory,
    segment_ids,
    padding_mask,
    cotangent,
    prefix_embed,
    prefix_first,
    first_bias,
    prefix_second,
    second_bias,
    adapter_down,
    down_bias,
    adapter_raise,
    raise_bias,
    norm_gain,
    norm_shift,
    self_query,
    self_key,
    self_value,
    self_output,
    cross_query,
    cross_key,
    cross_value,
    cross_output,
    feed_in,
    feed_out,
):
    row_count, length, model_width = tokens.shape
    flat_rows = row_count * length
    n = lax.axis_size("seq")
    batches = lax.axis_size("batch")
    down = adapter_down.shape[1]
    attended, mem_key, mem_value, *saved = self_forward(
        n,
        segment_ids,
        padding_mask,
        tokens.reshape(flat_rows, model_width),
        (self_query, self_key, self_value),
        (
            prefix_embed,
            prefix_first,
            first_bias.reshape(1, -1),
            prefix_second,
            second_bias.reshape(1, -1),
        ),
        memory.reshape(-1, model_width),
        (cross_key, cross_value),
    )
    layer_output, first_grad, out_grad, *mem_grads, weight_sums, vector_sums = middle(
        tokens.reshape(flat_rows, model_width),
        attended,
        cotangent.reshape(flat_rows, model_width),
        mem_key,
        mem_value,
        norm_gain,
        norm_shift,
        down_bias.reshape(1, -1),
        raise_bias.reshape(1, -1),
        (
            self_output,
            cross_query,
            cross_output,
            adapter_down,
            adapter_raise,
            feed_in,
            feed_out,
        ),
    )
    layer_output = layer_output.reshape(row_count, length, model_width)
    token_grad, memory_grad, prefix_grad, vector_sums, full_sums = self_backward(
        n,
        batches,
        first_grad,
        out_grad.reshape(n, -1, HD, length),
        weight_sums,
        mem_grads,
        (cross_key, cross_value),
        vector_sums,
        saved,
        (self_query, self_key, self_value),
    )
    *replicated, token_grad, memory_grad = finish(
        full_sums.reshape(-1, LANES),
        vector_sums,
        prefix_grad,
        prefix_embed,
        prefix_first,
        first_bias.reshape(1, -1),
        prefix_second,
        down,
        token_grad,
        memory_grad,
    )
    token_grad = token_grad.reshape(row_count, length, model_width)
    memory_grad = memory_grad.reshape(memory.shape)
    replicated = [
        value.reshape(-1) if value.shape[0] == 1 else value for value in replicated
    ]
    return (layer_output, token_grad, memory_grad, *replicated)


def solution(mesh):
    placed = (
        P("batch", "seq", None),
        P("batch", "seq", None),
        P("batch", "seq"),
        P("batch", "seq"),
        P("batch", "seq", None),
        P(),
        P(),
        P(),
        P(),
        P(),
        P(),
        P(),
        P(),
        P(),
        P(),
        P(),
        P(),
        P(),
        P(),
        P(),
        P(),
        P(),
        P(),
        P(),
        P(),
        P(),
    )
    return jax.shard_map(
        per_device,
        mesh=mesh,
        in_specs=placed,
        out_specs=(
            P("batch", "seq", None),
            P("batch", "seq", None),
            P("batch", "seq", None),
            P(),
            P(),
            P(),
            P(),
            P(),
            P(),
            P(),
            P(),
            P(),
            P(),
            P(),
        ),
        check_vma=False,
    )
```

```python
import functools

import jax
import jax.numpy as jnp
from jax import lax
from jax.experimental import pallas as pl
from jax.experimental.pallas import tpu as pltpu
from jax.sharding import PartitionSpec as P

H = 16
HD = 64
LANES = 128
PREFIX_ROWS = 32
VMEM_BYTES = 60 * 1024 * 1024
SUM_ROWS = 16
MESH = pl.DeviceIdType.MESH

masked_score = -1e30
norm_eps = 1e-05

def dot_nn(left, right):
    return lax.dot_general(
        left, right, (((1,), (0,)), ((), ())), preferred_element_type=jnp.float32
    )


def dot_nt(left, right):
    return lax.dot_general(
        left, right, (((1,), (1,)), ((), ())), preferred_element_type=jnp.float32
    )


def dot_tn(left, right):
    return lax.dot_general(
        left, right, (((0,), (0,)), ((), ())), preferred_element_type=jnp.float32
    )


def remote(source, target, send_sem, recv_sem, axis, peer):
    return pltpu.make_async_remote_copy(
        src_ref=source,
        dst_ref=target,
        send_sem=send_sem,
        recv_sem=recv_sem,
        device_id={axis: peer},
        device_id_type=MESH,
    )


def enter(sizes):
    barrier = pltpu.get_barrier_semaphore()
    for axis, size in sizes.items():
        for other in range(size):

            @pl.when(other != lax.axis_index(axis))
            def _():
                pl.semaphore_signal(barrier, inc=1, device_id={axis: other}, device_id_type=MESH)

    pl.semaphore_wait(barrier, sum(sizes.values()) - len(sizes))


def others(size, mine, body):
    for other in range(size):

        @pl.when(other != mine)
        def _():
            body(other)


def rows_of(index, size):
    return pl.ds(pl.multiple_of(index * size, size), size)


def span_of(start, size):
    return pl.ds(pl.multiple_of(start, LANES), size)


def own_columns(ref, first, me, width):
    if width % LANES == 0:
        return ref[:, pl.ds(pl.multiple_of(first + me * width, LANES), width)].astype(jnp.float32)
    share = LANES // width
    block = ref[:, pl.ds(pl.multiple_of(first + me // share * LANES, LANES), LANES)].astype(
        jnp.float32
    )
    picked = block[:, :width]
    for part in range(1, share):
        picked = jnp.where(me % share == part, block[:, part * width : (part + 1) * width], picked)
    return picked


def head_lanes(shape, head):
    lane = lax.broadcasted_iota(jnp.int32, shape, 1)
    return (lane >= head * HD) & (lane < (head + 1) * HD)


def self_forward_kernel(
    n,
    seg_ref,
    pad_ref,
    tok_ref,
    wq_in,
    wk_in,
    wv_in,
    emb_ref,
    first_in,
    fbias_ref,
    second_in,
    sbias_ref,
    mem_ref,
    wck_in,
    wcv_in,
    att_ref,
    mkey_out,
    mvalue_out,
    qx_out,
    kx_out,
    raw_out,
    pk_out,
    pv_out,
    pkt_out,
    ot_out,
    lse_out,
    send,
    recv,
    meta_send,
    meta,
    kx,
    qx,
    vt,
    hidden,
    pk,
    pv,
    pkt,
    pvt,
    stat,
    acc,
    o_send,
    o_recv,
    mem_all,
    wck,
    wcv,
    mkey_ref,
    mvalue_ref,
    wq_ref,
    wk_ref,
    wv_ref,
    first_ref,
    second_ref,
    send_sem,
    recv_sem,
    meta_send_sem,
    meta_recv_sem,
    o_send_sem,
    o_recv_sem,
    mem_send_sem,
    mem_recv_sem,
    out_sem,
    weight_sem,
    in_sem,
):
    low = jnp.bfloat16
    f32 = jnp.float32
    me = lax.axis_index("seq")
    length, width = tok_ref.shape
    group = width // n
    heads = group // HD
    plane = 2 * length
    planes = n // 2
    block = 2 * LANES
    per_block = block // group
    blocks = width // block
    step_rows = 256
    steps = plane // step_rows
    my_plane = me // 2
    my_side = lax.rem(me, 2)

    def meta_copy(peer, slot):
        return remote(
            meta_send, meta.at[slot], meta_send_sem.at[peer], meta_recv_sem.at[slot], "seq", peer
        )

    def qkv_copy(head, peer, slot):
        return remote(
            send.at[peer, head],
            recv.at[head, slot],
            send_sem.at[head, peer],
            recv_sem.at[head, slot],
            "seq",
            peer,
        )

    def out_copy(head, peer, slot):
        return remote(
            o_send.at[head, peer],
            o_recv.at[slot, head],
            o_send_sem.at[head, peer],
            o_recv_sem.at[head, slot],
            "seq",
            peer,
        )

    def mem_along(which, toward):
        part = mem_all.at[which, my_side]
        return remote(
            part,
            part,
            mem_send_sem.at[(toward + 1) // 2, which],
            mem_recv_sem.at[which],
            "seq",
            me + 2 * toward,
        )

    def mem_across(side):
        part = mem_all.at[:, side]
        return remote(
            part,
            part,
            mem_send_sem.at[0, planes],
            mem_recv_sem.at[planes],
            "seq",
            me + 1 - 2 * my_side,
        )

    def mem_hops(hop, body):
        for toward in (1, -1):
            which = my_plane - toward * hop
            ahead = my_plane + toward

            @pl.when((which >= 0) & (which < planes) & (ahead >= 0) & (ahead < planes))
            def _():
                body(mem_along(which, toward))

    def mem_arrivals(hop):
        for toward in (1, -1):
            which = my_plane - toward * hop

            @pl.when((which >= 0) & (which < planes))
            def _():
                mem_along(which, -toward).wait_recv()

    def block_at(step):
        if blocks >= planes:
            share = blocks // planes
            return lax.rem(my_plane + 1 + step // share, planes) * share + step % share
        return lax.rem(me // per_block + 1 + step, blocks)

    def weight_load(step, which):
        columns = rows_of(block_at(step), block)
        source = (wq_in, wk_in, wv_in)[which]
        target = (wq_ref, wk_ref, wv_ref)[which]
        return pltpu.make_async_copy(
            source.at[:, columns], target.at[:, columns], weight_sem.at[step, which]
        )

    for step in range(blocks):
        for which in range(3):
            weight_load(step, which).start()
    loads = [
        pltpu.make_async_copy(source, target, in_sem.at[index])
        for index, (source, target) in enumerate(
            ((first_in, first_ref), (second_in, second_ref), (wck_in, wck), (wcv_in, wcv))
        )
    ]
    for load in loads:
        load.start()
    segments = seg_ref[...]
    tags = jnp.where(pad_ref[...] == 1, segments, -1)
    row = lax.broadcasted_iota(jnp.int32, meta_send.shape, 0)
    meta_send[...] = jnp.where(row == 0, segments, tags)
    mem_all[my_plane, my_side] = mem_ref[...]
    enter({"seq": n})
    others(n, me, lambda peer: meta_copy(peer, me).start())
    meta[me] = meta_send[...]

    for step in range(blocks):
        at = block_at(step)
        columns = rows_of(at, block)
        for which, weight in enumerate((wq_ref, wk_ref, wv_ref)):
            weight_load(step, which).wait()
            piece = dot_nn(tok_ref[...], weight[:, columns]).T.astype(low)
            for part in range(per_block):
                for head in range(heads):
                    first = part * group + head * HD
                    send[at * per_block + part, head, which] = piece[first : first + HD]
        for part in range(per_block):
            peer = at * per_block + part

            @pl.when(peer != me)
            def _():
                qkv_copy(0, peer, me).start()

            @pl.when(peer == me)
            def _():
                for head in range(heads):
                    recv[head, me] = send[peer, head]

    mem_hops(0, lambda copy: copy.start())
    loads[0].wait()
    loads[1].wait()
    hidden[...] = jnp.zeros_like(hidden)
    hidden[: emb_ref.shape[0], :] = jnp.tanh(dot_nn(emb_ref[...], first_ref[...]) + fbias_ref[...])
    hidden_low = hidden[...].astype(low)
    prefix_key = dot_nn(hidden_low, own_columns(second_ref, 0, me, group).astype(low)) + own_columns(
        sbias_ref, 0, me, group
    )
    prefix_value = dot_nn(
        hidden_low, own_columns(second_ref, width, me, group).astype(low)
    ) + own_columns(sbias_ref, width, me, group)
    prefix_row = lax.broadcasted_iota(jnp.int32, (PREFIX_ROWS, HD), 0)
    prefix_open = jnp.where(prefix_row < emb_ref.shape[0], 0.0, masked_score)
    for head in range(heads):
        here = slice(head * HD, (head + 1) * HD)
        pk[head] = jnp.concatenate([prefix_key[:, here], prefix_open], axis=1).astype(low)
        pv[head] = prefix_value[:, here].astype(low)
    pkt[...] = prefix_key.T.astype(low).reshape(heads, HD, PREFIX_ROWS)
    pvt[:, :HD, :] = prefix_value.T.astype(low).reshape(heads, HD, PREFIX_ROWS)
    pvt[:, HD:, :] = jnp.ones((heads, SUM_ROWS, PREFIX_ROWS), low)
    vt[:, HD:, :] = jnp.ones((heads, SUM_ROWS, n * length), low)

    def arrive(head, chunk):
        @pl.when(chunk != me)
        def _():
            @pl.when(head == 0)
            def _():
                meta_copy(chunk, chunk).wait_recv()

            qkv_copy(head, chunk, chunk).wait_recv()

        here = rows_of(chunk, length)
        state = lax.broadcasted_iota(jnp.int32, (HD, length), 0)
        qx[head, :HD, here] = (recv[head, chunk, 0].astype(f32) * 0.125).astype(low)
        qx[head, HD:, here] = jnp.where(state == meta[chunk, 0:1, :], 1.0, 0.0).astype(low)
        is_open = jnp.where(state == meta[chunk, 1:2, :], 0.0, masked_score)
        kx[head, here, :] = jnp.concatenate(
            [recv[head, chunk, 1].astype(f32), is_open], axis=0
        ).T.astype(low)
        vt[head, :HD, here] = recv[head, chunk, 2]

    def open_plane(head, which):
        scores = dot_nn(pk[head], qx[head, :, rows_of(which, plane)])
        top = jnp.max(scores, axis=0, keepdims=True)
        raised = jnp.exp(scores - top)
        stat[which, head, 0:1, :] = top
        acc[which, head] = dot_nn(pvt[head], raised.astype(low))

    def pair_part(head, upper, lower, first, keys, diagonal):
        here = slice(first, first + step_rows)
        queries = qx[head, :, span_of(upper * plane + first, step_rows)]
        key_rows = span_of(lower * plane, keys)
        scores = dot_nn(kx[head, key_rows, :], queries)
        if diagonal:
            key_at = lax.broadcasted_iota(jnp.int32, scores.shape, 0)
            query_at = lax.broadcasted_iota(jnp.int32, scores.shape, 1) + first
            scores = jnp.where(key_at <= query_at, scores, masked_score)
        old_top = stat[upper, head, 0:1, here]
        top = jnp.maximum(old_top, jnp.max(scores, axis=0, keepdims=True))
        raised = jnp.exp(scores - top).astype(low)
        stat[upper, head, 0:1, here] = top
        acc[upper, head, :, here] = acc[upper, head, :, here] * jnp.exp(old_top - top) + dot_nn(
            vt[head, :, key_rows], raised
        )

    def pair(head, upper, lower):
        for part in range(steps):
            pair_part(head, upper, lower, part * step_rows, plane, False)

    def pair_diagonal(head, which):
        for part in range(steps):
            pair_part(head, which, which, part * step_rows, (part + 1) * step_rows, True)

    def close_plane(head, which):
        total = acc[which, head, HD : HD + 1, :]
        value = acc[which, head, :HD, :] / total
        acc[which, head, :HD, :] = value
        stat[which, head, 0:1, :] = stat[which, head, 0:1, :] + jnp.log(total)
        for part in range(2):
            chunk = 2 * which + part
            o_send[head, chunk] = value[:, part * length : (part + 1) * length].astype(low)

            @pl.when(chunk != me)
            def _():
                out_copy(head, chunk, me).start()

            @pl.when(chunk == me)
            def _():
                o_recv[me, head] = o_send[head, chunk]

    def project_memory():
        mem_across(1 - my_side).wait_recv()
        for load in loads[2:]:
            load.wait()
        whole = mem_all[...].reshape(mkey_ref.shape)

        def one(index, carry):
            here = rows_of(index, block)
            mkey_ref[:, here] = dot_nn(whole, wck[:, here]).astype(low)
            mvalue_ref[:, here] = dot_nn(whole, wcv[:, here]).astype(low)
            return carry

        lax.fori_loop(0, blocks, one, 0)

    def stage(index, carry):
        head = index // planes
        step = lax.rem(index, planes)

        @pl.when(head + 1 < heads)
        def _():
            there = lax.rem(my_plane + 1 + step, planes)
            for part in range(2):
                peer = 2 * there + part

                @pl.when(peer != me)
                def _():
                    qkv_copy(head, peer, me).wait_send()
                    qkv_copy(head + 1, peer, me).start()

        here = lax.rem(my_plane + step, planes)
        arrive(head, 2 * here)
        arrive(head, 2 * here + 1)
        open_plane(head, here)
        pair_diagonal(head, here)

        def earlier(back, inner):
            there = lax.rem(my_plane + back, planes)
            pair(head, jnp.maximum(here, there), jnp.minimum(here, there))

            @pl.when((step == planes - 1) & (there > here))
            def _():
                close_plane(head, there)

            return inner

        lax.fori_loop(0, step, earlier, 0)
        for hop in range(1, planes - 1):

            @pl.when(index == hop)
            def _():
                mem_arrivals(hop)
                mem_hops(hop, lambda copy: copy.start())

        @pl.when(index == planes - 1)
        def _():
            mem_arrivals(planes - 1)
            mem_across(my_side).start()

        @pl.when((my_plane + step >= planes) | (my_plane == 0))
        def _():
            close_plane(head, here)

        return carry

    lax.fori_loop(0, heads * planes, stage, 0)

    saves = []

    def save(source, target):
        copy = pltpu.make_async_copy(source, target, out_sem.at[len(saves)])
        copy.start()
        saves.append(copy)

    save(qx, qx_out)
    save(kx, kx_out)
    save(recv, raw_out)
    save(pk, pk_out)
    save(pv, pv_out)
    save(pkt, pkt_out)
    save(acc, ot_out)
    save(stat, lse_out)
    project_memory()
    save(mkey_ref, mkey_out)
    save(mvalue_ref, mvalue_out)
    for other in range(n):

        @pl.when(other != me)
        def _():
            for head in range(heads):
                out_copy(head, other, other).wait_recv()

        att_ref[:, other * group : (other + 1) * group] = (
            o_recv[other].reshape(group, length).astype(f32).T.astype(low)
        )

    def drain(peer):
        meta_copy(peer, me).wait_send()
        qkv_copy(heads - 1, peer, me).wait_send()
        for head in range(heads):
            out_copy(head, peer, me).wait_send()

    others(n, me, drain)
    for hop in range(planes - 1):
        mem_hops(hop, lambda copy: copy.wait_send())
    mem_across(my_side).wait_send()
    for copy in saves:
        copy.wait()


def self_forward(n, segments, padding, tokens, weights, prefix, memory, mem_weights):
    length, width = tokens.shape
    group = width // n
    heads = group // HD
    whole = n * length
    planes = n // 2
    low = jnp.bfloat16
    f32 = jnp.float32
    vmem = pl.BlockSpec(memory_space=pltpu.VMEM)
    anywhere = pl.BlockSpec(memory_space=pl.ANY)
    dma = pltpu.SemaphoreType.DMA
    shapes = (
        ((heads, 2 * HD, whole), low),
        ((heads, whole, 2 * HD), low),
        ((heads, n, 3, HD, length), low),
        ((heads, PREFIX_ROWS, 2 * HD), low),
        ((heads, PREFIX_ROWS, HD), low),
        ((heads, HD, PREFIX_ROWS), low),
        ((planes, heads, HD + SUM_ROWS, 2 * length), f32),
        ((planes, heads, 8, 2 * length), f32),
    )
    square = pltpu.VMEM((width, width), low)
    qx, kx, raw, pk, pv, pkt, acc, stat = (pltpu.VMEM(*shape) for shape in shapes)
    return pl.pallas_call(
        functools.partial(self_forward_kernel, n),
        out_shape=(
            jax.ShapeDtypeStruct((length, width), low),
            jax.ShapeDtypeStruct((n * memory.shape[0], width), low),
            jax.ShapeDtypeStruct((n * memory.shape[0], width), low),
        )
        + tuple(jax.ShapeDtypeStruct(*shape) for shape in shapes),
        in_specs=[vmem] * 3
        + [anywhere] * 3
        + [vmem, anywhere, vmem, anywhere, vmem, vmem]
        + [anywhere] * 2,
        out_specs=(vmem,) + (anywhere,) * 10,
        scratch_shapes=[
            pltpu.VMEM((n, heads, 3, HD, length), low),
            raw,
            pltpu.VMEM((8, length), jnp.int32),
            pltpu.VMEM((n, 8, length), jnp.int32),
            kx,
            qx,
            pltpu.VMEM((heads, HD + SUM_ROWS, whole), low),
            pltpu.VMEM((PREFIX_ROWS, weights[0].shape[0] // 2), f32),
            pk,
            pv,
            pkt,
            pltpu.VMEM((heads, HD + SUM_ROWS, PREFIX_ROWS), low),
            stat,
            acc,
            pltpu.VMEM((heads, n, HD, length), low),
            pltpu.VMEM((n, heads, HD, length), low),
            pltpu.VMEM((planes, 2) + memory.shape, low),
            square,
            square,
            pltpu.VMEM((n * memory.shape[0], width), low),
            pltpu.VMEM((n * memory.shape[0], width), low),
            square,
            square,
            square,
            pltpu.VMEM(prefix[1].shape, low),
            pltpu.VMEM(prefix[3].shape, low),
            dma((heads, n)),
            dma((heads, n)),
            dma((n,)),
            dma((n,)),
            dma((heads, n)),
            dma((heads, n)),
            dma((2, planes + 1)),
            dma((planes + 1,)),
            dma((10,)),
            dma((width // (2 * LANES), 3)),
            dma((4,)),
        ],
        compiler_params=pltpu.CompilerParams(
            collective_id=0, has_side_effects=True, vmem_limit_bytes=VMEM_BYTES
        ),
        name="self_forward",
    )(segments, padding, tokens, *weights, *prefix, memory, *mem_weights)


def self_backward_kernel(
    n,
    batches,
    base_in,
    do_in,
    sums_in,
    mkey_in,
    mvalue_in,
    wck_in,
    wcv_in,
    vecs_in,
    qx_in,
    kx_in,
    raw_in,
    pk_in,
    pv_in,
    pkt_in,
    ot_in,
    lse_in,
    wq_in,
    wk_in,
    wv_in,
    tg_ref,
    mgrad_ref,
    pkv_ref,
    vecs_ref,
    full_out,
    do_recv,
    qx,
    kx,
    raw,
    kt,
    values,
    dot,
    qdo,
    pk,
    pv,
    pkt,
    ot,
    stat,
    weights,
    dqt,
    dkv,
    g_send,
    g_recv,
    pre_ref,
    pre_all,
    pre_sum,
    pre_recv,
    sums_mine,
    sums_core,
    sums_x,
    sums_side,
    sums_z,
    full,
    mkey,
    mvalue,
    wck,
    wcv,
    mem_part,
    mem_side,
    mem_up,
    mem_down,
    vec_all,
    vec_sum,
    vec_y,
    vec_both,
    vec_z,
    product,
    base_ref,
    do_send_sem,
    do_recv_sem,
    g_send_sem,
    g_recv_sem,
    in_sem,
    send_sem,
    recv_sem,
):
    low = jnp.bfloat16
    f32 = jnp.float32
    me = lax.axis_index("seq")
    length, width = tg_ref.shape
    group = width // n
    heads = group // HD
    plane = 2 * length
    planes = n // 2
    step_rows = 256
    my_batch = lax.axis_index("batch")
    my_core = lax.rem(my_batch, 2)
    my_high = my_batch // 2
    highs = batches // 2
    my_plane = me // 2
    my_side = lax.rem(me, 2)
    beside = me + 1 - 2 * my_side
    used = [0]

    def numbers(count):
        used[0] += count
        return used[0] - count

    core_slot = numbers(2)
    x_slot = numbers(2 * highs)
    y_slot = numbers(3)
    z_slot = numbers(2 * planes)
    up_slot = numbers(planes)
    down_slot = numbers(planes)
    va_slot = numbers(batches)
    vb_slot = numbers(1)
    vc_slot = numbers(planes)
    pa_slot = numbers(batches)
    pb_slot = numbers(n)

    def send(source, target, first, peer_index, slot_index, axis, peer):
        return remote(
            source,
            target,
            send_sem.at[first + peer_index],
            recv_sem.at[first + slot_index],
            axis,
            peer,
        )

    half_rows = 2 * planes * highs * sums_z.shape[1]
    x_rows = half_rows // highs
    y_rows = x_rows // 2
    z_rows = y_rows // planes
    x_row = pl.multiple_of(my_high * x_rows, x_rows)
    y_row = pl.multiple_of(x_row + my_side * y_rows, y_rows)

    def part(row, count):
        return sums_mine.at[pl.ds(pl.multiple_of(row, count), count)]

    def reduce_core():
        return send(
            sums_in.at[1 - my_core], sums_core, core_slot, 0, 0, "batch", my_batch + 1 - 2 * my_core
        )

    def reduce_x(peer, slot):
        return send(
            part(peer * x_rows, x_rows),
            sums_x.at[slot],
            x_slot,
            peer,
            slot,
            "batch",
            2 * peer + my_core,
        )

    def reduce_y():
        return send(
            part(x_row + (1 - my_side) * y_rows, y_rows), sums_side, y_slot, 0, 0, "seq", beside
        )

    def reduce_z(peer, slot):
        return send(
            part(y_row + peer * z_rows, z_rows),
            sums_z.at[slot],
            z_slot,
            peer,
            slot,
            "seq",
            2 * peer + my_side,
        )

    def gather_z(peer, slot):
        piece = full.at[my_core, my_high, my_side, slot]
        return send(piece, piece, z_slot + planes, peer, slot, "seq", 2 * peer + my_side)

    def gather_y(side):
        piece = full.at[my_core, my_high, side]
        return send(piece, piece, y_slot + 1, 0, 0, "seq", beside)

    def gather_x(peer, slot):
        piece = full.at[my_core, slot]
        return send(piece, piece, x_slot + highs, peer, slot, "batch", 2 * peer + my_core)

    def gather_core(core):
        piece = full.at[core]
        return send(piece, piece, core_slot + 1, 0, 0, "batch", my_batch + 1 - 2 * my_core)

    def mem_across():
        return send(
            mem_part.at[:, 1 - my_side], mem_side, y_slot + 2, 0, 0, "seq", beside
        )

    def mem_hop(target, toward, peer=None):
        buffer, slot = (mem_up, up_slot) if toward > 0 else (mem_down, down_slot)
        return send(
            mem_part.at[target, my_side],
            buffer.at[target],
            slot,
            target,
            target,
            "seq",
            me + 2 * toward if peer is None else peer,
        )

    def mem_from(target, toward):
        return mem_hop(target, toward, me - 2 * toward)

    def mem_pass(toward):
        buffer = mem_up if toward > 0 else mem_down
        first = 0 if toward > 0 else planes - 1
        for target in range(planes):

            @pl.when((target - my_plane) * toward > 0)
            def _():
                @pl.when(my_plane != first)
                def _():
                    mem_from(target, toward).wait_recv()
                    mem_part[target, my_side] = (
                        mem_part[target, my_side].astype(f32) + buffer[target].astype(f32)
                    ).astype(low)

                mem_hop(target, toward).start()

    def mem_stage(at):
        pl.when(my_plane == at)(lambda: mem_pass(1))
        pl.when(my_plane == planes - 1 - at)(lambda: mem_pass(-1))

    def mem_end():
        value = mem_part[my_plane, my_side].astype(f32)
        mgrad_ref[...] = value.astype(low)

        @pl.when(my_plane > 0)
        def _():
            mem_from(my_plane, 1).wait_recv()
            mgrad_ref[...] = (mgrad_ref[...].astype(f32) + mem_up[my_plane].astype(f32)).astype(low)

        @pl.when(my_plane < planes - 1)
        def _():
            mem_from(my_plane, -1).wait_recv()
            mgrad_ref[...] = (
                mgrad_ref[...].astype(f32) + mem_down[my_plane].astype(f32)
            ).astype(low)

    def mem_drain():
        for target in range(planes):

            @pl.when(target > my_plane)
            def _():
                mem_hop(target, 1).wait_send()

            @pl.when(target < my_plane)
            def _():
                mem_hop(target, -1).wait_send()

    def vec_a(peer, slot):
        return send(vecs_in, vec_all.at[slot], va_slot, peer, slot, "batch", peer)

    def vec_b(side):
        return send(vec_sum, vec_y.at[side], vb_slot, 0, 0, "seq", beside)

    def vec_c(peer, slot):
        return send(vec_both, vec_z.at[slot], vc_slot, peer, slot, "seq", 2 * peer + my_side)

    def pre_a(peer, slot):
        return send(pre_ref, pre_all.at[slot], pa_slot, peer, slot, "batch", peer)

    def pre_b(peer, slot):
        return send(pre_sum, pre_recv.at[slot], pb_slot, peer, slot, "seq", peer)

    def do_copy(head, peer, slot):
        return remote(
            do_in.at[peer, head],
            do_recv.at[head, slot],
            do_send_sem.at[head, peer],
            do_recv_sem.at[head, slot],
            "seq",
            peer,
        )

    def q_copy(head, peer, slot):
        return remote(
            g_send.at[peer, head, 0],
            g_recv.at[0, slot, head],
            g_send_sem.at[0, head, peer],
            g_recv_sem.at[0, head, slot],
            "seq",
            peer,
        )

    def kv_copy(head, peer, slot):
        return remote(
            g_send.at[peer, head, pl.ds(1, 2)],
            g_recv.at[pl.ds(1, 2), slot, head],
            g_send_sem.at[1, head, peer],
            g_recv_sem.at[1, head, slot],
            "seq",
            peer,
        )

    def added(ref, size):
        value = ref[0].astype(f32)
        for other in range(1, size):
            value = value + ref[other].astype(f32)
        return value

    loads = [
        pltpu.make_async_copy(source, target, in_sem.at[index])
        for index, (source, target) in enumerate(
            (
                (raw_in, raw),
                (kx_in, kx),
                (pk_in, pk),
                (pv_in, pv),
                (pkt_in, pkt),
                (qx_in, qx),
                (ot_in, ot),
                (lse_in, stat),
                (sums_in.at[my_core], sums_mine),
                (vecs_in, vec_all.at[my_batch]),
                (mkey_in, mkey),
                (mvalue_in, mvalue),
                (wck_in, wck),
                (wcv_in, wcv),
                (base_in, base_ref),
                (wq_in, weights.at[0]),
                (wk_in, weights.at[1]),
                (wv_in, weights.at[2]),
            )
        )
    ]
    own_do = pltpu.make_async_copy(do_in.at[me], do_recv.at[:, me], in_sem.at[len(loads)])
    own_do.start()
    for load in loads:
        load.start()
    enter({"seq": n, "batch": batches})
    others(n, me, lambda peer: do_copy(0, peer, me).start())
    reduce_core().start()
    others(batches, my_batch, lambda peer: vec_a(peer, my_batch).start())
    dkv[...] = jnp.zeros_like(dkv)
    product[...] = jnp.zeros_like(product)
    pre_ref[...] = jnp.zeros_like(pre_ref)
    for load in loads[:14]:
        load.wait()
    own_do.wait()

    def turn(index, carry):
        head = index // n
        chunk = lax.rem(index, n)
        here = rows_of(chunk, length)
        kt[head, :, here] = raw[head, chunk, 1]
        values[head, here, :] = raw[head, chunk, 2].astype(f32).T.astype(low)
        return carry

    lax.fori_loop(0, heads * n, turn, 0)

    def memory_back(index, carry):
        here = rows_of(index, step_rows)
        value = dot_nt(mkey[...], wck[here, :]) + dot_nt(mvalue[...], wcv[here, :])
        mem_part[:, :, :, here] = value.astype(low).reshape(mem_part.shape[:3] + (step_rows,))
        return carry

    lax.fori_loop(0, width // step_rows, memory_back, 0)
    mem_across().start()

    def next_head(head):
        def move(peer):
            do_copy(head, peer, me).wait_send()
            do_copy(head + 1, peer, me).start()

        others(n, me, move)

    def arrive(head, which):
        for part in range(2):
            chunk = 2 * which + part

            @pl.when(chunk != me)
            def _():
                do_copy(head, chunk, chunk).wait_recv()

            grads = do_recv[head, chunk]
            dot[head, :, rows_of(chunk, length)] = grads
            grads = grads.astype(f32)
            query = raw[head, chunk, 0].astype(f32) * 0.125
            qdo[head, rows_of(chunk, length), :] = (
                jnp.concatenate([query, grads], axis=0).T.astype(low)
            )
            here = slice(part * length, (part + 1) * length)
            stat[which, head, 1:2, here] = jnp.sum(
                grads * ot[which, head, :HD, here], axis=0, keepdims=True
            )
        here = rows_of(which, plane)
        weight = jnp.exp(dot_nn(pk[head], qx[head, :, here]) - stat[which, head, 0:1, :])
        slope = weight * (dot_nn(pv[head], dot[head, :, here]) - stat[which, head, 1:2, :])
        both = jnp.concatenate([slope, weight], axis=0).astype(low)
        sums = dot_nn(both, qdo[head, here, :])
        pre_ref[head] += jnp.where(
            head_lanes((PREFIX_ROWS, 2 * HD), 0), sums[:PREFIX_ROWS], sums[PREFIX_ROWS:]
        )
        slope = slope.astype(low)
        dqt[which, head] = dot_nn(pkt[head], slope)

    def plus(first, second):
        return (first.astype(f32) + second.astype(f32)).astype(low)

    def sum_one():
        reduce_core().wait_recv()
        sums_mine[...] = plus(sums_mine[...], sums_core[...])
        others(highs, my_high, lambda peer: reduce_x(peer, my_high).start())

    def sum_two():
        here = pl.ds(x_row, x_rows)
        others(highs, my_high, lambda peer: reduce_x(peer, peer).wait_recv())
        sums_x[my_high] = sums_mine[here]
        sums_mine[here] = added(sums_x, highs).astype(low)
        reduce_y().start()

    def sum_three():
        here = pl.ds(y_row, y_rows)
        reduce_y().wait_recv()
        sums_mine[here] = plus(sums_mine[here], sums_side[...])
        others(planes, my_plane, lambda peer: reduce_z(peer, my_plane).start())

    def sum_four():
        here = pl.ds(pl.multiple_of(y_row + my_plane * z_rows, z_rows), z_rows)
        others(planes, my_plane, lambda peer: reduce_z(peer, peer).wait_recv())
        sums_z[my_plane] = sums_mine[here]
        full[my_core, my_high, my_side, my_plane] = added(sums_z, planes).astype(low)
        others(planes, my_plane, lambda peer: gather_z(peer, my_plane).start())

    def sum_five():
        others(planes, my_plane, lambda peer: gather_z(peer, peer).wait_recv())
        gather_y(my_side).start()

    def sum_six():
        gather_y(1 - my_side).wait_recv()
        others(highs, my_high, lambda peer: gather_x(peer, my_high).start())

    def sum_seven():
        others(highs, my_high, lambda peer: gather_x(peer, peer).wait_recv())
        gather_core(my_core).start()

    def sum_end():
        gather_core(1 - my_core).wait_recv()
        save_full.start()

    def vec_one():
        others(batches, my_batch, lambda peer: vec_a(peer, peer).wait_recv())
        vec_sum[...] = added(vec_all, batches)
        vec_b(my_side).start()
        vec_y[my_side] = vec_sum[...]

    def vec_two():
        vec_b(1 - my_side).wait_recv()
        value = (vec_y[0] + vec_y[1]).astype(f32)
        vec_both[...] = jnp.concatenate(
            [value[:, : width // 2], value[:, width // 2 :]], axis=0
        ).astype(low)
        others(planes, my_plane, lambda peer: vec_c(peer, my_plane).start())
        vec_z[my_plane] = vec_both[...]

    def vec_end():
        others(planes, my_plane, lambda peer: vec_c(peer, peer).wait_recv())
        value = added(vec_z, planes)
        vecs_ref[:, : width // 2] = value[:8]
        vecs_ref[:, width // 2 :] = value[8:]

    def mem_one():
        mem_across().wait_recv()
        mem_part[:, my_side] = plus(mem_part[:, my_side], mem_side[...])

    def stage_pa():
        others(batches, my_batch, lambda peer: pre_a(peer, my_batch).start())
        pre_all[my_batch] = pre_ref[...]

    def stage_pb():
        others(batches, my_batch, lambda peer: pre_a(peer, peer).wait_recv())
        pre_sum[...] = added(pre_all, batches).astype(low)
        others(n, me, lambda peer: pre_b(peer, me).start())
        pre_recv[me] = pre_sum[...]

    save_full = pltpu.make_async_copy(full, full_out, in_sem.at[0])

    def pair_part(head, upper, lower, first, count, diagonal):
        keys = span_of(lower * plane + first, count)
        here = span_of(upper * plane + first, plane - first)
        at = slice(first, plane)
        scores = dot_nn(kx[head, keys, :], qx[head, :, here])
        slope = dot_nn(values[head, keys, :], dot[head, :, here]) - stat[upper, head, 1:2, at]
        weight = jnp.exp(scores - stat[upper, head, 0:1, at])
        if diagonal:
            key_at = lax.broadcasted_iota(jnp.int32, scores.shape, 0)
            query_at = lax.broadcasted_iota(jnp.int32, scores.shape, 1)
            weight = jnp.where(key_at <= query_at, weight, 0.0)
        both = jnp.concatenate([(weight * slope).astype(low), weight.astype(low)], axis=0)
        sums = dot_nn(both, qdo[head, here, :])
        dkv[head, keys, :] += jnp.where(
            head_lanes((count, 2 * HD), 0), sums[:count], sums[count:]
        )
        dqt[upper, head, :, at] += dot_nn(kt[head, :, keys], both[:count])

    def pair(head, upper, lower, diagonal):
        if diagonal:
            pair_part(head, upper, lower, 0, length, True)
            pair_part(head, upper, lower, length, length, True)
        else:
            pair_part(head, upper, lower, 0, plane, False)

    def hand_queries(head, which):
        for part in range(2):
            chunk = 2 * which + part
            g_send[chunk, head, 0] = (
                dqt[which, head, :, part * length : (part + 1) * length] * 0.125
            ).astype(low)

            @pl.when(chunk != me)
            def _():
                q_copy(head, chunk, me).start()

            @pl.when(chunk == me)
            def _():
                g_recv[0, me, head] = g_send[chunk, head, 0]

    def hand_keys(head, which):
        for part in range(2):
            chunk = 2 * which + part
            turned = dkv[head, rows_of(chunk, length), :].T.astype(low)
            g_send[chunk, head, 1] = turned[:HD]
            g_send[chunk, head, 2] = turned[HD:]

            @pl.when(chunk != me)
            def _():
                kv_copy(head, chunk, me).start()

            @pl.when(chunk == me)
            def _():
                g_recv[pl.ds(1, 2), me, head] = g_send[chunk, head, pl.ds(1, 2)]

    rising = my_plane >= planes // 2
    total = heads * planes * (planes + 1) // 2
    hooks = [
        (2, sum_one),
        (3, mem_one),
        (4, lambda: mem_stage(0)),
        (5, vec_one),
        (5, sum_two),
        (7, sum_three),
        (8, vec_two),
        (10, sum_four),
        (12, sum_five),
        (14, sum_six),
        (16, vec_end),
        (17, sum_seven),
    ] + [(4 + 3 * at, functools.partial(mem_stage, at)) for at in range(1, planes - 1)]
    hooks += [
        (1 + head * total // heads, functools.partial(next_head, head)) for head in range(heads - 1)
    ]
    final = total - planes * (planes + 1) // 2
    hooks += [(final + planes + 1, stage_pa), (final + 2 * planes - 1, stage_pb)]

    def hook(pairs):
        for number, body in sorted(hooks, key=lambda item: item[0]):
            pl.when(pairs == number)(body)


    def stage(index, carry):
        head = index // planes
        step = lax.rem(index, planes)
        here = jnp.where(rising, step, planes - 1 - step)

        @pl.when((step == 0) | ((step == 1) & jnp.logical_not(rising)))
        def _():
            @pl.when(rising | (step == 0))
            def _():
                arrive(head, here)

            @pl.when(jnp.logical_not(rising) & (step == 1))
            def _():
                def rest(which, inner):
                    arrive(head, planes - 2 - which)
                    return inner

                lax.fori_loop(0, planes - 1, rest, 0)

        begun = head * (planes * (planes + 1) // 2) + step * planes - step * (step - 1) // 2
        hook(begun)
        pair(head, here, here, True)

        @pl.when(rising)
        def _():
            hand_queries(head, here)

        @pl.when(jnp.logical_not(rising))
        def _():
            hand_keys(head, here)

        def far(at, inner):
            there = jnp.where(rising, here + 1 + at, here - 1 - at)

            @pl.when(rising & (step == 0))
            def _():
                arrive(head, there)

            hook(begun + 1 + at)
            pair(head, jnp.maximum(here, there), jnp.minimum(here, there), False)
            return inner

        lax.fori_loop(0, planes - 1 - step, far, 0)

        @pl.when(rising)
        def _():
            hand_keys(head, here)

        @pl.when(jnp.logical_not(rising))
        def _():
            hand_queries(head, here)

        return carry

    lax.fori_loop(0, heads * planes, stage, 0)
    mem_end()
    for load in loads[14:]:
        load.wait()

    def gathered(peer):
        for head in range(heads):
            q_copy(head, peer, peer).wait_recv()
            kv_copy(head, peer, peer).wait_recv()

    half = width // 2

    def gather_plane(step, carry):
        which = lax.rem(my_plane + step, planes)
        for part in range(2):
            peer = 2 * which + part

            @pl.when(peer != me)
            def _():
                gathered(peer)

        columns = rows_of(which, 2 * group)
        for part in range(2):
            here = slice(part * half, (part + 1) * half)
            value = product[here, :]
            for kind in range(3):
                grads = g_recv[kind, pl.ds(2 * which, 2)].reshape(2 * group, length)
                value = value + dot_nn(weights[kind, here, columns], grads)
            product[here, :] = value
        return carry

    lax.fori_loop(0, planes, gather_plane, 0)
    sum_end()
    tile = 256
    for index in range(width // tile):
        here = slice(index * tile, (index + 1) * tile)
        tg_ref[:, here] = (base_ref[:, here] + product[here, :].T).astype(low)
    for other in range(n):

        @pl.when(other != me)
        def _():
            pre_b(other, other).wait_recv()

        value = pre_recv[other].astype(f32)
        for which in range(2):
            pkv_ref[:, which * width + other * group : which * width + (other + 1) * group] = (
                jnp.concatenate(
                    [value[head, :, which * HD : (which + 1) * HD] for head in range(heads)], axis=1
                )
            )

    def drain(peer):
        do_copy(heads - 1, peer, me).wait_send()
        pre_b(peer, me).wait_send()
        for head in range(heads):
            q_copy(head, peer, me).wait_send()
            kv_copy(head, peer, me).wait_send()

    others(n, me, drain)
    others(batches, my_batch, lambda peer: pre_a(peer, my_batch).wait_send())
    others(batches, my_batch, lambda peer: vec_a(peer, my_batch).wait_send())
    reduce_core().wait_send()
    others(highs, my_high, lambda peer: reduce_x(peer, my_high).wait_send())
    reduce_y().wait_send()
    others(planes, my_plane, lambda peer: reduce_z(peer, my_plane).wait_send())
    others(planes, my_plane, lambda peer: gather_z(peer, my_plane).wait_send())
    gather_y(my_side).wait_send()
    others(highs, my_high, lambda peer: gather_x(peer, my_high).wait_send())
    gather_core(my_core).wait_send()
    mem_across().wait_send()
    mem_drain()
    others(planes, my_plane, lambda peer: vec_c(peer, my_plane).wait_send())
    vec_b(my_side).wait_send()
    save_full.wait()


def self_backward(
    n, batches, first_grad, out_grad, sums, mem_grads, mem_weights, vecs, saved, weights
):
    length, width = first_grad.shape
    group = width // n
    heads = group // HD
    whole = n * length
    planes = n // 2
    low = jnp.bfloat16
    f32 = jnp.float32
    vmem = pl.BlockSpec(memory_space=pltpu.VMEM)
    anywhere = pl.BlockSpec(memory_space=pl.ANY)
    dma = pltpu.SemaphoreType.DMA
    sum_rows = sums.shape[0] // (n * batches)
    mem_len = mem_grads[0].shape[0]
    mem_rows = mem_len // n
    mem_part = pltpu.VMEM((planes, mem_rows, width), low)
    mem_low = pltpu.VMEM((mem_len, width), low)
    square = pltpu.VMEM((width, width), low)
    vec = pltpu.VMEM((8, width), f32)
    copies = 6 + 2 * (batches // 2) + 5 * planes + 2 * batches + n
    qx, kx, raw, pk, pv, pkt, ot, stat = (pltpu.VMEM(value.shape, value.dtype) for value in saved)
    return pl.pallas_call(
        functools.partial(self_backward_kernel, n, batches),
        out_shape=(
            jax.ShapeDtypeStruct((length, width), low),
            jax.ShapeDtypeStruct((mem_rows, width), low),
            jax.ShapeDtypeStruct((PREFIX_ROWS, 2 * width), f32),
            jax.ShapeDtypeStruct((8, width), f32),
            jax.ShapeDtypeStruct((2, batches // 2, 2, planes, sum_rows, LANES), low),
        ),
        in_specs=[anywhere] * 19,
        out_specs=(vmem, vmem, vmem, vmem, anywhere),
        scratch_shapes=[
            pltpu.VMEM((heads, n, HD, length), low),
            qx,
            kx,
            raw,
            pltpu.VMEM((heads, HD, whole), low),
            pltpu.VMEM((heads, whole, HD), low),
            pltpu.VMEM((heads, HD, whole), low),
            pltpu.VMEM((heads, whole, 2 * HD), low),
            pk,
            pv,
            pkt,
            ot,
            stat,
            pltpu.VMEM((3, width, width), low),
            pltpu.VMEM((planes, heads, HD, 2 * length), f32),
            pltpu.VMEM((heads, whole, 2 * HD), f32),
            pltpu.VMEM((n, heads, 3, HD, length), low),
            pltpu.VMEM((3, n, heads, HD, length), low),
            pltpu.VMEM((heads, PREFIX_ROWS, 2 * HD), f32),
            pltpu.VMEM((batches, heads, PREFIX_ROWS, 2 * HD), f32),
            pltpu.VMEM((heads, PREFIX_ROWS, 2 * HD), low),
            pltpu.VMEM((n, heads, PREFIX_ROWS, 2 * HD), low),
            pltpu.VMEM((sums.shape[0] // 2, LANES), low),
            pltpu.VMEM((sums.shape[0] // 2, LANES), low),
            pltpu.VMEM((batches // 2, sums.shape[0] // batches, LANES), low),
            pltpu.VMEM((planes * sum_rows, LANES), low),
            pltpu.VMEM((planes, sum_rows, LANES), low),
            pltpu.VMEM((2, batches // 2, 2, planes, sum_rows, LANES), low),
            mem_low,
            mem_low,
            square,
            square,
            pltpu.VMEM((planes, 2, mem_rows, width), low),
            mem_part,
            mem_part,
            mem_part,
            pltpu.VMEM((batches, 8, width), f32),
            vec,
            pltpu.VMEM((2, 8, width), f32),
            pltpu.VMEM((16, width // 2), low),
            pltpu.VMEM((planes, 16, width // 2), low),
            pltpu.VMEM((width, length), f32),
            pltpu.VMEM((length, width), f32),
            dma((heads, n)),
            dma((heads, n)),
            dma((2, heads, n)),
            dma((2, heads, n)),
            dma((19,)),
            dma((copies,)),
            dma((copies,)),
        ],
        compiler_params=pltpu.CompilerParams(
            collective_id=1, has_side_effects=True, vmem_limit_bytes=VMEM_BYTES
        ),
        name="self_backward",
    )(
        first_grad,
        out_grad,
        sums.reshape(2, -1, LANES),
        *mem_grads,
        *mem_weights,
        vecs,
        *saved,
        *weights,
    )


def both_parts(value):
    high = value.astype(jnp.bfloat16).astype(jnp.float32)
    return jnp.concatenate([high, value - high], axis=0).astype(jnp.bfloat16)


def finish_kernel(
    full_in,
    vecs_ref,
    pkv_ref,
    emb_ref,
    first_in,
    fbias_ref,
    second_in,
    token_in,
    mem_in,
    embed_out,
    first_out,
    fbias_out,
    second_out,
    sbias_out,
    down_out,
    dbias_out,
    raise_out,
    rbias_out,
    gain_out,
    shift_out,
    token_out,
    mem_out,
    full_ref,
    first_ref,
    second_ref,
    token_ref,
    mem_ref,
    first_grad,
    second_grad,
    down_grad,
    raise_grad,
    emb,
    hidden,
    out_sem,
    in_sem,
):
    f32 = jnp.float32
    low = jnp.bfloat16
    width = emb_ref.shape[1]
    down = dbias_out.shape[1]
    count = emb_ref.shape[0]
    first = down * width // LANES
    loads = [
        pltpu.make_async_copy(source, target, in_sem.at[index])
        for index, (source, target) in enumerate(
            (
                (full_in.at[first:], full_ref.at[first:]),
                (full_in.at[:first], full_ref.at[:first]),
                (first_in, first_ref),
                (second_in, second_ref),
                (token_in, token_ref),
                (mem_in, mem_ref),
            )
        )
    ]
    for load in loads:
        load.start()
    saves = []

    def save(source, target, rows=None):
        if rows is not None:
            source, target = source.at[rows], target.at[rows]
        copy = pltpu.make_async_copy(source, target, out_sem.at[len(saves)])
        copy.start()
        saves.append(copy)

    loads[0].wait()
    for index in range(width // LANES):
        raise_grad[:, index * LANES : (index + 1) * LANES] = full_ref[
            first + index * down : first + (index + 1) * down, :
        ].astype(f32)
    save(raise_grad, raise_out)
    loads[1].wait()
    for index in range(down // LANES):
        down_grad[:, index * LANES : (index + 1) * LANES] = full_ref[
            index * width : (index + 1) * width, :
        ].astype(f32)
    save(down_grad, down_out)
    for load in loads[4:]:
        load.wait()
    save(token_ref, token_out)
    save(mem_ref, mem_out)
    loads[2].wait()
    emb[...] = jnp.zeros_like(emb)
    emb[:count, :] = emb_ref[...].astype(f32)
    emb_low = emb[...].astype(low)
    row = lax.broadcasted_iota(jnp.int32, hidden.shape, 0)
    hidden[...] = jnp.where(
        row < count, jnp.tanh(dot_nn(emb_low, first_ref[...]) + fbias_ref[...]), 0.0
    )
    value = hidden[...]
    prefix = pkv_ref[...]
    parts = both_parts(prefix)
    hidden_twice = jnp.concatenate([value, value], axis=0).T.astype(low)
    tile = 128
    for index in range(second_grad.shape[0] // tile):
        here = slice(index * tile, (index + 1) * tile)
        second_grad[here, :] = dot_nn(hidden_twice[here, :], parts)
        save(second_grad, second_out, here)
    sbias_out[...] = jnp.sum(prefix, axis=0, keepdims=True)
    loads[3].wait()
    grad = dot_nt(parts, second_ref[...])
    grad = (grad[:PREFIX_ROWS] + grad[PREFIX_ROWS:]) * (1.0 - value * value)
    fbias_out[...] = jnp.sum(grad, axis=0, keepdims=True)
    parts = both_parts(grad)
    emb_twice = jnp.concatenate([emb[...], emb[...]], axis=0).T.astype(low)
    first_grad[...] = dot_nn(emb_twice, parts)
    save(first_grad, first_out)
    back = dot_nt(parts, first_ref[...])
    embed_out[...] = (back[:PREFIX_ROWS] + back[PREFIX_ROWS:])[:count, :]
    rbias_out[...] = vecs_ref[0:1, :]
    dbias_out[...] = vecs_ref[1:2, :down]
    gain_out[...] = vecs_ref[2:5, :]
    shift_out[...] = vecs_ref[5:8, :]
    for copy in saves:
        copy.wait()


def finish(full, vecs, prefix_grad, embed, first, first_bias, second, down, token_grad, memory_grad):
    f32 = jnp.float32
    count, width = embed.shape
    hidden = first.shape[1]
    vmem = pl.BlockSpec(memory_space=pltpu.VMEM)
    anywhere = pl.BlockSpec(memory_space=pl.ANY)
    shapes = (
        (count, width),
        (width, hidden),
        (1, hidden),
        (hidden, 2 * width),
        (1, 2 * width),
        (width, down),
        (1, down),
        (down, width),
        (1, width),
        (3, width),
        (3, width),
    )
    return pl.pallas_call(
        finish_kernel,
        out_shape=tuple(jax.ShapeDtypeStruct(shape, f32) for shape in shapes)
        + tuple(
            jax.ShapeDtypeStruct(value.shape, value.dtype) for value in (token_grad, memory_grad)
        ),
        in_specs=[anywhere, vmem, vmem, vmem, anywhere, vmem, anywhere, anywhere, anywhere],
        out_specs=(
            vmem,
            anywhere,
            vmem,
            anywhere,
            vmem,
            anywhere,
            vmem,
            anywhere,
            vmem,
            vmem,
            vmem,
            anywhere,
            anywhere,
        ),
        scratch_shapes=[
            pltpu.VMEM(full.shape, jnp.bfloat16),
            pltpu.VMEM(first.shape, jnp.bfloat16),
            pltpu.VMEM(second.shape, jnp.bfloat16),
            pltpu.VMEM(token_grad.shape, token_grad.dtype),
            pltpu.VMEM(memory_grad.shape, memory_grad.dtype),
            pltpu.VMEM((width, hidden), f32),
            pltpu.VMEM((hidden, 2 * width), f32),
            pltpu.VMEM((width, down), f32),
            pltpu.VMEM((down, width), f32),
            pltpu.VMEM((PREFIX_ROWS, width), f32),
            pltpu.VMEM((PREFIX_ROWS, hidden), f32),
            pltpu.SemaphoreType.DMA((5 + hidden // 128,)),
            pltpu.SemaphoreType.DMA((6,)),
        ],
        compiler_params=pltpu.CompilerParams(vmem_limit_bytes=VMEM_BYTES),
        name="finish",
    )(full, vecs, prefix_grad, embed, first, first_bias, second, token_grad, memory_grad)


def gelu_pair(value):
    size = jnp.abs(value)
    step = 1.0 / (1.0 + (0.3275911 * 0.7071067811865476) * size)
    bell = jnp.exp(-0.5 * value * value)
    poly = step * (
        0.127414796
        + step
        * (-0.142248368 + step * (0.7107068705 + step * (-0.7265760135 + step * 0.5307027145)))
    )
    act = jnp.maximum(value, 0.0) - size * (poly * bell)
    turn = bell * (0.3989422804014327 * size - poly)
    return act, jnp.where(value >= 0.0, 1.0 + turn, -turn)


def normed(value):
    center = jnp.mean(value, axis=-1, keepdims=True)
    centered = value - center
    scale = lax.rsqrt(jnp.mean(centered * centered, axis=-1, keepdims=True) + norm_eps)
    return centered * scale, scale


def norm_back(grad, scale, unit):
    return scale * (
        grad
        - jnp.mean(grad, axis=-1, keepdims=True)
        - unit * jnp.mean(grad * unit, axis=-1, keepdims=True)
    )


def middle_kernel(
    tok_in,
    att_in,
    cot_in,
    mkey_in,
    mvalue_in,
    gain_ref,
    shift_ref,
    dbias_ref,
    rbias_ref,
    wo_in,
    wcq_in,
    wco_in,
    wd_in,
    wr_in,
    win_in,
    wout_in,
    layer_out,
    fgrad_out,
    ograd_out,
    mkey_out,
    mvalue_out,
    sums_out,
    vecs_ref,
    tok_ref,
    att_ref,
    cot_ref,
    mkey_ref,
    mvalue_ref,
    out_ref,
    fgrad_ref,
    ograd_ref,
    sums_ref,
    wo,
    wcq,
    wco,
    wd,
    wr,
    win,
    wout,
    unit_one,
    unit_two,
    work,
    total,
    scale_one,
    scale_two,
    low_one,
    low_two,
    low_three,
    query,
    crossed,
    weights,
    slopes,
    acts,
    down_act,
    down_slope,
    down_grad,
    load_sem,
    win_sem,
    wout_sem,
    out_sem,
):
    length, width = tok_ref.shape
    resident = len(win.shape) == 2
    tile = 512 if resident else win.shape[2]
    tiles = win_in.shape[1] // tile
    slots = tiles if resident else win.shape[0]
    rows_step = 128
    low = jnp.bfloat16
    f32 = jnp.float32

    sources = (
        att_in,
        wo_in,
        tok_in,
        wcq_in,
        mkey_in,
        mvalue_in,
        wco_in,
        wd_in,
        wr_in,
        cot_in,
    )
    targets = (att_ref, wo, tok_ref, wcq, mkey_ref, mvalue_ref, wco, wd, wr, cot_ref)
    loads = [
        pltpu.make_async_copy(source, target, load_sem.at[index])
        for index, (source, target) in enumerate(zip(sources, targets))
    ]

    def win_load(which):
        slot = which % slots
        target = win.at[:, rows_of(which, tile)] if resident else win.at[slot]
        return pltpu.make_async_copy(win_in.at[:, rows_of(which, tile)], target, win_sem.at[slot])

    def wout_load(which):
        slot = which % slots
        target = wout.at[rows_of(which, tile), :] if resident else wout.at[slot]
        return pltpu.make_async_copy(wout_in.at[rows_of(which, tile), :], target, wout_sem.at[slot])

    for load in loads[:7]:
        load.start()

    def by_columns(extent, step, body):
        def one(index, carry):
            body(pl.ds(pl.multiple_of(index * step, step), step))
            return carry

        lax.fori_loop(0, extent // step, one, 0)

    def by_rows(body, init=0):
        def one(index, carry):
            return body(rows_of(index, rows_step), carry)

        return lax.fori_loop(0, length // rows_step, one, init)

    cols = 512
    half = width // 2

    for load in loads[:3]:
        load.wait()
    for load in loads[7:]:
        load.start()
    for which in range(slots):
        win_load(which).start()
    for which in range(slots):
        wout_load(which).start()

    def project_out(here):
        work[:, here] = tok_ref[:, here].astype(f32) + dot_nn(att_ref[...], wo[:, here])

    by_columns(width, cols, project_out)

    def first_norm(here, carry):
        unit, scale = normed(work[here, :])
        unit_one[here, :] = unit
        scale_one[here, :] = scale
        value = unit * gain_ref[0:1, :] + shift_ref[0:1, :]
        work[here, :] = value
        low_one[here, :] = value.astype(low)
        return carry

    by_rows(first_norm)

    loads[3].wait()

    def project_query(here):
        query[:, here] = dot_nn(low_one[...], wcq[:, here]).astype(low)

    by_columns(width, cols, project_query)
    per_block = LANES // HD

    def head_queries(here, head):
        both = query[:, here].astype(f32) * 0.125
        return jnp.where(head_lanes(both.shape, head), both, 0.0).astype(low)

    def cross_forward(block):
        here = rows_of(block, LANES)
        keys = mkey_ref[:, here]
        values = mvalue_ref[:, here].astype(f32).T.astype(low)
        outs = []
        for head in range(per_block):
            scores = dot_nt(keys, head_queries(here, head))
            raised = jnp.exp(scores - jnp.max(scores, axis=0, keepdims=True))
            share = 1.0 / jnp.sum(raised, axis=0, keepdims=True)
            weight = (raised * share).astype(low)
            weights[block * per_block + head] = weight
            outs.append(dot_nn(values[head * HD : (head + 1) * HD, :], weight))
        crossed[:, here] = jnp.concatenate(outs, axis=0).T.astype(low)

    loads[4].wait()
    loads[5].wait()

    def cross_forward_four(step, carry):
        for part in range(4):
            cross_forward(4 * step + part)
        return carry

    lax.fori_loop(0, width // LANES // 4, cross_forward_four, 0)

    loads[6].wait()

    def project_crossed(here):
        work[:, here] += dot_nn(crossed[...], wco[:, here])

    by_columns(width, cols, project_crossed)

    def second_norm(here, carry):
        unit, scale = normed(work[here, :])
        unit_two[here, :] = unit
        scale_two[here, :] = scale
        value = unit * gain_ref[1:2, :] + shift_ref[1:2, :]
        work[here, :] = value
        low_two[here, :] = value.astype(low)
        return carry

    by_rows(second_norm)

    step_cols = 256

    def feed_part(here, source):
        act, slope = gelu_pair(dot_nn(low_two[...], source))
        slopes[:, here] = slope.astype(low)
        return act.astype(low)

    if resident:

        def feed_forward(which, carry):
            here = rows_of(which, step_cols)

            @pl.when(which % (tile // step_cols) == 0)
            def _():
                win_load(which // (tile // step_cols)).wait()

            acts[:, here] = feed_part(here, win[:, here])
            return carry

        lax.fori_loop(0, tiles * tile // step_cols, feed_forward, 0)
        for which in range(tiles):
            wout_load(which).wait()

        def feed_out_part(here):
            total[:, here] = dot_nn(acts[...], wout[:, here])

        by_columns(width, step_cols, feed_out_part)
    else:
        total[...] = jnp.zeros_like(total)

        def feed_forward(which, carry):
            slot = lax.rem(which, slots)
            win_load(which).wait()
            wout_load(which).wait()
            total[...] += dot_nn(feed_part(rows_of(which, tile), win[slot]), wout[slot])

            @pl.when(which + slots < tiles)
            def _():
                win_load(which + slots).start()
                wout_load(which + slots).start()

            return carry

        lax.fori_loop(0, tiles, feed_forward, 0)

    loads[7].wait()
    loads[8].wait()
    loads[9].wait()
    act, slope = gelu_pair(dot_nn(low_two[...], wd[...]) + dbias_ref[...])
    down_act[...] = act.astype(low)
    down_slope[...] = slope.astype(low)

    def project_raise(here):
        work[:, here] += total[:, here] + 4.0 * (
            dot_nn(down_act[...], wr[:, here]) + rbias_ref[:, here]
        )

    by_columns(width, cols, project_raise)
    nothing = jnp.zeros((1, width), f32)

    def third_norm(here, carry):
        gain_sum, shift_sum, bias_sum = carry
        unit, scale = normed(work[here, :])
        gain = gain_ref[2:3, :]
        out_ref[here, :] = (unit * gain + shift_ref[2:3, :]).astype(low)
        grad = cot_ref[here, :].astype(f32)
        back = norm_back(grad * gain, scale, unit)
        total[here, :] = back
        back_low = back.astype(low)
        low_three[here, :] = back_low
        return (
            gain_sum + jnp.sum(grad * unit, axis=0, keepdims=True),
            shift_sum + jnp.sum(grad, axis=0, keepdims=True),
            bias_sum + jnp.sum(back_low.astype(f32), axis=0, keepdims=True),
        )

    gain_three, shift_three, bias_sum = by_rows(third_norm, (nothing, nothing, nothing))
    saves = []

    def save(source, target):
        copy = pltpu.make_async_copy(source, target, out_sem.at[len(saves)])
        copy.start()
        saves.append(copy)

    save(out_ref, layer_out)
    vecs_ref[0:1, :] = 4.0 * bias_sum

    back = 4.0 * dot_nt(low_three[...], wr[...]) * down_slope[...].astype(f32)
    back_low = back.astype(low)
    down_grad[...] = back_low
    vecs_ref[1:2, :] = jnp.concatenate(
        [
            jnp.sum(back_low.astype(f32), axis=0, keepdims=True),
            jnp.zeros((1, width - wd.shape[1]), f32),
        ],
        axis=1,
    )
    down = wd.shape[1]
    raise_sum = 4.0 * dot_tn(down_act[...], low_three[...])
    for index in range(width // LANES):
        sums_ref[pl.ds(down * width // LANES + index * down, down), :] = raise_sum[
            :, index * LANES : (index + 1) * LANES
        ].astype(low)
    down_sum = dot_tn(low_two[...], down_grad[...])
    for index in range(down // LANES):
        sums_ref[index * width : (index + 1) * width, :] = down_sum[
            :, index * LANES : (index + 1) * LANES
        ].astype(low)

    save(sums_ref, sums_out)

    if resident:

        def feed_slope(here):
            acts[:, here] = (
                dot_nt(low_three[...], wout[here, :]) * slopes[:, here].astype(f32)
            ).astype(low)

        by_columns(win_in.shape[1], step_cols, feed_slope)

        def feed_in_part(here):
            total[:, here] += dot_nt(acts[...], win[here, :])

        by_columns(width, step_cols, feed_in_part)
    else:

        def feed_backward(step, carry):
            which = tiles - 1 - step
            slot = lax.rem(which, slots)
            here = rows_of(which, tile)

            @pl.when(which < tiles - slots)
            def _():
                wout_load(which).wait()
                win_load(which).wait()

            grad = dot_nt(low_three[...], wout[slot]) * slopes[:, here].astype(f32)
            total[...] += dot_nt(grad.astype(low), win[slot])

            @pl.when(which >= slots)
            def _():
                win_load(which - slots).start()
                wout_load(which - slots).start()

            return carry

        lax.fori_loop(0, tiles, feed_backward, 0)

    def down_back(here):
        total[:, here] += dot_nt(down_grad[...], wd[here, :])

    by_columns(width, cols, down_back)

    def second_back(here, carry):
        gain_sum, shift_sum = carry
        grad = total[here, :]
        unit = unit_two[here, :]
        back = norm_back(grad * gain_ref[1:2, :], scale_two[here, :], unit)
        total[here, :] = back
        low_one[here, :] = back.astype(low)
        return (
            gain_sum + jnp.sum(grad * unit, axis=0, keepdims=True),
            shift_sum + jnp.sum(grad, axis=0, keepdims=True),
        )

    gain_two, shift_two = by_rows(second_back, (nothing, nothing))

    def crossed_back(here):
        crossed[:, here] = dot_nt(low_one[...], wco[here, :]).astype(low)

    by_columns(width, cols, crossed_back)

    def cross_backward(block):
        here = rows_of(block, LANES)
        values = mvalue_ref[:, here]
        keys = mkey_ref[:, here].astype(f32).T.astype(low)
        grads = crossed[:, here].astype(f32)
        outs = []
        key_sum = None
        for head in range(per_block):
            grad = jnp.where(head_lanes(grads.shape, head), grads, 0.0).astype(low)
            weight_low = weights[block * per_block + head]
            weight = weight_low.astype(f32)
            slope = dot_nt(values, grad)
            slope = weight * (slope - jnp.sum(weight * slope, axis=0, keepdims=True))
            slope = slope.astype(low)
            key_part = dot_nn(slope, head_queries(here, head))
            value_part = dot_nn(weight_low, grad)
            if key_sum is None:
                key_sum, value_sum = key_part, value_part
            else:
                key_sum, value_sum = key_sum + key_part, value_sum + value_part
            outs.append(dot_nn(keys[head * HD : (head + 1) * HD, :], slope))
        mkey_ref[:, here] = key_sum.astype(low)
        mvalue_ref[:, here] = value_sum.astype(low)
        query[:, here] = (jnp.concatenate(outs, axis=0) * 0.125).T.astype(low)

    def cross_backward_four(step, carry):
        for part in range(4):
            cross_backward(4 * step + part)
        return carry

    lax.fori_loop(0, width // LANES // 4, cross_backward_four, 0)
    save(mkey_ref, mkey_out)
    save(mvalue_ref, mvalue_out)

    def query_back(here):
        total[:, here] += dot_nt(query[...], wcq[here, :])

    by_columns(width, cols, query_back)

    def first_back(here, carry):
        gain_sum, shift_sum = carry
        grad = total[here, :]
        unit = unit_one[here, :]
        back = norm_back(grad * gain_ref[0:1, :], scale_one[here, :], unit)
        fgrad_ref[here, :] = back
        low_one[here, :] = back.astype(low)
        return (
            gain_sum + jnp.sum(grad * unit, axis=0, keepdims=True),
            shift_sum + jnp.sum(grad, axis=0, keepdims=True),
        )

    gain_one, shift_one = by_rows(first_back, (nothing, nothing))
    save(fgrad_ref, fgrad_out)

    for index in range(width // cols):
        here = slice(index * cols, (index + 1) * cols)
        ograd_ref[here, :] = dot_nt(low_one[...], wo[here, :]).T.astype(low)
        save(ograd_ref.at[here], ograd_out.at[here])
    for index, vector in enumerate(
        (gain_one, gain_two, gain_three, shift_one, shift_two, shift_three)
    ):
        vecs_ref[2 + index : 3 + index, :] = vector
    for copy in saves:
        copy.wait()


def middle(
    tokens, attended, cotangent, mem_key, mem_value, gains, shifts, down_bias, raise_bias, weights
):
    length, width = tokens.shape
    mem_len = mem_key.shape[0]
    down = weights[3].shape[1]
    feed = weights[5].shape[1]
    tile = 512 if mem_len <= 512 else 128
    resident = mem_len <= 512
    slots = feed // tile if resident else 2
    low = jnp.bfloat16
    f32 = jnp.float32
    vmem = pl.BlockSpec(memory_space=pltpu.VMEM)
    anywhere = pl.BlockSpec(memory_space=pl.ANY)
    square = pltpu.VMEM((width, width), low)
    wide = pltpu.VMEM((length, width), f32)
    narrow = pltpu.VMEM((length, width), low)
    return pl.pallas_call(
        middle_kernel,
        out_shape=(
            jax.ShapeDtypeStruct((length, width), low),
            jax.ShapeDtypeStruct((length, width), f32),
            jax.ShapeDtypeStruct((width, length), low),
            jax.ShapeDtypeStruct((mem_len, width), low),
            jax.ShapeDtypeStruct((mem_len, width), low),
            jax.ShapeDtypeStruct((2 * down * width // LANES, LANES), low),
            jax.ShapeDtypeStruct((8, width), f32),
        ),
        in_specs=[anywhere] * 5 + [vmem] * 4 + [anywhere] * 7,
        out_specs=(anywhere,) * 6 + (vmem,),
        scratch_shapes=[
            narrow,
            narrow,
            narrow,
            pltpu.VMEM((mem_len, width), low),
            pltpu.VMEM((mem_len, width), low),
            narrow,
            wide,
            pltpu.VMEM((width, length), low),
            pltpu.VMEM((2 * down * width // LANES, LANES), low),
            square,
            square,
            square,
            pltpu.VMEM((width, down), low),
            pltpu.VMEM((down, width), low),
            pltpu.VMEM((width, feed) if resident else (slots, width, tile), low),
            pltpu.VMEM((feed, width) if resident else (slots, tile, width), low),
            wide,
            wide,
            wide,
            wide,
            pltpu.VMEM((length, 1), f32),
            pltpu.VMEM((length, 1), f32),
            narrow,
            narrow,
            narrow,
            narrow,
            narrow,
            pltpu.VMEM((H, mem_len, length), low),
            pltpu.VMEM((length, feed), low),
            pltpu.VMEM((length, feed) if resident else (16, LANES), low),
            pltpu.VMEM((length, down), low),
            pltpu.VMEM((length, down), low),
            pltpu.VMEM((length, down), low),
            pltpu.SemaphoreType.DMA((10,)),
            pltpu.SemaphoreType.DMA((slots,)),
            pltpu.SemaphoreType.DMA((slots,)),
            pltpu.SemaphoreType.DMA((5 + width // 512,)),
        ],
        compiler_params=pltpu.CompilerParams(vmem_limit_bytes=VMEM_BYTES + 3 * 1024 * 1024),
        name="middle",
    )(tokens, attended, cotangent, mem_key, mem_value, gains, shifts, down_bias, raise_bias, *weights)


def per_device(
    tokens,
    memory,
    segment_ids,
    padding_mask,
    cotangent,
    prefix_embed,
    prefix_first,
    first_bias,
    prefix_second,
    second_bias,
    adapter_down,
    down_bias,
    adapter_raise,
    raise_bias,
    norm_gain,
    norm_shift,
    self_query,
    self_key,
    self_value,
    self_output,
    cross_query,
    cross_key,
    cross_value,
    cross_output,
    feed_in,
    feed_out,
):
    row_count, length, model_width = tokens.shape
    flat_rows = row_count * length
    n = lax.axis_size("seq")
    batches = lax.axis_size("batch")
    down = adapter_down.shape[1]
    attended, mem_key, mem_value, *saved = self_forward(
        n,
        segment_ids,
        padding_mask,
        tokens.reshape(flat_rows, model_width),
        (self_query, self_key, self_value),
        (
            prefix_embed,
            prefix_first,
            first_bias.reshape(1, -1),
            prefix_second,
            second_bias.reshape(1, -1),
        ),
        memory.reshape(-1, model_width),
        (cross_key, cross_value),
    )
    layer_output, first_grad, out_grad, *mem_grads, weight_sums, vector_sums = middle(
        tokens.reshape(flat_rows, model_width),
        attended,
        cotangent.reshape(flat_rows, model_width),
        mem_key,
        mem_value,
        norm_gain,
        norm_shift,
        down_bias.reshape(1, -1),
        raise_bias.reshape(1, -1),
        (
            self_output,
            cross_query,
            cross_output,
            adapter_down,
            adapter_raise,
            feed_in,
            feed_out,
        ),
    )
    layer_output = layer_output.reshape(row_count, length, model_width)
    token_grad, memory_grad, prefix_grad, vector_sums, full_sums = self_backward(
        n,
        batches,
        first_grad,
        out_grad.reshape(n, -1, HD, length),
        weight_sums,
        mem_grads,
        (cross_key, cross_value),
        vector_sums,
        saved,
        (self_query, self_key, self_value),
    )
    *replicated, token_grad, memory_grad = finish(
        full_sums.reshape(-1, LANES),
        vector_sums,
        prefix_grad,
        prefix_embed,
        prefix_first,
        first_bias.reshape(1, -1),
        prefix_second,
        down,
        token_grad,
        memory_grad,
    )
    token_grad = token_grad.reshape(row_count, length, model_width)
    memory_grad = memory_grad.reshape(memory.shape)
    replicated = [
        value.reshape(-1) if value.shape[0] == 1 else value for value in replicated
    ]
    return (layer_output, token_grad, memory_grad, *replicated)


def solution(mesh):
    placed = (
        P("batch", "seq", None),
        P("batch", "seq", None),
        P("batch", "seq"),
        P("batch", "seq"),
        P("batch", "seq", None),
        P(),
        P(),
        P(),
        P(),
        P(),
        P(),
        P(),
        P(),
        P(),
        P(),
        P(),
        P(),
        P(),
        P(),
        P(),
        P(),
        P(),
        P(),
        P(),
        P(),
        P(),
    )
    return jax.shard_map(
        per_device,
        mesh=mesh,
        in_specs=placed,
        out_specs=(
            P("batch", "seq", None),
            P("batch", "seq", None),
            P("batch", "seq", None),
            P(),
            P(),
            P(),
            P(),
            P(),
            P(),
            P(),
            P(),
            P(),
            P(),
            P(),
        ),
        check_vma=False,
    )
```

```python
import functools

import jax
import jax.numpy as jnp
from jax import lax
from jax.experimental import pallas as pl
from jax.experimental.pallas import tpu as pltpu
from jax.sharding import PartitionSpec as P

H = 16
HD = 64
LANES = 128
PREFIX_ROWS = 32
VMEM_BYTES = 60 * 1024 * 1024
SUM_ROWS = 16
MESH = pl.DeviceIdType.MESH

masked_score = -1e30
norm_eps = 1e-05

def dot_nn(left, right):
    return lax.dot_general(
        left, right, (((1,), (0,)), ((), ())), preferred_element_type=jnp.float32
    )


def dot_nt(left, right):
    return lax.dot_general(
        left, right, (((1,), (1,)), ((), ())), preferred_element_type=jnp.float32
    )


def dot_tn(left, right):
    return lax.dot_general(
        left, right, (((0,), (0,)), ((), ())), preferred_element_type=jnp.float32
    )


def remote(source, target, send_sem, recv_sem, axis, peer):
    return pltpu.make_async_remote_copy(
        src_ref=source,
        dst_ref=target,
        send_sem=send_sem,
        recv_sem=recv_sem,
        device_id={axis: peer},
        device_id_type=MESH,
    )


def enter(sizes):
    barrier = pltpu.get_barrier_semaphore()
    for axis, size in sizes.items():
        for other in range(size):

            @pl.when(other != lax.axis_index(axis))
            def _():
                pl.semaphore_signal(barrier, inc=1, device_id={axis: other}, device_id_type=MESH)

    pl.semaphore_wait(barrier, sum(sizes.values()) - len(sizes))


def others(size, mine, body):
    for other in range(size):

        @pl.when(other != mine)
        def _():
            body(other)


def rows_of(index, size):
    return pl.ds(pl.multiple_of(index * size, size), size)


def span_of(start, size):
    return pl.ds(pl.multiple_of(start, LANES), size)


def own_columns(ref, first, me, width):
    if width % LANES == 0:
        return ref[:, pl.ds(pl.multiple_of(first + me * width, LANES), width)].astype(jnp.float32)
    share = LANES // width
    block = ref[:, pl.ds(pl.multiple_of(first + me // share * LANES, LANES), LANES)].astype(
        jnp.float32
    )
    picked = block[:, :width]
    for part in range(1, share):
        picked = jnp.where(me % share == part, block[:, part * width : (part + 1) * width], picked)
    return picked


def head_lanes(shape, head):
    lane = lax.broadcasted_iota(jnp.int32, shape, 1)
    return (lane >= head * HD) & (lane < (head + 1) * HD)


def self_forward_kernel(
    n,
    seg_ref,
    pad_ref,
    tok_ref,
    wq_in,
    wk_in,
    wv_in,
    emb_ref,
    first_in,
    fbias_ref,
    second_in,
    sbias_ref,
    mem_ref,
    wck_in,
    wcv_in,
    att_ref,
    mkey_out,
    mvalue_out,
    qx_out,
    kx_out,
    raw_out,
    pk_out,
    pv_out,
    pkt_out,
    ot_out,
    lse_out,
    send,
    recv,
    meta_send,
    meta,
    kx,
    qx,
    vt,
    hidden,
    pk,
    pv,
    pkt,
    pvt,
    stat,
    acc,
    o_send,
    o_recv,
    mem_all,
    wck,
    wcv,
    mkey_ref,
    mvalue_ref,
    wq_ref,
    wk_ref,
    wv_ref,
    first_ref,
    second_ref,
    send_sem,
    recv_sem,
    meta_send_sem,
    meta_recv_sem,
    o_send_sem,
    o_recv_sem,
    mem_send_sem,
    mem_recv_sem,
    out_sem,
    weight_sem,
    in_sem,
):
    low = jnp.bfloat16
    f32 = jnp.float32
    me = lax.axis_index("seq")
    length, width = tok_ref.shape
    group = width // n
    heads = group // HD
    plane = 2 * length
    planes = n // 2
    block = 2 * LANES
    per_block = block // group
    blocks = width // block
    step_rows = 256
    steps = plane // step_rows
    my_plane = me // 2
    my_side = lax.rem(me, 2)

    def meta_copy(peer, slot):
        return remote(
            meta_send, meta.at[slot], meta_send_sem.at[peer], meta_recv_sem.at[slot], "seq", peer
        )

    def qkv_copy(head, peer, slot):
        return remote(
            send.at[peer, head],
            recv.at[head, slot],
            send_sem.at[head, peer],
            recv_sem.at[head, slot],
            "seq",
            peer,
        )

    def out_copy(head, peer, slot):
        return remote(
            o_send.at[head, peer],
            o_recv.at[slot, head],
            o_send_sem.at[head, peer],
            o_recv_sem.at[head, slot],
            "seq",
            peer,
        )

    def mem_along(which, toward):
        part = mem_all.at[which, my_side]
        return remote(
            part,
            part,
            mem_send_sem.at[(toward + 1) // 2, which],
            mem_recv_sem.at[which],
            "seq",
            me + 2 * toward,
        )

    def mem_across(side):
        part = mem_all.at[:, side]
        return remote(
            part,
            part,
            mem_send_sem.at[0, planes],
            mem_recv_sem.at[planes],
            "seq",
            me + 1 - 2 * my_side,
        )

    def mem_hops(hop, body):
        for toward in (1, -1):
            which = my_plane - toward * hop
            ahead = my_plane + toward

            @pl.when((which >= 0) & (which < planes) & (ahead >= 0) & (ahead < planes))
            def _():
                body(mem_along(which, toward))

    def mem_arrivals(hop):
        for toward in (1, -1):
            which = my_plane - toward * hop

            @pl.when((which >= 0) & (which < planes))
            def _():
                mem_along(which, -toward).wait_recv()

    def block_at(step):
        if blocks >= planes:
            share = blocks // planes
            return lax.rem(my_plane + 1 + step // share, planes) * share + step % share
        return lax.rem(me // per_block + 1 + step, blocks)

    def weight_load(step, which):
        columns = rows_of(block_at(step), block)
        source = (wq_in, wk_in, wv_in)[which]
        target = (wq_ref, wk_ref, wv_ref)[which]
        return pltpu.make_async_copy(
            source.at[:, columns], target.at[:, columns], weight_sem.at[step, which]
        )

    for step in range(blocks):
        for which in range(3):
            weight_load(step, which).start()
    loads = [
        pltpu.make_async_copy(source, target, in_sem.at[index])
        for index, (source, target) in enumerate(
            ((first_in, first_ref), (second_in, second_ref), (wck_in, wck), (wcv_in, wcv))
        )
    ]
    for load in loads:
        load.start()
    segments = seg_ref[...]
    tags = jnp.where(pad_ref[...] == 1, segments, -1)
    row = lax.broadcasted_iota(jnp.int32, meta_send.shape, 0)
    meta_send[...] = jnp.where(row == 0, segments, tags)
    mem_all[my_plane, my_side] = mem_ref[...]
    enter({"seq": n})
    others(n, me, lambda peer: meta_copy(peer, me).start())
    meta[me] = meta_send[...]

    for step in range(blocks):
        at = block_at(step)
        columns = rows_of(at, block)
        for which, weight in enumerate((wq_ref, wk_ref, wv_ref)):
            weight_load(step, which).wait()
            piece = dot_nn(tok_ref[...], weight[:, columns]).T.astype(low)
            for part in range(per_block):
                for head in range(heads):
                    first = part * group + head * HD
                    send[at * per_block + part, head, which] = piece[first : first + HD]
        for part in range(per_block):
            peer = at * per_block + part

            @pl.when(peer != me)
            def _():
                qkv_copy(0, peer, me).start()

            @pl.when(peer == me)
            def _():
                for head in range(heads):
                    recv[head, me] = send[peer, head]

    mem_hops(0, lambda copy: copy.start())
    loads[0].wait()
    loads[1].wait()
    hidden[...] = jnp.zeros_like(hidden)
    hidden[: emb_ref.shape[0], :] = jnp.tanh(dot_nn(emb_ref[...], first_ref[...]) + fbias_ref[...])
    hidden_low = hidden[...].astype(low)
    prefix_key = dot_nn(hidden_low, own_columns(second_ref, 0, me, group).astype(low)) + own_columns(
        sbias_ref, 0, me, group
    )
    prefix_value = dot_nn(
        hidden_low, own_columns(second_ref, width, me, group).astype(low)
    ) + own_columns(sbias_ref, width, me, group)
    prefix_row = lax.broadcasted_iota(jnp.int32, (PREFIX_ROWS, HD), 0)
    prefix_open = jnp.where(prefix_row < emb_ref.shape[0], 0.0, masked_score)
    for head in range(heads):
        here = slice(head * HD, (head + 1) * HD)
        pk[head] = jnp.concatenate([prefix_key[:, here], prefix_open], axis=1).astype(low)
        pv[head] = prefix_value[:, here].astype(low)
    pkt[...] = prefix_key.T.astype(low).reshape(heads, HD, PREFIX_ROWS)
    pvt[:, :HD, :] = prefix_value.T.astype(low).reshape(heads, HD, PREFIX_ROWS)
    pvt[:, HD:, :] = jnp.ones((heads, SUM_ROWS, PREFIX_ROWS), low)
    vt[:, HD:, :] = jnp.ones((heads, SUM_ROWS, n * length), low)

    def arrive(head, chunk):
        @pl.when(chunk != me)
        def _():
            @pl.when(head == 0)
            def _():
                meta_copy(chunk, chunk).wait_recv()

            qkv_copy(head, chunk, chunk).wait_recv()

        here = rows_of(chunk, length)
        state = lax.broadcasted_iota(jnp.int32, (HD, length), 0)
        qx[head, :HD, here] = (recv[head, chunk, 0].astype(f32) * 0.125).astype(low)
        qx[head, HD:, here] = jnp.where(state == meta[chunk, 0:1, :], 1.0, 0.0).astype(low)
        is_open = jnp.where(state == meta[chunk, 1:2, :], 0.0, masked_score)
        kx[head, here, :] = jnp.concatenate(
            [recv[head, chunk, 1].astype(f32), is_open], axis=0
        ).T.astype(low)
        vt[head, :HD, here] = recv[head, chunk, 2]

    def open_plane(head, which):
        scores = dot_nn(pk[head], qx[head, :, rows_of(which, plane)])
        top = jnp.max(scores, axis=0, keepdims=True)
        raised = jnp.exp(scores - top)
        stat[which, head, 0:1, :] = top
        acc[which, head] = dot_nn(pvt[head], raised.astype(low))

    def pair_part(head, upper, lower, first, keys, diagonal):
        here = slice(first, first + step_rows)
        queries = qx[head, :, span_of(upper * plane + first, step_rows)]
        key_rows = span_of(lower * plane, keys)
        scores = dot_nn(kx[head, key_rows, :], queries)
        if diagonal:
            key_at = lax.broadcasted_iota(jnp.int32, scores.shape, 0)
            query_at = lax.broadcasted_iota(jnp.int32, scores.shape, 1) + first
            scores = jnp.where(key_at <= query_at, scores, masked_score)
        old_top = stat[upper, head, 0:1, here]
        top = jnp.maximum(old_top, jnp.max(scores, axis=0, keepdims=True))
        raised = jnp.exp(scores - top).astype(low)
        stat[upper, head, 0:1, here] = top
        acc[upper, head, :, here] = acc[upper, head, :, here] * jnp.exp(old_top - top) + dot_nn(
            vt[head, :, key_rows], raised
        )

    def pair(head, upper, lower):
        for part in range(steps):
            pair_part(head, upper, lower, part * step_rows, plane, False)

    def pair_diagonal(head, which):
        for part in range(steps):
            pair_part(head, which, which, part * step_rows, (part + 1) * step_rows, True)

    def close_plane(head, which):
        total = acc[which, head, HD : HD + 1, :]
        value = acc[which, head, :HD, :] / total
        acc[which, head, :HD, :] = value
        stat[which, head, 0:1, :] = stat[which, head, 0:1, :] + jnp.log(total)
        for part in range(2):
            chunk = 2 * which + part
            o_send[head, chunk] = value[:, part * length : (part + 1) * length].astype(low)

            @pl.when(chunk != me)
            def _():
                out_copy(head, chunk, me).start()

            @pl.when(chunk == me)
            def _():
                o_recv[me, head] = o_send[head, chunk]

    def project_memory():
        mem_across(1 - my_side).wait_recv()
        for load in loads[2:]:
            load.wait()
        whole = mem_all[...].reshape(mkey_ref.shape)

        def one(index, carry):
            here = rows_of(index, block)
            mkey_ref[:, here] = dot_nn(whole, wck[:, here]).astype(low)
            mvalue_ref[:, here] = dot_nn(whole, wcv[:, here]).astype(low)
            return carry

        lax.fori_loop(0, blocks, one, 0)

    def stage(index, carry):
        head = index // planes
        step = lax.rem(index, planes)

        @pl.when(head + 1 < heads)
        def _():
            there = lax.rem(my_plane + 1 + step, planes)
            for part in range(2):
                peer = 2 * there + part

                @pl.when(peer != me)
                def _():
                    qkv_copy(head, peer, me).wait_send()
                    qkv_copy(head + 1, peer, me).start()

        here = lax.rem(my_plane + step, planes)
        arrive(head, 2 * here)
        arrive(head, 2 * here + 1)
        open_plane(head, here)
        pair_diagonal(head, here)

        def earlier(back, inner):
            there = lax.rem(my_plane + back, planes)
            pair(head, jnp.maximum(here, there), jnp.minimum(here, there))

            @pl.when((step == planes - 1) & (there > here))
            def _():
                close_plane(head, there)

            return inner

        lax.fori_loop(0, step, earlier, 0)
        for hop in range(1, planes - 1):

            @pl.when(index == hop)
            def _():
                mem_arrivals(hop)
                mem_hops(hop, lambda copy: copy.start())

        @pl.when(index == planes - 1)
        def _():
            mem_arrivals(planes - 1)
            mem_across(my_side).start()

        @pl.when((my_plane + step >= planes) | (my_plane == 0))
        def _():
            close_plane(head, here)

        return carry

    lax.fori_loop(0, heads * planes, stage, 0)

    saves = []

    def save(source, target):
        copy = pltpu.make_async_copy(source, target, out_sem.at[len(saves)])
        copy.start()
        saves.append(copy)

    save(qx, qx_out)
    save(kx, kx_out)
    save(recv, raw_out)
    save(pk, pk_out)
    save(pv, pv_out)
    save(pkt, pkt_out)
    save(acc, ot_out)
    save(stat, lse_out)
    project_memory()
    save(mkey_ref, mkey_out)
    save(mvalue_ref, mvalue_out)
    for other in range(n):

        @pl.when(other != me)
        def _():
            for head in range(heads):
                out_copy(head, other, other).wait_recv()

        att_ref[:, other * group : (other + 1) * group] = (
            o_recv[other].reshape(group, length).astype(f32).T.astype(low)
        )

    def drain(peer):
        meta_copy(peer, me).wait_send()
        qkv_copy(heads - 1, peer, me).wait_send()
        for head in range(heads):
            out_copy(head, peer, me).wait_send()

    others(n, me, drain)
    for hop in range(planes - 1):
        mem_hops(hop, lambda copy: copy.wait_send())
    mem_across(my_side).wait_send()
    for copy in saves:
        copy.wait()


def self_forward(n, segments, padding, tokens, weights, prefix, memory, mem_weights):
    length, width = tokens.shape
    group = width // n
    heads = group // HD
    whole = n * length
    planes = n // 2
    low = jnp.bfloat16
    f32 = jnp.float32
    vmem = pl.BlockSpec(memory_space=pltpu.VMEM)
    anywhere = pl.BlockSpec(memory_space=pl.ANY)
    dma = pltpu.SemaphoreType.DMA
    shapes = (
        ((heads, 2 * HD, whole), low),
        ((heads, whole, 2 * HD), low),
        ((heads, n, 3, HD, length), low),
        ((heads, PREFIX_ROWS, 2 * HD), low),
        ((heads, PREFIX_ROWS, HD), low),
        ((heads, HD, PREFIX_ROWS), low),
        ((planes, heads, HD + SUM_ROWS, 2 * length), f32),
        ((planes, heads, 8, 2 * length), f32),
    )
    square = pltpu.VMEM((width, width), low)
    qx, kx, raw, pk, pv, pkt, acc, stat = (pltpu.VMEM(*shape) for shape in shapes)
    return pl.pallas_call(
        functools.partial(self_forward_kernel, n),
        out_shape=(
            jax.ShapeDtypeStruct((length, width), low),
            jax.ShapeDtypeStruct((n * memory.shape[0], width), low),
            jax.ShapeDtypeStruct((n * memory.shape[0], width), low),
        )
        + tuple(jax.ShapeDtypeStruct(*shape) for shape in shapes),
        in_specs=[vmem] * 3
        + [anywhere] * 3
        + [vmem, anywhere, vmem, anywhere, vmem, vmem]
        + [anywhere] * 2,
        out_specs=(vmem,) + (anywhere,) * 10,
        scratch_shapes=[
            pltpu.VMEM((n, heads, 3, HD, length), low),
            raw,
            pltpu.VMEM((8, length), jnp.int32),
            pltpu.VMEM((n, 8, length), jnp.int32),
            kx,
            qx,
            pltpu.VMEM((heads, HD + SUM_ROWS, whole), low),
            pltpu.VMEM((PREFIX_ROWS, weights[0].shape[0] // 2), f32),
            pk,
            pv,
            pkt,
            pltpu.VMEM((heads, HD + SUM_ROWS, PREFIX_ROWS), low),
            stat,
            acc,
            pltpu.VMEM((heads, n, HD, length), low),
            pltpu.VMEM((n, heads, HD, length), low),
            pltpu.VMEM((planes, 2) + memory.shape, low),
            square,
            square,
            pltpu.VMEM((n * memory.shape[0], width), low),
            pltpu.VMEM((n * memory.shape[0], width), low),
            square,
            square,
            square,
            pltpu.VMEM(prefix[1].shape, low),
            pltpu.VMEM(prefix[3].shape, low),
            dma((heads, n)),
            dma((heads, n)),
            dma((n,)),
            dma((n,)),
            dma((heads, n)),
            dma((heads, n)),
            dma((2, planes + 1)),
            dma((planes + 1,)),
            dma((10,)),
            dma((width // (2 * LANES), 3)),
            dma((4,)),
        ],
        compiler_params=pltpu.CompilerParams(
            collective_id=0, has_side_effects=True, vmem_limit_bytes=VMEM_BYTES
        ),
        name="self_forward",
    )(segments, padding, tokens, *weights, *prefix, memory, *mem_weights)


def self_backward_kernel(
    n,
    batches,
    base_in,
    do_in,
    sums_in,
    mkey_in,
    mvalue_in,
    wck_in,
    wcv_in,
    vecs_in,
    qx_in,
    kx_in,
    raw_in,
    pk_in,
    pv_in,
    pkt_in,
    ot_in,
    lse_in,
    wq_in,
    wk_in,
    wv_in,
    tg_ref,
    mgrad_ref,
    pkv_ref,
    vecs_ref,
    full_out,
    do_recv,
    qx,
    kx,
    raw,
    kt,
    values,
    dot,
    qdo,
    pk,
    pv,
    pkt,
    ot,
    stat,
    weights,
    dqt,
    dkv,
    g_send,
    g_recv,
    pre_ref,
    pre_all,
    pre_sum,
    pre_recv,
    sums_mine,
    sums_core,
    sums_x,
    sums_side,
    sums_z,
    full,
    mkey,
    mvalue,
    wck,
    wcv,
    mem_part,
    mem_side,
    mem_up,
    mem_down,
    vec_all,
    vec_sum,
    vec_y,
    vec_both,
    vec_z,
    product,
    base_ref,
    do_send_sem,
    do_recv_sem,
    g_send_sem,
    g_recv_sem,
    in_sem,
    send_sem,
    recv_sem,
):
    low = jnp.bfloat16
    f32 = jnp.float32
    me = lax.axis_index("seq")
    length, width = tg_ref.shape
    group = width // n
    heads = group // HD
    plane = 2 * length
    planes = n // 2
    step_rows = 256
    my_batch = lax.axis_index("batch")
    my_core = lax.rem(my_batch, 2)
    my_high = my_batch // 2
    highs = batches // 2
    my_plane = me // 2
    my_side = lax.rem(me, 2)
    beside = me + 1 - 2 * my_side
    used = [0]

    def numbers(count):
        used[0] += count
        return used[0] - count

    core_slot = numbers(2)
    x_slot = numbers(2 * highs)
    y_slot = numbers(3)
    z_slot = numbers(2 * planes)
    up_slot = numbers(planes)
    down_slot = numbers(planes)
    va_slot = numbers(batches)
    vb_slot = numbers(1)
    vc_slot = numbers(planes)
    pa_slot = numbers(batches)
    pb_slot = numbers(n)

    def send(source, target, first, peer_index, slot_index, axis, peer):
        return remote(
            source,
            target,
            send_sem.at[first + peer_index],
            recv_sem.at[first + slot_index],
            axis,
            peer,
        )

    half_rows = 2 * planes * highs * sums_z.shape[1]
    x_rows = half_rows // highs
    y_rows = x_rows // 2
    z_rows = y_rows // planes
    x_row = pl.multiple_of(my_high * x_rows, x_rows)
    y_row = pl.multiple_of(x_row + my_side * y_rows, y_rows)

    def part(row, count):
        return sums_mine.at[pl.ds(pl.multiple_of(row, count), count)]

    def reduce_core():
        return send(
            sums_in.at[1 - my_core], sums_core, core_slot, 0, 0, "batch", my_batch + 1 - 2 * my_core
        )

    def reduce_x(peer, slot):
        return send(
            part(peer * x_rows, x_rows),
            sums_x.at[slot],
            x_slot,
            peer,
            slot,
            "batch",
            2 * peer + my_core,
        )

    def reduce_y():
        return send(
            part(x_row + (1 - my_side) * y_rows, y_rows), sums_side, y_slot, 0, 0, "seq", beside
        )

    def reduce_z(peer, slot):
        return send(
            part(y_row + peer * z_rows, z_rows),
            sums_z.at[slot],
            z_slot,
            peer,
            slot,
            "seq",
            2 * peer + my_side,
        )

    def gather_z(peer, slot):
        piece = full.at[my_core, my_high, my_side, slot]
        return send(piece, piece, z_slot + planes, peer, slot, "seq", 2 * peer + my_side)

    def gather_y(side):
        piece = full.at[my_core, my_high, side]
        return send(piece, piece, y_slot + 1, 0, 0, "seq", beside)

    def gather_x(peer, slot):
        piece = full.at[my_core, slot]
        return send(piece, piece, x_slot + highs, peer, slot, "batch", 2 * peer + my_core)

    def gather_core(core):
        piece = full.at[core]
        return send(piece, piece, core_slot + 1, 0, 0, "batch", my_batch + 1 - 2 * my_core)

    def mem_across():
        return send(
            mem_part.at[:, 1 - my_side], mem_side, y_slot + 2, 0, 0, "seq", beside
        )

    def mem_hop(target, toward, peer=None):
        buffer, slot = (mem_up, up_slot) if toward > 0 else (mem_down, down_slot)
        return send(
            mem_part.at[target, my_side],
            buffer.at[target],
            slot,
            target,
            target,
            "seq",
            me + 2 * toward if peer is None else peer,
        )

    def mem_from(target, toward):
        return mem_hop(target, toward, me - 2 * toward)

    def mem_pass(toward):
        buffer = mem_up if toward > 0 else mem_down
        first = 0 if toward > 0 else planes - 1
        for target in range(planes):

            @pl.when((target - my_plane) * toward > 0)
            def _():
                @pl.when(my_plane != first)
                def _():
                    mem_from(target, toward).wait_recv()
                    mem_part[target, my_side] = (
                        mem_part[target, my_side].astype(f32) + buffer[target].astype(f32)
                    ).astype(low)

                mem_hop(target, toward).start()

    def mem_stage(at):
        pl.when(my_plane == at)(lambda: mem_pass(1))
        pl.when(my_plane == planes - 1 - at)(lambda: mem_pass(-1))

    def mem_end():
        value = mem_part[my_plane, my_side].astype(f32)
        mgrad_ref[...] = value.astype(low)

        @pl.when(my_plane > 0)
        def _():
            mem_from(my_plane, 1).wait_recv()
            mgrad_ref[...] = (mgrad_ref[...].astype(f32) + mem_up[my_plane].astype(f32)).astype(low)

        @pl.when(my_plane < planes - 1)
        def _():
            mem_from(my_plane, -1).wait_recv()
            mgrad_ref[...] = (
                mgrad_ref[...].astype(f32) + mem_down[my_plane].astype(f32)
            ).astype(low)

    def mem_drain():
        for target in range(planes):

            @pl.when(target > my_plane)
            def _():
                mem_hop(target, 1).wait_send()

            @pl.when(target < my_plane)
            def _():
                mem_hop(target, -1).wait_send()

    def vec_a(peer, slot):
        return send(vecs_in, vec_all.at[slot], va_slot, peer, slot, "batch", peer)

    def vec_b(side):
        return send(vec_sum, vec_y.at[side], vb_slot, 0, 0, "seq", beside)

    def vec_c(peer, slot):
        return send(vec_both, vec_z.at[slot], vc_slot, peer, slot, "seq", 2 * peer + my_side)

    def pre_a(peer, slot):
        return send(pre_ref, pre_all.at[slot], pa_slot, peer, slot, "batch", peer)

    def pre_b(peer, slot):
        return send(pre_sum, pre_recv.at[slot], pb_slot, peer, slot, "seq", peer)

    def do_copy(head, peer, slot):
        return remote(
            do_in.at[peer, head],
            do_recv.at[head, slot],
            do_send_sem.at[head, peer],
            do_recv_sem.at[head, slot],
            "seq",
            peer,
        )

    def q_copy(head, peer, slot):
        return remote(
            g_send.at[peer, head, 0],
            g_recv.at[0, slot, head],
            g_send_sem.at[0, head, peer],
            g_recv_sem.at[0, head, slot],
            "seq",
            peer,
        )

    def kv_copy(head, peer, slot):
        return remote(
            g_send.at[peer, head, pl.ds(1, 2)],
            g_recv.at[pl.ds(1, 2), slot, head],
            g_send_sem.at[1, head, peer],
            g_recv_sem.at[1, head, slot],
            "seq",
            peer,
        )

    def added(ref, size):
        value = ref[0].astype(f32)
        for other in range(1, size):
            value = value + ref[other].astype(f32)
        return value

    loads = [
        pltpu.make_async_copy(source, target, in_sem.at[index])
        for index, (source, target) in enumerate(
            (
                (raw_in, raw),
                (kx_in, kx),
                (pk_in, pk),
                (pv_in, pv),
                (pkt_in, pkt),
                (qx_in, qx),
                (ot_in, ot),
                (lse_in, stat),
                (sums_in.at[my_core], sums_mine),
                (vecs_in, vec_all.at[my_batch]),
                (mkey_in, mkey),
                (mvalue_in, mvalue),
                (wck_in, wck),
                (wcv_in, wcv),
                (base_in, base_ref),
                (wq_in, weights.at[0]),
                (wk_in, weights.at[1]),
                (wv_in, weights.at[2]),
            )
        )
    ]
    own_do = pltpu.make_async_copy(do_in.at[me], do_recv.at[:, me], in_sem.at[len(loads)])
    own_do.start()
    for load in loads:
        load.start()
    enter({"seq": n, "batch": batches})
    others(n, me, lambda peer: do_copy(0, peer, me).start())
    reduce_core().start()
    others(batches, my_batch, lambda peer: vec_a(peer, my_batch).start())
    dkv[...] = jnp.zeros_like(dkv)
    product[...] = jnp.zeros_like(product)
    pre_ref[...] = jnp.zeros_like(pre_ref)
    for load in loads[:14]:
        load.wait()
    own_do.wait()

    def turn(index, carry):
        head = index // n
        chunk = lax.rem(index, n)
        here = rows_of(chunk, length)
        kt[head, :, here] = raw[head, chunk, 1]
        values[head, here, :] = raw[head, chunk, 2].astype(f32).T.astype(low)
        return carry

    lax.fori_loop(0, heads * n, turn, 0)

    def memory_back(index, carry):
        here = rows_of(index, step_rows)
        value = dot_nt(mkey[...], wck[here, :]) + dot_nt(mvalue[...], wcv[here, :])
        mem_part[:, :, :, here] = value.astype(low).reshape(mem_part.shape[:3] + (step_rows,))
        return carry

    lax.fori_loop(0, width // step_rows, memory_back, 0)
    mem_across().start()

    def next_head(head):
        def move(peer):
            do_copy(head, peer, me).wait_send()
            do_copy(head + 1, peer, me).start()

        others(n, me, move)

    def arrive(head, which):
        for part in range(2):
            chunk = 2 * which + part

            @pl.when(chunk != me)
            def _():
                do_copy(head, chunk, chunk).wait_recv()

            grads = do_recv[head, chunk]
            dot[head, :, rows_of(chunk, length)] = grads
            grads = grads.astype(f32)
            query = raw[head, chunk, 0].astype(f32) * 0.125
            qdo[head, rows_of(chunk, length), :] = (
                jnp.concatenate([query, grads], axis=0).T.astype(low)
            )
            here = slice(part * length, (part + 1) * length)
            stat[which, head, 1:2, here] = jnp.sum(
                grads * ot[which, head, :HD, here], axis=0, keepdims=True
            )
        here = rows_of(which, plane)
        weight = jnp.exp(dot_nn(pk[head], qx[head, :, here]) - stat[which, head, 0:1, :])
        slope = weight * (dot_nn(pv[head], dot[head, :, here]) - stat[which, head, 1:2, :])
        both = jnp.concatenate([slope, weight], axis=0).astype(low)
        sums = dot_nn(both, qdo[head, here, :])
        pre_ref[head] += jnp.where(
            head_lanes((PREFIX_ROWS, 2 * HD), 0), sums[:PREFIX_ROWS], sums[PREFIX_ROWS:]
        )
        slope = slope.astype(low)
        dqt[which, head] = dot_nn(pkt[head], slope)

    def plus(first, second):
        return (first.astype(f32) + second.astype(f32)).astype(low)

    def sum_one():
        reduce_core().wait_recv()
        sums_mine[...] = plus(sums_mine[...], sums_core[...])
        others(highs, my_high, lambda peer: reduce_x(peer, my_high).start())

    def sum_two():
        here = pl.ds(x_row, x_rows)
        others(highs, my_high, lambda peer: reduce_x(peer, peer).wait_recv())
        sums_x[my_high] = sums_mine[here]
        sums_mine[here] = added(sums_x, highs).astype(low)
        reduce_y().start()

    def sum_three():
        here = pl.ds(y_row, y_rows)
        reduce_y().wait_recv()
        sums_mine[here] = plus(sums_mine[here], sums_side[...])
        others(planes, my_plane, lambda peer: reduce_z(peer, my_plane).start())

    def sum_four():
        here = pl.ds(pl.multiple_of(y_row + my_plane * z_rows, z_rows), z_rows)
        others(planes, my_plane, lambda peer: reduce_z(peer, peer).wait_recv())
        sums_z[my_plane] = sums_mine[here]
        full[my_core, my_high, my_side, my_plane] = added(sums_z, planes).astype(low)
        others(planes, my_plane, lambda peer: gather_z(peer, my_plane).start())

    def sum_five():
        others(planes, my_plane, lambda peer: gather_z(peer, peer).wait_recv())
        gather_y(my_side).start()

    def sum_six():
        gather_y(1 - my_side).wait_recv()
        others(highs, my_high, lambda peer: gather_x(peer, my_high).start())

    def sum_seven():
        others(highs, my_high, lambda peer: gather_x(peer, peer).wait_recv())
        gather_core(my_core).start()

    def sum_end():
        gather_core(1 - my_core).wait_recv()
        save_full.start()

    def vec_one():
        others(batches, my_batch, lambda peer: vec_a(peer, peer).wait_recv())
        vec_sum[...] = added(vec_all, batches)
        vec_b(my_side).start()
        vec_y[my_side] = vec_sum[...]

    def vec_two():
        vec_b(1 - my_side).wait_recv()
        value = (vec_y[0] + vec_y[1]).astype(f32)
        vec_both[...] = jnp.concatenate(
            [value[:, : width // 2], value[:, width // 2 :]], axis=0
        ).astype(low)
        others(planes, my_plane, lambda peer: vec_c(peer, my_plane).start())
        vec_z[my_plane] = vec_both[...]

    def vec_end():
        others(planes, my_plane, lambda peer: vec_c(peer, peer).wait_recv())
        value = added(vec_z, planes)
        vecs_ref[:, : width // 2] = value[:8]
        vecs_ref[:, width // 2 :] = value[8:]

    def mem_one():
        mem_across().wait_recv()
        mem_part[:, my_side] = plus(mem_part[:, my_side], mem_side[...])

    def stage_pa():
        others(batches, my_batch, lambda peer: pre_a(peer, my_batch).start())
        pre_all[my_batch] = pre_ref[...]

    def stage_pb():
        others(batches, my_batch, lambda peer: pre_a(peer, peer).wait_recv())
        pre_sum[...] = added(pre_all, batches).astype(low)
        others(n, me, lambda peer: pre_b(peer, me).start())
        pre_recv[me] = pre_sum[...]

    save_full = pltpu.make_async_copy(full, full_out, in_sem.at[0])

    def pair_part(head, upper, lower, first, count, diagonal):
        keys = span_of(lower * plane + first, count)
        here = span_of(upper * plane + first, plane - first)
        at = slice(first, plane)
        scores = dot_nn(kx[head, keys, :], qx[head, :, here])
        slope = dot_nn(values[head, keys, :], dot[head, :, here]) - stat[upper, head, 1:2, at]
        weight = jnp.exp(scores - stat[upper, head, 0:1, at])
        if diagonal:
            key_at = lax.broadcasted_iota(jnp.int32, scores.shape, 0)
            query_at = lax.broadcasted_iota(jnp.int32, scores.shape, 1)
            weight = jnp.where(key_at <= query_at, weight, 0.0)
        both = jnp.concatenate([(weight * slope).astype(low), weight.astype(low)], axis=0)
        sums = dot_nn(both, qdo[head, here, :])
        dkv[head, keys, :] += jnp.where(
            head_lanes((count, 2 * HD), 0), sums[:count], sums[count:]
        )
        dqt[upper, head, :, at] += dot_nn(kt[head, :, keys], both[:count])

    def pair(head, upper, lower, diagonal):
        if diagonal:
            pair_part(head, upper, lower, 0, length, True)
            pair_part(head, upper, lower, length, length, True)
        else:
            pair_part(head, upper, lower, 0, plane, False)

    def hand_queries(head, which):
        for part in range(2):
            chunk = 2 * which + part
            g_send[chunk, head, 0] = (
                dqt[which, head, :, part * length : (part + 1) * length] * 0.125
            ).astype(low)

            @pl.when(chunk != me)
            def _():
                q_copy(head, chunk, me).start()

            @pl.when(chunk == me)
            def _():
                g_recv[0, me, head] = g_send[chunk, head, 0]

    def hand_keys(head, which):
        for part in range(2):
            chunk = 2 * which + part
            turned = dkv[head, rows_of(chunk, length), :].T.astype(low)
            g_send[chunk, head, 1] = turned[:HD]
            g_send[chunk, head, 2] = turned[HD:]

            @pl.when(chunk != me)
            def _():
                kv_copy(head, chunk, me).start()

            @pl.when(chunk == me)
            def _():
                g_recv[pl.ds(1, 2), me, head] = g_send[chunk, head, pl.ds(1, 2)]

    rising = my_plane >= planes // 2
    total = heads * planes * (planes + 1) // 2
    hooks = [
        (2, sum_one),
        (3, mem_one),
        (4, lambda: mem_stage(0)),
        (5, vec_one),
        (5, sum_two),
        (7, sum_three),
        (8, vec_two),
        (10, sum_four),
        (12, sum_five),
        (14, sum_six),
        (16, vec_end),
        (17, sum_seven),
    ] + [(4 + 3 * at, functools.partial(mem_stage, at)) for at in range(1, planes - 1)]
    hooks += [
        (1 + head * total // heads, functools.partial(next_head, head)) for head in range(heads - 1)
    ]
    final = total - planes * (planes + 1) // 2
    hooks += [(final + planes + 1, stage_pa), (final + 2 * planes - 1, stage_pb)]

    def hook(pairs):
        for number, body in sorted(hooks, key=lambda item: item[0]):
            pl.when(pairs == number)(body)


    def stage(index, carry):
        head = index // planes
        step = lax.rem(index, planes)
        here = jnp.where(rising, step, planes - 1 - step)

        @pl.when((step == 0) | ((step == 1) & jnp.logical_not(rising)))
        def _():
            @pl.when(rising | (step == 0))
            def _():
                arrive(head, here)

            @pl.when(jnp.logical_not(rising) & (step == 1))
            def _():
                def rest(which, inner):
                    arrive(head, planes - 2 - which)
                    return inner

                lax.fori_loop(0, planes - 1, rest, 0)

        begun = head * (planes * (planes + 1) // 2) + step * planes - step * (step - 1) // 2
        hook(begun)
        pair(head, here, here, True)

        @pl.when(rising)
        def _():
            hand_queries(head, here)

        @pl.when(jnp.logical_not(rising))
        def _():
            hand_keys(head, here)

        def far(at, inner):
            there = jnp.where(rising, here + 1 + at, here - 1 - at)

            @pl.when(rising & (step == 0))
            def _():
                arrive(head, there)

            hook(begun + 1 + at)
            pair(head, jnp.maximum(here, there), jnp.minimum(here, there), False)
            return inner

        lax.fori_loop(0, planes - 1 - step, far, 0)

        @pl.when(rising)
        def _():
            hand_keys(head, here)

        @pl.when(jnp.logical_not(rising))
        def _():
            hand_queries(head, here)

        return carry

    lax.fori_loop(0, heads * planes, stage, 0)
    mem_end()
    for load in loads[14:]:
        load.wait()

    def gathered(peer):
        for head in range(heads):
            q_copy(head, peer, peer).wait_recv()
            kv_copy(head, peer, peer).wait_recv()

    half = width // 2

    def gather_plane(step, carry):
        which = lax.rem(my_plane + step, planes)
        for part in range(2):
            peer = 2 * which + part

            @pl.when(peer != me)
            def _():
                gathered(peer)

        columns = rows_of(which, 2 * group)
        for part in range(2):
            here = slice(part * half, (part + 1) * half)
            value = product[here, :]
            for kind in range(3):
                grads = g_recv[kind, pl.ds(2 * which, 2)].reshape(2 * group, length)
                value = value + dot_nn(weights[kind, here, columns], grads)
            product[here, :] = value
        return carry

    lax.fori_loop(0, planes, gather_plane, 0)
    sum_end()
    tile = 256
    for index in range(width // tile):
        here = slice(index * tile, (index + 1) * tile)
        tg_ref[:, here] = (base_ref[:, here] + product[here, :].T).astype(low)
    for other in range(n):

        @pl.when(other != me)
        def _():
            pre_b(other, other).wait_recv()

        value = pre_recv[other].astype(f32)
        for which in range(2):
            pkv_ref[:, which * width + other * group : which * width + (other + 1) * group] = (
                jnp.concatenate(
                    [value[head, :, which * HD : (which + 1) * HD] for head in range(heads)], axis=1
                )
            )

    def drain(peer):
        do_copy(heads - 1, peer, me).wait_send()
        pre_b(peer, me).wait_send()
        for head in range(heads):
            q_copy(head, peer, me).wait_send()
            kv_copy(head, peer, me).wait_send()

    others(n, me, drain)
    others(batches, my_batch, lambda peer: pre_a(peer, my_batch).wait_send())
    others(batches, my_batch, lambda peer: vec_a(peer, my_batch).wait_send())
    reduce_core().wait_send()
    others(highs, my_high, lambda peer: reduce_x(peer, my_high).wait_send())
    reduce_y().wait_send()
    others(planes, my_plane, lambda peer: reduce_z(peer, my_plane).wait_send())
    others(planes, my_plane, lambda peer: gather_z(peer, my_plane).wait_send())
    gather_y(my_side).wait_send()
    others(highs, my_high, lambda peer: gather_x(peer, my_high).wait_send())
    gather_core(my_core).wait_send()
    mem_across().wait_send()
    mem_drain()
    others(planes, my_plane, lambda peer: vec_c(peer, my_plane).wait_send())
    vec_b(my_side).wait_send()
    save_full.wait()


def self_backward(
    n, batches, first_grad, out_grad, sums, mem_grads, mem_weights, vecs, saved, weights
):
    length, width = first_grad.shape
    group = width // n
    heads = group // HD
    whole = n * length
    planes = n // 2
    low = jnp.bfloat16
    f32 = jnp.float32
    vmem = pl.BlockSpec(memory_space=pltpu.VMEM)
    anywhere = pl.BlockSpec(memory_space=pl.ANY)
    dma = pltpu.SemaphoreType.DMA
    sum_rows = sums.shape[0] // (n * batches)
    mem_len = mem_grads[0].shape[0]
    mem_rows = mem_len // n
    mem_part = pltpu.VMEM((planes, mem_rows, width), low)
    mem_low = pltpu.VMEM((mem_len, width), low)
    square = pltpu.VMEM((width, width), low)
    vec = pltpu.VMEM((8, width), f32)
    copies = 6 + 2 * (batches // 2) + 5 * planes + 2 * batches + n
    qx, kx, raw, pk, pv, pkt, ot, stat = (pltpu.VMEM(value.shape, value.dtype) for value in saved)
    return pl.pallas_call(
        functools.partial(self_backward_kernel, n, batches),
        out_shape=(
            jax.ShapeDtypeStruct((length, width), low),
            jax.ShapeDtypeStruct((mem_rows, width), low),
            jax.ShapeDtypeStruct((PREFIX_ROWS, 2 * width), f32),
            jax.ShapeDtypeStruct((8, width), f32),
            jax.ShapeDtypeStruct((2, batches // 2, 2, planes, sum_rows, LANES), low),
        ),
        in_specs=[anywhere] * 19,
        out_specs=(vmem, vmem, vmem, vmem, anywhere),
        scratch_shapes=[
            pltpu.VMEM((heads, n, HD, length), low),
            qx,
            kx,
            raw,
            pltpu.VMEM((heads, HD, whole), low),
            pltpu.VMEM((heads, whole, HD), low),
            pltpu.VMEM((heads, HD, whole), low),
            pltpu.VMEM((heads, whole, 2 * HD), low),
            pk,
            pv,
            pkt,
            ot,
            stat,
            pltpu.VMEM((3, width, width), low),
            pltpu.VMEM((planes, heads, HD, 2 * length), f32),
            pltpu.VMEM((heads, whole, 2 * HD), f32),
            pltpu.VMEM((n, heads, 3, HD, length), low),
            pltpu.VMEM((3, n, heads, HD, length), low),
            pltpu.VMEM((heads, PREFIX_ROWS, 2 * HD), f32),
            pltpu.VMEM((batches, heads, PREFIX_ROWS, 2 * HD), f32),
            pltpu.VMEM((heads, PREFIX_ROWS, 2 * HD), low),
            pltpu.VMEM((n, heads, PREFIX_ROWS, 2 * HD), low),
            pltpu.VMEM((sums.shape[0] // 2, LANES), low),
            pltpu.VMEM((sums.shape[0] // 2, LANES), low),
            pltpu.VMEM((batches // 2, sums.shape[0] // batches, LANES), low),
            pltpu.VMEM((planes * sum_rows, LANES), low),
            pltpu.VMEM((planes, sum_rows, LANES), low),
            pltpu.VMEM((2, batches // 2, 2, planes, sum_rows, LANES), low),
            mem_low,
            mem_low,
            square,
            square,
            pltpu.VMEM((planes, 2, mem_rows, width), low),
            mem_part,
            mem_part,
            mem_part,
            pltpu.VMEM((batches, 8, width), f32),
            vec,
            pltpu.VMEM((2, 8, width), f32),
            pltpu.VMEM((16, width // 2), low),
            pltpu.VMEM((planes, 16, width // 2), low),
            pltpu.VMEM((width, length), f32),
            pltpu.VMEM((length, width), f32),
            dma((heads, n)),
            dma((heads, n)),
            dma((2, heads, n)),
            dma((2, heads, n)),
            dma((19,)),
            dma((copies,)),
            dma((copies,)),
        ],
        compiler_params=pltpu.CompilerParams(
            collective_id=1, has_side_effects=True, vmem_limit_bytes=VMEM_BYTES
        ),
        name="self_backward",
    )(
        first_grad,
        out_grad,
        sums.reshape(2, -1, LANES),
        *mem_grads,
        *mem_weights,
        vecs,
        *saved,
        *weights,
    )


def both_parts(value):
    high = value.astype(jnp.bfloat16).astype(jnp.float32)
    return jnp.concatenate([high, value - high], axis=0).astype(jnp.bfloat16)


def finish_kernel(
    full_in,
    vecs_ref,
    pkv_ref,
    emb_ref,
    first_in,
    fbias_ref,
    second_in,
    token_in,
    mem_in,
    embed_out,
    first_out,
    fbias_out,
    second_out,
    sbias_out,
    down_out,
    dbias_out,
    raise_out,
    rbias_out,
    gain_out,
    shift_out,
    token_out,
    mem_out,
    full_ref,
    first_ref,
    second_ref,
    token_ref,
    mem_ref,
    first_grad,
    second_grad,
    down_grad,
    raise_grad,
    emb,
    hidden,
    out_sem,
    in_sem,
):
    f32 = jnp.float32
    low = jnp.bfloat16
    width = emb_ref.shape[1]
    down = dbias_out.shape[1]
    count = emb_ref.shape[0]
    first = down * width // LANES
    loads = [
        pltpu.make_async_copy(source, target, in_sem.at[index])
        for index, (source, target) in enumerate(
            (
                (full_in.at[first:], full_ref.at[first:]),
                (full_in.at[:first], full_ref.at[:first]),
                (first_in, first_ref),
                (second_in, second_ref),
                (token_in, token_ref),
                (mem_in, mem_ref),
            )
        )
    ]
    for load in loads:
        load.start()
    saves = []

    def save(source, target, rows=None):
        if rows is not None:
            source, target = source.at[rows], target.at[rows]
        copy = pltpu.make_async_copy(source, target, out_sem.at[len(saves)])
        copy.start()
        saves.append(copy)

    loads[0].wait()
    for index in range(width // LANES):
        raise_grad[:, index * LANES : (index + 1) * LANES] = full_ref[
            first + index * down : first + (index + 1) * down, :
        ].astype(f32)
    save(raise_grad, raise_out)
    loads[1].wait()
    for index in range(down // LANES):
        down_grad[:, index * LANES : (index + 1) * LANES] = full_ref[
            index * width : (index + 1) * width, :
        ].astype(f32)
    save(down_grad, down_out)
    for load in loads[4:]:
        load.wait()
    save(token_ref, token_out)
    save(mem_ref, mem_out)
    loads[2].wait()
    emb[...] = jnp.zeros_like(emb)
    emb[:count, :] = emb_ref[...].astype(f32)
    emb_low = emb[...].astype(low)
    row = lax.broadcasted_iota(jnp.int32, hidden.shape, 0)
    hidden[...] = jnp.where(
        row < count, jnp.tanh(dot_nn(emb_low, first_ref[...]) + fbias_ref[...]), 0.0
    )
    value = hidden[...]
    prefix = pkv_ref[...]
    parts = both_parts(prefix)
    hidden_twice = jnp.concatenate([value, value], axis=0).T.astype(low)
    tile = 128
    for index in range(second_grad.shape[0] // tile):
        here = slice(index * tile, (index + 1) * tile)
        second_grad[here, :] = dot_nn(hidden_twice[here, :], parts)
        save(second_grad, second_out, here)
    sbias_out[...] = jnp.sum(prefix, axis=0, keepdims=True)
    loads[3].wait()
    grad = dot_nt(parts, second_ref[...])
    grad = (grad[:PREFIX_ROWS] + grad[PREFIX_ROWS:]) * (1.0 - value * value)
    fbias_out[...] = jnp.sum(grad, axis=0, keepdims=True)
    parts = both_parts(grad)
    emb_twice = jnp.concatenate([emb[...], emb[...]], axis=0).T.astype(low)
    first_grad[...] = dot_nn(emb_twice, parts)
    save(first_grad, first_out)
    back = dot_nt(parts, first_ref[...])
    embed_out[...] = (back[:PREFIX_ROWS] + back[PREFIX_ROWS:])[:count, :]
    rbias_out[...] = vecs_ref[0:1, :]
    dbias_out[...] = vecs_ref[1:2, :down]
    gain_out[...] = vecs_ref[2:5, :]
    shift_out[...] = vecs_ref[5:8, :]
    for copy in saves:
        copy.wait()


def finish(full, vecs, prefix_grad, embed, first, first_bias, second, down, token_grad, memory_grad):
    f32 = jnp.float32
    count, width = embed.shape
    hidden = first.shape[1]
    vmem = pl.BlockSpec(memory_space=pltpu.VMEM)
    anywhere = pl.BlockSpec(memory_space=pl.ANY)
    shapes = (
        (count, width),
        (width, hidden),
        (1, hidden),
        (hidden, 2 * width),
        (1, 2 * width),
        (width, down),
        (1, down),
        (down, width),
        (1, width),
        (3, width),
        (3, width),
    )
    return pl.pallas_call(
        finish_kernel,
        out_shape=tuple(jax.ShapeDtypeStruct(shape, f32) for shape in shapes)
        + tuple(
            jax.ShapeDtypeStruct(value.shape, value.dtype) for value in (token_grad, memory_grad)
        ),
        in_specs=[anywhere, vmem, vmem, vmem, anywhere, vmem, anywhere, anywhere, anywhere],
        out_specs=(
            vmem,
            anywhere,
            vmem,
            anywhere,
            vmem,
            anywhere,
            vmem,
            anywhere,
            vmem,
            vmem,
            vmem,
            anywhere,
            anywhere,
        ),
        scratch_shapes=[
            pltpu.VMEM(full.shape, jnp.bfloat16),
            pltpu.VMEM(first.shape, jnp.bfloat16),
            pltpu.VMEM(second.shape, jnp.bfloat16),
            pltpu.VMEM(token_grad.shape, token_grad.dtype),
            pltpu.VMEM(memory_grad.shape, memory_grad.dtype),
            pltpu.VMEM((width, hidden), f32),
            pltpu.VMEM((hidden, 2 * width), f32),
            pltpu.VMEM((width, down), f32),
            pltpu.VMEM((down, width), f32),
            pltpu.VMEM((PREFIX_ROWS, width), f32),
            pltpu.VMEM((PREFIX_ROWS, hidden), f32),
            pltpu.SemaphoreType.DMA((5 + hidden // 128,)),
            pltpu.SemaphoreType.DMA((6,)),
        ],
        compiler_params=pltpu.CompilerParams(vmem_limit_bytes=VMEM_BYTES),
        name="finish",
    )(full, vecs, prefix_grad, embed, first, first_bias, second, token_grad, memory_grad)


def gelu_pair(value):
    size = jnp.abs(value)
    step = 1.0 / (1.0 + (0.3275911 * 0.7071067811865476) * size)
    bell = jnp.exp(-0.5 * value * value)
    poly = step * (
        0.127414796
        + step
        * (-0.142248368 + step * (0.7107068705 + step * (-0.7265760135 + step * 0.5307027145)))
    )
    act = jnp.maximum(value, 0.0) - size * (poly * bell)
    turn = bell * (0.3989422804014327 * size - poly)
    return act, jnp.where(value >= 0.0, 1.0 + turn, -turn)


def normed(value):
    center = jnp.mean(value, axis=-1, keepdims=True)
    centered = value - center
    scale = lax.rsqrt(jnp.mean(centered * centered, axis=-1, keepdims=True) + norm_eps)
    return centered * scale, scale


def norm_back(grad, scale, unit):
    return scale * (
        grad
        - jnp.mean(grad, axis=-1, keepdims=True)
        - unit * jnp.mean(grad * unit, axis=-1, keepdims=True)
    )


def middle_kernel(
    tok_in,
    att_in,
    cot_in,
    mkey_in,
    mvalue_in,
    gain_ref,
    shift_ref,
    dbias_ref,
    rbias_ref,
    wo_in,
    wcq_in,
    wco_in,
    wd_in,
    wr_in,
    win_in,
    wout_in,
    layer_out,
    fgrad_out,
    ograd_out,
    mkey_out,
    mvalue_out,
    sums_out,
    vecs_ref,
    tok_ref,
    att_ref,
    cot_ref,
    mkey_ref,
    mvalue_ref,
    out_ref,
    fgrad_ref,
    ograd_ref,
    sums_ref,
    wo,
    wcq,
    wco,
    wd,
    wr,
    win,
    wout,
    unit_one,
    unit_two,
    work,
    total,
    scale_one,
    scale_two,
    low_one,
    low_two,
    low_three,
    query,
    crossed,
    weights,
    slopes,
    acts,
    down_act,
    down_slope,
    down_grad,
    load_sem,
    win_sem,
    wout_sem,
    out_sem,
):
    length, width = tok_ref.shape
    resident = len(win.shape) == 2
    tile = 512 if resident else win.shape[2]
    tiles = win_in.shape[1] // tile
    slots = tiles if resident else win.shape[0]
    rows_step = 128
    low = jnp.bfloat16
    f32 = jnp.float32

    sources = (
        att_in,
        wo_in,
        tok_in,
        wcq_in,
        mkey_in,
        mvalue_in,
        wco_in,
        wd_in,
        wr_in,
        cot_in,
    )
    targets = (att_ref, wo, tok_ref, wcq, mkey_ref, mvalue_ref, wco, wd, wr, cot_ref)
    loads = [
        pltpu.make_async_copy(source, target, load_sem.at[index])
        for index, (source, target) in enumerate(zip(sources, targets))
    ]

    def win_load(which):
        slot = which % slots
        target = win.at[:, rows_of(which, tile)] if resident else win.at[slot]
        return pltpu.make_async_copy(win_in.at[:, rows_of(which, tile)], target, win_sem.at[slot])

    def wout_load(which):
        slot = which % slots
        target = wout.at[rows_of(which, tile), :] if resident else wout.at[slot]
        return pltpu.make_async_copy(wout_in.at[rows_of(which, tile), :], target, wout_sem.at[slot])

    for load in loads[:7]:
        load.start()

    def by_columns(extent, step, body):
        def one(index, carry):
            body(pl.ds(pl.multiple_of(index * step, step), step))
            return carry

        lax.fori_loop(0, extent // step, one, 0)

    def by_rows(body, init=0):
        def one(index, carry):
            return body(rows_of(index, rows_step), carry)

        return lax.fori_loop(0, length // rows_step, one, init)

    cols = 512
    half = width // 2

    for load in loads[:3]:
        load.wait()
    for load in loads[7:]:
        load.start()
    for which in range(slots):
        win_load(which).start()
    for which in range(slots):
        wout_load(which).start()

    def project_out(here):
        work[:, here] = tok_ref[:, here].astype(f32) + dot_nn(att_ref[...], wo[:, here])

    by_columns(width, cols, project_out)

    def first_norm(here, carry):
        unit, scale = normed(work[here, :])
        unit_one[here, :] = unit
        scale_one[here, :] = scale
        value = unit * gain_ref[0:1, :] + shift_ref[0:1, :]
        work[here, :] = value
        low_one[here, :] = value.astype(low)
        return carry

    by_rows(first_norm)

    loads[3].wait()

    def project_query(here):
        query[:, here] = dot_nn(low_one[...], wcq[:, here]).astype(low)

    by_columns(width, cols, project_query)
    per_block = LANES // HD

    def stacked(value):
        return jnp.concatenate(
            [jnp.where(head_lanes(value.shape, head), value, 0.0) for head in range(per_block)],
            axis=0,
        ).astype(low)

    def unstacked(value):
        return jnp.concatenate(
            [
                value[head * HD : (head + 1) * HD, head * length : (head + 1) * length]
                for head in range(per_block)
            ],
            axis=0,
        )

    def block_queries(here):
        return stacked(query[:, here].astype(f32) * 0.125)

    def cross_forward(block):
        here = rows_of(block, LANES)
        scores = dot_nt(mkey_ref[:, here], block_queries(here))
        raised = jnp.exp(scores - jnp.max(scores, axis=0, keepdims=True))
        share = 1.0 / jnp.sum(raised, axis=0, keepdims=True)
        weight = (raised * share).astype(low)
        weights[block] = weight
        values = mvalue_ref[:, here].astype(f32).T.astype(low)
        crossed[:, here] = unstacked(dot_nn(values, weight)).T.astype(low)

    loads[4].wait()
    loads[5].wait()

    def cross_forward_both(step, carry):
        cross_forward(2 * step)
        cross_forward(2 * step + 1)
        return carry

    lax.fori_loop(0, width // LANES // 2, cross_forward_both, 0)

    loads[6].wait()

    def project_crossed(here):
        work[:, here] += dot_nn(crossed[...], wco[:, here])

    by_columns(width, cols, project_crossed)

    def second_norm(here, carry):
        unit, scale = normed(work[here, :])
        unit_two[here, :] = unit
        scale_two[here, :] = scale
        value = unit * gain_ref[1:2, :] + shift_ref[1:2, :]
        work[here, :] = value
        low_two[here, :] = value.astype(low)
        return carry

    by_rows(second_norm)

    step_cols = 512

    def feed_part(here, source):
        act, slope = gelu_pair(dot_nn(low_two[...], source))
        slopes[:, here] = slope.astype(low)
        return act.astype(low)

    if resident:

        def feed_forward(which, carry):
            here = rows_of(which, step_cols)

            @pl.when(which % (tile // step_cols) == 0)
            def _():
                win_load(which // (tile // step_cols)).wait()

            acts[:, here] = feed_part(here, win[:, here])
            return carry

        lax.fori_loop(0, tiles * tile // step_cols, feed_forward, 0)
        for which in range(tiles):
            wout_load(which).wait()

        def feed_out_part(here):
            total[:, here] = dot_nn(acts[...], wout[:, here])

        by_columns(width, step_cols, feed_out_part)
    else:
        total[...] = jnp.zeros_like(total)

        def feed_forward(which, carry):
            slot = lax.rem(which, slots)
            win_load(which).wait()
            wout_load(which).wait()
            total[...] += dot_nn(feed_part(rows_of(which, tile), win[slot]), wout[slot])

            @pl.when(which + slots < tiles)
            def _():
                win_load(which + slots).start()
                wout_load(which + slots).start()

            return carry

        lax.fori_loop(0, tiles, feed_forward, 0)

    loads[7].wait()
    loads[8].wait()
    loads[9].wait()
    act, slope = gelu_pair(dot_nn(low_two[...], wd[...]) + dbias_ref[...])
    down_act[...] = act.astype(low)
    down_slope[...] = slope.astype(low)

    def project_raise(here):
        work[:, here] += total[:, here] + 4.0 * (
            dot_nn(down_act[...], wr[:, here]) + rbias_ref[:, here]
        )

    by_columns(width, cols, project_raise)
    nothing = jnp.zeros((1, width), f32)

    def third_norm(here, carry):
        gain_sum, shift_sum, bias_sum = carry
        unit, scale = normed(work[here, :])
        gain = gain_ref[2:3, :]
        out_ref[here, :] = (unit * gain + shift_ref[2:3, :]).astype(low)
        grad = cot_ref[here, :].astype(f32)
        back = norm_back(grad * gain, scale, unit)
        total[here, :] = back
        back_low = back.astype(low)
        low_three[here, :] = back_low
        return (
            gain_sum + jnp.sum(grad * unit, axis=0, keepdims=True),
            shift_sum + jnp.sum(grad, axis=0, keepdims=True),
            bias_sum + jnp.sum(back_low.astype(f32), axis=0, keepdims=True),
        )

    gain_three, shift_three, bias_sum = by_rows(third_norm, (nothing, nothing, nothing))
    saves = []

    def save(source, target):
        copy = pltpu.make_async_copy(source, target, out_sem.at[len(saves)])
        copy.start()
        saves.append(copy)

    save(out_ref, layer_out)
    vecs_ref[0:1, :] = 4.0 * bias_sum

    back = 4.0 * dot_nt(low_three[...], wr[...]) * down_slope[...].astype(f32)
    back_low = back.astype(low)
    down_grad[...] = back_low
    vecs_ref[1:2, :] = jnp.concatenate(
        [
            jnp.sum(back_low.astype(f32), axis=0, keepdims=True),
            jnp.zeros((1, width - wd.shape[1]), f32),
        ],
        axis=1,
    )
    down = wd.shape[1]
    raise_sum = 4.0 * dot_tn(down_act[...], low_three[...])
    for index in range(width // LANES):
        sums_ref[pl.ds(down * width // LANES + index * down, down), :] = raise_sum[
            :, index * LANES : (index + 1) * LANES
        ].astype(low)
    down_sum = dot_tn(low_two[...], down_grad[...])
    for index in range(down // LANES):
        sums_ref[index * width : (index + 1) * width, :] = down_sum[
            :, index * LANES : (index + 1) * LANES
        ].astype(low)

    save(sums_ref, sums_out)

    if resident:

        def feed_slope(here):
            acts[:, here] = (
                dot_nt(low_three[...], wout[here, :]) * slopes[:, here].astype(f32)
            ).astype(low)

        by_columns(win_in.shape[1], step_cols, feed_slope)

        def feed_in_part(here):
            total[:, here] += dot_nt(acts[...], win[here, :])

        by_columns(width, step_cols, feed_in_part)
    else:

        def feed_backward(step, carry):
            which = tiles - 1 - step
            slot = lax.rem(which, slots)
            here = rows_of(which, tile)

            @pl.when(which < tiles - slots)
            def _():
                wout_load(which).wait()
                win_load(which).wait()

            grad = dot_nt(low_three[...], wout[slot]) * slopes[:, here].astype(f32)
            total[...] += dot_nt(grad.astype(low), win[slot])

            @pl.when(which >= slots)
            def _():
                win_load(which - slots).start()
                wout_load(which - slots).start()

            return carry

        lax.fori_loop(0, tiles, feed_backward, 0)

    def down_back(here):
        total[:, here] += dot_nt(down_grad[...], wd[here, :])

    by_columns(width, cols, down_back)

    def second_back(here, carry):
        gain_sum, shift_sum = carry
        grad = total[here, :]
        unit = unit_two[here, :]
        back = norm_back(grad * gain_ref[1:2, :], scale_two[here, :], unit)
        total[here, :] = back
        low_one[here, :] = back.astype(low)
        return (
            gain_sum + jnp.sum(grad * unit, axis=0, keepdims=True),
            shift_sum + jnp.sum(grad, axis=0, keepdims=True),
        )

    gain_two, shift_two = by_rows(second_back, (nothing, nothing))

    def crossed_back(here):
        crossed[:, here] = dot_nt(low_one[...], wco[here, :]).astype(low)

    by_columns(width, cols, crossed_back)

    def cross_backward(block):
        here = rows_of(block, LANES)
        grads = stacked(crossed[:, here].astype(f32))
        keys = mkey_ref[:, here].astype(f32).T.astype(low)
        slope = dot_nt(mvalue_ref[:, here], grads)
        weight_low = weights[block]
        weight = weight_low.astype(f32)
        slope = weight * (slope - jnp.sum(weight * slope, axis=0, keepdims=True))
        slope = slope.astype(low)
        queries = block_queries(here)
        mkey_ref[:, here] = dot_nn(slope, queries).astype(low)
        mvalue_ref[:, here] = dot_nn(weight_low, grads).astype(low)
        query[:, here] = (unstacked(dot_nn(keys, slope)) * 0.125).T.astype(low)

    def cross_backward_both(step, carry):
        cross_backward(2 * step)
        cross_backward(2 * step + 1)
        return carry

    lax.fori_loop(0, width // LANES // 2, cross_backward_both, 0)
    save(mkey_ref, mkey_out)
    save(mvalue_ref, mvalue_out)

    def query_back(here):
        total[:, here] += dot_nt(query[...], wcq[here, :])

    by_columns(width, cols, query_back)

    def first_back(here, carry):
        gain_sum, shift_sum = carry
        grad = total[here, :]
        unit = unit_one[here, :]
        back = norm_back(grad * gain_ref[0:1, :], scale_one[here, :], unit)
        fgrad_ref[here, :] = back
        low_one[here, :] = back.astype(low)
        return (
            gain_sum + jnp.sum(grad * unit, axis=0, keepdims=True),
            shift_sum + jnp.sum(grad, axis=0, keepdims=True),
        )

    gain_one, shift_one = by_rows(first_back, (nothing, nothing))
    save(fgrad_ref, fgrad_out)

    for index in range(width // cols):
        here = slice(index * cols, (index + 1) * cols)
        ograd_ref[here, :] = dot_nt(low_one[...], wo[here, :]).T.astype(low)
        save(ograd_ref.at[here], ograd_out.at[here])
    for index, vector in enumerate(
        (gain_one, gain_two, gain_three, shift_one, shift_two, shift_three)
    ):
        vecs_ref[2 + index : 3 + index, :] = vector
    for copy in saves:
        copy.wait()


def middle(
    tokens, attended, cotangent, mem_key, mem_value, gains, shifts, down_bias, raise_bias, weights
):
    length, width = tokens.shape
    mem_len = mem_key.shape[0]
    down = weights[3].shape[1]
    feed = weights[5].shape[1]
    tile = 512 if mem_len <= 512 else 128
    resident = mem_len <= 512
    slots = feed // tile if resident else 2
    low = jnp.bfloat16
    f32 = jnp.float32
    vmem = pl.BlockSpec(memory_space=pltpu.VMEM)
    anywhere = pl.BlockSpec(memory_space=pl.ANY)
    square = pltpu.VMEM((width, width), low)
    wide = pltpu.VMEM((length, width), f32)
    narrow = pltpu.VMEM((length, width), low)
    return pl.pallas_call(
        middle_kernel,
        out_shape=(
            jax.ShapeDtypeStruct((length, width), low),
            jax.ShapeDtypeStruct((length, width), f32),
            jax.ShapeDtypeStruct((width, length), low),
            jax.ShapeDtypeStruct((mem_len, width), low),
            jax.ShapeDtypeStruct((mem_len, width), low),
            jax.ShapeDtypeStruct((2 * down * width // LANES, LANES), low),
            jax.ShapeDtypeStruct((8, width), f32),
        ),
        in_specs=[anywhere] * 5 + [vmem] * 4 + [anywhere] * 7,
        out_specs=(anywhere,) * 6 + (vmem,),
        scratch_shapes=[
            narrow,
            narrow,
            narrow,
            pltpu.VMEM((mem_len, width), low),
            pltpu.VMEM((mem_len, width), low),
            narrow,
            wide,
            pltpu.VMEM((width, length), low),
            pltpu.VMEM((2 * down * width // LANES, LANES), low),
            square,
            square,
            square,
            pltpu.VMEM((width, down), low),
            pltpu.VMEM((down, width), low),
            pltpu.VMEM((width, feed) if resident else (slots, width, tile), low),
            pltpu.VMEM((feed, width) if resident else (slots, tile, width), low),
            wide,
            wide,
            wide,
            wide,
            pltpu.VMEM((length, 1), f32),
            pltpu.VMEM((length, 1), f32),
            narrow,
            narrow,
            narrow,
            narrow,
            narrow,
            pltpu.VMEM((width // LANES, mem_len, LANES // HD * length), low),
            pltpu.VMEM((length, feed), low),
            pltpu.VMEM((length, feed) if resident else (16, LANES), low),
            pltpu.VMEM((length, down), low),
            pltpu.VMEM((length, down), low),
            pltpu.VMEM((length, down), low),
            pltpu.SemaphoreType.DMA((10,)),
            pltpu.SemaphoreType.DMA((slots,)),
            pltpu.SemaphoreType.DMA((slots,)),
            pltpu.SemaphoreType.DMA((5 + width // 512,)),
        ],
        compiler_params=pltpu.CompilerParams(vmem_limit_bytes=VMEM_BYTES + 3 * 1024 * 1024),
        name="middle",
    )(tokens, attended, cotangent, mem_key, mem_value, gains, shifts, down_bias, raise_bias, *weights)


def per_device(
    tokens,
    memory,
    segment_ids,
    padding_mask,
    cotangent,
    prefix_embed,
    prefix_first,
    first_bias,
    prefix_second,
    second_bias,
    adapter_down,
    down_bias,
    adapter_raise,
    raise_bias,
    norm_gain,
    norm_shift,
    self_query,
    self_key,
    self_value,
    self_output,
    cross_query,
    cross_key,
    cross_value,
    cross_output,
    feed_in,
    feed_out,
):
    row_count, length, model_width = tokens.shape
    flat_rows = row_count * length
    n = lax.axis_size("seq")
    batches = lax.axis_size("batch")
    down = adapter_down.shape[1]
    attended, mem_key, mem_value, *saved = self_forward(
        n,
        segment_ids,
        padding_mask,
        tokens.reshape(flat_rows, model_width),
        (self_query, self_key, self_value),
        (
            prefix_embed,
            prefix_first,
            first_bias.reshape(1, -1),
            prefix_second,
            second_bias.reshape(1, -1),
        ),
        memory.reshape(-1, model_width),
        (cross_key, cross_value),
    )
    layer_output, first_grad, out_grad, *mem_grads, weight_sums, vector_sums = middle(
        tokens.reshape(flat_rows, model_width),
        attended,
        cotangent.reshape(flat_rows, model_width),
        mem_key,
        mem_value,
        norm_gain,
        norm_shift,
        down_bias.reshape(1, -1),
        raise_bias.reshape(1, -1),
        (
            self_output,
            cross_query,
            cross_output,
            adapter_down,
            adapter_raise,
            feed_in,
            feed_out,
        ),
    )
    layer_output = layer_output.reshape(row_count, length, model_width)
    token_grad, memory_grad, prefix_grad, vector_sums, full_sums = self_backward(
        n,
        batches,
        first_grad,
        out_grad.reshape(n, -1, HD, length),
        weight_sums,
        mem_grads,
        (cross_key, cross_value),
        vector_sums,
        saved,
        (self_query, self_key, self_value),
    )
    *replicated, token_grad, memory_grad = finish(
        full_sums.reshape(-1, LANES),
        vector_sums,
        prefix_grad,
        prefix_embed,
        prefix_first,
        first_bias.reshape(1, -1),
        prefix_second,
        down,
        token_grad,
        memory_grad,
    )
    token_grad = token_grad.reshape(row_count, length, model_width)
    memory_grad = memory_grad.reshape(memory.shape)
    replicated = [
        value.reshape(-1) if value.shape[0] == 1 else value for value in replicated
    ]
    return (layer_output, token_grad, memory_grad, *replicated)


def solution(mesh):
    placed = (
        P("batch", "seq", None),
        P("batch", "seq", None),
        P("batch", "seq"),
        P("batch", "seq"),
        P("batch", "seq", None),
        P(),
        P(),
        P(),
        P(),
        P(),
        P(),
        P(),
        P(),
        P(),
        P(),
        P(),
        P(),
        P(),
        P(),
        P(),
        P(),
        P(),
        P(),
        P(),
        P(),
        P(),
    )
    return jax.shard_map(
        per_device,
        mesh=mesh,
        in_specs=placed,
        out_specs=(
            P("batch", "seq", None),
            P("batch", "seq", None),
            P("batch", "seq", None),
            P(),
            P(),
            P(),
            P(),
            P(),
            P(),
            P(),
            P(),
            P(),
            P(),
            P(),
        ),
        check_vma=False,
    )
```

```python
import functools

import jax
import jax.numpy as jnp
from jax import lax
from jax.experimental import pallas as pl
from jax.experimental.pallas import tpu as pltpu
from jax.sharding import PartitionSpec as P

H = 16
HD = 64
LANES = 128
PREFIX_ROWS = 32
VMEM_BYTES = 60 * 1024 * 1024
SUM_ROWS = 16
MESH = pl.DeviceIdType.MESH

masked_score = -1e30
norm_eps = 1e-05

def dot_nn(left, right):
    return lax.dot_general(
        left, right, (((1,), (0,)), ((), ())), preferred_element_type=jnp.float32
    )


def dot_nt(left, right):
    return lax.dot_general(
        left, right, (((1,), (1,)), ((), ())), preferred_element_type=jnp.float32
    )


def dot_tn(left, right):
    return lax.dot_general(
        left, right, (((0,), (0,)), ((), ())), preferred_element_type=jnp.float32
    )


def remote(source, target, send_sem, recv_sem, axis, peer):
    return pltpu.make_async_remote_copy(
        src_ref=source,
        dst_ref=target,
        send_sem=send_sem,
        recv_sem=recv_sem,
        device_id={axis: peer},
        device_id_type=MESH,
    )


def enter(sizes):
    barrier = pltpu.get_barrier_semaphore()
    for axis, size in sizes.items():
        for other in range(size):

            @pl.when(other != lax.axis_index(axis))
            def _():
                pl.semaphore_signal(barrier, inc=1, device_id={axis: other}, device_id_type=MESH)

    pl.semaphore_wait(barrier, sum(sizes.values()) - len(sizes))


def others(size, mine, body):
    for other in range(size):

        @pl.when(other != mine)
        def _():
            body(other)


def rows_of(index, size):
    return pl.ds(pl.multiple_of(index * size, size), size)


def span_of(start, size):
    return pl.ds(pl.multiple_of(start, LANES), size)


def own_columns(ref, first, me, width):
    if width % LANES == 0:
        return ref[:, pl.ds(pl.multiple_of(first + me * width, LANES), width)].astype(jnp.float32)
    share = LANES // width
    block = ref[:, pl.ds(pl.multiple_of(first + me // share * LANES, LANES), LANES)].astype(
        jnp.float32
    )
    picked = block[:, :width]
    for part in range(1, share):
        picked = jnp.where(me % share == part, block[:, part * width : (part + 1) * width], picked)
    return picked


def head_lanes(shape, head):
    lane = lax.broadcasted_iota(jnp.int32, shape, 1)
    return (lane >= head * HD) & (lane < (head + 1) * HD)


def self_forward_kernel(
    n,
    seg_ref,
    pad_ref,
    tok_ref,
    wq_in,
    wk_in,
    wv_in,
    emb_ref,
    first_in,
    fbias_ref,
    second_in,
    sbias_ref,
    mem_ref,
    wck_in,
    wcv_in,
    att_ref,
    mkey_out,
    mvalue_out,
    qx_out,
    kx_out,
    raw_out,
    pk_out,
    pv_out,
    pkt_out,
    ot_out,
    lse_out,
    send,
    recv,
    meta_send,
    meta,
    kx,
    qx,
    vt,
    hidden,
    pk,
    pv,
    pkt,
    pvt,
    stat,
    acc,
    o_send,
    o_recv,
    mem_all,
    wck,
    wcv,
    mkey_ref,
    mvalue_ref,
    wq_ref,
    wk_ref,
    wv_ref,
    first_ref,
    second_ref,
    send_sem,
    recv_sem,
    meta_send_sem,
    meta_recv_sem,
    o_send_sem,
    o_recv_sem,
    mem_send_sem,
    mem_recv_sem,
    out_sem,
    weight_sem,
    in_sem,
):
    low = jnp.bfloat16
    f32 = jnp.float32
    me = lax.axis_index("seq")
    length, width = tok_ref.shape
    group = width // n
    heads = group // HD
    plane = 2 * length
    planes = n // 2
    block = 2 * LANES
    per_block = block // group
    blocks = width // block
    my_plane = me // 2
    my_side = lax.rem(me, 2)

    def meta_copy(peer, slot):
        return remote(
            meta_send, meta.at[slot], meta_send_sem.at[peer], meta_recv_sem.at[slot], "seq", peer
        )

    def qkv_copy(head, peer, slot):
        return remote(
            send.at[peer, head],
            recv.at[head, slot],
            send_sem.at[head, peer],
            recv_sem.at[head, slot],
            "seq",
            peer,
        )

    def out_copy(head, peer, slot):
        return remote(
            o_send.at[head, peer],
            o_recv.at[slot, head],
            o_send_sem.at[head, peer],
            o_recv_sem.at[head, slot],
            "seq",
            peer,
        )

    def mem_along(which, toward):
        part = mem_all.at[which, my_side]
        return remote(
            part,
            part,
            mem_send_sem.at[(toward + 1) // 2, which],
            mem_recv_sem.at[which],
            "seq",
            me + 2 * toward,
        )

    def mem_across(side):
        part = mem_all.at[:, side]
        return remote(
            part,
            part,
            mem_send_sem.at[0, planes],
            mem_recv_sem.at[planes],
            "seq",
            me + 1 - 2 * my_side,
        )

    def mem_hops(hop, body):
        for toward in (1, -1):
            which = my_plane - toward * hop
            ahead = my_plane + toward

            @pl.when((which >= 0) & (which < planes) & (ahead >= 0) & (ahead < planes))
            def _():
                body(mem_along(which, toward))

    def mem_arrivals(hop):
        for toward in (1, -1):
            which = my_plane - toward * hop

            @pl.when((which >= 0) & (which < planes))
            def _():
                mem_along(which, -toward).wait_recv()

    def block_at(step):
        if blocks >= planes:
            share = blocks // planes
            return lax.rem(my_plane + 1 + step // share, planes) * share + step % share
        return lax.rem(me // per_block + 1 + step, blocks)

    def weight_load(step, which):
        columns = rows_of(block_at(step), block)
        source = (wq_in, wk_in, wv_in)[which]
        target = (wq_ref, wk_ref, wv_ref)[which]
        return pltpu.make_async_copy(
            source.at[:, columns], target.at[:, columns], weight_sem.at[step, which]
        )

    for step in range(blocks):
        for which in range(3):
            weight_load(step, which).start()
    loads = [
        pltpu.make_async_copy(source, target, in_sem.at[index])
        for index, (source, target) in enumerate(
            ((first_in, first_ref), (second_in, second_ref), (wck_in, wck), (wcv_in, wcv))
        )
    ]
    for load in loads:
        load.start()
    segments = seg_ref[...]
    tags = jnp.where(pad_ref[...] == 1, segments, -1)
    row = lax.broadcasted_iota(jnp.int32, meta_send.shape, 0)
    meta_send[...] = jnp.where(row == 0, segments, tags)
    mem_all[my_plane, my_side] = mem_ref[...]
    enter({"seq": n})
    others(n, me, lambda peer: meta_copy(peer, me).start())
    meta[me] = meta_send[...]

    for step in range(blocks):
        at = block_at(step)
        columns = rows_of(at, block)
        for which, weight in enumerate((wq_ref, wk_ref, wv_ref)):
            weight_load(step, which).wait()
            piece = dot_nn(tok_ref[...], weight[:, columns]).T.astype(low)
            for part in range(per_block):
                for head in range(heads):
                    first = part * group + head * HD
                    send[at * per_block + part, head, which] = piece[first : first + HD]
        for part in range(per_block):
            peer = at * per_block + part

            @pl.when(peer != me)
            def _():
                qkv_copy(0, peer, me).start()

            @pl.when(peer == me)
            def _():
                for head in range(heads):
                    recv[head, me] = send[peer, head]

    mem_hops(0, lambda copy: copy.start())
    loads[0].wait()
    loads[1].wait()
    hidden[...] = jnp.zeros_like(hidden)
    hidden[: emb_ref.shape[0], :] = jnp.tanh(dot_nn(emb_ref[...], first_ref[...]) + fbias_ref[...])
    hidden_low = hidden[...].astype(low)
    prefix_key = dot_nn(hidden_low, own_columns(second_ref, 0, me, group).astype(low)) + own_columns(
        sbias_ref, 0, me, group
    )
    prefix_value = dot_nn(
        hidden_low, own_columns(second_ref, width, me, group).astype(low)
    ) + own_columns(sbias_ref, width, me, group)
    prefix_row = lax.broadcasted_iota(jnp.int32, (PREFIX_ROWS, HD), 0)
    prefix_open = jnp.where(prefix_row < emb_ref.shape[0], 0.0, masked_score)
    for head in range(heads):
        here = slice(head * HD, (head + 1) * HD)
        pk[head] = jnp.concatenate([prefix_key[:, here], prefix_open], axis=1).astype(low)
        pv[head] = prefix_value[:, here].astype(low)
    pkt[...] = prefix_key.T.astype(low).reshape(heads, HD, PREFIX_ROWS)
    pvt[:, :HD, :] = prefix_value.T.astype(low).reshape(heads, HD, PREFIX_ROWS)
    pvt[:, HD:, :] = jnp.ones((heads, SUM_ROWS, PREFIX_ROWS), low)
    vt[:, HD:, :] = jnp.ones((heads, SUM_ROWS, n * length), low)

    def arrive(head, chunk):
        @pl.when(chunk != me)
        def _():
            @pl.when(head == 0)
            def _():
                meta_copy(chunk, chunk).wait_recv()

            qkv_copy(head, chunk, chunk).wait_recv()

        here = rows_of(chunk, length)
        state = lax.broadcasted_iota(jnp.int32, (HD, length), 0)
        qx[head, :HD, here] = (recv[head, chunk, 0].astype(f32) * 0.125).astype(low)
        qx[head, HD:, here] = jnp.where(state == meta[chunk, 0:1, :], 1.0, 0.0).astype(low)
        is_open = jnp.where(state == meta[chunk, 1:2, :], 0.0, masked_score)
        kx[head, here, :] = jnp.concatenate(
            [recv[head, chunk, 1].astype(f32), is_open], axis=0
        ).T.astype(low)
        vt[head, :HD, here] = recv[head, chunk, 2]

    def open_plane(head, which):
        scores = dot_nn(pk[head], qx[head, :, rows_of(which, plane)])
        top = jnp.max(scores, axis=0, keepdims=True)
        raised = jnp.exp(scores - top)
        stat[which, head, 0:1, :] = top
        acc[which, head] = dot_nn(pvt[head], raised.astype(low))

    def pair_part(head, upper, lower, first, count, keys, diagonal):
        here = slice(first, first + count)
        queries = qx[head, :, span_of(upper * plane + first, count)]
        key_rows = span_of(lower * plane, keys)
        scores = dot_nn(kx[head, key_rows, :], queries)
        if diagonal:
            key_at = lax.broadcasted_iota(jnp.int32, scores.shape, 0)
            query_at = lax.broadcasted_iota(jnp.int32, scores.shape, 1) + first
            scores = jnp.where(key_at <= query_at, scores, masked_score)
        old_top = stat[upper, head, 0:1, here]
        top = jnp.maximum(old_top, jnp.max(scores, axis=0, keepdims=True))
        raised = jnp.exp(scores - top).astype(low)
        stat[upper, head, 0:1, here] = top
        acc[upper, head, :, here] = acc[upper, head, :, here] * jnp.exp(old_top - top) + dot_nn(
            vt[head, :, key_rows], raised
        )

    def pair(head, upper, lower):
        pair_part(head, upper, lower, 0, plane, plane, False)

    def pair_diagonal(head, which):
        for part in range(2):
            pair_part(head, which, which, part * length, length, (part + 1) * length, True)

    def close_plane(head, which):
        total = acc[which, head, HD : HD + 1, :]
        value = acc[which, head, :HD, :] / total
        acc[which, head, :HD, :] = value
        stat[which, head, 0:1, :] = stat[which, head, 0:1, :] + jnp.log(total)
        for part in range(2):
            chunk = 2 * which + part
            o_send[head, chunk] = value[:, part * length : (part + 1) * length].astype(low)

            @pl.when((chunk != me) & (head == heads - 1))
            def _():
                out_copy(head, chunk, me).start()

            @pl.when(chunk == me)
            def _():
                o_recv[me, head] = o_send[head, chunk]

    def project_memory():
        mem_across(1 - my_side).wait_recv()
        for load in loads[2:]:
            load.wait()
        whole = mem_all[...].reshape(mkey_ref.shape)

        def one(index, carry):
            here = rows_of(index, block)
            mkey_ref[:, here] = dot_nn(whole, wck[:, here]).astype(low)
            mvalue_ref[:, here] = dot_nn(whole, wcv[:, here]).astype(low)
            return carry

        lax.fori_loop(0, blocks, one, 0)

    def stage(index, carry):
        head = index // planes
        step = lax.rem(index, planes)

        @pl.when(head + 1 < heads)
        def _():
            there = lax.rem(my_plane + 1 + step, planes)
            for part in range(2):
                peer = 2 * there + part

                @pl.when(peer != me)
                def _():
                    qkv_copy(head, peer, me).wait_send()
                    qkv_copy(head + 1, peer, me).start()

        @pl.when((head == heads - 1) & (head > 0))
        def _():
            there = lax.rem(my_plane + 1 + step, planes)
            for part in range(2):
                peer = 2 * there + part

                @pl.when(peer != me)
                def _():
                    qkv_copy(head, peer, me).wait_send()
                    out_copy(head - 1, peer, me).start()

        here = lax.rem(my_plane + step, planes)
        arrive(head, 2 * here)
        arrive(head, 2 * here + 1)
        open_plane(head, here)
        pair_diagonal(head, here)

        def earlier(back, inner):
            there = lax.rem(my_plane + back, planes)
            pair(head, jnp.maximum(here, there), jnp.minimum(here, there))

            @pl.when((step == planes - 1) & (there > here))
            def _():
                close_plane(head, there)

            return inner

        lax.fori_loop(0, step, earlier, 0)
        for hop in range(1, planes - 1):

            @pl.when(index == hop)
            def _():
                mem_arrivals(hop)
                mem_hops(hop, lambda copy: copy.start())

        @pl.when(index == planes - 1)
        def _():
            mem_arrivals(planes - 1)
            mem_across(my_side).start()

        @pl.when((my_plane + step >= planes) | (my_plane == 0))
        def _():
            close_plane(head, here)

        return carry

    lax.fori_loop(0, heads * planes, stage, 0)

    saves = []

    def save(source, target):
        copy = pltpu.make_async_copy(source, target, out_sem.at[len(saves)])
        copy.start()
        saves.append(copy)

    save(qx, qx_out)
    save(kx, kx_out)
    save(recv, raw_out)
    save(pk, pk_out)
    save(pv, pv_out)
    save(pkt, pkt_out)
    save(acc, ot_out)
    save(stat, lse_out)
    project_memory()
    save(mkey_ref, mkey_out)
    save(mvalue_ref, mvalue_out)
    for other in range(n):

        @pl.when(other != me)
        def _():
            for head in range(heads):
                out_copy(head, other, other).wait_recv()

        att_ref[:, other * group : (other + 1) * group] = (
            o_recv[other].reshape(group, length).astype(f32).T.astype(low)
        )

    def drain(peer):
        meta_copy(peer, me).wait_send()
        if heads == 1:
            qkv_copy(0, peer, me).wait_send()
        for head in range(heads):
            out_copy(head, peer, me).wait_send()

    others(n, me, drain)
    for hop in range(planes - 1):
        mem_hops(hop, lambda copy: copy.wait_send())
    mem_across(my_side).wait_send()
    for copy in saves:
        copy.wait()


def self_forward(n, segments, padding, tokens, weights, prefix, memory, mem_weights):
    length, width = tokens.shape
    group = width // n
    heads = group // HD
    whole = n * length
    planes = n // 2
    low = jnp.bfloat16
    f32 = jnp.float32
    vmem = pl.BlockSpec(memory_space=pltpu.VMEM)
    anywhere = pl.BlockSpec(memory_space=pl.ANY)
    dma = pltpu.SemaphoreType.DMA
    shapes = (
        ((heads, 2 * HD, whole), low),
        ((heads, whole, 2 * HD), low),
        ((heads, n, 3, HD, length), low),
        ((heads, PREFIX_ROWS, 2 * HD), low),
        ((heads, PREFIX_ROWS, HD), low),
        ((heads, HD, PREFIX_ROWS), low),
        ((planes, heads, HD + SUM_ROWS, 2 * length), f32),
        ((planes, heads, 8, 2 * length), f32),
    )
    square = pltpu.VMEM((width, width), low)
    qx, kx, raw, pk, pv, pkt, acc, stat = (pltpu.VMEM(*shape) for shape in shapes)
    return pl.pallas_call(
        functools.partial(self_forward_kernel, n),
        out_shape=(
            jax.ShapeDtypeStruct((length, width), low),
            jax.ShapeDtypeStruct((n * memory.shape[0], width), low),
            jax.ShapeDtypeStruct((n * memory.shape[0], width), low),
        )
        + tuple(jax.ShapeDtypeStruct(*shape) for shape in shapes),
        in_specs=[vmem] * 3
        + [anywhere] * 3
        + [vmem, anywhere, vmem, anywhere, vmem, vmem]
        + [anywhere] * 2,
        out_specs=(vmem,) + (anywhere,) * 10,
        scratch_shapes=[
            pltpu.VMEM((n, heads, 3, HD, length), low),
            raw,
            pltpu.VMEM((8, length), jnp.int32),
            pltpu.VMEM((n, 8, length), jnp.int32),
            kx,
            qx,
            pltpu.VMEM((heads, HD + SUM_ROWS, whole), low),
            pltpu.VMEM((PREFIX_ROWS, weights[0].shape[0] // 2), f32),
            pk,
            pv,
            pkt,
            pltpu.VMEM((heads, HD + SUM_ROWS, PREFIX_ROWS), low),
            stat,
            acc,
            pltpu.VMEM((heads, n, HD, length), low),
            pltpu.VMEM((n, heads, HD, length), low),
            pltpu.VMEM((planes, 2) + memory.shape, low),
            square,
            square,
            pltpu.VMEM((n * memory.shape[0], width), low),
            pltpu.VMEM((n * memory.shape[0], width), low),
            square,
            square,
            square,
            pltpu.VMEM(prefix[1].shape, low),
            pltpu.VMEM(prefix[3].shape, low),
            dma((heads, n)),
            dma((heads, n)),
            dma((n,)),
            dma((n,)),
            dma((heads, n)),
            dma((heads, n)),
            dma((2, planes + 1)),
            dma((planes + 1,)),
            dma((10,)),
            dma((width // (2 * LANES), 3)),
            dma((4,)),
        ],
        compiler_params=pltpu.CompilerParams(
            collective_id=0, has_side_effects=True, vmem_limit_bytes=VMEM_BYTES
        ),
        name="self_forward",
    )(segments, padding, tokens, *weights, *prefix, memory, *mem_weights)


def self_backward_kernel(
    n,
    batches,
    base_in,
    do_in,
    sums_in,
    mkey_in,
    mvalue_in,
    wck_in,
    wcv_in,
    vecs_in,
    qx_in,
    kx_in,
    raw_in,
    pk_in,
    pv_in,
    pkt_in,
    ot_in,
    lse_in,
    wq_in,
    wk_in,
    wv_in,
    tg_ref,
    mgrad_ref,
    pkv_ref,
    vecs_ref,
    full_out,
    do_recv,
    qx,
    kx,
    raw,
    kt,
    values,
    dot,
    qdo,
    pk,
    pv,
    pkt,
    ot,
    stat,
    weights,
    dqt,
    dkv,
    g_send,
    g_recv,
    pre_ref,
    pre_all,
    pre_sum,
    pre_recv,
    sums_mine,
    sums_core,
    sums_x,
    sums_side,
    sums_z,
    full,
    mkey,
    mvalue,
    wck,
    wcv,
    mem_part,
    mem_side,
    mem_up,
    mem_down,
    vec_all,
    vec_sum,
    vec_y,
    vec_both,
    vec_z,
    product,
    base_ref,
    do_send_sem,
    do_recv_sem,
    g_send_sem,
    g_recv_sem,
    in_sem,
    send_sem,
    recv_sem,
):
    low = jnp.bfloat16
    f32 = jnp.float32
    me = lax.axis_index("seq")
    length, width = tg_ref.shape
    group = width // n
    heads = group // HD
    plane = 2 * length
    planes = n // 2
    step_rows = 256
    my_batch = lax.axis_index("batch")
    my_core = lax.rem(my_batch, 2)
    my_high = my_batch // 2
    highs = batches // 2
    my_plane = me // 2
    my_side = lax.rem(me, 2)
    beside = me + 1 - 2 * my_side
    used = [0]

    def numbers(count):
        used[0] += count
        return used[0] - count

    core_slot = numbers(2)
    x_slot = numbers(2 * highs)
    y_slot = numbers(3)
    z_slot = numbers(2 * planes)
    up_slot = numbers(planes)
    down_slot = numbers(planes)
    va_slot = numbers(batches)
    vb_slot = numbers(1)
    vc_slot = numbers(planes)
    pa_slot = numbers(batches)
    pb_slot = numbers(n)

    def send(source, target, first, peer_index, slot_index, axis, peer):
        return remote(
            source,
            target,
            send_sem.at[first + peer_index],
            recv_sem.at[first + slot_index],
            axis,
            peer,
        )

    half_rows = 2 * planes * highs * sums_z.shape[1]
    x_rows = half_rows // highs
    y_rows = x_rows // 2
    z_rows = y_rows // planes
    x_row = pl.multiple_of(my_high * x_rows, x_rows)
    y_row = pl.multiple_of(x_row + my_side * y_rows, y_rows)

    def part(row, count):
        return sums_mine.at[pl.ds(pl.multiple_of(row, count), count)]

    def reduce_core():
        return send(
            sums_in.at[1 - my_core], sums_core, core_slot, 0, 0, "batch", my_batch + 1 - 2 * my_core
        )

    def reduce_x(peer, slot):
        return send(
            part(peer * x_rows, x_rows),
            sums_x.at[slot],
            x_slot,
            peer,
            slot,
            "batch",
            2 * peer + my_core,
        )

    def reduce_y():
        return send(
            part(x_row + (1 - my_side) * y_rows, y_rows), sums_side, y_slot, 0, 0, "seq", beside
        )

    def reduce_z(peer, slot):
        return send(
            part(y_row + peer * z_rows, z_rows),
            sums_z.at[slot],
            z_slot,
            peer,
            slot,
            "seq",
            2 * peer + my_side,
        )

    def gather_z(peer, slot):
        piece = full.at[my_core, my_high, my_side, slot]
        return send(piece, piece, z_slot + planes, peer, slot, "seq", 2 * peer + my_side)

    def gather_y(side):
        piece = full.at[my_core, my_high, side]
        return send(piece, piece, y_slot + 1, 0, 0, "seq", beside)

    def gather_x(peer, slot):
        piece = full.at[my_core, slot]
        return send(piece, piece, x_slot + highs, peer, slot, "batch", 2 * peer + my_core)

    def gather_core(core):
        piece = full.at[core]
        return send(piece, piece, core_slot + 1, 0, 0, "batch", my_batch + 1 - 2 * my_core)

    def mem_across():
        return send(
            mem_part.at[:, 1 - my_side], mem_side, y_slot + 2, 0, 0, "seq", beside
        )

    def mem_hop(target, toward, peer=None):
        buffer, slot = (mem_up, up_slot) if toward > 0 else (mem_down, down_slot)
        return send(
            mem_part.at[target, my_side],
            buffer.at[target],
            slot,
            target,
            target,
            "seq",
            me + 2 * toward if peer is None else peer,
        )

    def mem_from(target, toward):
        return mem_hop(target, toward, me - 2 * toward)

    def mem_pass(toward):
        buffer = mem_up if toward > 0 else mem_down
        first = 0 if toward > 0 else planes - 1
        for target in range(planes):

            @pl.when((target - my_plane) * toward > 0)
            def _():
                @pl.when(my_plane != first)
                def _():
                    mem_from(target, toward).wait_recv()
                    mem_part[target, my_side] = (
                        mem_part[target, my_side].astype(f32) + buffer[target].astype(f32)
                    ).astype(low)

                mem_hop(target, toward).start()

    def mem_stage(at):
        pl.when(my_plane == at)(lambda: mem_pass(1))
        pl.when(my_plane == planes - 1 - at)(lambda: mem_pass(-1))

    def mem_end():
        value = mem_part[my_plane, my_side].astype(f32)
        mgrad_ref[...] = value.astype(low)

        @pl.when(my_plane > 0)
        def _():
            mem_from(my_plane, 1).wait_recv()
            mgrad_ref[...] = (mgrad_ref[...].astype(f32) + mem_up[my_plane].astype(f32)).astype(low)

        @pl.when(my_plane < planes - 1)
        def _():
            mem_from(my_plane, -1).wait_recv()
            mgrad_ref[...] = (
                mgrad_ref[...].astype(f32) + mem_down[my_plane].astype(f32)
            ).astype(low)

    def mem_drain():
        for target in range(planes):

            @pl.when(target > my_plane)
            def _():
                mem_hop(target, 1).wait_send()

            @pl.when(target < my_plane)
            def _():
                mem_hop(target, -1).wait_send()

    def vec_a(peer, slot):
        return send(vecs_in, vec_all.at[slot], va_slot, peer, slot, "batch", peer)

    def vec_b(side):
        return send(vec_sum, vec_y.at[side], vb_slot, 0, 0, "seq", beside)

    def vec_c(peer, slot):
        return send(vec_both, vec_z.at[slot], vc_slot, peer, slot, "seq", 2 * peer + my_side)

    def pre_a(peer, slot):
        return send(pre_ref, pre_all.at[slot], pa_slot, peer, slot, "batch", peer)

    def pre_b(peer, slot):
        return send(pre_sum, pre_recv.at[slot], pb_slot, peer, slot, "seq", peer)

    def do_copy(head, peer, slot):
        return remote(
            do_in.at[peer, head],
            do_recv.at[head, slot],
            do_send_sem.at[head, peer],
            do_recv_sem.at[head, slot],
            "seq",
            peer,
        )

    def q_copy(head, peer, slot):
        return remote(
            g_send.at[peer, head, 0],
            g_recv.at[0, slot, head],
            g_send_sem.at[0, head, peer],
            g_recv_sem.at[0, head, slot],
            "seq",
            peer,
        )

    def kv_copy(head, peer, slot):
        return remote(
            g_send.at[peer, head, pl.ds(1, 2)],
            g_recv.at[pl.ds(1, 2), slot, head],
            g_send_sem.at[1, head, peer],
            g_recv_sem.at[1, head, slot],
            "seq",
            peer,
        )

    def far_first(body):
        for index in range(n):
            peer = jnp.where(my_plane < planes // 2, n - 1 - index, index)

            @pl.when(peer != me)
            def _():
                body(peer)

    def added(ref, size):
        value = ref[0].astype(f32)
        for other in range(1, size):
            value = value + ref[other].astype(f32)
        return value

    loads = [
        pltpu.make_async_copy(source, target, in_sem.at[index])
        for index, (source, target) in enumerate(
            (
                (raw_in, raw),
                (kx_in, kx),
                (pk_in, pk),
                (pv_in, pv),
                (pkt_in, pkt),
                (qx_in, qx),
                (ot_in, ot),
                (lse_in, stat),
                (sums_in.at[my_core], sums_mine),
                (vecs_in, vec_all.at[my_batch]),
                (mkey_in, mkey),
                (mvalue_in, mvalue),
                (wck_in, wck),
                (wcv_in, wcv),
                (base_in, base_ref),
                (wq_in, weights.at[0]),
                (wk_in, weights.at[1]),
                (wv_in, weights.at[2]),
            )
        )
    ]
    own_do = pltpu.make_async_copy(do_in.at[me], do_recv.at[:, me], in_sem.at[len(loads)])
    own_do.start()
    for load in loads:
        load.start()
    enter({"seq": n, "batch": batches})
    far_first(lambda peer: do_copy(0, peer, me).start())
    reduce_core().start()
    others(batches, my_batch, lambda peer: vec_a(peer, my_batch).start())
    dkv[...] = jnp.zeros_like(dkv)
    product[...] = jnp.zeros_like(product)
    pre_ref[...] = jnp.zeros_like(pre_ref)
    for load in loads[:14]:
        load.wait()
    own_do.wait()

    def turn(index, carry):
        head = index // n
        chunk = lax.rem(index, n)
        here = rows_of(chunk, length)
        kt[head, :, here] = raw[head, chunk, 1]
        values[head, here, :] = raw[head, chunk, 2].astype(f32).T.astype(low)
        return carry

    lax.fori_loop(0, heads * n, turn, 0)

    def memory_back(index, carry):
        here = rows_of(index, step_rows)
        value = dot_nt(mkey[...], wck[here, :]) + dot_nt(mvalue[...], wcv[here, :])
        mem_part[:, :, :, here] = value.astype(low).reshape(mem_part.shape[:3] + (step_rows,))
        return carry

    lax.fori_loop(0, width // step_rows, memory_back, 0)
    mem_across().start()

    def next_head(head):
        def move(peer):
            do_copy(head, peer, me).wait_send()
            do_copy(head + 1, peer, me).start()

        far_first(move)

    def arrive(head, which):
        for part in range(2):
            chunk = 2 * which + part

            @pl.when(chunk != me)
            def _():
                do_copy(head, chunk, chunk).wait_recv()

            grads = do_recv[head, chunk]
            dot[head, :, rows_of(chunk, length)] = grads
            grads = grads.astype(f32)
            query = raw[head, chunk, 0].astype(f32) * 0.125
            qdo[head, rows_of(chunk, length), :] = (
                jnp.concatenate([query, grads], axis=0).T.astype(low)
            )
            here = slice(part * length, (part + 1) * length)
            stat[which, head, 1:2, here] = jnp.sum(
                grads * ot[which, head, :HD, here], axis=0, keepdims=True
            )
        here = rows_of(which, plane)
        weight = jnp.exp(dot_nn(pk[head], qx[head, :, here]) - stat[which, head, 0:1, :])
        slope = weight * (dot_nn(pv[head], dot[head, :, here]) - stat[which, head, 1:2, :])
        both = jnp.concatenate([slope, weight], axis=0).astype(low)
        sums = dot_nn(both, qdo[head, here, :])
        pre_ref[head] += jnp.where(
            head_lanes((PREFIX_ROWS, 2 * HD), 0), sums[:PREFIX_ROWS], sums[PREFIX_ROWS:]
        )
        slope = slope.astype(low)
        dqt[which, head] = dot_nn(pkt[head], slope)

    def plus(first, second):
        return (first.astype(f32) + second.astype(f32)).astype(low)

    def sum_one():
        reduce_core().wait_recv()
        sums_mine[...] = plus(sums_mine[...], sums_core[...])
        others(highs, my_high, lambda peer: reduce_x(peer, my_high).start())

    def sum_two():
        here = pl.ds(x_row, x_rows)
        others(highs, my_high, lambda peer: reduce_x(peer, peer).wait_recv())
        sums_x[my_high] = sums_mine[here]
        sums_mine[here] = added(sums_x, highs).astype(low)
        reduce_y().start()

    def sum_three():
        here = pl.ds(y_row, y_rows)
        reduce_y().wait_recv()
        sums_mine[here] = plus(sums_mine[here], sums_side[...])
        others(planes, my_plane, lambda peer: reduce_z(peer, my_plane).start())

    def sum_four():
        here = pl.ds(pl.multiple_of(y_row + my_plane * z_rows, z_rows), z_rows)
        others(planes, my_plane, lambda peer: reduce_z(peer, peer).wait_recv())
        sums_z[my_plane] = sums_mine[here]
        full[my_core, my_high, my_side, my_plane] = added(sums_z, planes).astype(low)
        others(planes, my_plane, lambda peer: gather_z(peer, my_plane).start())

    def sum_five():
        others(planes, my_plane, lambda peer: gather_z(peer, peer).wait_recv())
        gather_y(my_side).start()

    def sum_six():
        gather_y(1 - my_side).wait_recv()
        others(highs, my_high, lambda peer: gather_x(peer, my_high).start())

    def sum_seven():
        others(highs, my_high, lambda peer: gather_x(peer, peer).wait_recv())
        gather_core(my_core).start()

    def sum_end():
        gather_core(1 - my_core).wait_recv()
        save_full.start()

    def vec_one():
        others(batches, my_batch, lambda peer: vec_a(peer, peer).wait_recv())
        vec_sum[...] = added(vec_all, batches)
        vec_b(my_side).start()
        vec_y[my_side] = vec_sum[...]

    def vec_two():
        vec_b(1 - my_side).wait_recv()
        value = (vec_y[0] + vec_y[1]).astype(f32)
        vec_both[...] = jnp.concatenate(
            [value[:, : width // 2], value[:, width // 2 :]], axis=0
        ).astype(low)
        others(planes, my_plane, lambda peer: vec_c(peer, my_plane).start())
        vec_z[my_plane] = vec_both[...]

    def vec_end():
        others(planes, my_plane, lambda peer: vec_c(peer, peer).wait_recv())
        value = added(vec_z, planes)
        vecs_ref[:, : width // 2] = value[:8]
        vecs_ref[:, width // 2 :] = value[8:]

    def mem_one():
        mem_across().wait_recv()
        mem_part[:, my_side] = plus(mem_part[:, my_side], mem_side[...])

    def stage_pa():
        others(batches, my_batch, lambda peer: pre_a(peer, my_batch).start())
        pre_all[my_batch] = pre_ref[...]

    def stage_pb():
        others(batches, my_batch, lambda peer: pre_a(peer, peer).wait_recv())
        pre_sum[...] = added(pre_all, batches).astype(low)
        others(n, me, lambda peer: pre_b(peer, me).start())
        pre_recv[me] = pre_sum[...]

    save_full = pltpu.make_async_copy(full, full_out, in_sem.at[0])

    def pair_part(head, upper, lower, first, count, diagonal):
        keys = span_of(lower * plane + first, count)
        here = span_of(upper * plane + first, plane - first)
        at = slice(first, plane)
        scores = dot_nn(kx[head, keys, :], qx[head, :, here])
        slope = dot_nn(values[head, keys, :], dot[head, :, here]) - stat[upper, head, 1:2, at]
        weight = jnp.exp(scores - stat[upper, head, 0:1, at])
        if diagonal:
            key_at = lax.broadcasted_iota(jnp.int32, scores.shape, 0)
            query_at = lax.broadcasted_iota(jnp.int32, scores.shape, 1)
            weight = jnp.where(key_at <= query_at, weight, 0.0)
        both = jnp.concatenate([(weight * slope).astype(low), weight.astype(low)], axis=0)
        sums = dot_nn(both, qdo[head, here, :])
        dkv[head, keys, :] += jnp.where(
            head_lanes((count, 2 * HD), 0), sums[:count], sums[count:]
        )
        dqt[upper, head, :, at] += dot_nn(kt[head, :, keys], both[:count])

    def pair(head, upper, lower, diagonal):
        if diagonal:
            pair_part(head, upper, lower, 0, length, True)
            pair_part(head, upper, lower, length, length, True)
        else:
            pair_part(head, upper, lower, 0, plane, False)

    def hand_queries(head, which):
        for part in range(2):
            chunk = 2 * which + part
            g_send[chunk, head, 0] = (
                dqt[which, head, :, part * length : (part + 1) * length] * 0.125
            ).astype(low)

            @pl.when(chunk != me)
            def _():
                q_copy(head, chunk, me).start()

            @pl.when(chunk == me)
            def _():
                g_recv[0, me, head] = g_send[chunk, head, 0]

    def hand_keys(head, which):
        for part in range(2):
            chunk = 2 * which + part
            turned = dkv[head, rows_of(chunk, length), :].T.astype(low)
            g_send[chunk, head, 1] = turned[:HD]
            g_send[chunk, head, 2] = turned[HD:]

            @pl.when(chunk != me)
            def _():
                kv_copy(head, chunk, me).start()

            @pl.when(chunk == me)
            def _():
                g_recv[pl.ds(1, 2), me, head] = g_send[chunk, head, pl.ds(1, 2)]

    rising = my_plane >= planes // 2
    total = heads * planes * (planes + 1) // 2
    hooks = [
        (2, sum_one),
        (3, mem_one),
        (4, lambda: mem_stage(0)),
        (5, vec_one),
        (5, sum_two),
        (7, sum_three),
        (8, vec_two),
        (10, sum_four),
        (12, sum_five),
        (14, sum_six),
        (16, vec_end),
        (17, sum_seven),
    ] + [(4 + 3 * at, functools.partial(mem_stage, at)) for at in range(1, planes - 1)]
    hooks += [
        (1 + head * total // heads, functools.partial(next_head, head)) for head in range(heads - 1)
    ]
    final = total - planes * (planes + 1) // 2
    hooks += [(final + planes + 1, stage_pa), (final + 2 * planes - 1, stage_pb)]

    def hook(pairs):
        for number, body in sorted(hooks, key=lambda item: item[0]):
            pl.when(pairs == number)(body)


    def stage(index, carry):
        head = index // planes
        step = lax.rem(index, planes)
        here = jnp.where(rising, step, planes - 1 - step)

        @pl.when((step == 0) | ((step == 1) & jnp.logical_not(rising)))
        def _():
            @pl.when(rising | (step == 0))
            def _():
                arrive(head, here)

            @pl.when(jnp.logical_not(rising) & (step == 1))
            def _():
                def rest(which, inner):
                    arrive(head, planes - 2 - which)
                    return inner

                lax.fori_loop(0, planes - 1, rest, 0)

        begun = head * (planes * (planes + 1) // 2) + step * planes - step * (step - 1) // 2
        hook(begun)
        pair(head, here, here, True)

        @pl.when(rising)
        def _():
            hand_queries(head, here)

        @pl.when(jnp.logical_not(rising))
        def _():
            hand_keys(head, here)

        def far(at, inner):
            there = jnp.where(rising, here + 1 + at, here - 1 - at)

            @pl.when(rising & (step == 0))
            def _():
                arrive(head, there)

            hook(begun + 1 + at)
            pair(head, jnp.maximum(here, there), jnp.minimum(here, there), False)
            return inner

        lax.fori_loop(0, planes - 1 - step, far, 0)

        @pl.when(rising)
        def _():
            hand_keys(head, here)

        @pl.when(jnp.logical_not(rising))
        def _():
            hand_queries(head, here)

        return carry

    lax.fori_loop(0, heads * planes, stage, 0)
    mem_end()
    for load in loads[14:]:
        load.wait()

    def gathered(peer):
        for head in range(heads):
            q_copy(head, peer, peer).wait_recv()
            kv_copy(head, peer, peer).wait_recv()

    half = width // 2

    def gather_plane(step, carry):
        which = lax.rem(my_plane + step, planes)
        for part in range(2):
            peer = 2 * which + part

            @pl.when(peer != me)
            def _():
                gathered(peer)

        columns = rows_of(which, 2 * group)
        for part in range(2):
            here = slice(part * half, (part + 1) * half)
            value = product[here, :]
            for kind in range(3):
                grads = g_recv[kind, pl.ds(2 * which, 2)].reshape(2 * group, length)
                value = value + dot_nn(weights[kind, here, columns], grads)
            product[here, :] = value
        return carry

    lax.fori_loop(0, planes, gather_plane, 0)
    sum_end()
    tile = 256
    for index in range(width // tile):
        here = slice(index * tile, (index + 1) * tile)
        tg_ref[:, here] = (base_ref[:, here] + product[here, :].T).astype(low)
    for other in range(n):

        @pl.when(other != me)
        def _():
            pre_b(other, other).wait_recv()

        value = pre_recv[other].astype(f32)
        for which in range(2):
            pkv_ref[:, which * width + other * group : which * width + (other + 1) * group] = (
                jnp.concatenate(
                    [value[head, :, which * HD : (which + 1) * HD] for head in range(heads)], axis=1
                )
            )

    def drain(peer):
        do_copy(heads - 1, peer, me).wait_send()
        pre_b(peer, me).wait_send()
        for head in range(heads):
            q_copy(head, peer, me).wait_send()
            kv_copy(head, peer, me).wait_send()

    others(n, me, drain)
    others(batches, my_batch, lambda peer: pre_a(peer, my_batch).wait_send())
    others(batches, my_batch, lambda peer: vec_a(peer, my_batch).wait_send())
    reduce_core().wait_send()
    others(highs, my_high, lambda peer: reduce_x(peer, my_high).wait_send())
    reduce_y().wait_send()
    others(planes, my_plane, lambda peer: reduce_z(peer, my_plane).wait_send())
    others(planes, my_plane, lambda peer: gather_z(peer, my_plane).wait_send())
    gather_y(my_side).wait_send()
    others(highs, my_high, lambda peer: gather_x(peer, my_high).wait_send())
    gather_core(my_core).wait_send()
    mem_across().wait_send()
    mem_drain()
    others(planes, my_plane, lambda peer: vec_c(peer, my_plane).wait_send())
    vec_b(my_side).wait_send()
    save_full.wait()


def self_backward(
    n, batches, first_grad, out_grad, sums, mem_grads, mem_weights, vecs, saved, weights
):
    length, width = first_grad.shape
    group = width // n
    heads = group // HD
    whole = n * length
    planes = n // 2
    low = jnp.bfloat16
    f32 = jnp.float32
    vmem = pl.BlockSpec(memory_space=pltpu.VMEM)
    anywhere = pl.BlockSpec(memory_space=pl.ANY)
    dma = pltpu.SemaphoreType.DMA
    sum_rows = sums.shape[0] // (n * batches)
    mem_len = mem_grads[0].shape[0]
    mem_rows = mem_len // n
    mem_part = pltpu.VMEM((planes, mem_rows, width), low)
    mem_low = pltpu.VMEM((mem_len, width), low)
    square = pltpu.VMEM((width, width), low)
    vec = pltpu.VMEM((8, width), f32)
    copies = 6 + 2 * (batches // 2) + 5 * planes + 2 * batches + n
    qx, kx, raw, pk, pv, pkt, ot, stat = (pltpu.VMEM(value.shape, value.dtype) for value in saved)
    return pl.pallas_call(
        functools.partial(self_backward_kernel, n, batches),
        out_shape=(
            jax.ShapeDtypeStruct((length, width), low),
            jax.ShapeDtypeStruct((mem_rows, width), low),
            jax.ShapeDtypeStruct((PREFIX_ROWS, 2 * width), f32),
            jax.ShapeDtypeStruct((8, width), f32),
            jax.ShapeDtypeStruct((2, batches // 2, 2, planes, sum_rows, LANES), low),
        ),
        in_specs=[anywhere] * 19,
        out_specs=(vmem, vmem, vmem, vmem, anywhere),
        scratch_shapes=[
            pltpu.VMEM((heads, n, HD, length), low),
            qx,
            kx,
            raw,
            pltpu.VMEM((heads, HD, whole), low),
            pltpu.VMEM((heads, whole, HD), low),
            pltpu.VMEM((heads, HD, whole), low),
            pltpu.VMEM((heads, whole, 2 * HD), low),
            pk,
            pv,
            pkt,
            ot,
            stat,
            pltpu.VMEM((3, width, width), low),
            pltpu.VMEM((planes, heads, HD, 2 * length), f32),
            pltpu.VMEM((heads, whole, 2 * HD), f32),
            pltpu.VMEM((n, heads, 3, HD, length), low),
            pltpu.VMEM((3, n, heads, HD, length), low),
            pltpu.VMEM((heads, PREFIX_ROWS, 2 * HD), f32),
            pltpu.VMEM((batches, heads, PREFIX_ROWS, 2 * HD), f32),
            pltpu.VMEM((heads, PREFIX_ROWS, 2 * HD), low),
            pltpu.VMEM((n, heads, PREFIX_ROWS, 2 * HD), low),
            pltpu.VMEM((sums.shape[0] // 2, LANES), low),
            pltpu.VMEM((sums.shape[0] // 2, LANES), low),
            pltpu.VMEM((batches // 2, sums.shape[0] // batches, LANES), low),
            pltpu.VMEM((planes * sum_rows, LANES), low),
            pltpu.VMEM((planes, sum_rows, LANES), low),
            pltpu.VMEM((2, batches // 2, 2, planes, sum_rows, LANES), low),
            mem_low,
            mem_low,
            square,
            square,
            pltpu.VMEM((planes, 2, mem_rows, width), low),
            mem_part,
            mem_part,
            mem_part,
            pltpu.VMEM((batches, 8, width), f32),
            vec,
            pltpu.VMEM((2, 8, width), f32),
            pltpu.VMEM((16, width // 2), low),
            pltpu.VMEM((planes, 16, width // 2), low),
            pltpu.VMEM((width, length), f32),
            pltpu.VMEM((length, width), f32),
            dma((heads, n)),
            dma((heads, n)),
            dma((2, heads, n)),
            dma((2, heads, n)),
            dma((19,)),
            dma((copies,)),
            dma((copies,)),
        ],
        compiler_params=pltpu.CompilerParams(
            collective_id=1, has_side_effects=True, vmem_limit_bytes=VMEM_BYTES
        ),
        name="self_backward",
    )(
        first_grad,
        out_grad,
        sums.reshape(2, -1, LANES),
        *mem_grads,
        *mem_weights,
        vecs,
        *saved,
        *weights,
    )


def both_parts(value):
    high = value.astype(jnp.bfloat16).astype(jnp.float32)
    return jnp.concatenate([high, value - high], axis=0).astype(jnp.bfloat16)


def finish_kernel(
    full_in,
    vecs_ref,
    pkv_ref,
    emb_ref,
    first_in,
    fbias_ref,
    second_in,
    token_in,
    mem_in,
    embed_out,
    first_out,
    fbias_out,
    second_out,
    sbias_out,
    down_out,
    dbias_out,
    raise_out,
    rbias_out,
    gain_out,
    shift_out,
    token_out,
    mem_out,
    full_ref,
    first_ref,
    second_ref,
    token_ref,
    mem_ref,
    first_grad,
    second_grad,
    down_grad,
    raise_grad,
    emb,
    hidden,
    out_sem,
    in_sem,
):
    f32 = jnp.float32
    low = jnp.bfloat16
    width = emb_ref.shape[1]
    down = dbias_out.shape[1]
    count = emb_ref.shape[0]
    first = down * width // LANES
    loads = [
        pltpu.make_async_copy(source, target, in_sem.at[index])
        for index, (source, target) in enumerate(
            (
                (full_in.at[first:], full_ref.at[first:]),
                (full_in.at[:first], full_ref.at[:first]),
                (first_in, first_ref),
                (second_in, second_ref),
                (token_in, token_ref),
                (mem_in, mem_ref),
            )
        )
    ]
    for load in loads:
        load.start()
    saves = []

    def save(source, target, rows=None):
        if rows is not None:
            source, target = source.at[rows], target.at[rows]
        copy = pltpu.make_async_copy(source, target, out_sem.at[len(saves)])
        copy.start()
        saves.append(copy)

    loads[0].wait()
    for index in range(width // LANES):
        raise_grad[:, index * LANES : (index + 1) * LANES] = full_ref[
            first + index * down : first + (index + 1) * down, :
        ].astype(f32)
    save(raise_grad, raise_out)
    loads[1].wait()
    for index in range(down // LANES):
        down_grad[:, index * LANES : (index + 1) * LANES] = full_ref[
            index * width : (index + 1) * width, :
        ].astype(f32)
    save(down_grad, down_out)
    for load in loads[4:]:
        load.wait()
    save(token_ref, token_out)
    save(mem_ref, mem_out)
    loads[2].wait()
    emb[...] = jnp.zeros_like(emb)
    emb[:count, :] = emb_ref[...].astype(f32)
    emb_low = emb[...].astype(low)
    row = lax.broadcasted_iota(jnp.int32, hidden.shape, 0)
    hidden[...] = jnp.where(
        row < count, jnp.tanh(dot_nn(emb_low, first_ref[...]) + fbias_ref[...]), 0.0
    )
    value = hidden[...]
    prefix = pkv_ref[...]
    parts = both_parts(prefix)
    hidden_twice = jnp.concatenate([value, value], axis=0).T.astype(low)
    tile = 128
    for index in range(second_grad.shape[0] // tile):
        here = slice(index * tile, (index + 1) * tile)
        second_grad[here, :] = dot_nn(hidden_twice[here, :], parts)
        save(second_grad, second_out, here)
    sbias_out[...] = jnp.sum(prefix, axis=0, keepdims=True)
    loads[3].wait()
    grad = dot_nt(parts, second_ref[...])
    grad = (grad[:PREFIX_ROWS] + grad[PREFIX_ROWS:]) * (1.0 - value * value)
    fbias_out[...] = jnp.sum(grad, axis=0, keepdims=True)
    parts = both_parts(grad)
    emb_twice = jnp.concatenate([emb[...], emb[...]], axis=0).T.astype(low)
    first_grad[...] = dot_nn(emb_twice, parts)
    save(first_grad, first_out)
    back = dot_nt(parts, first_ref[...])
    embed_out[...] = (back[:PREFIX_ROWS] + back[PREFIX_ROWS:])[:count, :]
    rbias_out[...] = vecs_ref[0:1, :]
    dbias_out[...] = vecs_ref[1:2, :down]
    gain_out[...] = vecs_ref[2:5, :]
    shift_out[...] = vecs_ref[5:8, :]
    for copy in saves:
        copy.wait()


def finish(full, vecs, prefix_grad, embed, first, first_bias, second, down, token_grad, memory_grad):
    f32 = jnp.float32
    count, width = embed.shape
    hidden = first.shape[1]
    vmem = pl.BlockSpec(memory_space=pltpu.VMEM)
    anywhere = pl.BlockSpec(memory_space=pl.ANY)
    shapes = (
        (count, width),
        (width, hidden),
        (1, hidden),
        (hidden, 2 * width),
        (1, 2 * width),
        (width, down),
        (1, down),
        (down, width),
        (1, width),
        (3, width),
        (3, width),
    )
    return pl.pallas_call(
        finish_kernel,
        out_shape=tuple(jax.ShapeDtypeStruct(shape, f32) for shape in shapes)
        + tuple(
            jax.ShapeDtypeStruct(value.shape, value.dtype) for value in (token_grad, memory_grad)
        ),
        in_specs=[anywhere, vmem, vmem, vmem, anywhere, vmem, anywhere, anywhere, anywhere],
        out_specs=(
            vmem,
            anywhere,
            vmem,
            anywhere,
            vmem,
            anywhere,
            vmem,
            anywhere,
            vmem,
            vmem,
            vmem,
            anywhere,
            anywhere,
        ),
        scratch_shapes=[
            pltpu.VMEM(full.shape, jnp.bfloat16),
            pltpu.VMEM(first.shape, jnp.bfloat16),
            pltpu.VMEM(second.shape, jnp.bfloat16),
            pltpu.VMEM(token_grad.shape, token_grad.dtype),
            pltpu.VMEM(memory_grad.shape, memory_grad.dtype),
            pltpu.VMEM((width, hidden), f32),
            pltpu.VMEM((hidden, 2 * width), f32),
            pltpu.VMEM((width, down), f32),
            pltpu.VMEM((down, width), f32),
            pltpu.VMEM((PREFIX_ROWS, width), f32),
            pltpu.VMEM((PREFIX_ROWS, hidden), f32),
            pltpu.SemaphoreType.DMA((5 + hidden // 128,)),
            pltpu.SemaphoreType.DMA((6,)),
        ],
        compiler_params=pltpu.CompilerParams(vmem_limit_bytes=VMEM_BYTES),
        name="finish",
    )(full, vecs, prefix_grad, embed, first, first_bias, second, token_grad, memory_grad)


def gelu_pair(value):
    size = jnp.abs(value)
    step = 1.0 / (1.0 + (0.3275911 * 0.7071067811865476) * size)
    bell = jnp.exp(-0.5 * value * value)
    poly = step * (
        0.127414796
        + step
        * (-0.142248368 + step * (0.7107068705 + step * (-0.7265760135 + step * 0.5307027145)))
    )
    act = jnp.maximum(value, 0.0) - size * (poly * bell)
    turn = bell * (0.3989422804014327 * size - poly)
    return act, jnp.where(value >= 0.0, 1.0 + turn, -turn)


def normed(value):
    center = jnp.mean(value, axis=-1, keepdims=True)
    centered = value - center
    scale = lax.rsqrt(jnp.mean(centered * centered, axis=-1, keepdims=True) + norm_eps)
    return centered * scale, scale


def norm_back(grad, scale, unit):
    return scale * (
        grad
        - jnp.mean(grad, axis=-1, keepdims=True)
        - unit * jnp.mean(grad * unit, axis=-1, keepdims=True)
    )


def middle_kernel(
    tok_in,
    att_in,
    cot_in,
    mkey_in,
    mvalue_in,
    gain_ref,
    shift_ref,
    dbias_ref,
    rbias_ref,
    wo_in,
    wcq_in,
    wco_in,
    wd_in,
    wr_in,
    win_in,
    wout_in,
    layer_out,
    fgrad_out,
    ograd_out,
    mkey_out,
    mvalue_out,
    sums_out,
    vecs_ref,
    tok_ref,
    att_ref,
    cot_ref,
    mkey_ref,
    mvalue_ref,
    out_ref,
    fgrad_ref,
    ograd_ref,
    sums_ref,
    wo,
    wcq,
    wco,
    wd,
    wr,
    win,
    wout,
    unit_one,
    unit_two,
    work,
    total,
    scale_one,
    scale_two,
    low_one,
    low_two,
    low_three,
    query,
    crossed,
    weights,
    slopes,
    acts,
    down_act,
    down_slope,
    down_grad,
    load_sem,
    win_sem,
    wout_sem,
    out_sem,
):
    length, width = tok_ref.shape
    resident = len(win.shape) == 2
    tile = 512 if resident else win.shape[2]
    tiles = win_in.shape[1] // tile
    slots = tiles if resident else win.shape[0]
    rows_step = 128
    low = jnp.bfloat16
    f32 = jnp.float32

    sources = (
        att_in,
        wo_in,
        tok_in,
        wcq_in,
        mkey_in,
        mvalue_in,
        wco_in,
        wd_in,
        wr_in,
        cot_in,
    )
    targets = (att_ref, wo, tok_ref, wcq, mkey_ref, mvalue_ref, wco, wd, wr, cot_ref)
    loads = [
        pltpu.make_async_copy(source, target, load_sem.at[index])
        for index, (source, target) in enumerate(zip(sources, targets))
    ]

    def win_load(which):
        slot = which % slots
        target = win.at[:, rows_of(which, tile)] if resident else win.at[slot]
        return pltpu.make_async_copy(win_in.at[:, rows_of(which, tile)], target, win_sem.at[slot])

    def wout_load(which):
        slot = which % slots
        target = wout.at[rows_of(which, tile), :] if resident else wout.at[slot]
        return pltpu.make_async_copy(wout_in.at[rows_of(which, tile), :], target, wout_sem.at[slot])

    for load in loads[:7]:
        load.start()

    def by_columns(extent, step, body):
        def one(index, carry):
            body(pl.ds(pl.multiple_of(index * step, step), step))
            return carry

        lax.fori_loop(0, extent // step, one, 0)

    def by_rows(body, init=0):
        def one(index, carry):
            return body(rows_of(index, rows_step), carry)

        return lax.fori_loop(0, length // rows_step, one, init)

    cols = 512
    half = width // 2

    for load in loads[:3]:
        load.wait()
    for load in loads[7:]:
        load.start()
    for which in range(slots):
        win_load(which).start()
    for which in range(slots):
        wout_load(which).start()

    def project_out(here):
        work[:, here] = tok_ref[:, here].astype(f32) + dot_nn(att_ref[...], wo[:, here])

    by_columns(width, cols, project_out)

    def first_norm(here, carry):
        unit, scale = normed(work[here, :])
        unit_one[here, :] = unit
        scale_one[here, :] = scale
        value = unit * gain_ref[0:1, :] + shift_ref[0:1, :]
        work[here, :] = value
        low_one[here, :] = value.astype(low)
        return carry

    by_rows(first_norm)

    loads[3].wait()

    def project_query(here):
        query[:, here] = dot_nn(low_one[...], wcq[:, here]).astype(low)

    by_columns(width, cols, project_query)
    per_block = LANES // HD

    def stacked(value):
        return jnp.concatenate(
            [jnp.where(head_lanes(value.shape, head), value, 0.0) for head in range(per_block)],
            axis=0,
        ).astype(low)

    def unstacked(value):
        return jnp.concatenate(
            [
                value[head * HD : (head + 1) * HD, head * length : (head + 1) * length]
                for head in range(per_block)
            ],
            axis=0,
        )

    def block_queries(here):
        return stacked(query[:, here].astype(f32) * 0.125)

    def cross_forward(block):
        here = rows_of(block, LANES)
        scores = dot_nt(mkey_ref[:, here], block_queries(here))
        raised = jnp.exp(scores - jnp.max(scores, axis=0, keepdims=True))
        share = 1.0 / jnp.sum(raised, axis=0, keepdims=True)
        weight = (raised * share).astype(low)
        weights[block] = weight
        values = mvalue_ref[:, here].astype(f32).T.astype(low)
        crossed[:, here] = unstacked(dot_nn(values, weight)).T.astype(low)

    loads[4].wait()
    loads[5].wait()

    def cross_forward_both(step, carry):
        cross_forward(2 * step)
        cross_forward(2 * step + 1)
        return carry

    lax.fori_loop(0, width // LANES // 2, cross_forward_both, 0)

    loads[6].wait()

    def project_crossed(here):
        work[:, here] += dot_nn(crossed[...], wco[:, here])

    by_columns(width, cols, project_crossed)

    def second_norm(here, carry):
        unit, scale = normed(work[here, :])
        unit_two[here, :] = unit
        scale_two[here, :] = scale
        value = unit * gain_ref[1:2, :] + shift_ref[1:2, :]
        work[here, :] = value
        low_two[here, :] = value.astype(low)
        return carry

    by_rows(second_norm)

    step_cols = 512

    def feed_part(here, source):
        act, slope = gelu_pair(dot_nn(low_two[...], source))
        slopes[:, here] = slope.astype(low)
        return act.astype(low)

    if resident:

        def feed_forward(which, carry):
            here = rows_of(which, step_cols)

            @pl.when(which % (tile // step_cols) == 0)
            def _():
                win_load(which // (tile // step_cols)).wait()

            acts[:, here] = feed_part(here, win[:, here])
            return carry

        lax.fori_loop(0, tiles * tile // step_cols, feed_forward, 0)
        for which in range(tiles):
            wout_load(which).wait()

        def feed_out_part(here):
            total[:, here] = dot_nn(acts[...], wout[:, here])

        by_columns(width, step_cols, feed_out_part)
    else:
        total[...] = jnp.zeros_like(total)

        def feed_forward(which, carry):
            slot = lax.rem(which, slots)
            win_load(which).wait()
            wout_load(which).wait()
            total[...] += dot_nn(feed_part(rows_of(which, tile), win[slot]), wout[slot])

            @pl.when(which + slots < tiles)
            def _():
                win_load(which + slots).start()
                wout_load(which + slots).start()

            return carry

        lax.fori_loop(0, tiles, feed_forward, 0)

    loads[7].wait()
    loads[8].wait()
    loads[9].wait()
    act, slope = gelu_pair(dot_nn(low_two[...], wd[...]) + dbias_ref[...])
    down_act[...] = act.astype(low)
    down_slope[...] = slope.astype(low)

    def project_raise(here):
        work[:, here] += total[:, here] + 4.0 * (
            dot_nn(down_act[...], wr[:, here]) + rbias_ref[:, here]
        )

    by_columns(width, cols, project_raise)
    nothing = jnp.zeros((1, width), f32)

    def third_norm(here, carry):
        gain_sum, shift_sum, bias_sum = carry
        unit, scale = normed(work[here, :])
        gain = gain_ref[2:3, :]
        out_ref[here, :] = (unit * gain + shift_ref[2:3, :]).astype(low)
        grad = cot_ref[here, :].astype(f32)
        back = norm_back(grad * gain, scale, unit)
        total[here, :] = back
        back_low = back.astype(low)
        low_three[here, :] = back_low
        return (
            gain_sum + jnp.sum(grad * unit, axis=0, keepdims=True),
            shift_sum + jnp.sum(grad, axis=0, keepdims=True),
            bias_sum + jnp.sum(back_low.astype(f32), axis=0, keepdims=True),
        )

    gain_three, shift_three, bias_sum = by_rows(third_norm, (nothing, nothing, nothing))
    saves = []

    def save(source, target):
        copy = pltpu.make_async_copy(source, target, out_sem.at[len(saves)])
        copy.start()
        saves.append(copy)

    save(out_ref, layer_out)
    vecs_ref[0:1, :] = 4.0 * bias_sum

    back = 4.0 * dot_nt(low_three[...], wr[...]) * down_slope[...].astype(f32)
    back_low = back.astype(low)
    down_grad[...] = back_low
    vecs_ref[1:2, :] = jnp.concatenate(
        [
            jnp.sum(back_low.astype(f32), axis=0, keepdims=True),
            jnp.zeros((1, width - wd.shape[1]), f32),
        ],
        axis=1,
    )
    down = wd.shape[1]
    raise_sum = 4.0 * dot_tn(down_act[...], low_three[...])
    for index in range(width // LANES):
        sums_ref[pl.ds(down * width // LANES + index * down, down), :] = raise_sum[
            :, index * LANES : (index + 1) * LANES
        ].astype(low)
    down_sum = dot_tn(low_two[...], down_grad[...])
    for index in range(down // LANES):
        sums_ref[index * width : (index + 1) * width, :] = down_sum[
            :, index * LANES : (index + 1) * LANES
        ].astype(low)

    save(sums_ref, sums_out)

    if resident:

        def feed_slope(here):
            acts[:, here] = (
                dot_nt(low_three[...], wout[here, :]) * slopes[:, here].astype(f32)
            ).astype(low)

        by_columns(win_in.shape[1], step_cols, feed_slope)

        def feed_in_part(here):
            total[:, here] += dot_nt(acts[...], win[here, :])

        by_columns(width, step_cols, feed_in_part)
    else:

        def feed_backward(step, carry):
            which = tiles - 1 - step
            slot = lax.rem(which, slots)
            here = rows_of(which, tile)

            @pl.when(which < tiles - slots)
            def _():
                wout_load(which).wait()
                win_load(which).wait()

            grad = dot_nt(low_three[...], wout[slot]) * slopes[:, here].astype(f32)
            total[...] += dot_nt(grad.astype(low), win[slot])

            @pl.when(which >= slots)
            def _():
                win_load(which - slots).start()
                wout_load(which - slots).start()

            return carry

        lax.fori_loop(0, tiles, feed_backward, 0)

    def down_back(here):
        total[:, here] += dot_nt(down_grad[...], wd[here, :])

    by_columns(width, cols, down_back)

    def second_back(here, carry):
        gain_sum, shift_sum = carry
        grad = total[here, :]
        unit = unit_two[here, :]
        back = norm_back(grad * gain_ref[1:2, :], scale_two[here, :], unit)
        total[here, :] = back
        low_one[here, :] = back.astype(low)
        return (
            gain_sum + jnp.sum(grad * unit, axis=0, keepdims=True),
            shift_sum + jnp.sum(grad, axis=0, keepdims=True),
        )

    gain_two, shift_two = by_rows(second_back, (nothing, nothing))

    def crossed_back(here):
        crossed[:, here] = dot_nt(low_one[...], wco[here, :]).astype(low)

    by_columns(width, cols, crossed_back)

    def cross_backward(block):
        here = rows_of(block, LANES)
        grads = stacked(crossed[:, here].astype(f32))
        keys = mkey_ref[:, here].astype(f32).T.astype(low)
        slope = dot_nt(mvalue_ref[:, here], grads)
        weight_low = weights[block]
        weight = weight_low.astype(f32)
        slope = weight * (slope - jnp.sum(weight * slope, axis=0, keepdims=True))
        slope = slope.astype(low)
        queries = block_queries(here)
        mkey_ref[:, here] = dot_nn(slope, queries).astype(low)
        mvalue_ref[:, here] = dot_nn(weight_low, grads).astype(low)
        query[:, here] = (unstacked(dot_nn(keys, slope)) * 0.125).T.astype(low)

    def cross_backward_both(step, carry):
        cross_backward(2 * step)
        cross_backward(2 * step + 1)
        return carry

    lax.fori_loop(0, width // LANES // 2, cross_backward_both, 0)
    save(mkey_ref, mkey_out)
    save(mvalue_ref, mvalue_out)

    def query_back(here):
        total[:, here] += dot_nt(query[...], wcq[here, :])

    by_columns(width, cols, query_back)

    def first_back(here, carry):
        gain_sum, shift_sum = carry
        grad = total[here, :]
        unit = unit_one[here, :]
        back = norm_back(grad * gain_ref[0:1, :], scale_one[here, :], unit)
        fgrad_ref[here, :] = back
        low_one[here, :] = back.astype(low)
        return (
            gain_sum + jnp.sum(grad * unit, axis=0, keepdims=True),
            shift_sum + jnp.sum(grad, axis=0, keepdims=True),
        )

    gain_one, shift_one = by_rows(first_back, (nothing, nothing))
    save(fgrad_ref, fgrad_out)

    for index in range(width // cols):
        here = slice(index * cols, (index + 1) * cols)
        ograd_ref[here, :] = dot_nt(low_one[...], wo[here, :]).T.astype(low)
        save(ograd_ref.at[here], ograd_out.at[here])
    for index, vector in enumerate(
        (gain_one, gain_two, gain_three, shift_one, shift_two, shift_three)
    ):
        vecs_ref[2 + index : 3 + index, :] = vector
    for copy in saves:
        copy.wait()


def middle(
    tokens, attended, cotangent, mem_key, mem_value, gains, shifts, down_bias, raise_bias, weights
):
    length, width = tokens.shape
    mem_len = mem_key.shape[0]
    down = weights[3].shape[1]
    feed = weights[5].shape[1]
    tile = 512 if mem_len <= 512 else 128
    resident = mem_len <= 512
    slots = feed // tile if resident else 2
    low = jnp.bfloat16
    f32 = jnp.float32
    vmem = pl.BlockSpec(memory_space=pltpu.VMEM)
    anywhere = pl.BlockSpec(memory_space=pl.ANY)
    square = pltpu.VMEM((width, width), low)
    wide = pltpu.VMEM((length, width), f32)
    narrow = pltpu.VMEM((length, width), low)
    return pl.pallas_call(
        middle_kernel,
        out_shape=(
            jax.ShapeDtypeStruct((length, width), low),
            jax.ShapeDtypeStruct((length, width), f32),
            jax.ShapeDtypeStruct((width, length), low),
            jax.ShapeDtypeStruct((mem_len, width), low),
            jax.ShapeDtypeStruct((mem_len, width), low),
            jax.ShapeDtypeStruct((2 * down * width // LANES, LANES), low),
            jax.ShapeDtypeStruct((8, width), f32),
        ),
        in_specs=[anywhere] * 5 + [vmem] * 4 + [anywhere] * 7,
        out_specs=(anywhere,) * 6 + (vmem,),
        scratch_shapes=[
            narrow,
            narrow,
            narrow,
            pltpu.VMEM((mem_len, width), low),
            pltpu.VMEM((mem_len, width), low),
            narrow,
            wide,
            pltpu.VMEM((width, length), low),
            pltpu.VMEM((2 * down * width // LANES, LANES), low),
            square,
            square,
            square,
            pltpu.VMEM((width, down), low),
            pltpu.VMEM((down, width), low),
            pltpu.VMEM((width, feed) if resident else (slots, width, tile), low),
            pltpu.VMEM((feed, width) if resident else (slots, tile, width), low),
            wide,
            wide,
            wide,
            wide,
            pltpu.VMEM((length, 1), f32),
            pltpu.VMEM((length, 1), f32),
            narrow,
            narrow,
            narrow,
            narrow,
            narrow,
            pltpu.VMEM((width // LANES, mem_len, LANES // HD * length), low),
            pltpu.VMEM((length, feed), low),
            pltpu.VMEM((length, feed) if resident else (16, LANES), low),
            pltpu.VMEM((length, down), low),
            pltpu.VMEM((length, down), low),
            pltpu.VMEM((length, down), low),
            pltpu.SemaphoreType.DMA((10,)),
            pltpu.SemaphoreType.DMA((slots,)),
            pltpu.SemaphoreType.DMA((slots,)),
            pltpu.SemaphoreType.DMA((5 + width // 512,)),
        ],
        compiler_params=pltpu.CompilerParams(vmem_limit_bytes=VMEM_BYTES + 3 * 1024 * 1024),
        name="middle",
    )(tokens, attended, cotangent, mem_key, mem_value, gains, shifts, down_bias, raise_bias, *weights)


def per_device(
    tokens,
    memory,
    segment_ids,
    padding_mask,
    cotangent,
    prefix_embed,
    prefix_first,
    first_bias,
    prefix_second,
    second_bias,
    adapter_down,
    down_bias,
    adapter_raise,
    raise_bias,
    norm_gain,
    norm_shift,
    self_query,
    self_key,
    self_value,
    self_output,
    cross_query,
    cross_key,
    cross_value,
    cross_output,
    feed_in,
    feed_out,
):
    row_count, length, model_width = tokens.shape
    flat_rows = row_count * length
    n = lax.axis_size("seq")
    batches = lax.axis_size("batch")
    down = adapter_down.shape[1]
    attended, mem_key, mem_value, *saved = self_forward(
        n,
        segment_ids,
        padding_mask,
        tokens.reshape(flat_rows, model_width),
        (self_query, self_key, self_value),
        (
            prefix_embed,
            prefix_first,
            first_bias.reshape(1, -1),
            prefix_second,
            second_bias.reshape(1, -1),
        ),
        memory.reshape(-1, model_width),
        (cross_key, cross_value),
    )
    layer_output, first_grad, out_grad, *mem_grads, weight_sums, vector_sums = middle(
        tokens.reshape(flat_rows, model_width),
        attended,
        cotangent.reshape(flat_rows, model_width),
        mem_key,
        mem_value,
        norm_gain,
        norm_shift,
        down_bias.reshape(1, -1),
        raise_bias.reshape(1, -1),
        (
            self_output,
            cross_query,
            cross_output,
            adapter_down,
            adapter_raise,
            feed_in,
            feed_out,
        ),
    )
    layer_output = layer_output.reshape(row_count, length, model_width)
    token_grad, memory_grad, prefix_grad, vector_sums, full_sums = self_backward(
        n,
        batches,
        first_grad,
        out_grad.reshape(n, -1, HD, length),
        weight_sums,
        mem_grads,
        (cross_key, cross_value),
        vector_sums,
        saved,
        (self_query, self_key, self_value),
    )
    *replicated, token_grad, memory_grad = finish(
        full_sums.reshape(-1, LANES),
        vector_sums,
        prefix_grad,
        prefix_embed,
        prefix_first,
        first_bias.reshape(1, -1),
        prefix_second,
        down,
        token_grad,
        memory_grad,
    )
    token_grad = token_grad.reshape(row_count, length, model_width)
    memory_grad = memory_grad.reshape(memory.shape)
    replicated = [
        value.reshape(-1) if value.shape[0] == 1 else value for value in replicated
    ]
    return (layer_output, token_grad, memory_grad, *replicated)


def solution(mesh):
    placed = (
        P("batch", "seq", None),
        P("batch", "seq", None),
        P("batch", "seq"),
        P("batch", "seq"),
        P("batch", "seq", None),
        P(),
        P(),
        P(),
        P(),
        P(),
        P(),
        P(),
        P(),
        P(),
        P(),
        P(),
        P(),
        P(),
        P(),
        P(),
        P(),
        P(),
        P(),
        P(),
        P(),
        P(),
    )
    return jax.shard_map(
        per_device,
        mesh=mesh,
        in_specs=placed,
        out_specs=(
            P("batch", "seq", None),
            P("batch", "seq", None),
            P("batch", "seq", None),
            P(),
            P(),
            P(),
            P(),
            P(),
            P(),
            P(),
            P(),
            P(),
            P(),
            P(),
        ),
        check_vma=False,
    )
```

```python
import functools

import jax
import jax.numpy as jnp
from jax import lax
from jax.experimental import pallas as pl
from jax.experimental.pallas import tpu as pltpu
from jax.sharding import PartitionSpec as P

H = 16
HD = 64
LANES = 128
PREFIX_ROWS = 32
VMEM_BYTES = 60 * 1024 * 1024
SUM_ROWS = 16
MESH = pl.DeviceIdType.MESH

masked_score = -1e30
norm_eps = 1e-05

def dot_nn(left, right):
    return lax.dot_general(
        left, right, (((1,), (0,)), ((), ())), preferred_element_type=jnp.float32
    )


def dot_nt(left, right):
    return lax.dot_general(
        left, right, (((1,), (1,)), ((), ())), preferred_element_type=jnp.float32
    )


def dot_tn(left, right):
    return lax.dot_general(
        left, right, (((0,), (0,)), ((), ())), preferred_element_type=jnp.float32
    )


def remote(source, target, send_sem, recv_sem, axis, peer):
    return pltpu.make_async_remote_copy(
        src_ref=source,
        dst_ref=target,
        send_sem=send_sem,
        recv_sem=recv_sem,
        device_id={axis: peer},
        device_id_type=MESH,
    )


def enter(sizes):
    barrier = pltpu.get_barrier_semaphore()
    for axis, size in sizes.items():
        for other in range(size):

            @pl.when(other != lax.axis_index(axis))
            def _():
                pl.semaphore_signal(barrier, inc=1, device_id={axis: other}, device_id_type=MESH)

    pl.semaphore_wait(barrier, sum(sizes.values()) - len(sizes))


def others(size, mine, body):
    for other in range(size):

        @pl.when(other != mine)
        def _():
            body(other)


def rows_of(index, size):
    return pl.ds(pl.multiple_of(index * size, size), size)


def span_of(start, size):
    return pl.ds(pl.multiple_of(start, LANES), size)


def own_columns(ref, first, me, width):
    if width % LANES == 0:
        return ref[:, pl.ds(pl.multiple_of(first + me * width, LANES), width)].astype(jnp.float32)
    share = LANES // width
    block = ref[:, pl.ds(pl.multiple_of(first + me // share * LANES, LANES), LANES)].astype(
        jnp.float32
    )
    picked = block[:, :width]
    for part in range(1, share):
        picked = jnp.where(me % share == part, block[:, part * width : (part + 1) * width], picked)
    return picked


def head_lanes(shape, head):
    lane = lax.broadcasted_iota(jnp.int32, shape, 1)
    return (lane >= head * HD) & (lane < (head + 1) * HD)


def self_forward_kernel(
    n,
    seg_ref,
    pad_ref,
    tok_ref,
    wq_in,
    wk_in,
    wv_in,
    emb_ref,
    first_in,
    fbias_ref,
    second_in,
    sbias_ref,
    mem_ref,
    wck_in,
    wcv_in,
    att_ref,
    mkey_out,
    mvalue_out,
    qx_out,
    kx_out,
    raw_out,
    pk_out,
    pv_out,
    pkt_out,
    ot_out,
    lse_out,
    send,
    recv,
    meta_send,
    meta,
    kx,
    qx,
    vt,
    hidden,
    pk,
    pv,
    pkt,
    pvt,
    stat,
    acc,
    o_send,
    o_recv,
    mem_all,
    wck,
    wcv,
    mkey_ref,
    mvalue_ref,
    wq_ref,
    wk_ref,
    wv_ref,
    first_ref,
    second_ref,
    send_sem,
    recv_sem,
    meta_send_sem,
    meta_recv_sem,
    o_send_sem,
    o_recv_sem,
    mem_send_sem,
    mem_recv_sem,
    out_sem,
    weight_sem,
    in_sem,
):
    low = jnp.bfloat16
    f32 = jnp.float32
    me = lax.axis_index("seq")
    length, width = tok_ref.shape
    group = width // n
    heads = group // HD
    plane = 2 * length
    planes = n // 2
    block = 2 * LANES
    per_block = block // group
    blocks = width // block
    my_plane = me // 2
    my_side = lax.rem(me, 2)

    upward = my_plane >= planes // 2
    turn_sign = jnp.where(upward, 1, -1)

    def plane_after(step):
        return lax.rem(my_plane + planes + turn_sign * step, planes)

    def meta_copy(peer, slot):
        return remote(
            meta_send, meta.at[slot], meta_send_sem.at[peer], meta_recv_sem.at[slot], "seq", peer
        )

    def qkv_copy(head, peer, slot):
        return remote(
            send.at[peer, head],
            recv.at[head, slot],
            send_sem.at[head, peer],
            recv_sem.at[head, slot],
            "seq",
            peer,
        )

    def out_copy(head, peer, slot):
        return remote(
            o_send.at[head, peer],
            o_recv.at[slot, head],
            o_send_sem.at[head, peer],
            o_recv_sem.at[head, slot],
            "seq",
            peer,
        )

    def mem_along(which, toward):
        part = mem_all.at[which, my_side]
        return remote(
            part,
            part,
            mem_send_sem.at[(toward + 1) // 2, which],
            mem_recv_sem.at[which],
            "seq",
            me + 2 * toward,
        )

    def mem_across(side):
        part = mem_all.at[:, side]
        return remote(
            part,
            part,
            mem_send_sem.at[0, planes],
            mem_recv_sem.at[planes],
            "seq",
            me + 1 - 2 * my_side,
        )

    def mem_hops(hop, body):
        for toward in (1, -1):
            which = my_plane - toward * hop
            ahead = my_plane + toward

            @pl.when((which >= 0) & (which < planes) & (ahead >= 0) & (ahead < planes))
            def _():
                body(mem_along(which, toward))

    def mem_arrivals(hop):
        for toward in (1, -1):
            which = my_plane - toward * hop

            @pl.when((which >= 0) & (which < planes))
            def _():
                mem_along(which, -toward).wait_recv()

    def block_at(step):
        if blocks >= planes:
            share = blocks // planes
            return plane_after(1 + step // share) * share + step % share
        return lax.rem(me // per_block + 1 + step, blocks)

    def weight_load(step, which):
        columns = rows_of(block_at(step), block)
        source = (wq_in, wk_in, wv_in)[which]
        target = (wq_ref, wk_ref, wv_ref)[which]
        return pltpu.make_async_copy(
            source.at[:, columns], target.at[:, columns], weight_sem.at[step, which]
        )

    for step in range(blocks):
        for which in range(3):
            weight_load(step, which).start()
    loads = [
        pltpu.make_async_copy(source, target, in_sem.at[index])
        for index, (source, target) in enumerate(
            ((first_in, first_ref), (second_in, second_ref), (wck_in, wck), (wcv_in, wcv))
        )
    ]
    for load in loads:
        load.start()
    segments = seg_ref[...]
    tags = jnp.where(pad_ref[...] == 1, segments, -1)
    row = lax.broadcasted_iota(jnp.int32, meta_send.shape, 0)
    meta_send[...] = jnp.where(row == 0, segments, tags)
    mem_all[my_plane, my_side] = mem_ref[...]
    enter({"seq": n})
    others(n, me, lambda peer: meta_copy(peer, me).start())
    meta[me] = meta_send[...]

    for step in range(blocks):
        at = block_at(step)
        columns = rows_of(at, block)
        for which, weight in enumerate((wq_ref, wk_ref, wv_ref)):
            weight_load(step, which).wait()
            piece = dot_nn(tok_ref[...], weight[:, columns]).T.astype(low)
            for part in range(per_block):
                for head in range(heads):
                    first = part * group + head * HD
                    send[at * per_block + part, head, which] = piece[first : first + HD]
        for part in range(per_block):
            peer = at * per_block + part

            @pl.when(peer != me)
            def _():
                qkv_copy(0, peer, me).start()

            @pl.when(peer == me)
            def _():
                for head in range(heads):
                    recv[head, me] = send[peer, head]

    mem_hops(0, lambda copy: copy.start())
    loads[0].wait()
    loads[1].wait()
    hidden[...] = jnp.zeros_like(hidden)
    hidden[: emb_ref.shape[0], :] = jnp.tanh(dot_nn(emb_ref[...], first_ref[...]) + fbias_ref[...])
    hidden_low = hidden[...].astype(low)
    prefix_key = dot_nn(hidden_low, own_columns(second_ref, 0, me, group).astype(low)) + own_columns(
        sbias_ref, 0, me, group
    )
    prefix_value = dot_nn(
        hidden_low, own_columns(second_ref, width, me, group).astype(low)
    ) + own_columns(sbias_ref, width, me, group)
    prefix_row = lax.broadcasted_iota(jnp.int32, (PREFIX_ROWS, HD), 0)
    prefix_open = jnp.where(prefix_row < emb_ref.shape[0], 0.0, masked_score)
    for head in range(heads):
        here = slice(head * HD, (head + 1) * HD)
        pk[head] = jnp.concatenate([prefix_key[:, here], prefix_open], axis=1).astype(low)
        pv[head] = prefix_value[:, here].astype(low)
    pkt[...] = prefix_key.T.astype(low).reshape(heads, HD, PREFIX_ROWS)
    pvt[:, :HD, :] = prefix_value.T.astype(low).reshape(heads, HD, PREFIX_ROWS)
    pvt[:, HD:, :] = jnp.ones((heads, SUM_ROWS, PREFIX_ROWS), low)
    vt[:, HD:, :] = jnp.ones((heads, SUM_ROWS, n * length), low)

    def arrive(head, chunk):
        @pl.when(chunk != me)
        def _():
            @pl.when(head == 0)
            def _():
                meta_copy(chunk, chunk).wait_recv()

            qkv_copy(head, chunk, chunk).wait_recv()

        here = rows_of(chunk, length)
        state = lax.broadcasted_iota(jnp.int32, (HD, length), 0)
        qx[head, :HD, here] = (recv[head, chunk, 0].astype(f32) * 0.125).astype(low)
        qx[head, HD:, here] = jnp.where(state == meta[chunk, 0:1, :], 1.0, 0.0).astype(low)
        is_open = jnp.where(state == meta[chunk, 1:2, :], 0.0, masked_score)
        kx[head, here, :] = jnp.concatenate(
            [recv[head, chunk, 1].astype(f32), is_open], axis=0
        ).T.astype(low)
        vt[head, :HD, here] = recv[head, chunk, 2]

    def open_plane(head, which):
        scores = dot_nn(pk[head], qx[head, :, rows_of(which, plane)])
        top = jnp.max(scores, axis=0, keepdims=True)
        raised = jnp.exp(scores - top)
        stat[which, head, 0:1, :] = top
        acc[which, head] = dot_nn(pvt[head], raised.astype(low))

    def pair_part(head, upper, lower, first, count, keys, diagonal):
        here = slice(first, first + count)
        queries = qx[head, :, span_of(upper * plane + first, count)]
        key_rows = span_of(lower * plane, keys)
        scores = dot_nn(kx[head, key_rows, :], queries)
        if diagonal:
            key_at = lax.broadcasted_iota(jnp.int32, scores.shape, 0)
            query_at = lax.broadcasted_iota(jnp.int32, scores.shape, 1) + first
            scores = jnp.where(key_at <= query_at, scores, masked_score)
        old_top = stat[upper, head, 0:1, here]
        top = jnp.maximum(old_top, jnp.max(scores, axis=0, keepdims=True))
        raised = jnp.exp(scores - top).astype(low)
        stat[upper, head, 0:1, here] = top
        acc[upper, head, :, here] = acc[upper, head, :, here] * jnp.exp(old_top - top) + dot_nn(
            vt[head, :, key_rows], raised
        )

    def pair(head, upper, lower):
        pair_part(head, upper, lower, 0, plane, plane, False)

    def pair_diagonal(head, which):
        for part in range(2):
            pair_part(head, which, which, part * length, length, (part + 1) * length, True)

    def close_plane(head, which):
        total = acc[which, head, HD : HD + 1, :]
        value = acc[which, head, :HD, :] / total
        acc[which, head, :HD, :] = value
        stat[which, head, 0:1, :] = stat[which, head, 0:1, :] + jnp.log(total)
        for part in range(2):
            chunk = 2 * which + part
            o_send[head, chunk] = value[:, part * length : (part + 1) * length].astype(low)

            @pl.when((chunk != me) & (head == heads - 1))
            def _():
                out_copy(head, chunk, me).start()

            @pl.when(chunk == me)
            def _():
                o_recv[me, head] = o_send[head, chunk]

    def project_memory():
        mem_across(1 - my_side).wait_recv()
        for load in loads[2:]:
            load.wait()
        whole = mem_all[...].reshape(mkey_ref.shape)

        def one(index, carry):
            here = rows_of(index, block)
            mkey_ref[:, here] = dot_nn(whole, wck[:, here]).astype(low)
            mvalue_ref[:, here] = dot_nn(whole, wcv[:, here]).astype(low)
            return carry

        lax.fori_loop(0, blocks, one, 0)

    def stage(index, carry):
        head = index // planes
        step = lax.rem(index, planes)

        @pl.when(head + 1 < heads)
        def _():
            there = plane_after(1 + step)
            for part in range(2):
                peer = 2 * there + part

                @pl.when(peer != me)
                def _():
                    qkv_copy(head, peer, me).wait_send()
                    qkv_copy(head + 1, peer, me).start()

        @pl.when((head == heads - 1) & (head > 0))
        def _():
            there = plane_after(1 + step)
            for part in range(2):
                peer = 2 * there + part

                @pl.when(peer != me)
                def _():
                    qkv_copy(head, peer, me).wait_send()
                    out_copy(head - 1, peer, me).start()

        here = plane_after(step)
        arrive(head, 2 * here)
        arrive(head, 2 * here + 1)
        open_plane(head, here)
        pair_diagonal(head, here)

        def earlier(back, inner):
            there = plane_after(back)
            pair(head, jnp.maximum(here, there), jnp.minimum(here, there))

            @pl.when((step == planes - 1) & (there > here))
            def _():
                close_plane(head, there)

            return inner

        lax.fori_loop(0, step, earlier, 0)
        for hop in range(1, planes - 1):

            @pl.when(index == hop)
            def _():
                mem_arrivals(hop)
                mem_hops(hop, lambda copy: copy.start())

        @pl.when(index == planes - 1)
        def _():
            mem_arrivals(planes - 1)
            mem_across(my_side).start()

        @pl.when((upward & (my_plane + step >= planes)) | (step == planes - 1))
        def _():
            close_plane(head, here)

        @pl.when(jnp.logical_not(upward) & (step == my_plane))
        def _():
            def close(which, inner):
                close_plane(head, which)
                return inner

            lax.fori_loop(0, my_plane + 1, close, 0)

        return carry

    lax.fori_loop(0, heads * planes, stage, 0)

    saves = []

    def save(source, target):
        copy = pltpu.make_async_copy(source, target, out_sem.at[len(saves)])
        copy.start()
        saves.append(copy)

    save(qx, qx_out)
    save(kx, kx_out)
    save(recv, raw_out)
    save(pk, pk_out)
    save(pv, pv_out)
    save(pkt, pkt_out)
    save(acc, ot_out)
    save(stat, lse_out)
    project_memory()
    save(mkey_ref, mkey_out)
    save(mvalue_ref, mvalue_out)
    for other in range(n):

        @pl.when(other != me)
        def _():
            for head in range(heads):
                out_copy(head, other, other).wait_recv()

        att_ref[:, other * group : (other + 1) * group] = (
            o_recv[other].reshape(group, length).astype(f32).T.astype(low)
        )

    def drain(peer):
        meta_copy(peer, me).wait_send()
        if heads == 1:
            qkv_copy(0, peer, me).wait_send()
        for head in range(heads):
            out_copy(head, peer, me).wait_send()

    others(n, me, drain)
    for hop in range(planes - 1):
        mem_hops(hop, lambda copy: copy.wait_send())
    mem_across(my_side).wait_send()
    for copy in saves:
        copy.wait()


def self_forward(n, segments, padding, tokens, weights, prefix, memory, mem_weights):
    length, width = tokens.shape
    group = width // n
    heads = group // HD
    whole = n * length
    planes = n // 2
    low = jnp.bfloat16
    f32 = jnp.float32
    vmem = pl.BlockSpec(memory_space=pltpu.VMEM)
    anywhere = pl.BlockSpec(memory_space=pl.ANY)
    dma = pltpu.SemaphoreType.DMA
    shapes = (
        ((heads, 2 * HD, whole), low),
        ((heads, whole, 2 * HD), low),
        ((heads, n, 3, HD, length), low),
        ((heads, PREFIX_ROWS, 2 * HD), low),
        ((heads, PREFIX_ROWS, HD), low),
        ((heads, HD, PREFIX_ROWS), low),
        ((planes, heads, HD + SUM_ROWS, 2 * length), f32),
        ((planes, heads, 8, 2 * length), f32),
    )
    square = pltpu.VMEM((width, width), low)
    qx, kx, raw, pk, pv, pkt, acc, stat = (pltpu.VMEM(*shape) for shape in shapes)
    return pl.pallas_call(
        functools.partial(self_forward_kernel, n),
        out_shape=(
            jax.ShapeDtypeStruct((length, width), low),
            jax.ShapeDtypeStruct((n * memory.shape[0], width), low),
            jax.ShapeDtypeStruct((n * memory.shape[0], width), low),
        )
        + tuple(jax.ShapeDtypeStruct(*shape) for shape in shapes),
        in_specs=[vmem] * 3
        + [anywhere] * 3
        + [vmem, anywhere, vmem, anywhere, vmem, vmem]
        + [anywhere] * 2,
        out_specs=(vmem,) + (anywhere,) * 10,
        scratch_shapes=[
            pltpu.VMEM((n, heads, 3, HD, length), low),
            raw,
            pltpu.VMEM((8, length), jnp.int32),
            pltpu.VMEM((n, 8, length), jnp.int32),
            kx,
            qx,
            pltpu.VMEM((heads, HD + SUM_ROWS, whole), low),
            pltpu.VMEM((PREFIX_ROWS, weights[0].shape[0] // 2), f32),
            pk,
            pv,
            pkt,
            pltpu.VMEM((heads, HD + SUM_ROWS, PREFIX_ROWS), low),
            stat,
            acc,
            pltpu.VMEM((heads, n, HD, length), low),
            pltpu.VMEM((n, heads, HD, length), low),
            pltpu.VMEM((planes, 2) + memory.shape, low),
            square,
            square,
            pltpu.VMEM((n * memory.shape[0], width), low),
            pltpu.VMEM((n * memory.shape[0], width), low),
            square,
            square,
            square,
            pltpu.VMEM(prefix[1].shape, low),
            pltpu.VMEM(prefix[3].shape, low),
            dma((heads, n)),
            dma((heads, n)),
            dma((n,)),
            dma((n,)),
            dma((heads, n)),
            dma((heads, n)),
            dma((2, planes + 1)),
            dma((planes + 1,)),
            dma((10,)),
            dma((width // (2 * LANES), 3)),
            dma((4,)),
        ],
        compiler_params=pltpu.CompilerParams(
            collective_id=0, has_side_effects=True, vmem_limit_bytes=VMEM_BYTES
        ),
        name="self_forward",
    )(segments, padding, tokens, *weights, *prefix, memory, *mem_weights)


def self_backward_kernel(
    n,
    batches,
    base_in,
    do_in,
    sums_in,
    mkey_in,
    mvalue_in,
    wck_in,
    wcv_in,
    vecs_in,
    qx_in,
    kx_in,
    raw_in,
    pk_in,
    pv_in,
    pkt_in,
    ot_in,
    lse_in,
    wq_in,
    wk_in,
    wv_in,
    tg_ref,
    mgrad_ref,
    pkv_ref,
    vecs_ref,
    full_out,
    do_recv,
    qx,
    kx,
    raw,
    kt,
    values,
    dot,
    qdo,
    pk,
    pv,
    pkt,
    ot,
    stat,
    weights,
    dqt,
    dkv,
    g_send,
    g_recv,
    pre_ref,
    pre_all,
    pre_sum,
    pre_recv,
    sums_mine,
    sums_core,
    sums_x,
    sums_side,
    sums_z,
    full,
    mkey,
    mvalue,
    wck,
    wcv,
    mem_part,
    mem_side,
    mem_up,
    mem_down,
    vec_all,
    vec_sum,
    vec_y,
    vec_both,
    vec_z,
    product,
    base_ref,
    do_send_sem,
    do_recv_sem,
    g_send_sem,
    g_recv_sem,
    in_sem,
    send_sem,
    recv_sem,
):
    low = jnp.bfloat16
    f32 = jnp.float32
    me = lax.axis_index("seq")
    length, width = tg_ref.shape
    group = width // n
    heads = group // HD
    plane = 2 * length
    planes = n // 2
    step_rows = 256
    my_batch = lax.axis_index("batch")
    my_core = lax.rem(my_batch, 2)
    my_high = my_batch // 2
    highs = batches // 2
    my_plane = me // 2
    my_side = lax.rem(me, 2)
    beside = me + 1 - 2 * my_side
    used = [0]

    def numbers(count):
        used[0] += count
        return used[0] - count

    core_slot = numbers(2)
    x_slot = numbers(2 * highs)
    y_slot = numbers(3)
    z_slot = numbers(2 * planes)
    up_slot = numbers(planes)
    down_slot = numbers(planes)
    va_slot = numbers(batches)
    vb_slot = numbers(1)
    vc_slot = numbers(planes)
    pa_slot = numbers(batches)
    pb_slot = numbers(n)

    def send(source, target, first, peer_index, slot_index, axis, peer):
        return remote(
            source,
            target,
            send_sem.at[first + peer_index],
            recv_sem.at[first + slot_index],
            axis,
            peer,
        )

    half_rows = 2 * planes * highs * sums_z.shape[1]
    x_rows = half_rows // highs
    y_rows = x_rows // 2
    z_rows = y_rows // planes
    x_row = pl.multiple_of(my_high * x_rows, x_rows)
    y_row = pl.multiple_of(x_row + my_side * y_rows, y_rows)

    def part(row, count):
        return sums_mine.at[pl.ds(pl.multiple_of(row, count), count)]

    def reduce_core():
        return send(
            sums_in.at[1 - my_core], sums_core, core_slot, 0, 0, "batch", my_batch + 1 - 2 * my_core
        )

    def reduce_x(peer, slot):
        return send(
            part(peer * x_rows, x_rows),
            sums_x.at[slot],
            x_slot,
            peer,
            slot,
            "batch",
            2 * peer + my_core,
        )

    def reduce_y():
        return send(
            part(x_row + (1 - my_side) * y_rows, y_rows), sums_side, y_slot, 0, 0, "seq", beside
        )

    def reduce_z(peer, slot):
        return send(
            part(y_row + peer * z_rows, z_rows),
            sums_z.at[slot],
            z_slot,
            peer,
            slot,
            "seq",
            2 * peer + my_side,
        )

    def gather_z(peer, slot):
        piece = full.at[my_core, my_high, my_side, slot]
        return send(piece, piece, z_slot + planes, peer, slot, "seq", 2 * peer + my_side)

    def gather_y(side):
        piece = full.at[my_core, my_high, side]
        return send(piece, piece, y_slot + 1, 0, 0, "seq", beside)

    def gather_x(peer, slot):
        piece = full.at[my_core, slot]
        return send(piece, piece, x_slot + highs, peer, slot, "batch", 2 * peer + my_core)

    def gather_core(core):
        piece = full.at[core]
        return send(piece, piece, core_slot + 1, 0, 0, "batch", my_batch + 1 - 2 * my_core)

    def mem_across():
        return send(
            mem_part.at[:, 1 - my_side], mem_side, y_slot + 2, 0, 0, "seq", beside
        )

    def mem_hop(target, toward, peer=None):
        buffer, slot = (mem_up, up_slot) if toward > 0 else (mem_down, down_slot)
        return send(
            mem_part.at[target, my_side],
            buffer.at[target],
            slot,
            target,
            target,
            "seq",
            me + 2 * toward if peer is None else peer,
        )

    def mem_from(target, toward):
        return mem_hop(target, toward, me - 2 * toward)

    def mem_pass(toward):
        buffer = mem_up if toward > 0 else mem_down
        first = 0 if toward > 0 else planes - 1
        for target in range(planes):

            @pl.when((target - my_plane) * toward > 0)
            def _():
                @pl.when(my_plane != first)
                def _():
                    mem_from(target, toward).wait_recv()
                    mem_part[target, my_side] = (
                        mem_part[target, my_side].astype(f32) + buffer[target].astype(f32)
                    ).astype(low)

                mem_hop(target, toward).start()

    def mem_stage(at):
        pl.when(my_plane == at)(lambda: mem_pass(1))
        pl.when(my_plane == planes - 1 - at)(lambda: mem_pass(-1))

    def mem_end():
        value = mem_part[my_plane, my_side].astype(f32)
        mgrad_ref[...] = value.astype(low)

        @pl.when(my_plane > 0)
        def _():
            mem_from(my_plane, 1).wait_recv()
            mgrad_ref[...] = (mgrad_ref[...].astype(f32) + mem_up[my_plane].astype(f32)).astype(low)

        @pl.when(my_plane < planes - 1)
        def _():
            mem_from(my_plane, -1).wait_recv()
            mgrad_ref[...] = (
                mgrad_ref[...].astype(f32) + mem_down[my_plane].astype(f32)
            ).astype(low)

    def mem_drain():
        for target in range(planes):

            @pl.when(target > my_plane)
            def _():
                mem_hop(target, 1).wait_send()

            @pl.when(target < my_plane)
            def _():
                mem_hop(target, -1).wait_send()

    def vec_a(peer, slot):
        return send(vecs_in, vec_all.at[slot], va_slot, peer, slot, "batch", peer)

    def vec_b(side):
        return send(vec_sum, vec_y.at[side], vb_slot, 0, 0, "seq", beside)

    def vec_c(peer, slot):
        return send(vec_both, vec_z.at[slot], vc_slot, peer, slot, "seq", 2 * peer + my_side)

    def pre_a(peer, slot):
        return send(pre_ref, pre_all.at[slot], pa_slot, peer, slot, "batch", peer)

    def pre_b(peer, slot):
        return send(pre_sum, pre_recv.at[slot], pb_slot, peer, slot, "seq", peer)

    def do_copy(head, peer, slot):
        return remote(
            do_in.at[peer, head],
            do_recv.at[head, slot],
            do_send_sem.at[head, peer],
            do_recv_sem.at[head, slot],
            "seq",
            peer,
        )

    def q_copy(head, peer, slot):
        return remote(
            g_send.at[peer, head, 0],
            g_recv.at[0, slot, head],
            g_send_sem.at[0, head, peer],
            g_recv_sem.at[0, head, slot],
            "seq",
            peer,
        )

    def kv_copy(head, peer, slot):
        return remote(
            g_send.at[peer, head, pl.ds(1, 2)],
            g_recv.at[pl.ds(1, 2), slot, head],
            g_send_sem.at[1, head, peer],
            g_recv_sem.at[1, head, slot],
            "seq",
            peer,
        )

    def far_first(body):
        for index in range(n):
            peer = jnp.where(my_plane < planes // 2, n - 1 - index, index)

            @pl.when(peer != me)
            def _():
                body(peer)

    def added(ref, size):
        value = ref[0].astype(f32)
        for other in range(1, size):
            value = value + ref[other].astype(f32)
        return value

    loads = [
        pltpu.make_async_copy(source, target, in_sem.at[index])
        for index, (source, target) in enumerate(
            (
                (raw_in, raw),
                (kx_in, kx),
                (pk_in, pk),
                (pv_in, pv),
                (pkt_in, pkt),
                (qx_in, qx),
                (ot_in, ot),
                (lse_in, stat),
                (sums_in.at[my_core], sums_mine),
                (vecs_in, vec_all.at[my_batch]),
                (mkey_in, mkey),
                (mvalue_in, mvalue),
                (wck_in, wck),
                (wcv_in, wcv),
                (base_in, base_ref),
                (wq_in, weights.at[0]),
                (wk_in, weights.at[1]),
                (wv_in, weights.at[2]),
            )
        )
    ]
    own_do = pltpu.make_async_copy(do_in.at[me], do_recv.at[:, me], in_sem.at[len(loads)])
    own_do.start()
    for load in loads:
        load.start()
    enter({"seq": n, "batch": batches})
    far_first(lambda peer: do_copy(0, peer, me).start())
    reduce_core().start()
    others(batches, my_batch, lambda peer: vec_a(peer, my_batch).start())
    dkv[...] = jnp.zeros_like(dkv)
    product[...] = jnp.zeros_like(product)
    pre_ref[...] = jnp.zeros_like(pre_ref)
    for load in loads[:8]:
        load.wait()
    own_do.wait()

    def turn(index, carry):
        head = index // n
        chunk = lax.rem(index, n)
        here = rows_of(chunk, length)
        kt[head, :, here] = raw[head, chunk, 1]
        values[head, here, :] = raw[head, chunk, 2].astype(f32).T.astype(low)
        return carry

    lax.fori_loop(0, n, turn, 0)

    def turn_rest():
        lax.fori_loop(n, heads * n, turn, 0)

    def memory_back(index, carry):
        here = rows_of(index, step_rows)
        value = dot_nt(mkey[...], wck[here, :]) + dot_nt(mvalue[...], wcv[here, :])
        mem_part[:, :, :, here] = value.astype(low).reshape(mem_part.shape[:3] + (step_rows,))
        return carry

    def mem_begin():
        for load in loads[10:14]:
            load.wait()
        lax.fori_loop(0, width // step_rows, memory_back, 0)
        mem_across().start()

    def next_head(head):
        def move(peer):
            do_copy(head, peer, me).wait_send()
            do_copy(head + 1, peer, me).start()

        far_first(move)

    def arrive(head, which):
        for part in range(2):
            chunk = 2 * which + part

            @pl.when(chunk != me)
            def _():
                do_copy(head, chunk, chunk).wait_recv()

            grads = do_recv[head, chunk]
            dot[head, :, rows_of(chunk, length)] = grads
            grads = grads.astype(f32)
            query = raw[head, chunk, 0].astype(f32) * 0.125
            qdo[head, rows_of(chunk, length), :] = (
                jnp.concatenate([query, grads], axis=0).T.astype(low)
            )
            here = slice(part * length, (part + 1) * length)
            stat[which, head, 1:2, here] = jnp.sum(
                grads * ot[which, head, :HD, here], axis=0, keepdims=True
            )
        here = rows_of(which, plane)
        weight = jnp.exp(dot_nn(pk[head], qx[head, :, here]) - stat[which, head, 0:1, :])
        slope = weight * (dot_nn(pv[head], dot[head, :, here]) - stat[which, head, 1:2, :])
        both = jnp.concatenate([slope, weight], axis=0).astype(low)
        sums = dot_nn(both, qdo[head, here, :])
        pre_ref[head] += jnp.where(
            head_lanes((PREFIX_ROWS, 2 * HD), 0), sums[:PREFIX_ROWS], sums[PREFIX_ROWS:]
        )
        slope = slope.astype(low)
        dqt[which, head] = dot_nn(pkt[head], slope)

    def plus(first, second):
        return (first.astype(f32) + second.astype(f32)).astype(low)

    def sum_one():
        loads[8].wait()
        loads[9].wait()
        reduce_core().wait_recv()
        sums_mine[...] = plus(sums_mine[...], sums_core[...])
        others(highs, my_high, lambda peer: reduce_x(peer, my_high).start())

    def sum_two():
        here = pl.ds(x_row, x_rows)
        others(highs, my_high, lambda peer: reduce_x(peer, peer).wait_recv())
        sums_x[my_high] = sums_mine[here]
        sums_mine[here] = added(sums_x, highs).astype(low)
        reduce_y().start()

    def sum_three():
        here = pl.ds(y_row, y_rows)
        reduce_y().wait_recv()
        sums_mine[here] = plus(sums_mine[here], sums_side[...])
        others(planes, my_plane, lambda peer: reduce_z(peer, my_plane).start())

    def sum_four():
        here = pl.ds(pl.multiple_of(y_row + my_plane * z_rows, z_rows), z_rows)
        others(planes, my_plane, lambda peer: reduce_z(peer, peer).wait_recv())
        sums_z[my_plane] = sums_mine[here]
        full[my_core, my_high, my_side, my_plane] = added(sums_z, planes).astype(low)
        others(planes, my_plane, lambda peer: gather_z(peer, my_plane).start())

    def sum_five():
        others(planes, my_plane, lambda peer: gather_z(peer, peer).wait_recv())
        gather_y(my_side).start()

    def sum_six():
        gather_y(1 - my_side).wait_recv()
        others(highs, my_high, lambda peer: gather_x(peer, my_high).start())

    def sum_seven():
        others(highs, my_high, lambda peer: gather_x(peer, peer).wait_recv())
        gather_core(my_core).start()

    def sum_end():
        gather_core(1 - my_core).wait_recv()
        save_full.start()

    def vec_one():
        others(batches, my_batch, lambda peer: vec_a(peer, peer).wait_recv())
        vec_sum[...] = added(vec_all, batches)
        vec_b(my_side).start()
        vec_y[my_side] = vec_sum[...]

    def vec_two():
        vec_b(1 - my_side).wait_recv()
        value = (vec_y[0] + vec_y[1]).astype(f32)
        vec_both[...] = jnp.concatenate(
            [value[:, : width // 2], value[:, width // 2 :]], axis=0
        ).astype(low)
        others(planes, my_plane, lambda peer: vec_c(peer, my_plane).start())
        vec_z[my_plane] = vec_both[...]

    def vec_end():
        others(planes, my_plane, lambda peer: vec_c(peer, peer).wait_recv())
        value = added(vec_z, planes)
        vecs_ref[:, : width // 2] = value[:8]
        vecs_ref[:, width // 2 :] = value[8:]

    def mem_one():
        mem_across().wait_recv()
        mem_part[:, my_side] = plus(mem_part[:, my_side], mem_side[...])

    def stage_pa():
        others(batches, my_batch, lambda peer: pre_a(peer, my_batch).start())
        pre_all[my_batch] = pre_ref[...]

    def stage_pb():
        others(batches, my_batch, lambda peer: pre_a(peer, peer).wait_recv())
        pre_sum[...] = added(pre_all, batches).astype(low)
        others(n, me, lambda peer: pre_b(peer, me).start())
        pre_recv[me] = pre_sum[...]

    save_full = pltpu.make_async_copy(full, full_out, in_sem.at[0])

    def pair_part(head, upper, lower, first, count, diagonal):
        keys = span_of(lower * plane + first, count)
        here = span_of(upper * plane + first, plane - first)
        at = slice(first, plane)
        scores = dot_nn(kx[head, keys, :], qx[head, :, here])
        slope = dot_nn(values[head, keys, :], dot[head, :, here]) - stat[upper, head, 1:2, at]
        weight = jnp.exp(scores - stat[upper, head, 0:1, at])
        if diagonal:
            key_at = lax.broadcasted_iota(jnp.int32, scores.shape, 0)
            query_at = lax.broadcasted_iota(jnp.int32, scores.shape, 1)
            weight = jnp.where(key_at <= query_at, weight, 0.0)
        both = jnp.concatenate([(weight * slope).astype(low), weight.astype(low)], axis=0)
        sums = dot_nn(both, qdo[head, here, :])
        dkv[head, keys, :] += jnp.where(
            head_lanes((count, 2 * HD), 0), sums[:count], sums[count:]
        )
        dqt[upper, head, :, at] += dot_nn(kt[head, :, keys], both[:count])

    def pair(head, upper, lower, diagonal):
        if diagonal:
            pair_part(head, upper, lower, 0, length, True)
            pair_part(head, upper, lower, length, length, True)
        else:
            pair_part(head, upper, lower, 0, plane, False)

    def hand_queries(head, which):
        for part in range(2):
            chunk = 2 * which + part
            g_send[chunk, head, 0] = (
                dqt[which, head, :, part * length : (part + 1) * length] * 0.125
            ).astype(low)

            @pl.when(chunk != me)
            def _():
                q_copy(head, chunk, me).start()

            @pl.when(chunk == me)
            def _():
                g_recv[0, me, head] = g_send[chunk, head, 0]

    def hand_keys(head, which):
        for part in range(2):
            chunk = 2 * which + part
            turned = dkv[head, rows_of(chunk, length), :].T.astype(low)
            g_send[chunk, head, 1] = turned[:HD]
            g_send[chunk, head, 2] = turned[HD:]

            @pl.when(chunk != me)
            def _():
                kv_copy(head, chunk, me).start()

            @pl.when(chunk == me)
            def _():
                g_recv[pl.ds(1, 2), me, head] = g_send[chunk, head, pl.ds(1, 2)]

    rising = my_plane >= planes // 2
    total = heads * planes * (planes + 1) // 2
    hooks = [
        (2, sum_one),
        (3, mem_begin),
        (6, mem_one),
        (7, lambda: mem_stage(0)),
        (5, vec_one),
        (5, sum_two),
        (7, sum_three),
        (8, vec_two),
        (10, sum_four),
        (12, sum_five),
        (14, sum_six),
        (16, vec_end),
        (17, sum_seven),
    ] + [(7 + 3 * at, functools.partial(mem_stage, at)) for at in range(1, planes - 1)]
    hooks += [
        (1 + head * total // heads, functools.partial(next_head, head)) for head in range(heads - 1)
    ]
    if heads > 1:
        hooks.append((planes, turn_rest))
    final = total - planes * (planes + 1) // 2
    hooks += [(final + planes + 1, stage_pa), (final + 2 * planes - 1, stage_pb)]

    def hook(pairs):
        for number, body in sorted(hooks, key=lambda item: item[0]):
            pl.when(pairs == number)(body)


    def stage(index, carry):
        head = index // planes
        step = lax.rem(index, planes)
        here = jnp.where(rising, step, planes - 1 - step)

        @pl.when((step == 0) | ((step == 1) & jnp.logical_not(rising)))
        def _():
            @pl.when(rising | (step == 0))
            def _():
                arrive(head, here)

            @pl.when(jnp.logical_not(rising) & (step == 1))
            def _():
                def rest(which, inner):
                    arrive(head, planes - 2 - which)
                    return inner

                lax.fori_loop(0, planes - 1, rest, 0)

        begun = head * (planes * (planes + 1) // 2) + step * planes - step * (step - 1) // 2
        hook(begun)
        pair(head, here, here, True)

        @pl.when(rising)
        def _():
            hand_queries(head, here)

        @pl.when(jnp.logical_not(rising))
        def _():
            hand_keys(head, here)

        def far(at, inner):
            there = jnp.where(rising, here + 1 + at, here - 1 - at)

            @pl.when(rising & (step == 0))
            def _():
                arrive(head, there)

            hook(begun + 1 + at)
            pair(head, jnp.maximum(here, there), jnp.minimum(here, there), False)
            return inner

        lax.fori_loop(0, planes - 1 - step, far, 0)

        @pl.when(rising)
        def _():
            hand_keys(head, here)

        @pl.when(jnp.logical_not(rising))
        def _():
            hand_queries(head, here)

        return carry

    lax.fori_loop(0, heads * planes, stage, 0)
    mem_end()
    for load in loads[14:]:
        load.wait()

    def gathered(peer):
        for head in range(heads):
            q_copy(head, peer, peer).wait_recv()
            kv_copy(head, peer, peer).wait_recv()

    half = width // 2

    def gather_plane(step, carry):
        which = lax.rem(my_plane + step, planes)
        for part in range(2):
            peer = 2 * which + part

            @pl.when(peer != me)
            def _():
                gathered(peer)

        columns = rows_of(which, 2 * group)
        for part in range(2):
            here = slice(part * half, (part + 1) * half)
            value = product[here, :]
            for kind in range(3):
                grads = g_recv[kind, pl.ds(2 * which, 2)].reshape(2 * group, length)
                value = value + dot_nn(weights[kind, here, columns], grads)
            product[here, :] = value
        return carry

    lax.fori_loop(0, planes, gather_plane, 0)
    sum_end()
    tile = 256
    for index in range(width // tile):
        here = slice(index * tile, (index + 1) * tile)
        tg_ref[:, here] = (base_ref[:, here] + product[here, :].T).astype(low)
    for other in range(n):

        @pl.when(other != me)
        def _():
            pre_b(other, other).wait_recv()

        value = pre_recv[other].astype(f32)
        for which in range(2):
            pkv_ref[:, which * width + other * group : which * width + (other + 1) * group] = (
                jnp.concatenate(
                    [value[head, :, which * HD : (which + 1) * HD] for head in range(heads)], axis=1
                )
            )

    def drain(peer):
        do_copy(heads - 1, peer, me).wait_send()
        pre_b(peer, me).wait_send()
        for head in range(heads):
            q_copy(head, peer, me).wait_send()
            kv_copy(head, peer, me).wait_send()

    others(n, me, drain)
    others(batches, my_batch, lambda peer: pre_a(peer, my_batch).wait_send())
    others(batches, my_batch, lambda peer: vec_a(peer, my_batch).wait_send())
    reduce_core().wait_send()
    others(highs, my_high, lambda peer: reduce_x(peer, my_high).wait_send())
    reduce_y().wait_send()
    others(planes, my_plane, lambda peer: reduce_z(peer, my_plane).wait_send())
    others(planes, my_plane, lambda peer: gather_z(peer, my_plane).wait_send())
    gather_y(my_side).wait_send()
    others(highs, my_high, lambda peer: gather_x(peer, my_high).wait_send())
    gather_core(my_core).wait_send()
    mem_across().wait_send()
    mem_drain()
    others(planes, my_plane, lambda peer: vec_c(peer, my_plane).wait_send())
    vec_b(my_side).wait_send()
    save_full.wait()


def self_backward(
    n, batches, first_grad, out_grad, sums, mem_grads, mem_weights, vecs, saved, weights
):
    length, width = first_grad.shape
    group = width // n
    heads = group // HD
    whole = n * length
    planes = n // 2
    low = jnp.bfloat16
    f32 = jnp.float32
    vmem = pl.BlockSpec(memory_space=pltpu.VMEM)
    anywhere = pl.BlockSpec(memory_space=pl.ANY)
    dma = pltpu.SemaphoreType.DMA
    sum_rows = sums.shape[0] // (n * batches)
    mem_len = mem_grads[0].shape[0]
    mem_rows = mem_len // n
    mem_part = pltpu.VMEM((planes, mem_rows, width), low)
    mem_low = pltpu.VMEM((mem_len, width), low)
    square = pltpu.VMEM((width, width), low)
    vec = pltpu.VMEM((8, width), f32)
    copies = 6 + 2 * (batches // 2) + 5 * planes + 2 * batches + n
    qx, kx, raw, pk, pv, pkt, ot, stat = (pltpu.VMEM(value.shape, value.dtype) for value in saved)
    return pl.pallas_call(
        functools.partial(self_backward_kernel, n, batches),
        out_shape=(
            jax.ShapeDtypeStruct((length, width), low),
            jax.ShapeDtypeStruct((mem_rows, width), low),
            jax.ShapeDtypeStruct((PREFIX_ROWS, 2 * width), f32),
            jax.ShapeDtypeStruct((8, width), f32),
            jax.ShapeDtypeStruct((2, batches // 2, 2, planes, sum_rows, LANES), low),
        ),
        in_specs=[anywhere] * 19,
        out_specs=(vmem, vmem, vmem, vmem, anywhere),
        scratch_shapes=[
            pltpu.VMEM((heads, n, HD, length), low),
            qx,
            kx,
            raw,
            pltpu.VMEM((heads, HD, whole), low),
            pltpu.VMEM((heads, whole, HD), low),
            pltpu.VMEM((heads, HD, whole), low),
            pltpu.VMEM((heads, whole, 2 * HD), low),
            pk,
            pv,
            pkt,
            ot,
            stat,
            pltpu.VMEM((3, width, width), low),
            pltpu.VMEM((planes, heads, HD, 2 * length), f32),
            pltpu.VMEM((heads, whole, 2 * HD), f32),
            pltpu.VMEM((n, heads, 3, HD, length), low),
            pltpu.VMEM((3, n, heads, HD, length), low),
            pltpu.VMEM((heads, PREFIX_ROWS, 2 * HD), f32),
            pltpu.VMEM((batches, heads, PREFIX_ROWS, 2 * HD), f32),
            pltpu.VMEM((heads, PREFIX_ROWS, 2 * HD), low),
            pltpu.VMEM((n, heads, PREFIX_ROWS, 2 * HD), low),
            pltpu.VMEM((sums.shape[0] // 2, LANES), low),
            pltpu.VMEM((sums.shape[0] // 2, LANES), low),
            pltpu.VMEM((batches // 2, sums.shape[0] // batches, LANES), low),
            pltpu.VMEM((planes * sum_rows, LANES), low),
            pltpu.VMEM((planes, sum_rows, LANES), low),
            pltpu.VMEM((2, batches // 2, 2, planes, sum_rows, LANES), low),
            mem_low,
            mem_low,
            square,
            square,
            pltpu.VMEM((planes, 2, mem_rows, width), low),
            mem_part,
            mem_part,
            mem_part,
            pltpu.VMEM((batches, 8, width), f32),
            vec,
            pltpu.VMEM((2, 8, width), f32),
            pltpu.VMEM((16, width // 2), low),
            pltpu.VMEM((planes, 16, width // 2), low),
            pltpu.VMEM((width, length), f32),
            pltpu.VMEM((length, width), f32),
            dma((heads, n)),
            dma((heads, n)),
            dma((2, heads, n)),
            dma((2, heads, n)),
            dma((19,)),
            dma((copies,)),
            dma((copies,)),
        ],
        compiler_params=pltpu.CompilerParams(
            collective_id=1, has_side_effects=True, vmem_limit_bytes=VMEM_BYTES
        ),
        name="self_backward",
    )(
        first_grad,
        out_grad,
        sums.reshape(2, -1, LANES),
        *mem_grads,
        *mem_weights,
        vecs,
        *saved,
        *weights,
    )


def both_parts(value):
    high = value.astype(jnp.bfloat16).astype(jnp.float32)
    return jnp.concatenate([high, value - high], axis=0).astype(jnp.bfloat16)


def finish_kernel(
    full_in,
    vecs_ref,
    pkv_ref,
    emb_ref,
    first_in,
    fbias_ref,
    second_in,
    token_in,
    mem_in,
    embed_out,
    first_out,
    fbias_out,
    second_out,
    sbias_out,
    down_out,
    dbias_out,
    raise_out,
    rbias_out,
    gain_out,
    shift_out,
    token_out,
    mem_out,
    full_ref,
    first_ref,
    second_ref,
    token_ref,
    mem_ref,
    first_grad,
    second_grad,
    down_grad,
    raise_grad,
    emb,
    hidden,
    out_sem,
    in_sem,
):
    f32 = jnp.float32
    low = jnp.bfloat16
    width = emb_ref.shape[1]
    down = dbias_out.shape[1]
    count = emb_ref.shape[0]
    first = down * width // LANES
    loads = [
        pltpu.make_async_copy(source, target, in_sem.at[index])
        for index, (source, target) in enumerate(
            (
                (full_in.at[first:], full_ref.at[first:]),
                (full_in.at[:first], full_ref.at[:first]),
                (first_in, first_ref),
                (second_in, second_ref),
                (token_in, token_ref),
                (mem_in, mem_ref),
            )
        )
    ]
    for load in loads:
        load.start()
    saves = []

    def save(source, target, rows=None):
        if rows is not None:
            source, target = source.at[rows], target.at[rows]
        copy = pltpu.make_async_copy(source, target, out_sem.at[len(saves)])
        copy.start()
        saves.append(copy)

    loads[0].wait()
    for index in range(width // LANES):
        raise_grad[:, index * LANES : (index + 1) * LANES] = full_ref[
            first + index * down : first + (index + 1) * down, :
        ].astype(f32)
    save(raise_grad, raise_out)
    loads[1].wait()
    for index in range(down // LANES):
        down_grad[:, index * LANES : (index + 1) * LANES] = full_ref[
            index * width : (index + 1) * width, :
        ].astype(f32)
    save(down_grad, down_out)
    for load in loads[4:]:
        load.wait()
    save(token_ref, token_out)
    save(mem_ref, mem_out)
    loads[2].wait()
    emb[...] = jnp.zeros_like(emb)
    emb[:count, :] = emb_ref[...].astype(f32)
    emb_low = emb[...].astype(low)
    row = lax.broadcasted_iota(jnp.int32, hidden.shape, 0)
    hidden[...] = jnp.where(
        row < count, jnp.tanh(dot_nn(emb_low, first_ref[...]) + fbias_ref[...]), 0.0
    )
    value = hidden[...]
    prefix = pkv_ref[...]
    parts = both_parts(prefix)
    hidden_twice = jnp.concatenate([value, value], axis=0).T.astype(low)
    tile = 128
    for index in range(second_grad.shape[0] // tile):
        here = slice(index * tile, (index + 1) * tile)
        second_grad[here, :] = dot_nn(hidden_twice[here, :], parts)
        save(second_grad, second_out, here)
    sbias_out[...] = jnp.sum(prefix, axis=0, keepdims=True)
    loads[3].wait()
    grad = dot_nt(parts, second_ref[...])
    grad = (grad[:PREFIX_ROWS] + grad[PREFIX_ROWS:]) * (1.0 - value * value)
    fbias_out[...] = jnp.sum(grad, axis=0, keepdims=True)
    parts = both_parts(grad)
    emb_twice = jnp.concatenate([emb[...], emb[...]], axis=0).T.astype(low)
    first_grad[...] = dot_nn(emb_twice, parts)
    save(first_grad, first_out)
    back = dot_nt(parts, first_ref[...])
    embed_out[...] = (back[:PREFIX_ROWS] + back[PREFIX_ROWS:])[:count, :]
    rbias_out[...] = vecs_ref[0:1, :]
    dbias_out[...] = vecs_ref[1:2, :down]
    gain_out[...] = vecs_ref[2:5, :]
    shift_out[...] = vecs_ref[5:8, :]
    for copy in saves:
        copy.wait()


def finish(full, vecs, prefix_grad, embed, first, first_bias, second, down, token_grad, memory_grad):
    f32 = jnp.float32
    count, width = embed.shape
    hidden = first.shape[1]
    vmem = pl.BlockSpec(memory_space=pltpu.VMEM)
    anywhere = pl.BlockSpec(memory_space=pl.ANY)
    shapes = (
        (count, width),
        (width, hidden),
        (1, hidden),
        (hidden, 2 * width),
        (1, 2 * width),
        (width, down),
        (1, down),
        (down, width),
        (1, width),
        (3, width),
        (3, width),
    )
    return pl.pallas_call(
        finish_kernel,
        out_shape=tuple(jax.ShapeDtypeStruct(shape, f32) for shape in shapes)
        + tuple(
            jax.ShapeDtypeStruct(value.shape, value.dtype) for value in (token_grad, memory_grad)
        ),
        in_specs=[anywhere, vmem, vmem, vmem, anywhere, vmem, anywhere, anywhere, anywhere],
        out_specs=(
            vmem,
            anywhere,
            vmem,
            anywhere,
            vmem,
            anywhere,
            vmem,
            anywhere,
            vmem,
            vmem,
            vmem,
            anywhere,
            anywhere,
        ),
        scratch_shapes=[
            pltpu.VMEM(full.shape, jnp.bfloat16),
            pltpu.VMEM(first.shape, jnp.bfloat16),
            pltpu.VMEM(second.shape, jnp.bfloat16),
            pltpu.VMEM(token_grad.shape, token_grad.dtype),
            pltpu.VMEM(memory_grad.shape, memory_grad.dtype),
            pltpu.VMEM((width, hidden), f32),
            pltpu.VMEM((hidden, 2 * width), f32),
            pltpu.VMEM((width, down), f32),
            pltpu.VMEM((down, width), f32),
            pltpu.VMEM((PREFIX_ROWS, width), f32),
            pltpu.VMEM((PREFIX_ROWS, hidden), f32),
            pltpu.SemaphoreType.DMA((5 + hidden // 128,)),
            pltpu.SemaphoreType.DMA((6,)),
        ],
        compiler_params=pltpu.CompilerParams(vmem_limit_bytes=VMEM_BYTES),
        name="finish",
    )(full, vecs, prefix_grad, embed, first, first_bias, second, token_grad, memory_grad)


def gelu_pair(value):
    size = jnp.abs(value)
    step = 1.0 / (1.0 + (0.3275911 * 0.7071067811865476) * size)
    bell = jnp.exp(-0.5 * value * value)
    poly = step * (
        0.127414796
        + step
        * (-0.142248368 + step * (0.7107068705 + step * (-0.7265760135 + step * 0.5307027145)))
    )
    act = jnp.maximum(value, 0.0) - size * (poly * bell)
    turn = bell * (0.3989422804014327 * size - poly)
    return act, jnp.where(value >= 0.0, 1.0 + turn, -turn)


def normed(value):
    center = jnp.mean(value, axis=-1, keepdims=True)
    centered = value - center
    scale = lax.rsqrt(jnp.mean(centered * centered, axis=-1, keepdims=True) + norm_eps)
    return centered * scale, scale


def norm_back(grad, scale, unit):
    return scale * (
        grad
        - jnp.mean(grad, axis=-1, keepdims=True)
        - unit * jnp.mean(grad * unit, axis=-1, keepdims=True)
    )


def middle_kernel(
    tok_in,
    att_in,
    cot_in,
    mkey_in,
    mvalue_in,
    gain_ref,
    shift_ref,
    dbias_ref,
    rbias_ref,
    wo_in,
    wcq_in,
    wco_in,
    wd_in,
    wr_in,
    win_in,
    wout_in,
    layer_out,
    fgrad_out,
    ograd_out,
    mkey_out,
    mvalue_out,
    sums_out,
    vecs_ref,
    tok_ref,
    att_ref,
    cot_ref,
    mkey_ref,
    mvalue_ref,
    out_ref,
    fgrad_ref,
    ograd_ref,
    sums_ref,
    wo,
    wcq,
    wco,
    wd,
    wr,
    win,
    wout,
    unit_one,
    unit_two,
    work,
    total,
    scale_one,
    scale_two,
    low_one,
    low_two,
    low_three,
    query,
    crossed,
    weights,
    slopes,
    acts,
    down_act,
    down_slope,
    down_grad,
    load_sem,
    win_sem,
    wout_sem,
    out_sem,
):
    length, width = tok_ref.shape
    resident = len(win.shape) == 2
    tile = 512 if resident else win.shape[2]
    tiles = win_in.shape[1] // tile
    slots = tiles if resident else win.shape[0]
    rows_step = 128
    low = jnp.bfloat16
    f32 = jnp.float32

    sources = (
        att_in,
        wo_in,
        tok_in,
        wcq_in,
        mkey_in,
        mvalue_in,
        wco_in,
        wd_in,
        wr_in,
        cot_in,
    )
    targets = (att_ref, wo, tok_ref, wcq, mkey_ref, mvalue_ref, wco, wd, wr, cot_ref)
    loads = [
        pltpu.make_async_copy(source, target, load_sem.at[index])
        for index, (source, target) in enumerate(zip(sources, targets))
    ]

    def win_load(which):
        slot = which % slots
        target = win.at[:, rows_of(which, tile)] if resident else win.at[slot]
        return pltpu.make_async_copy(win_in.at[:, rows_of(which, tile)], target, win_sem.at[slot])

    def wout_load(which):
        slot = which % slots
        target = wout.at[rows_of(which, tile), :] if resident else wout.at[slot]
        return pltpu.make_async_copy(wout_in.at[rows_of(which, tile), :], target, wout_sem.at[slot])

    for load in loads[:7]:
        load.start()

    def by_columns(extent, step, body):
        def one(index, carry):
            body(pl.ds(pl.multiple_of(index * step, step), step))
            return carry

        lax.fori_loop(0, extent // step, one, 0)

    def by_rows(body, init=0):
        def one(index, carry):
            return body(rows_of(index, rows_step), carry)

        return lax.fori_loop(0, length // rows_step, one, init)

    cols = 512
    half = width // 2

    for load in loads[:3]:
        load.wait()
    for load in loads[7:]:
        load.start()
    for which in range(slots):
        win_load(which).start()
    for which in range(slots):
        wout_load(which).start()

    def project_out(here):
        work[:, here] = tok_ref[:, here].astype(f32) + dot_nn(att_ref[...], wo[:, here])

    by_columns(width, cols, project_out)

    def first_norm(here, carry):
        unit, scale = normed(work[here, :])
        unit_one[here, :] = unit
        scale_one[here, :] = scale
        value = unit * gain_ref[0:1, :] + shift_ref[0:1, :]
        work[here, :] = value
        low_one[here, :] = value.astype(low)
        return carry

    by_rows(first_norm)

    loads[3].wait()

    def project_query(here):
        query[:, here] = dot_nn(low_one[...], wcq[:, here]).astype(low)

    by_columns(width, cols, project_query)
    per_block = LANES // HD

    def stacked(value):
        return jnp.concatenate(
            [jnp.where(head_lanes(value.shape, head), value, 0.0) for head in range(per_block)],
            axis=0,
        ).astype(low)

    def unstacked(value):
        return jnp.concatenate(
            [
                value[head * HD : (head + 1) * HD, head * length : (head + 1) * length]
                for head in range(per_block)
            ],
            axis=0,
        )

    def block_queries(here):
        return stacked(query[:, here].astype(f32) * 0.125)

    def cross_forward(block):
        here = rows_of(block, LANES)
        scores = dot_nt(mkey_ref[:, here], block_queries(here))
        raised = jnp.exp(scores - jnp.max(scores, axis=0, keepdims=True))
        share = 1.0 / jnp.sum(raised, axis=0, keepdims=True)
        weight = (raised * share).astype(low)
        weights[block] = weight
        values = mvalue_ref[:, here].astype(f32).T.astype(low)
        crossed[:, here] = unstacked(dot_nn(values, weight)).T.astype(low)

    loads[4].wait()
    loads[5].wait()

    def cross_forward_both(step, carry):
        cross_forward(2 * step)
        cross_forward(2 * step + 1)
        return carry

    lax.fori_loop(0, width // LANES // 2, cross_forward_both, 0)

    loads[6].wait()

    def project_crossed(here):
        work[:, here] += dot_nn(crossed[...], wco[:, here])

    by_columns(width, cols, project_crossed)

    def second_norm(here, carry):
        unit, scale = normed(work[here, :])
        unit_two[here, :] = unit
        scale_two[here, :] = scale
        value = unit * gain_ref[1:2, :] + shift_ref[1:2, :]
        work[here, :] = value
        low_two[here, :] = value.astype(low)
        return carry

    by_rows(second_norm)

    step_cols = 512

    def feed_part(here, source):
        act, slope = gelu_pair(dot_nn(low_two[...], source))
        slopes[:, here] = slope.astype(low)
        return act.astype(low)

    if resident:

        def feed_forward(which, carry):
            here = rows_of(which, step_cols)

            @pl.when(which % (tile // step_cols) == 0)
            def _():
                win_load(which // (tile // step_cols)).wait()

            acts[:, here] = feed_part(here, win[:, here])
            return carry

        lax.fori_loop(0, tiles * tile // step_cols, feed_forward, 0)
        for which in range(tiles):
            wout_load(which).wait()

        def feed_out_part(here):
            total[:, here] = dot_nn(acts[...], wout[:, here])

        by_columns(width, step_cols, feed_out_part)
    else:
        total[...] = jnp.zeros_like(total)

        def feed_forward(which, carry):
            slot = lax.rem(which, slots)
            win_load(which).wait()
            wout_load(which).wait()
            total[...] += dot_nn(feed_part(rows_of(which, tile), win[slot]), wout[slot])

            @pl.when(which + slots < tiles)
            def _():
                win_load(which + slots).start()
                wout_load(which + slots).start()

            return carry

        lax.fori_loop(0, tiles, feed_forward, 0)

    loads[7].wait()
    loads[8].wait()
    loads[9].wait()
    act, slope = gelu_pair(dot_nn(low_two[...], wd[...]) + dbias_ref[...])
    down_act[...] = act.astype(low)
    down_slope[...] = slope.astype(low)

    def project_raise(here):
        work[:, here] += total[:, here] + 4.0 * (
            dot_nn(down_act[...], wr[:, here]) + rbias_ref[:, here]
        )

    by_columns(width, cols, project_raise)
    nothing = jnp.zeros((1, width), f32)

    def third_norm(here, carry):
        gain_sum, shift_sum, bias_sum = carry
        unit, scale = normed(work[here, :])
        gain = gain_ref[2:3, :]
        out_ref[here, :] = (unit * gain + shift_ref[2:3, :]).astype(low)
        grad = cot_ref[here, :].astype(f32)
        back = norm_back(grad * gain, scale, unit)
        total[here, :] = back
        back_low = back.astype(low)
        low_three[here, :] = back_low
        return (
            gain_sum + jnp.sum(grad * unit, axis=0, keepdims=True),
            shift_sum + jnp.sum(grad, axis=0, keepdims=True),
            bias_sum + jnp.sum(back_low.astype(f32), axis=0, keepdims=True),
        )

    gain_three, shift_three, bias_sum = by_rows(third_norm, (nothing, nothing, nothing))
    saves = []

    def save(source, target):
        copy = pltpu.make_async_copy(source, target, out_sem.at[len(saves)])
        copy.start()
        saves.append(copy)

    save(out_ref, layer_out)
    vecs_ref[0:1, :] = 4.0 * bias_sum

    back = 4.0 * dot_nt(low_three[...], wr[...]) * down_slope[...].astype(f32)
    back_low = back.astype(low)
    down_grad[...] = back_low
    vecs_ref[1:2, :] = jnp.concatenate(
        [
            jnp.sum(back_low.astype(f32), axis=0, keepdims=True),
            jnp.zeros((1, width - wd.shape[1]), f32),
        ],
        axis=1,
    )
    down = wd.shape[1]
    raise_sum = 4.0 * dot_tn(down_act[...], low_three[...])
    for index in range(width // LANES):
        sums_ref[pl.ds(down * width // LANES + index * down, down), :] = raise_sum[
            :, index * LANES : (index + 1) * LANES
        ].astype(low)
    down_sum = dot_tn(low_two[...], down_grad[...])
    for index in range(down // LANES):
        sums_ref[index * width : (index + 1) * width, :] = down_sum[
            :, index * LANES : (index + 1) * LANES
        ].astype(low)

    save(sums_ref, sums_out)

    if resident:

        def feed_slope(here):
            acts[:, here] = (
                dot_nt(low_three[...], wout[here, :]) * slopes[:, here].astype(f32)
            ).astype(low)

        by_columns(win_in.shape[1], step_cols, feed_slope)

        def feed_in_part(here):
            total[:, here] += dot_nt(acts[...], win[here, :])

        by_columns(width, step_cols, feed_in_part)
    else:

        def feed_backward(step, carry):
            which = tiles - 1 - step
            slot = lax.rem(which, slots)
            here = rows_of(which, tile)

            @pl.when(which < tiles - slots)
            def _():
                wout_load(which).wait()
                win_load(which).wait()

            grad = dot_nt(low_three[...], wout[slot]) * slopes[:, here].astype(f32)
            total[...] += dot_nt(grad.astype(low), win[slot])

            @pl.when(which >= slots)
            def _():
                win_load(which - slots).start()
                wout_load(which - slots).start()

            return carry

        lax.fori_loop(0, tiles, feed_backward, 0)

    def down_back(here):
        total[:, here] += dot_nt(down_grad[...], wd[here, :])

    by_columns(width, cols, down_back)

    def second_back(here, carry):
        gain_sum, shift_sum = carry
        grad = total[here, :]
        unit = unit_two[here, :]
        back = norm_back(grad * gain_ref[1:2, :], scale_two[here, :], unit)
        total[here, :] = back
        low_one[here, :] = back.astype(low)
        return (
            gain_sum + jnp.sum(grad * unit, axis=0, keepdims=True),
            shift_sum + jnp.sum(grad, axis=0, keepdims=True),
        )

    gain_two, shift_two = by_rows(second_back, (nothing, nothing))

    def crossed_back(here):
        crossed[:, here] = dot_nt(low_one[...], wco[here, :]).astype(low)

    by_columns(width, cols, crossed_back)

    def cross_backward(block):
        here = rows_of(block, LANES)
        grads = stacked(crossed[:, here].astype(f32))
        keys = mkey_ref[:, here].astype(f32).T.astype(low)
        slope = dot_nt(mvalue_ref[:, here], grads)
        weight_low = weights[block]
        weight = weight_low.astype(f32)
        slope = weight * (slope - jnp.sum(weight * slope, axis=0, keepdims=True))
        slope = slope.astype(low)
        queries = block_queries(here)
        mkey_ref[:, here] = dot_nn(slope, queries).astype(low)
        mvalue_ref[:, here] = dot_nn(weight_low, grads).astype(low)
        query[:, here] = (unstacked(dot_nn(keys, slope)) * 0.125).T.astype(low)

    def cross_backward_both(step, carry):
        cross_backward(2 * step)
        cross_backward(2 * step + 1)
        return carry

    lax.fori_loop(0, width // LANES // 2, cross_backward_both, 0)
    save(mkey_ref, mkey_out)
    save(mvalue_ref, mvalue_out)

    def query_back(here):
        total[:, here] += dot_nt(query[...], wcq[here, :])

    by_columns(width, cols, query_back)

    def first_back(here, carry):
        gain_sum, shift_sum = carry
        grad = total[here, :]
        unit = unit_one[here, :]
        back = norm_back(grad * gain_ref[0:1, :], scale_one[here, :], unit)
        fgrad_ref[here, :] = back
        low_one[here, :] = back.astype(low)
        return (
            gain_sum + jnp.sum(grad * unit, axis=0, keepdims=True),
            shift_sum + jnp.sum(grad, axis=0, keepdims=True),
        )

    gain_one, shift_one = by_rows(first_back, (nothing, nothing))
    save(fgrad_ref, fgrad_out)

    for index in range(width // cols):
        here = slice(index * cols, (index + 1) * cols)
        ograd_ref[here, :] = dot_nt(low_one[...], wo[here, :]).T.astype(low)
        save(ograd_ref.at[here], ograd_out.at[here])
    for index, vector in enumerate(
        (gain_one, gain_two, gain_three, shift_one, shift_two, shift_three)
    ):
        vecs_ref[2 + index : 3 + index, :] = vector
    for copy in saves:
        copy.wait()


def middle(
    tokens, attended, cotangent, mem_key, mem_value, gains, shifts, down_bias, raise_bias, weights
):
    length, width = tokens.shape
    mem_len = mem_key.shape[0]
    down = weights[3].shape[1]
    feed = weights[5].shape[1]
    tile = 512 if mem_len <= 512 else 128
    resident = mem_len <= 512
    slots = feed // tile if resident else 2
    low = jnp.bfloat16
    f32 = jnp.float32
    vmem = pl.BlockSpec(memory_space=pltpu.VMEM)
    anywhere = pl.BlockSpec(memory_space=pl.ANY)
    square = pltpu.VMEM((width, width), low)
    wide = pltpu.VMEM((length, width), f32)
    narrow = pltpu.VMEM((length, width), low)
    return pl.pallas_call(
        middle_kernel,
        out_shape=(
            jax.ShapeDtypeStruct((length, width), low),
            jax.ShapeDtypeStruct((length, width), f32),
            jax.ShapeDtypeStruct((width, length), low),
            jax.ShapeDtypeStruct((mem_len, width), low),
            jax.ShapeDtypeStruct((mem_len, width), low),
            jax.ShapeDtypeStruct((2 * down * width // LANES, LANES), low),
            jax.ShapeDtypeStruct((8, width), f32),
        ),
        in_specs=[anywhere] * 5 + [vmem] * 4 + [anywhere] * 7,
        out_specs=(anywhere,) * 6 + (vmem,),
        scratch_shapes=[
            narrow,
            narrow,
            narrow,
            pltpu.VMEM((mem_len, width), low),
            pltpu.VMEM((mem_len, width), low),
            narrow,
            wide,
            pltpu.VMEM((width, length), low),
            pltpu.VMEM((2 * down * width // LANES, LANES), low),
            square,
            square,
            square,
            pltpu.VMEM((width, down), low),
            pltpu.VMEM((down, width), low),
            pltpu.VMEM((width, feed) if resident else (slots, width, tile), low),
            pltpu.VMEM((feed, width) if resident else (slots, tile, width), low),
            wide,
            wide,
            wide,
            wide,
            pltpu.VMEM((length, 1), f32),
            pltpu.VMEM((length, 1), f32),
            narrow,
            narrow,
            narrow,
            narrow,
            narrow,
            pltpu.VMEM((width // LANES, mem_len, LANES // HD * length), low),
            pltpu.VMEM((length, feed), low),
            pltpu.VMEM((length, feed) if resident else (16, LANES), low),
            pltpu.VMEM((length, down), low),
            pltpu.VMEM((length, down), low),
            pltpu.VMEM((length, down), low),
            pltpu.SemaphoreType.DMA((10,)),
            pltpu.SemaphoreType.DMA((slots,)),
            pltpu.SemaphoreType.DMA((slots,)),
            pltpu.SemaphoreType.DMA((5 + width // 512,)),
        ],
        compiler_params=pltpu.CompilerParams(vmem_limit_bytes=VMEM_BYTES + 3 * 1024 * 1024),
        name="middle",
    )(tokens, attended, cotangent, mem_key, mem_value, gains, shifts, down_bias, raise_bias, *weights)


def per_device(
    tokens,
    memory,
    segment_ids,
    padding_mask,
    cotangent,
    prefix_embed,
    prefix_first,
    first_bias,
    prefix_second,
    second_bias,
    adapter_down,
    down_bias,
    adapter_raise,
    raise_bias,
    norm_gain,
    norm_shift,
    self_query,
    self_key,
    self_value,
    self_output,
    cross_query,
    cross_key,
    cross_value,
    cross_output,
    feed_in,
    feed_out,
):
    row_count, length, model_width = tokens.shape
    flat_rows = row_count * length
    n = lax.axis_size("seq")
    batches = lax.axis_size("batch")
    down = adapter_down.shape[1]
    attended, mem_key, mem_value, *saved = self_forward(
        n,
        segment_ids,
        padding_mask,
        tokens.reshape(flat_rows, model_width),
        (self_query, self_key, self_value),
        (
            prefix_embed,
            prefix_first,
            first_bias.reshape(1, -1),
            prefix_second,
            second_bias.reshape(1, -1),
        ),
        memory.reshape(-1, model_width),
        (cross_key, cross_value),
    )
    layer_output, first_grad, out_grad, *mem_grads, weight_sums, vector_sums = middle(
        tokens.reshape(flat_rows, model_width),
        attended,
        cotangent.reshape(flat_rows, model_width),
        mem_key,
        mem_value,
        norm_gain,
        norm_shift,
        down_bias.reshape(1, -1),
        raise_bias.reshape(1, -1),
        (
            self_output,
            cross_query,
            cross_output,
            adapter_down,
            adapter_raise,
            feed_in,
            feed_out,
        ),
    )
    layer_output = layer_output.reshape(row_count, length, model_width)
    token_grad, memory_grad, prefix_grad, vector_sums, full_sums = self_backward(
        n,
        batches,
        first_grad,
        out_grad.reshape(n, -1, HD, length),
        weight_sums,
        mem_grads,
        (cross_key, cross_value),
        vector_sums,
        saved,
        (self_query, self_key, self_value),
    )
    *replicated, token_grad, memory_grad = finish(
        full_sums.reshape(-1, LANES),
        vector_sums,
        prefix_grad,
        prefix_embed,
        prefix_first,
        first_bias.reshape(1, -1),
        prefix_second,
        down,
        token_grad,
        memory_grad,
    )
    token_grad = token_grad.reshape(row_count, length, model_width)
    memory_grad = memory_grad.reshape(memory.shape)
    replicated = [
        value.reshape(-1) if value.shape[0] == 1 else value for value in replicated
    ]
    return (layer_output, token_grad, memory_grad, *replicated)


def solution(mesh):
    placed = (
        P("batch", "seq", None),
        P("batch", "seq", None),
        P("batch", "seq"),
        P("batch", "seq"),
        P("batch", "seq", None),
        P(),
        P(),
        P(),
        P(),
        P(),
        P(),
        P(),
        P(),
        P(),
        P(),
        P(),
        P(),
        P(),
        P(),
        P(),
        P(),
        P(),
        P(),
        P(),
        P(),
        P(),
    )
    return jax.shard_map(
        per_device,
        mesh=mesh,
        in_specs=placed,
        out_specs=(
            P("batch", "seq", None),
            P("batch", "seq", None),
            P("batch", "seq", None),
            P(),
            P(),
            P(),
            P(),
            P(),
            P(),
            P(),
            P(),
            P(),
            P(),
            P(),
        ),
        check_vma=False,
    )
```

```python
import functools

import jax
import jax.numpy as jnp
from jax import lax
from jax.experimental import pallas as pl
from jax.experimental.pallas import tpu as pltpu
from jax.sharding import PartitionSpec as P

H = 16
HD = 64
LANES = 128
PREFIX_ROWS = 32
VMEM_BYTES = 60 * 1024 * 1024
SUM_ROWS = 16
MESH = pl.DeviceIdType.MESH

masked_score = -1e30
norm_eps = 1e-05

def dot_nn(left, right):
    return lax.dot_general(
        left, right, (((1,), (0,)), ((), ())), preferred_element_type=jnp.float32
    )


def dot_nt(left, right):
    return lax.dot_general(
        left, right, (((1,), (1,)), ((), ())), preferred_element_type=jnp.float32
    )


def dot_tn(left, right):
    return lax.dot_general(
        left, right, (((0,), (0,)), ((), ())), preferred_element_type=jnp.float32
    )


def remote(source, target, send_sem, recv_sem, axis, peer):
    return pltpu.make_async_remote_copy(
        src_ref=source,
        dst_ref=target,
        send_sem=send_sem,
        recv_sem=recv_sem,
        device_id={axis: peer},
        device_id_type=MESH,
    )


def enter(sizes):
    barrier = pltpu.get_barrier_semaphore()
    for axis, size in sizes.items():
        for other in range(size):

            @pl.when(other != lax.axis_index(axis))
            def _():
                pl.semaphore_signal(barrier, inc=1, device_id={axis: other}, device_id_type=MESH)

    pl.semaphore_wait(barrier, sum(sizes.values()) - len(sizes))


def others(size, mine, body):
    for other in range(size):

        @pl.when(other != mine)
        def _():
            body(other)


def rows_of(index, size):
    return pl.ds(pl.multiple_of(index * size, size), size)


def span_of(start, size):
    return pl.ds(pl.multiple_of(start, LANES), size)


def own_columns(ref, first, me, width):
    if width % LANES == 0:
        return ref[:, pl.ds(pl.multiple_of(first + me * width, LANES), width)].astype(jnp.float32)
    share = LANES // width
    block = ref[:, pl.ds(pl.multiple_of(first + me // share * LANES, LANES), LANES)].astype(
        jnp.float32
    )
    picked = block[:, :width]
    for part in range(1, share):
        picked = jnp.where(me % share == part, block[:, part * width : (part + 1) * width], picked)
    return picked


def head_lanes(shape, head):
    lane = lax.broadcasted_iota(jnp.int32, shape, 1)
    return (lane >= head * HD) & (lane < (head + 1) * HD)


def self_forward_kernel(
    n,
    seg_ref,
    pad_ref,
    tok_ref,
    wq_in,
    wk_in,
    wv_in,
    emb_ref,
    first_in,
    fbias_ref,
    second_in,
    sbias_ref,
    mem_ref,
    wck_in,
    wcv_in,
    att_ref,
    mkey_out,
    mvalue_out,
    qx_out,
    kx_out,
    raw_out,
    pk_out,
    pv_out,
    pkt_out,
    ot_out,
    lse_out,
    send,
    recv,
    meta_send,
    meta,
    kx,
    qx,
    vt,
    hidden,
    pk,
    pv,
    pkt,
    pvt,
    stat,
    acc,
    o_send,
    o_recv,
    mem_all,
    wck,
    wcv,
    mkey_ref,
    mvalue_ref,
    wq_ref,
    wk_ref,
    wv_ref,
    first_ref,
    second_ref,
    send_sem,
    recv_sem,
    meta_send_sem,
    meta_recv_sem,
    o_send_sem,
    o_recv_sem,
    mem_send_sem,
    mem_recv_sem,
    out_sem,
    weight_sem,
    in_sem,
):
    low = jnp.bfloat16
    f32 = jnp.float32
    me = lax.axis_index("seq")
    length, width = tok_ref.shape
    group = width // n
    heads = group // HD
    plane = 2 * length
    planes = n // 2
    block = 2 * LANES
    per_block = block // group
    blocks = width // block
    my_plane = me // 2
    my_side = lax.rem(me, 2)

    upward = my_plane >= planes // 2
    turn_sign = jnp.where(upward, 1, -1)

    def plane_after(step):
        return lax.rem(my_plane + planes + turn_sign * step, planes)

    def meta_copy(peer, slot):
        return remote(
            meta_send, meta.at[slot], meta_send_sem.at[peer], meta_recv_sem.at[slot], "seq", peer
        )

    def qkv_copy(head, peer, slot):
        return remote(
            send.at[peer, head],
            recv.at[head, slot],
            send_sem.at[head, peer],
            recv_sem.at[head, slot],
            "seq",
            peer,
        )

    def out_copy(head, peer, slot):
        return remote(
            o_send.at[head, peer],
            o_recv.at[slot, head],
            o_send_sem.at[head, peer],
            o_recv_sem.at[head, slot],
            "seq",
            peer,
        )

    def mem_along(which, toward):
        part = mem_all.at[which, my_side]
        return remote(
            part,
            part,
            mem_send_sem.at[(toward + 1) // 2, which],
            mem_recv_sem.at[which],
            "seq",
            me + 2 * toward,
        )

    def mem_across(side):
        part = mem_all.at[:, side]
        return remote(
            part,
            part,
            mem_send_sem.at[0, planes],
            mem_recv_sem.at[planes],
            "seq",
            me + 1 - 2 * my_side,
        )

    def mem_hops(hop, body):
        for toward in (1, -1):
            which = my_plane - toward * hop
            ahead = my_plane + toward

            @pl.when((which >= 0) & (which < planes) & (ahead >= 0) & (ahead < planes))
            def _():
                body(mem_along(which, toward))

    def mem_arrivals(hop):
        for toward in (1, -1):
            which = my_plane - toward * hop

            @pl.when((which >= 0) & (which < planes))
            def _():
                mem_along(which, -toward).wait_recv()

    def block_at(step):
        if blocks >= planes:
            share = blocks // planes
            return plane_after(1 + step // share) * share + step % share
        return lax.rem(me // per_block + 1 + step, blocks)

    def weight_load(step, which):
        columns = rows_of(block_at(step), block)
        source = (wq_in, wk_in, wv_in)[which]
        target = (wq_ref, wk_ref, wv_ref)[which]
        return pltpu.make_async_copy(
            source.at[:, columns], target.at[:, columns], weight_sem.at[step, which]
        )

    for step in range(blocks):
        for which in range(3):
            weight_load(step, which).start()
    loads = [
        pltpu.make_async_copy(source, target, in_sem.at[index])
        for index, (source, target) in enumerate(
            ((first_in, first_ref), (second_in, second_ref), (wck_in, wck), (wcv_in, wcv))
        )
    ]
    for load in loads:
        load.start()
    segments = seg_ref[...]
    tags = jnp.where(pad_ref[...] == 1, segments, -1)
    row = lax.broadcasted_iota(jnp.int32, meta_send.shape, 0)
    meta_send[...] = jnp.where(row == 0, segments, tags)
    mem_all[my_plane, my_side] = mem_ref[...]
    enter({"seq": n})
    others(n, me, lambda peer: meta_copy(peer, me).start())
    meta[me] = meta_send[...]

    for step in range(blocks):
        at = block_at(step)
        columns = rows_of(at, block)
        for which, weight in enumerate((wq_ref, wk_ref, wv_ref)):
            weight_load(step, which).wait()
            piece = dot_nn(tok_ref[...], weight[:, columns]).T.astype(low)
            for part in range(per_block):
                for head in range(heads):
                    first = part * group + head * HD
                    send[at * per_block + part, head, which] = piece[first : first + HD]
        for part in range(per_block):
            peer = at * per_block + part

            @pl.when(peer != me)
            def _():
                qkv_copy(0, peer, me).start()

            @pl.when(peer == me)
            def _():
                for head in range(heads):
                    recv[head, me] = send[peer, head]

    mem_hops(0, lambda copy: copy.start())
    loads[0].wait()
    loads[1].wait()
    hidden[...] = jnp.zeros_like(hidden)
    hidden[: emb_ref.shape[0], :] = jnp.tanh(dot_nn(emb_ref[...], first_ref[...]) + fbias_ref[...])
    hidden_low = hidden[...].astype(low)
    prefix_key = dot_nn(hidden_low, own_columns(second_ref, 0, me, group).astype(low)) + own_columns(
        sbias_ref, 0, me, group
    )
    prefix_value = dot_nn(
        hidden_low, own_columns(second_ref, width, me, group).astype(low)
    ) + own_columns(sbias_ref, width, me, group)
    prefix_row = lax.broadcasted_iota(jnp.int32, (PREFIX_ROWS, HD), 0)
    prefix_open = jnp.where(prefix_row < emb_ref.shape[0], 0.0, masked_score)
    for head in range(heads):
        here = slice(head * HD, (head + 1) * HD)
        pk[head] = jnp.concatenate([prefix_key[:, here], prefix_open], axis=1).astype(low)
        pv[head] = prefix_value[:, here].astype(low)
    pkt[...] = prefix_key.T.astype(low).reshape(heads, HD, PREFIX_ROWS)
    pvt[:, :HD, :] = prefix_value.T.astype(low).reshape(heads, HD, PREFIX_ROWS)
    pvt[:, HD:, :] = jnp.ones((heads, SUM_ROWS, PREFIX_ROWS), low)
    vt[:, HD:, :] = jnp.ones((heads, SUM_ROWS, n * length), low)

    def arrive(head, chunk):
        @pl.when(chunk != me)
        def _():
            @pl.when(head == 0)
            def _():
                meta_copy(chunk, chunk).wait_recv()

            qkv_copy(head, chunk, chunk).wait_recv()

        here = rows_of(chunk, length)
        state = lax.broadcasted_iota(jnp.int32, (HD, length), 0)
        qx[head, :HD, here] = (recv[head, chunk, 0].astype(f32) * 0.125).astype(low)
        qx[head, HD:, here] = jnp.where(state == meta[chunk, 0:1, :], 1.0, 0.0).astype(low)
        is_open = jnp.where(state == meta[chunk, 1:2, :], 0.0, masked_score)
        kx[head, here, :] = jnp.concatenate(
            [recv[head, chunk, 1].astype(f32), is_open], axis=0
        ).T.astype(low)
        vt[head, :HD, here] = recv[head, chunk, 2]

    def open_plane(head, which):
        scores = dot_nn(pk[head], qx[head, :, rows_of(which, plane)])
        top = jnp.max(scores, axis=0, keepdims=True)
        raised = jnp.exp(scores - top)
        stat[which, head, 0:1, :] = top
        acc[which, head] = dot_nn(pvt[head], raised.astype(low))

    def pair_part(head, upper, lower, first, count, keys, diagonal):
        here = slice(first, first + count)
        queries = qx[head, :, span_of(upper * plane + first, count)]
        key_rows = span_of(lower * plane, keys)
        scores = dot_nn(kx[head, key_rows, :], queries)
        if diagonal:
            key_at = lax.broadcasted_iota(jnp.int32, scores.shape, 0)
            query_at = lax.broadcasted_iota(jnp.int32, scores.shape, 1) + first
            scores = jnp.where(key_at <= query_at, scores, masked_score)
        old_top = stat[upper, head, 0:1, here]
        top = jnp.maximum(old_top, jnp.max(scores, axis=0, keepdims=True))
        raised = jnp.exp(scores - top).astype(low)
        stat[upper, head, 0:1, here] = top
        acc[upper, head, :, here] = acc[upper, head, :, here] * jnp.exp(old_top - top) + dot_nn(
            vt[head, :, key_rows], raised
        )

    def pair(head, upper, lower):
        pair_part(head, upper, lower, 0, plane, plane, False)

    def pair_diagonal(head, which):
        for part in range(2):
            pair_part(head, which, which, part * length, length, (part + 1) * length, True)

    def close_plane(head, which):
        total = acc[which, head, HD : HD + 1, :]
        value = acc[which, head, :HD, :] / total
        acc[which, head, :HD, :] = value
        stat[which, head, 0:1, :] = stat[which, head, 0:1, :] + jnp.log(total)
        for part in range(2):
            chunk = 2 * which + part
            o_send[head, chunk] = value[:, part * length : (part + 1) * length].astype(low)

            @pl.when((chunk != me) & (head == heads - 1))
            def _():
                out_copy(head, chunk, me).start()

            @pl.when(chunk == me)
            def _():
                o_recv[me, head] = o_send[head, chunk]

    def project_memory():
        mem_across(1 - my_side).wait_recv()
        for load in loads[2:]:
            load.wait()
        whole = mem_all[...].reshape(mkey_ref.shape)

        def one(index, carry):
            here = rows_of(index, block)
            mkey_ref[:, here] = dot_nn(whole, wck[:, here]).astype(low)
            mvalue_ref[:, here] = dot_nn(whole, wcv[:, here]).astype(low)
            return carry

        lax.fori_loop(0, blocks, one, 0)

    def stage(index, carry):
        head = index // planes
        step = lax.rem(index, planes)

        @pl.when(head + 1 < heads)
        def _():
            there = plane_after(1 + step)
            for part in range(2):
                peer = 2 * there + part

                @pl.when(peer != me)
                def _():
                    qkv_copy(head, peer, me).wait_send()
                    qkv_copy(head + 1, peer, me).start()

        @pl.when((head == heads - 1) & (head > 0))
        def _():
            there = plane_after(1 + step)
            for part in range(2):
                peer = 2 * there + part

                @pl.when(peer != me)
                def _():
                    qkv_copy(head, peer, me).wait_send()
                    out_copy(head - 1, peer, me).start()

        here = plane_after(step)
        arrive(head, 2 * here)
        arrive(head, 2 * here + 1)
        open_plane(head, here)
        pair_diagonal(head, here)

        def earlier(back, inner):
            there = plane_after(back)
            pair(head, jnp.maximum(here, there), jnp.minimum(here, there))

            @pl.when((step == planes - 1) & (there > here))
            def _():
                close_plane(head, there)

            return inner

        lax.fori_loop(0, step, earlier, 0)
        for hop in range(1, planes - 1):

            @pl.when(index == hop)
            def _():
                mem_arrivals(hop)
                mem_hops(hop, lambda copy: copy.start())

        @pl.when(index == planes - 1)
        def _():
            mem_arrivals(planes - 1)
            mem_across(my_side).start()

        @pl.when((upward & (my_plane + step >= planes)) | (step == planes - 1))
        def _():
            close_plane(head, here)

        @pl.when(jnp.logical_not(upward) & (step == my_plane))
        def _():
            def close(which, inner):
                close_plane(head, which)
                return inner

            lax.fori_loop(0, my_plane + 1, close, 0)

        return carry

    lax.fori_loop(0, heads * planes, stage, 0)

    saves = []

    def save(source, target):
        copy = pltpu.make_async_copy(source, target, out_sem.at[len(saves)])
        copy.start()
        saves.append(copy)

    save(qx, qx_out)
    save(kx, kx_out)
    save(recv, raw_out)
    save(pk, pk_out)
    save(pv, pv_out)
    save(pkt, pkt_out)
    save(acc, ot_out)
    save(stat, lse_out)
    project_memory()
    save(mkey_ref, mkey_out)
    save(mvalue_ref, mvalue_out)
    for other in range(n):

        @pl.when(other != me)
        def _():
            for head in range(heads):
                out_copy(head, other, other).wait_recv()

        att_ref[:, other * group : (other + 1) * group] = (
            o_recv[other].reshape(group, length).astype(f32).T.astype(low)
        )

    def drain(peer):
        meta_copy(peer, me).wait_send()
        if heads == 1:
            qkv_copy(0, peer, me).wait_send()
        for head in range(heads):
            out_copy(head, peer, me).wait_send()

    others(n, me, drain)
    for hop in range(planes - 1):
        mem_hops(hop, lambda copy: copy.wait_send())
    mem_across(my_side).wait_send()
    for copy in saves:
        copy.wait()


def self_forward(n, segments, padding, tokens, weights, prefix, memory, mem_weights):
    length, width = tokens.shape
    group = width // n
    heads = group // HD
    whole = n * length
    planes = n // 2
    low = jnp.bfloat16
    f32 = jnp.float32
    vmem = pl.BlockSpec(memory_space=pltpu.VMEM)
    anywhere = pl.BlockSpec(memory_space=pl.ANY)
    dma = pltpu.SemaphoreType.DMA
    shapes = (
        ((heads, 2 * HD, whole), low),
        ((heads, whole, 2 * HD), low),
        ((heads, n, 3, HD, length), low),
        ((heads, PREFIX_ROWS, 2 * HD), low),
        ((heads, PREFIX_ROWS, HD), low),
        ((heads, HD, PREFIX_ROWS), low),
        ((planes, heads, HD + SUM_ROWS, 2 * length), f32),
        ((planes, heads, 8, 2 * length), f32),
    )
    square = pltpu.VMEM((width, width), low)
    qx, kx, raw, pk, pv, pkt, acc, stat = (pltpu.VMEM(*shape) for shape in shapes)
    return pl.pallas_call(
        functools.partial(self_forward_kernel, n),
        out_shape=(
            jax.ShapeDtypeStruct((length, width), low),
            jax.ShapeDtypeStruct((n * memory.shape[0], width), low),
            jax.ShapeDtypeStruct((n * memory.shape[0], width), low),
        )
        + tuple(jax.ShapeDtypeStruct(*shape) for shape in shapes),
        in_specs=[vmem] * 3
        + [anywhere] * 3
        + [vmem, anywhere, vmem, anywhere, vmem, vmem]
        + [anywhere] * 2,
        out_specs=(vmem,) + (anywhere,) * 10,
        scratch_shapes=[
            pltpu.VMEM((n, heads, 3, HD, length), low),
            raw,
            pltpu.VMEM((8, length), jnp.int32),
            pltpu.VMEM((n, 8, length), jnp.int32),
            kx,
            qx,
            pltpu.VMEM((heads, HD + SUM_ROWS, whole), low),
            pltpu.VMEM((PREFIX_ROWS, weights[0].shape[0] // 2), f32),
            pk,
            pv,
            pkt,
            pltpu.VMEM((heads, HD + SUM_ROWS, PREFIX_ROWS), low),
            stat,
            acc,
            pltpu.VMEM((heads, n, HD, length), low),
            pltpu.VMEM((n, heads, HD, length), low),
            pltpu.VMEM((planes, 2) + memory.shape, low),
            square,
            square,
            pltpu.VMEM((n * memory.shape[0], width), low),
            pltpu.VMEM((n * memory.shape[0], width), low),
            square,
            square,
            square,
            pltpu.VMEM(prefix[1].shape, low),
            pltpu.VMEM(prefix[3].shape, low),
            dma((heads, n)),
            dma((heads, n)),
            dma((n,)),
            dma((n,)),
            dma((heads, n)),
            dma((heads, n)),
            dma((2, planes + 1)),
            dma((planes + 1,)),
            dma((10,)),
            dma((width // (2 * LANES), 3)),
            dma((4,)),
        ],
        compiler_params=pltpu.CompilerParams(
            collective_id=0, has_side_effects=True, vmem_limit_bytes=VMEM_BYTES
        ),
        name="self_forward",
    )(segments, padding, tokens, *weights, *prefix, memory, *mem_weights)


def self_backward_kernel(
    n,
    batches,
    base_in,
    do_in,
    sums_in,
    mkey_in,
    mvalue_in,
    wck_in,
    wcv_in,
    vecs_in,
    qx_in,
    kx_in,
    raw_in,
    pk_in,
    pv_in,
    pkt_in,
    ot_in,
    lse_in,
    wq_in,
    wk_in,
    wv_in,
    tg_ref,
    mgrad_ref,
    pkv_ref,
    vecs_ref,
    full_out,
    do_recv,
    qx,
    kx,
    raw,
    kt,
    values,
    dot,
    qdo,
    pk,
    pv,
    pkt,
    ot,
    stat,
    weights,
    dqt,
    dkv,
    g_send,
    g_recv,
    pre_ref,
    pre_all,
    pre_sum,
    pre_recv,
    sums_mine,
    sums_core,
    sums_x,
    sums_side,
    sums_z,
    full,
    mkey,
    mvalue,
    wck,
    wcv,
    mem_part,
    mem_side,
    mem_up,
    mem_down,
    vec_all,
    vec_sum,
    vec_y,
    vec_both,
    vec_z,
    product,
    base_ref,
    do_send_sem,
    do_recv_sem,
    g_send_sem,
    g_recv_sem,
    in_sem,
    send_sem,
    recv_sem,
):
    low = jnp.bfloat16
    f32 = jnp.float32
    me = lax.axis_index("seq")
    length, width = tg_ref.shape
    group = width // n
    heads = group // HD
    plane = 2 * length
    planes = n // 2
    step_rows = 256
    my_batch = lax.axis_index("batch")
    my_core = lax.rem(my_batch, 2)
    my_high = my_batch // 2
    highs = batches // 2
    my_plane = me // 2
    my_side = lax.rem(me, 2)
    beside = me + 1 - 2 * my_side
    used = [0]

    def numbers(count):
        used[0] += count
        return used[0] - count

    core_slot = numbers(2)
    x_slot = numbers(2 * highs)
    y_slot = numbers(3)
    z_slot = numbers(2 * planes)
    up_slot = numbers(planes)
    down_slot = numbers(planes)
    va_slot = numbers(batches)
    vb_slot = numbers(1)
    vc_slot = numbers(planes)
    pa_slot = numbers(batches)
    pb_slot = numbers(n)

    def send(source, target, first, peer_index, slot_index, axis, peer):
        return remote(
            source,
            target,
            send_sem.at[first + peer_index],
            recv_sem.at[first + slot_index],
            axis,
            peer,
        )

    half_rows = 2 * planes * highs * sums_z.shape[1]
    x_rows = half_rows // highs
    y_rows = x_rows // 2
    z_rows = y_rows // planes
    x_row = pl.multiple_of(my_high * x_rows, x_rows)
    y_row = pl.multiple_of(x_row + my_side * y_rows, y_rows)

    def part(row, count):
        return sums_mine.at[pl.ds(pl.multiple_of(row, count), count)]

    def reduce_core():
        return send(
            sums_in.at[1 - my_core], sums_core, core_slot, 0, 0, "batch", my_batch + 1 - 2 * my_core
        )

    def reduce_x(peer, slot):
        return send(
            part(peer * x_rows, x_rows),
            sums_x.at[slot],
            x_slot,
            peer,
            slot,
            "batch",
            2 * peer + my_core,
        )

    def reduce_y():
        return send(
            part(x_row + (1 - my_side) * y_rows, y_rows), sums_side, y_slot, 0, 0, "seq", beside
        )

    def reduce_z(peer, slot):
        return send(
            part(y_row + peer * z_rows, z_rows),
            sums_z.at[slot],
            z_slot,
            peer,
            slot,
            "seq",
            2 * peer + my_side,
        )

    def gather_z(peer, slot):
        piece = full.at[my_core, my_high, my_side, slot]
        return send(piece, piece, z_slot + planes, peer, slot, "seq", 2 * peer + my_side)

    def gather_y(side):
        piece = full.at[my_core, my_high, side]
        return send(piece, piece, y_slot + 1, 0, 0, "seq", beside)

    def gather_x(peer, slot):
        piece = full.at[my_core, slot]
        return send(piece, piece, x_slot + highs, peer, slot, "batch", 2 * peer + my_core)

    def gather_core(core):
        piece = full.at[core]
        return send(piece, piece, core_slot + 1, 0, 0, "batch", my_batch + 1 - 2 * my_core)

    def mem_across():
        return send(
            mem_part.at[:, 1 - my_side], mem_side, y_slot + 2, 0, 0, "seq", beside
        )

    def mem_hop(target, toward, peer=None):
        buffer, slot = (mem_up, up_slot) if toward > 0 else (mem_down, down_slot)
        return send(
            mem_part.at[target, my_side],
            buffer.at[target],
            slot,
            target,
            target,
            "seq",
            me + 2 * toward if peer is None else peer,
        )

    def mem_from(target, toward):
        return mem_hop(target, toward, me - 2 * toward)

    def mem_pass(toward):
        buffer = mem_up if toward > 0 else mem_down
        first = 0 if toward > 0 else planes - 1
        for target in range(planes):

            @pl.when((target - my_plane) * toward > 0)
            def _():
                @pl.when(my_plane != first)
                def _():
                    mem_from(target, toward).wait_recv()
                    mem_part[target, my_side] = (
                        mem_part[target, my_side].astype(f32) + buffer[target].astype(f32)
                    ).astype(low)

                mem_hop(target, toward).start()

    def mem_stage(at):
        pl.when(my_plane == at)(lambda: mem_pass(1))
        pl.when(my_plane == planes - 1 - at)(lambda: mem_pass(-1))

    def mem_end():
        value = mem_part[my_plane, my_side].astype(f32)
        mgrad_ref[...] = value.astype(low)

        @pl.when(my_plane > 0)
        def _():
            mem_from(my_plane, 1).wait_recv()
            mgrad_ref[...] = (mgrad_ref[...].astype(f32) + mem_up[my_plane].astype(f32)).astype(low)

        @pl.when(my_plane < planes - 1)
        def _():
            mem_from(my_plane, -1).wait_recv()
            mgrad_ref[...] = (
                mgrad_ref[...].astype(f32) + mem_down[my_plane].astype(f32)
            ).astype(low)

    def mem_drain():
        for target in range(planes):

            @pl.when(target > my_plane)
            def _():
                mem_hop(target, 1).wait_send()

            @pl.when(target < my_plane)
            def _():
                mem_hop(target, -1).wait_send()

    def vec_a(peer, slot):
        return send(vecs_in, vec_all.at[slot], va_slot, peer, slot, "batch", peer)

    def vec_b(side):
        return send(vec_sum, vec_y.at[side], vb_slot, 0, 0, "seq", beside)

    def vec_c(peer, slot):
        return send(vec_both, vec_z.at[slot], vc_slot, peer, slot, "seq", 2 * peer + my_side)

    def pre_a(peer, slot):
        return send(pre_ref, pre_all.at[slot], pa_slot, peer, slot, "batch", peer)

    def pre_b(peer, slot):
        return send(pre_sum, pre_recv.at[slot], pb_slot, peer, slot, "seq", peer)

    def do_copy(head, peer, slot):
        return remote(
            do_in.at[peer, head],
            do_recv.at[head, slot],
            do_send_sem.at[head, peer],
            do_recv_sem.at[head, slot],
            "seq",
            peer,
        )

    def q_copy(head, peer, slot):
        return remote(
            g_send.at[peer, head, 0],
            g_recv.at[0, slot, head],
            g_send_sem.at[0, head, peer],
            g_recv_sem.at[0, head, slot],
            "seq",
            peer,
        )

    def kv_copy(head, peer, slot):
        return remote(
            g_send.at[peer, head, pl.ds(1, 2)],
            g_recv.at[pl.ds(1, 2), slot, head],
            g_send_sem.at[1, head, peer],
            g_recv_sem.at[1, head, slot],
            "seq",
            peer,
        )

    def far_first(body):
        for index in range(n):
            peer = jnp.where(my_plane < planes // 2, n - 1 - index, index)

            @pl.when(peer != me)
            def _():
                body(peer)

    def added(ref, size):
        value = ref[0].astype(f32)
        for other in range(1, size):
            value = value + ref[other].astype(f32)
        return value

    loads = [
        pltpu.make_async_copy(source, target, in_sem.at[index])
        for index, (source, target) in enumerate(
            (
                (raw_in, raw),
                (kx_in, kx),
                (pk_in, pk),
                (pv_in, pv),
                (pkt_in, pkt),
                (qx_in, qx),
                (ot_in, ot),
                (lse_in, stat),
                (sums_in.at[my_core], sums_mine),
                (vecs_in, vec_all.at[my_batch]),
                (mkey_in, mkey),
                (mvalue_in, mvalue),
                (wck_in, wck),
                (wcv_in, wcv),
                (base_in, base_ref),
                (wq_in, weights.at[0]),
                (wk_in, weights.at[1]),
                (wv_in, weights.at[2]),
            )
        )
    ]
    own_do = pltpu.make_async_copy(do_in.at[me], do_recv.at[:, me], in_sem.at[len(loads)])
    own_do.start()
    for load in loads:
        load.start()
    enter({"seq": n, "batch": batches})
    far_first(lambda peer: do_copy(0, peer, me).start())
    reduce_core().start()
    others(batches, my_batch, lambda peer: vec_a(peer, my_batch).start())
    dkv[...] = jnp.zeros_like(dkv)
    product[...] = jnp.zeros_like(product)
    pre_ref[...] = jnp.zeros_like(pre_ref)
    for load in loads[:14]:
        load.wait()
    own_do.wait()

    def turn(index, carry):
        head = index // n
        chunk = lax.rem(index, n)
        here = rows_of(chunk, length)
        kt[head, :, here] = raw[head, chunk, 1]
        values[head, here, :] = raw[head, chunk, 2].astype(f32).T.astype(low)
        return carry

    lax.fori_loop(0, heads * n, turn, 0)

    def memory_back(index, carry):
        here = rows_of(index, step_rows)
        value = dot_nt(mkey[...], wck[here, :]) + dot_nt(mvalue[...], wcv[here, :])
        mem_part[:, :, :, here] = value.astype(low).reshape(mem_part.shape[:3] + (step_rows,))
        return carry

    lax.fori_loop(0, width // step_rows, memory_back, 0)
    mem_across().start()

    def next_head(head):
        def move(peer):
            do_copy(head, peer, me).wait_send()
            do_copy(head + 1, peer, me).start()

        far_first(move)

    def arrive(head, which):
        for part in range(2):
            chunk = 2 * which + part

            @pl.when(chunk != me)
            def _():
                do_copy(head, chunk, chunk).wait_recv()

            grads = do_recv[head, chunk]
            dot[head, :, rows_of(chunk, length)] = grads
            grads = grads.astype(f32)
            query = raw[head, chunk, 0].astype(f32) * 0.125
            qdo[head, rows_of(chunk, length), :] = (
                jnp.concatenate([query, grads], axis=0).T.astype(low)
            )
            here = slice(part * length, (part + 1) * length)
            stat[which, head, 1:2, here] = jnp.sum(
                grads * ot[which, head, :HD, here], axis=0, keepdims=True
            )
        here = rows_of(which, plane)
        weight = jnp.exp(dot_nn(pk[head], qx[head, :, here]) - stat[which, head, 0:1, :])
        slope = weight * (dot_nn(pv[head], dot[head, :, here]) - stat[which, head, 1:2, :])
        both = jnp.concatenate([slope, weight], axis=0).astype(low)
        sums = dot_nn(both, qdo[head, here, :])
        pre_ref[head] += jnp.where(
            head_lanes((PREFIX_ROWS, 2 * HD), 0), sums[:PREFIX_ROWS], sums[PREFIX_ROWS:]
        )
        slope = slope.astype(low)
        dqt[which, head] = dot_nn(pkt[head], slope)

    def plus(first, second):
        return (first.astype(f32) + second.astype(f32)).astype(low)

    def sum_one():
        reduce_core().wait_recv()
        sums_mine[...] = plus(sums_mine[...], sums_core[...])
        others(highs, my_high, lambda peer: reduce_x(peer, my_high).start())

    def sum_two():
        here = pl.ds(x_row, x_rows)
        others(highs, my_high, lambda peer: reduce_x(peer, peer).wait_recv())
        sums_x[my_high] = sums_mine[here]
        sums_mine[here] = added(sums_x, highs).astype(low)
        reduce_y().start()

    def sum_three():
        here = pl.ds(y_row, y_rows)
        reduce_y().wait_recv()
        sums_mine[here] = plus(sums_mine[here], sums_side[...])
        others(planes, my_plane, lambda peer: reduce_z(peer, my_plane).start())

    def sum_four():
        here = pl.ds(pl.multiple_of(y_row + my_plane * z_rows, z_rows), z_rows)
        others(planes, my_plane, lambda peer: reduce_z(peer, peer).wait_recv())
        sums_z[my_plane] = sums_mine[here]
        full[my_core, my_high, my_side, my_plane] = added(sums_z, planes).astype(low)
        others(planes, my_plane, lambda peer: gather_z(peer, my_plane).start())

    def sum_five():
        others(planes, my_plane, lambda peer: gather_z(peer, peer).wait_recv())
        gather_y(my_side).start()

    def sum_six():
        gather_y(1 - my_side).wait_recv()
        others(highs, my_high, lambda peer: gather_x(peer, my_high).start())

    def sum_seven():
        others(highs, my_high, lambda peer: gather_x(peer, peer).wait_recv())
        gather_core(my_core).start()

    def sum_end():
        gather_core(1 - my_core).wait_recv()
        save_full.start()

    def vec_one():
        others(batches, my_batch, lambda peer: vec_a(peer, peer).wait_recv())
        vec_sum[...] = added(vec_all, batches)
        vec_b(my_side).start()
        vec_y[my_side] = vec_sum[...]

    def vec_two():
        vec_b(1 - my_side).wait_recv()
        value = (vec_y[0] + vec_y[1]).astype(f32)
        vec_both[...] = jnp.concatenate(
            [value[:, : width // 2], value[:, width // 2 :]], axis=0
        ).astype(low)
        others(planes, my_plane, lambda peer: vec_c(peer, my_plane).start())
        vec_z[my_plane] = vec_both[...]

    def vec_end():
        others(planes, my_plane, lambda peer: vec_c(peer, peer).wait_recv())
        value = added(vec_z, planes)
        vecs_ref[:, : width // 2] = value[:8]
        vecs_ref[:, width // 2 :] = value[8:]

    def mem_one():
        mem_across().wait_recv()
        mem_part[:, my_side] = plus(mem_part[:, my_side], mem_side[...])

    def stage_pa():
        others(batches, my_batch, lambda peer: pre_a(peer, my_batch).start())
        pre_all[my_batch] = pre_ref[...]

    def stage_pb():
        others(batches, my_batch, lambda peer: pre_a(peer, peer).wait_recv())
        pre_sum[...] = added(pre_all, batches).astype(low)
        others(n, me, lambda peer: pre_b(peer, me).start())
        pre_recv[me] = pre_sum[...]

    save_full = pltpu.make_async_copy(full, full_out, in_sem.at[0])

    def pair_part(head, upper, lower, first, count, diagonal):
        keys = span_of(lower * plane + first, count)
        here = span_of(upper * plane + first, plane - first)
        at = slice(first, plane)
        scores = dot_nn(kx[head, keys, :], qx[head, :, here])
        slope = dot_nn(values[head, keys, :], dot[head, :, here]) - stat[upper, head, 1:2, at]
        weight = jnp.exp(scores - stat[upper, head, 0:1, at])
        if diagonal:
            key_at = lax.broadcasted_iota(jnp.int32, scores.shape, 0)
            query_at = lax.broadcasted_iota(jnp.int32, scores.shape, 1)
            weight = jnp.where(key_at <= query_at, weight, 0.0)
        slope = (weight * slope).astype(low)
        key_part = dot_nn(slope, qdo[head, here, :])
        value_part = dot_nn(weight.astype(low), qdo[head, here, :])
        dkv[head, keys, :] += jnp.where(head_lanes((count, 2 * HD), 0), key_part, value_part)
        dqt[upper, head, :, at] += dot_nn(kt[head, :, keys], slope)

    def pair(head, upper, lower, diagonal):
        if diagonal:
            pair_part(head, upper, lower, 0, length, True)
            pair_part(head, upper, lower, length, length, True)
        else:
            pair_part(head, upper, lower, 0, plane, False)

    def hand_queries(head, which):
        for part in range(2):
            chunk = 2 * which + part
            g_send[chunk, head, 0] = (
                dqt[which, head, :, part * length : (part + 1) * length] * 0.125
            ).astype(low)

            @pl.when(chunk != me)
            def _():
                q_copy(head, chunk, me).start()

            @pl.when(chunk == me)
            def _():
                g_recv[0, me, head] = g_send[chunk, head, 0]

    def hand_keys(head, which):
        for part in range(2):
            chunk = 2 * which + part
            turned = dkv[head, rows_of(chunk, length), :].T.astype(low)
            g_send[chunk, head, 1] = turned[:HD]
            g_send[chunk, head, 2] = turned[HD:]

            @pl.when(chunk != me)
            def _():
                kv_copy(head, chunk, me).start()

            @pl.when(chunk == me)
            def _():
                g_recv[pl.ds(1, 2), me, head] = g_send[chunk, head, pl.ds(1, 2)]

    rising = my_plane >= planes // 2
    total = heads * planes * (planes + 1) // 2
    hooks = [
        (2, sum_one),
        (3, mem_one),
        (4, lambda: mem_stage(0)),
        (5, vec_one),
        (5, sum_two),
        (7, sum_three),
        (8, vec_two),
        (10, sum_four),
        (12, sum_five),
        (14, sum_six),
        (16, vec_end),
        (17, sum_seven),
    ] + [(4 + 3 * at, functools.partial(mem_stage, at)) for at in range(1, planes - 1)]
    hooks += [
        (1 + head * total // heads, functools.partial(next_head, head)) for head in range(heads - 1)
    ]
    final = total - planes * (planes + 1) // 2
    hooks += [(final + planes + 1, stage_pa), (final + 2 * planes - 1, stage_pb)]

    def hook(pairs):
        for number, body in sorted(hooks, key=lambda item: item[0]):
            pl.when(pairs == number)(body)


    def stage(index, carry):
        head = index // planes
        step = lax.rem(index, planes)
        here = jnp.where(rising, step, planes - 1 - step)

        @pl.when((step == 0) | ((step == 1) & jnp.logical_not(rising)))
        def _():
            @pl.when(rising | (step == 0))
            def _():
                arrive(head, here)

            @pl.when(jnp.logical_not(rising) & (step == 1))
            def _():
                def rest(which, inner):
                    arrive(head, planes - 2 - which)
                    return inner

                lax.fori_loop(0, planes - 1, rest, 0)

        begun = head * (planes * (planes + 1) // 2) + step * planes - step * (step - 1) // 2
        hook(begun)
        pair(head, here, here, True)

        @pl.when(rising)
        def _():
            hand_queries(head, here)

        @pl.when(jnp.logical_not(rising))
        def _():
            hand_keys(head, here)

        def far(at, inner):
            there = jnp.where(rising, here + 1 + at, here - 1 - at)

            @pl.when(rising & (step == 0))
            def _():
                arrive(head, there)

            hook(begun + 1 + at)
            pair(head, jnp.maximum(here, there), jnp.minimum(here, there), False)
            return inner

        lax.fori_loop(0, planes - 1 - step, far, 0)

        @pl.when(rising)
        def _():
            hand_keys(head, here)

        @pl.when(jnp.logical_not(rising))
        def _():
            hand_queries(head, here)

        return carry

    lax.fori_loop(0, heads * planes, stage, 0)
    mem_end()
    for load in loads[14:]:
        load.wait()

    def gathered(peer):
        for head in range(heads):
            q_copy(head, peer, peer).wait_recv()
            kv_copy(head, peer, peer).wait_recv()

    half = width // 2

    def gather_plane(step, carry):
        which = lax.rem(my_plane + step, planes)
        for part in range(2):
            peer = 2 * which + part

            @pl.when(peer != me)
            def _():
                gathered(peer)

        columns = rows_of(which, 2 * group)
        for part in range(2):
            here = slice(part * half, (part + 1) * half)
            value = product[here, :]
            for kind in range(3):
                grads = g_recv[kind, pl.ds(2 * which, 2)].reshape(2 * group, length)
                value = value + dot_nn(weights[kind, here, columns], grads)
            product[here, :] = value
        return carry

    lax.fori_loop(0, planes, gather_plane, 0)
    sum_end()
    tile = 256
    for index in range(width // tile):
        here = slice(index * tile, (index + 1) * tile)
        tg_ref[:, here] = (base_ref[:, here] + product[here, :].T).astype(low)
    for other in range(n):

        @pl.when(other != me)
        def _():
            pre_b(other, other).wait_recv()

        value = pre_recv[other].astype(f32)
        for which in range(2):
            pkv_ref[:, which * width + other * group : which * width + (other + 1) * group] = (
                jnp.concatenate(
                    [value[head, :, which * HD : (which + 1) * HD] for head in range(heads)], axis=1
                )
            )

    def drain(peer):
        do_copy(heads - 1, peer, me).wait_send()
        pre_b(peer, me).wait_send()
        for head in range(heads):
            q_copy(head, peer, me).wait_send()
            kv_copy(head, peer, me).wait_send()

    others(n, me, drain)
    others(batches, my_batch, lambda peer: pre_a(peer, my_batch).wait_send())
    others(batches, my_batch, lambda peer: vec_a(peer, my_batch).wait_send())
    reduce_core().wait_send()
    others(highs, my_high, lambda peer: reduce_x(peer, my_high).wait_send())
    reduce_y().wait_send()
    others(planes, my_plane, lambda peer: reduce_z(peer, my_plane).wait_send())
    others(planes, my_plane, lambda peer: gather_z(peer, my_plane).wait_send())
    gather_y(my_side).wait_send()
    others(highs, my_high, lambda peer: gather_x(peer, my_high).wait_send())
    gather_core(my_core).wait_send()
    mem_across().wait_send()
    mem_drain()
    others(planes, my_plane, lambda peer: vec_c(peer, my_plane).wait_send())
    vec_b(my_side).wait_send()
    save_full.wait()


def self_backward(
    n, batches, first_grad, out_grad, sums, mem_grads, mem_weights, vecs, saved, weights
):
    length, width = first_grad.shape
    group = width // n
    heads = group // HD
    whole = n * length
    planes = n // 2
    low = jnp.bfloat16
    f32 = jnp.float32
    vmem = pl.BlockSpec(memory_space=pltpu.VMEM)
    anywhere = pl.BlockSpec(memory_space=pl.ANY)
    dma = pltpu.SemaphoreType.DMA
    sum_rows = sums.shape[0] // (n * batches)
    mem_len = mem_grads[0].shape[0]
    mem_rows = mem_len // n
    mem_part = pltpu.VMEM((planes, mem_rows, width), low)
    mem_low = pltpu.VMEM((mem_len, width), low)
    square = pltpu.VMEM((width, width), low)
    vec = pltpu.VMEM((8, width), f32)
    copies = 6 + 2 * (batches // 2) + 5 * planes + 2 * batches + n
    qx, kx, raw, pk, pv, pkt, ot, stat = (pltpu.VMEM(value.shape, value.dtype) for value in saved)
    return pl.pallas_call(
        functools.partial(self_backward_kernel, n, batches),
        out_shape=(
            jax.ShapeDtypeStruct((length, width), low),
            jax.ShapeDtypeStruct((mem_rows, width), low),
            jax.ShapeDtypeStruct((PREFIX_ROWS, 2 * width), f32),
            jax.ShapeDtypeStruct((8, width), f32),
            jax.ShapeDtypeStruct((2, batches // 2, 2, planes, sum_rows, LANES), low),
        ),
        in_specs=[anywhere] * 19,
        out_specs=(vmem, vmem, vmem, vmem, anywhere),
        scratch_shapes=[
            pltpu.VMEM((heads, n, HD, length), low),
            qx,
            kx,
            raw,
            pltpu.VMEM((heads, HD, whole), low),
            pltpu.VMEM((heads, whole, HD), low),
            pltpu.VMEM((heads, HD, whole), low),
            pltpu.VMEM((heads, whole, 2 * HD), low),
            pk,
            pv,
            pkt,
            ot,
            stat,
            pltpu.VMEM((3, width, width), low),
            pltpu.VMEM((planes, heads, HD, 2 * length), f32),
            pltpu.VMEM((heads, whole, 2 * HD), f32),
            pltpu.VMEM((n, heads, 3, HD, length), low),
            pltpu.VMEM((3, n, heads, HD, length), low),
            pltpu.VMEM((heads, PREFIX_ROWS, 2 * HD), f32),
            pltpu.VMEM((batches, heads, PREFIX_ROWS, 2 * HD), f32),
            pltpu.VMEM((heads, PREFIX_ROWS, 2 * HD), low),
            pltpu.VMEM((n, heads, PREFIX_ROWS, 2 * HD), low),
            pltpu.VMEM((sums.shape[0] // 2, LANES), low),
            pltpu.VMEM((sums.shape[0] // 2, LANES), low),
            pltpu.VMEM((batches // 2, sums.shape[0] // batches, LANES), low),
            pltpu.VMEM((planes * sum_rows, LANES), low),
            pltpu.VMEM((planes, sum_rows, LANES), low),
            pltpu.VMEM((2, batches // 2, 2, planes, sum_rows, LANES), low),
            mem_low,
            mem_low,
            square,
            square,
            pltpu.VMEM((planes, 2, mem_rows, width), low),
            mem_part,
            mem_part,
            mem_part,
            pltpu.VMEM((batches, 8, width), f32),
            vec,
            pltpu.VMEM((2, 8, width), f32),
            pltpu.VMEM((16, width // 2), low),
            pltpu.VMEM((planes, 16, width // 2), low),
            pltpu.VMEM((width, length), f32),
            pltpu.VMEM((length, width), f32),
            dma((heads, n)),
            dma((heads, n)),
            dma((2, heads, n)),
            dma((2, heads, n)),
            dma((19,)),
            dma((copies,)),
            dma((copies,)),
        ],
        compiler_params=pltpu.CompilerParams(
            collective_id=1, has_side_effects=True, vmem_limit_bytes=VMEM_BYTES
        ),
        name="self_backward",
    )(
        first_grad,
        out_grad,
        sums.reshape(2, -1, LANES),
        *mem_grads,
        *mem_weights,
        vecs,
        *saved,
        *weights,
    )


def both_parts(value):
    high = value.astype(jnp.bfloat16).astype(jnp.float32)
    return jnp.concatenate([high, value - high], axis=0).astype(jnp.bfloat16)


def finish_kernel(
    full_in,
    vecs_ref,
    pkv_ref,
    emb_ref,
    first_in,
    fbias_ref,
    second_in,
    token_in,
    mem_in,
    embed_out,
    first_out,
    fbias_out,
    second_out,
    sbias_out,
    down_out,
    dbias_out,
    raise_out,
    rbias_out,
    gain_out,
    shift_out,
    token_out,
    mem_out,
    full_ref,
    first_ref,
    second_ref,
    token_ref,
    mem_ref,
    first_grad,
    second_grad,
    down_grad,
    raise_grad,
    emb,
    hidden,
    out_sem,
    in_sem,
):
    f32 = jnp.float32
    low = jnp.bfloat16
    width = emb_ref.shape[1]
    down = dbias_out.shape[1]
    count = emb_ref.shape[0]
    first = down * width // LANES
    loads = [
        pltpu.make_async_copy(source, target, in_sem.at[index])
        for index, (source, target) in enumerate(
            (
                (full_in.at[first:], full_ref.at[first:]),
                (full_in.at[:first], full_ref.at[:first]),
                (first_in, first_ref),
                (second_in, second_ref),
                (token_in, token_ref),
                (mem_in, mem_ref),
            )
        )
    ]
    for load in loads:
        load.start()
    saves = []

    def save(source, target, rows=None):
        if rows is not None:
            source, target = source.at[rows], target.at[rows]
        copy = pltpu.make_async_copy(source, target, out_sem.at[len(saves)])
        copy.start()
        saves.append(copy)

    loads[0].wait()
    for index in range(width // LANES):
        raise_grad[:, index * LANES : (index + 1) * LANES] = full_ref[
            first + index * down : first + (index + 1) * down, :
        ].astype(f32)
    save(raise_grad, raise_out)
    loads[1].wait()
    for index in range(down // LANES):
        down_grad[:, index * LANES : (index + 1) * LANES] = full_ref[
            index * width : (index + 1) * width, :
        ].astype(f32)
    save(down_grad, down_out)
    for load in loads[4:]:
        load.wait()
    save(token_ref, token_out)
    save(mem_ref, mem_out)
    loads[2].wait()
    emb[...] = jnp.zeros_like(emb)
    emb[:count, :] = emb_ref[...].astype(f32)
    emb_low = emb[...].astype(low)
    row = lax.broadcasted_iota(jnp.int32, hidden.shape, 0)
    hidden[...] = jnp.where(
        row < count, jnp.tanh(dot_nn(emb_low, first_ref[...]) + fbias_ref[...]), 0.0
    )
    value = hidden[...]
    prefix = pkv_ref[...]
    parts = both_parts(prefix)
    hidden_twice = jnp.concatenate([value, value], axis=0).T.astype(low)
    tile = 128
    for index in range(second_grad.shape[0] // tile):
        here = slice(index * tile, (index + 1) * tile)
        second_grad[here, :] = dot_nn(hidden_twice[here, :], parts)
        save(second_grad, second_out, here)
    sbias_out[...] = jnp.sum(prefix, axis=0, keepdims=True)
    loads[3].wait()
    grad = dot_nt(parts, second_ref[...])
    grad = (grad[:PREFIX_ROWS] + grad[PREFIX_ROWS:]) * (1.0 - value * value)
    fbias_out[...] = jnp.sum(grad, axis=0, keepdims=True)
    parts = both_parts(grad)
    emb_twice = jnp.concatenate([emb[...], emb[...]], axis=0).T.astype(low)
    first_grad[...] = dot_nn(emb_twice, parts)
    save(first_grad, first_out)
    back = dot_nt(parts, first_ref[...])
    embed_out[...] = (back[:PREFIX_ROWS] + back[PREFIX_ROWS:])[:count, :]
    rbias_out[...] = vecs_ref[0:1, :]
    dbias_out[...] = vecs_ref[1:2, :down]
    gain_out[...] = vecs_ref[2:5, :]
    shift_out[...] = vecs_ref[5:8, :]
    for copy in saves:
        copy.wait()


def finish(full, vecs, prefix_grad, embed, first, first_bias, second, down, token_grad, memory_grad):
    f32 = jnp.float32
    count, width = embed.shape
    hidden = first.shape[1]
    vmem = pl.BlockSpec(memory_space=pltpu.VMEM)
    anywhere = pl.BlockSpec(memory_space=pl.ANY)
    shapes = (
        (count, width),
        (width, hidden),
        (1, hidden),
        (hidden, 2 * width),
        (1, 2 * width),
        (width, down),
        (1, down),
        (down, width),
        (1, width),
        (3, width),
        (3, width),
    )
    return pl.pallas_call(
        finish_kernel,
        out_shape=tuple(jax.ShapeDtypeStruct(shape, f32) for shape in shapes)
        + tuple(
            jax.ShapeDtypeStruct(value.shape, value.dtype) for value in (token_grad, memory_grad)
        ),
        in_specs=[anywhere, vmem, vmem, vmem, anywhere, vmem, anywhere, anywhere, anywhere],
        out_specs=(
            vmem,
            anywhere,
            vmem,
            anywhere,
            vmem,
            anywhere,
            vmem,
            anywhere,
            vmem,
            vmem,
            vmem,
            anywhere,
            anywhere,
        ),
        scratch_shapes=[
            pltpu.VMEM(full.shape, jnp.bfloat16),
            pltpu.VMEM(first.shape, jnp.bfloat16),
            pltpu.VMEM(second.shape, jnp.bfloat16),
            pltpu.VMEM(token_grad.shape, token_grad.dtype),
            pltpu.VMEM(memory_grad.shape, memory_grad.dtype),
            pltpu.VMEM((width, hidden), f32),
            pltpu.VMEM((hidden, 2 * width), f32),
            pltpu.VMEM((width, down), f32),
            pltpu.VMEM((down, width), f32),
            pltpu.VMEM((PREFIX_ROWS, width), f32),
            pltpu.VMEM((PREFIX_ROWS, hidden), f32),
            pltpu.SemaphoreType.DMA((5 + hidden // 128,)),
            pltpu.SemaphoreType.DMA((6,)),
        ],
        compiler_params=pltpu.CompilerParams(vmem_limit_bytes=VMEM_BYTES),
        name="finish",
    )(full, vecs, prefix_grad, embed, first, first_bias, second, token_grad, memory_grad)


def gelu_pair(value):
    size = jnp.abs(value)
    step = 1.0 / (1.0 + (0.3275911 * 0.7071067811865476) * size)
    bell = jnp.exp(-0.5 * value * value)
    poly = step * (
        0.127414796
        + step
        * (-0.142248368 + step * (0.7107068705 + step * (-0.7265760135 + step * 0.5307027145)))
    )
    act = jnp.maximum(value, 0.0) - size * (poly * bell)
    turn = bell * (0.3989422804014327 * size - poly)
    return act, jnp.where(value >= 0.0, 1.0 + turn, -turn)


def normed(value):
    center = jnp.mean(value, axis=-1, keepdims=True)
    centered = value - center
    scale = lax.rsqrt(jnp.mean(centered * centered, axis=-1, keepdims=True) + norm_eps)
    return centered * scale, scale


def norm_back(grad, scale, unit):
    return scale * (
        grad
        - jnp.mean(grad, axis=-1, keepdims=True)
        - unit * jnp.mean(grad * unit, axis=-1, keepdims=True)
    )


def middle_kernel(
    tok_in,
    att_in,
    cot_in,
    mkey_in,
    mvalue_in,
    gain_ref,
    shift_ref,
    dbias_ref,
    rbias_ref,
    wo_in,
    wcq_in,
    wco_in,
    wd_in,
    wr_in,
    win_in,
    wout_in,
    layer_out,
    fgrad_out,
    ograd_out,
    mkey_out,
    mvalue_out,
    sums_out,
    vecs_ref,
    tok_ref,
    att_ref,
    cot_ref,
    mkey_ref,
    mvalue_ref,
    out_ref,
    fgrad_ref,
    ograd_ref,
    sums_ref,
    wo,
    wcq,
    wco,
    wd,
    wr,
    win,
    wout,
    unit_one,
    unit_two,
    work,
    total,
    scale_one,
    scale_two,
    low_one,
    low_two,
    low_three,
    query,
    crossed,
    weights,
    slopes,
    acts,
    down_act,
    down_slope,
    down_grad,
    load_sem,
    win_sem,
    wout_sem,
    out_sem,
):
    length, width = tok_ref.shape
    resident = len(win.shape) == 2
    tile = 512 if resident else win.shape[2]
    tiles = win_in.shape[1] // tile
    slots = tiles if resident else win.shape[0]
    rows_step = 64
    low = jnp.bfloat16
    f32 = jnp.float32

    sources = (
        att_in,
        wo_in,
        tok_in,
        wcq_in,
        mkey_in,
        mvalue_in,
        wco_in,
        wd_in,
        wr_in,
        cot_in,
    )
    targets = (att_ref, wo, tok_ref, wcq, mkey_ref, mvalue_ref, wco, wd, wr, cot_ref)
    loads = [
        pltpu.make_async_copy(source, target, load_sem.at[index])
        for index, (source, target) in enumerate(zip(sources, targets))
    ]

    def win_load(which):
        slot = which % slots
        target = win.at[:, rows_of(which, tile)] if resident else win.at[slot]
        return pltpu.make_async_copy(win_in.at[:, rows_of(which, tile)], target, win_sem.at[slot])

    def wout_load(which):
        slot = which % slots
        target = wout.at[rows_of(which, tile), :] if resident else wout.at[slot]
        return pltpu.make_async_copy(wout_in.at[rows_of(which, tile), :], target, wout_sem.at[slot])

    for load in loads[:7]:
        load.start()

    def by_columns(extent, step, body):
        def one(index, carry):
            body(pl.ds(pl.multiple_of(index * step, step), step))
            return carry

        lax.fori_loop(0, extent // step, one, 0)

    def by_rows(body, init=0):
        def one(index, carry):
            return body(rows_of(index, rows_step), carry)

        return lax.fori_loop(0, length // rows_step, one, init)

    cols = 512
    half = width // 2

    for load in loads[:3]:
        load.wait()
    for load in loads[7:]:
        load.start()
    for which in range(slots):
        win_load(which).start()
    for which in range(slots):
        wout_load(which).start()

    def project_out(here):
        work[:, here] = tok_ref[:, here].astype(f32) + dot_nn(att_ref[...], wo[:, here])

    by_columns(width, cols, project_out)

    def first_norm(here, carry):
        unit, scale = normed(work[here, :])
        unit_one[here, :] = unit
        scale_one[here, :] = scale
        value = unit * gain_ref[0:1, :] + shift_ref[0:1, :]
        work[here, :] = value
        low_one[here, :] = value.astype(low)
        return carry

    by_rows(first_norm)

    loads[3].wait()

    def project_query(here):
        query[:, here] = dot_nn(low_one[...], wcq[:, here]).astype(low)

    by_columns(width, cols, project_query)
    per_block = LANES // HD

    def stacked(value):
        return jnp.concatenate(
            [jnp.where(head_lanes(value.shape, head), value, 0.0) for head in range(per_block)],
            axis=0,
        ).astype(low)

    def unstacked(value):
        return jnp.concatenate(
            [
                value[head * HD : (head + 1) * HD, head * length : (head + 1) * length]
                for head in range(per_block)
            ],
            axis=0,
        )

    def block_queries(here):
        return stacked(query[:, here].astype(f32) * 0.125)

    def cross_forward(block):
        here = rows_of(block, LANES)
        scores = dot_nt(mkey_ref[:, here], block_queries(here))
        raised = jnp.exp(scores - jnp.max(scores, axis=0, keepdims=True))
        share = 1.0 / jnp.sum(raised, axis=0, keepdims=True)
        weight = (raised * share).astype(low)
        weights[block] = weight
        values = mvalue_ref[:, here].astype(f32).T.astype(low)
        crossed[:, here] = unstacked(dot_nn(values, weight)).T.astype(low)

    loads[4].wait()
    loads[5].wait()

    def cross_forward_both(step, carry):
        cross_forward(2 * step)
        cross_forward(2 * step + 1)
        return carry

    lax.fori_loop(0, width // LANES // 2, cross_forward_both, 0)

    loads[6].wait()

    def project_crossed(here):
        work[:, here] += dot_nn(crossed[...], wco[:, here])

    by_columns(width, cols, project_crossed)

    def second_norm(here, carry):
        unit, scale = normed(work[here, :])
        unit_two[here, :] = unit
        scale_two[here, :] = scale
        value = unit * gain_ref[1:2, :] + shift_ref[1:2, :]
        work[here, :] = value
        low_two[here, :] = value.astype(low)
        return carry

    by_rows(second_norm)

    step_cols = 512

    def feed_part(here, source):
        act, slope = gelu_pair(dot_nn(low_two[...], source))
        slopes[:, here] = slope.astype(low)
        return act.astype(low)

    if resident:

        def feed_forward(which, carry):
            here = rows_of(which, step_cols)

            @pl.when(which % (tile // step_cols) == 0)
            def _():
                win_load(which // (tile // step_cols)).wait()

            acts[:, here] = feed_part(here, win[:, here])
            return carry

        lax.fori_loop(0, tiles * tile // step_cols, feed_forward, 0)
        for which in range(tiles):
            wout_load(which).wait()

        def feed_out_part(here):
            total[:, here] = dot_nn(acts[...], wout[:, here])

        by_columns(width, step_cols, feed_out_part)
    else:
        total[...] = jnp.zeros_like(total)

        def feed_forward(which, carry):
            slot = lax.rem(which, slots)
            win_load(which).wait()
            wout_load(which).wait()
            total[...] += dot_nn(feed_part(rows_of(which, tile), win[slot]), wout[slot])

            @pl.when(which + slots < tiles)
            def _():
                win_load(which + slots).start()
                wout_load(which + slots).start()

            return carry

        lax.fori_loop(0, tiles, feed_forward, 0)

    loads[7].wait()
    loads[8].wait()
    loads[9].wait()
    act, slope = gelu_pair(dot_nn(low_two[...], wd[...]) + dbias_ref[...])
    down_act[...] = act.astype(low)
    down_slope[...] = slope.astype(low)

    def project_raise(here):
        work[:, here] += total[:, here] + 4.0 * (
            dot_nn(down_act[...], wr[:, here]) + rbias_ref[:, here]
        )

    by_columns(width, cols, project_raise)
    nothing = jnp.zeros((1, width), f32)

    def third_norm(here, carry):
        gain_sum, shift_sum, bias_sum = carry
        unit, scale = normed(work[here, :])
        gain = gain_ref[2:3, :]
        out_ref[here, :] = (unit * gain + shift_ref[2:3, :]).astype(low)
        grad = cot_ref[here, :].astype(f32)
        back = norm_back(grad * gain, scale, unit)
        total[here, :] = back
        back_low = back.astype(low)
        low_three[here, :] = back_low
        return (
            gain_sum + jnp.sum(grad * unit, axis=0, keepdims=True),
            shift_sum + jnp.sum(grad, axis=0, keepdims=True),
            bias_sum + jnp.sum(back_low.astype(f32), axis=0, keepdims=True),
        )

    gain_three, shift_three, bias_sum = by_rows(third_norm, (nothing, nothing, nothing))
    saves = []

    def save(source, target):
        copy = pltpu.make_async_copy(source, target, out_sem.at[len(saves)])
        copy.start()
        saves.append(copy)

    save(out_ref, layer_out)
    vecs_ref[0:1, :] = 4.0 * bias_sum

    back = 4.0 * dot_nt(low_three[...], wr[...]) * down_slope[...].astype(f32)
    back_low = back.astype(low)
    down_grad[...] = back_low
    vecs_ref[1:2, :] = jnp.concatenate(
        [
            jnp.sum(back_low.astype(f32), axis=0, keepdims=True),
            jnp.zeros((1, width - wd.shape[1]), f32),
        ],
        axis=1,
    )
    down = wd.shape[1]
    raise_sum = 4.0 * dot_tn(down_act[...], low_three[...])
    for index in range(width // LANES):
        sums_ref[pl.ds(down * width // LANES + index * down, down), :] = raise_sum[
            :, index * LANES : (index + 1) * LANES
        ].astype(low)
    down_sum = dot_tn(low_two[...], down_grad[...])
    for index in range(down // LANES):
        sums_ref[index * width : (index + 1) * width, :] = down_sum[
            :, index * LANES : (index + 1) * LANES
        ].astype(low)

    save(sums_ref, sums_out)

    if resident:

        def feed_slope(here):
            acts[:, here] = (
                dot_nt(low_three[...], wout[here, :]) * slopes[:, here].astype(f32)
            ).astype(low)

        by_columns(win_in.shape[1], step_cols, feed_slope)

        def feed_in_part(here):
            total[:, here] += dot_nt(acts[...], win[here, :])

        by_columns(width, step_cols, feed_in_part)
    else:

        def feed_backward(step, carry):
            which = tiles - 1 - step
            slot = lax.rem(which, slots)
            here = rows_of(which, tile)

            @pl.when(which < tiles - slots)
            def _():
                wout_load(which).wait()
                win_load(which).wait()

            grad = dot_nt(low_three[...], wout[slot]) * slopes[:, here].astype(f32)
            total[...] += dot_nt(grad.astype(low), win[slot])

            @pl.when(which >= slots)
            def _():
                win_load(which - slots).start()
                wout_load(which - slots).start()

            return carry

        lax.fori_loop(0, tiles, feed_backward, 0)

    def down_back(here):
        total[:, here] += dot_nt(down_grad[...], wd[here, :])

    by_columns(width, cols, down_back)

    def second_back(here, carry):
        gain_sum, shift_sum = carry
        grad = total[here, :]
        unit = unit_two[here, :]
        back = norm_back(grad * gain_ref[1:2, :], scale_two[here, :], unit)
        total[here, :] = back
        low_one[here, :] = back.astype(low)
        return (
            gain_sum + jnp.sum(grad * unit, axis=0, keepdims=True),
            shift_sum + jnp.sum(grad, axis=0, keepdims=True),
        )

    gain_two, shift_two = by_rows(second_back, (nothing, nothing))

    def crossed_back(here):
        crossed[:, here] = dot_nt(low_one[...], wco[here, :]).astype(low)

    by_columns(width, cols, crossed_back)

    def cross_backward(block):
        here = rows_of(block, LANES)
        grads = stacked(crossed[:, here].astype(f32))
        keys = mkey_ref[:, here].astype(f32).T.astype(low)
        slope = dot_nt(mvalue_ref[:, here], grads)
        weight_low = weights[block]
        weight = weight_low.astype(f32)
        slope = weight * (slope - jnp.sum(weight * slope, axis=0, keepdims=True))
        slope = slope.astype(low)
        queries = block_queries(here)
        mkey_ref[:, here] = dot_nn(slope, queries).astype(low)
        mvalue_ref[:, here] = dot_nn(weight_low, grads).astype(low)
        query[:, here] = (unstacked(dot_nn(keys, slope)) * 0.125).T.astype(low)

    def cross_backward_both(step, carry):
        cross_backward(2 * step)
        cross_backward(2 * step + 1)
        return carry

    lax.fori_loop(0, width // LANES // 2, cross_backward_both, 0)
    save(mkey_ref, mkey_out)
    save(mvalue_ref, mvalue_out)

    def query_back(here):
        total[:, here] += dot_nt(query[...], wcq[here, :])

    by_columns(width, cols, query_back)

    def first_back(here, carry):
        gain_sum, shift_sum = carry
        grad = total[here, :]
        unit = unit_one[here, :]
        back = norm_back(grad * gain_ref[0:1, :], scale_one[here, :], unit)
        fgrad_ref[here, :] = back
        low_one[here, :] = back.astype(low)
        return (
            gain_sum + jnp.sum(grad * unit, axis=0, keepdims=True),
            shift_sum + jnp.sum(grad, axis=0, keepdims=True),
        )

    gain_one, shift_one = by_rows(first_back, (nothing, nothing))
    save(fgrad_ref, fgrad_out)

    for index in range(width // cols):
        here = slice(index * cols, (index + 1) * cols)
        ograd_ref[here, :] = dot_nt(low_one[...], wo[here, :]).T.astype(low)
        save(ograd_ref.at[here], ograd_out.at[here])
    for index, vector in enumerate(
        (gain_one, gain_two, gain_three, shift_one, shift_two, shift_three)
    ):
        vecs_ref[2 + index : 3 + index, :] = vector
    for copy in saves:
        copy.wait()


def middle(
    tokens, attended, cotangent, mem_key, mem_value, gains, shifts, down_bias, raise_bias, weights
):
    length, width = tokens.shape
    mem_len = mem_key.shape[0]
    down = weights[3].shape[1]
    feed = weights[5].shape[1]
    tile = 512 if mem_len <= 512 else 128
    resident = mem_len <= 512
    slots = feed // tile if resident else 2
    low = jnp.bfloat16
    f32 = jnp.float32
    vmem = pl.BlockSpec(memory_space=pltpu.VMEM)
    anywhere = pl.BlockSpec(memory_space=pl.ANY)
    square = pltpu.VMEM((width, width), low)
    wide = pltpu.VMEM((length, width), f32)
    narrow = pltpu.VMEM((length, width), low)
    return pl.pallas_call(
        middle_kernel,
        out_shape=(
            jax.ShapeDtypeStruct((length, width), low),
            jax.ShapeDtypeStruct((length, width), f32),
            jax.ShapeDtypeStruct((width, length), low),
            jax.ShapeDtypeStruct((mem_len, width), low),
            jax.ShapeDtypeStruct((mem_len, width), low),
            jax.ShapeDtypeStruct((2 * down * width // LANES, LANES), low),
            jax.ShapeDtypeStruct((8, width), f32),
        ),
        in_specs=[anywhere] * 5 + [vmem] * 4 + [anywhere] * 7,
        out_specs=(anywhere,) * 6 + (vmem,),
        scratch_shapes=[
            narrow,
            narrow,
            narrow,
            pltpu.VMEM((mem_len, width), low),
            pltpu.VMEM((mem_len, width), low),
            narrow,
            wide,
            pltpu.VMEM((width, length), low),
            pltpu.VMEM((2 * down * width // LANES, LANES), low),
            square,
            square,
            square,
            pltpu.VMEM((width, down), low),
            pltpu.VMEM((down, width), low),
            pltpu.VMEM((width, feed) if resident else (slots, width, tile), low),
            pltpu.VMEM((feed, width) if resident else (slots, tile, width), low),
            wide,
            wide,
            wide,
            wide,
            pltpu.VMEM((length, 1), f32),
            pltpu.VMEM((length, 1), f32),
            narrow,
            narrow,
            narrow,
            narrow,
            narrow,
            pltpu.VMEM((width // LANES, mem_len, LANES // HD * length), low),
            pltpu.VMEM((length, feed), low),
            pltpu.VMEM((length, feed) if resident else (16, LANES), low),
            pltpu.VMEM((length, down), low),
            pltpu.VMEM((length, down), low),
            pltpu.VMEM((length, down), low),
            pltpu.SemaphoreType.DMA((10,)),
            pltpu.SemaphoreType.DMA((slots,)),
            pltpu.SemaphoreType.DMA((slots,)),
            pltpu.SemaphoreType.DMA((5 + width // 512,)),
        ],
        compiler_params=pltpu.CompilerParams(vmem_limit_bytes=VMEM_BYTES + 3 * 1024 * 1024),
        name="middle",
    )(tokens, attended, cotangent, mem_key, mem_value, gains, shifts, down_bias, raise_bias, *weights)


def per_device(
    tokens,
    memory,
    segment_ids,
    padding_mask,
    cotangent,
    prefix_embed,
    prefix_first,
    first_bias,
    prefix_second,
    second_bias,
    adapter_down,
    down_bias,
    adapter_raise,
    raise_bias,
    norm_gain,
    norm_shift,
    self_query,
    self_key,
    self_value,
    self_output,
    cross_query,
    cross_key,
    cross_value,
    cross_output,
    feed_in,
    feed_out,
):
    row_count, length, model_width = tokens.shape
    flat_rows = row_count * length
    n = lax.axis_size("seq")
    batches = lax.axis_size("batch")
    down = adapter_down.shape[1]
    attended, mem_key, mem_value, *saved = self_forward(
        n,
        segment_ids,
        padding_mask,
        tokens.reshape(flat_rows, model_width),
        (self_query, self_key, self_value),
        (
            prefix_embed,
            prefix_first,
            first_bias.reshape(1, -1),
            prefix_second,
            second_bias.reshape(1, -1),
        ),
        memory.reshape(-1, model_width),
        (cross_key, cross_value),
    )
    layer_output, first_grad, out_grad, *mem_grads, weight_sums, vector_sums = middle(
        tokens.reshape(flat_rows, model_width),
        attended,
        cotangent.reshape(flat_rows, model_width),
        mem_key,
        mem_value,
        norm_gain,
        norm_shift,
        down_bias.reshape(1, -1),
        raise_bias.reshape(1, -1),
        (
            self_output,
            cross_query,
            cross_output,
            adapter_down,
            adapter_raise,
            feed_in,
            feed_out,
        ),
    )
    layer_output = layer_output.reshape(row_count, length, model_width)
    token_grad, memory_grad, prefix_grad, vector_sums, full_sums = self_backward(
        n,
        batches,
        first_grad,
        out_grad.reshape(n, -1, HD, length),
        weight_sums,
        mem_grads,
        (cross_key, cross_value),
        vector_sums,
        saved,
        (self_query, self_key, self_value),
    )
    *replicated, token_grad, memory_grad = finish(
        full_sums.reshape(-1, LANES),
        vector_sums,
        prefix_grad,
        prefix_embed,
        prefix_first,
        first_bias.reshape(1, -1),
        prefix_second,
        down,
        token_grad,
        memory_grad,
    )
    token_grad = token_grad.reshape(row_count, length, model_width)
    memory_grad = memory_grad.reshape(memory.shape)
    replicated = [
        value.reshape(-1) if value.shape[0] == 1 else value for value in replicated
    ]
    return (layer_output, token_grad, memory_grad, *replicated)


def solution(mesh):
    placed = (
        P("batch", "seq", None),
        P("batch", "seq", None),
        P("batch", "seq"),
        P("batch", "seq"),
        P("batch", "seq", None),
        P(),
        P(),
        P(),
        P(),
        P(),
        P(),
        P(),
        P(),
        P(),
        P(),
        P(),
        P(),
        P(),
        P(),
        P(),
        P(),
        P(),
        P(),
        P(),
        P(),
        P(),
    )
    return jax.shard_map(
        per_device,
        mesh=mesh,
        in_specs=placed,
        out_specs=(
            P("batch", "seq", None),
            P("batch", "seq", None),
            P("batch", "seq", None),
            P(),
            P(),
            P(),
            P(),
            P(),
            P(),
            P(),
            P(),
            P(),
            P(),
            P(),
        ),
        check_vma=False,
    )
```

```python
import functools

import jax
import jax.numpy as jnp
from jax import lax
from jax.experimental import pallas as pl
from jax.experimental.pallas import tpu as pltpu
from jax.sharding import PartitionSpec as P

H = 16
HD = 64
LANES = 128
PREFIX_ROWS = 32
VMEM_BYTES = 60 * 1024 * 1024
SUM_ROWS = 16
MESH = pl.DeviceIdType.MESH

masked_score = -1e30
norm_eps = 1e-05

def dot_nn(left, right):
    return lax.dot_general(
        left, right, (((1,), (0,)), ((), ())), preferred_element_type=jnp.float32
    )


def dot_nt(left, right):
    return lax.dot_general(
        left, right, (((1,), (1,)), ((), ())), preferred_element_type=jnp.float32
    )


def dot_tn(left, right):
    return lax.dot_general(
        left, right, (((0,), (0,)), ((), ())), preferred_element_type=jnp.float32
    )


def remote(source, target, send_sem, recv_sem, axis, peer):
    return pltpu.make_async_remote_copy(
        src_ref=source,
        dst_ref=target,
        send_sem=send_sem,
        recv_sem=recv_sem,
        device_id={axis: peer},
        device_id_type=MESH,
    )


def enter(sizes):
    barrier = pltpu.get_barrier_semaphore()
    for axis, size in sizes.items():
        for other in range(size):

            @pl.when(other != lax.axis_index(axis))
            def _():
                pl.semaphore_signal(barrier, inc=1, device_id={axis: other}, device_id_type=MESH)

    pl.semaphore_wait(barrier, sum(sizes.values()) - len(sizes))


def others(size, mine, body):
    for other in range(size):

        @pl.when(other != mine)
        def _():
            body(other)


def rows_of(index, size):
    return pl.ds(pl.multiple_of(index * size, size), size)


def span_of(start, size):
    return pl.ds(pl.multiple_of(start, LANES), size)


def own_columns(ref, first, me, width):
    if width % LANES == 0:
        return ref[:, pl.ds(pl.multiple_of(first + me * width, LANES), width)].astype(jnp.float32)
    share = LANES // width
    block = ref[:, pl.ds(pl.multiple_of(first + me // share * LANES, LANES), LANES)].astype(
        jnp.float32
    )
    picked = block[:, :width]
    for part in range(1, share):
        picked = jnp.where(me % share == part, block[:, part * width : (part + 1) * width], picked)
    return picked


def head_lanes(shape, head):
    lane = lax.broadcasted_iota(jnp.int32, shape, 1)
    return (lane >= head * HD) & (lane < (head + 1) * HD)


def self_forward_kernel(
    n,
    seg_ref,
    pad_ref,
    tok_ref,
    wq_in,
    wk_in,
    wv_in,
    emb_ref,
    first_in,
    fbias_ref,
    second_in,
    sbias_ref,
    mem_ref,
    wck_in,
    wcv_in,
    att_ref,
    mkey_out,
    mvalue_out,
    qx_out,
    kx_out,
    raw_out,
    pk_out,
    pv_out,
    pkt_out,
    ot_out,
    lse_out,
    send,
    recv,
    meta_send,
    meta,
    kx,
    qx,
    vt,
    hidden,
    pk,
    pv,
    pkt,
    pvt,
    stat,
    acc,
    o_send,
    o_recv,
    mem_all,
    wck,
    wcv,
    mkey_ref,
    mvalue_ref,
    wq_ref,
    wk_ref,
    wv_ref,
    first_ref,
    second_ref,
    send_sem,
    recv_sem,
    meta_send_sem,
    meta_recv_sem,
    o_send_sem,
    o_recv_sem,
    mem_send_sem,
    mem_recv_sem,
    out_sem,
    weight_sem,
    in_sem,
):
    low = jnp.bfloat16
    f32 = jnp.float32
    me = lax.axis_index("seq")
    length, width = tok_ref.shape
    group = width // n
    heads = group // HD
    plane = 2 * length
    planes = n // 2
    block = 2 * LANES
    per_block = block // group
    blocks = width // block
    my_plane = me // 2
    my_side = lax.rem(me, 2)

    upward = my_plane >= planes // 2
    turn_sign = jnp.where(upward, 1, -1)

    def plane_after(step):
        return lax.rem(my_plane + planes + turn_sign * step, planes)

    def meta_copy(peer, slot):
        return remote(
            meta_send, meta.at[slot], meta_send_sem.at[peer], meta_recv_sem.at[slot], "seq", peer
        )

    def qkv_copy(head, peer, slot):
        return remote(
            send.at[peer, head],
            recv.at[head, slot],
            send_sem.at[head, peer],
            recv_sem.at[head, slot],
            "seq",
            peer,
        )

    def out_copy(head, peer, slot):
        return remote(
            o_send.at[head, peer],
            o_recv.at[slot, head],
            o_send_sem.at[head, peer],
            o_recv_sem.at[head, slot],
            "seq",
            peer,
        )

    def mem_along(which, toward):
        part = mem_all.at[which, my_side]
        return remote(
            part,
            part,
            mem_send_sem.at[(toward + 1) // 2, which],
            mem_recv_sem.at[which],
            "seq",
            me + 2 * toward,
        )

    def mem_across(side):
        part = mem_all.at[:, side]
        return remote(
            part,
            part,
            mem_send_sem.at[0, planes],
            mem_recv_sem.at[planes],
            "seq",
            me + 1 - 2 * my_side,
        )

    def mem_hops(hop, body):
        for toward in (1, -1):
            which = my_plane - toward * hop
            ahead = my_plane + toward

            @pl.when((which >= 0) & (which < planes) & (ahead >= 0) & (ahead < planes))
            def _():
                body(mem_along(which, toward))

    def mem_arrivals(hop):
        for toward in (1, -1):
            which = my_plane - toward * hop

            @pl.when((which >= 0) & (which < planes))
            def _():
                mem_along(which, -toward).wait_recv()

    def block_at(step):
        if blocks >= planes:
            share = blocks // planes
            return plane_after(1 + step // share) * share + step % share
        return lax.rem(me // per_block + 1 + step, blocks)

    def weight_load(step, which):
        columns = rows_of(block_at(step), block)
        source = (wq_in, wk_in, wv_in)[which]
        target = (wq_ref, wk_ref, wv_ref)[which]
        return pltpu.make_async_copy(
            source.at[:, columns], target.at[:, columns], weight_sem.at[step, which]
        )

    for step in range(blocks):
        for which in range(3):
            weight_load(step, which).start()
    loads = [
        pltpu.make_async_copy(source, target, in_sem.at[index])
        for index, (source, target) in enumerate(
            ((first_in, first_ref), (second_in, second_ref), (wck_in, wck), (wcv_in, wcv))
        )
    ]
    for load in loads:
        load.start()
    segments = seg_ref[...]
    tags = jnp.where(pad_ref[...] == 1, segments, -1)
    row = lax.broadcasted_iota(jnp.int32, meta_send.shape, 0)
    meta_send[...] = jnp.where(row == 0, segments, tags)
    mem_all[my_plane, my_side] = mem_ref[...]
    enter({"seq": n})
    others(n, me, lambda peer: meta_copy(peer, me).start())
    meta[me] = meta_send[...]

    for step in range(blocks):
        at = block_at(step)
        columns = rows_of(at, block)
        for which, weight in enumerate((wq_ref, wk_ref, wv_ref)):
            weight_load(step, which).wait()
            piece = dot_nn(tok_ref[...], weight[:, columns]).T.astype(low)
            for part in range(per_block):
                for head in range(heads):
                    first = part * group + head * HD
                    send[at * per_block + part, head, which] = piece[first : first + HD]
        for part in range(per_block):
            peer = at * per_block + part

            @pl.when(peer != me)
            def _():
                qkv_copy(0, peer, me).start()

            @pl.when(peer == me)
            def _():
                for head in range(heads):
                    recv[head, me] = send[peer, head]

    mem_hops(0, lambda copy: copy.start())
    loads[0].wait()
    loads[1].wait()
    hidden[...] = jnp.zeros_like(hidden)
    hidden[: emb_ref.shape[0], :] = jnp.tanh(dot_nn(emb_ref[...], first_ref[...]) + fbias_ref[...])
    hidden_low = hidden[...].astype(low)
    prefix_key = dot_nn(hidden_low, own_columns(second_ref, 0, me, group).astype(low)) + own_columns(
        sbias_ref, 0, me, group
    )
    prefix_value = dot_nn(
        hidden_low, own_columns(second_ref, width, me, group).astype(low)
    ) + own_columns(sbias_ref, width, me, group)
    prefix_row = lax.broadcasted_iota(jnp.int32, (PREFIX_ROWS, HD), 0)
    prefix_open = jnp.where(prefix_row < emb_ref.shape[0], 0.0, masked_score)
    for head in range(heads):
        here = slice(head * HD, (head + 1) * HD)
        pk[head] = jnp.concatenate([prefix_key[:, here], prefix_open], axis=1).astype(low)
        pv[head] = prefix_value[:, here].astype(low)
    pkt[...] = prefix_key.T.astype(low).reshape(heads, HD, PREFIX_ROWS)
    pvt[:, :HD, :] = prefix_value.T.astype(low).reshape(heads, HD, PREFIX_ROWS)
    pvt[:, HD:, :] = jnp.ones((heads, SUM_ROWS, PREFIX_ROWS), low)
    vt[:, HD:, :] = jnp.ones((heads, SUM_ROWS, n * length), low)

    def arrive(head, chunk):
        @pl.when(chunk != me)
        def _():
            @pl.when(head == 0)
            def _():
                meta_copy(chunk, chunk).wait_recv()

            qkv_copy(head, chunk, chunk).wait_recv()

        here = rows_of(chunk, length)
        state = lax.broadcasted_iota(jnp.int32, (HD, length), 0)
        qx[head, :HD, here] = (recv[head, chunk, 0].astype(f32) * 0.125).astype(low)
        qx[head, HD:, here] = jnp.where(state == meta[chunk, 0:1, :], 1.0, 0.0).astype(low)
        is_open = jnp.where(state == meta[chunk, 1:2, :], 0.0, masked_score)
        kx[head, here, :] = jnp.concatenate(
            [recv[head, chunk, 1].astype(f32), is_open], axis=0
        ).T.astype(low)
        vt[head, :HD, here] = recv[head, chunk, 2]

    def open_plane(head, which):
        scores = dot_nn(pk[head], qx[head, :, rows_of(which, plane)])
        top = jnp.max(scores, axis=0, keepdims=True)
        raised = jnp.exp(scores - top)
        stat[which, head, 0:1, :] = top
        acc[which, head] = dot_nn(pvt[head], raised.astype(low))

    def pair_part(head, upper, lower, first, count, keys, diagonal):
        here = slice(first, first + count)
        queries = qx[head, :, span_of(upper * plane + first, count)]
        key_rows = span_of(lower * plane, keys)
        scores = dot_nn(kx[head, key_rows, :], queries)
        if diagonal:
            key_at = lax.broadcasted_iota(jnp.int32, scores.shape, 0)
            query_at = lax.broadcasted_iota(jnp.int32, scores.shape, 1) + first
            scores = jnp.where(key_at <= query_at, scores, masked_score)
        old_top = stat[upper, head, 0:1, here]
        top = jnp.maximum(old_top, jnp.max(scores, axis=0, keepdims=True))
        raised = jnp.exp(scores - top).astype(low)
        stat[upper, head, 0:1, here] = top
        acc[upper, head, :, here] = acc[upper, head, :, here] * jnp.exp(old_top - top) + dot_nn(
            vt[head, :, key_rows], raised
        )

    def pair(head, upper, lower):
        pair_part(head, upper, lower, 0, plane, plane, False)

    def pair_diagonal(head, which):
        for part in range(2):
            pair_part(head, which, which, part * length, length, (part + 1) * length, True)

    def close_plane(head, which):
        total = acc[which, head, HD : HD + 1, :]
        value = acc[which, head, :HD, :] / total
        acc[which, head, :HD, :] = value
        stat[which, head, 0:1, :] = stat[which, head, 0:1, :] + jnp.log(total)
        for part in range(2):
            chunk = 2 * which + part
            o_send[head, chunk] = value[:, part * length : (part + 1) * length].astype(low)

            @pl.when((chunk != me) & (head == heads - 1))
            def _():
                out_copy(head, chunk, me).start()

            @pl.when(chunk == me)
            def _():
                o_recv[me, head] = o_send[head, chunk]

    def project_memory():
        mem_across(1 - my_side).wait_recv()
        for load in loads[2:]:
            load.wait()
        whole = mem_all[...].reshape(mkey_ref.shape)

        def one(index, carry):
            here = rows_of(index, block)
            mkey_ref[:, here] = dot_nn(whole, wck[:, here]).astype(low)
            mvalue_ref[:, here] = dot_nn(whole, wcv[:, here]).astype(low)
            return carry

        lax.fori_loop(0, blocks, one, 0)

    def stage(index, carry):
        head = index // planes
        step = lax.rem(index, planes)

        @pl.when(head + 1 < heads)
        def _():
            there = plane_after(1 + step)
            for part in range(2):
                peer = 2 * there + part

                @pl.when(peer != me)
                def _():
                    qkv_copy(head, peer, me).wait_send()
                    qkv_copy(head + 1, peer, me).start()

        @pl.when((head == heads - 1) & (head > 0))
        def _():
            there = plane_after(1 + step)
            for part in range(2):
                peer = 2 * there + part

                @pl.when(peer != me)
                def _():
                    qkv_copy(head, peer, me).wait_send()
                    out_copy(head - 1, peer, me).start()

        here = plane_after(step)
        arrive(head, 2 * here)
        arrive(head, 2 * here + 1)
        open_plane(head, here)
        pair_diagonal(head, here)

        def earlier(back, inner):
            there = plane_after(back)
            pair(head, jnp.maximum(here, there), jnp.minimum(here, there))

            @pl.when((step == planes - 1) & (there > here))
            def _():
                close_plane(head, there)

            return inner

        lax.fori_loop(0, step, earlier, 0)
        for hop in range(1, planes - 1):

            @pl.when(index == hop)
            def _():
                mem_arrivals(hop)
                mem_hops(hop, lambda copy: copy.start())

        @pl.when(index == planes - 1)
        def _():
            mem_arrivals(planes - 1)
            mem_across(my_side).start()

        @pl.when((upward & (my_plane + step >= planes)) | (step == planes - 1))
        def _():
            close_plane(head, here)

        @pl.when(jnp.logical_not(upward) & (step == my_plane))
        def _():
            def close(which, inner):
                close_plane(head, which)
                return inner

            lax.fori_loop(0, my_plane + 1, close, 0)

        return carry

    lax.fori_loop(0, heads * planes, stage, 0)

    saves = []

    def save(source, target):
        copy = pltpu.make_async_copy(source, target, out_sem.at[len(saves)])
        copy.start()
        saves.append(copy)

    save(qx, qx_out)
    save(kx, kx_out)
    save(recv, raw_out)
    save(pk, pk_out)
    save(pv, pv_out)
    save(pkt, pkt_out)
    save(acc, ot_out)
    save(stat, lse_out)
    project_memory()
    save(mkey_ref, mkey_out)
    save(mvalue_ref, mvalue_out)
    for other in range(n):

        @pl.when(other != me)
        def _():
            for head in range(heads):
                out_copy(head, other, other).wait_recv()

        att_ref[:, other * group : (other + 1) * group] = (
            o_recv[other].reshape(group, length).astype(f32).T.astype(low)
        )

    def drain(peer):
        meta_copy(peer, me).wait_send()
        if heads == 1:
            qkv_copy(0, peer, me).wait_send()
        for head in range(heads):
            out_copy(head, peer, me).wait_send()

    others(n, me, drain)
    for hop in range(planes - 1):
        mem_hops(hop, lambda copy: copy.wait_send())
    mem_across(my_side).wait_send()
    for copy in saves:
        copy.wait()


def self_forward(n, segments, padding, tokens, weights, prefix, memory, mem_weights):
    length, width = tokens.shape
    group = width // n
    heads = group // HD
    whole = n * length
    planes = n // 2
    low = jnp.bfloat16
    f32 = jnp.float32
    vmem = pl.BlockSpec(memory_space=pltpu.VMEM)
    anywhere = pl.BlockSpec(memory_space=pl.ANY)
    dma = pltpu.SemaphoreType.DMA
    shapes = (
        ((heads, 2 * HD, whole), low),
        ((heads, whole, 2 * HD), low),
        ((heads, n, 3, HD, length), low),
        ((heads, PREFIX_ROWS, 2 * HD), low),
        ((heads, PREFIX_ROWS, HD), low),
        ((heads, HD, PREFIX_ROWS), low),
        ((planes, heads, HD + SUM_ROWS, 2 * length), f32),
        ((planes, heads, 8, 2 * length), f32),
    )
    square = pltpu.VMEM((width, width), low)
    qx, kx, raw, pk, pv, pkt, acc, stat = (pltpu.VMEM(*shape) for shape in shapes)
    return pl.pallas_call(
        functools.partial(self_forward_kernel, n),
        out_shape=(
            jax.ShapeDtypeStruct((length, width), low),
            jax.ShapeDtypeStruct((n * memory.shape[0], width), low),
            jax.ShapeDtypeStruct((n * memory.shape[0], width), low),
        )
        + tuple(jax.ShapeDtypeStruct(*shape) for shape in shapes),
        in_specs=[vmem] * 3
        + [anywhere] * 3
        + [vmem, anywhere, vmem, anywhere, vmem, vmem]
        + [anywhere] * 2,
        out_specs=(vmem,) + (anywhere,) * 10,
        scratch_shapes=[
            pltpu.VMEM((n, heads, 3, HD, length), low),
            raw,
            pltpu.VMEM((8, length), jnp.int32),
            pltpu.VMEM((n, 8, length), jnp.int32),
            kx,
            qx,
            pltpu.VMEM((heads, HD + SUM_ROWS, whole), low),
            pltpu.VMEM((PREFIX_ROWS, weights[0].shape[0] // 2), f32),
            pk,
            pv,
            pkt,
            pltpu.VMEM((heads, HD + SUM_ROWS, PREFIX_ROWS), low),
            stat,
            acc,
            pltpu.VMEM((heads, n, HD, length), low),
            pltpu.VMEM((n, heads, HD, length), low),
            pltpu.VMEM((planes, 2) + memory.shape, low),
            square,
            square,
            pltpu.VMEM((n * memory.shape[0], width), low),
            pltpu.VMEM((n * memory.shape[0], width), low),
            square,
            square,
            square,
            pltpu.VMEM(prefix[1].shape, low),
            pltpu.VMEM(prefix[3].shape, low),
            dma((heads, n)),
            dma((heads, n)),
            dma((n,)),
            dma((n,)),
            dma((heads, n)),
            dma((heads, n)),
            dma((2, planes + 1)),
            dma((planes + 1,)),
            dma((10,)),
            dma((width // (2 * LANES), 3)),
            dma((4,)),
        ],
        compiler_params=pltpu.CompilerParams(
            collective_id=0, has_side_effects=True, vmem_limit_bytes=VMEM_BYTES
        ),
        name="self_forward",
    )(segments, padding, tokens, *weights, *prefix, memory, *mem_weights)


def self_backward_kernel(
    n,
    batches,
    base_in,
    do_in,
    sums_in,
    mkey_in,
    mvalue_in,
    wck_in,
    wcv_in,
    vecs_in,
    qx_in,
    kx_in,
    raw_in,
    pk_in,
    pv_in,
    pkt_in,
    ot_in,
    lse_in,
    wq_in,
    wk_in,
    wv_in,
    tg_ref,
    mgrad_ref,
    pkv_ref,
    vecs_ref,
    full_out,
    do_recv,
    qx,
    kx,
    raw,
    kt,
    values,
    dot,
    qdo,
    pk,
    pv,
    pkt,
    ot,
    stat,
    weights,
    dqt,
    dkv,
    g_send,
    g_recv,
    pre_ref,
    pre_all,
    pre_sum,
    pre_recv,
    sums_mine,
    sums_core,
    sums_x,
    sums_side,
    sums_z,
    full,
    mkey,
    mvalue,
    wck,
    wcv,
    mem_part,
    mem_side,
    mem_up,
    mem_down,
    vec_all,
    vec_sum,
    vec_y,
    vec_both,
    vec_z,
    product,
    base_ref,
    do_send_sem,
    do_recv_sem,
    g_send_sem,
    g_recv_sem,
    in_sem,
    send_sem,
    recv_sem,
):
    low = jnp.bfloat16
    f32 = jnp.float32
    me = lax.axis_index("seq")
    length, width = tg_ref.shape
    group = width // n
    heads = group // HD
    plane = 2 * length
    planes = n // 2
    step_rows = 256
    my_batch = lax.axis_index("batch")
    my_core = lax.rem(my_batch, 2)
    my_high = my_batch // 2
    highs = batches // 2
    my_plane = me // 2
    my_side = lax.rem(me, 2)
    beside = me + 1 - 2 * my_side
    used = [0]

    def numbers(count):
        used[0] += count
        return used[0] - count

    core_slot = numbers(2)
    x_slot = numbers(2 * highs)
    y_slot = numbers(3)
    z_slot = numbers(2 * planes)
    up_slot = numbers(planes)
    down_slot = numbers(planes)
    va_slot = numbers(batches)
    vb_slot = numbers(1)
    vc_slot = numbers(planes)
    pa_slot = numbers(batches)
    pb_slot = numbers(n)

    def send(source, target, first, peer_index, slot_index, axis, peer):
        return remote(
            source,
            target,
            send_sem.at[first + peer_index],
            recv_sem.at[first + slot_index],
            axis,
            peer,
        )

    half_rows = 2 * planes * highs * sums_z.shape[1]
    x_rows = half_rows // highs
    y_rows = x_rows // 2
    z_rows = y_rows // planes
    x_row = pl.multiple_of(my_high * x_rows, x_rows)
    y_row = pl.multiple_of(x_row + my_side * y_rows, y_rows)

    def part(row, count):
        return sums_mine.at[pl.ds(pl.multiple_of(row, count), count)]

    def reduce_core():
        return send(
            sums_in.at[1 - my_core], sums_core, core_slot, 0, 0, "batch", my_batch + 1 - 2 * my_core
        )

    def reduce_x(peer, slot):
        return send(
            part(peer * x_rows, x_rows),
            sums_x.at[slot],
            x_slot,
            peer,
            slot,
            "batch",
            2 * peer + my_core,
        )

    def reduce_y():
        return send(
            part(x_row + (1 - my_side) * y_rows, y_rows), sums_side, y_slot, 0, 0, "seq", beside
        )

    def reduce_z(peer, slot):
        return send(
            part(y_row + peer * z_rows, z_rows),
            sums_z.at[slot],
            z_slot,
            peer,
            slot,
            "seq",
            2 * peer + my_side,
        )

    def gather_z(peer, slot):
        piece = full.at[my_core, my_high, my_side, slot]
        return send(piece, piece, z_slot + planes, peer, slot, "seq", 2 * peer + my_side)

    def gather_y(side):
        piece = full.at[my_core, my_high, side]
        return send(piece, piece, y_slot + 1, 0, 0, "seq", beside)

    def gather_x(peer, slot):
        piece = full.at[my_core, slot]
        return send(piece, piece, x_slot + highs, peer, slot, "batch", 2 * peer + my_core)

    def gather_core(core):
        piece = full.at[core]
        return send(piece, piece, core_slot + 1, 0, 0, "batch", my_batch + 1 - 2 * my_core)

    def mem_across():
        return send(
            mem_part.at[:, 1 - my_side], mem_side, y_slot + 2, 0, 0, "seq", beside
        )

    def mem_hop(target, toward, peer=None):
        buffer, slot = (mem_up, up_slot) if toward > 0 else (mem_down, down_slot)
        return send(
            mem_part.at[target, my_side],
            buffer.at[target],
            slot,
            target,
            target,
            "seq",
            me + 2 * toward if peer is None else peer,
        )

    def mem_from(target, toward):
        return mem_hop(target, toward, me - 2 * toward)

    def mem_pass(toward):
        buffer = mem_up if toward > 0 else mem_down
        first = 0 if toward > 0 else planes - 1
        for target in range(planes):

            @pl.when((target - my_plane) * toward > 0)
            def _():
                @pl.when(my_plane != first)
                def _():
                    mem_from(target, toward).wait_recv()
                    mem_part[target, my_side] = (
                        mem_part[target, my_side].astype(f32) + buffer[target].astype(f32)
                    ).astype(low)

                mem_hop(target, toward).start()

    def mem_stage(at):
        pl.when(my_plane == at)(lambda: mem_pass(1))
        pl.when(my_plane == planes - 1 - at)(lambda: mem_pass(-1))

    def mem_end():
        value = mem_part[my_plane, my_side].astype(f32)
        mgrad_ref[...] = value.astype(low)

        @pl.when(my_plane > 0)
        def _():
            mem_from(my_plane, 1).wait_recv()
            mgrad_ref[...] = (mgrad_ref[...].astype(f32) + mem_up[my_plane].astype(f32)).astype(low)

        @pl.when(my_plane < planes - 1)
        def _():
            mem_from(my_plane, -1).wait_recv()
            mgrad_ref[...] = (
                mgrad_ref[...].astype(f32) + mem_down[my_plane].astype(f32)
            ).astype(low)

    def mem_drain():
        for target in range(planes):

            @pl.when(target > my_plane)
            def _():
                mem_hop(target, 1).wait_send()

            @pl.when(target < my_plane)
            def _():
                mem_hop(target, -1).wait_send()

    def vec_a(peer, slot):
        return send(vecs_in, vec_all.at[slot], va_slot, peer, slot, "batch", peer)

    def vec_b(side):
        return send(vec_sum, vec_y.at[side], vb_slot, 0, 0, "seq", beside)

    def vec_c(peer, slot):
        return send(vec_both, vec_z.at[slot], vc_slot, peer, slot, "seq", 2 * peer + my_side)

    def pre_a(peer, slot):
        return send(pre_ref, pre_all.at[slot], pa_slot, peer, slot, "batch", peer)

    def pre_b(peer, slot):
        return send(pre_sum, pre_recv.at[slot], pb_slot, peer, slot, "seq", peer)

    def do_copy(head, peer, slot):
        return remote(
            do_in.at[peer, head],
            do_recv.at[head, slot],
            do_send_sem.at[head, peer],
            do_recv_sem.at[head, slot],
            "seq",
            peer,
        )

    def q_copy(head, peer, slot):
        return remote(
            g_send.at[peer, head, 0],
            g_recv.at[0, slot, head],
            g_send_sem.at[0, head, peer],
            g_recv_sem.at[0, head, slot],
            "seq",
            peer,
        )

    def kv_copy(head, peer, slot):
        return remote(
            g_send.at[peer, head, pl.ds(1, 2)],
            g_recv.at[pl.ds(1, 2), slot, head],
            g_send_sem.at[1, head, peer],
            g_recv_sem.at[1, head, slot],
            "seq",
            peer,
        )

    def far_first(body):
        for index in range(n):
            peer = jnp.where(my_plane < planes // 2, n - 1 - index, index)

            @pl.when(peer != me)
            def _():
                body(peer)

    def added(ref, size):
        value = ref[0].astype(f32)
        for other in range(1, size):
            value = value + ref[other].astype(f32)
        return value

    loads = [
        pltpu.make_async_copy(source, target, in_sem.at[index])
        for index, (source, target) in enumerate(
            (
                (raw_in, raw),
                (kx_in, kx),
                (pk_in, pk),
                (pv_in, pv),
                (pkt_in, pkt),
                (qx_in, qx),
                (ot_in, ot),
                (lse_in, stat),
                (sums_in.at[my_core], sums_mine),
                (vecs_in, vec_all.at[my_batch]),
                (mkey_in, mkey),
                (mvalue_in, mvalue),
                (wck_in, wck),
                (wcv_in, wcv),
                (base_in, base_ref),
                (wq_in, weights.at[0]),
                (wk_in, weights.at[1]),
                (wv_in, weights.at[2]),
            )
        )
    ]
    own_do = pltpu.make_async_copy(do_in.at[me], do_recv.at[:, me], in_sem.at[len(loads)])
    own_do.start()
    for load in loads:
        load.start()
    enter({"seq": n, "batch": batches})
    far_first(lambda peer: do_copy(0, peer, me).start())
    reduce_core().start()
    others(batches, my_batch, lambda peer: vec_a(peer, my_batch).start())
    dkv[...] = jnp.zeros_like(dkv)
    product[...] = jnp.zeros_like(product)
    pre_ref[...] = jnp.zeros_like(pre_ref)
    for load in loads[:14]:
        load.wait()
    own_do.wait()

    def turn(index, carry):
        head = index // n
        chunk = lax.rem(index, n)
        here = rows_of(chunk, length)
        kt[head, :, here] = raw[head, chunk, 1]
        values[head, here, :] = raw[head, chunk, 2].astype(f32).T.astype(low)
        return carry

    lax.fori_loop(0, heads * n, turn, 0)

    def memory_back(index, carry):
        here = rows_of(index, step_rows)
        value = dot_nt(mkey[...], wck[here, :]) + dot_nt(mvalue[...], wcv[here, :])
        mem_part[:, :, :, here] = value.astype(low).reshape(mem_part.shape[:3] + (step_rows,))
        return carry

    lax.fori_loop(0, width // step_rows, memory_back, 0)
    mem_across().start()

    def next_head(head):
        def move(peer):
            do_copy(head, peer, me).wait_send()
            do_copy(head + 1, peer, me).start()

        far_first(move)

    def arrive(head, which):
        for part in range(2):
            chunk = 2 * which + part

            @pl.when(chunk != me)
            def _():
                do_copy(head, chunk, chunk).wait_recv()

            grads = do_recv[head, chunk]
            dot[head, :, rows_of(chunk, length)] = grads
            grads = grads.astype(f32)
            query = raw[head, chunk, 0].astype(f32) * 0.125
            qdo[head, rows_of(chunk, length), :] = (
                jnp.concatenate([query, grads], axis=0).T.astype(low)
            )
            here = slice(part * length, (part + 1) * length)
            stat[which, head, 1:2, here] = jnp.sum(
                grads * ot[which, head, :HD, here], axis=0, keepdims=True
            )
        here = rows_of(which, plane)
        weight = jnp.exp(dot_nn(pk[head], qx[head, :, here]) - stat[which, head, 0:1, :])
        slope = weight * (dot_nn(pv[head], dot[head, :, here]) - stat[which, head, 1:2, :])
        both = jnp.concatenate([slope, weight], axis=0).astype(low)
        sums = dot_nn(both, qdo[head, here, :])
        pre_ref[head] += jnp.where(
            head_lanes((PREFIX_ROWS, 2 * HD), 0), sums[:PREFIX_ROWS], sums[PREFIX_ROWS:]
        )
        slope = slope.astype(low)
        dqt[which, head] = dot_nn(pkt[head], slope)

    def plus(first, second):
        return (first.astype(f32) + second.astype(f32)).astype(low)

    def sum_one():
        reduce_core().wait_recv()
        sums_mine[...] = plus(sums_mine[...], sums_core[...])
        others(highs, my_high, lambda peer: reduce_x(peer, my_high).start())

    def sum_two():
        here = pl.ds(x_row, x_rows)
        others(highs, my_high, lambda peer: reduce_x(peer, peer).wait_recv())
        sums_x[my_high] = sums_mine[here]
        sums_mine[here] = added(sums_x, highs).astype(low)
        reduce_y().start()

    def sum_three():
        here = pl.ds(y_row, y_rows)
        reduce_y().wait_recv()
        sums_mine[here] = plus(sums_mine[here], sums_side[...])
        others(planes, my_plane, lambda peer: reduce_z(peer, my_plane).start())

    def sum_four():
        here = pl.ds(pl.multiple_of(y_row + my_plane * z_rows, z_rows), z_rows)
        others(planes, my_plane, lambda peer: reduce_z(peer, peer).wait_recv())
        sums_z[my_plane] = sums_mine[here]
        full[my_core, my_high, my_side, my_plane] = added(sums_z, planes).astype(low)
        others(planes, my_plane, lambda peer: gather_z(peer, my_plane).start())

    def sum_five():
        others(planes, my_plane, lambda peer: gather_z(peer, peer).wait_recv())
        gather_y(my_side).start()

    def sum_six():
        gather_y(1 - my_side).wait_recv()
        others(highs, my_high, lambda peer: gather_x(peer, my_high).start())

    def sum_seven():
        others(highs, my_high, lambda peer: gather_x(peer, peer).wait_recv())
        gather_core(my_core).start()

    def sum_end():
        gather_core(1 - my_core).wait_recv()
        save_full.start()

    def vec_one():
        others(batches, my_batch, lambda peer: vec_a(peer, peer).wait_recv())
        vec_sum[...] = added(vec_all, batches)
        vec_b(my_side).start()
        vec_y[my_side] = vec_sum[...]

    def vec_two():
        vec_b(1 - my_side).wait_recv()
        value = (vec_y[0] + vec_y[1]).astype(f32)
        vec_both[...] = jnp.concatenate(
            [value[:, : width // 2], value[:, width // 2 :]], axis=0
        ).astype(low)
        others(planes, my_plane, lambda peer: vec_c(peer, my_plane).start())
        vec_z[my_plane] = vec_both[...]

    def vec_end():
        others(planes, my_plane, lambda peer: vec_c(peer, peer).wait_recv())
        value = added(vec_z, planes)
        vecs_ref[:, : width // 2] = value[:8]
        vecs_ref[:, width // 2 :] = value[8:]

    def mem_one():
        mem_across().wait_recv()
        mem_part[:, my_side] = plus(mem_part[:, my_side], mem_side[...])

    def stage_pa():
        others(batches, my_batch, lambda peer: pre_a(peer, my_batch).start())
        pre_all[my_batch] = pre_ref[...]

    def stage_pb():
        others(batches, my_batch, lambda peer: pre_a(peer, peer).wait_recv())
        pre_sum[...] = added(pre_all, batches).astype(low)
        others(n, me, lambda peer: pre_b(peer, me).start())
        pre_recv[me] = pre_sum[...]

    save_full = pltpu.make_async_copy(full, full_out, in_sem.at[0])

    def pair_part(head, upper, lower, first, count, diagonal, at=None):
        keys = span_of(lower * plane + (first if at is None else at * count), count)
        here = span_of(upper * plane + first, plane - first)
        at = slice(first, plane)
        scores = dot_nn(kx[head, keys, :], qx[head, :, here])
        slope = dot_nn(values[head, keys, :], dot[head, :, here]) - stat[upper, head, 1:2, at]
        weight = jnp.exp(scores - stat[upper, head, 0:1, at])
        if diagonal:
            key_at = lax.broadcasted_iota(jnp.int32, scores.shape, 0)
            query_at = lax.broadcasted_iota(jnp.int32, scores.shape, 1)
            weight = jnp.where(key_at <= query_at, weight, 0.0)
        slope = (weight * slope).astype(low)
        key_part = dot_nn(slope, qdo[head, here, :])
        value_part = dot_nn(weight.astype(low), qdo[head, here, :])
        dkv[head, keys, :] += jnp.where(head_lanes((count, 2 * HD), 0), key_part, value_part)
        dqt[upper, head, :, at] += dot_nn(kt[head, :, keys], slope)

    def pair(head, upper, lower, diagonal):
        if diagonal:
            for part in range(plane // step_rows):
                pair_part(head, upper, lower, part * step_rows, step_rows, True)
        else:

            def one(at, carry):
                pair_part(head, upper, lower, 0, step_rows, False, at)
                return carry

            lax.fori_loop(0, plane // step_rows, one, 0)

    def hand_queries(head, which):
        for part in range(2):
            chunk = 2 * which + part
            g_send[chunk, head, 0] = (
                dqt[which, head, :, part * length : (part + 1) * length] * 0.125
            ).astype(low)

            @pl.when(chunk != me)
            def _():
                q_copy(head, chunk, me).start()

            @pl.when(chunk == me)
            def _():
                g_recv[0, me, head] = g_send[chunk, head, 0]

    def hand_keys(head, which):
        for part in range(2):
            chunk = 2 * which + part
            turned = dkv[head, rows_of(chunk, length), :].T.astype(low)
            g_send[chunk, head, 1] = turned[:HD]
            g_send[chunk, head, 2] = turned[HD:]

            @pl.when(chunk != me)
            def _():
                kv_copy(head, chunk, me).start()

            @pl.when(chunk == me)
            def _():
                g_recv[pl.ds(1, 2), me, head] = g_send[chunk, head, pl.ds(1, 2)]

    rising = my_plane >= planes // 2
    total = heads * planes * (planes + 1) // 2
    hooks = [
        (2, sum_one),
        (3, mem_one),
        (4, lambda: mem_stage(0)),
        (5, vec_one),
        (5, sum_two),
        (7, sum_three),
        (8, vec_two),
        (10, sum_four),
        (12, sum_five),
        (14, sum_six),
        (16, vec_end),
        (17, sum_seven),
    ] + [(4 + 3 * at, functools.partial(mem_stage, at)) for at in range(1, planes - 1)]
    hooks += [
        (1 + head * total // heads, functools.partial(next_head, head)) for head in range(heads - 1)
    ]
    final = total - planes * (planes + 1) // 2
    hooks += [(final + planes + 1, stage_pa), (final + 2 * planes - 1, stage_pb)]

    def hook(pairs):
        for number, body in sorted(hooks, key=lambda item: item[0]):
            pl.when(pairs == number)(body)


    def stage(index, carry):
        head = index // planes
        step = lax.rem(index, planes)
        here = jnp.where(rising, step, planes - 1 - step)

        @pl.when((step == 0) | ((step == 1) & jnp.logical_not(rising)))
        def _():
            @pl.when(rising | (step == 0))
            def _():
                arrive(head, here)

            @pl.when(jnp.logical_not(rising) & (step == 1))
            def _():
                def rest(which, inner):
                    arrive(head, planes - 2 - which)
                    return inner

                lax.fori_loop(0, planes - 1, rest, 0)

        begun = head * (planes * (planes + 1) // 2) + step * planes - step * (step - 1) // 2
        hook(begun)
        pair(head, here, here, True)

        @pl.when(rising)
        def _():
            hand_queries(head, here)

        @pl.when(jnp.logical_not(rising))
        def _():
            hand_keys(head, here)

        def far(at, inner):
            there = jnp.where(rising, here + 1 + at, here - 1 - at)

            @pl.when(rising & (step == 0))
            def _():
                arrive(head, there)

            hook(begun + 1 + at)
            pair(head, jnp.maximum(here, there), jnp.minimum(here, there), False)
            return inner

        lax.fori_loop(0, planes - 1 - step, far, 0)

        @pl.when(rising)
        def _():
            hand_keys(head, here)

        @pl.when(jnp.logical_not(rising))
        def _():
            hand_queries(head, here)

        return carry

    lax.fori_loop(0, heads * planes, stage, 0)
    mem_end()
    for load in loads[14:]:
        load.wait()

    def gathered(peer):
        for head in range(heads):
            q_copy(head, peer, peer).wait_recv()
            kv_copy(head, peer, peer).wait_recv()

    half = width // 2

    def gather_plane(step, carry):
        which = lax.rem(my_plane + step, planes)
        for part in range(2):
            peer = 2 * which + part

            @pl.when(peer != me)
            def _():
                gathered(peer)

        columns = rows_of(which, 2 * group)
        for part in range(2):
            here = slice(part * half, (part + 1) * half)
            value = product[here, :]
            for kind in range(3):
                grads = g_recv[kind, pl.ds(2 * which, 2)].reshape(2 * group, length)
                value = value + dot_nn(weights[kind, here, columns], grads)
            product[here, :] = value
        return carry

    lax.fori_loop(0, planes, gather_plane, 0)
    sum_end()
    tile = 256
    for index in range(width // tile):
        here = slice(index * tile, (index + 1) * tile)
        tg_ref[:, here] = (base_ref[:, here] + product[here, :].T).astype(low)
    for other in range(n):

        @pl.when(other != me)
        def _():
            pre_b(other, other).wait_recv()

        value = pre_recv[other].astype(f32)
        for which in range(2):
            pkv_ref[:, which * width + other * group : which * width + (other + 1) * group] = (
                jnp.concatenate(
                    [value[head, :, which * HD : (which + 1) * HD] for head in range(heads)], axis=1
                )
            )

    def drain(peer):
        do_copy(heads - 1, peer, me).wait_send()
        pre_b(peer, me).wait_send()
        for head in range(heads):
            q_copy(head, peer, me).wait_send()
            kv_copy(head, peer, me).wait_send()

    others(n, me, drain)
    others(batches, my_batch, lambda peer: pre_a(peer, my_batch).wait_send())
    others(batches, my_batch, lambda peer: vec_a(peer, my_batch).wait_send())
    reduce_core().wait_send()
    others(highs, my_high, lambda peer: reduce_x(peer, my_high).wait_send())
    reduce_y().wait_send()
    others(planes, my_plane, lambda peer: reduce_z(peer, my_plane).wait_send())
    others(planes, my_plane, lambda peer: gather_z(peer, my_plane).wait_send())
    gather_y(my_side).wait_send()
    others(highs, my_high, lambda peer: gather_x(peer, my_high).wait_send())
    gather_core(my_core).wait_send()
    mem_across().wait_send()
    mem_drain()
    others(planes, my_plane, lambda peer: vec_c(peer, my_plane).wait_send())
    vec_b(my_side).wait_send()
    save_full.wait()


def self_backward(
    n, batches, first_grad, out_grad, sums, mem_grads, mem_weights, vecs, saved, weights
):
    length, width = first_grad.shape
    group = width // n
    heads = group // HD
    whole = n * length
    planes = n // 2
    low = jnp.bfloat16
    f32 = jnp.float32
    vmem = pl.BlockSpec(memory_space=pltpu.VMEM)
    anywhere = pl.BlockSpec(memory_space=pl.ANY)
    dma = pltpu.SemaphoreType.DMA
    sum_rows = sums.shape[0] // (n * batches)
    mem_len = mem_grads[0].shape[0]
    mem_rows = mem_len // n
    mem_part = pltpu.VMEM((planes, mem_rows, width), low)
    mem_low = pltpu.VMEM((mem_len, width), low)
    square = pltpu.VMEM((width, width), low)
    vec = pltpu.VMEM((8, width), f32)
    copies = 6 + 2 * (batches // 2) + 5 * planes + 2 * batches + n
    qx, kx, raw, pk, pv, pkt, ot, stat = (pltpu.VMEM(value.shape, value.dtype) for value in saved)
    return pl.pallas_call(
        functools.partial(self_backward_kernel, n, batches),
        out_shape=(
            jax.ShapeDtypeStruct((length, width), low),
            jax.ShapeDtypeStruct((mem_rows, width), low),
            jax.ShapeDtypeStruct((PREFIX_ROWS, 2 * width), f32),
            jax.ShapeDtypeStruct((8, width), f32),
            jax.ShapeDtypeStruct((2, batches // 2, 2, planes, sum_rows, LANES), low),
        ),
        in_specs=[anywhere] * 19,
        out_specs=(vmem, vmem, vmem, vmem, anywhere),
        scratch_shapes=[
            pltpu.VMEM((heads, n, HD, length), low),
            qx,
            kx,
            raw,
            pltpu.VMEM((heads, HD, whole), low),
            pltpu.VMEM((heads, whole, HD), low),
            pltpu.VMEM((heads, HD, whole), low),
            pltpu.VMEM((heads, whole, 2 * HD), low),
            pk,
            pv,
            pkt,
            ot,
            stat,
            pltpu.VMEM((3, width, width), low),
            pltpu.VMEM((planes, heads, HD, 2 * length), f32),
            pltpu.VMEM((heads, whole, 2 * HD), f32),
            pltpu.VMEM((n, heads, 3, HD, length), low),
            pltpu.VMEM((3, n, heads, HD, length), low),
            pltpu.VMEM((heads, PREFIX_ROWS, 2 * HD), f32),
            pltpu.VMEM((batches, heads, PREFIX_ROWS, 2 * HD), f32),
            pltpu.VMEM((heads, PREFIX_ROWS, 2 * HD), low),
            pltpu.VMEM((n, heads, PREFIX_ROWS, 2 * HD), low),
            pltpu.VMEM((sums.shape[0] // 2, LANES), low),
            pltpu.VMEM((sums.shape[0] // 2, LANES), low),
            pltpu.VMEM((batches // 2, sums.shape[0] // batches, LANES), low),
            pltpu.VMEM((planes * sum_rows, LANES), low),
            pltpu.VMEM((planes, sum_rows, LANES), low),
            pltpu.VMEM((2, batches // 2, 2, planes, sum_rows, LANES), low),
            mem_low,
            mem_low,
            square,
            square,
            pltpu.VMEM((planes, 2, mem_rows, width), low),
            mem_part,
            mem_part,
            mem_part,
            pltpu.VMEM((batches, 8, width), f32),
            vec,
            pltpu.VMEM((2, 8, width), f32),
            pltpu.VMEM((16, width // 2), low),
            pltpu.VMEM((planes, 16, width // 2), low),
            pltpu.VMEM((width, length), f32),
            pltpu.VMEM((length, width), f32),
            dma((heads, n)),
            dma((heads, n)),
            dma((2, heads, n)),
            dma((2, heads, n)),
            dma((19,)),
            dma((copies,)),
            dma((copies,)),
        ],
        compiler_params=pltpu.CompilerParams(
            collective_id=1, has_side_effects=True, vmem_limit_bytes=VMEM_BYTES
        ),
        name="self_backward",
    )(
        first_grad,
        out_grad,
        sums.reshape(2, -1, LANES),
        *mem_grads,
        *mem_weights,
        vecs,
        *saved,
        *weights,
    )


def both_parts(value):
    high = value.astype(jnp.bfloat16).astype(jnp.float32)
    return jnp.concatenate([high, value - high], axis=0).astype(jnp.bfloat16)


def finish_kernel(
    full_in,
    vecs_ref,
    pkv_ref,
    emb_ref,
    first_in,
    fbias_ref,
    second_in,
    token_in,
    mem_in,
    embed_out,
    first_out,
    fbias_out,
    second_out,
    sbias_out,
    down_out,
    dbias_out,
    raise_out,
    rbias_out,
    gain_out,
    shift_out,
    token_out,
    mem_out,
    full_ref,
    first_ref,
    second_ref,
    token_ref,
    mem_ref,
    first_grad,
    second_grad,
    down_grad,
    raise_grad,
    emb,
    hidden,
    out_sem,
    in_sem,
):
    f32 = jnp.float32
    low = jnp.bfloat16
    width = emb_ref.shape[1]
    down = dbias_out.shape[1]
    count = emb_ref.shape[0]
    first = down * width // LANES
    loads = [
        pltpu.make_async_copy(source, target, in_sem.at[index])
        for index, (source, target) in enumerate(
            (
                (full_in.at[first:], full_ref.at[first:]),
                (full_in.at[:first], full_ref.at[:first]),
                (first_in, first_ref),
                (second_in, second_ref),
                (token_in, token_ref),
                (mem_in, mem_ref),
            )
        )
    ]
    for load in loads:
        load.start()
    saves = []

    def save(source, target, rows=None):
        if rows is not None:
            source, target = source.at[rows], target.at[rows]
        copy = pltpu.make_async_copy(source, target, out_sem.at[len(saves)])
        copy.start()
        saves.append(copy)

    loads[0].wait()
    for index in range(width // LANES):
        raise_grad[:, index * LANES : (index + 1) * LANES] = full_ref[
            first + index * down : first + (index + 1) * down, :
        ].astype(f32)
    save(raise_grad, raise_out)
    loads[1].wait()
    for index in range(down // LANES):
        down_grad[:, index * LANES : (index + 1) * LANES] = full_ref[
            index * width : (index + 1) * width, :
        ].astype(f32)
    save(down_grad, down_out)
    for load in loads[4:]:
        load.wait()
    save(token_ref, token_out)
    save(mem_ref, mem_out)
    loads[2].wait()
    emb[...] = jnp.zeros_like(emb)
    emb[:count, :] = emb_ref[...].astype(f32)
    emb_low = emb[...].astype(low)
    row = lax.broadcasted_iota(jnp.int32, hidden.shape, 0)
    hidden[...] = jnp.where(
        row < count, jnp.tanh(dot_nn(emb_low, first_ref[...]) + fbias_ref[...]), 0.0
    )
    value = hidden[...]
    prefix = pkv_ref[...]
    parts = both_parts(prefix)
    hidden_twice = jnp.concatenate([value, value], axis=0).T.astype(low)
    tile = 128
    for index in range(second_grad.shape[0] // tile):
        here = slice(index * tile, (index + 1) * tile)
        second_grad[here, :] = dot_nn(hidden_twice[here, :], parts)
        save(second_grad, second_out, here)
    sbias_out[...] = jnp.sum(prefix, axis=0, keepdims=True)
    loads[3].wait()
    grad = dot_nt(parts, second_ref[...])
    grad = (grad[:PREFIX_ROWS] + grad[PREFIX_ROWS:]) * (1.0 - value * value)
    fbias_out[...] = jnp.sum(grad, axis=0, keepdims=True)
    parts = both_parts(grad)
    emb_twice = jnp.concatenate([emb[...], emb[...]], axis=0).T.astype(low)
    first_grad[...] = dot_nn(emb_twice, parts)
    save(first_grad, first_out)
    back = dot_nt(parts, first_ref[...])
    embed_out[...] = (back[:PREFIX_ROWS] + back[PREFIX_ROWS:])[:count, :]
    rbias_out[...] = vecs_ref[0:1, :]
    dbias_out[...] = vecs_ref[1:2, :down]
    gain_out[...] = vecs_ref[2:5, :]
    shift_out[...] = vecs_ref[5:8, :]
    for copy in saves:
        copy.wait()


def finish(full, vecs, prefix_grad, embed, first, first_bias, second, down, token_grad, memory_grad):
    f32 = jnp.float32
    count, width = embed.shape
    hidden = first.shape[1]
    vmem = pl.BlockSpec(memory_space=pltpu.VMEM)
    anywhere = pl.BlockSpec(memory_space=pl.ANY)
    shapes = (
        (count, width),
        (width, hidden),
        (1, hidden),
        (hidden, 2 * width),
        (1, 2 * width),
        (width, down),
        (1, down),
        (down, width),
        (1, width),
        (3, width),
        (3, width),
    )
    return pl.pallas_call(
        finish_kernel,
        out_shape=tuple(jax.ShapeDtypeStruct(shape, f32) for shape in shapes)
        + tuple(
            jax.ShapeDtypeStruct(value.shape, value.dtype) for value in (token_grad, memory_grad)
        ),
        in_specs=[anywhere, vmem, vmem, vmem, anywhere, vmem, anywhere, anywhere, anywhere],
        out_specs=(
            vmem,
            anywhere,
            vmem,
            anywhere,
            vmem,
            anywhere,
            vmem,
            anywhere,
            vmem,
            vmem,
            vmem,
            anywhere,
            anywhere,
        ),
        scratch_shapes=[
            pltpu.VMEM(full.shape, jnp.bfloat16),
            pltpu.VMEM(first.shape, jnp.bfloat16),
            pltpu.VMEM(second.shape, jnp.bfloat16),
            pltpu.VMEM(token_grad.shape, token_grad.dtype),
            pltpu.VMEM(memory_grad.shape, memory_grad.dtype),
            pltpu.VMEM((width, hidden), f32),
            pltpu.VMEM((hidden, 2 * width), f32),
            pltpu.VMEM((width, down), f32),
            pltpu.VMEM((down, width), f32),
            pltpu.VMEM((PREFIX_ROWS, width), f32),
            pltpu.VMEM((PREFIX_ROWS, hidden), f32),
            pltpu.SemaphoreType.DMA((5 + hidden // 128,)),
            pltpu.SemaphoreType.DMA((6,)),
        ],
        compiler_params=pltpu.CompilerParams(vmem_limit_bytes=VMEM_BYTES),
        name="finish",
    )(full, vecs, prefix_grad, embed, first, first_bias, second, token_grad, memory_grad)


def gelu_pair(value):
    size = jnp.abs(value)
    step = 1.0 / (1.0 + (0.3275911 * 0.7071067811865476) * size)
    bell = jnp.exp(-0.5 * value * value)
    poly = step * (
        0.127414796
        + step
        * (-0.142248368 + step * (0.7107068705 + step * (-0.7265760135 + step * 0.5307027145)))
    )
    act = jnp.maximum(value, 0.0) - size * (poly * bell)
    turn = bell * (0.3989422804014327 * size - poly)
    return act, jnp.where(value >= 0.0, 1.0 + turn, -turn)


def normed(value):
    center = jnp.mean(value, axis=-1, keepdims=True)
    centered = value - center
    scale = lax.rsqrt(jnp.mean(centered * centered, axis=-1, keepdims=True) + norm_eps)
    return centered * scale, scale


def norm_back(grad, scale, unit):
    return scale * (
        grad
        - jnp.mean(grad, axis=-1, keepdims=True)
        - unit * jnp.mean(grad * unit, axis=-1, keepdims=True)
    )


def middle_kernel(
    tok_in,
    att_in,
    cot_in,
    mkey_in,
    mvalue_in,
    gain_ref,
    shift_ref,
    dbias_ref,
    rbias_ref,
    wo_in,
    wcq_in,
    wco_in,
    wd_in,
    wr_in,
    win_in,
    wout_in,
    layer_out,
    fgrad_out,
    ograd_out,
    mkey_out,
    mvalue_out,
    sums_out,
    vecs_ref,
    tok_ref,
    att_ref,
    cot_ref,
    mkey_ref,
    mvalue_ref,
    out_ref,
    fgrad_ref,
    ograd_ref,
    sums_ref,
    wo,
    wcq,
    wco,
    wd,
    wr,
    win,
    wout,
    unit_one,
    unit_two,
    work,
    total,
    scale_one,
    scale_two,
    low_one,
    low_two,
    low_three,
    query,
    crossed,
    weights,
    slopes,
    acts,
    down_act,
    down_slope,
    down_grad,
    load_sem,
    win_sem,
    wout_sem,
    out_sem,
):
    length, width = tok_ref.shape
    resident = len(win.shape) == 2
    tile = 512 if resident else win.shape[2]
    tiles = win_in.shape[1] // tile
    slots = tiles if resident else win.shape[0]
    rows_step = length // 2
    low = jnp.bfloat16
    f32 = jnp.float32

    sources = (
        att_in,
        wo_in,
        tok_in,
        wcq_in,
        mkey_in,
        mvalue_in,
        wco_in,
        wd_in,
        wr_in,
        cot_in,
    )
    targets = (att_ref, wo, tok_ref, wcq, mkey_ref, mvalue_ref, wco, wd, wr, cot_ref)
    loads = [
        pltpu.make_async_copy(source, target, load_sem.at[index])
        for index, (source, target) in enumerate(zip(sources, targets))
    ]

    def win_load(which):
        slot = which % slots
        target = win.at[:, rows_of(which, tile)] if resident else win.at[slot]
        return pltpu.make_async_copy(win_in.at[:, rows_of(which, tile)], target, win_sem.at[slot])

    def wout_load(which):
        slot = which % slots
        target = wout.at[rows_of(which, tile), :] if resident else wout.at[slot]
        return pltpu.make_async_copy(wout_in.at[rows_of(which, tile), :], target, wout_sem.at[slot])

    for load in loads[:7]:
        load.start()

    def by_columns(extent, step, body):
        def one(index, carry):
            body(pl.ds(pl.multiple_of(index * step, step), step))
            return carry

        lax.fori_loop(0, extent // step, one, 0)

    def by_rows(body, init=0):
        def one(index, carry):
            return body(rows_of(index, rows_step), carry)

        return lax.fori_loop(0, length // rows_step, one, init)

    cols = 512
    half = width // 2

    for load in loads[:3]:
        load.wait()
    for load in loads[7:]:
        load.start()
    for which in range(slots):
        win_load(which).start()
    for which in range(slots):
        wout_load(which).start()

    def project_out(here):
        work[:, here] = tok_ref[:, here].astype(f32) + dot_nn(att_ref[...], wo[:, here])

    by_columns(width, cols, project_out)

    def first_norm(here, carry):
        unit, scale = normed(work[here, :])
        unit_one[here, :] = unit
        scale_one[here, :] = scale
        value = unit * gain_ref[0:1, :] + shift_ref[0:1, :]
        work[here, :] = value
        low_one[here, :] = value.astype(low)
        return carry

    by_rows(first_norm)

    loads[3].wait()

    def project_query(here):
        query[:, here] = dot_nn(low_one[...], wcq[:, here]).astype(low)

    by_columns(width, cols, project_query)
    per_block = LANES // HD

    def stacked(value):
        return jnp.concatenate(
            [jnp.where(head_lanes(value.shape, head), value, 0.0) for head in range(per_block)],
            axis=0,
        ).astype(low)

    def unstacked(value):
        return jnp.concatenate(
            [
                value[head * HD : (head + 1) * HD, head * length : (head + 1) * length]
                for head in range(per_block)
            ],
            axis=0,
        )

    def block_queries(here):
        return stacked(query[:, here].astype(f32) * 0.125)

    def cross_forward(block):
        here = rows_of(block, LANES)
        scores = dot_nt(mkey_ref[:, here], block_queries(here))
        raised = jnp.exp(scores - jnp.max(scores, axis=0, keepdims=True))
        share = 1.0 / jnp.sum(raised, axis=0, keepdims=True)
        weight = (raised * share).astype(low)
        weights[block] = weight
        values = mvalue_ref[:, here].astype(f32).T.astype(low)
        crossed[:, here] = unstacked(dot_nn(values, weight)).T.astype(low)

    loads[4].wait()
    loads[5].wait()

    def cross_forward_both(step, carry):
        cross_forward(2 * step)
        cross_forward(2 * step + 1)
        return carry

    lax.fori_loop(0, width // LANES // 2, cross_forward_both, 0)

    loads[6].wait()

    def project_crossed(here):
        work[:, here] += dot_nn(crossed[...], wco[:, here])

    by_columns(width, cols, project_crossed)

    def second_norm(here, carry):
        unit, scale = normed(work[here, :])
        unit_two[here, :] = unit
        scale_two[here, :] = scale
        value = unit * gain_ref[1:2, :] + shift_ref[1:2, :]
        work[here, :] = value
        low_two[here, :] = value.astype(low)
        return carry

    by_rows(second_norm)

    step_cols = 512

    def feed_part(here, source):
        act, slope = gelu_pair(dot_nn(low_two[...], source))
        slopes[:, here] = slope.astype(low)
        return act.astype(low)

    if resident:

        def feed_forward(which, carry):
            here = rows_of(which, step_cols)

            @pl.when(which % (tile // step_cols) == 0)
            def _():
                win_load(which // (tile // step_cols)).wait()

            acts[:, here] = feed_part(here, win[:, here])
            return carry

        lax.fori_loop(0, tiles * tile // step_cols, feed_forward, 0)
        for which in range(tiles):
            wout_load(which).wait()

        def feed_out_part(here):
            total[:, here] = dot_nn(acts[...], wout[:, here])

        by_columns(width, step_cols, feed_out_part)
    else:
        total[...] = jnp.zeros_like(total)

        def feed_forward(which, carry):
            slot = lax.rem(which, slots)
            win_load(which).wait()
            wout_load(which).wait()
            total[...] += dot_nn(feed_part(rows_of(which, tile), win[slot]), wout[slot])

            @pl.when(which + slots < tiles)
            def _():
                win_load(which + slots).start()
                wout_load(which + slots).start()

            return carry

        lax.fori_loop(0, tiles, feed_forward, 0)

    loads[7].wait()
    loads[8].wait()
    loads[9].wait()
    act, slope = gelu_pair(dot_nn(low_two[...], wd[...]) + dbias_ref[...])
    down_act[...] = act.astype(low)
    down_slope[...] = slope.astype(low)

    def project_raise(here):
        work[:, here] += total[:, here] + 4.0 * (
            dot_nn(down_act[...], wr[:, here]) + rbias_ref[:, here]
        )

    by_columns(width, cols, project_raise)
    nothing = jnp.zeros((1, width), f32)

    def third_norm(here, carry):
        gain_sum, shift_sum, bias_sum = carry
        unit, scale = normed(work[here, :])
        gain = gain_ref[2:3, :]
        out_ref[here, :] = (unit * gain + shift_ref[2:3, :]).astype(low)
        grad = cot_ref[here, :].astype(f32)
        back = norm_back(grad * gain, scale, unit)
        total[here, :] = back
        back_low = back.astype(low)
        low_three[here, :] = back_low
        return (
            gain_sum + jnp.sum(grad * unit, axis=0, keepdims=True),
            shift_sum + jnp.sum(grad, axis=0, keepdims=True),
            bias_sum + jnp.sum(back_low.astype(f32), axis=0, keepdims=True),
        )

    gain_three, shift_three, bias_sum = by_rows(third_norm, (nothing, nothing, nothing))
    saves = []

    def save(source, target):
        copy = pltpu.make_async_copy(source, target, out_sem.at[len(saves)])
        copy.start()
        saves.append(copy)

    save(out_ref, layer_out)
    vecs_ref[0:1, :] = 4.0 * bias_sum

    back = 4.0 * dot_nt(low_three[...], wr[...]) * down_slope[...].astype(f32)
    back_low = back.astype(low)
    down_grad[...] = back_low
    vecs_ref[1:2, :] = jnp.concatenate(
        [
            jnp.sum(back_low.astype(f32), axis=0, keepdims=True),
            jnp.zeros((1, width - wd.shape[1]), f32),
        ],
        axis=1,
    )
    down = wd.shape[1]
    raise_sum = 4.0 * dot_tn(down_act[...], low_three[...])
    for index in range(width // LANES):
        sums_ref[pl.ds(down * width // LANES + index * down, down), :] = raise_sum[
            :, index * LANES : (index + 1) * LANES
        ].astype(low)
    down_sum = dot_tn(low_two[...], down_grad[...])
    for index in range(down // LANES):
        sums_ref[index * width : (index + 1) * width, :] = down_sum[
            :, index * LANES : (index + 1) * LANES
        ].astype(low)

    save(sums_ref, sums_out)

    if resident:

        def feed_slope(here):
            acts[:, here] = (
                dot_nt(low_three[...], wout[here, :]) * slopes[:, here].astype(f32)
            ).astype(low)

        by_columns(win_in.shape[1], step_cols, feed_slope)

        def feed_in_part(here):
            total[:, here] += dot_nt(acts[...], win[here, :])

        by_columns(width, step_cols, feed_in_part)
    else:

        def feed_backward(step, carry):
            which = tiles - 1 - step
            slot = lax.rem(which, slots)
            here = rows_of(which, tile)

            @pl.when(which < tiles - slots)
            def _():
                wout_load(which).wait()
                win_load(which).wait()

            grad = dot_nt(low_three[...], wout[slot]) * slopes[:, here].astype(f32)
            total[...] += dot_nt(grad.astype(low), win[slot])

            @pl.when(which >= slots)
            def _():
                win_load(which - slots).start()
                wout_load(which - slots).start()

            return carry

        lax.fori_loop(0, tiles, feed_backward, 0)

    def down_back(here):
        total[:, here] += dot_nt(down_grad[...], wd[here, :])

    by_columns(width, cols, down_back)

    def second_back(here, carry):
        gain_sum, shift_sum = carry
        grad = total[here, :]
        unit = unit_two[here, :]
        back = norm_back(grad * gain_ref[1:2, :], scale_two[here, :], unit)
        total[here, :] = back
        low_one[here, :] = back.astype(low)
        return (
            gain_sum + jnp.sum(grad * unit, axis=0, keepdims=True),
            shift_sum + jnp.sum(grad, axis=0, keepdims=True),
        )

    gain_two, shift_two = by_rows(second_back, (nothing, nothing))

    def crossed_back(here):
        crossed[:, here] = dot_nt(low_one[...], wco[here, :]).astype(low)

    by_columns(width, cols, crossed_back)

    def cross_backward(block):
        here = rows_of(block, LANES)
        grads = stacked(crossed[:, here].astype(f32))
        keys = mkey_ref[:, here].astype(f32).T.astype(low)
        slope = dot_nt(mvalue_ref[:, here], grads)
        weight_low = weights[block]
        weight = weight_low.astype(f32)
        slope = weight * (slope - jnp.sum(weight * slope, axis=0, keepdims=True))
        slope = slope.astype(low)
        queries = block_queries(here)
        mkey_ref[:, here] = dot_nn(slope, queries).astype(low)
        mvalue_ref[:, here] = dot_nn(weight_low, grads).astype(low)
        query[:, here] = (unstacked(dot_nn(keys, slope)) * 0.125).T.astype(low)

    def cross_backward_both(step, carry):
        cross_backward(2 * step)
        cross_backward(2 * step + 1)
        return carry

    lax.fori_loop(0, width // LANES // 2, cross_backward_both, 0)
    save(mkey_ref, mkey_out)
    save(mvalue_ref, mvalue_out)

    def query_back(here):
        total[:, here] += dot_nt(query[...], wcq[here, :])

    by_columns(width, cols, query_back)

    def first_back(here, carry):
        gain_sum, shift_sum = carry
        grad = total[here, :]
        unit = unit_one[here, :]
        back = norm_back(grad * gain_ref[0:1, :], scale_one[here, :], unit)
        fgrad_ref[here, :] = back
        low_one[here, :] = back.astype(low)
        return (
            gain_sum + jnp.sum(grad * unit, axis=0, keepdims=True),
            shift_sum + jnp.sum(grad, axis=0, keepdims=True),
        )

    gain_one, shift_one = by_rows(first_back, (nothing, nothing))
    save(fgrad_ref, fgrad_out)

    for index in range(width // cols):
        here = slice(index * cols, (index + 1) * cols)
        ograd_ref[here, :] = dot_nt(low_one[...], wo[here, :]).T.astype(low)
        save(ograd_ref.at[here], ograd_out.at[here])
    for index, vector in enumerate(
        (gain_one, gain_two, gain_three, shift_one, shift_two, shift_three)
    ):
        vecs_ref[2 + index : 3 + index, :] = vector
    for copy in saves:
        copy.wait()


def middle(
    tokens, attended, cotangent, mem_key, mem_value, gains, shifts, down_bias, raise_bias, weights
):
    length, width = tokens.shape
    mem_len = mem_key.shape[0]
    down = weights[3].shape[1]
    feed = weights[5].shape[1]
    tile = 512 if mem_len <= 512 else 128
    resident = mem_len <= 512
    slots = feed // tile if resident else 2
    low = jnp.bfloat16
    f32 = jnp.float32
    vmem = pl.BlockSpec(memory_space=pltpu.VMEM)
    anywhere = pl.BlockSpec(memory_space=pl.ANY)
    square = pltpu.VMEM((width, width), low)
    wide = pltpu.VMEM((length, width), f32)
    narrow = pltpu.VMEM((length, width), low)
    return pl.pallas_call(
        middle_kernel,
        out_shape=(
            jax.ShapeDtypeStruct((length, width), low),
            jax.ShapeDtypeStruct((length, width), f32),
            jax.ShapeDtypeStruct((width, length), low),
            jax.ShapeDtypeStruct((mem_len, width), low),
            jax.ShapeDtypeStruct((mem_len, width), low),
            jax.ShapeDtypeStruct((2 * down * width // LANES, LANES), low),
            jax.ShapeDtypeStruct((8, width), f32),
        ),
        in_specs=[anywhere] * 5 + [vmem] * 4 + [anywhere] * 7,
        out_specs=(anywhere,) * 6 + (vmem,),
        scratch_shapes=[
            narrow,
            narrow,
            narrow,
            pltpu.VMEM((mem_len, width), low),
            pltpu.VMEM((mem_len, width), low),
            narrow,
            wide,
            pltpu.VMEM((width, length), low),
            pltpu.VMEM((2 * down * width // LANES, LANES), low),
            square,
            square,
            square,
            pltpu.VMEM((width, down), low),
            pltpu.VMEM((down, width), low),
            pltpu.VMEM((width, feed) if resident else (slots, width, tile), low),
            pltpu.VMEM((feed, width) if resident else (slots, tile, width), low),
            wide,
            wide,
            wide,
            wide,
            pltpu.VMEM((length, 1), f32),
            pltpu.VMEM((length, 1), f32),
            narrow,
            narrow,
            narrow,
            narrow,
            narrow,
            pltpu.VMEM((width // LANES, mem_len, LANES // HD * length), low),
            pltpu.VMEM((length, feed), low),
            pltpu.VMEM((length, feed) if resident else (16, LANES), low),
            pltpu.VMEM((length, down), low),
            pltpu.VMEM((length, down), low),
            pltpu.VMEM((length, down), low),
            pltpu.SemaphoreType.DMA((10,)),
            pltpu.SemaphoreType.DMA((slots,)),
            pltpu.SemaphoreType.DMA((slots,)),
            pltpu.SemaphoreType.DMA((5 + width // 512,)),
        ],
        compiler_params=pltpu.CompilerParams(vmem_limit_bytes=VMEM_BYTES + 3 * 1024 * 1024),
        name="middle",
    )(tokens, attended, cotangent, mem_key, mem_value, gains, shifts, down_bias, raise_bias, *weights)


def per_device(
    tokens,
    memory,
    segment_ids,
    padding_mask,
    cotangent,
    prefix_embed,
    prefix_first,
    first_bias,
    prefix_second,
    second_bias,
    adapter_down,
    down_bias,
    adapter_raise,
    raise_bias,
    norm_gain,
    norm_shift,
    self_query,
    self_key,
    self_value,
    self_output,
    cross_query,
    cross_key,
    cross_value,
    cross_output,
    feed_in,
    feed_out,
):
    row_count, length, model_width = tokens.shape
    flat_rows = row_count * length
    n = lax.axis_size("seq")
    batches = lax.axis_size("batch")
    down = adapter_down.shape[1]
    attended, mem_key, mem_value, *saved = self_forward(
        n,
        segment_ids,
        padding_mask,
        tokens.reshape(flat_rows, model_width),
        (self_query, self_key, self_value),
        (
            prefix_embed,
            prefix_first,
            first_bias.reshape(1, -1),
            prefix_second,
            second_bias.reshape(1, -1),
        ),
        memory.reshape(-1, model_width),
        (cross_key, cross_value),
    )
    layer_output, first_grad, out_grad, *mem_grads, weight_sums, vector_sums = middle(
        tokens.reshape(flat_rows, model_width),
        attended,
        cotangent.reshape(flat_rows, model_width),
        mem_key,
        mem_value,
        norm_gain,
        norm_shift,
        down_bias.reshape(1, -1),
        raise_bias.reshape(1, -1),
        (
            self_output,
            cross_query,
            cross_output,
            adapter_down,
            adapter_raise,
            feed_in,
            feed_out,
        ),
    )
    layer_output = layer_output.reshape(row_count, length, model_width)
    token_grad, memory_grad, prefix_grad, vector_sums, full_sums = self_backward(
        n,
        batches,
        first_grad,
        out_grad.reshape(n, -1, HD, length),
        weight_sums,
        mem_grads,
        (cross_key, cross_value),
        vector_sums,
        saved,
        (self_query, self_key, self_value),
    )
    *replicated, token_grad, memory_grad = finish(
        full_sums.reshape(-1, LANES),
        vector_sums,
        prefix_grad,
        prefix_embed,
        prefix_first,
        first_bias.reshape(1, -1),
        prefix_second,
        down,
        token_grad,
        memory_grad,
    )
    token_grad = token_grad.reshape(row_count, length, model_width)
    memory_grad = memory_grad.reshape(memory.shape)
    replicated = [
        value.reshape(-1) if value.shape[0] == 1 else value for value in replicated
    ]
    return (layer_output, token_grad, memory_grad, *replicated)


def solution(mesh):
    placed = (
        P("batch", "seq", None),
        P("batch", "seq", None),
        P("batch", "seq"),
        P("batch", "seq"),
        P("batch", "seq", None),
        P(),
        P(),
        P(),
        P(),
        P(),
        P(),
        P(),
        P(),
        P(),
        P(),
        P(),
        P(),
        P(),
        P(),
        P(),
        P(),
        P(),
        P(),
        P(),
        P(),
        P(),
    )
    return jax.shard_map(
        per_device,
        mesh=mesh,
        in_specs=placed,
        out_specs=(
            P("batch", "seq", None),
            P("batch", "seq", None),
            P("batch", "seq", None),
            P(),
            P(),
            P(),
            P(),
            P(),
            P(),
            P(),
            P(),
            P(),
            P(),
            P(),
        ),
        check_vma=False,
    )
```

```python
import functools

import jax
import jax.numpy as jnp
from jax import lax
from jax.experimental import pallas as pl
from jax.experimental.pallas import tpu as pltpu
from jax.sharding import PartitionSpec as P

H = 16
HD = 64
LANES = 128
PREFIX_ROWS = 32
VMEM_BYTES = 60 * 1024 * 1024
SUM_ROWS = 16
MESH = pl.DeviceIdType.MESH

masked_score = -1e30
norm_eps = 1e-05

def dot_nn(left, right):
    return lax.dot_general(
        left, right, (((1,), (0,)), ((), ())), preferred_element_type=jnp.float32
    )


def dot_nt(left, right):
    return lax.dot_general(
        left, right, (((1,), (1,)), ((), ())), preferred_element_type=jnp.float32
    )


def dot_tn(left, right):
    return lax.dot_general(
        left, right, (((0,), (0,)), ((), ())), preferred_element_type=jnp.float32
    )


def remote(source, target, send_sem, recv_sem, axis, peer):
    return pltpu.make_async_remote_copy(
        src_ref=source,
        dst_ref=target,
        send_sem=send_sem,
        recv_sem=recv_sem,
        device_id={axis: peer},
        device_id_type=MESH,
    )


def enter(sizes):
    barrier = pltpu.get_barrier_semaphore()
    for axis, size in sizes.items():
        for other in range(size):

            @pl.when(other != lax.axis_index(axis))
            def _():
                pl.semaphore_signal(barrier, inc=1, device_id={axis: other}, device_id_type=MESH)

    pl.semaphore_wait(barrier, sum(sizes.values()) - len(sizes))


def others(size, mine, body):
    for other in range(size):

        @pl.when(other != mine)
        def _():
            body(other)


def rows_of(index, size):
    return pl.ds(pl.multiple_of(index * size, size), size)


def span_of(start, size):
    return pl.ds(pl.multiple_of(start, LANES), size)


def own_columns(ref, first, me, width):
    if width % LANES == 0:
        return ref[:, pl.ds(pl.multiple_of(first + me * width, LANES), width)].astype(jnp.float32)
    share = LANES // width
    block = ref[:, pl.ds(pl.multiple_of(first + me // share * LANES, LANES), LANES)].astype(
        jnp.float32
    )
    picked = block[:, :width]
    for part in range(1, share):
        picked = jnp.where(me % share == part, block[:, part * width : (part + 1) * width], picked)
    return picked


def head_lanes(shape, head):
    lane = lax.broadcasted_iota(jnp.int32, shape, 1)
    return (lane >= head * HD) & (lane < (head + 1) * HD)


def self_forward_kernel(
    n,
    seg_ref,
    pad_ref,
    tok_ref,
    wq_in,
    wk_in,
    wv_in,
    emb_ref,
    first_in,
    fbias_ref,
    second_in,
    sbias_ref,
    mem_ref,
    wck_in,
    wcv_in,
    att_ref,
    mkey_out,
    mvalue_out,
    qx_out,
    kx_out,
    raw_out,
    pk_out,
    pv_out,
    pkt_out,
    ot_out,
    lse_out,
    send,
    recv,
    meta_send,
    meta,
    kx,
    qx,
    vt,
    hidden,
    pk,
    pv,
    pkt,
    pvt,
    stat,
    acc,
    o_send,
    o_recv,
    mem_all,
    wck,
    wcv,
    mkey_ref,
    mvalue_ref,
    wq_ref,
    wk_ref,
    wv_ref,
    first_ref,
    second_ref,
    send_sem,
    recv_sem,
    meta_send_sem,
    meta_recv_sem,
    o_send_sem,
    o_recv_sem,
    mem_send_sem,
    mem_recv_sem,
    out_sem,
    weight_sem,
    in_sem,
):
    low = jnp.bfloat16
    f32 = jnp.float32
    me = lax.axis_index("seq")
    length, width = tok_ref.shape
    group = width // n
    heads = group // HD
    plane = 2 * length
    planes = n // 2
    block = 2 * LANES
    per_block = block // group
    blocks = width // block
    my_plane = me // 2
    my_side = lax.rem(me, 2)

    upward = my_plane >= planes // 2
    turn_sign = jnp.where(upward, 1, -1)

    def plane_after(step):
        return lax.rem(my_plane + planes + turn_sign * step, planes)

    def meta_copy(peer, slot):
        return remote(
            meta_send, meta.at[slot], meta_send_sem.at[peer], meta_recv_sem.at[slot], "seq", peer
        )

    def qkv_copy(head, peer, slot):
        return remote(
            send.at[peer, head],
            recv.at[head, slot],
            send_sem.at[head, peer],
            recv_sem.at[head, slot],
            "seq",
            peer,
        )

    def out_copy(head, peer, slot):
        return remote(
            o_send.at[head, peer],
            o_recv.at[slot, head],
            o_send_sem.at[head, peer],
            o_recv_sem.at[head, slot],
            "seq",
            peer,
        )

    def mem_along(which, toward):
        part = mem_all.at[which, my_side]
        return remote(
            part,
            part,
            mem_send_sem.at[(toward + 1) // 2, which],
            mem_recv_sem.at[which],
            "seq",
            me + 2 * toward,
        )

    def mem_across(side):
        part = mem_all.at[:, side]
        return remote(
            part,
            part,
            mem_send_sem.at[0, planes],
            mem_recv_sem.at[planes],
            "seq",
            me + 1 - 2 * my_side,
        )

    def mem_hops(hop, body):
        for toward in (1, -1):
            which = my_plane - toward * hop
            ahead = my_plane + toward

            @pl.when((which >= 0) & (which < planes) & (ahead >= 0) & (ahead < planes))
            def _():
                body(mem_along(which, toward))

    def mem_arrivals(hop):
        for toward in (1, -1):
            which = my_plane - toward * hop

            @pl.when((which >= 0) & (which < planes))
            def _():
                mem_along(which, -toward).wait_recv()

    def block_at(step):
        if blocks >= planes:
            share = blocks // planes
            return plane_after(1 + step // share) * share + step % share
        return lax.rem(me // per_block + 1 + step, blocks)

    def weight_load(step, which):
        columns = rows_of(block_at(step), block)
        source = (wq_in, wk_in, wv_in)[which]
        target = (wq_ref, wk_ref, wv_ref)[which]
        return pltpu.make_async_copy(
            source.at[:, columns], target.at[:, columns], weight_sem.at[step, which]
        )

    for step in range(blocks):
        for which in range(3):
            weight_load(step, which).start()
    loads = [
        pltpu.make_async_copy(source, target, in_sem.at[index])
        for index, (source, target) in enumerate(
            ((first_in, first_ref), (second_in, second_ref), (wck_in, wck), (wcv_in, wcv))
        )
    ]
    for load in loads:
        load.start()
    segments = seg_ref[...]
    tags = jnp.where(pad_ref[...] == 1, segments, -1)
    row = lax.broadcasted_iota(jnp.int32, meta_send.shape, 0)
    meta_send[...] = jnp.where(row == 0, segments, tags)
    mem_all[my_plane, my_side] = mem_ref[...]
    enter({"seq": n})
    others(n, me, lambda peer: meta_copy(peer, me).start())
    meta[me] = meta_send[...]

    for step in range(blocks):
        at = block_at(step)
        columns = rows_of(at, block)
        for which, weight in enumerate((wq_ref, wk_ref, wv_ref)):
            weight_load(step, which).wait()
            piece = dot_nn(tok_ref[...], weight[:, columns]).T.astype(low)
            for part in range(per_block):
                for head in range(heads):
                    first = part * group + head * HD
                    send[at * per_block + part, head, which] = piece[first : first + HD]
        for part in range(per_block):
            peer = at * per_block + part

            @pl.when(peer != me)
            def _():
                qkv_copy(0, peer, me).start()

            @pl.when(peer == me)
            def _():
                for head in range(heads):
                    recv[head, me] = send[peer, head]

    mem_hops(0, lambda copy: copy.start())
    loads[0].wait()
    loads[1].wait()
    hidden[...] = jnp.zeros_like(hidden)
    hidden[: emb_ref.shape[0], :] = jnp.tanh(dot_nn(emb_ref[...], first_ref[...]) + fbias_ref[...])
    hidden_low = hidden[...].astype(low)
    prefix_key = dot_nn(hidden_low, own_columns(second_ref, 0, me, group).astype(low)) + own_columns(
        sbias_ref, 0, me, group
    )
    prefix_value = dot_nn(
        hidden_low, own_columns(second_ref, width, me, group).astype(low)
    ) + own_columns(sbias_ref, width, me, group)
    prefix_row = lax.broadcasted_iota(jnp.int32, (PREFIX_ROWS, HD), 0)
    prefix_open = jnp.where(prefix_row < emb_ref.shape[0], 0.0, masked_score)
    for head in range(heads):
        here = slice(head * HD, (head + 1) * HD)
        pk[head] = jnp.concatenate([prefix_key[:, here], prefix_open], axis=1).astype(low)
        pv[head] = prefix_value[:, here].astype(low)
    pkt[...] = prefix_key.T.astype(low).reshape(heads, HD, PREFIX_ROWS)
    pvt[:, :HD, :] = prefix_value.T.astype(low).reshape(heads, HD, PREFIX_ROWS)
    pvt[:, HD:, :] = jnp.ones((heads, SUM_ROWS, PREFIX_ROWS), low)
    vt[:, HD:, :] = jnp.ones((heads, SUM_ROWS, n * length), low)

    def arrive(head, chunk):
        @pl.when(chunk != me)
        def _():
            @pl.when(head == 0)
            def _():
                meta_copy(chunk, chunk).wait_recv()

            qkv_copy(head, chunk, chunk).wait_recv()

        here = rows_of(chunk, length)
        state = lax.broadcasted_iota(jnp.int32, (HD, length), 0)
        qx[head, :HD, here] = (recv[head, chunk, 0].astype(f32) * 0.125).astype(low)
        qx[head, HD:, here] = jnp.where(state == meta[chunk, 0:1, :], 1.0, 0.0).astype(low)
        is_open = jnp.where(state == meta[chunk, 1:2, :], 0.0, masked_score)
        kx[head, here, :] = jnp.concatenate(
            [recv[head, chunk, 1].astype(f32), is_open], axis=0
        ).T.astype(low)
        vt[head, :HD, here] = recv[head, chunk, 2]

    def open_plane(head, which):
        scores = dot_nn(pk[head], qx[head, :, rows_of(which, plane)])
        top = jnp.max(scores, axis=0, keepdims=True)
        raised = jnp.exp(scores - top)
        stat[which, head, 0:1, :] = top
        acc[which, head] = dot_nn(pvt[head], raised.astype(low))

    def pair_part(head, upper, lower, first, count, keys, diagonal):
        here = slice(first, first + count)
        queries = qx[head, :, span_of(upper * plane + first, count)]
        key_rows = span_of(lower * plane, keys)
        scores = dot_nn(kx[head, key_rows, :], queries)
        if diagonal:
            key_at = lax.broadcasted_iota(jnp.int32, scores.shape, 0)
            query_at = lax.broadcasted_iota(jnp.int32, scores.shape, 1) + first
            scores = jnp.where(key_at <= query_at, scores, masked_score)
        old_top = stat[upper, head, 0:1, here]
        top = jnp.maximum(old_top, jnp.max(scores, axis=0, keepdims=True))
        raised = jnp.exp(scores - top).astype(low)
        stat[upper, head, 0:1, here] = top
        acc[upper, head, :, here] = acc[upper, head, :, here] * jnp.exp(old_top - top) + dot_nn(
            vt[head, :, key_rows], raised
        )

    def pair(head, upper, lower):
        pair_part(head, upper, lower, 0, plane, plane, False)

    def pair_diagonal(head, which):
        for part in range(2):
            pair_part(head, which, which, part * length, length, (part + 1) * length, True)

    def close_plane(head, which):
        total = acc[which, head, HD : HD + 1, :]
        value = acc[which, head, :HD, :] / total
        acc[which, head, :HD, :] = value
        stat[which, head, 0:1, :] = stat[which, head, 0:1, :] + jnp.log(total)
        for part in range(2):
            chunk = 2 * which + part
            o_send[head, chunk] = value[:, part * length : (part + 1) * length].astype(low)

            @pl.when((chunk != me) & (head == heads - 1))
            def _():
                out_copy(head, chunk, me).start()

            @pl.when(chunk == me)
            def _():
                o_recv[me, head] = o_send[head, chunk]

    def project_memory():
        mem_across(1 - my_side).wait_recv()
        for load in loads[2:]:
            load.wait()
        whole = mem_all[...].reshape(mkey_ref.shape)

        def one(index, carry):
            here = rows_of(index, block)
            mkey_ref[:, here] = dot_nn(whole, wck[:, here]).astype(low)
            mvalue_ref[:, here] = dot_nn(whole, wcv[:, here]).astype(low)
            return carry

        lax.fori_loop(0, blocks, one, 0)

    def stage(index, carry):
        head = index // planes
        step = lax.rem(index, planes)

        @pl.when(head + 1 < heads)
        def _():
            there = plane_after(1 + step)
            for part in range(2):
                peer = 2 * there + part

                @pl.when(peer != me)
                def _():
                    qkv_copy(head, peer, me).wait_send()
                    qkv_copy(head + 1, peer, me).start()

        @pl.when((head == heads - 1) & (head > 0))
        def _():
            there = plane_after(1 + step)
            for part in range(2):
                peer = 2 * there + part

                @pl.when(peer != me)
                def _():
                    qkv_copy(head, peer, me).wait_send()
                    out_copy(head - 1, peer, me).start()

        here = plane_after(step)
        arrive(head, 2 * here)
        arrive(head, 2 * here + 1)
        open_plane(head, here)
        pair_diagonal(head, here)

        def earlier(back, inner):
            there = plane_after(back)
            pair(head, jnp.maximum(here, there), jnp.minimum(here, there))

            @pl.when((step == planes - 1) & (there > here))
            def _():
                close_plane(head, there)

            return inner

        lax.fori_loop(0, step, earlier, 0)
        for hop in range(1, planes - 1):

            @pl.when(index == hop)
            def _():
                mem_arrivals(hop)
                mem_hops(hop, lambda copy: copy.start())

        @pl.when(index == planes - 1)
        def _():
            mem_arrivals(planes - 1)
            mem_across(my_side).start()

        @pl.when((upward & (my_plane + step >= planes)) | (step == planes - 1))
        def _():
            close_plane(head, here)

        @pl.when(jnp.logical_not(upward) & (step == my_plane))
        def _():
            def close(which, inner):
                close_plane(head, which)
                return inner

            lax.fori_loop(0, my_plane + 1, close, 0)

        return carry

    lax.fori_loop(0, heads * planes, stage, 0)

    saves = []

    def save(source, target):
        copy = pltpu.make_async_copy(source, target, out_sem.at[len(saves)])
        copy.start()
        saves.append(copy)

    save(qx, qx_out)
    save(kx, kx_out)
    save(recv, raw_out)
    save(pk, pk_out)
    save(pv, pv_out)
    save(pkt, pkt_out)
    save(acc, ot_out)
    save(stat, lse_out)
    project_memory()
    save(mkey_ref, mkey_out)
    save(mvalue_ref, mvalue_out)
    for other in range(n):

        @pl.when(other != me)
        def _():
            for head in range(heads):
                out_copy(head, other, other).wait_recv()

        att_ref[:, other * group : (other + 1) * group] = (
            o_recv[other].reshape(group, length).astype(f32).T.astype(low)
        )

    def drain(peer):
        meta_copy(peer, me).wait_send()
        if heads == 1:
            qkv_copy(0, peer, me).wait_send()
        for head in range(heads):
            out_copy(head, peer, me).wait_send()

    others(n, me, drain)
    for hop in range(planes - 1):
        mem_hops(hop, lambda copy: copy.wait_send())
    mem_across(my_side).wait_send()
    for copy in saves:
        copy.wait()


def self_forward(n, segments, padding, tokens, weights, prefix, memory, mem_weights):
    length, width = tokens.shape
    group = width // n
    heads = group // HD
    whole = n * length
    planes = n // 2
    low = jnp.bfloat16
    f32 = jnp.float32
    vmem = pl.BlockSpec(memory_space=pltpu.VMEM)
    anywhere = pl.BlockSpec(memory_space=pl.ANY)
    dma = pltpu.SemaphoreType.DMA
    shapes = (
        ((heads, 2 * HD, whole), low),
        ((heads, whole, 2 * HD), low),
        ((heads, n, 3, HD, length), low),
        ((heads, PREFIX_ROWS, 2 * HD), low),
        ((heads, PREFIX_ROWS, HD), low),
        ((heads, HD, PREFIX_ROWS), low),
        ((planes, heads, HD + SUM_ROWS, 2 * length), f32),
        ((planes, heads, 8, 2 * length), f32),
    )
    square = pltpu.VMEM((width, width), low)
    qx, kx, raw, pk, pv, pkt, acc, stat = (pltpu.VMEM(*shape) for shape in shapes)
    return pl.pallas_call(
        functools.partial(self_forward_kernel, n),
        out_shape=(
            jax.ShapeDtypeStruct((length, width), low),
            jax.ShapeDtypeStruct((n * memory.shape[0], width), low),
            jax.ShapeDtypeStruct((n * memory.shape[0], width), low),
        )
        + tuple(jax.ShapeDtypeStruct(*shape) for shape in shapes),
        in_specs=[vmem] * 3
        + [anywhere] * 3
        + [vmem, anywhere, vmem, anywhere, vmem, vmem]
        + [anywhere] * 2,
        out_specs=(vmem,) + (anywhere,) * 10,
        scratch_shapes=[
            pltpu.VMEM((n, heads, 3, HD, length), low),
            raw,
            pltpu.VMEM((8, length), jnp.int32),
            pltpu.VMEM((n, 8, length), jnp.int32),
            kx,
            qx,
            pltpu.VMEM((heads, HD + SUM_ROWS, whole), low),
            pltpu.VMEM((PREFIX_ROWS, weights[0].shape[0] // 2), f32),
            pk,
            pv,
            pkt,
            pltpu.VMEM((heads, HD + SUM_ROWS, PREFIX_ROWS), low),
            stat,
            acc,
            pltpu.VMEM((heads, n, HD, length), low),
            pltpu.VMEM((n, heads, HD, length), low),
            pltpu.VMEM((planes, 2) + memory.shape, low),
            square,
            square,
            pltpu.VMEM((n * memory.shape[0], width), low),
            pltpu.VMEM((n * memory.shape[0], width), low),
            square,
            square,
            square,
            pltpu.VMEM(prefix[1].shape, low),
            pltpu.VMEM(prefix[3].shape, low),
            dma((heads, n)),
            dma((heads, n)),
            dma((n,)),
            dma((n,)),
            dma((heads, n)),
            dma((heads, n)),
            dma((2, planes + 1)),
            dma((planes + 1,)),
            dma((10,)),
            dma((width // (2 * LANES), 3)),
            dma((4,)),
        ],
        compiler_params=pltpu.CompilerParams(
            collective_id=0, has_side_effects=True, vmem_limit_bytes=VMEM_BYTES
        ),
        name="self_forward",
    )(segments, padding, tokens, *weights, *prefix, memory, *mem_weights)


def self_backward_kernel(
    n,
    batches,
    base_in,
    do_in,
    sums_in,
    mkey_in,
    mvalue_in,
    wck_in,
    wcv_in,
    vecs_in,
    qx_in,
    kx_in,
    raw_in,
    pk_in,
    pv_in,
    pkt_in,
    ot_in,
    lse_in,
    wq_in,
    wk_in,
    wv_in,
    tg_ref,
    mgrad_ref,
    pkv_ref,
    vecs_ref,
    full_out,
    do_recv,
    qx,
    kx,
    raw,
    kt,
    values,
    dot,
    qdo,
    pk,
    pv,
    pkt,
    ot,
    stat,
    weights,
    dqt,
    dkv,
    g_send,
    g_recv,
    pre_ref,
    pre_all,
    pre_sum,
    pre_recv,
    sums_mine,
    sums_core,
    sums_x,
    sums_side,
    sums_z,
    full,
    mkey,
    mvalue,
    wck,
    wcv,
    mem_part,
    mem_side,
    mem_up,
    mem_down,
    vec_all,
    vec_sum,
    vec_y,
    vec_both,
    vec_z,
    product,
    base_ref,
    do_send_sem,
    do_recv_sem,
    g_send_sem,
    g_recv_sem,
    in_sem,
    send_sem,
    recv_sem,
):
    low = jnp.bfloat16
    f32 = jnp.float32
    me = lax.axis_index("seq")
    length, width = tg_ref.shape
    group = width // n
    heads = group // HD
    plane = 2 * length
    planes = n // 2
    step_rows = 256
    my_batch = lax.axis_index("batch")
    my_core = lax.rem(my_batch, 2)
    my_high = my_batch // 2
    highs = batches // 2
    my_plane = me // 2
    my_side = lax.rem(me, 2)
    beside = me + 1 - 2 * my_side
    used = [0]

    def numbers(count):
        used[0] += count
        return used[0] - count

    core_slot = numbers(2)
    x_slot = numbers(2 * highs)
    y_slot = numbers(3)
    z_slot = numbers(2 * planes)
    up_slot = numbers(planes)
    down_slot = numbers(planes)
    va_slot = numbers(batches)
    vb_slot = numbers(1)
    vc_slot = numbers(planes)
    pa_slot = numbers(batches)
    pb_slot = numbers(n)

    def send(source, target, first, peer_index, slot_index, axis, peer):
        return remote(
            source,
            target,
            send_sem.at[first + peer_index],
            recv_sem.at[first + slot_index],
            axis,
            peer,
        )

    half_rows = 2 * planes * highs * sums_z.shape[1]
    x_rows = half_rows // highs
    y_rows = x_rows // 2
    z_rows = y_rows // planes
    x_row = pl.multiple_of(my_high * x_rows, x_rows)
    y_row = pl.multiple_of(x_row + my_side * y_rows, y_rows)

    def part(row, count):
        return sums_mine.at[pl.ds(pl.multiple_of(row, count), count)]

    def reduce_core():
        return send(
            sums_in.at[1 - my_core], sums_core, core_slot, 0, 0, "batch", my_batch + 1 - 2 * my_core
        )

    def reduce_x(peer, slot):
        return send(
            part(peer * x_rows, x_rows),
            sums_x.at[slot],
            x_slot,
            peer,
            slot,
            "batch",
            2 * peer + my_core,
        )

    def reduce_y():
        return send(
            part(x_row + (1 - my_side) * y_rows, y_rows), sums_side, y_slot, 0, 0, "seq", beside
        )

    def reduce_z(peer, slot):
        return send(
            part(y_row + peer * z_rows, z_rows),
            sums_z.at[slot],
            z_slot,
            peer,
            slot,
            "seq",
            2 * peer + my_side,
        )

    def gather_z(peer, slot):
        piece = full.at[my_core, my_high, my_side, slot]
        return send(piece, piece, z_slot + planes, peer, slot, "seq", 2 * peer + my_side)

    def gather_y(side):
        piece = full.at[my_core, my_high, side]
        return send(piece, piece, y_slot + 1, 0, 0, "seq", beside)

    def gather_x(peer, slot):
        piece = full.at[my_core, slot]
        return send(piece, piece, x_slot + highs, peer, slot, "batch", 2 * peer + my_core)

    def gather_core(core):
        piece = full.at[core]
        return send(piece, piece, core_slot + 1, 0, 0, "batch", my_batch + 1 - 2 * my_core)

    def mem_across():
        return send(
            mem_part.at[:, 1 - my_side], mem_side, y_slot + 2, 0, 0, "seq", beside
        )

    def mem_hop(target, toward, peer=None):
        buffer, slot = (mem_up, up_slot) if toward > 0 else (mem_down, down_slot)
        return send(
            mem_part.at[target, my_side],
            buffer.at[target],
            slot,
            target,
            target,
            "seq",
            me + 2 * toward if peer is None else peer,
        )

    def mem_from(target, toward):
        return mem_hop(target, toward, me - 2 * toward)

    def mem_pass(toward):
        buffer = mem_up if toward > 0 else mem_down
        first = 0 if toward > 0 else planes - 1
        for target in range(planes):

            @pl.when((target - my_plane) * toward > 0)
            def _():
                @pl.when(my_plane != first)
                def _():
                    mem_from(target, toward).wait_recv()
                    mem_part[target, my_side] = (
                        mem_part[target, my_side].astype(f32) + buffer[target].astype(f32)
                    ).astype(low)

                mem_hop(target, toward).start()

    def mem_stage(at):
        pl.when(my_plane == at)(lambda: mem_pass(1))
        pl.when(my_plane == planes - 1 - at)(lambda: mem_pass(-1))

    def mem_end():
        value = mem_part[my_plane, my_side].astype(f32)
        mgrad_ref[...] = value.astype(low)

        @pl.when(my_plane > 0)
        def _():
            mem_from(my_plane, 1).wait_recv()
            mgrad_ref[...] = (mgrad_ref[...].astype(f32) + mem_up[my_plane].astype(f32)).astype(low)

        @pl.when(my_plane < planes - 1)
        def _():
            mem_from(my_plane, -1).wait_recv()
            mgrad_ref[...] = (
                mgrad_ref[...].astype(f32) + mem_down[my_plane].astype(f32)
            ).astype(low)

    def mem_drain():
        for target in range(planes):

            @pl.when(target > my_plane)
            def _():
                mem_hop(target, 1).wait_send()

            @pl.when(target < my_plane)
            def _():
                mem_hop(target, -1).wait_send()

    def vec_a(peer, slot):
        return send(vecs_in, vec_all.at[slot], va_slot, peer, slot, "batch", peer)

    def vec_b(side):
        return send(vec_sum, vec_y.at[side], vb_slot, 0, 0, "seq", beside)

    def vec_c(peer, slot):
        return send(vec_both, vec_z.at[slot], vc_slot, peer, slot, "seq", 2 * peer + my_side)

    def pre_a(peer, slot):
        return send(pre_ref, pre_all.at[slot], pa_slot, peer, slot, "batch", peer)

    def pre_b(peer, slot):
        return send(pre_sum, pre_recv.at[slot], pb_slot, peer, slot, "seq", peer)

    def do_copy(head, peer, slot):
        return remote(
            do_in.at[peer, head],
            do_recv.at[head, slot],
            do_send_sem.at[head, peer],
            do_recv_sem.at[head, slot],
            "seq",
            peer,
        )

    def q_copy(head, peer, slot):
        return remote(
            g_send.at[peer, head, 0],
            g_recv.at[0, slot, head],
            g_send_sem.at[0, head, peer],
            g_recv_sem.at[0, head, slot],
            "seq",
            peer,
        )

    def kv_copy(head, peer, slot):
        return remote(
            g_send.at[peer, head, pl.ds(1, 2)],
            g_recv.at[pl.ds(1, 2), slot, head],
            g_send_sem.at[1, head, peer],
            g_recv_sem.at[1, head, slot],
            "seq",
            peer,
        )

    def far_first(body):
        for index in range(n):
            peer = jnp.where(my_plane < planes // 2, n - 1 - index, index)

            @pl.when(peer != me)
            def _():
                body(peer)

    def added(ref, size):
        value = ref[0].astype(f32)
        for other in range(1, size):
            value = value + ref[other].astype(f32)
        return value

    loads = [
        pltpu.make_async_copy(source, target, in_sem.at[index])
        for index, (source, target) in enumerate(
            (
                (raw_in, raw),
                (mkey_in, mkey),
                (wck_in, wck),
                (mvalue_in, mvalue),
                (wcv_in, wcv),
                (sums_in.at[my_core], sums_mine),
                (vecs_in, vec_all.at[my_batch]),
                (pk_in, pk),
                (pv_in, pv),
                (pkt_in, pkt),
                (lse_in, stat),
                (ot_in, ot),
                (qx_in, qx),
                (kx_in, kx),
                (base_in, base_ref),
                (wq_in, weights.at[0]),
                (wk_in, weights.at[1]),
                (wv_in, weights.at[2]),
            )
        )
    ]
    own_do = pltpu.make_async_copy(do_in.at[me], do_recv.at[:, me], in_sem.at[len(loads)])
    own_do.start()
    for load in loads:
        load.start()
    enter({"seq": n, "batch": batches})
    far_first(lambda peer: do_copy(0, peer, me).start())
    reduce_core().start()
    others(batches, my_batch, lambda peer: vec_a(peer, my_batch).start())
    dkv[...] = jnp.zeros_like(dkv)
    product[...] = jnp.zeros_like(product)
    pre_ref[...] = jnp.zeros_like(pre_ref)
    loads[0].wait()

    def turn(index, carry):
        head = index // n
        chunk = lax.rem(index, n)
        here = rows_of(chunk, length)
        kt[head, :, here] = raw[head, chunk, 1]
        values[head, here, :] = raw[head, chunk, 2].astype(f32).T.astype(low)
        return carry

    lax.fori_loop(0, heads * n, turn, 0)
    for load in loads[1:5]:
        load.wait()

    def memory_back(index, carry):
        here = rows_of(index, step_rows)
        value = dot_nt(mkey[...], wck[here, :]) + dot_nt(mvalue[...], wcv[here, :])
        mem_part[:, :, :, here] = value.astype(low).reshape(mem_part.shape[:3] + (step_rows,))
        return carry

    lax.fori_loop(0, width // step_rows, memory_back, 0)
    mem_across().start()
    for load in loads[5:14]:
        load.wait()
    own_do.wait()

    def next_head(head):
        def move(peer):
            do_copy(head, peer, me).wait_send()
            do_copy(head + 1, peer, me).start()

        far_first(move)

    def arrive(head, which):
        for part in range(2):
            chunk = 2 * which + part

            @pl.when(chunk != me)
            def _():
                do_copy(head, chunk, chunk).wait_recv()

            grads = do_recv[head, chunk]
            dot[head, :, rows_of(chunk, length)] = grads
            grads = grads.astype(f32)
            query = raw[head, chunk, 0].astype(f32) * 0.125
            qdo[head, rows_of(chunk, length), :] = (
                jnp.concatenate([query, grads], axis=0).T.astype(low)
            )
            here = slice(part * length, (part + 1) * length)
            stat[which, head, 1:2, here] = jnp.sum(
                grads * ot[which, head, :HD, here], axis=0, keepdims=True
            )
        here = rows_of(which, plane)
        weight = jnp.exp(dot_nn(pk[head], qx[head, :, here]) - stat[which, head, 0:1, :])
        slope = weight * (dot_nn(pv[head], dot[head, :, here]) - stat[which, head, 1:2, :])
        both = jnp.concatenate([slope, weight], axis=0).astype(low)
        sums = dot_nn(both, qdo[head, here, :])
        pre_ref[head] += jnp.where(
            head_lanes((PREFIX_ROWS, 2 * HD), 0), sums[:PREFIX_ROWS], sums[PREFIX_ROWS:]
        )
        slope = slope.astype(low)
        dqt[which, head] = dot_nn(pkt[head], slope)

    def plus(first, second):
        return (first.astype(f32) + second.astype(f32)).astype(low)

    def sum_one():
        reduce_core().wait_recv()
        sums_mine[...] = plus(sums_mine[...], sums_core[...])
        others(highs, my_high, lambda peer: reduce_x(peer, my_high).start())

    def sum_two():
        here = pl.ds(x_row, x_rows)
        others(highs, my_high, lambda peer: reduce_x(peer, peer).wait_recv())
        sums_x[my_high] = sums_mine[here]
        sums_mine[here] = added(sums_x, highs).astype(low)
        reduce_y().start()

    def sum_three():
        here = pl.ds(y_row, y_rows)
        reduce_y().wait_recv()
        sums_mine[here] = plus(sums_mine[here], sums_side[...])
        others(planes, my_plane, lambda peer: reduce_z(peer, my_plane).start())

    def sum_four():
        here = pl.ds(pl.multiple_of(y_row + my_plane * z_rows, z_rows), z_rows)
        others(planes, my_plane, lambda peer: reduce_z(peer, peer).wait_recv())
        sums_z[my_plane] = sums_mine[here]
        full[my_core, my_high, my_side, my_plane] = added(sums_z, planes).astype(low)
        others(planes, my_plane, lambda peer: gather_z(peer, my_plane).start())

    def sum_five():
        others(planes, my_plane, lambda peer: gather_z(peer, peer).wait_recv())
        gather_y(my_side).start()

    def sum_six():
        gather_y(1 - my_side).wait_recv()
        others(highs, my_high, lambda peer: gather_x(peer, my_high).start())

    def sum_seven():
        others(highs, my_high, lambda peer: gather_x(peer, peer).wait_recv())
        gather_core(my_core).start()

    def sum_end():
        gather_core(1 - my_core).wait_recv()
        save_full.start()

    def vec_one():
        others(batches, my_batch, lambda peer: vec_a(peer, peer).wait_recv())
        vec_sum[...] = added(vec_all, batches)
        vec_b(my_side).start()
        vec_y[my_side] = vec_sum[...]

    def vec_two():
        vec_b(1 - my_side).wait_recv()
        value = (vec_y[0] + vec_y[1]).astype(f32)
        vec_both[...] = jnp.concatenate(
            [value[:, : width // 2], value[:, width // 2 :]], axis=0
        ).astype(low)
        others(planes, my_plane, lambda peer: vec_c(peer, my_plane).start())
        vec_z[my_plane] = vec_both[...]

    def vec_end():
        others(planes, my_plane, lambda peer: vec_c(peer, peer).wait_recv())
        value = added(vec_z, planes)
        vecs_ref[:, : width // 2] = value[:8]
        vecs_ref[:, width // 2 :] = value[8:]

    def mem_one():
        mem_across().wait_recv()
        mem_part[:, my_side] = plus(mem_part[:, my_side], mem_side[...])

    def stage_pa():
        others(batches, my_batch, lambda peer: pre_a(peer, my_batch).start())
        pre_all[my_batch] = pre_ref[...]

    def stage_pb():
        others(batches, my_batch, lambda peer: pre_a(peer, peer).wait_recv())
        pre_sum[...] = added(pre_all, batches).astype(low)
        others(n, me, lambda peer: pre_b(peer, me).start())
        pre_recv[me] = pre_sum[...]

    save_full = pltpu.make_async_copy(full, full_out, in_sem.at[0])

    def pair_part(head, upper, lower, first, count, diagonal):
        keys = span_of(lower * plane + first, count)
        here = span_of(upper * plane + first, plane - first)
        at = slice(first, plane)
        scores = dot_nn(kx[head, keys, :], qx[head, :, here])
        slope = dot_nn(values[head, keys, :], dot[head, :, here]) - stat[upper, head, 1:2, at]
        weight = jnp.exp(scores - stat[upper, head, 0:1, at])
        if diagonal:
            key_at = lax.broadcasted_iota(jnp.int32, scores.shape, 0)
            query_at = lax.broadcasted_iota(jnp.int32, scores.shape, 1)
            weight = jnp.where(key_at <= query_at, weight, 0.0)
        slope = (weight * slope).astype(low)
        key_part = dot_nn(slope, qdo[head, here, :])
        value_part = dot_nn(weight.astype(low), qdo[head, here, :])
        dkv[head, keys, :] += jnp.where(head_lanes((count, 2 * HD), 0), key_part, value_part)
        dqt[upper, head, :, at] += dot_nn(kt[head, :, keys], slope)

    def pair(head, upper, lower, diagonal):
        if diagonal:
            pair_part(head, upper, lower, 0, length, True)
            pair_part(head, upper, lower, length, length, True)
        else:
            pair_part(head, upper, lower, 0, plane, False)

    def hand_queries(head, which):
        for part in range(2):
            chunk = 2 * which + part
            g_send[chunk, head, 0] = (
                dqt[which, head, :, part * length : (part + 1) * length] * 0.125
            ).astype(low)

            @pl.when(chunk != me)
            def _():
                q_copy(head, chunk, me).start()

            @pl.when(chunk == me)
            def _():
                g_recv[0, me, head] = g_send[chunk, head, 0]

    def hand_keys(head, which):
        for part in range(2):
            chunk = 2 * which + part
            turned = dkv[head, rows_of(chunk, length), :].T.astype(low)
            g_send[chunk, head, 1] = turned[:HD]
            g_send[chunk, head, 2] = turned[HD:]

            @pl.when(chunk != me)
            def _():
                kv_copy(head, chunk, me).start()

            @pl.when(chunk == me)
            def _():
                g_recv[pl.ds(1, 2), me, head] = g_send[chunk, head, pl.ds(1, 2)]

    rising = my_plane >= planes // 2
    total = heads * planes * (planes + 1) // 2
    hooks = [
        (2, sum_one),
        (3, mem_one),
        (4, lambda: mem_stage(0)),
        (5, vec_one),
        (5, sum_two),
        (7, sum_three),
        (8, vec_two),
        (10, sum_four),
        (13, sum_five),
        (15, sum_six),
        (16, vec_end),
        (18, sum_seven),
    ] + [(4 + 4 * at, functools.partial(mem_stage, at)) for at in range(1, planes - 1)]
    hooks += [
        (1 + head * total // heads, functools.partial(next_head, head)) for head in range(heads - 1)
    ]
    final = total - planes * (planes + 1) // 2
    hooks += [(final + planes + 1, stage_pa), (final + 2 * planes - 1, stage_pb)]

    def hook(pairs):
        for number, body in sorted(hooks, key=lambda item: item[0]):
            pl.when(pairs == number)(body)


    def stage(index, carry):
        head = index // planes
        step = lax.rem(index, planes)
        here = jnp.where(rising, step, planes - 1 - step)

        @pl.when((step == 0) | ((step == 1) & jnp.logical_not(rising)))
        def _():
            @pl.when(rising | (step == 0))
            def _():
                arrive(head, here)

            @pl.when(jnp.logical_not(rising) & (step == 1))
            def _():
                def rest(which, inner):
                    arrive(head, planes - 2 - which)
                    return inner

                lax.fori_loop(0, planes - 1, rest, 0)

        begun = head * (planes * (planes + 1) // 2) + step * planes - step * (step - 1) // 2
        hook(begun)
        pair(head, here, here, True)

        @pl.when(rising)
        def _():
            hand_queries(head, here)

        @pl.when(jnp.logical_not(rising))
        def _():
            hand_keys(head, here)

        def far(at, inner):
            there = jnp.where(rising, here + 1 + at, here - 1 - at)

            @pl.when(rising & (step == 0))
            def _():
                arrive(head, there)

            hook(begun + 1 + at)
            pair(head, jnp.maximum(here, there), jnp.minimum(here, there), False)
            return inner

        lax.fori_loop(0, planes - 1 - step, far, 0)

        @pl.when(rising)
        def _():
            hand_keys(head, here)

        @pl.when(jnp.logical_not(rising))
        def _():
            hand_queries(head, here)

        return carry

    lax.fori_loop(0, heads * planes, stage, 0)
    for load in loads[14:]:
        load.wait()

    def gathered(peer):
        for head in range(heads):
            q_copy(head, peer, peer).wait_recv()
            kv_copy(head, peer, peer).wait_recv()

    half = width // 2

    def gather_plane(step, carry):
        which = lax.rem(my_plane + step, planes)
        for part in range(2):
            peer = 2 * which + part

            @pl.when(peer != me)
            def _():
                gathered(peer)

        columns = rows_of(which, 2 * group)
        for part in range(2):
            here = slice(part * half, (part + 1) * half)
            value = product[here, :]
            for kind in range(3):
                grads = g_recv[kind, pl.ds(2 * which, 2)].reshape(2 * group, length)
                value = value + dot_nn(weights[kind, here, columns], grads)
            product[here, :] = value
        return carry

    lax.fori_loop(0, planes - 1, gather_plane, 0)
    for other in range(n):

        @pl.when(other != me)
        def _():
            pre_b(other, other).wait_recv()

        value = pre_recv[other].astype(f32)
        for which in range(2):
            pkv_ref[:, which * width + other * group : which * width + (other + 1) * group] = (
                jnp.concatenate(
                    [value[head, :, which * HD : (which + 1) * HD] for head in range(heads)], axis=1
                )
            )

    mem_end()
    sum_end()
    gather_plane(planes - 1, 0)
    tile = 256
    for index in range(width // tile):
        here = slice(index * tile, (index + 1) * tile)
        tg_ref[:, here] = (base_ref[:, here] + product[here, :].T).astype(low)
    def drain(peer):
        do_copy(heads - 1, peer, me).wait_send()
        pre_b(peer, me).wait_send()
        for head in range(heads):
            q_copy(head, peer, me).wait_send()
            kv_copy(head, peer, me).wait_send()

    others(n, me, drain)
    others(batches, my_batch, lambda peer: pre_a(peer, my_batch).wait_send())
    others(batches, my_batch, lambda peer: vec_a(peer, my_batch).wait_send())
    reduce_core().wait_send()
    others(highs, my_high, lambda peer: reduce_x(peer, my_high).wait_send())
    reduce_y().wait_send()
    others(planes, my_plane, lambda peer: reduce_z(peer, my_plane).wait_send())
    others(planes, my_plane, lambda peer: gather_z(peer, my_plane).wait_send())
    gather_y(my_side).wait_send()
    others(highs, my_high, lambda peer: gather_x(peer, my_high).wait_send())
    gather_core(my_core).wait_send()
    mem_across().wait_send()
    mem_drain()
    others(planes, my_plane, lambda peer: vec_c(peer, my_plane).wait_send())
    vec_b(my_side).wait_send()
    save_full.wait()


def self_backward(
    n, batches, first_grad, out_grad, sums, mem_grads, mem_weights, vecs, saved, weights
):
    length, width = first_grad.shape
    group = width // n
    heads = group // HD
    whole = n * length
    planes = n // 2
    low = jnp.bfloat16
    f32 = jnp.float32
    vmem = pl.BlockSpec(memory_space=pltpu.VMEM)
    anywhere = pl.BlockSpec(memory_space=pl.ANY)
    dma = pltpu.SemaphoreType.DMA
    sum_rows = sums.shape[0] // (n * batches)
    mem_len = mem_grads[0].shape[0]
    mem_rows = mem_len // n
    mem_part = pltpu.VMEM((planes, mem_rows, width), low)
    mem_low = pltpu.VMEM((mem_len, width), low)
    square = pltpu.VMEM((width, width), low)
    vec = pltpu.VMEM((8, width), f32)
    copies = 6 + 2 * (batches // 2) + 5 * planes + 2 * batches + n
    qx, kx, raw, pk, pv, pkt, ot, stat = (pltpu.VMEM(value.shape, value.dtype) for value in saved)
    return pl.pallas_call(
        functools.partial(self_backward_kernel, n, batches),
        out_shape=(
            jax.ShapeDtypeStruct((length, width), low),
            jax.ShapeDtypeStruct((mem_rows, width), low),
            jax.ShapeDtypeStruct((PREFIX_ROWS, 2 * width), f32),
            jax.ShapeDtypeStruct((8, width), f32),
            jax.ShapeDtypeStruct((2, batches // 2, 2, planes, sum_rows, LANES), low),
        ),
        in_specs=[anywhere] * 19,
        out_specs=(vmem, vmem, vmem, vmem, anywhere),
        scratch_shapes=[
            pltpu.VMEM((heads, n, HD, length), low),
            qx,
            kx,
            raw,
            pltpu.VMEM((heads, HD, whole), low),
            pltpu.VMEM((heads, whole, HD), low),
            pltpu.VMEM((heads, HD, whole), low),
            pltpu.VMEM((heads, whole, 2 * HD), low),
            pk,
            pv,
            pkt,
            ot,
            stat,
            pltpu.VMEM((3, width, width), low),
            pltpu.VMEM((planes, heads, HD, 2 * length), f32),
            pltpu.VMEM((heads, whole, 2 * HD), f32),
            pltpu.VMEM((n, heads, 3, HD, length), low),
            pltpu.VMEM((3, n, heads, HD, length), low),
            pltpu.VMEM((heads, PREFIX_ROWS, 2 * HD), f32),
            pltpu.VMEM((batches, heads, PREFIX_ROWS, 2 * HD), f32),
            pltpu.VMEM((heads, PREFIX_ROWS, 2 * HD), low),
            pltpu.VMEM((n, heads, PREFIX_ROWS, 2 * HD), low),
            pltpu.VMEM((sums.shape[0] // 2, LANES), low),
            pltpu.VMEM((sums.shape[0] // 2, LANES), low),
            pltpu.VMEM((batches // 2, sums.shape[0] // batches, LANES), low),
            pltpu.VMEM((planes * sum_rows, LANES), low),
            pltpu.VMEM((planes, sum_rows, LANES), low),
            pltpu.VMEM((2, batches // 2, 2, planes, sum_rows, LANES), low),
            mem_low,
            mem_low,
            square,
            square,
            pltpu.VMEM((planes, 2, mem_rows, width), low),
            mem_part,
            mem_part,
            mem_part,
            pltpu.VMEM((batches, 8, width), f32),
            vec,
            pltpu.VMEM((2, 8, width), f32),
            pltpu.VMEM((16, width // 2), low),
            pltpu.VMEM((planes, 16, width // 2), low),
            pltpu.VMEM((width, length), f32),
            pltpu.VMEM((length, width), f32),
            dma((heads, n)),
            dma((heads, n)),
            dma((2, heads, n)),
            dma((2, heads, n)),
            dma((19,)),
            dma((copies,)),
            dma((copies,)),
        ],
        compiler_params=pltpu.CompilerParams(
            collective_id=1, has_side_effects=True, vmem_limit_bytes=VMEM_BYTES
        ),
        name="self_backward",
    )(
        first_grad,
        out_grad,
        sums.reshape(2, -1, LANES),
        *mem_grads,
        *mem_weights,
        vecs,
        *saved,
        *weights,
    )


def both_parts(value):
    high = value.astype(jnp.bfloat16).astype(jnp.float32)
    return jnp.concatenate([high, value - high], axis=0).astype(jnp.bfloat16)


def finish_kernel(
    full_in,
    vecs_ref,
    pkv_ref,
    emb_ref,
    first_in,
    fbias_ref,
    second_in,
    token_in,
    mem_in,
    embed_out,
    first_out,
    fbias_out,
    second_out,
    sbias_out,
    down_out,
    dbias_out,
    raise_out,
    rbias_out,
    gain_out,
    shift_out,
    token_out,
    mem_out,
    full_ref,
    first_ref,
    second_ref,
    token_ref,
    mem_ref,
    first_grad,
    second_grad,
    down_grad,
    raise_grad,
    emb,
    hidden,
    out_sem,
    in_sem,
):
    f32 = jnp.float32
    low = jnp.bfloat16
    width = emb_ref.shape[1]
    down = dbias_out.shape[1]
    count = emb_ref.shape[0]
    first = down * width // LANES
    loads = [
        pltpu.make_async_copy(source, target, in_sem.at[index])
        for index, (source, target) in enumerate(
            (
                (full_in.at[first:], full_ref.at[first:]),
                (full_in.at[:first], full_ref.at[:first]),
                (first_in, first_ref),
                (second_in, second_ref),
                (token_in, token_ref),
                (mem_in, mem_ref),
            )
        )
    ]
    for load in loads:
        load.start()
    saves = []

    def save(source, target, rows=None):
        if rows is not None:
            source, target = source.at[rows], target.at[rows]
        copy = pltpu.make_async_copy(source, target, out_sem.at[len(saves)])
        copy.start()
        saves.append(copy)

    loads[0].wait()
    for index in range(width // LANES):
        raise_grad[:, index * LANES : (index + 1) * LANES] = full_ref[
            first + index * down : first + (index + 1) * down, :
        ].astype(f32)
    save(raise_grad, raise_out)
    loads[1].wait()
    for index in range(down // LANES):
        down_grad[:, index * LANES : (index + 1) * LANES] = full_ref[
            index * width : (index + 1) * width, :
        ].astype(f32)
    save(down_grad, down_out)
    for load in loads[4:]:
        load.wait()
    save(token_ref, token_out)
    save(mem_ref, mem_out)
    loads[2].wait()
    emb[...] = jnp.zeros_like(emb)
    emb[:count, :] = emb_ref[...].astype(f32)
    emb_low = emb[...].astype(low)
    row = lax.broadcasted_iota(jnp.int32, hidden.shape, 0)
    hidden[...] = jnp.where(
        row < count, jnp.tanh(dot_nn(emb_low, first_ref[...]) + fbias_ref[...]), 0.0
    )
    value = hidden[...]
    prefix = pkv_ref[...]
    parts = both_parts(prefix)
    hidden_twice = jnp.concatenate([value, value], axis=0).T.astype(low)
    tile = 128
    for index in range(second_grad.shape[0] // tile):
        here = slice(index * tile, (index + 1) * tile)
        second_grad[here, :] = dot_nn(hidden_twice[here, :], parts)
        save(second_grad, second_out, here)
    sbias_out[...] = jnp.sum(prefix, axis=0, keepdims=True)
    loads[3].wait()
    grad = dot_nt(parts, second_ref[...])
    grad = (grad[:PREFIX_ROWS] + grad[PREFIX_ROWS:]) * (1.0 - value * value)
    fbias_out[...] = jnp.sum(grad, axis=0, keepdims=True)
    parts = both_parts(grad)
    emb_twice = jnp.concatenate([emb[...], emb[...]], axis=0).T.astype(low)
    first_grad[...] = dot_nn(emb_twice, parts)
    save(first_grad, first_out)
    back = dot_nt(parts, first_ref[...])
    embed_out[...] = (back[:PREFIX_ROWS] + back[PREFIX_ROWS:])[:count, :]
    rbias_out[...] = vecs_ref[0:1, :]
    dbias_out[...] = vecs_ref[1:2, :down]
    gain_out[...] = vecs_ref[2:5, :]
    shift_out[...] = vecs_ref[5:8, :]
    for copy in saves:
        copy.wait()


def finish(full, vecs, prefix_grad, embed, first, first_bias, second, down, token_grad, memory_grad):
    f32 = jnp.float32
    count, width = embed.shape
    hidden = first.shape[1]
    vmem = pl.BlockSpec(memory_space=pltpu.VMEM)
    anywhere = pl.BlockSpec(memory_space=pl.ANY)
    shapes = (
        (count, width),
        (width, hidden),
        (1, hidden),
        (hidden, 2 * width),
        (1, 2 * width),
        (width, down),
        (1, down),
        (down, width),
        (1, width),
        (3, width),
        (3, width),
    )
    return pl.pallas_call(
        finish_kernel,
        out_shape=tuple(jax.ShapeDtypeStruct(shape, f32) for shape in shapes)
        + tuple(
            jax.ShapeDtypeStruct(value.shape, value.dtype) for value in (token_grad, memory_grad)
        ),
        in_specs=[anywhere, vmem, vmem, vmem, anywhere, vmem, anywhere, anywhere, anywhere],
        out_specs=(
            vmem,
            anywhere,
            vmem,
            anywhere,
            vmem,
            anywhere,
            vmem,
            anywhere,
            vmem,
            vmem,
            vmem,
            anywhere,
            anywhere,
        ),
        scratch_shapes=[
            pltpu.VMEM(full.shape, jnp.bfloat16),
            pltpu.VMEM(first.shape, jnp.bfloat16),
            pltpu.VMEM(second.shape, jnp.bfloat16),
            pltpu.VMEM(token_grad.shape, token_grad.dtype),
            pltpu.VMEM(memory_grad.shape, memory_grad.dtype),
            pltpu.VMEM((width, hidden), f32),
            pltpu.VMEM((hidden, 2 * width), f32),
            pltpu.VMEM((width, down), f32),
            pltpu.VMEM((down, width), f32),
            pltpu.VMEM((PREFIX_ROWS, width), f32),
            pltpu.VMEM((PREFIX_ROWS, hidden), f32),
            pltpu.SemaphoreType.DMA((5 + hidden // 128,)),
            pltpu.SemaphoreType.DMA((6,)),
        ],
        compiler_params=pltpu.CompilerParams(vmem_limit_bytes=VMEM_BYTES),
        name="finish",
    )(full, vecs, prefix_grad, embed, first, first_bias, second, token_grad, memory_grad)


def gelu_pair(value):
    size = jnp.abs(value)
    step = 1.0 / (1.0 + (0.3275911 * 0.7071067811865476) * size)
    bell = jnp.exp(-0.5 * value * value)
    poly = step * (
        0.127414796
        + step
        * (-0.142248368 + step * (0.7107068705 + step * (-0.7265760135 + step * 0.5307027145)))
    )
    act = jnp.maximum(value, 0.0) - size * (poly * bell)
    turn = bell * (0.3989422804014327 * size - poly)
    return act, jnp.where(value >= 0.0, 1.0 + turn, -turn)


def normed(value):
    center = jnp.mean(value, axis=-1, keepdims=True)
    centered = value - center
    scale = lax.rsqrt(jnp.mean(centered * centered, axis=-1, keepdims=True) + norm_eps)
    return centered * scale, scale


def norm_back(grad, scale, unit):
    return scale * (
        grad
        - jnp.mean(grad, axis=-1, keepdims=True)
        - unit * jnp.mean(grad * unit, axis=-1, keepdims=True)
    )


def middle_kernel(
    tok_in,
    att_in,
    cot_in,
    mkey_in,
    mvalue_in,
    gain_ref,
    shift_ref,
    dbias_ref,
    rbias_ref,
    wo_in,
    wcq_in,
    wco_in,
    wd_in,
    wr_in,
    win_in,
    wout_in,
    layer_out,
    fgrad_out,
    ograd_out,
    mkey_out,
    mvalue_out,
    sums_out,
    vecs_ref,
    tok_ref,
    att_ref,
    cot_ref,
    mkey_ref,
    mvalue_ref,
    out_ref,
    fgrad_ref,
    ograd_ref,
    sums_ref,
    wo,
    wcq,
    wco,
    wd,
    wr,
    win,
    wout,
    unit_one,
    unit_two,
    work,
    total,
    scale_one,
    scale_two,
    low_one,
    low_two,
    low_three,
    query,
    crossed,
    weights,
    slopes,
    acts,
    down_act,
    down_slope,
    down_grad,
    load_sem,
    win_sem,
    wout_sem,
    out_sem,
):
    length, width = tok_ref.shape
    resident = len(win.shape) == 2
    tile = 512 if resident else win.shape[2]
    tiles = win_in.shape[1] // tile
    slots = tiles if resident else win.shape[0]
    rows_step = length // 2
    low = jnp.bfloat16
    f32 = jnp.float32

    sources = (
        att_in,
        wo_in,
        tok_in,
        wcq_in,
        mkey_in,
        mvalue_in,
        wco_in,
        wd_in,
        wr_in,
        cot_in,
    )
    targets = (att_ref, wo, tok_ref, wcq, mkey_ref, mvalue_ref, wco, wd, wr, cot_ref)
    loads = [
        pltpu.make_async_copy(source, target, load_sem.at[index])
        for index, (source, target) in enumerate(zip(sources, targets))
    ]

    def win_load(which):
        slot = which % slots
        target = win.at[:, rows_of(which, tile)] if resident else win.at[slot]
        return pltpu.make_async_copy(win_in.at[:, rows_of(which, tile)], target, win_sem.at[slot])

    def wout_load(which):
        slot = which % slots
        target = wout.at[rows_of(which, tile), :] if resident else wout.at[slot]
        return pltpu.make_async_copy(wout_in.at[rows_of(which, tile), :], target, wout_sem.at[slot])

    for load in loads[:7]:
        load.start()

    def by_columns(extent, step, body):
        def one(index, carry):
            body(pl.ds(pl.multiple_of(index * step, step), step))
            return carry

        lax.fori_loop(0, extent // step, one, 0)

    def by_rows(body, init=0):
        def one(index, carry):
            return body(rows_of(index, rows_step), carry)

        return lax.fori_loop(0, length // rows_step, one, init)

    cols = 512
    half = width // 2

    for load in loads[:3]:
        load.wait()
    for load in loads[7:]:
        load.start()
    for which in range(slots):
        win_load(which).start()
    for which in range(slots):
        wout_load(which).start()

    def project_out(here):
        work[:, here] = tok_ref[:, here].astype(f32) + dot_nn(att_ref[...], wo[:, here])

    by_columns(width, cols, project_out)

    def first_norm(here, carry):
        unit, scale = normed(work[here, :])
        unit_one[here, :] = unit
        scale_one[here, :] = scale
        value = unit * gain_ref[0:1, :] + shift_ref[0:1, :]
        work[here, :] = value
        low_one[here, :] = value.astype(low)
        return carry

    by_rows(first_norm)

    loads[3].wait()

    def project_query(here):
        query[:, here] = dot_nn(low_one[...], wcq[:, here]).astype(low)

    by_columns(width, cols, project_query)
    per_block = LANES // HD

    def stacked(value):
        return jnp.concatenate(
            [jnp.where(head_lanes(value.shape, head), value, 0.0) for head in range(per_block)],
            axis=0,
        ).astype(low)

    def unstacked(value):
        return jnp.concatenate(
            [
                value[head * HD : (head + 1) * HD, head * length : (head + 1) * length]
                for head in range(per_block)
            ],
            axis=0,
        )

    def block_queries(here):
        return stacked(query[:, here].astype(f32) * 0.125)

    def cross_forward(block):
        here = rows_of(block, LANES)
        scores = dot_nt(mkey_ref[:, here], block_queries(here))
        raised = jnp.exp(scores - jnp.max(scores, axis=0, keepdims=True))
        share = 1.0 / jnp.sum(raised, axis=0, keepdims=True)
        weight = (raised * share).astype(low)
        weights[block] = weight
        values = mvalue_ref[:, here].astype(f32).T.astype(low)
        crossed[:, here] = unstacked(dot_nn(values, weight)).T.astype(low)

    loads[4].wait()
    loads[5].wait()

    def cross_forward_both(step, carry):
        cross_forward(2 * step)
        cross_forward(2 * step + 1)
        return carry

    lax.fori_loop(0, width // LANES // 2, cross_forward_both, 0)

    loads[6].wait()

    def project_crossed(here):
        work[:, here] += dot_nn(crossed[...], wco[:, here])

    by_columns(width, cols, project_crossed)

    def second_norm(here, carry):
        unit, scale = normed(work[here, :])
        unit_two[here, :] = unit
        scale_two[here, :] = scale
        value = unit * gain_ref[1:2, :] + shift_ref[1:2, :]
        work[here, :] = value
        low_two[here, :] = value.astype(low)
        return carry

    by_rows(second_norm)

    step_cols = 512

    def feed_part(here, source):
        act, slope = gelu_pair(dot_nn(low_two[...], source))
        slopes[:, here] = slope.astype(low)
        return act.astype(low)

    if resident:

        def feed_forward(which, carry):
            here = rows_of(which, step_cols)

            @pl.when(which % (tile // step_cols) == 0)
            def _():
                win_load(which // (tile // step_cols)).wait()

            acts[:, here] = feed_part(here, win[:, here])
            return carry

        lax.fori_loop(0, tiles * tile // step_cols, feed_forward, 0)
        for which in range(tiles):
            wout_load(which).wait()

        def feed_out_part(here):
            total[:, here] = dot_nn(acts[...], wout[:, here])

        by_columns(width, step_cols, feed_out_part)
    else:
        total[...] = jnp.zeros_like(total)

        def feed_forward(which, carry):
            slot = lax.rem(which, slots)
            win_load(which).wait()
            wout_load(which).wait()
            total[...] += dot_nn(feed_part(rows_of(which, tile), win[slot]), wout[slot])

            @pl.when(which + slots < tiles)
            def _():
                win_load(which + slots).start()
                wout_load(which + slots).start()

            return carry

        lax.fori_loop(0, tiles, feed_forward, 0)

    loads[7].wait()
    loads[8].wait()
    loads[9].wait()
    act, slope = gelu_pair(dot_nn(low_two[...], wd[...]) + dbias_ref[...])
    down_act[...] = act.astype(low)
    down_slope[...] = slope.astype(low)

    def project_raise(here):
        work[:, here] += total[:, here] + 4.0 * (
            dot_nn(down_act[...], wr[:, here]) + rbias_ref[:, here]
        )

    by_columns(width, cols, project_raise)
    nothing = jnp.zeros((1, width), f32)

    def third_norm(here, carry):
        gain_sum, shift_sum, bias_sum = carry
        unit, scale = normed(work[here, :])
        gain = gain_ref[2:3, :]
        out_ref[here, :] = (unit * gain + shift_ref[2:3, :]).astype(low)
        grad = cot_ref[here, :].astype(f32)
        back = norm_back(grad * gain, scale, unit)
        total[here, :] = back
        back_low = back.astype(low)
        low_three[here, :] = back_low
        return (
            gain_sum + jnp.sum(grad * unit, axis=0, keepdims=True),
            shift_sum + jnp.sum(grad, axis=0, keepdims=True),
            bias_sum + jnp.sum(back_low.astype(f32), axis=0, keepdims=True),
        )

    gain_three, shift_three, bias_sum = by_rows(third_norm, (nothing, nothing, nothing))
    saves = []

    def save(source, target):
        copy = pltpu.make_async_copy(source, target, out_sem.at[len(saves)])
        copy.start()
        saves.append(copy)

    save(out_ref, layer_out)
    vecs_ref[0:1, :] = 4.0 * bias_sum

    back = 4.0 * dot_nt(low_three[...], wr[...]) * down_slope[...].astype(f32)
    back_low = back.astype(low)
    down_grad[...] = back_low
    vecs_ref[1:2, :] = jnp.concatenate(
        [
            jnp.sum(back_low.astype(f32), axis=0, keepdims=True),
            jnp.zeros((1, width - wd.shape[1]), f32),
        ],
        axis=1,
    )
    down = wd.shape[1]
    raise_sum = 4.0 * dot_tn(down_act[...], low_three[...])
    for index in range(width // LANES):
        sums_ref[pl.ds(down * width // LANES + index * down, down), :] = raise_sum[
            :, index * LANES : (index + 1) * LANES
        ].astype(low)
    down_sum = dot_tn(low_two[...], down_grad[...])
    for index in range(down // LANES):
        sums_ref[index * width : (index + 1) * width, :] = down_sum[
            :, index * LANES : (index + 1) * LANES
        ].astype(low)

    save(sums_ref, sums_out)

    if resident:

        def feed_slope(here):
            acts[:, here] = (
                dot_nt(low_three[...], wout[here, :]) * slopes[:, here].astype(f32)
            ).astype(low)

        by_columns(win_in.shape[1], step_cols, feed_slope)

        def feed_in_part(here):
            total[:, here] += dot_nt(acts[...], win[here, :])

        by_columns(width, step_cols, feed_in_part)
    else:

        def feed_backward(step, carry):
            which = tiles - 1 - step
            slot = lax.rem(which, slots)
            here = rows_of(which, tile)

            @pl.when(which < tiles - slots)
            def _():
                wout_load(which).wait()
                win_load(which).wait()

            grad = dot_nt(low_three[...], wout[slot]) * slopes[:, here].astype(f32)
            total[...] += dot_nt(grad.astype(low), win[slot])

            @pl.when(which >= slots)
            def _():
                win_load(which - slots).start()
                wout_load(which - slots).start()

            return carry

        lax.fori_loop(0, tiles, feed_backward, 0)

    def down_back(here):
        total[:, here] += dot_nt(down_grad[...], wd[here, :])

    by_columns(width, cols, down_back)

    def second_back(here, carry):
        gain_sum, shift_sum = carry
        grad = total[here, :]
        unit = unit_two[here, :]
        back = norm_back(grad * gain_ref[1:2, :], scale_two[here, :], unit)
        total[here, :] = back
        low_one[here, :] = back.astype(low)
        return (
            gain_sum + jnp.sum(grad * unit, axis=0, keepdims=True),
            shift_sum + jnp.sum(grad, axis=0, keepdims=True),
        )

    gain_two, shift_two = by_rows(second_back, (nothing, nothing))

    def crossed_back(here):
        crossed[:, here] = dot_nt(low_one[...], wco[here, :]).astype(low)

    by_columns(width, cols, crossed_back)

    def cross_backward(block):
        here = rows_of(block, LANES)
        grads = stacked(crossed[:, here].astype(f32))
        keys = mkey_ref[:, here].astype(f32).T.astype(low)
        slope = dot_nt(mvalue_ref[:, here], grads)
        weight_low = weights[block]
        weight = weight_low.astype(f32)
        slope = weight * (slope - jnp.sum(weight * slope, axis=0, keepdims=True))
        slope = slope.astype(low)
        queries = block_queries(here)
        mkey_ref[:, here] = dot_nn(slope, queries).astype(low)
        mvalue_ref[:, here] = dot_nn(weight_low, grads).astype(low)
        query[:, here] = (unstacked(dot_nn(keys, slope)) * 0.125).T.astype(low)

    def cross_backward_both(step, carry):
        cross_backward(2 * step)
        cross_backward(2 * step + 1)
        return carry

    lax.fori_loop(0, width // LANES // 2, cross_backward_both, 0)
    save(mkey_ref, mkey_out)
    save(mvalue_ref, mvalue_out)

    def query_back(here):
        total[:, here] += dot_nt(query[...], wcq[here, :])

    by_columns(width, cols, query_back)

    def first_back(here, carry):
        gain_sum, shift_sum = carry
        grad = total[here, :]
        unit = unit_one[here, :]
        back = norm_back(grad * gain_ref[0:1, :], scale_one[here, :], unit)
        fgrad_ref[here, :] = back
        low_one[here, :] = back.astype(low)
        return (
            gain_sum + jnp.sum(grad * unit, axis=0, keepdims=True),
            shift_sum + jnp.sum(grad, axis=0, keepdims=True),
        )

    gain_one, shift_one = by_rows(first_back, (nothing, nothing))
    save(fgrad_ref, fgrad_out)

    for index in range(width // cols):
        here = slice(index * cols, (index + 1) * cols)
        ograd_ref[here, :] = dot_nt(low_one[...], wo[here, :]).T.astype(low)
        save(ograd_ref.at[here], ograd_out.at[here])
    for index, vector in enumerate(
        (gain_one, gain_two, gain_three, shift_one, shift_two, shift_three)
    ):
        vecs_ref[2 + index : 3 + index, :] = vector
    for copy in saves:
        copy.wait()


def middle(
    tokens, attended, cotangent, mem_key, mem_value, gains, shifts, down_bias, raise_bias, weights
):
    length, width = tokens.shape
    mem_len = mem_key.shape[0]
    down = weights[3].shape[1]
    feed = weights[5].shape[1]
    tile = 512 if mem_len <= 512 else 128
    resident = mem_len <= 512
    slots = feed // tile if resident else 2
    low = jnp.bfloat16
    f32 = jnp.float32
    vmem = pl.BlockSpec(memory_space=pltpu.VMEM)
    anywhere = pl.BlockSpec(memory_space=pl.ANY)
    square = pltpu.VMEM((width, width), low)
    wide = pltpu.VMEM((length, width), f32)
    narrow = pltpu.VMEM((length, width), low)
    return pl.pallas_call(
        middle_kernel,
        out_shape=(
            jax.ShapeDtypeStruct((length, width), low),
            jax.ShapeDtypeStruct((length, width), f32),
            jax.ShapeDtypeStruct((width, length), low),
            jax.ShapeDtypeStruct((mem_len, width), low),
            jax.ShapeDtypeStruct((mem_len, width), low),
            jax.ShapeDtypeStruct((2 * down * width // LANES, LANES), low),
            jax.ShapeDtypeStruct((8, width), f32),
        ),
        in_specs=[anywhere] * 5 + [vmem] * 4 + [anywhere] * 7,
        out_specs=(anywhere,) * 6 + (vmem,),
        scratch_shapes=[
            narrow,
            narrow,
            narrow,
            pltpu.VMEM((mem_len, width), low),
            pltpu.VMEM((mem_len, width), low),
            narrow,
            wide,
            pltpu.VMEM((width, length), low),
            pltpu.VMEM((2 * down * width // LANES, LANES), low),
            square,
            square,
            square,
            pltpu.VMEM((width, down), low),
            pltpu.VMEM((down, width), low),
            pltpu.VMEM((width, feed) if resident else (slots, width, tile), low),
            pltpu.VMEM((feed, width) if resident else (slots, tile, width), low),
            wide,
            wide,
            wide,
            wide,
            pltpu.VMEM((length, 1), f32),
            pltpu.VMEM((length, 1), f32),
            narrow,
            narrow,
            narrow,
            narrow,
            narrow,
            pltpu.VMEM((width // LANES, mem_len, LANES // HD * length), low),
            pltpu.VMEM((length, feed), low),
            pltpu.VMEM((length, feed) if resident else (16, LANES), low),
            pltpu.VMEM((length, down), low),
            pltpu.VMEM((length, down), low),
            pltpu.VMEM((length, down), low),
            pltpu.SemaphoreType.DMA((10,)),
            pltpu.SemaphoreType.DMA((slots,)),
            pltpu.SemaphoreType.DMA((slots,)),
            pltpu.SemaphoreType.DMA((5 + width // 512,)),
        ],
        compiler_params=pltpu.CompilerParams(vmem_limit_bytes=VMEM_BYTES + 3 * 1024 * 1024),
        name="middle",
    )(tokens, attended, cotangent, mem_key, mem_value, gains, shifts, down_bias, raise_bias, *weights)


def per_device(
    tokens,
    memory,
    segment_ids,
    padding_mask,
    cotangent,
    prefix_embed,
    prefix_first,
    first_bias,
    prefix_second,
    second_bias,
    adapter_down,
    down_bias,
    adapter_raise,
    raise_bias,
    norm_gain,
    norm_shift,
    self_query,
    self_key,
    self_value,
    self_output,
    cross_query,
    cross_key,
    cross_value,
    cross_output,
    feed_in,
    feed_out,
):
    row_count, length, model_width = tokens.shape
    flat_rows = row_count * length
    n = lax.axis_size("seq")
    batches = lax.axis_size("batch")
    down = adapter_down.shape[1]
    attended, mem_key, mem_value, *saved = self_forward(
        n,
        segment_ids,
        padding_mask,
        tokens.reshape(flat_rows, model_width),
        (self_query, self_key, self_value),
        (
            prefix_embed,
            prefix_first,
            first_bias.reshape(1, -1),
            prefix_second,
            second_bias.reshape(1, -1),
        ),
        memory.reshape(-1, model_width),
        (cross_key, cross_value),
    )
    layer_output, first_grad, out_grad, *mem_grads, weight_sums, vector_sums = middle(
        tokens.reshape(flat_rows, model_width),
        attended,
        cotangent.reshape(flat_rows, model_width),
        mem_key,
        mem_value,
        norm_gain,
        norm_shift,
        down_bias.reshape(1, -1),
        raise_bias.reshape(1, -1),
        (
            self_output,
            cross_query,
            cross_output,
            adapter_down,
            adapter_raise,
            feed_in,
            feed_out,
        ),
    )
    layer_output = layer_output.reshape(row_count, length, model_width)
    token_grad, memory_grad, prefix_grad, vector_sums, full_sums = self_backward(
        n,
        batches,
        first_grad,
        out_grad.reshape(n, -1, HD, length),
        weight_sums,
        mem_grads,
        (cross_key, cross_value),
        vector_sums,
        saved,
        (self_query, self_key, self_value),
    )
    *replicated, token_grad, memory_grad = finish(
        full_sums.reshape(-1, LANES),
        vector_sums,
        prefix_grad,
        prefix_embed,
        prefix_first,
        first_bias.reshape(1, -1),
        prefix_second,
        down,
        token_grad,
        memory_grad,
    )
    token_grad = token_grad.reshape(row_count, length, model_width)
    memory_grad = memory_grad.reshape(memory.shape)
    replicated = [
        value.reshape(-1) if value.shape[0] == 1 else value for value in replicated
    ]
    return (layer_output, token_grad, memory_grad, *replicated)


def solution(mesh):
    placed = (
        P("batch", "seq", None),
        P("batch", "seq", None),
        P("batch", "seq"),
        P("batch", "seq"),
        P("batch", "seq", None),
        P(),
        P(),
        P(),
        P(),
        P(),
        P(),
        P(),
        P(),
        P(),
        P(),
        P(),
        P(),
        P(),
        P(),
        P(),
        P(),
        P(),
        P(),
        P(),
        P(),
        P(),
    )
    return jax.shard_map(
        per_device,
        mesh=mesh,
        in_specs=placed,
        out_specs=(
            P("batch", "seq", None),
            P("batch", "seq", None),
            P("batch", "seq", None),
            P(),
            P(),
            P(),
            P(),
            P(),
            P(),
            P(),
            P(),
            P(),
            P(),
            P(),
        ),
        check_vma=False,
    )
```

```python
import functools

import jax
import jax.numpy as jnp
from jax import lax
from jax.experimental import pallas as pl
from jax.experimental.pallas import tpu as pltpu
from jax.sharding import PartitionSpec as P

H = 16
HD = 64
LANES = 128
PREFIX_ROWS = 32
VMEM_BYTES = 60 * 1024 * 1024
SUM_ROWS = 16
MESH = pl.DeviceIdType.MESH

masked_score = -1e30
norm_eps = 1e-05

def dot_nn(left, right):
    return lax.dot_general(
        left, right, (((1,), (0,)), ((), ())), preferred_element_type=jnp.float32
    )


def dot_nt(left, right):
    return lax.dot_general(
        left, right, (((1,), (1,)), ((), ())), preferred_element_type=jnp.float32
    )


def dot_tn(left, right):
    return lax.dot_general(
        left, right, (((0,), (0,)), ((), ())), preferred_element_type=jnp.float32
    )


def remote(source, target, send_sem, recv_sem, axis, peer):
    return pltpu.make_async_remote_copy(
        src_ref=source,
        dst_ref=target,
        send_sem=send_sem,
        recv_sem=recv_sem,
        device_id={axis: peer},
        device_id_type=MESH,
    )


def enter(sizes):
    barrier = pltpu.get_barrier_semaphore()
    for axis, size in sizes.items():
        for other in range(size):

            @pl.when(other != lax.axis_index(axis))
            def _():
                pl.semaphore_signal(barrier, inc=1, device_id={axis: other}, device_id_type=MESH)

    pl.semaphore_wait(barrier, sum(sizes.values()) - len(sizes))


def others(size, mine, body):
    for other in range(size):

        @pl.when(other != mine)
        def _():
            body(other)


def rows_of(index, size):
    return pl.ds(pl.multiple_of(index * size, size), size)


def span_of(start, size):
    return pl.ds(pl.multiple_of(start, LANES), size)


def own_columns(ref, first, me, width):
    if width % LANES == 0:
        return ref[:, pl.ds(pl.multiple_of(first + me * width, LANES), width)].astype(jnp.float32)
    share = LANES // width
    block = ref[:, pl.ds(pl.multiple_of(first + me // share * LANES, LANES), LANES)].astype(
        jnp.float32
    )
    picked = block[:, :width]
    for part in range(1, share):
        picked = jnp.where(me % share == part, block[:, part * width : (part + 1) * width], picked)
    return picked


def head_lanes(shape, head):
    lane = lax.broadcasted_iota(jnp.int32, shape, 1)
    return (lane >= head * HD) & (lane < (head + 1) * HD)


def self_forward_kernel(
    n,
    seg_ref,
    pad_ref,
    tok_ref,
    wq_in,
    wk_in,
    wv_in,
    emb_ref,
    first_in,
    fbias_ref,
    second_in,
    sbias_ref,
    mem_ref,
    wck_in,
    wcv_in,
    att_ref,
    mkey_out,
    mvalue_out,
    qx_out,
    kx_out,
    raw_out,
    pk_out,
    pv_out,
    pkt_out,
    ot_out,
    lse_out,
    send,
    recv,
    meta_send,
    meta,
    kx,
    qx,
    vt,
    hidden,
    pk,
    pv,
    pkt,
    pvt,
    stat,
    acc,
    o_send,
    o_recv,
    mem_all,
    wck,
    wcv,
    mkey_ref,
    mvalue_ref,
    wq_ref,
    wk_ref,
    wv_ref,
    first_ref,
    second_ref,
    send_sem,
    recv_sem,
    meta_send_sem,
    meta_recv_sem,
    o_send_sem,
    o_recv_sem,
    mem_send_sem,
    mem_recv_sem,
    out_sem,
    weight_sem,
    in_sem,
):
    low = jnp.bfloat16
    f32 = jnp.float32
    me = lax.axis_index("seq")
    length, width = tok_ref.shape
    group = width // n
    heads = group // HD
    plane = 2 * length
    planes = n // 2
    block = 2 * LANES
    per_block = block // group
    blocks = width // block
    my_plane = me // 2
    my_side = lax.rem(me, 2)

    upward = my_plane >= planes // 2
    turn_sign = jnp.where(upward, 1, -1)

    def plane_after(step):
        return lax.rem(my_plane + planes + turn_sign * step, planes)

    def meta_copy(peer, slot):
        return remote(
            meta_send, meta.at[slot], meta_send_sem.at[peer], meta_recv_sem.at[slot], "seq", peer
        )

    def qkv_copy(head, peer, slot):
        return remote(
            send.at[peer, head],
            recv.at[head, slot],
            send_sem.at[head, peer],
            recv_sem.at[head, slot],
            "seq",
            peer,
        )

    def out_copy(head, peer, slot):
        return remote(
            o_send.at[head, peer],
            o_recv.at[slot, head],
            o_send_sem.at[head, peer],
            o_recv_sem.at[head, slot],
            "seq",
            peer,
        )

    def mem_along(which, toward):
        part = mem_all.at[which, my_side]
        return remote(
            part,
            part,
            mem_send_sem.at[(toward + 1) // 2, which],
            mem_recv_sem.at[which],
            "seq",
            me + 2 * toward,
        )

    def mem_across(side):
        part = mem_all.at[:, side]
        return remote(
            part,
            part,
            mem_send_sem.at[0, planes],
            mem_recv_sem.at[planes],
            "seq",
            me + 1 - 2 * my_side,
        )

    def mem_hops(hop, body):
        for toward in (1, -1):
            which = my_plane - toward * hop
            ahead = my_plane + toward

            @pl.when((which >= 0) & (which < planes) & (ahead >= 0) & (ahead < planes))
            def _():
                body(mem_along(which, toward))

    def mem_arrivals(hop):
        for toward in (1, -1):
            which = my_plane - toward * hop

            @pl.when((which >= 0) & (which < planes))
            def _():
                mem_along(which, -toward).wait_recv()

    def block_at(step):
        if blocks >= planes:
            share = blocks // planes
            return plane_after(1 + step // share) * share + step % share
        return lax.rem(me // per_block + 1 + step, blocks)

    def weight_load(step, which):
        columns = rows_of(block_at(step), block)
        source = (wq_in, wk_in, wv_in)[which]
        target = (wq_ref, wk_ref, wv_ref)[which]
        return pltpu.make_async_copy(
            source.at[:, columns], target.at[:, columns], weight_sem.at[step, which]
        )

    for step in range(blocks):
        for which in range(3):
            weight_load(step, which).start()
    loads = [
        pltpu.make_async_copy(source, target, in_sem.at[index])
        for index, (source, target) in enumerate(
            ((first_in, first_ref), (second_in, second_ref), (wck_in, wck), (wcv_in, wcv))
        )
    ]
    for load in loads:
        load.start()
    segments = seg_ref[...]
    tags = jnp.where(pad_ref[...] == 1, segments, -1)
    row = lax.broadcasted_iota(jnp.int32, meta_send.shape, 0)
    meta_send[...] = jnp.where(row == 0, segments, tags)
    mem_all[my_plane, my_side] = mem_ref[...]
    enter({"seq": n})
    others(n, me, lambda peer: meta_copy(peer, me).start())
    meta[me] = meta_send[...]

    for step in range(blocks):
        at = block_at(step)
        columns = rows_of(at, block)
        for which, weight in enumerate((wq_ref, wk_ref, wv_ref)):
            weight_load(step, which).wait()
            piece = dot_nn(tok_ref[...], weight[:, columns]).T.astype(low)
            for part in range(per_block):
                for head in range(heads):
                    first = part * group + head * HD
                    send[at * per_block + part, head, which] = piece[first : first + HD]
        for part in range(per_block):
            peer = at * per_block + part

            @pl.when(peer != me)
            def _():
                qkv_copy(0, peer, me).start()

            @pl.when(peer == me)
            def _():
                for head in range(heads):
                    recv[head, me] = send[peer, head]

    mem_hops(0, lambda copy: copy.start())
    loads[0].wait()
    loads[1].wait()
    hidden[...] = jnp.zeros_like(hidden)
    hidden[: emb_ref.shape[0], :] = jnp.tanh(dot_nn(emb_ref[...], first_ref[...]) + fbias_ref[...])
    hidden_low = hidden[...].astype(low)
    prefix_key = dot_nn(hidden_low, own_columns(second_ref, 0, me, group).astype(low)) + own_columns(
        sbias_ref, 0, me, group
    )
    prefix_value = dot_nn(
        hidden_low, own_columns(second_ref, width, me, group).astype(low)
    ) + own_columns(sbias_ref, width, me, group)
    prefix_row = lax.broadcasted_iota(jnp.int32, (PREFIX_ROWS, HD), 0)
    prefix_open = jnp.where(prefix_row < emb_ref.shape[0], 0.0, masked_score)
    for head in range(heads):
        here = slice(head * HD, (head + 1) * HD)
        pk[head] = jnp.concatenate([prefix_key[:, here], prefix_open], axis=1).astype(low)
        pv[head] = prefix_value[:, here].astype(low)
    pkt[...] = prefix_key.T.astype(low).reshape(heads, HD, PREFIX_ROWS)
    pvt[:, :HD, :] = prefix_value.T.astype(low).reshape(heads, HD, PREFIX_ROWS)
    pvt[:, HD:, :] = jnp.ones((heads, SUM_ROWS, PREFIX_ROWS), low)
    vt[:, HD:, :] = jnp.ones((heads, SUM_ROWS, n * length), low)

    def arrive(head, chunk):
        @pl.when(chunk != me)
        def _():
            @pl.when(head == 0)
            def _():
                meta_copy(chunk, chunk).wait_recv()

            qkv_copy(head, chunk, chunk).wait_recv()

        here = rows_of(chunk, length)
        state = lax.broadcasted_iota(jnp.int32, (HD, length), 0)
        qx[head, :HD, here] = (recv[head, chunk, 0].astype(f32) * 0.125).astype(low)
        qx[head, HD:, here] = jnp.where(state == meta[chunk, 0:1, :], 1.0, 0.0).astype(low)
        is_open = jnp.where(state == meta[chunk, 1:2, :], 0.0, masked_score)
        kx[head, here, :] = jnp.concatenate(
            [recv[head, chunk, 1].astype(f32), is_open], axis=0
        ).T.astype(low)
        vt[head, :HD, here] = recv[head, chunk, 2]

    def open_plane(head, which):
        scores = dot_nn(pk[head], qx[head, :, rows_of(which, plane)])
        top = jnp.max(scores, axis=0, keepdims=True)
        raised = jnp.exp(scores - top)
        stat[which, head, 0:1, :] = top
        acc[which, head] = dot_nn(pvt[head], raised.astype(low))

    def pair_part(head, upper, lower, first, count, keys, diagonal):
        here = slice(first, first + count)
        queries = qx[head, :, span_of(upper * plane + first, count)]
        key_rows = span_of(lower * plane, keys)
        scores = dot_nn(kx[head, key_rows, :], queries)
        if diagonal:
            key_at = lax.broadcasted_iota(jnp.int32, scores.shape, 0)
            query_at = lax.broadcasted_iota(jnp.int32, scores.shape, 1) + first
            scores = jnp.where(key_at <= query_at, scores, masked_score)
        old_top = stat[upper, head, 0:1, here]
        top = jnp.maximum(old_top, jnp.max(scores, axis=0, keepdims=True))
        raised = jnp.exp(scores - top).astype(low)
        stat[upper, head, 0:1, here] = top
        acc[upper, head, :, here] = acc[upper, head, :, here] * jnp.exp(old_top - top) + dot_nn(
            vt[head, :, key_rows], raised
        )

    def pair(head, upper, lower):
        pair_part(head, upper, lower, 0, plane, plane, False)

    def pair_diagonal(head, which):
        for part in range(2):
            pair_part(head, which, which, part * length, length, (part + 1) * length, True)

    def close_plane(head, which):
        total = acc[which, head, HD : HD + 1, :]
        value = acc[which, head, :HD, :] / total
        acc[which, head, :HD, :] = value
        stat[which, head, 0:1, :] = stat[which, head, 0:1, :] + jnp.log(total)
        for part in range(2):
            chunk = 2 * which + part
            o_send[head, chunk] = value[:, part * length : (part + 1) * length].astype(low)

            @pl.when((chunk != me) & (head == heads - 1))
            def _():
                out_copy(head, chunk, me).start()

            @pl.when(chunk == me)
            def _():
                o_recv[me, head] = o_send[head, chunk]

    def project_memory():
        mem_across(1 - my_side).wait_recv()
        for load in loads[2:]:
            load.wait()
        whole = mem_all[...].reshape(mkey_ref.shape)

        def one(index, carry):
            here = rows_of(index, block)
            mkey_ref[:, here] = dot_nn(whole, wck[:, here]).astype(low)
            mvalue_ref[:, here] = dot_nn(whole, wcv[:, here]).astype(low)
            return carry

        lax.fori_loop(0, blocks, one, 0)

    def stage(index, carry):
        head = index // planes
        step = lax.rem(index, planes)

        @pl.when(head + 1 < heads)
        def _():
            there = plane_after(1 + step)
            for part in range(2):
                peer = 2 * there + part

                @pl.when(peer != me)
                def _():
                    qkv_copy(head, peer, me).wait_send()
                    qkv_copy(head + 1, peer, me).start()

        @pl.when((head == heads - 1) & (head > 0))
        def _():
            there = plane_after(1 + step)
            for part in range(2):
                peer = 2 * there + part

                @pl.when(peer != me)
                def _():
                    qkv_copy(head, peer, me).wait_send()
                    out_copy(head - 1, peer, me).start()

        here = plane_after(step)
        arrive(head, 2 * here)
        arrive(head, 2 * here + 1)
        open_plane(head, here)
        pair_diagonal(head, here)

        def earlier(back, inner):
            there = plane_after(back)
            pair(head, jnp.maximum(here, there), jnp.minimum(here, there))

            @pl.when((step == planes - 1) & (there > here))
            def _():
                close_plane(head, there)

            return inner

        lax.fori_loop(0, step, earlier, 0)
        for hop in range(1, planes - 1):

            @pl.when(index == hop)
            def _():
                mem_arrivals(hop)
                mem_hops(hop, lambda copy: copy.start())

        @pl.when(index == planes - 1)
        def _():
            mem_arrivals(planes - 1)
            mem_across(my_side).start()

        @pl.when((upward & (my_plane + step >= planes)) | (step == planes - 1))
        def _():
            close_plane(head, here)

        @pl.when(jnp.logical_not(upward) & (step == my_plane))
        def _():
            def close(which, inner):
                close_plane(head, which)
                return inner

            lax.fori_loop(0, my_plane + 1, close, 0)

        return carry

    lax.fori_loop(0, heads * planes, stage, 0)

    saves = []

    def save(source, target):
        copy = pltpu.make_async_copy(source, target, out_sem.at[len(saves)])
        copy.start()
        saves.append(copy)

    save(qx, qx_out)
    save(kx, kx_out)
    save(recv, raw_out)
    save(pk, pk_out)
    save(pv, pv_out)
    save(pkt, pkt_out)
    save(acc, ot_out)
    save(stat, lse_out)
    project_memory()
    save(mkey_ref, mkey_out)
    save(mvalue_ref, mvalue_out)
    for other in range(n):

        @pl.when(other != me)
        def _():
            for head in range(heads):
                out_copy(head, other, other).wait_recv()

        att_ref[:, other * group : (other + 1) * group] = (
            o_recv[other].reshape(group, length).astype(f32).T.astype(low)
        )

    def drain(peer):
        meta_copy(peer, me).wait_send()
        if heads == 1:
            qkv_copy(0, peer, me).wait_send()
        for head in range(heads):
            out_copy(head, peer, me).wait_send()

    others(n, me, drain)
    for hop in range(planes - 1):
        mem_hops(hop, lambda copy: copy.wait_send())
    mem_across(my_side).wait_send()
    for copy in saves:
        copy.wait()


def self_forward(n, segments, padding, tokens, weights, prefix, memory, mem_weights):
    length, width = tokens.shape
    group = width // n
    heads = group // HD
    whole = n * length
    planes = n // 2
    low = jnp.bfloat16
    f32 = jnp.float32
    vmem = pl.BlockSpec(memory_space=pltpu.VMEM)
    anywhere = pl.BlockSpec(memory_space=pl.ANY)
    dma = pltpu.SemaphoreType.DMA
    shapes = (
        ((heads, 2 * HD, whole), low),
        ((heads, whole, 2 * HD), low),
        ((heads, n, 3, HD, length), low),
        ((heads, PREFIX_ROWS, 2 * HD), low),
        ((heads, PREFIX_ROWS, HD), low),
        ((heads, HD, PREFIX_ROWS), low),
        ((planes, heads, HD + SUM_ROWS, 2 * length), f32),
        ((planes, heads, 8, 2 * length), f32),
    )
    square = pltpu.VMEM((width, width), low)
    qx, kx, raw, pk, pv, pkt, acc, stat = (pltpu.VMEM(*shape) for shape in shapes)
    return pl.pallas_call(
        functools.partial(self_forward_kernel, n),
        out_shape=(
            jax.ShapeDtypeStruct((length, width), low),
            jax.ShapeDtypeStruct((n * memory.shape[0], width), low),
            jax.ShapeDtypeStruct((n * memory.shape[0], width), low),
        )
        + tuple(jax.ShapeDtypeStruct(*shape) for shape in shapes),
        in_specs=[vmem] * 3
        + [anywhere] * 3
        + [vmem, anywhere, vmem, anywhere, vmem, vmem]
        + [anywhere] * 2,
        out_specs=(vmem,) + (anywhere,) * 10,
        scratch_shapes=[
            pltpu.VMEM((n, heads, 3, HD, length), low),
            raw,
            pltpu.VMEM((8, length), jnp.int32),
            pltpu.VMEM((n, 8, length), jnp.int32),
            kx,
            qx,
            pltpu.VMEM((heads, HD + SUM_ROWS, whole), low),
            pltpu.VMEM((PREFIX_ROWS, weights[0].shape[0] // 2), f32),
            pk,
            pv,
            pkt,
            pltpu.VMEM((heads, HD + SUM_ROWS, PREFIX_ROWS), low),
            stat,
            acc,
            pltpu.VMEM((heads, n, HD, length), low),
            pltpu.VMEM((n, heads, HD, length), low),
            pltpu.VMEM((planes, 2) + memory.shape, low),
            square,
            square,
            pltpu.VMEM((n * memory.shape[0], width), low),
            pltpu.VMEM((n * memory.shape[0], width), low),
            square,
            square,
            square,
            pltpu.VMEM(prefix[1].shape, low),
            pltpu.VMEM(prefix[3].shape, low),
            dma((heads, n)),
            dma((heads, n)),
            dma((n,)),
            dma((n,)),
            dma((heads, n)),
            dma((heads, n)),
            dma((2, planes + 1)),
            dma((planes + 1,)),
            dma((10,)),
            dma((width // (2 * LANES), 3)),
            dma((4,)),
        ],
        compiler_params=pltpu.CompilerParams(
            collective_id=0, has_side_effects=True, vmem_limit_bytes=VMEM_BYTES
        ),
        name="self_forward",
    )(segments, padding, tokens, *weights, *prefix, memory, *mem_weights)


def self_backward_kernel(
    n,
    batches,
    base_in,
    do_in,
    sums_in,
    mkey_in,
    mvalue_in,
    wck_in,
    wcv_in,
    vecs_in,
    qx_in,
    kx_in,
    raw_in,
    pk_in,
    pv_in,
    pkt_in,
    ot_in,
    lse_in,
    wq_in,
    wk_in,
    wv_in,
    tg_ref,
    mgrad_ref,
    pkv_ref,
    vecs_ref,
    full_out,
    do_recv,
    qx,
    kx,
    raw,
    kt,
    values,
    dot,
    qdo,
    pk,
    pv,
    pkt,
    ot,
    stat,
    weights,
    dqt,
    dkv,
    g_send,
    g_recv,
    pre_ref,
    pre_all,
    pre_sum,
    pre_recv,
    sums_mine,
    sums_core,
    sums_x,
    sums_side,
    sums_z,
    full,
    mkey,
    mvalue,
    wck,
    wcv,
    mem_part,
    mem_side,
    mem_up,
    mem_down,
    vec_all,
    vec_sum,
    vec_y,
    vec_both,
    vec_z,
    product,
    base_ref,
    do_send_sem,
    do_recv_sem,
    g_send_sem,
    g_recv_sem,
    in_sem,
    send_sem,
    recv_sem,
):
    low = jnp.bfloat16
    f32 = jnp.float32
    me = lax.axis_index("seq")
    length, width = tg_ref.shape
    group = width // n
    heads = group // HD
    plane = 2 * length
    planes = n // 2
    step_rows = 256
    my_batch = lax.axis_index("batch")
    my_core = lax.rem(my_batch, 2)
    my_high = my_batch // 2
    highs = batches // 2
    my_plane = me // 2
    my_side = lax.rem(me, 2)
    beside = me + 1 - 2 * my_side
    used = [0]

    def numbers(count):
        used[0] += count
        return used[0] - count

    core_slot = numbers(2)
    x_slot = numbers(2 * highs)
    y_slot = numbers(3)
    z_slot = numbers(2 * planes)
    up_slot = numbers(planes)
    down_slot = numbers(planes)
    va_slot = numbers(batches)
    vb_slot = numbers(1)
    vc_slot = numbers(planes)
    pa_slot = numbers(batches)
    pb_slot = numbers(n)

    def send(source, target, first, peer_index, slot_index, axis, peer):
        return remote(
            source,
            target,
            send_sem.at[first + peer_index],
            recv_sem.at[first + slot_index],
            axis,
            peer,
        )

    half_rows = 2 * planes * highs * sums_z.shape[1]
    x_rows = half_rows // highs
    y_rows = x_rows // 2
    z_rows = y_rows // planes
    x_row = pl.multiple_of(my_high * x_rows, x_rows)
    y_row = pl.multiple_of(x_row + my_side * y_rows, y_rows)

    def part(row, count):
        return sums_mine.at[pl.ds(pl.multiple_of(row, count), count)]

    def reduce_core():
        return send(
            sums_in.at[1 - my_core], sums_core, core_slot, 0, 0, "batch", my_batch + 1 - 2 * my_core
        )

    def reduce_x(peer, slot):
        return send(
            part(peer * x_rows, x_rows),
            sums_x.at[slot],
            x_slot,
            peer,
            slot,
            "batch",
            2 * peer + my_core,
        )

    def reduce_y():
        return send(
            part(x_row + (1 - my_side) * y_rows, y_rows), sums_side, y_slot, 0, 0, "seq", beside
        )

    def reduce_z(peer, slot):
        return send(
            part(y_row + peer * z_rows, z_rows),
            sums_z.at[slot],
            z_slot,
            peer,
            slot,
            "seq",
            2 * peer + my_side,
        )

    def gather_z(peer, slot):
        piece = full.at[my_core, my_high, my_side, slot]
        return send(piece, piece, z_slot + planes, peer, slot, "seq", 2 * peer + my_side)

    def gather_y(side):
        piece = full.at[my_core, my_high, side]
        return send(piece, piece, y_slot + 1, 0, 0, "seq", beside)

    def gather_x(peer, slot):
        piece = full.at[my_core, slot]
        return send(piece, piece, x_slot + highs, peer, slot, "batch", 2 * peer + my_core)

    def gather_core(core):
        piece = full.at[core]
        return send(piece, piece, core_slot + 1, 0, 0, "batch", my_batch + 1 - 2 * my_core)

    def mem_across():
        return send(
            mem_part.at[:, 1 - my_side], mem_side, y_slot + 2, 0, 0, "seq", beside
        )

    def mem_hop(target, toward, peer=None):
        buffer, slot = (mem_up, up_slot) if toward > 0 else (mem_down, down_slot)
        return send(
            mem_part.at[target, my_side],
            buffer.at[target],
            slot,
            target,
            target,
            "seq",
            me + 2 * toward if peer is None else peer,
        )

    def mem_from(target, toward):
        return mem_hop(target, toward, me - 2 * toward)

    def mem_pass(toward):
        buffer = mem_up if toward > 0 else mem_down
        first = 0 if toward > 0 else planes - 1
        for target in range(planes):

            @pl.when((target - my_plane) * toward > 0)
            def _():
                @pl.when(my_plane != first)
                def _():
                    mem_from(target, toward).wait_recv()
                    mem_part[target, my_side] = (
                        mem_part[target, my_side].astype(f32) + buffer[target].astype(f32)
                    ).astype(low)

                mem_hop(target, toward).start()

    def mem_stage(at):
        pl.when(my_plane == at)(lambda: mem_pass(1))
        pl.when(my_plane == planes - 1 - at)(lambda: mem_pass(-1))

    def mem_end():
        value = mem_part[my_plane, my_side].astype(f32)
        mgrad_ref[...] = value.astype(low)

        @pl.when(my_plane > 0)
        def _():
            mem_from(my_plane, 1).wait_recv()
            mgrad_ref[...] = (mgrad_ref[...].astype(f32) + mem_up[my_plane].astype(f32)).astype(low)

        @pl.when(my_plane < planes - 1)
        def _():
            mem_from(my_plane, -1).wait_recv()
            mgrad_ref[...] = (
                mgrad_ref[...].astype(f32) + mem_down[my_plane].astype(f32)
            ).astype(low)

    def mem_drain():
        for target in range(planes):

            @pl.when(target > my_plane)
            def _():
                mem_hop(target, 1).wait_send()

            @pl.when(target < my_plane)
            def _():
                mem_hop(target, -1).wait_send()

    def vec_a(peer, slot):
        return send(vecs_in, vec_all.at[slot], va_slot, peer, slot, "batch", peer)

    def vec_b(side):
        return send(vec_sum, vec_y.at[side], vb_slot, 0, 0, "seq", beside)

    def vec_c(peer, slot):
        return send(vec_both, vec_z.at[slot], vc_slot, peer, slot, "seq", 2 * peer + my_side)

    def pre_a(peer, slot):
        return send(pre_ref, pre_all.at[slot], pa_slot, peer, slot, "batch", peer)

    def pre_b(peer, slot):
        return send(pre_sum, pre_recv.at[slot], pb_slot, peer, slot, "seq", peer)

    def do_copy(head, peer, slot):
        return remote(
            do_in.at[peer, head],
            do_recv.at[head, slot],
            do_send_sem.at[head, peer],
            do_recv_sem.at[head, slot],
            "seq",
            peer,
        )

    def q_copy(head, peer, slot):
        return remote(
            g_send.at[peer, head, 0],
            g_recv.at[0, slot, head],
            g_send_sem.at[0, head, peer],
            g_recv_sem.at[0, head, slot],
            "seq",
            peer,
        )

    def kv_copy(head, peer, slot):
        return remote(
            g_send.at[peer, head, pl.ds(1, 2)],
            g_recv.at[pl.ds(1, 2), slot, head],
            g_send_sem.at[1, head, peer],
            g_recv_sem.at[1, head, slot],
            "seq",
            peer,
        )

    def far_first(body):
        for index in range(n):
            peer = jnp.where(my_plane < planes // 2, n - 1 - index, index)

            @pl.when(peer != me)
            def _():
                body(peer)

    def added(ref, size):
        value = ref[0].astype(f32)
        for other in range(1, size):
            value = value + ref[other].astype(f32)
        return value

    loads = [
        pltpu.make_async_copy(source, target, in_sem.at[index])
        for index, (source, target) in enumerate(
            (
                (raw_in, raw),
                (mkey_in, mkey),
                (wck_in, wck),
                (mvalue_in, mvalue),
                (wcv_in, wcv),
                (sums_in.at[my_core], sums_mine),
                (vecs_in, vec_all.at[my_batch]),
                (pk_in, pk),
                (pv_in, pv),
                (pkt_in, pkt),
                (lse_in, stat),
                (ot_in, ot),
                (qx_in, qx),
                (kx_in, kx),
                (base_in, base_ref),
                (wq_in, weights.at[0]),
                (wk_in, weights.at[1]),
                (wv_in, weights.at[2]),
            )
        )
    ]
    own_do = pltpu.make_async_copy(do_in.at[me], do_recv.at[:, me], in_sem.at[len(loads)])
    own_do.start()
    for load in loads:
        load.start()
    enter({"seq": n, "batch": batches})
    far_first(lambda peer: do_copy(0, peer, me).start())
    reduce_core().start()
    others(batches, my_batch, lambda peer: vec_a(peer, my_batch).start())
    dkv[...] = jnp.zeros_like(dkv)
    product[...] = jnp.zeros_like(product)
    pre_ref[...] = jnp.zeros_like(pre_ref)
    loads[0].wait()

    def turn(index, carry):
        head = index // n
        chunk = lax.rem(index, n)
        here = rows_of(chunk, length)
        kt[head, :, here] = raw[head, chunk, 1]
        values[head, here, :] = raw[head, chunk, 2].astype(f32).T.astype(low)
        return carry

    lax.fori_loop(0, heads * n, turn, 0)
    for load in loads[1:5]:
        load.wait()

    def memory_back(index, carry):
        here = rows_of(index, step_rows)
        value = dot_nt(mkey[...], wck[here, :]) + dot_nt(mvalue[...], wcv[here, :])
        mem_part[:, :, :, here] = value.astype(low).reshape(mem_part.shape[:3] + (step_rows,))
        return carry

    lax.fori_loop(0, width // step_rows, memory_back, 0)
    mem_across().start()
    for load in loads[5:14]:
        load.wait()
    own_do.wait()

    def next_head(head):
        def move(peer):
            do_copy(head, peer, me).wait_send()
            do_copy(head + 1, peer, me).start()

        far_first(move)

    def arrive(head, which):
        for part in range(2):
            chunk = 2 * which + part

            @pl.when(chunk != me)
            def _():
                do_copy(head, chunk, chunk).wait_recv()

            grads = do_recv[head, chunk]
            dot[head, :, rows_of(chunk, length)] = grads
            grads = grads.astype(f32)
            query = raw[head, chunk, 0].astype(f32) * 0.125
            qdo[head, rows_of(chunk, length), :] = (
                jnp.concatenate([query, grads], axis=0).T.astype(low)
            )
            here = slice(part * length, (part + 1) * length)
            stat[which, head, 1:2, here] = jnp.sum(
                grads * ot[which, head, :HD, here], axis=0, keepdims=True
            )
        here = rows_of(which, plane)
        weight = jnp.exp(dot_nn(pk[head], qx[head, :, here]) - stat[which, head, 0:1, :])
        slope = weight * (dot_nn(pv[head], dot[head, :, here]) - stat[which, head, 1:2, :])
        both = jnp.concatenate([slope, weight], axis=0).astype(low)
        sums = dot_nn(both, qdo[head, here, :])
        pre_ref[head] += jnp.where(
            head_lanes((PREFIX_ROWS, 2 * HD), 0), sums[:PREFIX_ROWS], sums[PREFIX_ROWS:]
        )
        slope = slope.astype(low)
        dqt[which, head] = dot_nn(pkt[head], slope)

    def plus(first, second):
        return (first.astype(f32) + second.astype(f32)).astype(low)

    def sum_one():
        reduce_core().wait_recv()
        sums_mine[...] = plus(sums_mine[...], sums_core[...])
        others(highs, my_high, lambda peer: reduce_x(peer, my_high).start())

    def sum_two():
        here = pl.ds(x_row, x_rows)
        others(highs, my_high, lambda peer: reduce_x(peer, peer).wait_recv())
        sums_x[my_high] = sums_mine[here]
        sums_mine[here] = added(sums_x, highs).astype(low)
        reduce_y().start()

    def sum_three():
        here = pl.ds(y_row, y_rows)
        reduce_y().wait_recv()
        sums_mine[here] = plus(sums_mine[here], sums_side[...])
        others(planes, my_plane, lambda peer: reduce_z(peer, my_plane).start())

    def sum_four():
        here = pl.ds(pl.multiple_of(y_row + my_plane * z_rows, z_rows), z_rows)
        others(planes, my_plane, lambda peer: reduce_z(peer, peer).wait_recv())
        sums_z[my_plane] = sums_mine[here]
        full[my_core, my_high, my_side, my_plane] = added(sums_z, planes).astype(low)
        others(planes, my_plane, lambda peer: gather_z(peer, my_plane).start())

    def sum_five():
        others(planes, my_plane, lambda peer: gather_z(peer, peer).wait_recv())
        gather_y(my_side).start()

    def sum_six():
        gather_y(1 - my_side).wait_recv()
        others(highs, my_high, lambda peer: gather_x(peer, my_high).start())

    def sum_seven():
        others(highs, my_high, lambda peer: gather_x(peer, peer).wait_recv())
        gather_core(my_core).start()

    def sum_end():
        gather_core(1 - my_core).wait_recv()
        save_full.start()

    def vec_one():
        others(batches, my_batch, lambda peer: vec_a(peer, peer).wait_recv())
        vec_sum[...] = added(vec_all, batches)
        vec_b(my_side).start()
        vec_y[my_side] = vec_sum[...]

    def vec_two():
        vec_b(1 - my_side).wait_recv()
        value = (vec_y[0] + vec_y[1]).astype(f32)
        vec_both[...] = jnp.concatenate(
            [value[:, : width // 2], value[:, width // 2 :]], axis=0
        ).astype(low)
        others(planes, my_plane, lambda peer: vec_c(peer, my_plane).start())
        vec_z[my_plane] = vec_both[...]

    def vec_end():
        others(planes, my_plane, lambda peer: vec_c(peer, peer).wait_recv())
        value = added(vec_z, planes)
        vecs_ref[:, : width // 2] = value[:8]
        vecs_ref[:, width // 2 :] = value[8:]

    def mem_one():
        mem_across().wait_recv()
        mem_part[:, my_side] = plus(mem_part[:, my_side], mem_side[...])

    def stage_pa():
        others(batches, my_batch, lambda peer: pre_a(peer, my_batch).start())
        pre_all[my_batch] = pre_ref[...]

    def stage_pb():
        others(batches, my_batch, lambda peer: pre_a(peer, peer).wait_recv())
        pre_sum[...] = added(pre_all, batches).astype(low)
        others(n, me, lambda peer: pre_b(peer, me).start())
        pre_recv[me] = pre_sum[...]

    save_full = pltpu.make_async_copy(full, full_out, in_sem.at[0])

    def pair_part(head, upper, lower, first, count, diagonal):
        keys = span_of(lower * plane + first, count)
        here = span_of(upper * plane + first, plane - first)
        at = slice(first, plane)
        scores = dot_nn(kx[head, keys, :], qx[head, :, here])
        slope = dot_nn(values[head, keys, :], dot[head, :, here]) - stat[upper, head, 1:2, at]
        weight = jnp.exp(scores - stat[upper, head, 0:1, at])
        if diagonal:
            key_at = lax.broadcasted_iota(jnp.int32, scores.shape, 0)
            query_at = lax.broadcasted_iota(jnp.int32, scores.shape, 1)
            weight = jnp.where(key_at <= query_at, weight, 0.0)
        slope = (weight * slope).astype(low)
        key_part = dot_nn(slope, qdo[head, here, :])
        value_part = dot_nn(weight.astype(low), qdo[head, here, :])
        dkv[head, keys, :] += jnp.where(head_lanes((count, 2 * HD), 0), key_part, value_part)
        dqt[upper, head, :, at] += dot_nn(kt[head, :, keys], slope)

    def pair(head, upper, lower, diagonal):
        if diagonal:
            pair_part(head, upper, lower, 0, length, True)
            pair_part(head, upper, lower, length, length, True)
        else:
            pair_part(head, upper, lower, 0, plane, False)

    def hand_queries(head, which):
        for part in range(2):
            chunk = 2 * which + part
            g_send[chunk, head, 0] = (
                dqt[which, head, :, part * length : (part + 1) * length] * 0.125
            ).astype(low)

            @pl.when(chunk != me)
            def _():
                q_copy(head, chunk, me).start()

            @pl.when(chunk == me)
            def _():
                g_recv[0, me, head] = g_send[chunk, head, 0]

    def hand_keys(head, which):
        for part in range(2):
            chunk = 2 * which + part
            turned = dkv[head, rows_of(chunk, length), :].T.astype(low)
            g_send[chunk, head, 1] = turned[:HD]
            g_send[chunk, head, 2] = turned[HD:]

            @pl.when(chunk != me)
            def _():
                kv_copy(head, chunk, me).start()

            @pl.when(chunk == me)
            def _():
                g_recv[pl.ds(1, 2), me, head] = g_send[chunk, head, pl.ds(1, 2)]

    upper_half = my_plane >= planes // 2
    lead = jnp.where(upper_half, my_plane, planes - 1 - my_plane)
    total = heads * planes * (planes + 1) // 2
    hooks = [
        (2, sum_one),
        (3, mem_one),
        (4, lambda: mem_stage(0)),
        (5, vec_one),
        (5, sum_two),
        (7, sum_three),
        (8, vec_two),
        (10, sum_four),
        (12, sum_five),
        (14, sum_six),
        (16, vec_end),
        (17, sum_seven),
    ] + [(4 + 3 * at, functools.partial(mem_stage, at)) for at in range(1, planes - 1)]
    hooks += [
        (1 + head * total // heads, functools.partial(next_head, head)) for head in range(heads - 1)
    ]
    final = total - planes * (planes + 1) // 2
    hooks += [(final + planes + 1, stage_pa), (final + 2 * planes - 1, stage_pb)]

    def hook(pairs):
        for number, body in sorted(hooks, key=lambda item: item[0]):
            pl.when(pairs == number)(body)


    def stage(index, begun):
        head = index // planes
        step = lax.rem(index, planes)
        late = step >= lead
        rising = upper_half != late
        past = jnp.where(late, step - lead, step)
        here = jnp.where(rising, past, planes - 1 - past)
        stop = jnp.where(rising, jnp.where(late, my_plane, planes - 1), jnp.where(late, my_plane, 0))
        count = jnp.where(rising, stop - here, here - stop)

        @pl.when(step == 0)
        def _():
            arrive(head, here)

        @pl.when(jnp.logical_not(upper_half) & (step == 1))
        def _():
            def rest(which, inner):
                arrive(head, planes - 2 - which)
                return inner

            lax.fori_loop(0, planes - 1, rest, 0)

        hook(begun)
        pair(head, here, here, True)

        @pl.when(rising)
        def _():
            hand_queries(head, here)

        @pl.when(jnp.logical_not(rising))
        def _():
            hand_keys(head, here)

        def far(at, inner):
            there = jnp.where(rising, here + 1 + at, here - 1 - at)

            @pl.when(upper_half & (step == 0))
            def _():
                arrive(head, there)

            hook(begun + 1 + at)
            pair(head, jnp.maximum(here, there), jnp.minimum(here, there), False)
            return inner

        lax.fori_loop(0, count, far, 0)

        @pl.when(rising)
        def _():
            hand_keys(head, here)

        @pl.when(jnp.logical_not(rising))
        def _():
            hand_queries(head, here)

        return begun + 1 + count

    lax.fori_loop(0, heads * planes, stage, 0)
    for load in loads[14:]:
        load.wait()

    def gathered(peer):
        for head in range(heads):
            q_copy(head, peer, peer).wait_recv()
            kv_copy(head, peer, peer).wait_recv()

    half = width // 2

    def gather_plane(step, carry):
        which = lax.rem(my_plane + step, planes)
        for part in range(2):
            peer = 2 * which + part

            @pl.when(peer != me)
            def _():
                gathered(peer)

        columns = rows_of(which, 2 * group)
        for part in range(2):
            here = slice(part * half, (part + 1) * half)
            value = product[here, :]
            for kind in range(3):
                grads = g_recv[kind, pl.ds(2 * which, 2)].reshape(2 * group, length)
                value = value + dot_nn(weights[kind, here, columns], grads)
            product[here, :] = value
        return carry

    lax.fori_loop(0, planes - 1, gather_plane, 0)
    for other in range(n):

        @pl.when(other != me)
        def _():
            pre_b(other, other).wait_recv()

        value = pre_recv[other].astype(f32)
        for which in range(2):
            pkv_ref[:, which * width + other * group : which * width + (other + 1) * group] = (
                jnp.concatenate(
                    [value[head, :, which * HD : (which + 1) * HD] for head in range(heads)], axis=1
                )
            )

    mem_end()
    gather_plane(planes - 1, 0)
    sum_end()
    tile = 256
    for index in range(width // tile):
        here = slice(index * tile, (index + 1) * tile)
        tg_ref[:, here] = (base_ref[:, here] + product[here, :].T).astype(low)
    def drain(peer):
        do_copy(heads - 1, peer, me).wait_send()
        pre_b(peer, me).wait_send()
        for head in range(heads):
            q_copy(head, peer, me).wait_send()
            kv_copy(head, peer, me).wait_send()

    others(n, me, drain)
    others(batches, my_batch, lambda peer: pre_a(peer, my_batch).wait_send())
    others(batches, my_batch, lambda peer: vec_a(peer, my_batch).wait_send())
    reduce_core().wait_send()
    others(highs, my_high, lambda peer: reduce_x(peer, my_high).wait_send())
    reduce_y().wait_send()
    others(planes, my_plane, lambda peer: reduce_z(peer, my_plane).wait_send())
    others(planes, my_plane, lambda peer: gather_z(peer, my_plane).wait_send())
    gather_y(my_side).wait_send()
    others(highs, my_high, lambda peer: gather_x(peer, my_high).wait_send())
    gather_core(my_core).wait_send()
    mem_across().wait_send()
    mem_drain()
    others(planes, my_plane, lambda peer: vec_c(peer, my_plane).wait_send())
    vec_b(my_side).wait_send()
    save_full.wait()


def self_backward(
    n, batches, first_grad, out_grad, sums, mem_grads, mem_weights, vecs, saved, weights
):
    length, width = first_grad.shape
    group = width // n
    heads = group // HD
    whole = n * length
    planes = n // 2
    low = jnp.bfloat16
    f32 = jnp.float32
    vmem = pl.BlockSpec(memory_space=pltpu.VMEM)
    anywhere = pl.BlockSpec(memory_space=pl.ANY)
    dma = pltpu.SemaphoreType.DMA
    sum_rows = sums.shape[0] // (n * batches)
    mem_len = mem_grads[0].shape[0]
    mem_rows = mem_len // n
    mem_part = pltpu.VMEM((planes, mem_rows, width), low)
    mem_low = pltpu.VMEM((mem_len, width), low)
    square = pltpu.VMEM((width, width), low)
    vec = pltpu.VMEM((8, width), f32)
    copies = 6 + 2 * (batches // 2) + 5 * planes + 2 * batches + n
    qx, kx, raw, pk, pv, pkt, ot, stat = (pltpu.VMEM(value.shape, value.dtype) for value in saved)
    return pl.pallas_call(
        functools.partial(self_backward_kernel, n, batches),
        out_shape=(
            jax.ShapeDtypeStruct((length, width), low),
            jax.ShapeDtypeStruct((mem_rows, width), low),
            jax.ShapeDtypeStruct((PREFIX_ROWS, 2 * width), f32),
            jax.ShapeDtypeStruct((8, width), f32),
            jax.ShapeDtypeStruct((2, batches // 2, 2, planes, sum_rows, LANES), low),
        ),
        in_specs=[anywhere] * 19,
        out_specs=(vmem, vmem, vmem, vmem, anywhere),
        scratch_shapes=[
            pltpu.VMEM((heads, n, HD, length), low),
            qx,
            kx,
            raw,
            pltpu.VMEM((heads, HD, whole), low),
            pltpu.VMEM((heads, whole, HD), low),
            pltpu.VMEM((heads, HD, whole), low),
            pltpu.VMEM((heads, whole, 2 * HD), low),
            pk,
            pv,
            pkt,
            ot,
            stat,
            pltpu.VMEM((3, width, width), low),
            pltpu.VMEM((planes, heads, HD, 2 * length), f32),
            pltpu.VMEM((heads, whole, 2 * HD), f32),
            pltpu.VMEM((n, heads, 3, HD, length), low),
            pltpu.VMEM((3, n, heads, HD, length), low),
            pltpu.VMEM((heads, PREFIX_ROWS, 2 * HD), f32),
            pltpu.VMEM((batches, heads, PREFIX_ROWS, 2 * HD), f32),
            pltpu.VMEM((heads, PREFIX_ROWS, 2 * HD), low),
            pltpu.VMEM((n, heads, PREFIX_ROWS, 2 * HD), low),
            pltpu.VMEM((sums.shape[0] // 2, LANES), low),
            pltpu.VMEM((sums.shape[0] // 2, LANES), low),
            pltpu.VMEM((batches // 2, sums.shape[0] // batches, LANES), low),
            pltpu.VMEM((planes * sum_rows, LANES), low),
            pltpu.VMEM((planes, sum_rows, LANES), low),
            pltpu.VMEM((2, batches // 2, 2, planes, sum_rows, LANES), low),
            mem_low,
            mem_low,
            square,
            square,
            pltpu.VMEM((planes, 2, mem_rows, width), low),
            mem_part,
            mem_part,
            mem_part,
            pltpu.VMEM((batches, 8, width), f32),
            vec,
            pltpu.VMEM((2, 8, width), f32),
            pltpu.VMEM((16, width // 2), low),
            pltpu.VMEM((planes, 16, width // 2), low),
            pltpu.VMEM((width, length), f32),
            pltpu.VMEM((length, width), f32),
            dma((heads, n)),
            dma((heads, n)),
            dma((2, heads, n)),
            dma((2, heads, n)),
            dma((19,)),
            dma((copies,)),
            dma((copies,)),
        ],
        compiler_params=pltpu.CompilerParams(
            collective_id=1, has_side_effects=True, vmem_limit_bytes=VMEM_BYTES
        ),
        name="self_backward",
    )(
        first_grad,
        out_grad,
        sums.reshape(2, -1, LANES),
        *mem_grads,
        *mem_weights,
        vecs,
        *saved,
        *weights,
    )


def both_parts(value):
    high = value.astype(jnp.bfloat16).astype(jnp.float32)
    return jnp.concatenate([high, value - high], axis=0).astype(jnp.bfloat16)


def finish_kernel(
    full_in,
    vecs_ref,
    pkv_ref,
    emb_ref,
    first_in,
    fbias_ref,
    second_in,
    token_in,
    mem_in,
    embed_out,
    first_out,
    fbias_out,
    second_out,
    sbias_out,
    down_out,
    dbias_out,
    raise_out,
    rbias_out,
    gain_out,
    shift_out,
    token_out,
    mem_out,
    full_ref,
    first_ref,
    second_ref,
    token_ref,
    mem_ref,
    first_grad,
    second_grad,
    down_grad,
    raise_grad,
    emb,
    hidden,
    out_sem,
    in_sem,
):
    f32 = jnp.float32
    low = jnp.bfloat16
    width = emb_ref.shape[1]
    down = dbias_out.shape[1]
    count = emb_ref.shape[0]
    first = down * width // LANES
    loads = [
        pltpu.make_async_copy(source, target, in_sem.at[index])
        for index, (source, target) in enumerate(
            (
                (full_in.at[first:], full_ref.at[first:]),
                (full_in.at[:first], full_ref.at[:first]),
                (first_in, first_ref),
                (second_in, second_ref),
                (token_in, token_ref),
                (mem_in, mem_ref),
            )
        )
    ]
    for load in loads:
        load.start()
    saves = []

    def save(source, target, rows=None):
        if rows is not None:
            source, target = source.at[rows], target.at[rows]
        copy = pltpu.make_async_copy(source, target, out_sem.at[len(saves)])
        copy.start()
        saves.append(copy)

    loads[0].wait()
    for index in range(width // LANES):
        raise_grad[:, index * LANES : (index + 1) * LANES] = full_ref[
            first + index * down : first + (index + 1) * down, :
        ].astype(f32)
    save(raise_grad, raise_out)
    loads[1].wait()
    for index in range(down // LANES):
        down_grad[:, index * LANES : (index + 1) * LANES] = full_ref[
            index * width : (index + 1) * width, :
        ].astype(f32)
    save(down_grad, down_out)
    for load in loads[4:]:
        load.wait()
    save(token_ref, token_out)
    save(mem_ref, mem_out)
    loads[2].wait()
    emb[...] = jnp.zeros_like(emb)
    emb[:count, :] = emb_ref[...].astype(f32)
    emb_low = emb[...].astype(low)
    row = lax.broadcasted_iota(jnp.int32, hidden.shape, 0)
    hidden[...] = jnp.where(
        row < count, jnp.tanh(dot_nn(emb_low, first_ref[...]) + fbias_ref[...]), 0.0
    )
    value = hidden[...]
    prefix = pkv_ref[...]
    parts = both_parts(prefix)
    hidden_twice = jnp.concatenate([value, value], axis=0).T.astype(low)
    tile = 128
    for index in range(second_grad.shape[0] // tile):
        here = slice(index * tile, (index + 1) * tile)
        second_grad[here, :] = dot_nn(hidden_twice[here, :], parts)
        save(second_grad, second_out, here)
    sbias_out[...] = jnp.sum(prefix, axis=0, keepdims=True)
    loads[3].wait()
    grad = dot_nt(parts, second_ref[...])
    grad = (grad[:PREFIX_ROWS] + grad[PREFIX_ROWS:]) * (1.0 - value * value)
    fbias_out[...] = jnp.sum(grad, axis=0, keepdims=True)
    parts = both_parts(grad)
    emb_twice = jnp.concatenate([emb[...], emb[...]], axis=0).T.astype(low)
    first_grad[...] = dot_nn(emb_twice, parts)
    save(first_grad, first_out)
    back = dot_nt(parts, first_ref[...])
    embed_out[...] = (back[:PREFIX_ROWS] + back[PREFIX_ROWS:])[:count, :]
    rbias_out[...] = vecs_ref[0:1, :]
    dbias_out[...] = vecs_ref[1:2, :down]
    gain_out[...] = vecs_ref[2:5, :]
    shift_out[...] = vecs_ref[5:8, :]
    for copy in saves:
        copy.wait()


def finish(full, vecs, prefix_grad, embed, first, first_bias, second, down, token_grad, memory_grad):
    f32 = jnp.float32
    count, width = embed.shape
    hidden = first.shape[1]
    vmem = pl.BlockSpec(memory_space=pltpu.VMEM)
    anywhere = pl.BlockSpec(memory_space=pl.ANY)
    shapes = (
        (count, width),
        (width, hidden),
        (1, hidden),
        (hidden, 2 * width),
        (1, 2 * width),
        (width, down),
        (1, down),
        (down, width),
        (1, width),
        (3, width),
        (3, width),
    )
    return pl.pallas_call(
        finish_kernel,
        out_shape=tuple(jax.ShapeDtypeStruct(shape, f32) for shape in shapes)
        + tuple(
            jax.ShapeDtypeStruct(value.shape, value.dtype) for value in (token_grad, memory_grad)
        ),
        in_specs=[anywhere, vmem, vmem, vmem, anywhere, vmem, anywhere, anywhere, anywhere],
        out_specs=(
            vmem,
            anywhere,
            vmem,
            anywhere,
            vmem,
            anywhere,
            vmem,
            anywhere,
            vmem,
            vmem,
            vmem,
            anywhere,
            anywhere,
        ),
        scratch_shapes=[
            pltpu.VMEM(full.shape, jnp.bfloat16),
            pltpu.VMEM(first.shape, jnp.bfloat16),
            pltpu.VMEM(second.shape, jnp.bfloat16),
            pltpu.VMEM(token_grad.shape, token_grad.dtype),
            pltpu.VMEM(memory_grad.shape, memory_grad.dtype),
            pltpu.VMEM((width, hidden), f32),
            pltpu.VMEM((hidden, 2 * width), f32),
            pltpu.VMEM((width, down), f32),
            pltpu.VMEM((down, width), f32),
            pltpu.VMEM((PREFIX_ROWS, width), f32),
            pltpu.VMEM((PREFIX_ROWS, hidden), f32),
            pltpu.SemaphoreType.DMA((5 + hidden // 128,)),
            pltpu.SemaphoreType.DMA((6,)),
        ],
        compiler_params=pltpu.CompilerParams(vmem_limit_bytes=VMEM_BYTES),
        name="finish",
    )(full, vecs, prefix_grad, embed, first, first_bias, second, token_grad, memory_grad)


def gelu_pair(value):
    size = jnp.abs(value)
    step = 1.0 / (1.0 + (0.3275911 * 0.7071067811865476) * size)
    bell = jnp.exp(-0.5 * value * value)
    poly = step * (
        0.127414796
        + step
        * (-0.142248368 + step * (0.7107068705 + step * (-0.7265760135 + step * 0.5307027145)))
    )
    act = jnp.maximum(value, 0.0) - size * (poly * bell)
    turn = bell * (0.3989422804014327 * size - poly)
    return act, jnp.where(value >= 0.0, 1.0 + turn, -turn)


def normed(value):
    center = jnp.mean(value, axis=-1, keepdims=True)
    centered = value - center
    scale = lax.rsqrt(jnp.mean(centered * centered, axis=-1, keepdims=True) + norm_eps)
    return centered * scale, scale


def norm_back(grad, scale, unit):
    return scale * (
        grad
        - jnp.mean(grad, axis=-1, keepdims=True)
        - unit * jnp.mean(grad * unit, axis=-1, keepdims=True)
    )


def middle_kernel(
    tok_in,
    att_in,
    cot_in,
    mkey_in,
    mvalue_in,
    gain_ref,
    shift_ref,
    dbias_ref,
    rbias_ref,
    wo_in,
    wcq_in,
    wco_in,
    wd_in,
    wr_in,
    win_in,
    wout_in,
    layer_out,
    fgrad_out,
    ograd_out,
    mkey_out,
    mvalue_out,
    sums_out,
    vecs_ref,
    tok_ref,
    att_ref,
    cot_ref,
    mkey_ref,
    mvalue_ref,
    out_ref,
    fgrad_ref,
    ograd_ref,
    sums_ref,
    wo,
    wcq,
    wco,
    wd,
    wr,
    win,
    wout,
    unit_one,
    unit_two,
    work,
    total,
    scale_one,
    scale_two,
    low_one,
    low_two,
    low_three,
    query,
    crossed,
    weights,
    slopes,
    acts,
    down_act,
    down_slope,
    down_grad,
    load_sem,
    win_sem,
    wout_sem,
    out_sem,
):
    length, width = tok_ref.shape
    resident = len(win.shape) == 2
    tile = 512 if resident else win.shape[2]
    tiles = win_in.shape[1] // tile
    slots = tiles if resident else win.shape[0]
    rows_step = length // 2
    low = jnp.bfloat16
    f32 = jnp.float32

    sources = (
        att_in,
        wo_in,
        tok_in,
        wcq_in,
        mkey_in,
        mvalue_in,
        wco_in,
        wd_in,
        wr_in,
        cot_in,
    )
    targets = (att_ref, wo, tok_ref, wcq, mkey_ref, mvalue_ref, wco, wd, wr, cot_ref)
    loads = [
        pltpu.make_async_copy(source, target, load_sem.at[index])
        for index, (source, target) in enumerate(zip(sources, targets))
    ]

    def win_load(which):
        slot = which % slots
        target = win.at[:, rows_of(which, tile)] if resident else win.at[slot]
        return pltpu.make_async_copy(win_in.at[:, rows_of(which, tile)], target, win_sem.at[slot])

    def wout_load(which):
        slot = which % slots
        target = wout.at[rows_of(which, tile), :] if resident else wout.at[slot]
        return pltpu.make_async_copy(wout_in.at[rows_of(which, tile), :], target, wout_sem.at[slot])

    for load in loads[:7]:
        load.start()

    def by_columns(extent, step, body):
        def one(index, carry):
            body(pl.ds(pl.multiple_of(index * step, step), step))
            return carry

        lax.fori_loop(0, extent // step, one, 0)

    def by_rows(body, init=0):
        def one(index, carry):
            return body(rows_of(index, rows_step), carry)

        return lax.fori_loop(0, length // rows_step, one, init)

    cols = 512
    half = width // 2

    for load in loads[:3]:
        load.wait()
    for load in loads[7:]:
        load.start()
    for which in range(slots):
        win_load(which).start()
    for which in range(slots):
        wout_load(which).start()

    def project_out(here):
        work[:, here] = tok_ref[:, here].astype(f32) + dot_nn(att_ref[...], wo[:, here])

    by_columns(width, cols, project_out)

    def first_norm(here, carry):
        unit, scale = normed(work[here, :])
        unit_one[here, :] = unit
        scale_one[here, :] = scale
        value = unit * gain_ref[0:1, :] + shift_ref[0:1, :]
        work[here, :] = value
        low_one[here, :] = value.astype(low)
        return carry

    by_rows(first_norm)

    loads[3].wait()

    def project_query(here):
        query[:, here] = dot_nn(low_one[...], wcq[:, here]).astype(low)

    by_columns(width, cols, project_query)
    per_block = LANES // HD

    def stacked(value):
        return jnp.concatenate(
            [jnp.where(head_lanes(value.shape, head), value, 0.0) for head in range(per_block)],
            axis=0,
        ).astype(low)

    def unstacked(value):
        return jnp.concatenate(
            [
                value[head * HD : (head + 1) * HD, head * length : (head + 1) * length]
                for head in range(per_block)
            ],
            axis=0,
        )

    def block_queries(here):
        return stacked(query[:, here].astype(f32) * 0.125)

    def cross_forward(block):
        here = rows_of(block, LANES)
        scores = dot_nt(mkey_ref[:, here], block_queries(here))
        raised = jnp.exp(scores - jnp.max(scores, axis=0, keepdims=True))
        share = 1.0 / jnp.sum(raised, axis=0, keepdims=True)
        weight = (raised * share).astype(low)
        weights[block] = weight
        values = mvalue_ref[:, here].astype(f32).T.astype(low)
        crossed[:, here] = unstacked(dot_nn(values, weight)).T.astype(low)

    loads[4].wait()
    loads[5].wait()

    def cross_forward_both(step, carry):
        cross_forward(2 * step)
        cross_forward(2 * step + 1)
        return carry

    lax.fori_loop(0, width // LANES // 2, cross_forward_both, 0)

    loads[6].wait()

    def project_crossed(here):
        work[:, here] += dot_nn(crossed[...], wco[:, here])

    by_columns(width, cols, project_crossed)

    def second_norm(here, carry):
        unit, scale = normed(work[here, :])
        unit_two[here, :] = unit
        scale_two[here, :] = scale
        value = unit * gain_ref[1:2, :] + shift_ref[1:2, :]
        work[here, :] = value
        low_two[here, :] = value.astype(low)
        return carry

    by_rows(second_norm)

    step_cols = 512

    def feed_part(here, source):
        act, slope = gelu_pair(dot_nn(low_two[...], source))
        slopes[:, here] = slope.astype(low)
        return act.astype(low)

    if resident:

        def feed_forward(which, carry):
            here = rows_of(which, step_cols)

            @pl.when(which % (tile // step_cols) == 0)
            def _():
                win_load(which // (tile // step_cols)).wait()

            acts[:, here] = feed_part(here, win[:, here])
            return carry

        lax.fori_loop(0, tiles * tile // step_cols, feed_forward, 0)
        for which in range(tiles):
            wout_load(which).wait()

        def feed_out_part(here):
            total[:, here] = dot_nn(acts[...], wout[:, here])

        by_columns(width, step_cols, feed_out_part)
    else:
        total[...] = jnp.zeros_like(total)

        def feed_forward(which, carry):
            slot = lax.rem(which, slots)
            win_load(which).wait()
            wout_load(which).wait()
            total[...] += dot_nn(feed_part(rows_of(which, tile), win[slot]), wout[slot])

            @pl.when(which + slots < tiles)
            def _():
                win_load(which + slots).start()
                wout_load(which + slots).start()

            return carry

        lax.fori_loop(0, tiles, feed_forward, 0)

    loads[7].wait()
    loads[8].wait()
    loads[9].wait()
    act, slope = gelu_pair(dot_nn(low_two[...], wd[...]) + dbias_ref[...])
    down_act[...] = act.astype(low)
    down_slope[...] = slope.astype(low)

    def project_raise(here):
        work[:, here] += total[:, here] + 4.0 * (
            dot_nn(down_act[...], wr[:, here]) + rbias_ref[:, here]
        )

    by_columns(width, cols, project_raise)
    nothing = jnp.zeros((1, width), f32)

    def third_norm(here, carry):
        gain_sum, shift_sum, bias_sum = carry
        unit, scale = normed(work[here, :])
        gain = gain_ref[2:3, :]
        out_ref[here, :] = (unit * gain + shift_ref[2:3, :]).astype(low)
        grad = cot_ref[here, :].astype(f32)
        back = norm_back(grad * gain, scale, unit)
        total[here, :] = back
        back_low = back.astype(low)
        low_three[here, :] = back_low
        return (
            gain_sum + jnp.sum(grad * unit, axis=0, keepdims=True),
            shift_sum + jnp.sum(grad, axis=0, keepdims=True),
            bias_sum + jnp.sum(back_low.astype(f32), axis=0, keepdims=True),
        )

    gain_three, shift_three, bias_sum = by_rows(third_norm, (nothing, nothing, nothing))
    saves = []

    def save(source, target):
        copy = pltpu.make_async_copy(source, target, out_sem.at[len(saves)])
        copy.start()
        saves.append(copy)

    save(out_ref, layer_out)
    vecs_ref[0:1, :] = 4.0 * bias_sum

    back = 4.0 * dot_nt(low_three[...], wr[...]) * down_slope[...].astype(f32)
    back_low = back.astype(low)
    down_grad[...] = back_low
    vecs_ref[1:2, :] = jnp.concatenate(
        [
            jnp.sum(back_low.astype(f32), axis=0, keepdims=True),
            jnp.zeros((1, width - wd.shape[1]), f32),
        ],
        axis=1,
    )
    down = wd.shape[1]
    raise_sum = 4.0 * dot_tn(down_act[...], low_three[...])
    for index in range(width // LANES):
        sums_ref[pl.ds(down * width // LANES + index * down, down), :] = raise_sum[
            :, index * LANES : (index + 1) * LANES
        ].astype(low)
    down_sum = dot_tn(low_two[...], down_grad[...])
    for index in range(down // LANES):
        sums_ref[index * width : (index + 1) * width, :] = down_sum[
            :, index * LANES : (index + 1) * LANES
        ].astype(low)

    save(sums_ref, sums_out)

    if resident:

        def feed_slope(here):
            acts[:, here] = (
                dot_nt(low_three[...], wout[here, :]) * slopes[:, here].astype(f32)
            ).astype(low)

        by_columns(win_in.shape[1], step_cols, feed_slope)

        def feed_in_part(here):
            total[:, here] += dot_nt(acts[...], win[here, :])

        by_columns(width, step_cols, feed_in_part)
    else:

        def feed_backward(step, carry):
            which = tiles - 1 - step
            slot = lax.rem(which, slots)
            here = rows_of(which, tile)

            @pl.when(which < tiles - slots)
            def _():
                wout_load(which).wait()
                win_load(which).wait()

            grad = dot_nt(low_three[...], wout[slot]) * slopes[:, here].astype(f32)
            total[...] += dot_nt(grad.astype(low), win[slot])

            @pl.when(which >= slots)
            def _():
                win_load(which - slots).start()
                wout_load(which - slots).start()

            return carry

        lax.fori_loop(0, tiles, feed_backward, 0)

    def down_back(here):
        total[:, here] += dot_nt(down_grad[...], wd[here, :])

    by_columns(width, cols, down_back)

    def second_back(here, carry):
        gain_sum, shift_sum = carry
        grad = total[here, :]
        unit = unit_two[here, :]
        back = norm_back(grad * gain_ref[1:2, :], scale_two[here, :], unit)
        total[here, :] = back
        low_one[here, :] = back.astype(low)
        return (
            gain_sum + jnp.sum(grad * unit, axis=0, keepdims=True),
            shift_sum + jnp.sum(grad, axis=0, keepdims=True),
        )

    gain_two, shift_two = by_rows(second_back, (nothing, nothing))

    def crossed_back(here):
        crossed[:, here] = dot_nt(low_one[...], wco[here, :]).astype(low)

    by_columns(width, cols, crossed_back)

    def cross_backward(block):
        here = rows_of(block, LANES)
        grads = stacked(crossed[:, here].astype(f32))
        keys = mkey_ref[:, here].astype(f32).T.astype(low)
        slope = dot_nt(mvalue_ref[:, here], grads)
        weight_low = weights[block]
        weight = weight_low.astype(f32)
        slope = weight * (slope - jnp.sum(weight * slope, axis=0, keepdims=True))
        slope = slope.astype(low)
        queries = block_queries(here)
        mkey_ref[:, here] = dot_nn(slope, queries).astype(low)
        mvalue_ref[:, here] = dot_nn(weight_low, grads).astype(low)
        query[:, here] = (unstacked(dot_nn(keys, slope)) * 0.125).T.astype(low)

    def cross_backward_both(step, carry):
        cross_backward(2 * step)
        cross_backward(2 * step + 1)
        return carry

    lax.fori_loop(0, width // LANES // 2, cross_backward_both, 0)
    save(mkey_ref, mkey_out)
    save(mvalue_ref, mvalue_out)

    def query_back(here):
        total[:, here] += dot_nt(query[...], wcq[here, :])

    by_columns(width, cols, query_back)

    def first_back(here, carry):
        gain_sum, shift_sum = carry
        grad = total[here, :]
        unit = unit_one[here, :]
        back = norm_back(grad * gain_ref[0:1, :], scale_one[here, :], unit)
        fgrad_ref[here, :] = back
        low_one[here, :] = back.astype(low)
        return (
            gain_sum + jnp.sum(grad * unit, axis=0, keepdims=True),
            shift_sum + jnp.sum(grad, axis=0, keepdims=True),
        )

    gain_one, shift_one = by_rows(first_back, (nothing, nothing))
    save(fgrad_ref, fgrad_out)

    for index in range(width // cols):
        here = slice(index * cols, (index + 1) * cols)
        ograd_ref[here, :] = dot_nt(low_one[...], wo[here, :]).T.astype(low)
        save(ograd_ref.at[here], ograd_out.at[here])
    for index, vector in enumerate(
        (gain_one, gain_two, gain_three, shift_one, shift_two, shift_three)
    ):
        vecs_ref[2 + index : 3 + index, :] = vector
    for copy in saves:
        copy.wait()


def middle(
    tokens, attended, cotangent, mem_key, mem_value, gains, shifts, down_bias, raise_bias, weights
):
    length, width = tokens.shape
    mem_len = mem_key.shape[0]
    down = weights[3].shape[1]
    feed = weights[5].shape[1]
    tile = 512 if mem_len <= 512 else 128
    resident = mem_len <= 512
    slots = feed // tile if resident else 2
    low = jnp.bfloat16
    f32 = jnp.float32
    vmem = pl.BlockSpec(memory_space=pltpu.VMEM)
    anywhere = pl.BlockSpec(memory_space=pl.ANY)
    square = pltpu.VMEM((width, width), low)
    wide = pltpu.VMEM((length, width), f32)
    narrow = pltpu.VMEM((length, width), low)
    return pl.pallas_call(
        middle_kernel,
        out_shape=(
            jax.ShapeDtypeStruct((length, width), low),
            jax.ShapeDtypeStruct((length, width), f32),
            jax.ShapeDtypeStruct((width, length), low),
            jax.ShapeDtypeStruct((mem_len, width), low),
            jax.ShapeDtypeStruct((mem_len, width), low),
            jax.ShapeDtypeStruct((2 * down * width // LANES, LANES), low),
            jax.ShapeDtypeStruct((8, width), f32),
        ),
        in_specs=[anywhere] * 5 + [vmem] * 4 + [anywhere] * 7,
        out_specs=(anywhere,) * 6 + (vmem,),
        scratch_shapes=[
            narrow,
            narrow,
            narrow,
            pltpu.VMEM((mem_len, width), low),
            pltpu.VMEM((mem_len, width), low),
            narrow,
            wide,
            pltpu.VMEM((width, length), low),
            pltpu.VMEM((2 * down * width // LANES, LANES), low),
            square,
            square,
            square,
            pltpu.VMEM((width, down), low),
            pltpu.VMEM((down, width), low),
            pltpu.VMEM((width, feed) if resident else (slots, width, tile), low),
            pltpu.VMEM((feed, width) if resident else (slots, tile, width), low),
            wide,
            wide,
            wide,
            wide,
            pltpu.VMEM((length, 1), f32),
            pltpu.VMEM((length, 1), f32),
            narrow,
            narrow,
            narrow,
            narrow,
            narrow,
            pltpu.VMEM((width // LANES, mem_len, LANES // HD * length), low),
            pltpu.VMEM((length, feed), low),
            pltpu.VMEM((length, feed) if resident else (16, LANES), low),
            pltpu.VMEM((length, down), low),
            pltpu.VMEM((length, down), low),
            pltpu.VMEM((length, down), low),
            pltpu.SemaphoreType.DMA((10,)),
            pltpu.SemaphoreType.DMA((slots,)),
            pltpu.SemaphoreType.DMA((slots,)),
            pltpu.SemaphoreType.DMA((5 + width // 512,)),
        ],
        compiler_params=pltpu.CompilerParams(vmem_limit_bytes=VMEM_BYTES + 3 * 1024 * 1024),
        name="middle",
    )(tokens, attended, cotangent, mem_key, mem_value, gains, shifts, down_bias, raise_bias, *weights)


def per_device(
    tokens,
    memory,
    segment_ids,
    padding_mask,
    cotangent,
    prefix_embed,
    prefix_first,
    first_bias,
    prefix_second,
    second_bias,
    adapter_down,
    down_bias,
    adapter_raise,
    raise_bias,
    norm_gain,
    norm_shift,
    self_query,
    self_key,
    self_value,
    self_output,
    cross_query,
    cross_key,
    cross_value,
    cross_output,
    feed_in,
    feed_out,
):
    row_count, length, model_width = tokens.shape
    flat_rows = row_count * length
    n = lax.axis_size("seq")
    batches = lax.axis_size("batch")
    down = adapter_down.shape[1]
    attended, mem_key, mem_value, *saved = self_forward(
        n,
        segment_ids,
        padding_mask,
        tokens.reshape(flat_rows, model_width),
        (self_query, self_key, self_value),
        (
            prefix_embed,
            prefix_first,
            first_bias.reshape(1, -1),
            prefix_second,
            second_bias.reshape(1, -1),
        ),
        memory.reshape(-1, model_width),
        (cross_key, cross_value),
    )
    layer_output, first_grad, out_grad, *mem_grads, weight_sums, vector_sums = middle(
        tokens.reshape(flat_rows, model_width),
        attended,
        cotangent.reshape(flat_rows, model_width),
        mem_key,
        mem_value,
        norm_gain,
        norm_shift,
        down_bias.reshape(1, -1),
        raise_bias.reshape(1, -1),
        (
            self_output,
            cross_query,
            cross_output,
            adapter_down,
            adapter_raise,
            feed_in,
            feed_out,
        ),
    )
    layer_output = layer_output.reshape(row_count, length, model_width)
    token_grad, memory_grad, prefix_grad, vector_sums, full_sums = self_backward(
        n,
        batches,
        first_grad,
        out_grad.reshape(n, -1, HD, length),
        weight_sums,
        mem_grads,
        (cross_key, cross_value),
        vector_sums,
        saved,
        (self_query, self_key, self_value),
    )
    *replicated, token_grad, memory_grad = finish(
        full_sums.reshape(-1, LANES),
        vector_sums,
        prefix_grad,
        prefix_embed,
        prefix_first,
        first_bias.reshape(1, -1),
        prefix_second,
        down,
        token_grad,
        memory_grad,
    )
    token_grad = token_grad.reshape(row_count, length, model_width)
    memory_grad = memory_grad.reshape(memory.shape)
    replicated = [
        value.reshape(-1) if value.shape[0] == 1 else value for value in replicated
    ]
    return (layer_output, token_grad, memory_grad, *replicated)


def solution(mesh):
    placed = (
        P("batch", "seq", None),
        P("batch", "seq", None),
        P("batch", "seq"),
        P("batch", "seq"),
        P("batch", "seq", None),
        P(),
        P(),
        P(),
        P(),
        P(),
        P(),
        P(),
        P(),
        P(),
        P(),
        P(),
        P(),
        P(),
        P(),
        P(),
        P(),
        P(),
        P(),
        P(),
        P(),
        P(),
    )
    return jax.shard_map(
        per_device,
        mesh=mesh,
        in_specs=placed,
        out_specs=(
            P("batch", "seq", None),
            P("batch", "seq", None),
            P("batch", "seq", None),
            P(),
            P(),
            P(),
            P(),
            P(),
            P(),
            P(),
            P(),
            P(),
            P(),
            P(),
        ),
        check_vma=False,
    )
```

```python
import functools

import jax
import jax.numpy as jnp
from jax import lax
from jax.experimental import pallas as pl
from jax.experimental.pallas import tpu as pltpu
from jax.sharding import PartitionSpec as P

H = 16
HD = 64
LANES = 128
PREFIX_ROWS = 32
VMEM_BYTES = 60 * 1024 * 1024
SUM_ROWS = 16
MESH = pl.DeviceIdType.MESH

masked_score = -1e30
norm_eps = 1e-05

def dot_nn(left, right):
    return lax.dot_general(
        left, right, (((1,), (0,)), ((), ())), preferred_element_type=jnp.float32
    )


def dot_nt(left, right):
    return lax.dot_general(
        left, right, (((1,), (1,)), ((), ())), preferred_element_type=jnp.float32
    )


def dot_tn(left, right):
    return lax.dot_general(
        left, right, (((0,), (0,)), ((), ())), preferred_element_type=jnp.float32
    )


def remote(source, target, send_sem, recv_sem, axis, peer):
    return pltpu.make_async_remote_copy(
        src_ref=source,
        dst_ref=target,
        send_sem=send_sem,
        recv_sem=recv_sem,
        device_id={axis: peer},
        device_id_type=MESH,
    )


def enter(sizes):
    barrier = pltpu.get_barrier_semaphore()
    for axis, size in sizes.items():
        for other in range(size):

            @pl.when(other != lax.axis_index(axis))
            def _():
                pl.semaphore_signal(barrier, inc=1, device_id={axis: other}, device_id_type=MESH)

    pl.semaphore_wait(barrier, sum(sizes.values()) - len(sizes))


def others(size, mine, body):
    for other in range(size):

        @pl.when(other != mine)
        def _():
            body(other)


def rows_of(index, size):
    return pl.ds(pl.multiple_of(index * size, size), size)


def span_of(start, size):
    return pl.ds(pl.multiple_of(start, LANES), size)


def own_columns(ref, first, me, width):
    if width % LANES == 0:
        return ref[:, pl.ds(pl.multiple_of(first + me * width, LANES), width)].astype(jnp.float32)
    share = LANES // width
    block = ref[:, pl.ds(pl.multiple_of(first + me // share * LANES, LANES), LANES)].astype(
        jnp.float32
    )
    picked = block[:, :width]
    for part in range(1, share):
        picked = jnp.where(me % share == part, block[:, part * width : (part + 1) * width], picked)
    return picked


def head_lanes(shape, head):
    lane = lax.broadcasted_iota(jnp.int32, shape, 1)
    return (lane >= head * HD) & (lane < (head + 1) * HD)


def self_forward_kernel(
    n,
    seg_ref,
    pad_ref,
    tok_ref,
    wq_in,
    wk_in,
    wv_in,
    emb_ref,
    first_in,
    fbias_ref,
    second_in,
    sbias_ref,
    mem_ref,
    wck_in,
    wcv_in,
    att_ref,
    mkey_out,
    mvalue_out,
    qx_out,
    kx_out,
    raw_out,
    pk_out,
    pv_out,
    pkt_out,
    ot_out,
    lse_out,
    send,
    recv,
    meta_send,
    meta,
    kx,
    qx,
    vt,
    hidden,
    pk,
    pv,
    pkt,
    pvt,
    stat,
    acc,
    o_send,
    o_recv,
    mem_all,
    wck,
    wcv,
    mkey_ref,
    mvalue_ref,
    wq_ref,
    wk_ref,
    wv_ref,
    first_ref,
    second_ref,
    send_sem,
    recv_sem,
    meta_send_sem,
    meta_recv_sem,
    o_send_sem,
    o_recv_sem,
    mem_send_sem,
    mem_recv_sem,
    out_sem,
    weight_sem,
    in_sem,
):
    low = jnp.bfloat16
    f32 = jnp.float32
    me = lax.axis_index("seq")
    length, width = tok_ref.shape
    group = width // n
    heads = group // HD
    plane = 2 * length
    planes = n // 2
    block = 2 * LANES
    per_block = block // group
    blocks = width // block
    my_plane = me // 2
    my_side = lax.rem(me, 2)

    upward = my_plane >= planes // 2
    turn_sign = jnp.where(upward, 1, -1)

    def plane_after(step):
        return lax.rem(my_plane + planes + turn_sign * step, planes)

    def meta_copy(peer, slot):
        return remote(
            meta_send, meta.at[slot], meta_send_sem.at[peer], meta_recv_sem.at[slot], "seq", peer
        )

    def qkv_copy(head, peer, slot):
        return remote(
            send.at[peer, head],
            recv.at[head, slot],
            send_sem.at[head, peer],
            recv_sem.at[head, slot],
            "seq",
            peer,
        )

    def out_copy(head, peer, slot):
        return remote(
            o_send.at[head, peer],
            o_recv.at[slot, head],
            o_send_sem.at[head, peer],
            o_recv_sem.at[head, slot],
            "seq",
            peer,
        )

    def mem_along(which, toward):
        part = mem_all.at[which, my_side]
        return remote(
            part,
            part,
            mem_send_sem.at[(toward + 1) // 2, which],
            mem_recv_sem.at[which],
            "seq",
            me + 2 * toward,
        )

    def mem_across(side):
        part = mem_all.at[:, side]
        return remote(
            part,
            part,
            mem_send_sem.at[0, planes],
            mem_recv_sem.at[planes],
            "seq",
            me + 1 - 2 * my_side,
        )

    def mem_hops(hop, body):
        for toward in (1, -1):
            which = my_plane - toward * hop
            ahead = my_plane + toward

            @pl.when((which >= 0) & (which < planes) & (ahead >= 0) & (ahead < planes))
            def _():
                body(mem_along(which, toward))

    def mem_arrivals(hop):
        for toward in (1, -1):
            which = my_plane - toward * hop

            @pl.when((which >= 0) & (which < planes))
            def _():
                mem_along(which, -toward).wait_recv()

    def block_at(step):
        if blocks >= planes:
            share = blocks // planes
            return plane_after(1 + step // share) * share + step % share
        return lax.rem(me // per_block + 1 + step, blocks)

    def weight_load(step, which):
        columns = rows_of(block_at(step), block)
        source = (wq_in, wk_in, wv_in)[which]
        target = (wq_ref, wk_ref, wv_ref)[which]
        return pltpu.make_async_copy(
            source.at[:, columns], target.at[:, columns], weight_sem.at[step, which]
        )

    for step in range(blocks):
        for which in range(3):
            weight_load(step, which).start()
    loads = [
        pltpu.make_async_copy(source, target, in_sem.at[index])
        for index, (source, target) in enumerate(
            ((first_in, first_ref), (second_in, second_ref), (wck_in, wck), (wcv_in, wcv))
        )
    ]
    for load in loads:
        load.start()
    segments = seg_ref[...]
    tags = jnp.where(pad_ref[...] == 1, segments, -1)
    row = lax.broadcasted_iota(jnp.int32, meta_send.shape, 0)
    meta_send[...] = jnp.where(row == 0, segments, tags)
    mem_all[my_plane, my_side] = mem_ref[...]
    enter({"seq": n})
    others(n, me, lambda peer: meta_copy(peer, me).start())
    meta[me] = meta_send[...]

    for step in range(blocks):
        at = block_at(step)
        columns = rows_of(at, block)
        for which, weight in enumerate((wq_ref, wk_ref, wv_ref)):
            weight_load(step, which).wait()
            piece = dot_nn(tok_ref[...], weight[:, columns]).T.astype(low)
            for part in range(per_block):
                for head in range(heads):
                    first = part * group + head * HD
                    send[at * per_block + part, head, which] = piece[first : first + HD]
        for part in range(per_block):
            peer = at * per_block + part

            @pl.when(peer != me)
            def _():
                qkv_copy(0, peer, me).start()

            @pl.when(peer == me)
            def _():
                for head in range(heads):
                    recv[head, me] = send[peer, head]

    mem_hops(0, lambda copy: copy.start())
    loads[0].wait()
    loads[1].wait()
    hidden[...] = jnp.zeros_like(hidden)
    hidden[: emb_ref.shape[0], :] = jnp.tanh(dot_nn(emb_ref[...], first_ref[...]) + fbias_ref[...])
    hidden_low = hidden[...].astype(low)
    prefix_key = dot_nn(hidden_low, own_columns(second_ref, 0, me, group).astype(low)) + own_columns(
        sbias_ref, 0, me, group
    )
    prefix_value = dot_nn(
        hidden_low, own_columns(second_ref, width, me, group).astype(low)
    ) + own_columns(sbias_ref, width, me, group)
    prefix_row = lax.broadcasted_iota(jnp.int32, (PREFIX_ROWS, HD), 0)
    prefix_open = jnp.where(prefix_row < emb_ref.shape[0], 0.0, masked_score)
    for head in range(heads):
        here = slice(head * HD, (head + 1) * HD)
        pk[head] = jnp.concatenate([prefix_key[:, here], prefix_open], axis=1).astype(low)
        pv[head] = prefix_value[:, here].astype(low)
    pkt[...] = prefix_key.T.astype(low).reshape(heads, HD, PREFIX_ROWS)
    pvt[:, :HD, :] = prefix_value.T.astype(low).reshape(heads, HD, PREFIX_ROWS)
    pvt[:, HD:, :] = jnp.ones((heads, SUM_ROWS, PREFIX_ROWS), low)
    vt[:, HD:, :] = jnp.ones((heads, SUM_ROWS, n * length), low)

    def arrive(head, chunk):
        @pl.when(chunk != me)
        def _():
            @pl.when(head == 0)
            def _():
                meta_copy(chunk, chunk).wait_recv()

            qkv_copy(head, chunk, chunk).wait_recv()

        here = rows_of(chunk, length)
        state = lax.broadcasted_iota(jnp.int32, (HD, length), 0)
        qx[head, :HD, here] = (recv[head, chunk, 0].astype(f32) * 0.125).astype(low)
        qx[head, HD:, here] = jnp.where(state == meta[chunk, 0:1, :], 1.0, 0.0).astype(low)
        is_open = jnp.where(state == meta[chunk, 1:2, :], 0.0, masked_score)
        kx[head, here, :] = jnp.concatenate(
            [recv[head, chunk, 1].astype(f32), is_open], axis=0
        ).T.astype(low)
        vt[head, :HD, here] = recv[head, chunk, 2]

    def open_plane(head, which):
        scores = dot_nn(pk[head], qx[head, :, rows_of(which, plane)])
        top = jnp.max(scores, axis=0, keepdims=True)
        raised = jnp.exp(scores - top)
        stat[which, head, 0:1, :] = top
        acc[which, head] = dot_nn(pvt[head], raised.astype(low))

    def pair_part(head, upper, lower, first, count, keys, diagonal):
        here = slice(first, first + count)
        queries = qx[head, :, span_of(upper * plane + first, count)]
        key_rows = span_of(lower * plane, keys)
        scores = dot_nn(kx[head, key_rows, :], queries)
        if diagonal:
            key_at = lax.broadcasted_iota(jnp.int32, scores.shape, 0)
            query_at = lax.broadcasted_iota(jnp.int32, scores.shape, 1) + first
            scores = jnp.where(key_at <= query_at, scores, masked_score)
        old_top = stat[upper, head, 0:1, here]
        top = jnp.maximum(old_top, jnp.max(scores, axis=0, keepdims=True))
        raised = jnp.exp(scores - top).astype(low)
        stat[upper, head, 0:1, here] = top
        acc[upper, head, :, here] = acc[upper, head, :, here] * jnp.exp(old_top - top) + dot_nn(
            vt[head, :, key_rows], raised
        )

    def pair(head, upper, lower):
        pair_part(head, upper, lower, 0, plane, plane, False)

    def pair_diagonal(head, which):
        for part in range(2):
            pair_part(head, which, which, part * length, length, (part + 1) * length, True)

    def close_plane(head, which):
        total = acc[which, head, HD : HD + 1, :]
        value = acc[which, head, :HD, :] / total
        acc[which, head, :HD, :] = value
        stat[which, head, 0:1, :] = stat[which, head, 0:1, :] + jnp.log(total)
        for part in range(2):
            chunk = 2 * which + part
            o_send[head, chunk] = value[:, part * length : (part + 1) * length].astype(low)

            @pl.when((chunk != me) & (head == heads - 1))
            def _():
                out_copy(head, chunk, me).start()

            @pl.when(chunk == me)
            def _():
                o_recv[me, head] = o_send[head, chunk]

    def project_memory():
        mem_across(1 - my_side).wait_recv()
        for load in loads[2:]:
            load.wait()
        whole = mem_all[...].reshape(mkey_ref.shape)

        def one(index, carry):
            here = rows_of(index, block)
            mkey_ref[:, here] = dot_nn(whole, wck[:, here]).astype(low)
            mvalue_ref[:, here] = dot_nn(whole, wcv[:, here]).astype(low)
            return carry

        lax.fori_loop(0, blocks, one, 0)

    def stage(index, carry):
        head = index // planes
        step = lax.rem(index, planes)

        @pl.when(head + 1 < heads)
        def _():
            there = plane_after(1 + step)
            for part in range(2):
                peer = 2 * there + part

                @pl.when(peer != me)
                def _():
                    qkv_copy(head, peer, me).wait_send()
                    qkv_copy(head + 1, peer, me).start()

        @pl.when((head == heads - 1) & (head > 0))
        def _():
            there = plane_after(1 + step)
            for part in range(2):
                peer = 2 * there + part

                @pl.when(peer != me)
                def _():
                    qkv_copy(head, peer, me).wait_send()
                    out_copy(head - 1, peer, me).start()

        here = plane_after(step)
        arrive(head, 2 * here)
        arrive(head, 2 * here + 1)
        open_plane(head, here)
        pair_diagonal(head, here)

        def earlier(back, inner):
            there = plane_after(back)
            pair(head, jnp.maximum(here, there), jnp.minimum(here, there))

            @pl.when((step == planes - 1) & (there > here))
            def _():
                close_plane(head, there)

            return inner

        lax.fori_loop(0, step, earlier, 0)
        for hop in range(1, planes - 1):

            @pl.when(index == hop)
            def _():
                mem_arrivals(hop)
                mem_hops(hop, lambda copy: copy.start())

        @pl.when(index == planes - 1)
        def _():
            mem_arrivals(planes - 1)
            mem_across(my_side).start()

        @pl.when((upward & (my_plane + step >= planes)) | (step == planes - 1))
        def _():
            close_plane(head, here)

        @pl.when(jnp.logical_not(upward) & (step == my_plane))
        def _():
            def close(which, inner):
                close_plane(head, which)
                return inner

            lax.fori_loop(0, my_plane + 1, close, 0)

        return carry

    lax.fori_loop(0, heads * planes, stage, 0)

    saves = []

    def save(source, target):
        copy = pltpu.make_async_copy(source, target, out_sem.at[len(saves)])
        copy.start()
        saves.append(copy)

    save(qx, qx_out)
    save(kx, kx_out)
    save(recv, raw_out)
    save(pk, pk_out)
    save(pv, pv_out)
    save(pkt, pkt_out)
    save(acc, ot_out)
    save(stat, lse_out)
    project_memory()
    save(mkey_ref, mkey_out)
    save(mvalue_ref, mvalue_out)
    for other in range(n):

        @pl.when(other != me)
        def _():
            for head in range(heads):
                out_copy(head, other, other).wait_recv()

        att_ref[:, other * group : (other + 1) * group] = (
            o_recv[other].reshape(group, length).astype(f32).T.astype(low)
        )

    def drain(peer):
        meta_copy(peer, me).wait_send()
        if heads == 1:
            qkv_copy(0, peer, me).wait_send()
        for head in range(heads):
            out_copy(head, peer, me).wait_send()

    others(n, me, drain)
    for hop in range(planes - 1):
        mem_hops(hop, lambda copy: copy.wait_send())
    mem_across(my_side).wait_send()
    for copy in saves:
        copy.wait()


def self_forward(n, segments, padding, tokens, weights, prefix, memory, mem_weights):
    length, width = tokens.shape
    group = width // n
    heads = group // HD
    whole = n * length
    planes = n // 2
    low = jnp.bfloat16
    f32 = jnp.float32
    vmem = pl.BlockSpec(memory_space=pltpu.VMEM)
    anywhere = pl.BlockSpec(memory_space=pl.ANY)
    dma = pltpu.SemaphoreType.DMA
    shapes = (
        ((heads, 2 * HD, whole), low),
        ((heads, whole, 2 * HD), low),
        ((heads, n, 3, HD, length), low),
        ((heads, PREFIX_ROWS, 2 * HD), low),
        ((heads, PREFIX_ROWS, HD), low),
        ((heads, HD, PREFIX_ROWS), low),
        ((planes, heads, HD + SUM_ROWS, 2 * length), f32),
        ((planes, heads, 8, 2 * length), f32),
    )
    square = pltpu.VMEM((width, width), low)
    qx, kx, raw, pk, pv, pkt, acc, stat = (pltpu.VMEM(*shape) for shape in shapes)
    return pl.pallas_call(
        functools.partial(self_forward_kernel, n),
        out_shape=(
            jax.ShapeDtypeStruct((length, width), low),
            jax.ShapeDtypeStruct((n * memory.shape[0], width), low),
            jax.ShapeDtypeStruct((n * memory.shape[0], width), low),
        )
        + tuple(jax.ShapeDtypeStruct(*shape) for shape in shapes),
        in_specs=[vmem] * 3
        + [anywhere] * 3
        + [vmem, anywhere, vmem, anywhere, vmem, vmem]
        + [anywhere] * 2,
        out_specs=(vmem,) + (anywhere,) * 10,
        scratch_shapes=[
            pltpu.VMEM((n, heads, 3, HD, length), low),
            raw,
            pltpu.VMEM((8, length), jnp.int32),
            pltpu.VMEM((n, 8, length), jnp.int32),
            kx,
            qx,
            pltpu.VMEM((heads, HD + SUM_ROWS, whole), low),
            pltpu.VMEM((PREFIX_ROWS, weights[0].shape[0] // 2), f32),
            pk,
            pv,
            pkt,
            pltpu.VMEM((heads, HD + SUM_ROWS, PREFIX_ROWS), low),
            stat,
            acc,
            pltpu.VMEM((heads, n, HD, length), low),
            pltpu.VMEM((n, heads, HD, length), low),
            pltpu.VMEM((planes, 2) + memory.shape, low),
            square,
            square,
            pltpu.VMEM((n * memory.shape[0], width), low),
            pltpu.VMEM((n * memory.shape[0], width), low),
            square,
            square,
            square,
            pltpu.VMEM(prefix[1].shape, low),
            pltpu.VMEM(prefix[3].shape, low),
            dma((heads, n)),
            dma((heads, n)),
            dma((n,)),
            dma((n,)),
            dma((heads, n)),
            dma((heads, n)),
            dma((2, planes + 1)),
            dma((planes + 1,)),
            dma((10,)),
            dma((width // (2 * LANES), 3)),
            dma((4,)),
        ],
        compiler_params=pltpu.CompilerParams(
            collective_id=0, has_side_effects=True, vmem_limit_bytes=VMEM_BYTES
        ),
        name="self_forward",
    )(segments, padding, tokens, *weights, *prefix, memory, *mem_weights)


def both_parts(value):
    high = value.astype(jnp.bfloat16).astype(jnp.float32)
    return jnp.concatenate([high, value - high], axis=0).astype(jnp.bfloat16)


def self_backward_kernel(
    n,
    batches,
    base_in,
    do_in,
    sums_in,
    mkey_in,
    mvalue_in,
    wck_in,
    wcv_in,
    vecs_in,
    qx_in,
    kx_in,
    raw_in,
    pk_in,
    pv_in,
    pkt_in,
    ot_in,
    lse_in,
    wq_in,
    wk_in,
    wv_in,
    first_in,
    second_in,
    emb_ref,
    fbias_ref,
    tg_ref,
    mgrad_ref,
    pkv_ref,
    hidden_ref,
    hgrad_ref,
    embed_ref,
    vecs_ref,
    full_out,
    do_recv,
    qx,
    kx,
    raw,
    kt,
    values,
    dot,
    qdo,
    pk,
    pv,
    pkt,
    ot,
    stat,
    weights,
    dqt,
    dkv,
    g_send,
    g_recv,
    pre_ref,
    pre_all,
    pre_sum,
    pre_recv,
    sums_mine,
    sums_core,
    sums_x,
    sums_side,
    sums_z,
    full,
    mkey,
    mvalue,
    wck,
    wcv,
    mem_part,
    mem_side,
    mem_up,
    mem_down,
    vec_all,
    vec_sum,
    vec_y,
    vec_both,
    vec_z,
    product,
    first,
    second,
    base_ref,
    do_send_sem,
    do_recv_sem,
    g_send_sem,
    g_recv_sem,
    in_sem,
    send_sem,
    recv_sem,
):
    low = jnp.bfloat16
    f32 = jnp.float32
    me = lax.axis_index("seq")
    length, width = tg_ref.shape
    group = width // n
    heads = group // HD
    plane = 2 * length
    planes = n // 2
    step_rows = 256
    my_batch = lax.axis_index("batch")
    my_core = lax.rem(my_batch, 2)
    my_high = my_batch // 2
    highs = batches // 2
    my_plane = me // 2
    my_side = lax.rem(me, 2)
    beside = me + 1 - 2 * my_side
    used = [0]

    def numbers(count):
        used[0] += count
        return used[0] - count

    core_slot = numbers(2)
    x_slot = numbers(2 * highs)
    y_slot = numbers(3)
    z_slot = numbers(2 * planes)
    up_slot = numbers(planes)
    down_slot = numbers(planes)
    va_slot = numbers(batches)
    vb_slot = numbers(1)
    vc_slot = numbers(planes)
    pa_slot = numbers(batches)
    pb_slot = numbers(n)

    def send(source, target, first, peer_index, slot_index, axis, peer):
        return remote(
            source,
            target,
            send_sem.at[first + peer_index],
            recv_sem.at[first + slot_index],
            axis,
            peer,
        )

    half_rows = 2 * planes * highs * sums_z.shape[1]
    x_rows = half_rows // highs
    y_rows = x_rows // 2
    z_rows = y_rows // planes
    x_row = pl.multiple_of(my_high * x_rows, x_rows)
    y_row = pl.multiple_of(x_row + my_side * y_rows, y_rows)

    def part(row, count):
        return sums_mine.at[pl.ds(pl.multiple_of(row, count), count)]

    def reduce_core():
        return send(
            sums_in.at[1 - my_core], sums_core, core_slot, 0, 0, "batch", my_batch + 1 - 2 * my_core
        )

    def reduce_x(peer, slot):
        return send(
            part(peer * x_rows, x_rows),
            sums_x.at[slot],
            x_slot,
            peer,
            slot,
            "batch",
            2 * peer + my_core,
        )

    def reduce_y():
        return send(
            part(x_row + (1 - my_side) * y_rows, y_rows), sums_side, y_slot, 0, 0, "seq", beside
        )

    def reduce_z(peer, slot):
        return send(
            part(y_row + peer * z_rows, z_rows),
            sums_z.at[slot],
            z_slot,
            peer,
            slot,
            "seq",
            2 * peer + my_side,
        )

    def gather_z(peer, slot):
        piece = full.at[my_core, my_high, my_side, slot]
        return send(piece, piece, z_slot + planes, peer, slot, "seq", 2 * peer + my_side)

    def gather_y(side):
        piece = full.at[my_core, my_high, side]
        return send(piece, piece, y_slot + 1, 0, 0, "seq", beside)

    def gather_x(peer, slot):
        piece = full.at[my_core, slot]
        return send(piece, piece, x_slot + highs, peer, slot, "batch", 2 * peer + my_core)

    def gather_core(core):
        piece = full.at[core]
        return send(piece, piece, core_slot + 1, 0, 0, "batch", my_batch + 1 - 2 * my_core)

    def mem_across():
        return send(
            mem_part.at[:, 1 - my_side], mem_side, y_slot + 2, 0, 0, "seq", beside
        )

    def mem_hop(target, toward, peer=None):
        buffer, slot = (mem_up, up_slot) if toward > 0 else (mem_down, down_slot)
        return send(
            mem_part.at[target, my_side],
            buffer.at[target],
            slot,
            target,
            target,
            "seq",
            me + 2 * toward if peer is None else peer,
        )

    def mem_from(target, toward):
        return mem_hop(target, toward, me - 2 * toward)

    def mem_pass(toward):
        buffer = mem_up if toward > 0 else mem_down
        first = 0 if toward > 0 else planes - 1
        for target in range(planes):

            @pl.when((target - my_plane) * toward > 0)
            def _():
                @pl.when(my_plane != first)
                def _():
                    mem_from(target, toward).wait_recv()
                    mem_part[target, my_side] = (
                        mem_part[target, my_side].astype(f32) + buffer[target].astype(f32)
                    ).astype(low)

                mem_hop(target, toward).start()

    def mem_stage(at):
        pl.when(my_plane == at)(lambda: mem_pass(1))
        pl.when(my_plane == planes - 1 - at)(lambda: mem_pass(-1))

    def mem_end():
        value = mem_part[my_plane, my_side].astype(f32)
        mgrad_ref[...] = value.astype(low)

        @pl.when(my_plane > 0)
        def _():
            mem_from(my_plane, 1).wait_recv()
            mgrad_ref[...] = (mgrad_ref[...].astype(f32) + mem_up[my_plane].astype(f32)).astype(low)

        @pl.when(my_plane < planes - 1)
        def _():
            mem_from(my_plane, -1).wait_recv()
            mgrad_ref[...] = (
                mgrad_ref[...].astype(f32) + mem_down[my_plane].astype(f32)
            ).astype(low)

    def mem_drain():
        for target in range(planes):

            @pl.when(target > my_plane)
            def _():
                mem_hop(target, 1).wait_send()

            @pl.when(target < my_plane)
            def _():
                mem_hop(target, -1).wait_send()

    def vec_a(peer, slot):
        return send(vecs_in, vec_all.at[slot], va_slot, peer, slot, "batch", peer)

    def vec_b(side):
        return send(vec_sum, vec_y.at[side], vb_slot, 0, 0, "seq", beside)

    def vec_c(peer, slot):
        return send(vec_both, vec_z.at[slot], vc_slot, peer, slot, "seq", 2 * peer + my_side)

    def pre_a(peer, slot):
        return send(pre_ref, pre_all.at[slot], pa_slot, peer, slot, "batch", peer)

    def pre_b(peer, slot):
        return send(pre_sum, pre_recv.at[slot], pb_slot, peer, slot, "seq", peer)

    def do_copy(head, peer, slot):
        return remote(
            do_in.at[peer, head],
            do_recv.at[head, slot],
            do_send_sem.at[head, peer],
            do_recv_sem.at[head, slot],
            "seq",
            peer,
        )

    def q_copy(head, peer, slot):
        return remote(
            g_send.at[peer, head, 0],
            g_recv.at[0, slot, head],
            g_send_sem.at[0, head, peer],
            g_recv_sem.at[0, head, slot],
            "seq",
            peer,
        )

    def kv_copy(head, peer, slot):
        return remote(
            g_send.at[peer, head, pl.ds(1, 2)],
            g_recv.at[pl.ds(1, 2), slot, head],
            g_send_sem.at[1, head, peer],
            g_recv_sem.at[1, head, slot],
            "seq",
            peer,
        )

    def far_first(body):
        for index in range(n):
            peer = jnp.where(my_plane < planes // 2, n - 1 - index, index)

            @pl.when(peer != me)
            def _():
                body(peer)

    def added(ref, size):
        value = ref[0].astype(f32)
        for other in range(1, size):
            value = value + ref[other].astype(f32)
        return value

    loads = [
        pltpu.make_async_copy(source, target, in_sem.at[index])
        for index, (source, target) in enumerate(
            (
                (raw_in, raw),
                (kx_in, kx),
                (pk_in, pk),
                (pv_in, pv),
                (pkt_in, pkt),
                (qx_in, qx),
                (ot_in, ot),
                (lse_in, stat),
                (sums_in.at[my_core], sums_mine),
                (vecs_in, vec_all.at[my_batch]),
                (mkey_in, mkey),
                (mvalue_in, mvalue),
                (wck_in, wck),
                (wcv_in, wcv),
                (base_in, base_ref),
                (wq_in, weights.at[0]),
                (wk_in, weights.at[1]),
                (wv_in, weights.at[2]),
                (first_in, first),
                (second_in, second),
            )
        )
    ]
    own_do = pltpu.make_async_copy(do_in.at[me], do_recv.at[:, me], in_sem.at[len(loads)])
    own_do.start()
    for load in loads:
        load.start()
    enter({"seq": n, "batch": batches})
    far_first(lambda peer: do_copy(0, peer, me).start())
    reduce_core().start()
    others(batches, my_batch, lambda peer: vec_a(peer, my_batch).start())
    dkv[...] = jnp.zeros_like(dkv)
    product[...] = jnp.zeros_like(product)
    pre_ref[...] = jnp.zeros_like(pre_ref)
    for load in loads[:14]:
        load.wait()
    own_do.wait()

    def turn(index, carry):
        head = index // n
        chunk = lax.rem(index, n)
        here = rows_of(chunk, length)
        kt[head, :, here] = raw[head, chunk, 1]
        values[head, here, :] = raw[head, chunk, 2].astype(f32).T.astype(low)
        return carry

    lax.fori_loop(0, heads * n, turn, 0)

    def memory_back(index, carry):
        here = rows_of(index, step_rows)
        value = dot_nt(mkey[...], wck[here, :]) + dot_nt(mvalue[...], wcv[here, :])
        mem_part[:, :, :, here] = value.astype(low).reshape(mem_part.shape[:3] + (step_rows,))
        return carry

    lax.fori_loop(0, width // step_rows, memory_back, 0)
    mem_across().start()

    def next_head(head):
        def move(peer):
            do_copy(head, peer, me).wait_send()
            do_copy(head + 1, peer, me).start()

        far_first(move)

    def arrive(head, which):
        for part in range(2):
            chunk = 2 * which + part

            @pl.when(chunk != me)
            def _():
                do_copy(head, chunk, chunk).wait_recv()

            grads = do_recv[head, chunk]
            dot[head, :, rows_of(chunk, length)] = grads
            grads = grads.astype(f32)
            query = raw[head, chunk, 0].astype(f32) * 0.125
            qdo[head, rows_of(chunk, length), :] = (
                jnp.concatenate([query, grads], axis=0).T.astype(low)
            )
            here = slice(part * length, (part + 1) * length)
            stat[which, head, 1:2, here] = jnp.sum(
                grads * ot[which, head, :HD, here], axis=0, keepdims=True
            )
        here = rows_of(which, plane)
        weight = jnp.exp(dot_nn(pk[head], qx[head, :, here]) - stat[which, head, 0:1, :])
        slope = weight * (dot_nn(pv[head], dot[head, :, here]) - stat[which, head, 1:2, :])
        both = jnp.concatenate([slope, weight], axis=0).astype(low)
        sums = dot_nn(both, qdo[head, here, :])
        pre_ref[head] += jnp.where(
            head_lanes((PREFIX_ROWS, 2 * HD), 0), sums[:PREFIX_ROWS], sums[PREFIX_ROWS:]
        )
        slope = slope.astype(low)
        dqt[which, head] = dot_nn(pkt[head], slope)

    def plus(first, second):
        return (first.astype(f32) + second.astype(f32)).astype(low)

    def sum_one():
        reduce_core().wait_recv()
        sums_mine[...] = plus(sums_mine[...], sums_core[...])
        others(highs, my_high, lambda peer: reduce_x(peer, my_high).start())

    def sum_two():
        here = pl.ds(x_row, x_rows)
        others(highs, my_high, lambda peer: reduce_x(peer, peer).wait_recv())
        sums_x[my_high] = sums_mine[here]
        sums_mine[here] = added(sums_x, highs).astype(low)
        reduce_y().start()

    def sum_three():
        here = pl.ds(y_row, y_rows)
        reduce_y().wait_recv()
        sums_mine[here] = plus(sums_mine[here], sums_side[...])
        others(planes, my_plane, lambda peer: reduce_z(peer, my_plane).start())

    def sum_four():
        here = pl.ds(pl.multiple_of(y_row + my_plane * z_rows, z_rows), z_rows)
        others(planes, my_plane, lambda peer: reduce_z(peer, peer).wait_recv())
        sums_z[my_plane] = sums_mine[here]
        full[my_core, my_high, my_side, my_plane] = added(sums_z, planes).astype(low)
        others(planes, my_plane, lambda peer: gather_z(peer, my_plane).start())

    def sum_five():
        others(planes, my_plane, lambda peer: gather_z(peer, peer).wait_recv())
        gather_y(my_side).start()

    def sum_six():
        gather_y(1 - my_side).wait_recv()
        others(highs, my_high, lambda peer: gather_x(peer, my_high).start())

    def sum_seven():
        others(highs, my_high, lambda peer: gather_x(peer, peer).wait_recv())
        gather_core(my_core).start()

    def sum_end():
        gather_core(1 - my_core).wait_recv()
        save_full.start()

    def vec_one():
        others(batches, my_batch, lambda peer: vec_a(peer, peer).wait_recv())
        vec_sum[...] = added(vec_all, batches)
        vec_b(my_side).start()
        vec_y[my_side] = vec_sum[...]

    def vec_two():
        vec_b(1 - my_side).wait_recv()
        value = (vec_y[0] + vec_y[1]).astype(f32)
        vec_both[...] = jnp.concatenate(
            [value[:, : width // 2], value[:, width // 2 :]], axis=0
        ).astype(low)
        others(planes, my_plane, lambda peer: vec_c(peer, my_plane).start())
        vec_z[my_plane] = vec_both[...]

    def vec_end():
        others(planes, my_plane, lambda peer: vec_c(peer, peer).wait_recv())
        value = added(vec_z, planes)
        vecs_ref[:, : width // 2] = value[:8]
        vecs_ref[:, width // 2 :] = value[8:]

    def mem_one():
        mem_across().wait_recv()
        mem_part[:, my_side] = plus(mem_part[:, my_side], mem_side[...])

    def stage_pa():
        others(batches, my_batch, lambda peer: pre_a(peer, my_batch).start())
        pre_all[my_batch] = pre_ref[...]

    def stage_pb():
        others(batches, my_batch, lambda peer: pre_a(peer, peer).wait_recv())
        pre_sum[...] = added(pre_all, batches).astype(low)
        others(n, me, lambda peer: pre_b(peer, me).start())
        pre_recv[me] = pre_sum[...]

    save_full = pltpu.make_async_copy(full, full_out, in_sem.at[0])

    def pair_part(head, upper, lower, first, count, diagonal, at=None):
        keys = span_of(lower * plane + (first if at is None else at * count), count)
        here = span_of(upper * plane + first, plane - first)
        at = slice(first, plane)
        scores = dot_nn(kx[head, keys, :], qx[head, :, here])
        slope = dot_nn(values[head, keys, :], dot[head, :, here]) - stat[upper, head, 1:2, at]
        weight = jnp.exp(scores - stat[upper, head, 0:1, at])
        if diagonal:
            key_at = lax.broadcasted_iota(jnp.int32, scores.shape, 0)
            query_at = lax.broadcasted_iota(jnp.int32, scores.shape, 1)
            weight = jnp.where(key_at <= query_at, weight, 0.0)
        slope = (weight * slope).astype(low)
        key_part = dot_nn(slope, qdo[head, here, :])
        value_part = dot_nn(weight.astype(low), qdo[head, here, :])
        dkv[head, keys, :] += jnp.where(head_lanes((count, 2 * HD), 0), key_part, value_part)
        dqt[upper, head, :, at] += dot_nn(kt[head, :, keys], slope)

    def pair(head, upper, lower, diagonal):
        if diagonal:
            for part in range(plane // step_rows):
                pair_part(head, upper, lower, part * step_rows, step_rows, True)
        else:

            def one(at, carry):
                pair_part(head, upper, lower, 0, step_rows, False, at)
                return carry

            lax.fori_loop(0, plane // step_rows, one, 0)

    def hand_queries(head, which):
        for part in range(2):
            chunk = 2 * which + part
            g_send[chunk, head, 0] = (
                dqt[which, head, :, part * length : (part + 1) * length] * 0.125
            ).astype(low)

            @pl.when(chunk != me)
            def _():
                q_copy(head, chunk, me).start()

            @pl.when(chunk == me)
            def _():
                g_recv[0, me, head] = g_send[chunk, head, 0]

    def hand_keys(head, which):
        for part in range(2):
            chunk = 2 * which + part
            turned = dkv[head, rows_of(chunk, length), :].T.astype(low)
            g_send[chunk, head, 1] = turned[:HD]
            g_send[chunk, head, 2] = turned[HD:]

            @pl.when(chunk != me)
            def _():
                kv_copy(head, chunk, me).start()

            @pl.when(chunk == me)
            def _():
                g_recv[pl.ds(1, 2), me, head] = g_send[chunk, head, pl.ds(1, 2)]

    rising = my_plane >= planes // 2
    total = heads * planes * (planes + 1) // 2
    hooks = [
        (2, sum_one),
        (3, mem_one),
        (4, lambda: mem_stage(0)),
        (5, vec_one),
        (5, sum_two),
        (7, sum_three),
        (8, vec_two),
        (10, sum_four),
        (12, sum_five),
        (14, sum_six),
        (16, vec_end),
        (17, sum_seven),
    ] + [(4 + 3 * at, functools.partial(mem_stage, at)) for at in range(1, planes - 1)]
    hooks += [
        (1 + head * total // heads, functools.partial(next_head, head)) for head in range(heads - 1)
    ]
    final = total - planes * (planes + 1) // 2
    hooks += [(final + planes + 1, stage_pa), (final + 2 * planes - 1, stage_pb)]

    def hook(pairs):
        for number, body in sorted(hooks, key=lambda item: item[0]):
            pl.when(pairs == number)(body)


    def stage(index, carry):
        head = index // planes
        step = lax.rem(index, planes)
        here = jnp.where(rising, step, planes - 1 - step)

        @pl.when((step == 0) | ((step == 1) & jnp.logical_not(rising)))
        def _():
            @pl.when(rising | (step == 0))
            def _():
                arrive(head, here)

            @pl.when(jnp.logical_not(rising) & (step == 1))
            def _():
                def rest(which, inner):
                    arrive(head, planes - 2 - which)
                    return inner

                lax.fori_loop(0, planes - 1, rest, 0)

        begun = head * (planes * (planes + 1) // 2) + step * planes - step * (step - 1) // 2
        hook(begun)
        pair(head, here, here, True)

        @pl.when(rising)
        def _():
            hand_queries(head, here)

        @pl.when(jnp.logical_not(rising))
        def _():
            hand_keys(head, here)

        def far(at, inner):
            there = jnp.where(rising, here + 1 + at, here - 1 - at)

            @pl.when(rising & (step == 0))
            def _():
                arrive(head, there)

            hook(begun + 1 + at)
            pair(head, jnp.maximum(here, there), jnp.minimum(here, there), False)
            return inner

        lax.fori_loop(0, planes - 1 - step, far, 0)

        @pl.when(rising)
        def _():
            hand_keys(head, here)

        @pl.when(jnp.logical_not(rising))
        def _():
            hand_queries(head, here)

        return carry

    lax.fori_loop(0, heads * planes, stage, 0)
    mem_end()
    for load in loads[14:]:
        load.wait()

    def gathered(peer):
        for head in range(heads):
            q_copy(head, peer, peer).wait_recv()
            kv_copy(head, peer, peer).wait_recv()

    half = width // 2

    def gather_plane(step, carry):
        which = lax.rem(my_plane + step, planes)
        for part in range(2):
            peer = 2 * which + part

            @pl.when(peer != me)
            def _():
                gathered(peer)

        columns = rows_of(which, 2 * group)
        for part in range(2):
            here = slice(part * half, (part + 1) * half)
            value = product[here, :]
            for kind in range(3):
                grads = g_recv[kind, pl.ds(2 * which, 2)].reshape(2 * group, length)
                value = value + dot_nn(weights[kind, here, columns], grads)
            product[here, :] = value
        return carry

    lax.fori_loop(0, planes - 1, gather_plane, 0)
    for other in range(n):

        @pl.when(other != me)
        def _():
            pre_b(other, other).wait_recv()

        value = pre_recv[other].astype(f32)
        for which in range(2):
            pkv_ref[:, which * width + other * group : which * width + (other + 1) * group] = (
                jnp.concatenate(
                    [value[head, :, which * HD : (which + 1) * HD] for head in range(heads)], axis=1
                )
            )

    count = emb_ref.shape[0]
    hidden_ref[...] = jnp.zeros_like(hidden_ref)
    hidden_ref[:count, :] = jnp.tanh(dot_nn(emb_ref[...], first[...]) + fbias_ref[...])
    value = hidden_ref[...]
    grad = dot_nt(both_parts(pkv_ref[...]), second[...])
    grad = (grad[:PREFIX_ROWS] + grad[PREFIX_ROWS:]) * (1.0 - value * value)
    hgrad_ref[...] = grad
    back = dot_nt(both_parts(grad), first[...])
    embed_ref[...] = back[:PREFIX_ROWS] + back[PREFIX_ROWS:]
    gather_plane(planes - 1, 0)
    sum_end()
    tile = 256
    for index in range(width // tile):
        here = slice(index * tile, (index + 1) * tile)
        tg_ref[:, here] = (base_ref[:, here] + product[here, :].T).astype(low)
    def drain(peer):
        do_copy(heads - 1, peer, me).wait_send()
        pre_b(peer, me).wait_send()
        for head in range(heads):
            q_copy(head, peer, me).wait_send()
            kv_copy(head, peer, me).wait_send()

    others(n, me, drain)
    others(batches, my_batch, lambda peer: pre_a(peer, my_batch).wait_send())
    others(batches, my_batch, lambda peer: vec_a(peer, my_batch).wait_send())
    reduce_core().wait_send()
    others(highs, my_high, lambda peer: reduce_x(peer, my_high).wait_send())
    reduce_y().wait_send()
    others(planes, my_plane, lambda peer: reduce_z(peer, my_plane).wait_send())
    others(planes, my_plane, lambda peer: gather_z(peer, my_plane).wait_send())
    gather_y(my_side).wait_send()
    others(highs, my_high, lambda peer: gather_x(peer, my_high).wait_send())
    gather_core(my_core).wait_send()
    mem_across().wait_send()
    mem_drain()
    others(planes, my_plane, lambda peer: vec_c(peer, my_plane).wait_send())
    vec_b(my_side).wait_send()
    save_full.wait()


def self_backward(
    n, batches, first_grad, out_grad, sums, mem_grads, mem_weights, vecs, saved, weights, prefix
):
    length, width = first_grad.shape
    group = width // n
    heads = group // HD
    whole = n * length
    planes = n // 2
    low = jnp.bfloat16
    f32 = jnp.float32
    vmem = pl.BlockSpec(memory_space=pltpu.VMEM)
    anywhere = pl.BlockSpec(memory_space=pl.ANY)
    dma = pltpu.SemaphoreType.DMA
    sum_rows = sums.shape[0] // (n * batches)
    mem_len = mem_grads[0].shape[0]
    mem_rows = mem_len // n
    mem_part = pltpu.VMEM((planes, mem_rows, width), low)
    mem_low = pltpu.VMEM((mem_len, width), low)
    square = pltpu.VMEM((width, width), low)
    vec = pltpu.VMEM((8, width), f32)
    copies = 6 + 2 * (batches // 2) + 5 * planes + 2 * batches + n
    qx, kx, raw, pk, pv, pkt, ot, stat = (pltpu.VMEM(value.shape, value.dtype) for value in saved)
    return pl.pallas_call(
        functools.partial(self_backward_kernel, n, batches),
        out_shape=(
            jax.ShapeDtypeStruct((length, width), low),
            jax.ShapeDtypeStruct((mem_rows, width), low),
            jax.ShapeDtypeStruct((PREFIX_ROWS, 2 * width), f32),
            jax.ShapeDtypeStruct((PREFIX_ROWS, prefix[0].shape[1]), f32),
            jax.ShapeDtypeStruct((PREFIX_ROWS, prefix[0].shape[1]), f32),
            jax.ShapeDtypeStruct((PREFIX_ROWS, width), f32),
            jax.ShapeDtypeStruct((8, width), f32),
            jax.ShapeDtypeStruct((2, batches // 2, 2, planes, sum_rows, LANES), low),
        ),
        in_specs=[anywhere] * 21 + [vmem] * 2,
        out_specs=(vmem,) * 7 + (anywhere,),
        scratch_shapes=[
            pltpu.VMEM((heads, n, HD, length), low),
            qx,
            kx,
            raw,
            pltpu.VMEM((heads, HD, whole), low),
            pltpu.VMEM((heads, whole, HD), low),
            pltpu.VMEM((heads, HD, whole), low),
            pltpu.VMEM((heads, whole, 2 * HD), low),
            pk,
            pv,
            pkt,
            ot,
            stat,
            pltpu.VMEM((3, width, width), low),
            pltpu.VMEM((planes, heads, HD, 2 * length), f32),
            pltpu.VMEM((heads, whole, 2 * HD), f32),
            pltpu.VMEM((n, heads, 3, HD, length), low),
            pltpu.VMEM((3, n, heads, HD, length), low),
            pltpu.VMEM((heads, PREFIX_ROWS, 2 * HD), f32),
            pltpu.VMEM((batches, heads, PREFIX_ROWS, 2 * HD), f32),
            pltpu.VMEM((heads, PREFIX_ROWS, 2 * HD), low),
            pltpu.VMEM((n, heads, PREFIX_ROWS, 2 * HD), low),
            pltpu.VMEM((sums.shape[0] // 2, LANES), low),
            pltpu.VMEM((sums.shape[0] // 2, LANES), low),
            pltpu.VMEM((batches // 2, sums.shape[0] // batches, LANES), low),
            pltpu.VMEM((planes * sum_rows, LANES), low),
            pltpu.VMEM((planes, sum_rows, LANES), low),
            pltpu.VMEM((2, batches // 2, 2, planes, sum_rows, LANES), low),
            mem_low,
            mem_low,
            square,
            square,
            pltpu.VMEM((planes, 2, mem_rows, width), low),
            mem_part,
            mem_part,
            mem_part,
            pltpu.VMEM((batches, 8, width), f32),
            vec,
            pltpu.VMEM((2, 8, width), f32),
            pltpu.VMEM((16, width // 2), low),
            pltpu.VMEM((planes, 16, width // 2), low),
            pltpu.VMEM((width, length), f32),
            pltpu.VMEM(prefix[0].shape, low),
            pltpu.VMEM(prefix[1].shape, low),
            pltpu.VMEM((length, width), f32),
            dma((heads, n)),
            dma((heads, n)),
            dma((2, heads, n)),
            dma((2, heads, n)),
            dma((21,)),
            dma((copies,)),
            dma((copies,)),
        ],
        compiler_params=pltpu.CompilerParams(
            collective_id=1, has_side_effects=True, vmem_limit_bytes=VMEM_BYTES
        ),
        name="self_backward",
    )(
        first_grad,
        out_grad,
        sums.reshape(2, -1, LANES),
        *mem_grads,
        *mem_weights,
        vecs,
        *saved,
        *weights,
        *prefix,
    )


def finish_kernel(
    full_in,
    vecs_ref,
    pkv_ref,
    hidden_ref,
    hgrad_ref,
    embed_ref,
    emb_ref,
    token_in,
    mem_in,
    embed_out,
    first_out,
    fbias_out,
    second_out,
    sbias_out,
    down_out,
    dbias_out,
    raise_out,
    rbias_out,
    gain_out,
    shift_out,
    token_out,
    mem_out,
    full_ref,
    token_ref,
    mem_ref,
    first_grad,
    second_grad,
    down_grad,
    raise_grad,
    emb,
    out_sem,
    in_sem,
):
    f32 = jnp.float32
    low = jnp.bfloat16
    width = emb_ref.shape[1]
    down = dbias_out.shape[1]
    count = emb_ref.shape[0]
    first = down * width // LANES
    loads = [
        pltpu.make_async_copy(source, target, in_sem.at[index])
        for index, (source, target) in enumerate(
            (
                (full_in.at[first:], full_ref.at[first:]),
                (full_in.at[:first], full_ref.at[:first]),
                (token_in, token_ref),
                (mem_in, mem_ref),
            )
        )
    ]
    for load in loads:
        load.start()
    saves = []

    def save(source, target, rows=None):
        if rows is not None:
            source, target = source.at[rows], target.at[rows]
        copy = pltpu.make_async_copy(source, target, out_sem.at[len(saves)])
        copy.start()
        saves.append(copy)

    loads[0].wait()
    for index in range(width // LANES):
        raise_grad[:, index * LANES : (index + 1) * LANES] = full_ref[
            first + index * down : first + (index + 1) * down, :
        ].astype(f32)
    save(raise_grad, raise_out)
    loads[1].wait()
    for index in range(down // LANES):
        down_grad[:, index * LANES : (index + 1) * LANES] = full_ref[
            index * width : (index + 1) * width, :
        ].astype(f32)
    save(down_grad, down_out)
    for load in loads[2:]:
        load.wait()
    save(token_ref, token_out)
    save(mem_ref, mem_out)
    emb[...] = jnp.zeros_like(emb)
    emb[:count, :] = emb_ref[...].astype(f32)
    value = hidden_ref[...]
    prefix = pkv_ref[...]
    parts = both_parts(prefix)
    hidden_twice = jnp.concatenate([value, value], axis=0).T.astype(low)
    tile = 128
    for index in range(second_grad.shape[0] // tile):
        here = slice(index * tile, (index + 1) * tile)
        second_grad[here, :] = dot_nn(hidden_twice[here, :], parts)
        save(second_grad, second_out, here)
    sbias_out[...] = jnp.sum(prefix, axis=0, keepdims=True)
    grad = hgrad_ref[...]
    fbias_out[...] = jnp.sum(grad, axis=0, keepdims=True)
    parts = both_parts(grad)
    emb_twice = jnp.concatenate([emb[...], emb[...]], axis=0).T.astype(low)
    first_grad[...] = dot_nn(emb_twice, parts)
    save(first_grad, first_out)
    embed_out[...] = embed_ref[:count, :]
    rbias_out[...] = vecs_ref[0:1, :]
    dbias_out[...] = vecs_ref[1:2, :down]
    gain_out[...] = vecs_ref[2:5, :]
    shift_out[...] = vecs_ref[5:8, :]
    for copy in saves:
        copy.wait()


def finish(full, vecs, prefix_sums, embed, down, token_grad, memory_grad):
    f32 = jnp.float32
    count, width = embed.shape
    hidden = prefix_sums[1].shape[1]
    vmem = pl.BlockSpec(memory_space=pltpu.VMEM)
    anywhere = pl.BlockSpec(memory_space=pl.ANY)
    shapes = (
        (count, width),
        (width, hidden),
        (1, hidden),
        (hidden, 2 * width),
        (1, 2 * width),
        (width, down),
        (1, down),
        (down, width),
        (1, width),
        (3, width),
        (3, width),
    )
    return pl.pallas_call(
        finish_kernel,
        out_shape=tuple(jax.ShapeDtypeStruct(shape, f32) for shape in shapes)
        + tuple(
            jax.ShapeDtypeStruct(value.shape, value.dtype) for value in (token_grad, memory_grad)
        ),
        in_specs=[anywhere] + [vmem] * 6 + [anywhere] * 2,
        out_specs=(
            vmem,
            anywhere,
            vmem,
            anywhere,
            vmem,
            anywhere,
            vmem,
            anywhere,
            vmem,
            vmem,
            vmem,
            anywhere,
            anywhere,
        ),
        scratch_shapes=[
            pltpu.VMEM(full.shape, jnp.bfloat16),
            pltpu.VMEM(token_grad.shape, token_grad.dtype),
            pltpu.VMEM(memory_grad.shape, memory_grad.dtype),
            pltpu.VMEM((width, hidden), f32),
            pltpu.VMEM((hidden, 2 * width), f32),
            pltpu.VMEM((width, down), f32),
            pltpu.VMEM((down, width), f32),
            pltpu.VMEM((PREFIX_ROWS, width), f32),
            pltpu.SemaphoreType.DMA((5 + hidden // 128,)),
            pltpu.SemaphoreType.DMA((4,)),
        ],
        compiler_params=pltpu.CompilerParams(vmem_limit_bytes=VMEM_BYTES),
        name="finish",
    )(full, vecs, *prefix_sums, embed, token_grad, memory_grad)


def gelu_pair(value):
    size = jnp.abs(value)
    step = 1.0 / (1.0 + (0.3275911 * 0.7071067811865476) * size)
    bell = jnp.exp(-0.5 * value * value)
    poly = step * (
        0.127414796
        + step
        * (-0.142248368 + step * (0.7107068705 + step * (-0.7265760135 + step * 0.5307027145)))
    )
    act = jnp.maximum(value, 0.0) - size * (poly * bell)
    turn = bell * (0.3989422804014327 * size - poly)
    return act, jnp.where(value >= 0.0, 1.0 + turn, -turn)


def normed(value):
    center = jnp.mean(value, axis=-1, keepdims=True)
    centered = value - center
    scale = lax.rsqrt(jnp.mean(centered * centered, axis=-1, keepdims=True) + norm_eps)
    return centered * scale, scale


def norm_back(grad, scale, unit):
    return scale * (
        grad
        - jnp.mean(grad, axis=-1, keepdims=True)
        - unit * jnp.mean(grad * unit, axis=-1, keepdims=True)
    )


def middle_kernel(
    tok_in,
    att_in,
    cot_in,
    mkey_in,
    mvalue_in,
    gain_ref,
    shift_ref,
    dbias_ref,
    rbias_ref,
    wo_in,
    wcq_in,
    wco_in,
    wd_in,
    wr_in,
    win_in,
    wout_in,
    layer_out,
    fgrad_out,
    ograd_out,
    mkey_out,
    mvalue_out,
    sums_out,
    vecs_ref,
    tok_ref,
    att_ref,
    cot_ref,
    mkey_ref,
    mvalue_ref,
    out_ref,
    fgrad_ref,
    ograd_ref,
    sums_ref,
    wo,
    wcq,
    wco,
    wd,
    wr,
    win,
    wout,
    unit_one,
    unit_two,
    work,
    total,
    scale_one,
    scale_two,
    low_one,
    low_two,
    low_three,
    query,
    crossed,
    weights,
    slopes,
    acts,
    down_act,
    down_slope,
    down_grad,
    load_sem,
    win_sem,
    wout_sem,
    out_sem,
):
    length, width = tok_ref.shape
    resident = len(win.shape) == 2
    tile = 512 if resident else win.shape[2]
    tiles = win_in.shape[1] // tile
    slots = tiles if resident else win.shape[0]
    rows_step = length // 2
    low = jnp.bfloat16
    f32 = jnp.float32

    sources = (
        att_in,
        wo_in,
        tok_in,
        wcq_in,
        mkey_in,
        mvalue_in,
        wco_in,
        wd_in,
        wr_in,
        cot_in,
    )
    targets = (att_ref, wo, tok_ref, wcq, mkey_ref, mvalue_ref, wco, wd, wr, cot_ref)
    loads = [
        pltpu.make_async_copy(source, target, load_sem.at[index])
        for index, (source, target) in enumerate(zip(sources, targets))
    ]

    def win_load(which):
        slot = which % slots
        target = win.at[:, rows_of(which, tile)] if resident else win.at[slot]
        return pltpu.make_async_copy(win_in.at[:, rows_of(which, tile)], target, win_sem.at[slot])

    def wout_load(which):
        slot = which % slots
        target = wout.at[rows_of(which, tile), :] if resident else wout.at[slot]
        return pltpu.make_async_copy(wout_in.at[rows_of(which, tile), :], target, wout_sem.at[slot])

    for load in loads[:7]:
        load.start()

    def by_columns(extent, step, body):
        def one(index, carry):
            body(pl.ds(pl.multiple_of(index * step, step), step))
            return carry

        lax.fori_loop(0, extent // step, one, 0)

    def by_rows(body, init=0):
        def one(index, carry):
            return body(rows_of(index, rows_step), carry)

        return lax.fori_loop(0, length // rows_step, one, init)

    cols = 512
    half = width // 2

    for load in loads[:3]:
        load.wait()
    for load in loads[7:]:
        load.start()
    for which in range(slots):
        win_load(which).start()
    for which in range(slots):
        wout_load(which).start()

    def project_out(here):
        work[:, here] = tok_ref[:, here].astype(f32) + dot_nn(att_ref[...], wo[:, here])

    by_columns(width, cols, project_out)

    def first_norm(here, carry):
        unit, scale = normed(work[here, :])
        unit_one[here, :] = unit
        scale_one[here, :] = scale
        value = unit * gain_ref[0:1, :] + shift_ref[0:1, :]
        work[here, :] = value
        low_one[here, :] = value.astype(low)
        return carry

    by_rows(first_norm)

    loads[3].wait()

    def project_query(here):
        query[:, here] = dot_nn(low_one[...], wcq[:, here]).astype(low)

    by_columns(width, cols, project_query)
    per_block = LANES // HD

    def stacked(value):
        return jnp.concatenate(
            [jnp.where(head_lanes(value.shape, head), value, 0.0) for head in range(per_block)],
            axis=0,
        ).astype(low)

    def unstacked(value):
        return jnp.concatenate(
            [
                value[head * HD : (head + 1) * HD, head * length : (head + 1) * length]
                for head in range(per_block)
            ],
            axis=0,
        )

    def block_queries(here):
        return stacked(query[:, here].astype(f32) * 0.125)

    def cross_forward(block):
        here = rows_of(block, LANES)
        scores = dot_nt(mkey_ref[:, here], block_queries(here))
        raised = jnp.exp(scores - jnp.max(scores, axis=0, keepdims=True))
        share = 1.0 / jnp.sum(raised, axis=0, keepdims=True)
        weight = (raised * share).astype(low)
        weights[block] = weight
        values = mvalue_ref[:, here].astype(f32).T.astype(low)
        crossed[:, here] = unstacked(dot_nn(values, weight)).T.astype(low)

    loads[4].wait()
    loads[5].wait()

    def cross_forward_four(step, carry):
        for part in range(4):
            cross_forward(4 * step + part)
        return carry

    lax.fori_loop(0, width // LANES // 4, cross_forward_four, 0)

    loads[6].wait()

    def project_crossed(here):
        work[:, here] += dot_nn(crossed[...], wco[:, here])

    by_columns(width, cols, project_crossed)

    def second_norm(here, carry):
        unit, scale = normed(work[here, :])
        unit_two[here, :] = unit
        scale_two[here, :] = scale
        value = unit * gain_ref[1:2, :] + shift_ref[1:2, :]
        work[here, :] = value
        low_two[here, :] = value.astype(low)
        return carry

    by_rows(second_norm)

    step_cols = 512

    def feed_part(here, source):
        act, slope = gelu_pair(dot_nn(low_two[...], source))
        slopes[:, here] = slope.astype(low)
        return act.astype(low)

    if resident:

        def feed_forward(which, carry):
            here = rows_of(which, step_cols)

            @pl.when(which % (tile // step_cols) == 0)
            def _():
                win_load(which // (tile // step_cols)).wait()

            acts[:, here] = feed_part(here, win[:, here])
            return carry

        lax.fori_loop(0, tiles * tile // step_cols, feed_forward, 0)
        for which in range(tiles):
            wout_load(which).wait()

        def feed_out_part(here):
            total[:, here] = dot_nn(acts[...], wout[:, here])

        by_columns(width, step_cols, feed_out_part)
    else:
        total[...] = jnp.zeros_like(total)

        def feed_forward(which, carry):
            slot = lax.rem(which, slots)
            win_load(which).wait()
            wout_load(which).wait()
            total[...] += dot_nn(feed_part(rows_of(which, tile), win[slot]), wout[slot])

            @pl.when(which + slots < tiles)
            def _():
                win_load(which + slots).start()
                wout_load(which + slots).start()

            return carry

        lax.fori_loop(0, tiles, feed_forward, 0)

    loads[7].wait()
    loads[8].wait()
    loads[9].wait()
    act, slope = gelu_pair(dot_nn(low_two[...], wd[...]) + dbias_ref[...])
    down_act[...] = act.astype(low)
    down_slope[...] = slope.astype(low)

    def project_raise(here):
        work[:, here] += total[:, here] + 4.0 * (
            dot_nn(down_act[...], wr[:, here]) + rbias_ref[:, here]
        )

    by_columns(width, cols, project_raise)
    nothing = jnp.zeros((1, width), f32)

    def third_norm(here, carry):
        gain_sum, shift_sum, bias_sum = carry
        unit, scale = normed(work[here, :])
        gain = gain_ref[2:3, :]
        out_ref[here, :] = (unit * gain + shift_ref[2:3, :]).astype(low)
        grad = cot_ref[here, :].astype(f32)
        back = norm_back(grad * gain, scale, unit)
        total[here, :] = back
        back_low = back.astype(low)
        low_three[here, :] = back_low
        return (
            gain_sum + jnp.sum(grad * unit, axis=0, keepdims=True),
            shift_sum + jnp.sum(grad, axis=0, keepdims=True),
            bias_sum + jnp.sum(back_low.astype(f32), axis=0, keepdims=True),
        )

    gain_three, shift_three, bias_sum = by_rows(third_norm, (nothing, nothing, nothing))
    saves = []

    def save(source, target):
        copy = pltpu.make_async_copy(source, target, out_sem.at[len(saves)])
        copy.start()
        saves.append(copy)

    save(out_ref, layer_out)
    vecs_ref[0:1, :] = 4.0 * bias_sum

    back = 4.0 * dot_nt(low_three[...], wr[...]) * down_slope[...].astype(f32)
    back_low = back.astype(low)
    down_grad[...] = back_low
    vecs_ref[1:2, :] = jnp.concatenate(
        [
            jnp.sum(back_low.astype(f32), axis=0, keepdims=True),
            jnp.zeros((1, width - wd.shape[1]), f32),
        ],
        axis=1,
    )
    down = wd.shape[1]
    raise_sum = 4.0 * dot_tn(down_act[...], low_three[...])
    for index in range(width // LANES):
        sums_ref[pl.ds(down * width // LANES + index * down, down), :] = raise_sum[
            :, index * LANES : (index + 1) * LANES
        ].astype(low)
    down_sum = dot_tn(low_two[...], down_grad[...])
    for index in range(down // LANES):
        sums_ref[index * width : (index + 1) * width, :] = down_sum[
            :, index * LANES : (index + 1) * LANES
        ].astype(low)

    save(sums_ref, sums_out)

    if resident:

        def feed_slope(here):
            acts[:, here] = (
                dot_nt(low_three[...], wout[here, :]) * slopes[:, here].astype(f32)
            ).astype(low)

        by_columns(win_in.shape[1], step_cols, feed_slope)

        def feed_in_part(here):
            total[:, here] += dot_nt(acts[...], win[here, :])

        by_columns(width, step_cols, feed_in_part)
    else:

        def feed_backward(step, carry):
            which = tiles - 1 - step
            slot = lax.rem(which, slots)
            here = rows_of(which, tile)

            @pl.when(which < tiles - slots)
            def _():
                wout_load(which).wait()
                win_load(which).wait()

            grad = dot_nt(low_three[...], wout[slot]) * slopes[:, here].astype(f32)
            total[...] += dot_nt(grad.astype(low), win[slot])

            @pl.when(which >= slots)
            def _():
                win_load(which - slots).start()
                wout_load(which - slots).start()

            return carry

        lax.fori_loop(0, tiles, feed_backward, 0)

    def down_back(here):
        total[:, here] += dot_nt(down_grad[...], wd[here, :])

    by_columns(width, cols, down_back)

    def second_back(here, carry):
        gain_sum, shift_sum = carry
        grad = total[here, :]
        unit = unit_two[here, :]
        back = norm_back(grad * gain_ref[1:2, :], scale_two[here, :], unit)
        total[here, :] = back
        low_one[here, :] = back.astype(low)
        return (
            gain_sum + jnp.sum(grad * unit, axis=0, keepdims=True),
            shift_sum + jnp.sum(grad, axis=0, keepdims=True),
        )

    gain_two, shift_two = by_rows(second_back, (nothing, nothing))

    def crossed_back(here):
        crossed[:, here] = dot_nt(low_one[...], wco[here, :]).astype(low)

    by_columns(width, cols, crossed_back)

    def cross_backward(block):
        here = rows_of(block, LANES)
        grads = stacked(crossed[:, here].astype(f32))
        keys = mkey_ref[:, here].astype(f32).T.astype(low)
        slope = dot_nt(mvalue_ref[:, here], grads)
        weight_low = weights[block]
        weight = weight_low.astype(f32)
        slope = weight * (slope - jnp.sum(weight * slope, axis=0, keepdims=True))
        slope = slope.astype(low)
        queries = block_queries(here)
        mkey_ref[:, here] = dot_nn(slope, queries).astype(low)
        mvalue_ref[:, here] = dot_nn(weight_low, grads).astype(low)
        query[:, here] = (unstacked(dot_nn(keys, slope)) * 0.125).T.astype(low)

    def cross_backward_four(step, carry):
        for part in range(4):
            cross_backward(4 * step + part)
        return carry

    lax.fori_loop(0, width // LANES // 4, cross_backward_four, 0)
    save(mkey_ref, mkey_out)
    save(mvalue_ref, mvalue_out)

    def query_back(here):
        total[:, here] += dot_nt(query[...], wcq[here, :])

    by_columns(width, cols, query_back)

    def first_back(here, carry):
        gain_sum, shift_sum = carry
        grad = total[here, :]
        unit = unit_one[here, :]
        back = norm_back(grad * gain_ref[0:1, :], scale_one[here, :], unit)
        fgrad_ref[here, :] = back
        low_one[here, :] = back.astype(low)
        return (
            gain_sum + jnp.sum(grad * unit, axis=0, keepdims=True),
            shift_sum + jnp.sum(grad, axis=0, keepdims=True),
        )

    gain_one, shift_one = by_rows(first_back, (nothing, nothing))
    save(fgrad_ref, fgrad_out)

    for index in range(width // cols):
        here = slice(index * cols, (index + 1) * cols)
        ograd_ref[here, :] = dot_nt(low_one[...], wo[here, :]).T.astype(low)
        save(ograd_ref.at[here], ograd_out.at[here])
    for index, vector in enumerate(
        (gain_one, gain_two, gain_three, shift_one, shift_two, shift_three)
    ):
        vecs_ref[2 + index : 3 + index, :] = vector
    for copy in saves:
        copy.wait()


def middle(
    tokens, attended, cotangent, mem_key, mem_value, gains, shifts, down_bias, raise_bias, weights
):
    length, width = tokens.shape
    mem_len = mem_key.shape[0]
    down = weights[3].shape[1]
    feed = weights[5].shape[1]
    tile = 512 if mem_len <= 512 else 128
    resident = mem_len <= 512
    slots = feed // tile if resident else 2
    low = jnp.bfloat16
    f32 = jnp.float32
    vmem = pl.BlockSpec(memory_space=pltpu.VMEM)
    anywhere = pl.BlockSpec(memory_space=pl.ANY)
    square = pltpu.VMEM((width, width), low)
    wide = pltpu.VMEM((length, width), f32)
    narrow = pltpu.VMEM((length, width), low)
    return pl.pallas_call(
        middle_kernel,
        out_shape=(
            jax.ShapeDtypeStruct((length, width), low),
            jax.ShapeDtypeStruct((length, width), f32),
            jax.ShapeDtypeStruct((width, length), low),
            jax.ShapeDtypeStruct((mem_len, width), low),
            jax.ShapeDtypeStruct((mem_len, width), low),
            jax.ShapeDtypeStruct((2 * down * width // LANES, LANES), low),
            jax.ShapeDtypeStruct((8, width), f32),
        ),
        in_specs=[anywhere] * 5 + [vmem] * 4 + [anywhere] * 7,
        out_specs=(anywhere,) * 6 + (vmem,),
        scratch_shapes=[
            narrow,
            narrow,
            narrow,
            pltpu.VMEM((mem_len, width), low),
            pltpu.VMEM((mem_len, width), low),
            narrow,
            wide,
            pltpu.VMEM((width, length), low),
            pltpu.VMEM((2 * down * width // LANES, LANES), low),
            square,
            square,
            square,
            pltpu.VMEM((width, down), low),
            pltpu.VMEM((down, width), low),
            pltpu.VMEM((width, feed) if resident else (slots, width, tile), low),
            pltpu.VMEM((feed, width) if resident else (slots, tile, width), low),
            wide,
            wide,
            wide,
            wide,
            pltpu.VMEM((length, 1), f32),
            pltpu.VMEM((length, 1), f32),
            narrow,
            narrow,
            narrow,
            narrow,
            narrow,
            pltpu.VMEM((width // LANES, mem_len, LANES // HD * length), low),
            pltpu.VMEM((length, feed), low),
            pltpu.VMEM((length, feed) if resident else (16, LANES), low),
            pltpu.VMEM((length, down), low),
            pltpu.VMEM((length, down), low),
            pltpu.VMEM((length, down), low),
            pltpu.SemaphoreType.DMA((10,)),
            pltpu.SemaphoreType.DMA((slots,)),
            pltpu.SemaphoreType.DMA((slots,)),
            pltpu.SemaphoreType.DMA((5 + width // 512,)),
        ],
        compiler_params=pltpu.CompilerParams(vmem_limit_bytes=VMEM_BYTES + 3 * 1024 * 1024),
        name="middle",
    )(tokens, attended, cotangent, mem_key, mem_value, gains, shifts, down_bias, raise_bias, *weights)


def per_device(
    tokens,
    memory,
    segment_ids,
    padding_mask,
    cotangent,
    prefix_embed,
    prefix_first,
    first_bias,
    prefix_second,
    second_bias,
    adapter_down,
    down_bias,
    adapter_raise,
    raise_bias,
    norm_gain,
    norm_shift,
    self_query,
    self_key,
    self_value,
    self_output,
    cross_query,
    cross_key,
    cross_value,
    cross_output,
    feed_in,
    feed_out,
):
    row_count, length, model_width = tokens.shape
    flat_rows = row_count * length
    n = lax.axis_size("seq")
    batches = lax.axis_size("batch")
    down = adapter_down.shape[1]
    attended, mem_key, mem_value, *saved = self_forward(
        n,
        segment_ids,
        padding_mask,
        tokens.reshape(flat_rows, model_width),
        (self_query, self_key, self_value),
        (
            prefix_embed,
            prefix_first,
            first_bias.reshape(1, -1),
            prefix_second,
            second_bias.reshape(1, -1),
        ),
        memory.reshape(-1, model_width),
        (cross_key, cross_value),
    )
    layer_output, first_grad, out_grad, *mem_grads, weight_sums, vector_sums = middle(
        tokens.reshape(flat_rows, model_width),
        attended,
        cotangent.reshape(flat_rows, model_width),
        mem_key,
        mem_value,
        norm_gain,
        norm_shift,
        down_bias.reshape(1, -1),
        raise_bias.reshape(1, -1),
        (
            self_output,
            cross_query,
            cross_output,
            adapter_down,
            adapter_raise,
            feed_in,
            feed_out,
        ),
    )
    layer_output = layer_output.reshape(row_count, length, model_width)
    token_grad, memory_grad, *prefix_sums, vector_sums, full_sums = self_backward(
        n,
        batches,
        first_grad,
        out_grad.reshape(n, -1, HD, length),
        weight_sums,
        mem_grads,
        (cross_key, cross_value),
        vector_sums,
        saved,
        (self_query, self_key, self_value),
        (prefix_first, prefix_second, prefix_embed, first_bias.reshape(1, -1)),
    )
    *replicated, token_grad, memory_grad = finish(
        full_sums.reshape(-1, LANES),
        vector_sums,
        prefix_sums,
        prefix_embed,
        down,
        token_grad,
        memory_grad,
    )
    token_grad = token_grad.reshape(row_count, length, model_width)
    memory_grad = memory_grad.reshape(memory.shape)
    replicated = [
        value.reshape(-1) if value.shape[0] == 1 else value for value in replicated
    ]
    return (layer_output, token_grad, memory_grad, *replicated)


def solution(mesh):
    placed = (
        P("batch", "seq", None),
        P("batch", "seq", None),
        P("batch", "seq"),
        P("batch", "seq"),
        P("batch", "seq", None),
        P(),
        P(),
        P(),
        P(),
        P(),
        P(),
        P(),
        P(),
        P(),
        P(),
        P(),
        P(),
        P(),
        P(),
        P(),
        P(),
        P(),
        P(),
        P(),
        P(),
        P(),
    )
    return jax.shard_map(
        per_device,
        mesh=mesh,
        in_specs=placed,
        out_specs=(
            P("batch", "seq", None),
            P("batch", "seq", None),
            P("batch", "seq", None),
            P(),
            P(),
            P(),
            P(),
            P(),
            P(),
            P(),
            P(),
            P(),
            P(),
            P(),
        ),
        check_vma=False,
    )
```

```python
import functools

import jax
import jax.numpy as jnp
from jax import lax
from jax.experimental import pallas as pl
from jax.experimental.pallas import tpu as pltpu
from jax.sharding import PartitionSpec as P

H = 16
HD = 64
LANES = 128
PREFIX_ROWS = 32
VMEM_BYTES = 60 * 1024 * 1024
SUM_ROWS = 16
MESH = pl.DeviceIdType.MESH

masked_score = -1e30
norm_eps = 1e-05

def dot_nn(left, right):
    return lax.dot_general(
        left, right, (((1,), (0,)), ((), ())), preferred_element_type=jnp.float32
    )


def dot_nt(left, right):
    return lax.dot_general(
        left, right, (((1,), (1,)), ((), ())), preferred_element_type=jnp.float32
    )


def dot_tn(left, right):
    return lax.dot_general(
        left, right, (((0,), (0,)), ((), ())), preferred_element_type=jnp.float32
    )


def remote(source, target, send_sem, recv_sem, axis, peer):
    return pltpu.make_async_remote_copy(
        src_ref=source,
        dst_ref=target,
        send_sem=send_sem,
        recv_sem=recv_sem,
        device_id={axis: peer},
        device_id_type=MESH,
    )


def enter(sizes):
    barrier = pltpu.get_barrier_semaphore()
    for axis, size in sizes.items():
        for other in range(size):

            @pl.when(other != lax.axis_index(axis))
            def _():
                pl.semaphore_signal(barrier, inc=1, device_id={axis: other}, device_id_type=MESH)

    pl.semaphore_wait(barrier, sum(sizes.values()) - len(sizes))


def others(size, mine, body):
    for other in range(size):

        @pl.when(other != mine)
        def _():
            body(other)


def rows_of(index, size):
    return pl.ds(pl.multiple_of(index * size, size), size)


def span_of(start, size):
    return pl.ds(pl.multiple_of(start, LANES), size)


def own_columns(ref, first, me, width):
    if width % LANES == 0:
        return ref[:, pl.ds(pl.multiple_of(first + me * width, LANES), width)].astype(jnp.float32)
    share = LANES // width
    block = ref[:, pl.ds(pl.multiple_of(first + me // share * LANES, LANES), LANES)].astype(
        jnp.float32
    )
    picked = block[:, :width]
    for part in range(1, share):
        picked = jnp.where(me % share == part, block[:, part * width : (part + 1) * width], picked)
    return picked


def head_lanes(shape, head):
    lane = lax.broadcasted_iota(jnp.int32, shape, 1)
    return (lane >= head * HD) & (lane < (head + 1) * HD)


def self_forward_kernel(
    n,
    seg_ref,
    pad_ref,
    tok_ref,
    wq_in,
    wk_in,
    wv_in,
    emb_ref,
    first_in,
    fbias_ref,
    second_in,
    sbias_ref,
    mem_ref,
    wck_in,
    wcv_in,
    att_ref,
    mkey_out,
    mvalue_out,
    qx_out,
    kx_out,
    raw_out,
    pk_out,
    pv_out,
    pkt_out,
    ot_out,
    lse_out,
    send,
    recv,
    meta_send,
    meta,
    kx,
    qx,
    vt,
    hidden,
    pk,
    pv,
    pkt,
    pvt,
    stat,
    acc,
    o_send,
    o_recv,
    mem_all,
    wck,
    wcv,
    mkey_ref,
    mvalue_ref,
    wq_ref,
    wk_ref,
    wv_ref,
    first_ref,
    second_ref,
    send_sem,
    recv_sem,
    meta_send_sem,
    meta_recv_sem,
    o_send_sem,
    o_recv_sem,
    mem_send_sem,
    mem_recv_sem,
    out_sem,
    weight_sem,
    in_sem,
):
    low = jnp.bfloat16
    f32 = jnp.float32
    me = lax.axis_index("seq")
    length, width = tok_ref.shape
    group = width // n
    heads = group // HD
    plane = 2 * length
    planes = n // 2
    block = 2 * LANES
    per_block = block // group
    blocks = width // block
    my_plane = me // 2
    my_side = lax.rem(me, 2)

    upward = my_plane >= planes // 2
    turn_sign = jnp.where(upward, 1, -1)

    def plane_after(step):
        return lax.rem(my_plane + planes + turn_sign * step, planes)

    def meta_copy(peer, slot):
        return remote(
            meta_send, meta.at[slot], meta_send_sem.at[peer], meta_recv_sem.at[slot], "seq", peer
        )

    def qkv_copy(head, peer, slot):
        return remote(
            send.at[peer, head],
            recv.at[head, slot],
            send_sem.at[head, peer],
            recv_sem.at[head, slot],
            "seq",
            peer,
        )

    def out_copy(head, peer, slot):
        return remote(
            o_send.at[head, peer],
            o_recv.at[slot, head],
            o_send_sem.at[head, peer],
            o_recv_sem.at[head, slot],
            "seq",
            peer,
        )

    def mem_along(which, toward):
        part = mem_all.at[which, my_side]
        return remote(
            part,
            part,
            mem_send_sem.at[(toward + 1) // 2, which],
            mem_recv_sem.at[which],
            "seq",
            me + 2 * toward,
        )

    def mem_across(side):
        part = mem_all.at[:, side]
        return remote(
            part,
            part,
            mem_send_sem.at[0, planes],
            mem_recv_sem.at[planes],
            "seq",
            me + 1 - 2 * my_side,
        )

    def mem_hops(hop, body):
        for toward in (1, -1):
            which = my_plane - toward * hop
            ahead = my_plane + toward

            @pl.when((which >= 0) & (which < planes) & (ahead >= 0) & (ahead < planes))
            def _():
                body(mem_along(which, toward))

    def mem_arrivals(hop):
        for toward in (1, -1):
            which = my_plane - toward * hop

            @pl.when((which >= 0) & (which < planes))
            def _():
                mem_along(which, -toward).wait_recv()

    def block_at(step):
        if blocks >= planes:
            share = blocks // planes
            return plane_after(1 + step // share) * share + step % share
        return lax.rem(me // per_block + 1 + step, blocks)

    def weight_load(step, which):
        columns = rows_of(block_at(step), block)
        source = (wq_in, wk_in, wv_in)[which]
        target = (wq_ref, wk_ref, wv_ref)[which]
        return pltpu.make_async_copy(
            source.at[:, columns], target.at[:, columns], weight_sem.at[step, which]
        )

    for step in range(blocks):
        for which in range(3):
            weight_load(step, which).start()
    loads = [
        pltpu.make_async_copy(source, target, in_sem.at[index])
        for index, (source, target) in enumerate(
            ((first_in, first_ref), (second_in, second_ref), (wck_in, wck), (wcv_in, wcv))
        )
    ]
    for load in loads:
        load.start()
    segments = seg_ref[...]
    tags = jnp.where(pad_ref[...] == 1, segments, -1)
    row = lax.broadcasted_iota(jnp.int32, meta_send.shape, 0)
    meta_send[...] = jnp.where(row == 0, segments, tags)
    mem_all[my_plane, my_side] = mem_ref[...]
    enter({"seq": n})
    others(n, me, lambda peer: meta_copy(peer, me).start())
    meta[me] = meta_send[...]

    for step in range(blocks):
        at = block_at(step)
        columns = rows_of(at, block)
        for which, weight in enumerate((wq_ref, wk_ref, wv_ref)):
            weight_load(step, which).wait()
            piece = dot_nn(tok_ref[...], weight[:, columns]).T.astype(low)
            for part in range(per_block):
                for head in range(heads):
                    first = part * group + head * HD
                    send[at * per_block + part, head, which] = piece[first : first + HD]
        for part in range(per_block):
            peer = at * per_block + part

            @pl.when(peer != me)
            def _():
                qkv_copy(0, peer, me).start()

            @pl.when(peer == me)
            def _():
                for head in range(heads):
                    recv[head, me] = send[peer, head]

    mem_hops(0, lambda copy: copy.start())
    loads[0].wait()
    loads[1].wait()
    hidden[...] = jnp.zeros_like(hidden)
    hidden[: emb_ref.shape[0], :] = jnp.tanh(dot_nn(emb_ref[...], first_ref[...]) + fbias_ref[...])
    hidden_low = hidden[...].astype(low)
    prefix_key = dot_nn(hidden_low, own_columns(second_ref, 0, me, group).astype(low)) + own_columns(
        sbias_ref, 0, me, group
    )
    prefix_value = dot_nn(
        hidden_low, own_columns(second_ref, width, me, group).astype(low)
    ) + own_columns(sbias_ref, width, me, group)
    prefix_row = lax.broadcasted_iota(jnp.int32, (PREFIX_ROWS, HD), 0)
    prefix_open = jnp.where(prefix_row < emb_ref.shape[0], 0.0, masked_score)
    for head in range(heads):
        here = slice(head * HD, (head + 1) * HD)
        pk[head] = jnp.concatenate([prefix_key[:, here], prefix_open], axis=1).astype(low)
        pv[head] = prefix_value[:, here].astype(low)
    pkt[...] = prefix_key.T.astype(low).reshape(heads, HD, PREFIX_ROWS)
    pvt[:, :HD, :] = prefix_value.T.astype(low).reshape(heads, HD, PREFIX_ROWS)
    pvt[:, HD:, :] = jnp.ones((heads, SUM_ROWS, PREFIX_ROWS), low)
    vt[:, HD:, :] = jnp.ones((heads, SUM_ROWS, n * length), low)

    def arrive(head, chunk):
        @pl.when(chunk != me)
        def _():
            @pl.when(head == 0)
            def _():
                meta_copy(chunk, chunk).wait_recv()

            qkv_copy(head, chunk, chunk).wait_recv()

        here = rows_of(chunk, length)
        state = lax.broadcasted_iota(jnp.int32, (HD, length), 0)
        qx[head, :HD, here] = (recv[head, chunk, 0].astype(f32) * 0.125).astype(low)
        qx[head, HD:, here] = jnp.where(state == meta[chunk, 0:1, :], 1.0, 0.0).astype(low)
        is_open = jnp.where(state == meta[chunk, 1:2, :], 0.0, masked_score)
        kx[head, here, :] = jnp.concatenate(
            [recv[head, chunk, 1].astype(f32), is_open], axis=0
        ).T.astype(low)
        vt[head, :HD, here] = recv[head, chunk, 2]

    def open_plane(head, which):
        scores = dot_nn(pk[head], qx[head, :, rows_of(which, plane)])
        top = jnp.max(scores, axis=0, keepdims=True)
        raised = jnp.exp(scores - top)
        stat[which, head, 0:1, :] = top
        acc[which, head] = dot_nn(pvt[head], raised.astype(low))

    def pair_part(head, upper, lower, first, count, keys, diagonal):
        here = slice(first, first + count)
        queries = qx[head, :, span_of(upper * plane + first, count)]
        key_rows = span_of(lower * plane, keys)
        scores = dot_nn(kx[head, key_rows, :], queries)
        if diagonal:
            key_at = lax.broadcasted_iota(jnp.int32, scores.shape, 0)
            query_at = lax.broadcasted_iota(jnp.int32, scores.shape, 1) + first
            scores = jnp.where(key_at <= query_at, scores, masked_score)
        old_top = stat[upper, head, 0:1, here]
        top = jnp.maximum(old_top, jnp.max(scores, axis=0, keepdims=True))
        raised = jnp.exp(scores - top).astype(low)
        stat[upper, head, 0:1, here] = top
        acc[upper, head, :, here] = acc[upper, head, :, here] * jnp.exp(old_top - top) + dot_nn(
            vt[head, :, key_rows], raised
        )

    def pair(head, upper, lower):
        pair_part(head, upper, lower, 0, plane, plane, False)

    def pair_diagonal(head, which):
        for part in range(2):
            pair_part(head, which, which, part * length, length, (part + 1) * length, True)

    def close_plane(head, which):
        total = acc[which, head, HD : HD + 1, :]
        value = acc[which, head, :HD, :] / total
        acc[which, head, :HD, :] = value
        stat[which, head, 0:1, :] = stat[which, head, 0:1, :] + jnp.log(total)
        for part in range(2):
            chunk = 2 * which + part
            o_send[head, chunk] = value[:, part * length : (part + 1) * length].astype(low)

            @pl.when((chunk != me) & (head == heads - 1))
            def _():
                out_copy(head, chunk, me).start()

            @pl.when(chunk == me)
            def _():
                o_recv[me, head] = o_send[head, chunk]

    def project_memory():
        mem_across(1 - my_side).wait_recv()
        for load in loads[2:]:
            load.wait()
        whole = mem_all[...].reshape(mkey_ref.shape)

        def one(index, carry):
            here = rows_of(index, block)
            mkey_ref[:, here] = dot_nn(whole, wck[:, here]).astype(low)
            mvalue_ref[:, here] = dot_nn(whole, wcv[:, here]).astype(low)
            return carry

        lax.fori_loop(0, blocks, one, 0)

    def stage(index, carry):
        head = index // planes
        step = lax.rem(index, planes)

        @pl.when(head + 1 < heads)
        def _():
            there = plane_after(1 + step)
            for part in range(2):
                peer = 2 * there + part

                @pl.when(peer != me)
                def _():
                    qkv_copy(head, peer, me).wait_send()
                    qkv_copy(head + 1, peer, me).start()

        @pl.when((head == heads - 1) & (head > 0))
        def _():
            there = plane_after(1 + step)
            for part in range(2):
                peer = 2 * there + part

                @pl.when(peer != me)
                def _():
                    qkv_copy(head, peer, me).wait_send()
                    out_copy(head - 1, peer, me).start()

        here = plane_after(step)
        arrive(head, 2 * here)
        arrive(head, 2 * here + 1)
        open_plane(head, here)
        pair_diagonal(head, here)

        def earlier(back, inner):
            there = plane_after(back)
            pair(head, jnp.maximum(here, there), jnp.minimum(here, there))

            @pl.when((step == planes - 1) & (there > here))
            def _():
                close_plane(head, there)

            return inner

        lax.fori_loop(0, step, earlier, 0)
        for hop in range(1, planes - 1):

            @pl.when(index == hop)
            def _():
                mem_arrivals(hop)
                mem_hops(hop, lambda copy: copy.start())

        @pl.when(index == planes - 1)
        def _():
            mem_arrivals(planes - 1)
            mem_across(my_side).start()

        @pl.when((upward & (my_plane + step >= planes)) | (step == planes - 1))
        def _():
            close_plane(head, here)

        @pl.when(jnp.logical_not(upward) & (step == my_plane))
        def _():
            def close(which, inner):
                close_plane(head, which)
                return inner

            lax.fori_loop(0, my_plane + 1, close, 0)

        return carry

    lax.fori_loop(0, heads * planes, stage, 0)

    saves = []

    def save(source, target):
        copy = pltpu.make_async_copy(source, target, out_sem.at[len(saves)])
        copy.start()
        saves.append(copy)

    save(qx, qx_out)
    save(kx, kx_out)
    save(recv, raw_out)
    save(pk, pk_out)
    save(pv, pv_out)
    save(pkt, pkt_out)
    save(acc, ot_out)
    save(stat, lse_out)
    project_memory()
    save(mkey_ref, mkey_out)
    save(mvalue_ref, mvalue_out)
    for other in range(n):

        @pl.when(other != me)
        def _():
            for head in range(heads):
                out_copy(head, other, other).wait_recv()

        att_ref[:, other * group : (other + 1) * group] = (
            o_recv[other].reshape(group, length).astype(f32).T.astype(low)
        )

    def drain(peer):
        meta_copy(peer, me).wait_send()
        if heads == 1:
            qkv_copy(0, peer, me).wait_send()
        for head in range(heads):
            out_copy(head, peer, me).wait_send()

    others(n, me, drain)
    for hop in range(planes - 1):
        mem_hops(hop, lambda copy: copy.wait_send())
    mem_across(my_side).wait_send()
    for copy in saves:
        copy.wait()


def self_forward(n, segments, padding, tokens, weights, prefix, memory, mem_weights):
    length, width = tokens.shape
    group = width // n
    heads = group // HD
    whole = n * length
    planes = n // 2
    low = jnp.bfloat16
    f32 = jnp.float32
    vmem = pl.BlockSpec(memory_space=pltpu.VMEM)
    anywhere = pl.BlockSpec(memory_space=pl.ANY)
    dma = pltpu.SemaphoreType.DMA
    shapes = (
        ((heads, 2 * HD, whole), low),
        ((heads, whole, 2 * HD), low),
        ((heads, n, 3, HD, length), low),
        ((heads, PREFIX_ROWS, 2 * HD), low),
        ((heads, PREFIX_ROWS, HD), low),
        ((heads, HD, PREFIX_ROWS), low),
        ((planes, heads, HD + SUM_ROWS, 2 * length), f32),
        ((planes, heads, 8, 2 * length), f32),
    )
    square = pltpu.VMEM((width, width), low)
    qx, kx, raw, pk, pv, pkt, acc, stat = (pltpu.VMEM(*shape) for shape in shapes)
    return pl.pallas_call(
        functools.partial(self_forward_kernel, n),
        out_shape=(
            jax.ShapeDtypeStruct((length, width), low),
            jax.ShapeDtypeStruct((n * memory.shape[0], width), low),
            jax.ShapeDtypeStruct((n * memory.shape[0], width), low),
        )
        + tuple(jax.ShapeDtypeStruct(*shape) for shape in shapes),
        in_specs=[vmem] * 3
        + [anywhere] * 3
        + [vmem, anywhere, vmem, anywhere, vmem, vmem]
        + [anywhere] * 2,
        out_specs=(vmem,) + (anywhere,) * 10,
        scratch_shapes=[
            pltpu.VMEM((n, heads, 3, HD, length), low),
            raw,
            pltpu.VMEM((8, length), jnp.int32),
            pltpu.VMEM((n, 8, length), jnp.int32),
            kx,
            qx,
            pltpu.VMEM((heads, HD + SUM_ROWS, whole), low),
            pltpu.VMEM((PREFIX_ROWS, weights[0].shape[0] // 2), f32),
            pk,
            pv,
            pkt,
            pltpu.VMEM((heads, HD + SUM_ROWS, PREFIX_ROWS), low),
            stat,
            acc,
            pltpu.VMEM((heads, n, HD, length), low),
            pltpu.VMEM((n, heads, HD, length), low),
            pltpu.VMEM((planes, 2) + memory.shape, low),
            square,
            square,
            pltpu.VMEM((n * memory.shape[0], width), low),
            pltpu.VMEM((n * memory.shape[0], width), low),
            square,
            square,
            square,
            pltpu.VMEM(prefix[1].shape, low),
            pltpu.VMEM(prefix[3].shape, low),
            dma((heads, n)),
            dma((heads, n)),
            dma((n,)),
            dma((n,)),
            dma((heads, n)),
            dma((heads, n)),
            dma((2, planes + 1)),
            dma((planes + 1,)),
            dma((10,)),
            dma((width // (2 * LANES), 3)),
            dma((4,)),
        ],
        compiler_params=pltpu.CompilerParams(
            collective_id=0, has_side_effects=True, vmem_limit_bytes=VMEM_BYTES
        ),
        name="self_forward",
    )(segments, padding, tokens, *weights, *prefix, memory, *mem_weights)


def both_parts(value):
    high = value.astype(jnp.bfloat16).astype(jnp.float32)
    return jnp.concatenate([high, value - high], axis=0).astype(jnp.bfloat16)


def self_backward_kernel(
    n,
    batches,
    base_in,
    do_in,
    sums_in,
    mkey_in,
    mvalue_in,
    wck_in,
    wcv_in,
    vecs_in,
    qx_in,
    kx_in,
    raw_in,
    pk_in,
    pv_in,
    pkt_in,
    ot_in,
    lse_in,
    wq_in,
    wk_in,
    wv_in,
    first_in,
    second_in,
    emb_ref,
    fbias_ref,
    tg_ref,
    mgrad_ref,
    pkv_ref,
    hidden_ref,
    hgrad_ref,
    embed_ref,
    vecs_ref,
    full_out,
    do_recv,
    qx,
    kx,
    raw,
    kt,
    values,
    dot,
    qdo,
    pk,
    pv,
    pkt,
    ot,
    stat,
    weights,
    dqt,
    dkv,
    g_send,
    g_recv,
    pre_ref,
    pre_all,
    pre_sum,
    pre_recv,
    sums_mine,
    sums_core,
    sums_x,
    sums_side,
    sums_z,
    sums_far,
    full,
    mkey,
    mvalue,
    wck,
    wcv,
    mem_part,
    mem_side,
    mem_up,
    mem_down,
    vec_all,
    vec_sum,
    vec_y,
    vec_both,
    vec_z,
    product,
    first,
    second,
    base_ref,
    do_send_sem,
    do_recv_sem,
    g_send_sem,
    g_recv_sem,
    in_sem,
    send_sem,
    recv_sem,
):
    low = jnp.bfloat16
    f32 = jnp.float32
    me = lax.axis_index("seq")
    length, width = tg_ref.shape
    group = width // n
    heads = group // HD
    plane = 2 * length
    planes = n // 2
    step_rows = 256
    my_batch = lax.axis_index("batch")
    my_core = lax.rem(my_batch, 2)
    my_high = my_batch // 2
    highs = batches // 2
    my_plane = me // 2
    my_side = lax.rem(me, 2)
    beside = me + 1 - 2 * my_side
    used = [0]

    def numbers(count):
        used[0] += count
        return used[0] - count

    core_slot = numbers(2)
    x_slot = numbers(2 * highs)
    y_slot = numbers(3)
    z_slot = numbers(2 * planes + 2)
    up_slot = numbers(planes)
    down_slot = numbers(planes)
    va_slot = numbers(batches)
    vb_slot = numbers(1)
    vc_slot = numbers(planes)
    pa_slot = numbers(batches)
    pb_slot = numbers(n)

    def send(source, target, first, peer_index, slot_index, axis, peer):
        return remote(
            source,
            target,
            send_sem.at[first + peer_index],
            recv_sem.at[first + slot_index],
            axis,
            peer,
        )

    half_rows = 2 * planes * highs * sums_far.shape[0]
    x_rows = half_rows // highs
    y_rows = x_rows // 2
    z_rows = y_rows // planes
    x_row = pl.multiple_of(my_high * x_rows, x_rows)
    y_row = pl.multiple_of(x_row + my_side * y_rows, y_rows)

    def part(row, count):
        return sums_mine.at[pl.ds(pl.multiple_of(row, count), count)]

    def reduce_core():
        return send(
            sums_in.at[1 - my_core], sums_core, core_slot, 0, 0, "batch", my_batch + 1 - 2 * my_core
        )

    def reduce_x(peer, slot):
        return send(
            part(peer * x_rows, x_rows),
            sums_x.at[slot],
            x_slot,
            peer,
            slot,
            "batch",
            2 * peer + my_core,
        )

    def reduce_y():
        return send(
            part(x_row + (1 - my_side) * y_rows, y_rows), sums_side, y_slot, 0, 0, "seq", beside
        )

    near = planes // 2
    my_half = my_plane // near
    my_place = lax.rem(my_plane, near)
    far_plane = my_plane + near - 2 * near * my_half

    def piece_rows(half, place):
        return pl.ds(pl.multiple_of(y_row + (half * near + place) * z_rows, z_rows), z_rows)

    def reduce_near(half, peer, slot):
        return send(
            sums_mine.at[piece_rows(half, peer)],
            sums_z.at[half, slot],
            z_slot + half * near,
            peer,
            slot,
            "seq",
            2 * (my_half * near + peer) + my_side,
        )

    def reduce_far():
        return send(
            sums_mine.at[piece_rows(1 - my_half, my_place)],
            sums_far,
            z_slot + planes,
            0,
            0,
            "seq",
            2 * far_plane + my_side,
        )

    def gather_far(which):
        piece = full.at[my_core, my_high, my_side, which]
        return send(
            piece, piece, z_slot + planes + 1, 0, 0, "seq", 2 * far_plane + my_side
        )

    def gather_near(half, peer, slot):
        piece = full.at[my_core, my_high, my_side, half * near + slot]
        return send(
            piece,
            piece,
            z_slot + planes + 2 + half * near,
            peer,
            slot,
            "seq",
            2 * (my_half * near + peer) + my_side,
        )

    def both_halves(make, slot, action):
        def one(peer):
            for half in range(2):
                action(make(half, peer, peer if slot is None else slot))

        others(near, my_place, one)

    def gather_y(side):
        piece = full.at[my_core, my_high, side]
        return send(piece, piece, y_slot + 1, 0, 0, "seq", beside)

    def gather_x(peer, slot):
        piece = full.at[my_core, slot]
        return send(piece, piece, x_slot + highs, peer, slot, "batch", 2 * peer + my_core)

    def gather_core(core):
        piece = full.at[core]
        return send(piece, piece, core_slot + 1, 0, 0, "batch", my_batch + 1 - 2 * my_core)

    def mem_across():
        return send(
            mem_part.at[:, 1 - my_side], mem_side, y_slot + 2, 0, 0, "seq", beside
        )

    def mem_hop(target, toward, peer=None):
        buffer, slot = (mem_up, up_slot) if toward > 0 else (mem_down, down_slot)
        return send(
            mem_part.at[target, my_side],
            buffer.at[target],
            slot,
            target,
            target,
            "seq",
            me + 2 * toward if peer is None else peer,
        )

    def mem_from(target, toward):
        return mem_hop(target, toward, me - 2 * toward)

    def mem_pass(toward):
        buffer = mem_up if toward > 0 else mem_down
        first = 0 if toward > 0 else planes - 1
        for target in range(planes):

            @pl.when((target - my_plane) * toward > 0)
            def _():
                @pl.when(my_plane != first)
                def _():
                    mem_from(target, toward).wait_recv()
                    mem_part[target, my_side] = (
                        mem_part[target, my_side].astype(f32) + buffer[target].astype(f32)
                    ).astype(low)

                mem_hop(target, toward).start()

    def mem_stage(at):
        pl.when(my_plane == at)(lambda: mem_pass(1))
        pl.when(my_plane == planes - 1 - at)(lambda: mem_pass(-1))

    def mem_end():
        value = mem_part[my_plane, my_side].astype(f32)
        mgrad_ref[...] = value.astype(low)

        @pl.when(my_plane > 0)
        def _():
            mem_from(my_plane, 1).wait_recv()
            mgrad_ref[...] = (mgrad_ref[...].astype(f32) + mem_up[my_plane].astype(f32)).astype(low)

        @pl.when(my_plane < planes - 1)
        def _():
            mem_from(my_plane, -1).wait_recv()
            mgrad_ref[...] = (
                mgrad_ref[...].astype(f32) + mem_down[my_plane].astype(f32)
            ).astype(low)

    def mem_drain():
        for target in range(planes):

            @pl.when(target > my_plane)
            def _():
                mem_hop(target, 1).wait_send()

            @pl.when(target < my_plane)
            def _():
                mem_hop(target, -1).wait_send()

    def vec_a(peer, slot):
        return send(vecs_in, vec_all.at[slot], va_slot, peer, slot, "batch", peer)

    def vec_b(side):
        return send(vec_sum, vec_y.at[side], vb_slot, 0, 0, "seq", beside)

    def vec_c(peer, slot):
        return send(vec_both, vec_z.at[slot], vc_slot, peer, slot, "seq", 2 * peer + my_side)

    def pre_a(peer, slot):
        return send(pre_ref, pre_all.at[slot], pa_slot, peer, slot, "batch", peer)

    def pre_b(peer, slot):
        return send(pre_sum, pre_recv.at[slot], pb_slot, peer, slot, "seq", peer)

    def do_copy(head, peer, slot):
        return remote(
            do_in.at[peer, head],
            do_recv.at[head, slot],
            do_send_sem.at[head, peer],
            do_recv_sem.at[head, slot],
            "seq",
            peer,
        )

    def q_copy(head, peer, slot):
        return remote(
            g_send.at[peer, head, 0],
            g_recv.at[0, slot, head],
            g_send_sem.at[0, head, peer],
            g_recv_sem.at[0, head, slot],
            "seq",
            peer,
        )

    def kv_copy(head, peer, slot):
        return remote(
            g_send.at[peer, head, pl.ds(1, 2)],
            g_recv.at[pl.ds(1, 2), slot, head],
            g_send_sem.at[1, head, peer],
            g_recv_sem.at[1, head, slot],
            "seq",
            peer,
        )

    def far_first(body):
        for index in range(n):
            peer = jnp.where(my_plane < planes // 2, n - 1 - index, index)

            @pl.when(peer != me)
            def _():
                body(peer)

    def added(ref, size):
        value = ref[0].astype(f32)
        for other in range(1, size):
            value = value + ref[other].astype(f32)
        return value

    loads = [
        pltpu.make_async_copy(source, target, in_sem.at[index])
        for index, (source, target) in enumerate(
            (
                (raw_in, raw),
                (kx_in, kx),
                (pk_in, pk),
                (pv_in, pv),
                (pkt_in, pkt),
                (qx_in, qx),
                (ot_in, ot),
                (lse_in, stat),
                (sums_in.at[my_core], sums_mine),
                (vecs_in, vec_all.at[my_batch]),
                (mkey_in, mkey),
                (mvalue_in, mvalue),
                (wck_in, wck),
                (wcv_in, wcv),
                (base_in, base_ref),
                (wq_in, weights.at[0]),
                (wk_in, weights.at[1]),
                (wv_in, weights.at[2]),
                (first_in, first),
                (second_in, second),
            )
        )
    ]
    own_do = pltpu.make_async_copy(do_in.at[me], do_recv.at[:, me], in_sem.at[len(loads)])
    own_do.start()
    for load in loads:
        load.start()
    enter({"seq": n, "batch": batches})
    far_first(lambda peer: do_copy(0, peer, me).start())
    reduce_core().start()
    others(batches, my_batch, lambda peer: vec_a(peer, my_batch).start())
    dkv[...] = jnp.zeros_like(dkv)
    product[...] = jnp.zeros_like(product)
    pre_ref[...] = jnp.zeros_like(pre_ref)
    for load in loads[:14]:
        load.wait()
    own_do.wait()

    def turn(index, carry):
        head = index // n
        chunk = lax.rem(index, n)
        here = rows_of(chunk, length)
        kt[head, :, here] = raw[head, chunk, 1]
        values[head, here, :] = raw[head, chunk, 2].astype(f32).T.astype(low)
        return carry

    lax.fori_loop(0, heads * n, turn, 0)

    def memory_back(index, carry):
        here = rows_of(index, step_rows)
        value = dot_nt(mkey[...], wck[here, :]) + dot_nt(mvalue[...], wcv[here, :])
        mem_part[:, :, :, here] = value.astype(low).reshape(mem_part.shape[:3] + (step_rows,))
        return carry

    lax.fori_loop(0, width // step_rows, memory_back, 0)
    mem_across().start()

    def next_head(head):
        def move(peer):
            do_copy(head, peer, me).wait_send()
            do_copy(head + 1, peer, me).start()

        far_first(move)

    def arrive(head, which):
        for part in range(2):
            chunk = 2 * which + part

            @pl.when(chunk != me)
            def _():
                do_copy(head, chunk, chunk).wait_recv()

            grads = do_recv[head, chunk]
            dot[head, :, rows_of(chunk, length)] = grads
            grads = grads.astype(f32)
            query = raw[head, chunk, 0].astype(f32) * 0.125
            qdo[head, rows_of(chunk, length), :] = (
                jnp.concatenate([query, grads], axis=0).T.astype(low)
            )
            here = slice(part * length, (part + 1) * length)
            stat[which, head, 1:2, here] = jnp.sum(
                grads * ot[which, head, :HD, here], axis=0, keepdims=True
            )
        here = rows_of(which, plane)
        weight = jnp.exp(dot_nn(pk[head], qx[head, :, here]) - stat[which, head, 0:1, :])
        slope = weight * (dot_nn(pv[head], dot[head, :, here]) - stat[which, head, 1:2, :])
        both = jnp.concatenate([slope, weight], axis=0).astype(low)
        sums = dot_nn(both, qdo[head, here, :])
        pre_ref[head] += jnp.where(
            head_lanes((PREFIX_ROWS, 2 * HD), 0), sums[:PREFIX_ROWS], sums[PREFIX_ROWS:]
        )
        slope = slope.astype(low)
        dqt[which, head] = dot_nn(pkt[head], slope)

    def plus(first, second):
        return (first.astype(f32) + second.astype(f32)).astype(low)

    def sum_one():
        reduce_core().wait_recv()
        sums_mine[...] = plus(sums_mine[...], sums_core[...])
        others(highs, my_high, lambda peer: reduce_x(peer, my_high).start())

    def sum_two():
        here = pl.ds(x_row, x_rows)
        others(highs, my_high, lambda peer: reduce_x(peer, peer).wait_recv())
        sums_x[my_high] = sums_mine[here]
        sums_mine[here] = added(sums_x, highs).astype(low)
        reduce_y().start()

    def sum_three():
        here = pl.ds(y_row, y_rows)
        reduce_y().wait_recv()
        sums_mine[here] = plus(sums_mine[here], sums_side[...])
        both_halves(reduce_near, my_place, lambda copy: copy.start())

    def sum_four():
        both_halves(reduce_near, None, lambda copy: copy.wait_recv())
        for half in range(2):
            here = piece_rows(half, my_place)
            sums_z[half, my_place] = sums_mine[here]
            value = sums_z[half, 0].astype(f32)
            for other in range(1, near):
                value = value + sums_z[half, other].astype(f32)
            sums_mine[here] = value.astype(low)
        reduce_far().start()

    def sum_across():
        reduce_far().wait_recv()
        full[my_core, my_high, my_side, my_plane] = plus(
            sums_mine[piece_rows(my_half, my_place)], sums_far[...]
        )
        gather_far(my_plane).start()

    def sum_return():
        gather_far(far_plane).wait_recv()
        both_halves(gather_near, my_place, lambda copy: copy.start())

    def sum_five():
        both_halves(gather_near, None, lambda copy: copy.wait_recv())
        gather_y(my_side).start()

    def sum_six():
        gather_y(1 - my_side).wait_recv()
        others(highs, my_high, lambda peer: gather_x(peer, my_high).start())

    def sum_seven():
        others(highs, my_high, lambda peer: gather_x(peer, peer).wait_recv())
        gather_core(my_core).start()

    def sum_end():
        gather_core(1 - my_core).wait_recv()
        save_full.start()

    def vec_one():
        others(batches, my_batch, lambda peer: vec_a(peer, peer).wait_recv())
        vec_sum[...] = added(vec_all, batches)
        vec_b(my_side).start()
        vec_y[my_side] = vec_sum[...]

    def vec_two():
        vec_b(1 - my_side).wait_recv()
        value = (vec_y[0] + vec_y[1]).astype(f32)
        vec_both[...] = jnp.concatenate(
            [value[:, : width // 2], value[:, width // 2 :]], axis=0
        ).astype(low)
        others(planes, my_plane, lambda peer: vec_c(peer, my_plane).start())
        vec_z[my_plane] = vec_both[...]

    def vec_end():
        others(planes, my_plane, lambda peer: vec_c(peer, peer).wait_recv())
        value = added(vec_z, planes)
        vecs_ref[:, : width // 2] = value[:8]
        vecs_ref[:, width // 2 :] = value[8:]

    def mem_one():
        mem_across().wait_recv()
        mem_part[:, my_side] = plus(mem_part[:, my_side], mem_side[...])

    def stage_pa():
        others(batches, my_batch, lambda peer: pre_a(peer, my_batch).start())
        pre_all[my_batch] = pre_ref[...]

    def stage_pb():
        others(batches, my_batch, lambda peer: pre_a(peer, peer).wait_recv())
        pre_sum[...] = added(pre_all, batches).astype(low)
        others(n, me, lambda peer: pre_b(peer, me).start())
        pre_recv[me] = pre_sum[...]

    save_full = pltpu.make_async_copy(full, full_out, in_sem.at[0])

    def pair_part(head, upper, lower, first, count, diagonal, at=None):
        keys = span_of(lower * plane + (first if at is None else at * count), count)
        here = span_of(upper * plane + first, plane - first)
        at = slice(first, plane)
        scores = dot_nn(kx[head, keys, :], qx[head, :, here])
        slope = dot_nn(values[head, keys, :], dot[head, :, here]) - stat[upper, head, 1:2, at]
        weight = jnp.exp(scores - stat[upper, head, 0:1, at])
        if diagonal:
            key_at = lax.broadcasted_iota(jnp.int32, scores.shape, 0)
            query_at = lax.broadcasted_iota(jnp.int32, scores.shape, 1)
            weight = jnp.where(key_at <= query_at, weight, 0.0)
        slope = (weight * slope).astype(low)
        key_part = dot_nn(slope, qdo[head, here, :])
        value_part = dot_nn(weight.astype(low), qdo[head, here, :])
        dkv[head, keys, :] += jnp.where(head_lanes((count, 2 * HD), 0), key_part, value_part)
        dqt[upper, head, :, at] += dot_nn(kt[head, :, keys], slope)

    def pair(head, upper, lower, diagonal):
        if diagonal:
            for part in range(plane // step_rows):
                pair_part(head, upper, lower, part * step_rows, step_rows, True)
        else:

            def one(at, carry):
                pair_part(head, upper, lower, 0, step_rows, False, at)
                return carry

            lax.fori_loop(0, plane // step_rows, one, 0)

    def hand_queries(head, which):
        for part in range(2):
            chunk = 2 * which + part
            g_send[chunk, head, 0] = (
                dqt[which, head, :, part * length : (part + 1) * length] * 0.125
            ).astype(low)

            @pl.when(chunk != me)
            def _():
                q_copy(head, chunk, me).start()

            @pl.when(chunk == me)
            def _():
                g_recv[0, me, head] = g_send[chunk, head, 0]

    def hand_keys(head, which):
        for part in range(2):
            chunk = 2 * which + part
            turned = dkv[head, rows_of(chunk, length), :].T.astype(low)
            g_send[chunk, head, 1] = turned[:HD]
            g_send[chunk, head, 2] = turned[HD:]

            @pl.when(chunk != me)
            def _():
                kv_copy(head, chunk, me).start()

            @pl.when(chunk == me)
            def _():
                g_recv[pl.ds(1, 2), me, head] = g_send[chunk, head, pl.ds(1, 2)]

    rising = my_plane >= planes // 2
    total = heads * planes * (planes + 1) // 2
    hooks = [
        (2, sum_one),
        (3, mem_one),
        (4, lambda: mem_stage(0)),
        (5, vec_one),
        (5, sum_two),
        (7, sum_three),
        (8, vec_two),
        (9, sum_four),
        (11, sum_across),
        (13, sum_return),
        (15, sum_five),
        (16, sum_six),
        (16, vec_end),
        (19, sum_seven),
    ] + [(4 + 3 * at, functools.partial(mem_stage, at)) for at in range(1, planes - 1)]
    hooks += [
        (1 + head * total // heads, functools.partial(next_head, head)) for head in range(heads - 1)
    ]
    final = total - planes * (planes + 1) // 2
    hooks += [(final + planes + 1, stage_pa), (final + 2 * planes - 1, stage_pb)]

    def hook(pairs):
        for number, body in sorted(hooks, key=lambda item: item[0]):
            pl.when(pairs == number)(body)


    def stage(index, carry):
        head = index // planes
        step = lax.rem(index, planes)
        here = jnp.where(rising, step, planes - 1 - step)

        @pl.when((step == 0) | ((step == 1) & jnp.logical_not(rising)))
        def _():
            @pl.when(rising | (step == 0))
            def _():
                arrive(head, here)

            @pl.when(jnp.logical_not(rising) & (step == 1))
            def _():
                def rest(which, inner):
                    arrive(head, planes - 2 - which)
                    return inner

                lax.fori_loop(0, planes - 1, rest, 0)

        begun = head * (planes * (planes + 1) // 2) + step * planes - step * (step - 1) // 2
        hook(begun)
        pair(head, here, here, True)

        @pl.when(rising)
        def _():
            hand_queries(head, here)

        @pl.when(jnp.logical_not(rising))
        def _():
            hand_keys(head, here)

        def far(at, inner):
            there = jnp.where(rising, here + 1 + at, here - 1 - at)

            @pl.when(rising & (step == 0))
            def _():
                arrive(head, there)

            hook(begun + 1 + at)
            pair(head, jnp.maximum(here, there), jnp.minimum(here, there), False)
            return inner

        lax.fori_loop(0, planes - 1 - step, far, 0)

        @pl.when(rising)
        def _():
            hand_keys(head, here)

        @pl.when(jnp.logical_not(rising))
        def _():
            hand_queries(head, here)

        return carry

    lax.fori_loop(0, heads * planes, stage, 0)
    mem_end()
    for load in loads[14:]:
        load.wait()

    def gathered(peer):
        for head in range(heads):
            q_copy(head, peer, peer).wait_recv()
            kv_copy(head, peer, peer).wait_recv()

    half = width // 2

    def gather_plane(step, carry):
        which = lax.rem(my_plane + step, planes)
        for part in range(2):
            peer = 2 * which + part

            @pl.when(peer != me)
            def _():
                gathered(peer)

        columns = rows_of(which, 2 * group)
        for part in range(2):
            here = slice(part * half, (part + 1) * half)
            value = product[here, :]
            for kind in range(3):
                grads = g_recv[kind, pl.ds(2 * which, 2)].reshape(2 * group, length)
                value = value + dot_nn(weights[kind, here, columns], grads)
            product[here, :] = value
        return carry

    lax.fori_loop(0, planes - 1, gather_plane, 0)
    for other in range(n):

        @pl.when(other != me)
        def _():
            pre_b(other, other).wait_recv()

        value = pre_recv[other].astype(f32)
        for which in range(2):
            pkv_ref[:, which * width + other * group : which * width + (other + 1) * group] = (
                jnp.concatenate(
                    [value[head, :, which * HD : (which + 1) * HD] for head in range(heads)], axis=1
                )
            )

    count = emb_ref.shape[0]
    hidden_ref[...] = jnp.zeros_like(hidden_ref)
    hidden_ref[:count, :] = jnp.tanh(dot_nn(emb_ref[...], first[...]) + fbias_ref[...])
    value = hidden_ref[...]
    grad = dot_nt(both_parts(pkv_ref[...]), second[...])
    grad = (grad[:PREFIX_ROWS] + grad[PREFIX_ROWS:]) * (1.0 - value * value)
    hgrad_ref[...] = grad
    back = dot_nt(both_parts(grad), first[...])
    embed_ref[...] = back[:PREFIX_ROWS] + back[PREFIX_ROWS:]
    gather_plane(planes - 1, 0)
    sum_end()
    tile = 256
    for index in range(width // tile):
        here = slice(index * tile, (index + 1) * tile)
        tg_ref[:, here] = (base_ref[:, here] + product[here, :].T).astype(low)
    def drain(peer):
        do_copy(heads - 1, peer, me).wait_send()
        pre_b(peer, me).wait_send()
        for head in range(heads):
            q_copy(head, peer, me).wait_send()
            kv_copy(head, peer, me).wait_send()

    others(n, me, drain)
    others(batches, my_batch, lambda peer: pre_a(peer, my_batch).wait_send())
    others(batches, my_batch, lambda peer: vec_a(peer, my_batch).wait_send())
    reduce_core().wait_send()
    others(highs, my_high, lambda peer: reduce_x(peer, my_high).wait_send())
    reduce_y().wait_send()
    both_halves(reduce_near, my_place, lambda copy: copy.wait_send())
    both_halves(gather_near, my_place, lambda copy: copy.wait_send())
    reduce_far().wait_send()
    gather_far(my_plane).wait_send()
    gather_y(my_side).wait_send()
    others(highs, my_high, lambda peer: gather_x(peer, my_high).wait_send())
    gather_core(my_core).wait_send()
    mem_across().wait_send()
    mem_drain()
    others(planes, my_plane, lambda peer: vec_c(peer, my_plane).wait_send())
    vec_b(my_side).wait_send()
    save_full.wait()


def self_backward(
    n, batches, first_grad, out_grad, sums, mem_grads, mem_weights, vecs, saved, weights, prefix
):
    length, width = first_grad.shape
    group = width // n
    heads = group // HD
    whole = n * length
    planes = n // 2
    low = jnp.bfloat16
    f32 = jnp.float32
    vmem = pl.BlockSpec(memory_space=pltpu.VMEM)
    anywhere = pl.BlockSpec(memory_space=pl.ANY)
    dma = pltpu.SemaphoreType.DMA
    sum_rows = sums.shape[0] // (n * batches)
    mem_len = mem_grads[0].shape[0]
    mem_rows = mem_len // n
    mem_part = pltpu.VMEM((planes, mem_rows, width), low)
    mem_low = pltpu.VMEM((mem_len, width), low)
    square = pltpu.VMEM((width, width), low)
    vec = pltpu.VMEM((8, width), f32)
    copies = 8 + 2 * (batches // 2) + 5 * planes + 2 * batches + n
    qx, kx, raw, pk, pv, pkt, ot, stat = (pltpu.VMEM(value.shape, value.dtype) for value in saved)
    return pl.pallas_call(
        functools.partial(self_backward_kernel, n, batches),
        out_shape=(
            jax.ShapeDtypeStruct((length, width), low),
            jax.ShapeDtypeStruct((mem_rows, width), low),
            jax.ShapeDtypeStruct((PREFIX_ROWS, 2 * width), f32),
            jax.ShapeDtypeStruct((PREFIX_ROWS, prefix[0].shape[1]), f32),
            jax.ShapeDtypeStruct((PREFIX_ROWS, prefix[0].shape[1]), f32),
            jax.ShapeDtypeStruct((PREFIX_ROWS, width), f32),
            jax.ShapeDtypeStruct((8, width), f32),
            jax.ShapeDtypeStruct((2, batches // 2, 2, planes, sum_rows, LANES), low),
        ),
        in_specs=[anywhere] * 21 + [vmem] * 2,
        out_specs=(vmem,) * 7 + (anywhere,),
        scratch_shapes=[
            pltpu.VMEM((heads, n, HD, length), low),
            qx,
            kx,
            raw,
            pltpu.VMEM((heads, HD, whole), low),
            pltpu.VMEM((heads, whole, HD), low),
            pltpu.VMEM((heads, HD, whole), low),
            pltpu.VMEM((heads, whole, 2 * HD), low),
            pk,
            pv,
            pkt,
            ot,
            stat,
            pltpu.VMEM((3, width, width), low),
            pltpu.VMEM((planes, heads, HD, 2 * length), f32),
            pltpu.VMEM((heads, whole, 2 * HD), f32),
            pltpu.VMEM((n, heads, 3, HD, length), low),
            pltpu.VMEM((3, n, heads, HD, length), low),
            pltpu.VMEM((heads, PREFIX_ROWS, 2 * HD), f32),
            pltpu.VMEM((batches, heads, PREFIX_ROWS, 2 * HD), f32),
            pltpu.VMEM((heads, PREFIX_ROWS, 2 * HD), low),
            pltpu.VMEM((n, heads, PREFIX_ROWS, 2 * HD), low),
            pltpu.VMEM((sums.shape[0] // 2, LANES), low),
            pltpu.VMEM((sums.shape[0] // 2, LANES), low),
            pltpu.VMEM((batches // 2, sums.shape[0] // batches, LANES), low),
            pltpu.VMEM((planes * sum_rows, LANES), low),
            pltpu.VMEM((2, planes // 2, sum_rows, LANES), low),
            pltpu.VMEM((sum_rows, LANES), low),
            pltpu.VMEM((2, batches // 2, 2, planes, sum_rows, LANES), low),
            mem_low,
            mem_low,
            square,
            square,
            pltpu.VMEM((planes, 2, mem_rows, width), low),
            mem_part,
            mem_part,
            mem_part,
            pltpu.VMEM((batches, 8, width), f32),
            vec,
            pltpu.VMEM((2, 8, width), f32),
            pltpu.VMEM((16, width // 2), low),
            pltpu.VMEM((planes, 16, width // 2), low),
            pltpu.VMEM((width, length), f32),
            pltpu.VMEM(prefix[0].shape, low),
            pltpu.VMEM(prefix[1].shape, low),
            pltpu.VMEM((length, width), f32),
            dma((heads, n)),
            dma((heads, n)),
            dma((2, heads, n)),
            dma((2, heads, n)),
            dma((21,)),
            dma((copies,)),
            dma((copies,)),
        ],
        compiler_params=pltpu.CompilerParams(
            collective_id=1, has_side_effects=True, vmem_limit_bytes=VMEM_BYTES
        ),
        name="self_backward",
    )(
        first_grad,
        out_grad,
        sums.reshape(2, -1, LANES),
        *mem_grads,
        *mem_weights,
        vecs,
        *saved,
        *weights,
        *prefix,
    )


def finish_kernel(
    full_in,
    vecs_ref,
    pkv_ref,
    hidden_ref,
    hgrad_ref,
    embed_ref,
    emb_ref,
    token_in,
    mem_in,
    embed_out,
    first_out,
    fbias_out,
    second_out,
    sbias_out,
    down_out,
    dbias_out,
    raise_out,
    rbias_out,
    gain_out,
    shift_out,
    token_out,
    mem_out,
    full_ref,
    token_ref,
    mem_ref,
    first_grad,
    second_grad,
    down_grad,
    raise_grad,
    emb,
    out_sem,
    in_sem,
):
    f32 = jnp.float32
    low = jnp.bfloat16
    width = emb_ref.shape[1]
    down = dbias_out.shape[1]
    count = emb_ref.shape[0]
    first = down * width // LANES
    loads = [
        pltpu.make_async_copy(source, target, in_sem.at[index])
        for index, (source, target) in enumerate(
            (
                (full_in.at[first:], full_ref.at[first:]),
                (full_in.at[:first], full_ref.at[:first]),
                (token_in, token_ref),
                (mem_in, mem_ref),
            )
        )
    ]
    for load in loads:
        load.start()
    saves = []

    def save(source, target, rows=None):
        if rows is not None:
            source, target = source.at[rows], target.at[rows]
        copy = pltpu.make_async_copy(source, target, out_sem.at[len(saves)])
        copy.start()
        saves.append(copy)

    loads[0].wait()
    for index in range(width // LANES):
        raise_grad[:, index * LANES : (index + 1) * LANES] = full_ref[
            first + index * down : first + (index + 1) * down, :
        ].astype(f32)
    save(raise_grad, raise_out)
    loads[1].wait()
    for index in range(down // LANES):
        down_grad[:, index * LANES : (index + 1) * LANES] = full_ref[
            index * width : (index + 1) * width, :
        ].astype(f32)
    save(down_grad, down_out)
    for load in loads[2:]:
        load.wait()
    save(token_ref, token_out)
    save(mem_ref, mem_out)
    emb[...] = jnp.zeros_like(emb)
    emb[:count, :] = emb_ref[...].astype(f32)
    value = hidden_ref[...]
    prefix = pkv_ref[...]
    parts = both_parts(prefix)
    hidden_twice = jnp.concatenate([value, value], axis=0).T.astype(low)
    tile = 128
    for index in range(second_grad.shape[0] // tile):
        here = slice(index * tile, (index + 1) * tile)
        second_grad[here, :] = dot_nn(hidden_twice[here, :], parts)
        save(second_grad, second_out, here)
    sbias_out[...] = jnp.sum(prefix, axis=0, keepdims=True)
    grad = hgrad_ref[...]
    fbias_out[...] = jnp.sum(grad, axis=0, keepdims=True)
    parts = both_parts(grad)
    emb_twice = jnp.concatenate([emb[...], emb[...]], axis=0).T.astype(low)
    first_grad[...] = dot_nn(emb_twice, parts)
    save(first_grad, first_out)
    embed_out[...] = embed_ref[:count, :]
    rbias_out[...] = vecs_ref[0:1, :]
    dbias_out[...] = vecs_ref[1:2, :down]
    gain_out[...] = vecs_ref[2:5, :]
    shift_out[...] = vecs_ref[5:8, :]
    for copy in saves:
        copy.wait()


def finish(full, vecs, prefix_sums, embed, down, token_grad, memory_grad):
    f32 = jnp.float32
    count, width = embed.shape
    hidden = prefix_sums[1].shape[1]
    vmem = pl.BlockSpec(memory_space=pltpu.VMEM)
    anywhere = pl.BlockSpec(memory_space=pl.ANY)
    shapes = (
        (count, width),
        (width, hidden),
        (1, hidden),
        (hidden, 2 * width),
        (1, 2 * width),
        (width, down),
        (1, down),
        (down, width),
        (1, width),
        (3, width),
        (3, width),
    )
    return pl.pallas_call(
        finish_kernel,
        out_shape=tuple(jax.ShapeDtypeStruct(shape, f32) for shape in shapes)
        + tuple(
            jax.ShapeDtypeStruct(value.shape, value.dtype) for value in (token_grad, memory_grad)
        ),
        in_specs=[anywhere] + [vmem] * 6 + [anywhere] * 2,
        out_specs=(
            vmem,
            anywhere,
            vmem,
            anywhere,
            vmem,
            anywhere,
            vmem,
            anywhere,
            vmem,
            vmem,
            vmem,
            anywhere,
            anywhere,
        ),
        scratch_shapes=[
            pltpu.VMEM(full.shape, jnp.bfloat16),
            pltpu.VMEM(token_grad.shape, token_grad.dtype),
            pltpu.VMEM(memory_grad.shape, memory_grad.dtype),
            pltpu.VMEM((width, hidden), f32),
            pltpu.VMEM((hidden, 2 * width), f32),
            pltpu.VMEM((width, down), f32),
            pltpu.VMEM((down, width), f32),
            pltpu.VMEM((PREFIX_ROWS, width), f32),
            pltpu.SemaphoreType.DMA((5 + hidden // 128,)),
            pltpu.SemaphoreType.DMA((4,)),
        ],
        compiler_params=pltpu.CompilerParams(vmem_limit_bytes=VMEM_BYTES),
        name="finish",
    )(full, vecs, *prefix_sums, embed, token_grad, memory_grad)


def gelu_pair(value):
    size = jnp.abs(value)
    step = 1.0 / (1.0 + (0.3275911 * 0.7071067811865476) * size)
    bell = jnp.exp(-0.5 * value * value)
    poly = step * (
        0.127414796
        + step
        * (-0.142248368 + step * (0.7107068705 + step * (-0.7265760135 + step * 0.5307027145)))
    )
    act = jnp.maximum(value, 0.0) - size * (poly * bell)
    turn = bell * (0.3989422804014327 * size - poly)
    return act, jnp.where(value >= 0.0, 1.0 + turn, -turn)


def normed(value):
    center = jnp.mean(value, axis=-1, keepdims=True)
    centered = value - center
    scale = lax.rsqrt(jnp.mean(centered * centered, axis=-1, keepdims=True) + norm_eps)
    return centered * scale, scale


def norm_back(grad, scale, unit):
    return scale * (
        grad
        - jnp.mean(grad, axis=-1, keepdims=True)
        - unit * jnp.mean(grad * unit, axis=-1, keepdims=True)
    )


def middle_kernel(
    tok_in,
    att_in,
    cot_in,
    mkey_in,
    mvalue_in,
    gain_ref,
    shift_ref,
    dbias_ref,
    rbias_ref,
    wo_in,
    wcq_in,
    wco_in,
    wd_in,
    wr_in,
    win_in,
    wout_in,
    layer_out,
    fgrad_out,
    ograd_out,
    mkey_out,
    mvalue_out,
    sums_out,
    vecs_ref,
    tok_ref,
    att_ref,
    cot_ref,
    mkey_ref,
    mvalue_ref,
    out_ref,
    fgrad_ref,
    ograd_ref,
    sums_ref,
    wo,
    wcq,
    wco,
    wd,
    wr,
    win,
    wout,
    unit_one,
    unit_two,
    work,
    total,
    scale_one,
    scale_two,
    low_one,
    low_two,
    low_three,
    query,
    crossed,
    weights,
    slopes,
    acts,
    down_act,
    down_slope,
    down_grad,
    load_sem,
    win_sem,
    wout_sem,
    out_sem,
):
    length, width = tok_ref.shape
    resident = len(win.shape) == 2
    tile = 512 if resident else win.shape[2]
    tiles = win_in.shape[1] // tile
    slots = tiles if resident else win.shape[0]
    rows_step = length // 2
    low = jnp.bfloat16
    f32 = jnp.float32

    sources = (
        att_in,
        wo_in,
        tok_in,
        wcq_in,
        mkey_in,
        mvalue_in,
        wco_in,
        wd_in,
        wr_in,
        cot_in,
    )
    targets = (att_ref, wo, tok_ref, wcq, mkey_ref, mvalue_ref, wco, wd, wr, cot_ref)
    loads = [
        pltpu.make_async_copy(source, target, load_sem.at[index])
        for index, (source, target) in enumerate(zip(sources, targets))
    ]

    def win_load(which):
        slot = which % slots
        target = win.at[:, rows_of(which, tile)] if resident else win.at[slot]
        return pltpu.make_async_copy(win_in.at[:, rows_of(which, tile)], target, win_sem.at[slot])

    def wout_load(which):
        slot = which % slots
        target = wout.at[rows_of(which, tile), :] if resident else wout.at[slot]
        return pltpu.make_async_copy(wout_in.at[rows_of(which, tile), :], target, wout_sem.at[slot])

    for load in loads[:7]:
        load.start()

    def by_columns(extent, step, body):
        def one(index, carry):
            body(pl.ds(pl.multiple_of(index * step, step), step))
            return carry

        lax.fori_loop(0, extent // step, one, 0)

    def by_rows(body, init=0):
        def one(index, carry):
            return body(rows_of(index, rows_step), carry)

        return lax.fori_loop(0, length // rows_step, one, init)

    cols = 512
    half = width // 2

    for load in loads[:3]:
        load.wait()
    for load in loads[7:]:
        load.start()
    for which in range(slots):
        win_load(which).start()
    for which in range(slots):
        wout_load(which).start()

    def project_out(here):
        work[:, here] = tok_ref[:, here].astype(f32) + dot_nn(att_ref[...], wo[:, here])

    by_columns(width, cols, project_out)

    def first_norm(here, carry):
        unit, scale = normed(work[here, :])
        unit_one[here, :] = unit
        scale_one[here, :] = scale
        value = unit * gain_ref[0:1, :] + shift_ref[0:1, :]
        work[here, :] = value
        low_one[here, :] = value.astype(low)
        return carry

    by_rows(first_norm)

    loads[3].wait()

    def project_query(here):
        query[:, here] = dot_nn(low_one[...], wcq[:, here]).astype(low)

    by_columns(width, cols, project_query)
    per_block = LANES // HD

    def stacked(value):
        return jnp.concatenate(
            [jnp.where(head_lanes(value.shape, head), value, 0.0) for head in range(per_block)],
            axis=0,
        ).astype(low)

    def unstacked(value):
        return jnp.concatenate(
            [
                value[head * HD : (head + 1) * HD, head * length : (head + 1) * length]
                for head in range(per_block)
            ],
            axis=0,
        )

    def block_queries(here):
        return stacked(query[:, here].astype(f32) * 0.125)

    def cross_forward(block):
        here = rows_of(block, LANES)
        scores = dot_nt(mkey_ref[:, here], block_queries(here))
        raised = jnp.exp(scores - jnp.max(scores, axis=0, keepdims=True))
        share = 1.0 / jnp.sum(raised, axis=0, keepdims=True)
        weight = (raised * share).astype(low)
        weights[block] = weight
        values = mvalue_ref[:, here].astype(f32).T.astype(low)
        crossed[:, here] = unstacked(dot_nn(values, weight)).T.astype(low)

    loads[4].wait()
    loads[5].wait()

    def cross_forward_four(step, carry):
        for part in range(4):
            cross_forward(4 * step + part)
        return carry

    lax.fori_loop(0, width // LANES // 4, cross_forward_four, 0)

    loads[6].wait()

    def project_crossed(here):
        work[:, here] += dot_nn(crossed[...], wco[:, here])

    by_columns(width, cols, project_crossed)

    def second_norm(here, carry):
        unit, scale = normed(work[here, :])
        unit_two[here, :] = unit
        scale_two[here, :] = scale
        value = unit * gain_ref[1:2, :] + shift_ref[1:2, :]
        work[here, :] = value
        low_two[here, :] = value.astype(low)
        return carry

    by_rows(second_norm)

    step_cols = 512

    def feed_part(here, source):
        act, slope = gelu_pair(dot_nn(low_two[...], source))
        slopes[:, here] = slope.astype(low)
        return act.astype(low)

    if resident:

        def feed_forward(which, carry):
            here = rows_of(which, step_cols)

            @pl.when(which % (tile // step_cols) == 0)
            def _():
                win_load(which // (tile // step_cols)).wait()

            acts[:, here] = feed_part(here, win[:, here])
            return carry

        lax.fori_loop(0, tiles * tile // step_cols, feed_forward, 0)
        for which in range(tiles):
            wout_load(which).wait()

        def feed_out_part(here):
            total[:, here] = dot_nn(acts[...], wout[:, here])

        by_columns(width, step_cols, feed_out_part)
    else:
        total[...] = jnp.zeros_like(total)

        def feed_forward(which, carry):
            slot = lax.rem(which, slots)
            win_load(which).wait()
            wout_load(which).wait()
            total[...] += dot_nn(feed_part(rows_of(which, tile), win[slot]), wout[slot])

            @pl.when(which + slots < tiles)
            def _():
                win_load(which + slots).start()
                wout_load(which + slots).start()

            return carry

        lax.fori_loop(0, tiles, feed_forward, 0)

    loads[7].wait()
    loads[8].wait()
    loads[9].wait()
    act, slope = gelu_pair(dot_nn(low_two[...], wd[...]) + dbias_ref[...])
    down_act[...] = act.astype(low)
    down_slope[...] = slope.astype(low)

    def project_raise(here):
        work[:, here] += total[:, here] + 4.0 * (
            dot_nn(down_act[...], wr[:, here]) + rbias_ref[:, here]
        )

    by_columns(width, cols, project_raise)
    nothing = jnp.zeros((1, width), f32)

    def third_norm(here, carry):
        gain_sum, shift_sum, bias_sum = carry
        unit, scale = normed(work[here, :])
        gain = gain_ref[2:3, :]
        out_ref[here, :] = (unit * gain + shift_ref[2:3, :]).astype(low)
        grad = cot_ref[here, :].astype(f32)
        back = norm_back(grad * gain, scale, unit)
        total[here, :] = back
        back_low = back.astype(low)
        low_three[here, :] = back_low
        return (
            gain_sum + jnp.sum(grad * unit, axis=0, keepdims=True),
            shift_sum + jnp.sum(grad, axis=0, keepdims=True),
            bias_sum + jnp.sum(back_low.astype(f32), axis=0, keepdims=True),
        )

    gain_three, shift_three, bias_sum = by_rows(third_norm, (nothing, nothing, nothing))
    saves = []

    def save(source, target):
        copy = pltpu.make_async_copy(source, target, out_sem.at[len(saves)])
        copy.start()
        saves.append(copy)

    save(out_ref, layer_out)
    vecs_ref[0:1, :] = 4.0 * bias_sum

    back = 4.0 * dot_nt(low_three[...], wr[...]) * down_slope[...].astype(f32)
    back_low = back.astype(low)
    down_grad[...] = back_low
    vecs_ref[1:2, :] = jnp.concatenate(
        [
            jnp.sum(back_low.astype(f32), axis=0, keepdims=True),
            jnp.zeros((1, width - wd.shape[1]), f32),
        ],
        axis=1,
    )
    down = wd.shape[1]
    raise_sum = 4.0 * dot_tn(down_act[...], low_three[...])
    for index in range(width // LANES):
        sums_ref[pl.ds(down * width // LANES + index * down, down), :] = raise_sum[
            :, index * LANES : (index + 1) * LANES
        ].astype(low)
    down_sum = dot_tn(low_two[...], down_grad[...])
    for index in range(down // LANES):
        sums_ref[index * width : (index + 1) * width, :] = down_sum[
            :, index * LANES : (index + 1) * LANES
        ].astype(low)

    save(sums_ref, sums_out)

    if resident:

        def feed_slope(here):
            acts[:, here] = (
                dot_nt(low_three[...], wout[here, :]) * slopes[:, here].astype(f32)
            ).astype(low)

        by_columns(win_in.shape[1], step_cols, feed_slope)

        def feed_in_part(here):
            total[:, here] += dot_nt(acts[...], win[here, :])

        by_columns(width, step_cols, feed_in_part)
    else:

        def feed_backward(step, carry):
            which = tiles - 1 - step
            slot = lax.rem(which, slots)
            here = rows_of(which, tile)

            @pl.when(which < tiles - slots)
            def _():
                wout_load(which).wait()
                win_load(which).wait()

            grad = dot_nt(low_three[...], wout[slot]) * slopes[:, here].astype(f32)
            total[...] += dot_nt(grad.astype(low), win[slot])

            @pl.when(which >= slots)
            def _():
                win_load(which - slots).start()
                wout_load(which - slots).start()

            return carry

        lax.fori_loop(0, tiles, feed_backward, 0)

    def down_back(here):
        total[:, here] += dot_nt(down_grad[...], wd[here, :])

    by_columns(width, cols, down_back)

    def second_back(here, carry):
        gain_sum, shift_sum = carry
        grad = total[here, :]
        unit = unit_two[here, :]
        back = norm_back(grad * gain_ref[1:2, :], scale_two[here, :], unit)
        total[here, :] = back
        low_one[here, :] = back.astype(low)
        return (
            gain_sum + jnp.sum(grad * unit, axis=0, keepdims=True),
            shift_sum + jnp.sum(grad, axis=0, keepdims=True),
        )

    gain_two, shift_two = by_rows(second_back, (nothing, nothing))

    def crossed_back(here):
        crossed[:, here] = dot_nt(low_one[...], wco[here, :]).astype(low)

    by_columns(width, cols, crossed_back)

    def cross_backward(block):
        here = rows_of(block, LANES)
        grads = stacked(crossed[:, here].astype(f32))
        keys = mkey_ref[:, here].astype(f32).T.astype(low)
        slope = dot_nt(mvalue_ref[:, here], grads)
        weight_low = weights[block]
        weight = weight_low.astype(f32)
        slope = weight * (slope - jnp.sum(weight * slope, axis=0, keepdims=True))
        slope = slope.astype(low)
        queries = block_queries(here)
        mkey_ref[:, here] = dot_nn(slope, queries).astype(low)
        mvalue_ref[:, here] = dot_nn(weight_low, grads).astype(low)
        query[:, here] = (unstacked(dot_nn(keys, slope)) * 0.125).T.astype(low)

    def cross_backward_four(step, carry):
        for part in range(4):
            cross_backward(4 * step + part)
        return carry

    lax.fori_loop(0, width // LANES // 4, cross_backward_four, 0)
    save(mkey_ref, mkey_out)
    save(mvalue_ref, mvalue_out)

    def query_back(here):
        total[:, here] += dot_nt(query[...], wcq[here, :])

    by_columns(width, cols, query_back)

    def first_back(here, carry):
        gain_sum, shift_sum = carry
        grad = total[here, :]
        unit = unit_one[here, :]
        back = norm_back(grad * gain_ref[0:1, :], scale_one[here, :], unit)
        fgrad_ref[here, :] = back
        low_one[here, :] = back.astype(low)
        return (
            gain_sum + jnp.sum(grad * unit, axis=0, keepdims=True),
            shift_sum + jnp.sum(grad, axis=0, keepdims=True),
        )

    gain_one, shift_one = by_rows(first_back, (nothing, nothing))
    save(fgrad_ref, fgrad_out)

    for index in range(width // cols):
        here = slice(index * cols, (index + 1) * cols)
        ograd_ref[here, :] = dot_nt(low_one[...], wo[here, :]).T.astype(low)
        save(ograd_ref.at[here], ograd_out.at[here])
    for index, vector in enumerate(
        (gain_one, gain_two, gain_three, shift_one, shift_two, shift_three)
    ):
        vecs_ref[2 + index : 3 + index, :] = vector
    for copy in saves:
        copy.wait()


def middle(
    tokens, attended, cotangent, mem_key, mem_value, gains, shifts, down_bias, raise_bias, weights
):
    length, width = tokens.shape
    mem_len = mem_key.shape[0]
    down = weights[3].shape[1]
    feed = weights[5].shape[1]
    tile = 512 if mem_len <= 512 else 128
    resident = mem_len <= 512
    slots = feed // tile if resident else 2
    low = jnp.bfloat16
    f32 = jnp.float32
    vmem = pl.BlockSpec(memory_space=pltpu.VMEM)
    anywhere = pl.BlockSpec(memory_space=pl.ANY)
    square = pltpu.VMEM((width, width), low)
    wide = pltpu.VMEM((length, width), f32)
    narrow = pltpu.VMEM((length, width), low)
    return pl.pallas_call(
        middle_kernel,
        out_shape=(
            jax.ShapeDtypeStruct((length, width), low),
            jax.ShapeDtypeStruct((length, width), f32),
            jax.ShapeDtypeStruct((width, length), low),
            jax.ShapeDtypeStruct((mem_len, width), low),
            jax.ShapeDtypeStruct((mem_len, width), low),
            jax.ShapeDtypeStruct((2 * down * width // LANES, LANES), low),
            jax.ShapeDtypeStruct((8, width), f32),
        ),
        in_specs=[anywhere] * 5 + [vmem] * 4 + [anywhere] * 7,
        out_specs=(anywhere,) * 6 + (vmem,),
        scratch_shapes=[
            narrow,
            narrow,
            narrow,
            pltpu.VMEM((mem_len, width), low),
            pltpu.VMEM((mem_len, width), low),
            narrow,
            wide,
            pltpu.VMEM((width, length), low),
            pltpu.VMEM((2 * down * width // LANES, LANES), low),
            square,
            square,
            square,
            pltpu.VMEM((width, down), low),
            pltpu.VMEM((down, width), low),
            pltpu.VMEM((width, feed) if resident else (slots, width, tile), low),
            pltpu.VMEM((feed, width) if resident else (slots, tile, width), low),
            wide,
            wide,
            wide,
            wide,
            pltpu.VMEM((length, 1), f32),
            pltpu.VMEM((length, 1), f32),
            narrow,
            narrow,
            narrow,
            narrow,
            narrow,
            pltpu.VMEM((width // LANES, mem_len, LANES // HD * length), low),
            pltpu.VMEM((length, feed), low),
            pltpu.VMEM((length, feed) if resident else (16, LANES), low),
            pltpu.VMEM((length, down), low),
            pltpu.VMEM((length, down), low),
            pltpu.VMEM((length, down), low),
            pltpu.SemaphoreType.DMA((10,)),
            pltpu.SemaphoreType.DMA((slots,)),
            pltpu.SemaphoreType.DMA((slots,)),
            pltpu.SemaphoreType.DMA((5 + width // 512,)),
        ],
        compiler_params=pltpu.CompilerParams(vmem_limit_bytes=VMEM_BYTES + 3 * 1024 * 1024),
        name="middle",
    )(tokens, attended, cotangent, mem_key, mem_value, gains, shifts, down_bias, raise_bias, *weights)


def per_device(
    tokens,
    memory,
    segment_ids,
    padding_mask,
    cotangent,
    prefix_embed,
    prefix_first,
    first_bias,
    prefix_second,
    second_bias,
    adapter_down,
    down_bias,
    adapter_raise,
    raise_bias,
    norm_gain,
    norm_shift,
    self_query,
    self_key,
    self_value,
    self_output,
    cross_query,
    cross_key,
    cross_value,
    cross_output,
    feed_in,
    feed_out,
):
    row_count, length, model_width = tokens.shape
    flat_rows = row_count * length
    n = lax.axis_size("seq")
    batches = lax.axis_size("batch")
    down = adapter_down.shape[1]
    attended, mem_key, mem_value, *saved = self_forward(
        n,
        segment_ids,
        padding_mask,
        tokens.reshape(flat_rows, model_width),
        (self_query, self_key, self_value),
        (
            prefix_embed,
            prefix_first,
            first_bias.reshape(1, -1),
            prefix_second,
            second_bias.reshape(1, -1),
        ),
        memory.reshape(-1, model_width),
        (cross_key, cross_value),
    )
    layer_output, first_grad, out_grad, *mem_grads, weight_sums, vector_sums = middle(
        tokens.reshape(flat_rows, model_width),
        attended,
        cotangent.reshape(flat_rows, model_width),
        mem_key,
        mem_value,
        norm_gain,
        norm_shift,
        down_bias.reshape(1, -1),
        raise_bias.reshape(1, -1),
        (
            self_output,
            cross_query,
            cross_output,
            adapter_down,
            adapter_raise,
            feed_in,
            feed_out,
        ),
    )
    layer_output = layer_output.reshape(row_count, length, model_width)
    token_grad, memory_grad, *prefix_sums, vector_sums, full_sums = self_backward(
        n,
        batches,
        first_grad,
        out_grad.reshape(n, -1, HD, length),
        weight_sums,
        mem_grads,
        (cross_key, cross_value),
        vector_sums,
        saved,
        (self_query, self_key, self_value),
        (prefix_first, prefix_second, prefix_embed, first_bias.reshape(1, -1)),
    )
    *replicated, token_grad, memory_grad = finish(
        full_sums.reshape(-1, LANES),
        vector_sums,
        prefix_sums,
        prefix_embed,
        down,
        token_grad,
        memory_grad,
    )
    token_grad = token_grad.reshape(row_count, length, model_width)
    memory_grad = memory_grad.reshape(memory.shape)
    replicated = [
        value.reshape(-1) if value.shape[0] == 1 else value for value in replicated
    ]
    return (layer_output, token_grad, memory_grad, *replicated)


def solution(mesh):
    placed = (
        P("batch", "seq", None),
        P("batch", "seq", None),
        P("batch", "seq"),
        P("batch", "seq"),
        P("batch", "seq", None),
        P(),
        P(),
        P(),
        P(),
        P(),
        P(),
        P(),
        P(),
        P(),
        P(),
        P(),
        P(),
        P(),
        P(),
        P(),
        P(),
        P(),
        P(),
        P(),
        P(),
        P(),
    )
    return jax.shard_map(
        per_device,
        mesh=mesh,
        in_specs=placed,
        out_specs=(
            P("batch", "seq", None),
            P("batch", "seq", None),
            P("batch", "seq", None),
            P(),
            P(),
            P(),
            P(),
            P(),
            P(),
            P(),
            P(),
            P(),
            P(),
            P(),
        ),
        check_vma=False,
    )
```

```python
import functools

import jax
import jax.numpy as jnp
from jax import lax
from jax.experimental import pallas as pl
from jax.experimental.pallas import tpu as pltpu
from jax.sharding import PartitionSpec as P

H = 16
HD = 64
LANES = 128
PREFIX_ROWS = 32
VMEM_BYTES = 60 * 1024 * 1024
SUM_ROWS = 16
MESH = pl.DeviceIdType.MESH

masked_score = -1e30
norm_eps = 1e-05

def dot_nn(left, right):
    return lax.dot_general(
        left, right, (((1,), (0,)), ((), ())), preferred_element_type=jnp.float32
    )


def dot_nt(left, right):
    return lax.dot_general(
        left, right, (((1,), (1,)), ((), ())), preferred_element_type=jnp.float32
    )


def dot_tn(left, right):
    return lax.dot_general(
        left, right, (((0,), (0,)), ((), ())), preferred_element_type=jnp.float32
    )


def remote(source, target, send_sem, recv_sem, axis, peer):
    return pltpu.make_async_remote_copy(
        src_ref=source,
        dst_ref=target,
        send_sem=send_sem,
        recv_sem=recv_sem,
        device_id={axis: peer},
        device_id_type=MESH,
    )


def enter(sizes):
    barrier = pltpu.get_barrier_semaphore()
    for axis, size in sizes.items():
        for other in range(size):

            @pl.when(other != lax.axis_index(axis))
            def _():
                pl.semaphore_signal(barrier, inc=1, device_id={axis: other}, device_id_type=MESH)

    pl.semaphore_wait(barrier, sum(sizes.values()) - len(sizes))


def others(size, mine, body):
    for other in range(size):

        @pl.when(other != mine)
        def _():
            body(other)


def rows_of(index, size):
    return pl.ds(pl.multiple_of(index * size, size), size)


def span_of(start, size):
    return pl.ds(pl.multiple_of(start, LANES), size)


def own_columns(ref, first, me, width):
    if width % LANES == 0:
        return ref[:, pl.ds(pl.multiple_of(first + me * width, LANES), width)].astype(jnp.float32)
    share = LANES // width
    block = ref[:, pl.ds(pl.multiple_of(first + me // share * LANES, LANES), LANES)].astype(
        jnp.float32
    )
    picked = block[:, :width]
    for part in range(1, share):
        picked = jnp.where(me % share == part, block[:, part * width : (part + 1) * width], picked)
    return picked


def head_lanes(shape, head):
    lane = lax.broadcasted_iota(jnp.int32, shape, 1)
    return (lane >= head * HD) & (lane < (head + 1) * HD)


def self_forward_kernel(
    n,
    seg_ref,
    pad_ref,
    tok_ref,
    wq_in,
    wk_in,
    wv_in,
    emb_ref,
    first_in,
    fbias_ref,
    second_in,
    sbias_ref,
    mem_ref,
    wck_in,
    wcv_in,
    att_ref,
    mkey_out,
    mvalue_out,
    qx_out,
    kx_out,
    raw_out,
    pk_out,
    pv_out,
    pkt_out,
    ot_out,
    lse_out,
    send,
    recv,
    meta_send,
    meta,
    kx,
    qx,
    vt,
    hidden,
    pk,
    pv,
    pkt,
    pvt,
    stat,
    acc,
    o_send,
    o_recv,
    mem_all,
    wck,
    wcv,
    mkey_ref,
    mvalue_ref,
    wq_ref,
    wk_ref,
    wv_ref,
    first_ref,
    second_ref,
    send_sem,
    recv_sem,
    meta_send_sem,
    meta_recv_sem,
    o_send_sem,
    o_recv_sem,
    mem_send_sem,
    mem_recv_sem,
    out_sem,
    weight_sem,
    in_sem,
):
    low = jnp.bfloat16
    f32 = jnp.float32
    me = lax.axis_index("seq")
    length, width = tok_ref.shape
    group = width // n
    heads = group // HD
    plane = 2 * length
    planes = n // 2
    block = 2 * LANES
    per_block = block // group
    blocks = width // block
    my_plane = me // 2
    my_side = lax.rem(me, 2)

    upward = my_plane >= planes // 2
    turn_sign = jnp.where(upward, 1, -1)

    def plane_after(step):
        return lax.rem(my_plane + planes + turn_sign * step, planes)

    def meta_copy(peer, slot):
        return remote(
            meta_send, meta.at[slot], meta_send_sem.at[peer], meta_recv_sem.at[slot], "seq", peer
        )

    def qkv_copy(head, peer, slot):
        return remote(
            send.at[peer, head],
            recv.at[head, slot],
            send_sem.at[head, peer],
            recv_sem.at[head, slot],
            "seq",
            peer,
        )

    def out_copy(head, peer, slot):
        return remote(
            o_send.at[head, peer],
            o_recv.at[slot, head],
            o_send_sem.at[head, peer],
            o_recv_sem.at[head, slot],
            "seq",
            peer,
        )

    def mem_along(which, toward):
        part = mem_all.at[which, my_side]
        return remote(
            part,
            part,
            mem_send_sem.at[(toward + 1) // 2, which],
            mem_recv_sem.at[which],
            "seq",
            me + 2 * toward,
        )

    def mem_across(side):
        part = mem_all.at[:, side]
        return remote(
            part,
            part,
            mem_send_sem.at[0, planes],
            mem_recv_sem.at[planes],
            "seq",
            me + 1 - 2 * my_side,
        )

    def mem_hops(hop, body):
        for toward in (1, -1):
            which = my_plane - toward * hop
            ahead = my_plane + toward

            @pl.when((which >= 0) & (which < planes) & (ahead >= 0) & (ahead < planes))
            def _():
                body(mem_along(which, toward))

    def mem_arrivals(hop):
        for toward in (1, -1):
            which = my_plane - toward * hop

            @pl.when((which >= 0) & (which < planes))
            def _():
                mem_along(which, -toward).wait_recv()

    def block_at(step):
        if blocks >= planes:
            share = blocks // planes
            return plane_after(1 + step // share) * share + step % share
        return lax.rem(me // per_block + 1 + step, blocks)

    def weight_load(step, which):
        columns = rows_of(block_at(step), block)
        source = (wq_in, wk_in, wv_in)[which]
        target = (wq_ref, wk_ref, wv_ref)[which]
        return pltpu.make_async_copy(
            source.at[:, columns], target.at[:, columns], weight_sem.at[step, which]
        )

    for step in range(blocks):
        for which in range(3):
            weight_load(step, which).start()
    loads = [
        pltpu.make_async_copy(source, target, in_sem.at[index])
        for index, (source, target) in enumerate(
            ((first_in, first_ref), (second_in, second_ref), (wck_in, wck), (wcv_in, wcv))
        )
    ]
    for load in loads:
        load.start()
    segments = seg_ref[...]
    tags = jnp.where(pad_ref[...] == 1, segments, -1)
    row = lax.broadcasted_iota(jnp.int32, meta_send.shape, 0)
    meta_send[...] = jnp.where(row == 0, segments, tags)
    mem_all[my_plane, my_side] = mem_ref[...]
    enter({"seq": n})
    others(n, me, lambda peer: meta_copy(peer, me).start())
    meta[me] = meta_send[...]

    for step in range(blocks):
        at = block_at(step)
        columns = rows_of(at, block)
        for which, weight in enumerate((wq_ref, wk_ref, wv_ref)):
            weight_load(step, which).wait()
            piece = dot_nn(tok_ref[...], weight[:, columns]).T.astype(low)
            for part in range(per_block):
                for head in range(heads):
                    first = part * group + head * HD
                    send[at * per_block + part, head, which] = piece[first : first + HD]
        for part in range(per_block):
            peer = at * per_block + part

            @pl.when(peer != me)
            def _():
                qkv_copy(0, peer, me).start()

            @pl.when(peer == me)
            def _():
                for head in range(heads):
                    recv[head, me] = send[peer, head]

    mem_hops(0, lambda copy: copy.start())
    loads[0].wait()
    loads[1].wait()
    hidden[...] = jnp.zeros_like(hidden)
    hidden[: emb_ref.shape[0], :] = jnp.tanh(dot_nn(emb_ref[...], first_ref[...]) + fbias_ref[...])
    hidden_low = hidden[...].astype(low)
    prefix_key = dot_nn(hidden_low, own_columns(second_ref, 0, me, group).astype(low)) + own_columns(
        sbias_ref, 0, me, group
    )
    prefix_value = dot_nn(
        hidden_low, own_columns(second_ref, width, me, group).astype(low)
    ) + own_columns(sbias_ref, width, me, group)
    prefix_row = lax.broadcasted_iota(jnp.int32, (PREFIX_ROWS, HD), 0)
    prefix_open = jnp.where(prefix_row < emb_ref.shape[0], 0.0, masked_score)
    for head in range(heads):
        here = slice(head * HD, (head + 1) * HD)
        pk[head] = jnp.concatenate([prefix_key[:, here], prefix_open], axis=1).astype(low)
        pv[head] = prefix_value[:, here].astype(low)
    pkt[...] = prefix_key.T.astype(low).reshape(heads, HD, PREFIX_ROWS)
    pvt[:, :HD, :] = prefix_value.T.astype(low).reshape(heads, HD, PREFIX_ROWS)
    pvt[:, HD:, :] = jnp.ones((heads, SUM_ROWS, PREFIX_ROWS), low)
    vt[:, HD:, :] = jnp.ones((heads, SUM_ROWS, n * length), low)

    def arrive(head, chunk):
        @pl.when(chunk != me)
        def _():
            @pl.when(head == 0)
            def _():
                meta_copy(chunk, chunk).wait_recv()

            qkv_copy(head, chunk, chunk).wait_recv()

        here = rows_of(chunk, length)
        state = lax.broadcasted_iota(jnp.int32, (HD, length), 0)
        qx[head, :HD, here] = (recv[head, chunk, 0].astype(f32) * 0.125).astype(low)
        qx[head, HD:, here] = jnp.where(state == meta[chunk, 0:1, :], 1.0, 0.0).astype(low)
        is_open = jnp.where(state == meta[chunk, 1:2, :], 0.0, masked_score)
        kx[head, here, :] = jnp.concatenate(
            [recv[head, chunk, 1].astype(f32), is_open], axis=0
        ).T.astype(low)
        vt[head, :HD, here] = recv[head, chunk, 2]

    def open_plane(head, which):
        scores = dot_nn(pk[head], qx[head, :, rows_of(which, plane)])
        top = jnp.max(scores, axis=0, keepdims=True)
        raised = jnp.exp(scores - top)
        stat[which, head, 0:1, :] = top
        acc[which, head] = dot_nn(pvt[head], raised.astype(low))

    def pair_part(head, upper, lower, first, count, keys, diagonal):
        here = slice(first, first + count)
        queries = qx[head, :, span_of(upper * plane + first, count)]
        key_rows = span_of(lower * plane, keys)
        scores = dot_nn(kx[head, key_rows, :], queries)
        if diagonal:
            key_at = lax.broadcasted_iota(jnp.int32, scores.shape, 0)
            query_at = lax.broadcasted_iota(jnp.int32, scores.shape, 1) + first
            scores = jnp.where(key_at <= query_at, scores, masked_score)
        old_top = stat[upper, head, 0:1, here]
        top = jnp.maximum(old_top, jnp.max(scores, axis=0, keepdims=True))
        raised = jnp.exp(scores - top).astype(low)
        stat[upper, head, 0:1, here] = top
        acc[upper, head, :, here] = acc[upper, head, :, here] * jnp.exp(old_top - top) + dot_nn(
            vt[head, :, key_rows], raised
        )

    def pair(head, upper, lower):
        pair_part(head, upper, lower, 0, plane, plane, False)

    def pair_diagonal(head, which):
        for part in range(2):
            pair_part(head, which, which, part * length, length, (part + 1) * length, True)

    def close_plane(head, which):
        total = acc[which, head, HD : HD + 1, :]
        value = acc[which, head, :HD, :] / total
        acc[which, head, :HD, :] = value
        stat[which, head, 0:1, :] = stat[which, head, 0:1, :] + jnp.log(total)
        for part in range(2):
            chunk = 2 * which + part
            o_send[head, chunk] = value[:, part * length : (part + 1) * length].astype(low)

            @pl.when((chunk != me) & (head == heads - 1))
            def _():
                out_copy(head, chunk, me).start()

            @pl.when(chunk == me)
            def _():
                o_recv[me, head] = o_send[head, chunk]

    def project_memory():
        mem_across(1 - my_side).wait_recv()
        for load in loads[2:]:
            load.wait()
        whole = mem_all[...].reshape(mkey_ref.shape)

        def one(index, carry):
            here = rows_of(index, block)
            mkey_ref[:, here] = dot_nn(whole, wck[:, here]).astype(low)
            mvalue_ref[:, here] = dot_nn(whole, wcv[:, here]).astype(low)
            return carry

        lax.fori_loop(0, blocks, one, 0)

    def stage(index, carry):
        head = index // planes
        step = lax.rem(index, planes)

        @pl.when(head + 1 < heads)
        def _():
            there = plane_after(1 + step)
            for part in range(2):
                peer = 2 * there + part

                @pl.when(peer != me)
                def _():
                    qkv_copy(head, peer, me).wait_send()
                    qkv_copy(head + 1, peer, me).start()

        @pl.when((head == heads - 1) & (head > 0))
        def _():
            there = plane_after(1 + step)
            for part in range(2):
                peer = 2 * there + part

                @pl.when(peer != me)
                def _():
                    qkv_copy(head, peer, me).wait_send()
                    out_copy(head - 1, peer, me).start()

        here = plane_after(step)
        arrive(head, 2 * here)
        arrive(head, 2 * here + 1)
        open_plane(head, here)
        pair_diagonal(head, here)

        def earlier(back, inner):
            there = plane_after(back)
            pair(head, jnp.maximum(here, there), jnp.minimum(here, there))

            @pl.when((step == planes - 1) & (there > here))
            def _():
                close_plane(head, there)

            return inner

        lax.fori_loop(0, step, earlier, 0)
        for hop in range(1, planes - 1):

            @pl.when(index == hop)
            def _():
                mem_arrivals(hop)
                mem_hops(hop, lambda copy: copy.start())

        @pl.when(index == planes - 1)
        def _():
            mem_arrivals(planes - 1)
            mem_across(my_side).start()

        @pl.when((upward & (my_plane + step >= planes)) | (step == planes - 1))
        def _():
            close_plane(head, here)

        @pl.when(jnp.logical_not(upward) & (step == my_plane))
        def _():
            def close(which, inner):
                close_plane(head, which)
                return inner

            lax.fori_loop(0, my_plane + 1, close, 0)

        return carry

    lax.fori_loop(0, heads * planes, stage, 0)

    saves = []

    def save(source, target):
        copy = pltpu.make_async_copy(source, target, out_sem.at[len(saves)])
        copy.start()
        saves.append(copy)

    save(qx, qx_out)
    save(kx, kx_out)
    save(recv, raw_out)
    save(pk, pk_out)
    save(pv, pv_out)
    save(pkt, pkt_out)
    save(acc, ot_out)
    save(stat, lse_out)
    project_memory()
    save(mkey_ref, mkey_out)
    save(mvalue_ref, mvalue_out)
    for other in range(n):

        @pl.when(other != me)
        def _():
            for head in range(heads):
                out_copy(head, other, other).wait_recv()

        att_ref[:, other * group : (other + 1) * group] = (
            o_recv[other].reshape(group, length).astype(f32).T.astype(low)
        )

    def drain(peer):
        meta_copy(peer, me).wait_send()
        if heads == 1:
            qkv_copy(0, peer, me).wait_send()
        for head in range(heads):
            out_copy(head, peer, me).wait_send()

    others(n, me, drain)
    for hop in range(planes - 1):
        mem_hops(hop, lambda copy: copy.wait_send())
    mem_across(my_side).wait_send()
    for copy in saves:
        copy.wait()


def self_forward(n, segments, padding, tokens, weights, prefix, memory, mem_weights):
    length, width = tokens.shape
    group = width // n
    heads = group // HD
    whole = n * length
    planes = n // 2
    low = jnp.bfloat16
    f32 = jnp.float32
    vmem = pl.BlockSpec(memory_space=pltpu.VMEM)
    anywhere = pl.BlockSpec(memory_space=pl.ANY)
    dma = pltpu.SemaphoreType.DMA
    shapes = (
        ((heads, 2 * HD, whole), low),
        ((heads, whole, 2 * HD), low),
        ((heads, n, 3, HD, length), low),
        ((heads, PREFIX_ROWS, 2 * HD), low),
        ((heads, PREFIX_ROWS, HD), low),
        ((heads, HD, PREFIX_ROWS), low),
        ((planes, heads, HD + SUM_ROWS, 2 * length), f32),
        ((planes, heads, 8, 2 * length), f32),
    )
    square = pltpu.VMEM((width, width), low)
    qx, kx, raw, pk, pv, pkt, acc, stat = (pltpu.VMEM(*shape) for shape in shapes)
    return pl.pallas_call(
        functools.partial(self_forward_kernel, n),
        out_shape=(
            jax.ShapeDtypeStruct((length, width), low),
            jax.ShapeDtypeStruct((n * memory.shape[0], width), low),
            jax.ShapeDtypeStruct((n * memory.shape[0], width), low),
        )
        + tuple(jax.ShapeDtypeStruct(*shape) for shape in shapes),
        in_specs=[vmem] * 3
        + [anywhere] * 3
        + [vmem, anywhere, vmem, anywhere, vmem, vmem]
        + [anywhere] * 2,
        out_specs=(vmem,) + (anywhere,) * 10,
        scratch_shapes=[
            pltpu.VMEM((n, heads, 3, HD, length), low),
            raw,
            pltpu.VMEM((8, length), jnp.int32),
            pltpu.VMEM((n, 8, length), jnp.int32),
            kx,
            qx,
            pltpu.VMEM((heads, HD + SUM_ROWS, whole), low),
            pltpu.VMEM((PREFIX_ROWS, weights[0].shape[0] // 2), f32),
            pk,
            pv,
            pkt,
            pltpu.VMEM((heads, HD + SUM_ROWS, PREFIX_ROWS), low),
            stat,
            acc,
            pltpu.VMEM((heads, n, HD, length), low),
            pltpu.VMEM((n, heads, HD, length), low),
            pltpu.VMEM((planes, 2) + memory.shape, low),
            square,
            square,
            pltpu.VMEM((n * memory.shape[0], width), low),
            pltpu.VMEM((n * memory.shape[0], width), low),
            square,
            square,
            square,
            pltpu.VMEM(prefix[1].shape, low),
            pltpu.VMEM(prefix[3].shape, low),
            dma((heads, n)),
            dma((heads, n)),
            dma((n,)),
            dma((n,)),
            dma((heads, n)),
            dma((heads, n)),
            dma((2, planes + 1)),
            dma((planes + 1,)),
            dma((10,)),
            dma((width // (2 * LANES), 3)),
            dma((4,)),
        ],
        compiler_params=pltpu.CompilerParams(
            collective_id=0, has_side_effects=True, vmem_limit_bytes=VMEM_BYTES
        ),
        name="self_forward",
    )(segments, padding, tokens, *weights, *prefix, memory, *mem_weights)


def both_parts(value):
    high = value.astype(jnp.bfloat16).astype(jnp.float32)
    return jnp.concatenate([high, value - high], axis=0).astype(jnp.bfloat16)


def self_backward_kernel(
    n,
    batches,
    base_in,
    do_in,
    sums_in,
    mkey_in,
    mvalue_in,
    wck_in,
    wcv_in,
    vecs_in,
    qx_in,
    kx_in,
    raw_in,
    pk_in,
    pv_in,
    pkt_in,
    ot_in,
    lse_in,
    wq_in,
    wk_in,
    wv_in,
    first_in,
    second_in,
    emb_ref,
    fbias_ref,
    tg_ref,
    mgrad_ref,
    pkv_ref,
    hidden_ref,
    hgrad_ref,
    embed_ref,
    vecs_ref,
    full_out,
    do_recv,
    qx,
    kx,
    raw,
    kt,
    values,
    dot,
    qdo,
    pk,
    pv,
    pkt,
    ot,
    stat,
    weights,
    dqt,
    dkv,
    g_send,
    g_recv,
    pre_ref,
    pre_all,
    pre_sum,
    pre_recv,
    sums_mine,
    sums_core,
    sums_x,
    sums_side,
    sums_z,
    sums_far,
    full,
    mkey,
    mvalue,
    wck,
    wcv,
    mem_part,
    mem_side,
    mem_up,
    mem_down,
    vec_all,
    vec_sum,
    vec_y,
    vec_both,
    vec_z,
    product,
    first,
    second,
    base_ref,
    do_send_sem,
    do_recv_sem,
    g_send_sem,
    g_recv_sem,
    in_sem,
    send_sem,
    recv_sem,
):
    low = jnp.bfloat16
    f32 = jnp.float32
    me = lax.axis_index("seq")
    length, width = tg_ref.shape
    group = width // n
    heads = group // HD
    plane = 2 * length
    planes = n // 2
    step_rows = 256
    my_batch = lax.axis_index("batch")
    my_core = lax.rem(my_batch, 2)
    my_high = my_batch // 2
    highs = batches // 2
    my_plane = me // 2
    my_side = lax.rem(me, 2)
    beside = me + 1 - 2 * my_side
    used = [0]

    def numbers(count):
        used[0] += count
        return used[0] - count

    core_slot = numbers(2)
    x_slot = numbers(2 * highs)
    y_slot = numbers(3)
    z_slot = numbers(2 * planes + 2)
    up_slot = numbers(planes)
    down_slot = numbers(planes)
    va_slot = numbers(batches)
    vb_slot = numbers(1)
    vc_slot = numbers(planes)
    pa_slot = numbers(batches)
    pb_slot = numbers(n)

    def send(source, target, first, peer_index, slot_index, axis, peer):
        return remote(
            source,
            target,
            send_sem.at[first + peer_index],
            recv_sem.at[first + slot_index],
            axis,
            peer,
        )

    half_rows = 2 * planes * highs * sums_far.shape[0]
    x_rows = half_rows // highs
    y_rows = x_rows // 2
    z_rows = y_rows // planes
    x_row = pl.multiple_of(my_high * x_rows, x_rows)
    y_row = pl.multiple_of(x_row + my_side * y_rows, y_rows)

    def part(row, count):
        return sums_mine.at[pl.ds(pl.multiple_of(row, count), count)]

    def reduce_core():
        return send(
            sums_in.at[1 - my_core], sums_core, core_slot, 0, 0, "batch", my_batch + 1 - 2 * my_core
        )

    def reduce_x(peer, slot):
        return send(
            part(peer * x_rows, x_rows),
            sums_x.at[slot],
            x_slot,
            peer,
            slot,
            "batch",
            2 * peer + my_core,
        )

    def reduce_y():
        return send(
            part(x_row + (1 - my_side) * y_rows, y_rows), sums_side, y_slot, 0, 0, "seq", beside
        )

    near = planes // 2
    my_half = my_plane // near
    my_place = lax.rem(my_plane, near)
    far_plane = my_plane + near - 2 * near * my_half

    def piece_rows(half, place):
        return pl.ds(pl.multiple_of(y_row + (half * near + place) * z_rows, z_rows), z_rows)

    def reduce_near(half, peer, slot):
        return send(
            sums_mine.at[piece_rows(half, peer)],
            sums_z.at[half, slot],
            z_slot + half * near,
            peer,
            slot,
            "seq",
            2 * (my_half * near + peer) + my_side,
        )

    def reduce_far():
        return send(
            sums_mine.at[piece_rows(1 - my_half, my_place)],
            sums_far,
            z_slot + planes,
            0,
            0,
            "seq",
            2 * far_plane + my_side,
        )

    def gather_far(which):
        piece = full.at[my_core, my_high, my_side, which]
        return send(
            piece, piece, z_slot + planes + 1, 0, 0, "seq", 2 * far_plane + my_side
        )

    def gather_near(half, peer, slot):
        piece = full.at[my_core, my_high, my_side, half * near + slot]
        return send(
            piece,
            piece,
            z_slot + planes + 2 + half * near,
            peer,
            slot,
            "seq",
            2 * (my_half * near + peer) + my_side,
        )

    def both_halves(make, slot, action):
        def one(peer):
            for half in range(2):
                action(make(half, peer, peer if slot is None else slot))

        others(near, my_place, one)

    def gather_y(side):
        piece = full.at[my_core, my_high, side]
        return send(piece, piece, y_slot + 1, 0, 0, "seq", beside)

    def gather_x(peer, slot):
        piece = full.at[my_core, slot]
        return send(piece, piece, x_slot + highs, peer, slot, "batch", 2 * peer + my_core)

    def gather_core(core):
        piece = full.at[core]
        return send(piece, piece, core_slot + 1, 0, 0, "batch", my_batch + 1 - 2 * my_core)

    def mem_across():
        return send(
            mem_part.at[:, 1 - my_side], mem_side, y_slot + 2, 0, 0, "seq", beside
        )

    def mem_hop(target, toward, peer=None):
        buffer, slot = (mem_up, up_slot) if toward > 0 else (mem_down, down_slot)
        return send(
            mem_part.at[target, my_side],
            buffer.at[target],
            slot,
            target,
            target,
            "seq",
            me + 2 * toward if peer is None else peer,
        )

    def mem_from(target, toward):
        return mem_hop(target, toward, me - 2 * toward)

    def mem_pass(toward):
        buffer = mem_up if toward > 0 else mem_down
        first = 0 if toward > 0 else planes - 1
        for target in range(planes):

            @pl.when((target - my_plane) * toward > 0)
            def _():
                @pl.when(my_plane != first)
                def _():
                    mem_from(target, toward).wait_recv()
                    mem_part[target, my_side] = (
                        mem_part[target, my_side].astype(f32) + buffer[target].astype(f32)
                    ).astype(low)

                mem_hop(target, toward).start()

    def mem_stage(at):
        pl.when(my_plane == at)(lambda: mem_pass(1))
        pl.when(my_plane == planes - 1 - at)(lambda: mem_pass(-1))

    def mem_end():
        value = mem_part[my_plane, my_side].astype(f32)
        mgrad_ref[...] = value.astype(low)

        @pl.when(my_plane > 0)
        def _():
            mem_from(my_plane, 1).wait_recv()
            mgrad_ref[...] = (mgrad_ref[...].astype(f32) + mem_up[my_plane].astype(f32)).astype(low)

        @pl.when(my_plane < planes - 1)
        def _():
            mem_from(my_plane, -1).wait_recv()
            mgrad_ref[...] = (
                mgrad_ref[...].astype(f32) + mem_down[my_plane].astype(f32)
            ).astype(low)

    def mem_drain():
        for target in range(planes):

            @pl.when(target > my_plane)
            def _():
                mem_hop(target, 1).wait_send()

            @pl.when(target < my_plane)
            def _():
                mem_hop(target, -1).wait_send()

    def vec_a(peer, slot):
        return send(vecs_in, vec_all.at[slot], va_slot, peer, slot, "batch", peer)

    def vec_b(side):
        return send(vec_sum, vec_y.at[side], vb_slot, 0, 0, "seq", beside)

    def vec_c(peer, slot):
        return send(vec_both, vec_z.at[slot], vc_slot, peer, slot, "seq", 2 * peer + my_side)

    def pre_a(peer, slot):
        return send(pre_ref, pre_all.at[slot], pa_slot, peer, slot, "batch", peer)

    def pre_b(peer, slot):
        return send(pre_sum, pre_recv.at[slot], pb_slot, peer, slot, "seq", peer)

    def do_copy(head, peer, slot):
        return remote(
            do_in.at[peer, head],
            do_recv.at[head, slot],
            do_send_sem.at[head, peer],
            do_recv_sem.at[head, slot],
            "seq",
            peer,
        )

    def q_copy(head, peer, slot):
        return remote(
            g_send.at[peer, head, 0],
            g_recv.at[0, slot, head],
            g_send_sem.at[0, head, peer],
            g_recv_sem.at[0, head, slot],
            "seq",
            peer,
        )

    def kv_copy(head, peer, slot):
        return remote(
            g_send.at[peer, head, pl.ds(1, 2)],
            g_recv.at[pl.ds(1, 2), slot, head],
            g_send_sem.at[1, head, peer],
            g_recv_sem.at[1, head, slot],
            "seq",
            peer,
        )

    def far_first(body):
        for index in range(n):
            peer = jnp.where(my_plane < planes // 2, n - 1 - index, index)

            @pl.when(peer != me)
            def _():
                body(peer)

    def added(ref, size):
        value = ref[0].astype(f32)
        for other in range(1, size):
            value = value + ref[other].astype(f32)
        return value

    loads = [
        pltpu.make_async_copy(source, target, in_sem.at[index])
        for index, (source, target) in enumerate(
            (
                (raw_in, raw),
                (kx_in, kx),
                (pk_in, pk),
                (pv_in, pv),
                (pkt_in, pkt),
                (qx_in, qx),
                (ot_in, ot),
                (lse_in, stat),
                (sums_in.at[my_core], sums_mine),
                (vecs_in, vec_all.at[my_batch]),
                (mkey_in, mkey),
                (mvalue_in, mvalue),
                (wck_in, wck),
                (wcv_in, wcv),
                (base_in, base_ref),
                (wq_in, weights.at[0]),
                (wk_in, weights.at[1]),
                (wv_in, weights.at[2]),
                (first_in, first),
                (second_in, second),
            )
        )
    ]
    own_do = pltpu.make_async_copy(do_in.at[me], do_recv.at[:, me], in_sem.at[len(loads)])
    own_do.start()
    for load in loads:
        load.start()
    enter({"seq": n, "batch": batches})
    far_first(lambda peer: do_copy(0, peer, me).start())
    reduce_core().start()
    others(batches, my_batch, lambda peer: vec_a(peer, my_batch).start())
    dkv[...] = jnp.zeros_like(dkv)
    product[...] = jnp.zeros_like(product)
    pre_ref[...] = jnp.zeros_like(pre_ref)
    for load in loads[:14]:
        load.wait()
    own_do.wait()

    def turn(index, carry):
        head = index // n
        chunk = lax.rem(index, n)
        here = rows_of(chunk, length)
        kt[head, :, here] = raw[head, chunk, 1]
        values[head, here, :] = raw[head, chunk, 2].astype(f32).T.astype(low)
        return carry

    lax.fori_loop(0, heads * n, turn, 0)

    def memory_back(index, carry):
        here = rows_of(index, step_rows)
        value = dot_nt(mkey[...], wck[here, :]) + dot_nt(mvalue[...], wcv[here, :])
        mem_part[:, :, :, here] = value.astype(low).reshape(mem_part.shape[:3] + (step_rows,))
        return carry

    lax.fori_loop(0, width // step_rows, memory_back, 0)
    mem_across().start()

    def next_head(head):
        def move(peer):
            do_copy(head, peer, me).wait_send()
            do_copy(head + 1, peer, me).start()

        far_first(move)

    def arrive(head, which):
        for part in range(2):
            chunk = 2 * which + part

            @pl.when(chunk != me)
            def _():
                do_copy(head, chunk, chunk).wait_recv()

            grads = do_recv[head, chunk]
            dot[head, :, rows_of(chunk, length)] = grads
            grads = grads.astype(f32)
            query = raw[head, chunk, 0].astype(f32) * 0.125
            qdo[head, rows_of(chunk, length), :] = (
                jnp.concatenate([query, grads], axis=0).T.astype(low)
            )
            here = slice(part * length, (part + 1) * length)
            stat[which, head, 1:2, here] = jnp.sum(
                grads * ot[which, head, :HD, here], axis=0, keepdims=True
            )
        here = rows_of(which, plane)
        weight = jnp.exp(dot_nn(pk[head], qx[head, :, here]) - stat[which, head, 0:1, :])
        slope = weight * (dot_nn(pv[head], dot[head, :, here]) - stat[which, head, 1:2, :])
        both = jnp.concatenate([slope, weight], axis=0).astype(low)
        sums = dot_nn(both, qdo[head, here, :])
        pre_ref[head] += jnp.where(
            head_lanes((PREFIX_ROWS, 2 * HD), 0), sums[:PREFIX_ROWS], sums[PREFIX_ROWS:]
        )
        slope = slope.astype(low)
        dqt[which, head] = dot_nn(pkt[head], slope)

    def plus(first, second):
        return (first.astype(f32) + second.astype(f32)).astype(low)

    def sum_one():
        reduce_core().wait_recv()
        sums_mine[...] = plus(sums_mine[...], sums_core[...])
        others(highs, my_high, lambda peer: reduce_x(peer, my_high).start())

    def sum_two():
        here = pl.ds(x_row, x_rows)
        others(highs, my_high, lambda peer: reduce_x(peer, peer).wait_recv())
        sums_x[my_high] = sums_mine[here]
        sums_mine[here] = added(sums_x, highs).astype(low)
        reduce_y().start()

    def sum_three():
        here = pl.ds(y_row, y_rows)
        reduce_y().wait_recv()
        sums_mine[here] = plus(sums_mine[here], sums_side[...])
        both_halves(reduce_near, my_place, lambda copy: copy.start())

    def sum_four():
        both_halves(reduce_near, None, lambda copy: copy.wait_recv())
        for half in range(2):
            here = piece_rows(half, my_place)
            sums_z[half, my_place] = sums_mine[here]
            value = sums_z[half, 0].astype(f32)
            for other in range(1, near):
                value = value + sums_z[half, other].astype(f32)
            sums_mine[here] = value.astype(low)
        reduce_far().start()

    def sum_across():
        reduce_far().wait_recv()
        full[my_core, my_high, my_side, my_plane] = plus(
            sums_mine[piece_rows(my_half, my_place)], sums_far[...]
        )
        gather_far(my_plane).start()

    def sum_return():
        gather_far(far_plane).wait_recv()
        both_halves(gather_near, my_place, lambda copy: copy.start())

    def sum_five():
        both_halves(gather_near, None, lambda copy: copy.wait_recv())
        gather_y(my_side).start()

    def sum_six():
        gather_y(1 - my_side).wait_recv()
        others(highs, my_high, lambda peer: gather_x(peer, my_high).start())

    def sum_seven():
        others(highs, my_high, lambda peer: gather_x(peer, peer).wait_recv())
        gather_core(my_core).start()

    def sum_end():
        gather_core(1 - my_core).wait_recv()
        save_full.start()

    def vec_one():
        others(batches, my_batch, lambda peer: vec_a(peer, peer).wait_recv())
        vec_sum[...] = added(vec_all, batches)
        vec_b(my_side).start()
        vec_y[my_side] = vec_sum[...]

    def vec_two():
        vec_b(1 - my_side).wait_recv()
        value = (vec_y[0] + vec_y[1]).astype(f32)
        vec_both[...] = jnp.concatenate(
            [value[:, : width // 2], value[:, width // 2 :]], axis=0
        ).astype(low)
        others(planes, my_plane, lambda peer: vec_c(peer, my_plane).start())
        vec_z[my_plane] = vec_both[...]

    def vec_end():
        others(planes, my_plane, lambda peer: vec_c(peer, peer).wait_recv())
        value = added(vec_z, planes)
        vecs_ref[:, : width // 2] = value[:8]
        vecs_ref[:, width // 2 :] = value[8:]

    def mem_one():
        mem_across().wait_recv()
        mem_part[:, my_side] = plus(mem_part[:, my_side], mem_side[...])

    def stage_pa():
        others(batches, my_batch, lambda peer: pre_a(peer, my_batch).start())
        pre_all[my_batch] = pre_ref[...]

    def stage_pb():
        others(batches, my_batch, lambda peer: pre_a(peer, peer).wait_recv())
        pre_sum[...] = added(pre_all, batches).astype(low)
        others(n, me, lambda peer: pre_b(peer, me).start())
        pre_recv[me] = pre_sum[...]

    save_full = pltpu.make_async_copy(full, full_out, in_sem.at[0])

    def pair_part(head, upper, lower, first, count, diagonal, at=None):
        keys = span_of(lower * plane + (first if at is None else at * count), count)
        here = span_of(upper * plane + first, plane - first)
        at = slice(first, plane)
        scores = dot_nn(kx[head, keys, :], qx[head, :, here])
        slope = dot_nn(values[head, keys, :], dot[head, :, here]) - stat[upper, head, 1:2, at]
        weight = jnp.exp(scores - stat[upper, head, 0:1, at])
        if diagonal:
            key_at = lax.broadcasted_iota(jnp.int32, scores.shape, 0)
            query_at = lax.broadcasted_iota(jnp.int32, scores.shape, 1)
            weight = jnp.where(key_at <= query_at, weight, 0.0)
        slope = (weight * slope).astype(low)
        key_part = dot_nn(slope, qdo[head, here, :])
        value_part = dot_nn(weight.astype(low), qdo[head, here, :])
        dkv[head, keys, :] += jnp.where(head_lanes((count, 2 * HD), 0), key_part, value_part)
        dqt[upper, head, :, at] += dot_nn(kt[head, :, keys], slope)

    def pair(head, upper, lower, diagonal):
        if diagonal:
            for part in range(plane // step_rows):
                pair_part(head, upper, lower, part * step_rows, step_rows, True)
        else:

            def one(at, carry):
                pair_part(head, upper, lower, 0, step_rows, False, at)
                return carry

            lax.fori_loop(0, plane // step_rows, one, 0)

    def hand_queries(head, which):
        for part in range(2):
            chunk = 2 * which + part
            g_send[chunk, head, 0] = (
                dqt[which, head, :, part * length : (part + 1) * length] * 0.125
            ).astype(low)

            @pl.when(chunk != me)
            def _():
                q_copy(head, chunk, me).start()

            @pl.when(chunk == me)
            def _():
                g_recv[0, me, head] = g_send[chunk, head, 0]

    def hand_keys(head, which):
        for part in range(2):
            chunk = 2 * which + part
            turned = dkv[head, rows_of(chunk, length), :].T.astype(low)
            g_send[chunk, head, 1] = turned[:HD]
            g_send[chunk, head, 2] = turned[HD:]

            @pl.when(chunk != me)
            def _():
                kv_copy(head, chunk, me).start()

            @pl.when(chunk == me)
            def _():
                g_recv[pl.ds(1, 2), me, head] = g_send[chunk, head, pl.ds(1, 2)]

    rising = my_plane >= planes // 2
    total = heads * planes * (planes + 1) // 2
    hooks = [
        (2, sum_one),
        (3, mem_one),
        (4, lambda: mem_stage(0)),
        (5, vec_one),
        (5, sum_two),
        (7, sum_three),
        (8, vec_two),
        (9, sum_four),
        (11, sum_across),
        (13, sum_return),
        (15, sum_five),
        (16, vec_end),
        (17, sum_six),
    ] + [(4 + 3 * at, functools.partial(mem_stage, at)) for at in range(1, planes - 1)]
    hooks += [
        (1 + head * total // heads, functools.partial(next_head, head)) for head in range(heads - 1)
    ]
    final = total - planes * (planes + 1) // 2
    hooks += [(final + planes + 1, stage_pa), (final + 2 * planes - 1, stage_pb)]

    def hook(pairs):
        for number, body in sorted(hooks, key=lambda item: item[0]):
            pl.when(pairs == number)(body)


    def stage(index, carry):
        head = index // planes
        step = lax.rem(index, planes)
        here = jnp.where(rising, step, planes - 1 - step)

        @pl.when((step == 0) | ((step == 1) & jnp.logical_not(rising)))
        def _():
            @pl.when(rising | (step == 0))
            def _():
                arrive(head, here)

            @pl.when(jnp.logical_not(rising) & (step == 1))
            def _():
                def rest(which, inner):
                    arrive(head, planes - 2 - which)
                    return inner

                lax.fori_loop(0, planes - 1, rest, 0)

        begun = head * (planes * (planes + 1) // 2) + step * planes - step * (step - 1) // 2
        hook(begun)
        pair(head, here, here, True)

        @pl.when(rising)
        def _():
            hand_queries(head, here)

        @pl.when(jnp.logical_not(rising))
        def _():
            hand_keys(head, here)

        def far(at, inner):
            there = jnp.where(rising, here + 1 + at, here - 1 - at)

            @pl.when(rising & (step == 0))
            def _():
                arrive(head, there)

            hook(begun + 1 + at)
            pair(head, jnp.maximum(here, there), jnp.minimum(here, there), False)
            return inner

        lax.fori_loop(0, planes - 1 - step, far, 0)

        @pl.when(rising)
        def _():
            hand_keys(head, here)

        @pl.when(jnp.logical_not(rising))
        def _():
            hand_queries(head, here)

        return carry

    lax.fori_loop(0, heads * planes, stage, 0)
    sum_seven()
    mem_end()
    for load in loads[14:]:
        load.wait()

    def gathered(peer):
        for head in range(heads):
            q_copy(head, peer, peer).wait_recv()
            kv_copy(head, peer, peer).wait_recv()

    half = width // 2

    def gather_plane(step, carry):
        which = lax.rem(my_plane + step, planes)
        for part in range(2):
            peer = 2 * which + part

            @pl.when(peer != me)
            def _():
                gathered(peer)

        columns = rows_of(which, 2 * group)
        for part in range(2):
            here = slice(part * half, (part + 1) * half)
            value = product[here, :]
            for kind in range(3):
                grads = g_recv[kind, pl.ds(2 * which, 2)].reshape(2 * group, length)
                value = value + dot_nn(weights[kind, here, columns], grads)
            product[here, :] = value
        return carry

    lax.fori_loop(0, planes - 1, gather_plane, 0)
    for other in range(n):

        @pl.when(other != me)
        def _():
            pre_b(other, other).wait_recv()

        value = pre_recv[other].astype(f32)
        for which in range(2):
            pkv_ref[:, which * width + other * group : which * width + (other + 1) * group] = (
                jnp.concatenate(
                    [value[head, :, which * HD : (which + 1) * HD] for head in range(heads)], axis=1
                )
            )

    count = emb_ref.shape[0]
    hidden_ref[...] = jnp.zeros_like(hidden_ref)
    hidden_ref[:count, :] = jnp.tanh(dot_nn(emb_ref[...], first[...]) + fbias_ref[...])
    value = hidden_ref[...]
    grad = dot_nt(both_parts(pkv_ref[...]), second[...])
    grad = (grad[:PREFIX_ROWS] + grad[PREFIX_ROWS:]) * (1.0 - value * value)
    hgrad_ref[...] = grad
    back = dot_nt(both_parts(grad), first[...])
    embed_ref[...] = back[:PREFIX_ROWS] + back[PREFIX_ROWS:]
    gather_plane(planes - 1, 0)
    sum_end()
    tile = 256
    for index in range(width // tile):
        here = slice(index * tile, (index + 1) * tile)
        tg_ref[:, here] = (base_ref[:, here] + product[here, :].T).astype(low)
    def drain(peer):
        do_copy(heads - 1, peer, me).wait_send()
        pre_b(peer, me).wait_send()
        for head in range(heads):
            q_copy(head, peer, me).wait_send()
            kv_copy(head, peer, me).wait_send()

    others(n, me, drain)
    others(batches, my_batch, lambda peer: pre_a(peer, my_batch).wait_send())
    others(batches, my_batch, lambda peer: vec_a(peer, my_batch).wait_send())
    reduce_core().wait_send()
    others(highs, my_high, lambda peer: reduce_x(peer, my_high).wait_send())
    reduce_y().wait_send()
    both_halves(reduce_near, my_place, lambda copy: copy.wait_send())
    both_halves(gather_near, my_place, lambda copy: copy.wait_send())
    reduce_far().wait_send()
    gather_far(my_plane).wait_send()
    gather_y(my_side).wait_send()
    others(highs, my_high, lambda peer: gather_x(peer, my_high).wait_send())
    gather_core(my_core).wait_send()
    mem_across().wait_send()
    mem_drain()
    others(planes, my_plane, lambda peer: vec_c(peer, my_plane).wait_send())
    vec_b(my_side).wait_send()
    save_full.wait()


def self_backward(
    n, batches, first_grad, out_grad, sums, mem_grads, mem_weights, vecs, saved, weights, prefix
):
    length, width = first_grad.shape
    group = width // n
    heads = group // HD
    whole = n * length
    planes = n // 2
    low = jnp.bfloat16
    f32 = jnp.float32
    vmem = pl.BlockSpec(memory_space=pltpu.VMEM)
    anywhere = pl.BlockSpec(memory_space=pl.ANY)
    dma = pltpu.SemaphoreType.DMA
    sum_rows = sums.shape[0] // (n * batches)
    mem_len = mem_grads[0].shape[0]
    mem_rows = mem_len // n
    mem_part = pltpu.VMEM((planes, mem_rows, width), low)
    mem_low = pltpu.VMEM((mem_len, width), low)
    square = pltpu.VMEM((width, width), low)
    vec = pltpu.VMEM((8, width), f32)
    copies = 8 + 2 * (batches // 2) + 5 * planes + 2 * batches + n
    qx, kx, raw, pk, pv, pkt, ot, stat = (pltpu.VMEM(value.shape, value.dtype) for value in saved)
    return pl.pallas_call(
        functools.partial(self_backward_kernel, n, batches),
        out_shape=(
            jax.ShapeDtypeStruct((length, width), low),
            jax.ShapeDtypeStruct((mem_rows, width), low),
            jax.ShapeDtypeStruct((PREFIX_ROWS, 2 * width), f32),
            jax.ShapeDtypeStruct((PREFIX_ROWS, prefix[0].shape[1]), f32),
            jax.ShapeDtypeStruct((PREFIX_ROWS, prefix[0].shape[1]), f32),
            jax.ShapeDtypeStruct((PREFIX_ROWS, width), f32),
            jax.ShapeDtypeStruct((8, width), f32),
            jax.ShapeDtypeStruct((2, batches // 2, 2, planes, sum_rows, LANES), low),
        ),
        in_specs=[anywhere] * 21 + [vmem] * 2,
        out_specs=(vmem,) * 7 + (anywhere,),
        scratch_shapes=[
            pltpu.VMEM((heads, n, HD, length), low),
            qx,
            kx,
            raw,
            pltpu.VMEM((heads, HD, whole), low),
            pltpu.VMEM((heads, whole, HD), low),
            pltpu.VMEM((heads, HD, whole), low),
            pltpu.VMEM((heads, whole, 2 * HD), low),
            pk,
            pv,
            pkt,
            ot,
            stat,
            pltpu.VMEM((3, width, width), low),
            pltpu.VMEM((planes, heads, HD, 2 * length), f32),
            pltpu.VMEM((heads, whole, 2 * HD), f32),
            pltpu.VMEM((n, heads, 3, HD, length), low),
            pltpu.VMEM((3, n, heads, HD, length), low),
            pltpu.VMEM((heads, PREFIX_ROWS, 2 * HD), f32),
            pltpu.VMEM((batches, heads, PREFIX_ROWS, 2 * HD), f32),
            pltpu.VMEM((heads, PREFIX_ROWS, 2 * HD), low),
            pltpu.VMEM((n, heads, PREFIX_ROWS, 2 * HD), low),
            pltpu.VMEM((sums.shape[0] // 2, LANES), low),
            pltpu.VMEM((sums.shape[0] // 2, LANES), low),
            pltpu.VMEM((batches // 2, sums.shape[0] // batches, LANES), low),
            pltpu.VMEM((planes * sum_rows, LANES), low),
            pltpu.VMEM((2, planes // 2, sum_rows, LANES), low),
            pltpu.VMEM((sum_rows, LANES), low),
            pltpu.VMEM((2, batches // 2, 2, planes, sum_rows, LANES), low),
            mem_low,
            mem_low,
            square,
            square,
            pltpu.VMEM((planes, 2, mem_rows, width), low),
            mem_part,
            mem_part,
            mem_part,
            pltpu.VMEM((batches, 8, width), f32),
            vec,
            pltpu.VMEM((2, 8, width), f32),
            pltpu.VMEM((16, width // 2), low),
            pltpu.VMEM((planes, 16, width // 2), low),
            pltpu.VMEM((width, length), f32),
            pltpu.VMEM(prefix[0].shape, low),
            pltpu.VMEM(prefix[1].shape, low),
            pltpu.VMEM((length, width), f32),
            dma((heads, n)),
            dma((heads, n)),
            dma((2, heads, n)),
            dma((2, heads, n)),
            dma((21,)),
            dma((copies,)),
            dma((copies,)),
        ],
        compiler_params=pltpu.CompilerParams(
            collective_id=1, has_side_effects=True, vmem_limit_bytes=VMEM_BYTES
        ),
        name="self_backward",
    )(
        first_grad,
        out_grad,
        sums.reshape(2, -1, LANES),
        *mem_grads,
        *mem_weights,
        vecs,
        *saved,
        *weights,
        *prefix,
    )


def finish_kernel(
    full_in,
    vecs_ref,
    pkv_ref,
    hidden_ref,
    hgrad_ref,
    embed_ref,
    emb_ref,
    token_in,
    mem_in,
    embed_out,
    first_out,
    fbias_out,
    second_out,
    sbias_out,
    down_out,
    dbias_out,
    raise_out,
    rbias_out,
    gain_out,
    shift_out,
    token_out,
    mem_out,
    full_ref,
    token_ref,
    mem_ref,
    first_grad,
    second_grad,
    down_grad,
    raise_grad,
    emb,
    out_sem,
    in_sem,
):
    f32 = jnp.float32
    low = jnp.bfloat16
    width = emb_ref.shape[1]
    down = dbias_out.shape[1]
    count = emb_ref.shape[0]
    first = down * width // LANES
    loads = [
        pltpu.make_async_copy(source, target, in_sem.at[index])
        for index, (source, target) in enumerate(
            (
                (full_in.at[first:], full_ref.at[first:]),
                (full_in.at[:first], full_ref.at[:first]),
                (token_in, token_ref),
                (mem_in, mem_ref),
            )
        )
    ]
    for load in loads:
        load.start()
    saves = []

    def save(source, target, rows=None):
        if rows is not None:
            source, target = source.at[rows], target.at[rows]
        copy = pltpu.make_async_copy(source, target, out_sem.at[len(saves)])
        copy.start()
        saves.append(copy)

    loads[0].wait()
    for index in range(width // LANES):
        raise_grad[:, index * LANES : (index + 1) * LANES] = full_ref[
            first + index * down : first + (index + 1) * down, :
        ].astype(f32)
    save(raise_grad, raise_out)
    loads[1].wait()
    for index in range(down // LANES):
        down_grad[:, index * LANES : (index + 1) * LANES] = full_ref[
            index * width : (index + 1) * width, :
        ].astype(f32)
    save(down_grad, down_out)
    for load in loads[2:]:
        load.wait()
    save(token_ref, token_out)
    save(mem_ref, mem_out)
    emb[...] = jnp.zeros_like(emb)
    emb[:count, :] = emb_ref[...].astype(f32)
    value = hidden_ref[...]
    prefix = pkv_ref[...]
    parts = both_parts(prefix)
    hidden_twice = jnp.concatenate([value, value], axis=0).T.astype(low)
    tile = 128
    for index in range(second_grad.shape[0] // tile):
        here = slice(index * tile, (index + 1) * tile)
        second_grad[here, :] = dot_nn(hidden_twice[here, :], parts)
        save(second_grad, second_out, here)
    sbias_out[...] = jnp.sum(prefix, axis=0, keepdims=True)
    grad = hgrad_ref[...]
    fbias_out[...] = jnp.sum(grad, axis=0, keepdims=True)
    parts = both_parts(grad)
    emb_twice = jnp.concatenate([emb[...], emb[...]], axis=0).T.astype(low)
    first_grad[...] = dot_nn(emb_twice, parts)
    save(first_grad, first_out)
    embed_out[...] = embed_ref[:count, :]
    rbias_out[...] = vecs_ref[0:1, :]
    dbias_out[...] = vecs_ref[1:2, :down]
    gain_out[...] = vecs_ref[2:5, :]
    shift_out[...] = vecs_ref[5:8, :]
    for copy in saves:
        copy.wait()


def finish(full, vecs, prefix_sums, embed, down, token_grad, memory_grad):
    f32 = jnp.float32
    count, width = embed.shape
    hidden = prefix_sums[1].shape[1]
    vmem = pl.BlockSpec(memory_space=pltpu.VMEM)
    anywhere = pl.BlockSpec(memory_space=pl.ANY)
    shapes = (
        (count, width),
        (width, hidden),
        (1, hidden),
        (hidden, 2 * width),
        (1, 2 * width),
        (width, down),
        (1, down),
        (down, width),
        (1, width),
        (3, width),
        (3, width),
    )
    return pl.pallas_call(
        finish_kernel,
        out_shape=tuple(jax.ShapeDtypeStruct(shape, f32) for shape in shapes)
        + tuple(
            jax.ShapeDtypeStruct(value.shape, value.dtype) for value in (token_grad, memory_grad)
        ),
        in_specs=[anywhere] + [vmem] * 6 + [anywhere] * 2,
        out_specs=(
            vmem,
            anywhere,
            vmem,
            anywhere,
            vmem,
            anywhere,
            vmem,
            anywhere,
            vmem,
            vmem,
            vmem,
            anywhere,
            anywhere,
        ),
        scratch_shapes=[
            pltpu.VMEM(full.shape, jnp.bfloat16),
            pltpu.VMEM(token_grad.shape, token_grad.dtype),
            pltpu.VMEM(memory_grad.shape, memory_grad.dtype),
            pltpu.VMEM((width, hidden), f32),
            pltpu.VMEM((hidden, 2 * width), f32),
            pltpu.VMEM((width, down), f32),
            pltpu.VMEM((down, width), f32),
            pltpu.VMEM((PREFIX_ROWS, width), f32),
            pltpu.SemaphoreType.DMA((5 + hidden // 128,)),
            pltpu.SemaphoreType.DMA((4,)),
        ],
        compiler_params=pltpu.CompilerParams(vmem_limit_bytes=VMEM_BYTES),
        name="finish",
    )(full, vecs, *prefix_sums, embed, token_grad, memory_grad)


def gelu_pair(value):
    size = jnp.abs(value)
    step = 1.0 / (1.0 + (0.3275911 * 0.7071067811865476) * size)
    bell = jnp.exp(-0.5 * value * value)
    poly = step * (
        0.127414796
        + step
        * (-0.142248368 + step * (0.7107068705 + step * (-0.7265760135 + step * 0.5307027145)))
    )
    act = jnp.maximum(value, 0.0) - size * (poly * bell)
    turn = bell * (0.3989422804014327 * size - poly)
    return act, jnp.where(value >= 0.0, 1.0 + turn, -turn)


def normed(value):
    center = jnp.mean(value, axis=-1, keepdims=True)
    centered = value - center
    scale = lax.rsqrt(jnp.mean(centered * centered, axis=-1, keepdims=True) + norm_eps)
    return centered * scale, scale


def norm_back(grad, scale, unit):
    return scale * (
        grad
        - jnp.mean(grad, axis=-1, keepdims=True)
        - unit * jnp.mean(grad * unit, axis=-1, keepdims=True)
    )


def middle_kernel(
    tok_in,
    att_in,
    cot_in,
    mkey_in,
    mvalue_in,
    gain_ref,
    shift_ref,
    dbias_ref,
    rbias_ref,
    wo_in,
    wcq_in,
    wco_in,
    wd_in,
    wr_in,
    win_in,
    wout_in,
    layer_out,
    fgrad_out,
    ograd_out,
    mkey_out,
    mvalue_out,
    sums_out,
    vecs_ref,
    tok_ref,
    att_ref,
    cot_ref,
    mkey_ref,
    mvalue_ref,
    out_ref,
    fgrad_ref,
    ograd_ref,
    sums_ref,
    wo,
    wcq,
    wco,
    wd,
    wr,
    win,
    wout,
    unit_one,
    unit_two,
    work,
    total,
    scale_one,
    scale_two,
    low_one,
    low_two,
    low_three,
    query,
    crossed,
    weights,
    slopes,
    acts,
    down_act,
    down_slope,
    down_grad,
    load_sem,
    win_sem,
    wout_sem,
    out_sem,
):
    length, width = tok_ref.shape
    resident = len(win.shape) == 2
    tile = 512 if resident else win.shape[2]
    tiles = win_in.shape[1] // tile
    slots = tiles if resident else win.shape[0]
    rows_step = length // 2
    low = jnp.bfloat16
    f32 = jnp.float32

    sources = (
        att_in,
        wo_in,
        tok_in,
        wcq_in,
        mkey_in,
        mvalue_in,
        wco_in,
        wd_in,
        wr_in,
        cot_in,
    )
    targets = (att_ref, wo, tok_ref, wcq, mkey_ref, mvalue_ref, wco, wd, wr, cot_ref)
    loads = [
        pltpu.make_async_copy(source, target, load_sem.at[index])
        for index, (source, target) in enumerate(zip(sources, targets))
    ]

    def win_load(which):
        slot = which % slots
        target = win.at[:, rows_of(which, tile)] if resident else win.at[slot]
        return pltpu.make_async_copy(win_in.at[:, rows_of(which, tile)], target, win_sem.at[slot])

    def wout_load(which):
        slot = which % slots
        target = wout.at[rows_of(which, tile), :] if resident else wout.at[slot]
        return pltpu.make_async_copy(wout_in.at[rows_of(which, tile), :], target, wout_sem.at[slot])

    for load in loads[:7]:
        load.start()

    def by_columns(extent, step, body):
        def one(index, carry):
            body(pl.ds(pl.multiple_of(index * step, step), step))
            return carry

        lax.fori_loop(0, extent // step, one, 0)

    def by_rows(body, init=0):
        def one(index, carry):
            return body(rows_of(index, rows_step), carry)

        return lax.fori_loop(0, length // rows_step, one, init)

    cols = 512
    half = width // 2

    for load in loads[:3]:
        load.wait()
    for load in loads[7:]:
        load.start()
    for which in range(slots):
        win_load(which).start()
    for which in range(slots):
        wout_load(which).start()

    def project_out(here):
        work[:, here] = tok_ref[:, here].astype(f32) + dot_nn(att_ref[...], wo[:, here])

    by_columns(width, cols, project_out)

    def first_norm(here, carry):
        unit, scale = normed(work[here, :])
        unit_one[here, :] = unit
        scale_one[here, :] = scale
        value = unit * gain_ref[0:1, :] + shift_ref[0:1, :]
        work[here, :] = value
        low_one[here, :] = value.astype(low)
        return carry

    by_rows(first_norm)

    loads[3].wait()

    def project_query(here):
        query[:, here] = dot_nn(low_one[...], wcq[:, here]).astype(low)

    by_columns(width, cols, project_query)
    per_block = LANES // HD

    def stacked(value):
        return jnp.concatenate(
            [jnp.where(head_lanes(value.shape, head), value, 0.0) for head in range(per_block)],
            axis=0,
        ).astype(low)

    def unstacked(value):
        return jnp.concatenate(
            [
                value[head * HD : (head + 1) * HD, head * length : (head + 1) * length]
                for head in range(per_block)
            ],
            axis=0,
        )

    def block_queries(here):
        return stacked(query[:, here].astype(f32) * 0.125)

    def cross_forward(block):
        here = rows_of(block, LANES)
        scores = dot_nt(mkey_ref[:, here], block_queries(here))
        raised = jnp.exp(scores - jnp.max(scores, axis=0, keepdims=True))
        share = 1.0 / jnp.sum(raised, axis=0, keepdims=True)
        weight = (raised * share).astype(low)
        weights[block] = weight
        values = mvalue_ref[:, here].astype(f32).T.astype(low)
        crossed[:, here] = unstacked(dot_nn(values, weight)).T.astype(low)

    loads[4].wait()
    loads[5].wait()

    def cross_forward_four(step, carry):
        for part in range(4):
            cross_forward(4 * step + part)
        return carry

    lax.fori_loop(0, width // LANES // 4, cross_forward_four, 0)

    loads[6].wait()

    def project_crossed(here):
        work[:, here] += dot_nn(crossed[...], wco[:, here])

    by_columns(width, cols, project_crossed)

    def second_norm(here, carry):
        unit, scale = normed(work[here, :])
        unit_two[here, :] = unit
        scale_two[here, :] = scale
        value = unit * gain_ref[1:2, :] + shift_ref[1:2, :]
        work[here, :] = value
        low_two[here, :] = value.astype(low)
        return carry

    by_rows(second_norm)

    step_cols = 512

    def feed_part(here, source):
        act, slope = gelu_pair(dot_nn(low_two[...], source))
        slopes[:, here] = slope.astype(low)
        return act.astype(low)

    if resident:

        def feed_forward(which, carry):
            here = rows_of(which, step_cols)

            @pl.when(which % (tile // step_cols) == 0)
            def _():
                win_load(which // (tile // step_cols)).wait()

            acts[:, here] = feed_part(here, win[:, here])
            return carry

        lax.fori_loop(0, tiles * tile // step_cols, feed_forward, 0)
        for which in range(tiles):
            wout_load(which).wait()

        def feed_out_part(here):
            total[:, here] = dot_nn(acts[...], wout[:, here])

        by_columns(width, step_cols, feed_out_part)
    else:
        total[...] = jnp.zeros_like(total)

        def feed_forward(which, carry):
            slot = lax.rem(which, slots)
            win_load(which).wait()
            wout_load(which).wait()
            total[...] += dot_nn(feed_part(rows_of(which, tile), win[slot]), wout[slot])

            @pl.when(which + slots < tiles)
            def _():
                win_load(which + slots).start()
                wout_load(which + slots).start()

            return carry

        lax.fori_loop(0, tiles, feed_forward, 0)

    loads[7].wait()
    loads[8].wait()
    loads[9].wait()
    act, slope = gelu_pair(dot_nn(low_two[...], wd[...]) + dbias_ref[...])
    down_act[...] = act.astype(low)
    down_slope[...] = slope.astype(low)

    def project_raise(here):
        work[:, here] += total[:, here] + 4.0 * (
            dot_nn(down_act[...], wr[:, here]) + rbias_ref[:, here]
        )

    by_columns(width, cols, project_raise)
    nothing = jnp.zeros((1, width), f32)

    def third_norm(here, carry):
        gain_sum, shift_sum, bias_sum = carry
        unit, scale = normed(work[here, :])
        gain = gain_ref[2:3, :]
        out_ref[here, :] = (unit * gain + shift_ref[2:3, :]).astype(low)
        grad = cot_ref[here, :].astype(f32)
        back = norm_back(grad * gain, scale, unit)
        total[here, :] = back
        back_low = back.astype(low)
        low_three[here, :] = back_low
        return (
            gain_sum + jnp.sum(grad * unit, axis=0, keepdims=True),
            shift_sum + jnp.sum(grad, axis=0, keepdims=True),
            bias_sum + jnp.sum(back_low.astype(f32), axis=0, keepdims=True),
        )

    gain_three, shift_three, bias_sum = by_rows(third_norm, (nothing, nothing, nothing))
    saves = []

    def save(source, target):
        copy = pltpu.make_async_copy(source, target, out_sem.at[len(saves)])
        copy.start()
        saves.append(copy)

    save(out_ref, layer_out)
    vecs_ref[0:1, :] = 4.0 * bias_sum

    back = 4.0 * dot_nt(low_three[...], wr[...]) * down_slope[...].astype(f32)
    back_low = back.astype(low)
    down_grad[...] = back_low
    vecs_ref[1:2, :] = jnp.concatenate(
        [
            jnp.sum(back_low.astype(f32), axis=0, keepdims=True),
            jnp.zeros((1, width - wd.shape[1]), f32),
        ],
        axis=1,
    )
    down = wd.shape[1]
    raise_sum = 4.0 * dot_tn(down_act[...], low_three[...])
    for index in range(width // LANES):
        sums_ref[pl.ds(down * width // LANES + index * down, down), :] = raise_sum[
            :, index * LANES : (index + 1) * LANES
        ].astype(low)
    down_sum = dot_tn(low_two[...], down_grad[...])
    for index in range(down // LANES):
        sums_ref[index * width : (index + 1) * width, :] = down_sum[
            :, index * LANES : (index + 1) * LANES
        ].astype(low)

    save(sums_ref, sums_out)

    if resident:

        def feed_slope(here):
            acts[:, here] = (
                dot_nt(low_three[...], wout[here, :]) * slopes[:, here].astype(f32)
            ).astype(low)

        by_columns(win_in.shape[1], step_cols, feed_slope)

        def feed_in_part(here):
            total[:, here] += dot_nt(acts[...], win[here, :])

        by_columns(width, step_cols, feed_in_part)
    else:

        def feed_backward(step, carry):
            which = tiles - 1 - step
            slot = lax.rem(which, slots)
            here = rows_of(which, tile)

            @pl.when(which < tiles - slots)
            def _():
                wout_load(which).wait()
                win_load(which).wait()

            grad = dot_nt(low_three[...], wout[slot]) * slopes[:, here].astype(f32)
            total[...] += dot_nt(grad.astype(low), win[slot])

            @pl.when(which >= slots)
            def _():
                win_load(which - slots).start()
                wout_load(which - slots).start()

            return carry

        lax.fori_loop(0, tiles, feed_backward, 0)

    def down_back(here):
        total[:, here] += dot_nt(down_grad[...], wd[here, :])

    by_columns(width, cols, down_back)

    def second_back(here, carry):
        gain_sum, shift_sum = carry
        grad = total[here, :]
        unit = unit_two[here, :]
        back = norm_back(grad * gain_ref[1:2, :], scale_two[here, :], unit)
        total[here, :] = back
        low_one[here, :] = back.astype(low)
        return (
            gain_sum + jnp.sum(grad * unit, axis=0, keepdims=True),
            shift_sum + jnp.sum(grad, axis=0, keepdims=True),
        )

    gain_two, shift_two = by_rows(second_back, (nothing, nothing))

    def crossed_back(here):
        crossed[:, here] = dot_nt(low_one[...], wco[here, :]).astype(low)

    by_columns(width, cols, crossed_back)

    def cross_backward(block):
        here = rows_of(block, LANES)
        grads = stacked(crossed[:, here].astype(f32))
        keys = mkey_ref[:, here].astype(f32).T.astype(low)
        slope = dot_nt(mvalue_ref[:, here], grads)
        weight_low = weights[block]
        weight = weight_low.astype(f32)
        slope = weight * (slope - jnp.sum(weight * slope, axis=0, keepdims=True))
        slope = slope.astype(low)
        queries = block_queries(here)
        mkey_ref[:, here] = dot_nn(slope, queries).astype(low)
        mvalue_ref[:, here] = dot_nn(weight_low, grads).astype(low)
        query[:, here] = (unstacked(dot_nn(keys, slope)) * 0.125).T.astype(low)

    def cross_backward_four(step, carry):
        for part in range(4):
            cross_backward(4 * step + part)
        return carry

    lax.fori_loop(0, width // LANES // 4, cross_backward_four, 0)
    save(mkey_ref, mkey_out)
    save(mvalue_ref, mvalue_out)

    def query_back(here):
        total[:, here] += dot_nt(query[...], wcq[here, :])

    by_columns(width, cols, query_back)

    def first_back(here, carry):
        gain_sum, shift_sum = carry
        grad = total[here, :]
        unit = unit_one[here, :]
        back = norm_back(grad * gain_ref[0:1, :], scale_one[here, :], unit)
        fgrad_ref[here, :] = back
        low_one[here, :] = back.astype(low)
        return (
            gain_sum + jnp.sum(grad * unit, axis=0, keepdims=True),
            shift_sum + jnp.sum(grad, axis=0, keepdims=True),
        )

    gain_one, shift_one = by_rows(first_back, (nothing, nothing))
    save(fgrad_ref, fgrad_out)

    for index in range(width // cols):
        here = slice(index * cols, (index + 1) * cols)
        ograd_ref[here, :] = dot_nt(low_one[...], wo[here, :]).T.astype(low)
        save(ograd_ref.at[here], ograd_out.at[here])
    for index, vector in enumerate(
        (gain_one, gain_two, gain_three, shift_one, shift_two, shift_three)
    ):
        vecs_ref[2 + index : 3 + index, :] = vector
    for copy in saves:
        copy.wait()


def middle(
    tokens, attended, cotangent, mem_key, mem_value, gains, shifts, down_bias, raise_bias, weights
):
    length, width = tokens.shape
    mem_len = mem_key.shape[0]
    down = weights[3].shape[1]
    feed = weights[5].shape[1]
    tile = 512 if mem_len <= 512 else 128
    resident = mem_len <= 512
    slots = feed // tile if resident else 2
    low = jnp.bfloat16
    f32 = jnp.float32
    vmem = pl.BlockSpec(memory_space=pltpu.VMEM)
    anywhere = pl.BlockSpec(memory_space=pl.ANY)
    square = pltpu.VMEM((width, width), low)
    wide = pltpu.VMEM((length, width), f32)
    narrow = pltpu.VMEM((length, width), low)
    return pl.pallas_call(
        middle_kernel,
        out_shape=(
            jax.ShapeDtypeStruct((length, width), low),
            jax.ShapeDtypeStruct((length, width), f32),
            jax.ShapeDtypeStruct((width, length), low),
            jax.ShapeDtypeStruct((mem_len, width), low),
            jax.ShapeDtypeStruct((mem_len, width), low),
            jax.ShapeDtypeStruct((2 * down * width // LANES, LANES), low),
            jax.ShapeDtypeStruct((8, width), f32),
        ),
        in_specs=[anywhere] * 5 + [vmem] * 4 + [anywhere] * 7,
        out_specs=(anywhere,) * 6 + (vmem,),
        scratch_shapes=[
            narrow,
            narrow,
            narrow,
            pltpu.VMEM((mem_len, width), low),
            pltpu.VMEM((mem_len, width), low),
            narrow,
            wide,
            pltpu.VMEM((width, length), low),
            pltpu.VMEM((2 * down * width // LANES, LANES), low),
            square,
            square,
            square,
            pltpu.VMEM((width, down), low),
            pltpu.VMEM((down, width), low),
            pltpu.VMEM((width, feed) if resident else (slots, width, tile), low),
            pltpu.VMEM((feed, width) if resident else (slots, tile, width), low),
            wide,
            wide,
            wide,
            wide,
            pltpu.VMEM((length, 1), f32),
            pltpu.VMEM((length, 1), f32),
            narrow,
            narrow,
            narrow,
            narrow,
            narrow,
            pltpu.VMEM((width // LANES, mem_len, LANES // HD * length), low),
            pltpu.VMEM((length, feed), low),
            pltpu.VMEM((length, feed) if resident else (16, LANES), low),
            pltpu.VMEM((length, down), low),
            pltpu.VMEM((length, down), low),
            pltpu.VMEM((length, down), low),
            pltpu.SemaphoreType.DMA((10,)),
            pltpu.SemaphoreType.DMA((slots,)),
            pltpu.SemaphoreType.DMA((slots,)),
            pltpu.SemaphoreType.DMA((5 + width // 512,)),
        ],
        compiler_params=pltpu.CompilerParams(vmem_limit_bytes=VMEM_BYTES + 3 * 1024 * 1024),
        name="middle",
    )(tokens, attended, cotangent, mem_key, mem_value, gains, shifts, down_bias, raise_bias, *weights)


def per_device(
    tokens,
    memory,
    segment_ids,
    padding_mask,
    cotangent,
    prefix_embed,
    prefix_first,
    first_bias,
    prefix_second,
    second_bias,
    adapter_down,
    down_bias,
    adapter_raise,
    raise_bias,
    norm_gain,
    norm_shift,
    self_query,
    self_key,
    self_value,
    self_output,
    cross_query,
    cross_key,
    cross_value,
    cross_output,
    feed_in,
    feed_out,
):
    row_count, length, model_width = tokens.shape
    flat_rows = row_count * length
    n = lax.axis_size("seq")
    batches = lax.axis_size("batch")
    down = adapter_down.shape[1]
    attended, mem_key, mem_value, *saved = self_forward(
        n,
        segment_ids,
        padding_mask,
        tokens.reshape(flat_rows, model_width),
        (self_query, self_key, self_value),
        (
            prefix_embed,
            prefix_first,
            first_bias.reshape(1, -1),
            prefix_second,
            second_bias.reshape(1, -1),
        ),
        memory.reshape(-1, model_width),
        (cross_key, cross_value),
    )
    layer_output, first_grad, out_grad, *mem_grads, weight_sums, vector_sums = middle(
        tokens.reshape(flat_rows, model_width),
        attended,
        cotangent.reshape(flat_rows, model_width),
        mem_key,
        mem_value,
        norm_gain,
        norm_shift,
        down_bias.reshape(1, -1),
        raise_bias.reshape(1, -1),
        (
            self_output,
            cross_query,
            cross_output,
            adapter_down,
            adapter_raise,
            feed_in,
            feed_out,
        ),
    )
    layer_output = layer_output.reshape(row_count, length, model_width)
    token_grad, memory_grad, *prefix_sums, vector_sums, full_sums = self_backward(
        n,
        batches,
        first_grad,
        out_grad.reshape(n, -1, HD, length),
        weight_sums,
        mem_grads,
        (cross_key, cross_value),
        vector_sums,
        saved,
        (self_query, self_key, self_value),
        (prefix_first, prefix_second, prefix_embed, first_bias.reshape(1, -1)),
    )
    *replicated, token_grad, memory_grad = finish(
        full_sums.reshape(-1, LANES),
        vector_sums,
        prefix_sums,
        prefix_embed,
        down,
        token_grad,
        memory_grad,
    )
    token_grad = token_grad.reshape(row_count, length, model_width)
    memory_grad = memory_grad.reshape(memory.shape)
    replicated = [
        value.reshape(-1) if value.shape[0] == 1 else value for value in replicated
    ]
    return (layer_output, token_grad, memory_grad, *replicated)


def solution(mesh):
    placed = (
        P("batch", "seq", None),
        P("batch", "seq", None),
        P("batch", "seq"),
        P("batch", "seq"),
        P("batch", "seq", None),
        P(),
        P(),
        P(),
        P(),
        P(),
        P(),
        P(),
        P(),
        P(),
        P(),
        P(),
        P(),
        P(),
        P(),
        P(),
        P(),
        P(),
        P(),
        P(),
        P(),
        P(),
    )
    return jax.shard_map(
        per_device,
        mesh=mesh,
        in_specs=placed,
        out_specs=(
            P("batch", "seq", None),
            P("batch", "seq", None),
            P("batch", "seq", None),
            P(),
            P(),
            P(),
            P(),
            P(),
            P(),
            P(),
            P(),
            P(),
            P(),
            P(),
        ),
        check_vma=False,
    )
```
